32 devices in a mesh: dp: 8 (over y, x, core), mp: 4 (over z).
Axes of the slice: x: 2, y: 2, z: 4, core: 2. Of those that a mesh axis runs over, the one named last changes fastest.
Arguments:
- tokens: bfloat16 [8192, 1024], P('dp'), may hold values from -6 to 6
- cotangent: bfloat16 [8192, 1024], P('dp'), may hold values from -6 to 6
- ln_gains: float32 [2, 1024], replicated, may hold values from 0.5 to 1.5
- ln_biases: float32 [2, 1024], replicated, may hold values from -2 to 2
- w_qkv: bfloat16 [1024, 3, 1024], P(None, None, 'mp'), may hold values from -0.1875 to 0.1875
- w_o: bfloat16 [1024, 1024], P('mp'), may hold values from -0.75 to 0.75
- w_in: bfloat16 [1024, 4096], P(None, 'mp'), may hold values from -0.1875 to 0.1875
- w_out: bfloat16 [4096, 1024], P('mp'), may hold values from -0.1875 to 0.1875
- w_router: bfloat16 [1024, 8], replicated, may hold values from -0.125 to 0.125
- w_coef: bfloat16 [1024, 2], replicated, may hold values from -0.1875 to 0.1875
- w_up: bfloat16 [8, 1024, 4096], P('dp', None, 'mp'), may hold values from -0.1875 to 0.1875
- w_down: bfloat16 [8, 4096, 1024], P('dp', 'mp'), may hold values from -3 to 3
- routes: int32 [8192, 1], P('dp'), may hold values from 0 to 7; in each aligned block of 1024 rows (0 to 1023, 1024 to 2047, ...) at most 256 rows name the same one
- long_group: int32 [2], replicated, may hold values from 1 to 4096, as said below
Outputs:
- output: bfloat16 [8192, 1024], P('dp')
- grad_tokens: bfloat16 [8192, 1024], P('dp')
- grad_gains: float32 [2, 1024], P(None, 'dp')
- grad_biases: float32 [2, 1024], P(None, 'dp')
- grad_qkv: float32 [1024, 3, 1024], P('dp', None, 'mp')
- grad_o: float32 [1024, 1024], P('mp', 'dp')
- grad_in: float32 [1024, 4096], P('dp', 'mp')
- grad_out: float32 [4096, 1024], P('mp', 'dp')
- grad_router: float32 [1024, 8], P('dp')
- grad_coef: float32 [1024, 2], P('dp')
- grad_up: float32 [8, 1024, 4096], P('dp', None, 'mp')
- grad_down: float32 [8, 4096, 1024], P('dp', 'mp')
The draws below stay inside these ranges and needn't reach their ends.
Inputs may be any that keep to these rules, and one draw needn't show every extreme that they name: `routes`: in the rows of one device (1024 rows) no expert is named by more than 256 rows, a bound that some block reaches. `long_group`: at least one group's first sequence fills the whole group (4096 rows).
All inputs are finite; a program needn't handle non-finite values.
Results may differ from the reference program's by a relative error of at most 0.015.
Values may be sent and summed in bfloat16 or wider, within the bound.
No kernel may reach another device: no remote copies, remote signals or barrier semaphores. Data moves between devices by JAX's collectives and lax.ppermute only.
A program may use at most 320 MiB of HBM per device.

```python
import math
from functools import partial
import jax
import jax.numpy as jnp
import numpy as np
from jax import lax

D = 1024
HEADS = 16
HD = 64
FF = 4096
TOK_DEV = 1024
TOKENS = 8192
GROUPS = 2
EXPERTS = 8
CAP = 256
N_DP = 8


def draw_long_group(key, part):
    key = jax.random.fold_in(key, 7)
    first, second = jax.random.split(key)
    lengths = jax.random.randint(first, (GROUPS,), 1, 4 * TOK_DEV)
    chosen = jax.random.randint(second, (), 0, GROUPS)
    return jnp.where(jnp.arange(GROUPS) == chosen, 4 * TOK_DEV, lengths).astype(jnp.int32)


def shard_levels(rng, extent, cuts, smallest, top_value):
    level = 1.0
    for axis_at, shards_of in cuts:
        heights = jax.random.uniform(jax.random.fold_in(jax.random.fold_in(rng, 6), axis_at), (shards_of,), jnp.float32, smallest / len(cuts), top_value / len(cuts))
        level = level * jnp.repeat(jnp.exp(heights), extent[axis_at] // shards_of).reshape((-1,) + (1,) * (len(extent) - 1 - axis_at))
    return level


def deal_out(key, own, number, rows, count, top, bound, skew):
    order = jax.random.permutation(key, count)
    crowded, usual = portions_of(count, rows * top, bound, skew, True), portions_of(count, rows * top, bound, skew, False)
    places = jnp.arange(count)

    def named(sizes, turn):
        used = int((sizes > 0).sum())
        fixed = max(1, used // 4)
        moved = fixed + (places - fixed + turn * (used - fixed)) % max(1, count - fixed)
        return jnp.zeros((count,), jnp.int32).at[order[jnp.where(places < fixed, places, moved)]].set(jnp.asarray(sizes, jnp.int32))

    sizes = jnp.where(number % 4 == 0, named(crowded, number // 4), named(usual, number - number // 4 - 1))
    mixed = jax.random.permutation(jax.random.fold_in(own, 3), count)
    source_of, sink = mixed[0:count // 2 * 2:2], mixed[1:count // 2 * 2:2]
    room = jnp.minimum(sizes[source_of] - 1, bound - sizes[sink]) // 2
    room = jnp.where((source_of == order[0]) | (sink == order[0]) | (sizes[sink] == 0), 0, jnp.maximum(room, 0))
    moved = jax.random.randint(jax.random.fold_in(own, 4), (count // 2,), 0, 1 << 20) % (room + 1)
    sizes = sizes.at[source_of].add(-moved).at[sink].add(moved)
    labels = jnp.searchsorted(jnp.cumsum(sizes), jnp.arange(rows * top), side="right").astype(jnp.int32)
    listing = labels.reshape(top, rows).T
    listing = listing[jax.random.permutation(jax.random.fold_in(own, 1), rows)]
    turn = jax.random.randint(jax.random.fold_in(own, 2), (rows, 1), 0, top)
    return jnp.take_along_axis(listing, (jnp.arange(top)[None, :] + turn) % top, axis=1)


def portions_of(count, total, reach, lean, full):
    weights = [(1 << 20) // math.isqrt(standing ** lean) + 1 for standing in range(1, count + 1)]
    largest = reach if full else min(reach, max(-(-total // count), total * weights[0] // sum(weights)))
    least = 1 if total - largest >= count - 1 else 0
    holding, surplus = [largest] + [least] * (count - 1), total - largest - least * (count - 1)
    while surplus > 0:
        free = [i for i in range(1, count) if holding[i] < largest] or [i for i in range(1, count) if holding[i] < reach]
        pool, budget = sum([weights[i] for i in free]), surplus
        for i in free:
            extra = min(reach - holding[i], max(1, budget * weights[i] // pool), surplus)
            holding[i] = holding[i] + extra
            surplus = surplus - extra
    return np.array(holding)


def scatter_about(own_key, shape, spread, reach, shards=(), kind=jnp.bfloat16):
    array = spread * jax.random.normal(own_key, shape, jnp.float32)
    if shards:
        array = array * shard_levels(own_key, shape, shards, -0.22, 0.18)
    return jnp.clip(array, -reach, reach).astype(kind)


def setup_inputs(seed: int = 0) -> dict:
    key_list = jax.random.split(jax.random.key(seed), 15)
    tokens = scatter_about(key_list[0], (TOKENS, D), 1.0, 6.0, ((0, 8),))
    cotangent = scatter_about(key_list[1], (TOKENS, D), 1.0, 6.0, ((0, 8),))
    ln_gains = jnp.clip(1.0 + 0.1 * jax.random.normal(key_list[2], (2, D), jnp.float32), 0.5, 1.5)
    ln_biases = scatter_about(key_list[3], (2, D), 0.3, 2.0, (), jnp.float32)
    w_qkv = scatter_about(key_list[4], (D, 3, D), D ** -0.5, 0.1875, ((2, 4),))
    w_o = scatter_about(key_list[5], (D, D), (D // 16) ** -0.5, 0.75, ((0, 4),))
    w_in = scatter_about(key_list[6], (D, FF), D ** -0.5, 0.1875, ((1, 4),))
    w_out = scatter_about(key_list[7], (FF, D), (FF // 4) ** -0.5, 0.1875, ((0, 4),))
    w_router = scatter_about(key_list[8], (D, EXPERTS), (2 * D) ** -0.5, 0.125)
    w_coef = scatter_about(key_list[9], (D, 2), D ** -0.5, 0.1875)
    w_up = scatter_about(key_list[10], (EXPERTS, D, FF), D ** -0.5, 0.1875, ((0, 8), (2, 4)))
    w_down = scatter_about(key_list[11], (EXPERTS, FF, D), (0.025 * EXPERTS), 3.0, ((0, 8), (1, 4)))
    routes_keys = jax.random.split(jax.random.fold_in(key_list[12], 1), TOKENS // TOK_DEV)
    routes_turns = jax.random.permutation(jax.random.fold_in(key_list[12], 3), TOKENS // TOK_DEV)
    routes = jax.vmap(lambda own, number: deal_out(jax.random.fold_in(key_list[12], 2), own, number, TOK_DEV, EXPERTS, 1, CAP, 1))(routes_keys, routes_turns).reshape((TOKENS, 1))
    long_group = draw_long_group(jax.random.fold_in(key_list[14], 71), 0)
    return dict(tokens=tokens, cotangent=cotangent, ln_gains=ln_gains, ln_biases=ln_biases, w_qkv=w_qkv, w_o=w_o, w_in=w_in, w_out=w_out, w_router=w_router, w_coef=w_coef, w_up=w_up, w_down=w_down, routes=routes, long_group=long_group)


EPS = 1e-05
HIGH = lax.Precision.HIGHEST

@jax.custom_vjp
def low(v):
    return lax.optimization_barrier(v.astype(jnp.bfloat16)).astype(jnp.float32)

@jax.custom_vjp
def low_back(v):
    return v

def low_keep(v):
    return (low(v), None)

def low_pass(kept, grad):
    return (grad,)

def back_keep(v):
    return (v, None)

def back_low(kept, grad):
    return (low(grad),)
low.defvjp(low_keep, low_pass)
low_back.defvjp(back_keep, back_low)

def layer_norm(v, gain, bias):
    mean = lax.optimization_barrier(jnp.mean(v, axis=-1, keepdims=True))
    centred = v - mean
    var = lax.optimization_barrier(jnp.mean(centred * centred, axis=-1, keepdims=True))
    return centred * lax.rsqrt(var + EPS) * gain + bias

def gelu_tanh(v):
    return jax.nn.gelu(v, approximate=True)

def group_attention(query, keys, values, first_len):
    length = query.shape[0]
    qrows = min(1024, length)
    blocks = length // qrows
    kpos = jnp.arange(length, dtype=jnp.int32)
    kdoc = kpos >= first_len

    def block(index):
        qb = lax.dynamic_slice_in_dim(query, index * qrows, qrows, 0)
        qpos = index * qrows + jnp.arange(qrows, dtype=jnp.int32)
        qdoc = qpos >= first_len
        scores = jnp.einsum('qhe,khe->hqk', qb, keys, precision=HIGH) * 0.125
        scores = low_back(scores)
        visible = (kpos[None, :] <= qpos[:, None]) & (kdoc[None, :] == qdoc[:, None])
        scores = jnp.where(visible[None], scores, -1e+30)
        probs = low(jax.nn.softmax(scores, axis=-1))
        return jnp.einsum('hqk,khe->qhe', probs, values, precision=HIGH)
    out = lax.map(jax.checkpoint(block), jnp.arange(blocks, dtype=jnp.int32))
    return out.reshape(length, query.shape[1], query.shape[2])

def forward(x, gains, biases, w_qkv, w_o, w_in, w_out, w_router, w_coef, w_up, w_down, picked, index, flags):
    rows = x.shape[0]
    a = low(layer_norm(x, gains[0], biases[0]))
    qkv = jnp.einsum('td,dcf->tcf', a, w_qkv, precision=HIGH)
    query = low(low_back(qkv[:, 0])).reshape(GROUPS, 4 * TOK_DEV, HEADS, HD)
    keys = low(low_back(qkv[:, 1])).reshape(GROUPS, 4 * TOK_DEV, HEADS, HD)
    values = low(low_back(qkv[:, 2])).reshape(GROUPS, 4 * TOK_DEV, HEADS, HD)

    def step(carry, item):
        return (carry, jax.checkpoint(group_attention)(item[0], item[1], item[2], item[3]))
    _, attended = lax.scan(step, jnp.float32(0.0), (query, keys, values, flags))
    attended = low(low_back(attended.reshape(rows, D)))
    h = x + low_back(jnp.dot(attended, w_o, precision=HIGH))
    b = low(layer_norm(h, gains[1], biases[1]))
    probs = jax.nn.softmax(jnp.dot(b, w_router, precision=HIGH), axis=-1)
    gate = lax.optimization_barrier(jnp.sum(probs * picked, axis=-1))
    coef = jax.nn.softmax(jnp.dot(b, w_coef, precision=HIGH), axis=-1)
    up = low_back(jnp.dot(b, w_in, precision=HIGH))
    hidden = low(gelu_tanh(up))
    dense = low_back(jnp.dot(hidden, w_out, precision=HIGH))
    per_expert = N_DP * CAP
    buffer = jnp.zeros((EXPERTS * per_expert, D), jnp.float32).at[index].set(b)
    buffer = buffer.reshape(EXPERTS, per_expert, D)
    expert_up = low_back(jnp.einsum('erd,edf->erf', buffer, w_up, precision=HIGH))
    expert_hidden = low(gelu_tanh(expert_up))
    expert_out = jnp.einsum('erf,efd->erd', expert_hidden, w_down, precision=HIGH)
    expert_tok = low_back(expert_out.reshape(EXPERTS * per_expert, D)[index])
    mix = coef[:, 0:1] * dense + (coef[:, 1] * gate)[:, None] * expert_tok
    return h + mix

def reference(tokens, cotangent, ln_gains, ln_biases, w_qkv, w_o, w_in, w_out, w_router, w_coef, w_up, w_down, routes, long_group):
    route = routes[:, 0].astype(jnp.int32)
    rows = route.shape[0]
    picked_i = (route[:, None] == jnp.arange(EXPERTS, dtype=jnp.int32)[None, :]).astype(jnp.int32)
    blocked = picked_i.reshape(N_DP, TOK_DEV, EXPERTS)
    slot = lax.optimization_barrier(jnp.sum((jnp.cumsum(blocked, axis=1) - blocked) * blocked, axis=2)).reshape(rows).astype(jnp.int32)
    source = (jnp.arange(rows, dtype=jnp.int32) // TOK_DEV).astype(jnp.int32)
    index = (route * (N_DP * CAP) + source * CAP + slot).astype(jnp.int32)
    picked = picked_i.astype(jnp.float32)
    floats = [tokens, ln_gains, ln_biases, w_qkv, w_o, w_in, w_out, w_router, w_coef, w_up, w_down]
    floats = [item.astype(jnp.float32) for item in floats]
    out, pull = jax.vjp(partial(forward, picked=picked, index=index, flags=long_group.astype(jnp.int32)), *floats)
    grads = pull(cotangent.astype(jnp.float32))
    return (out.astype(jnp.bfloat16), grads[0].astype(jnp.bfloat16), grads[1], grads[2], grads[3], grads[4], grads[5], grads[6], grads[7], grads[8], grads[9], grads[10])
```

```python
from functools import partial

import jax
import jax.numpy as jnp
from jax import lax
from jax.experimental import pallas as pl
from jax.experimental.pallas import tpu as pltpu
from jax.sharding import PartitionSpec as P

HD = 64
GROUP = 4
EPS = 1e-05
LOG2E = 1.4426950408889634
SCALE2 = 0.125 * LOG2E
HIDE = -1e30
BF = jnp.bfloat16
F32 = jnp.float32


def layer_norm(v, gain, bias):
    mean = jnp.mean(v, axis=-1, keepdims=True)
    centred = v - mean
    var = jnp.mean(centred * centred, axis=-1, keepdims=True)
    return centred * lax.rsqrt(var + EPS) * gain + bias


def gelu_tanh(v):
    return jax.nn.gelu(v, approximate=True)


def mm(a, b):
    return jnp.dot(a, b, preferred_element_type=F32)


def ein(spec, a, b):
    return jnp.einsum(spec, a, b, preferred_element_type=F32)


def fill_keys(k_s, place, keys, first_len, blk):
    rows = place * blk + lax.broadcasted_iota(jnp.int32, (blk, 128), 0)
    lane = lax.broadcasted_iota(jnp.int32, (blk, 128), 1)
    wide = jnp.concatenate([keys.astype(F32).T, jnp.zeros((blk, 128 - HD), F32)], axis=1)
    wide = jnp.where((lane == HD) & (rows < first_len), HIDE, wide)
    k_s[pl.ds(place * blk, blk), :] = wide.astype(BF)


def wide_query(query, place, first_len, blk):
    cols = place * blk + lax.broadcasted_iota(jnp.int32, (128 - HD, blk), 1)
    sub = lax.broadcasted_iota(jnp.int32, (128 - HD, blk), 0)
    extra = jnp.where((sub == 0) & (cols >= first_len), 1.0, 0.0)
    return jnp.concatenate([query, extra.astype(BF)], axis=0)


def causal(blk):
    keys = lax.broadcasted_iota(jnp.int32, (blk, blk), 0)
    queries = lax.broadcasted_iota(jnp.int32, (blk, blk), 1)
    return keys <= queries


def attend_kernel(blk, per, len_ref, qkv_ref, o_ref, lse_ref, k_s):
    i = pl.program_id(0)
    first_len = len_ref[0]

    def part(which, j):
        return qkv_ref[j // per, HD * which : HD * (which + 1), pl.ds((j % per) * blk, blk)]

    fill_keys(k_s, i, part(1, i), first_len, blk)
    query = wide_query(part(0, i), i, first_len, blk)

    def scores(j):
        return mm(k_s[pl.ds(pl.multiple_of(j * blk, blk), blk), :], query)

    s = jnp.where(causal(blk), scores(i), HIDE)
    top = jnp.max(s, axis=0, keepdims=True)
    p = jnp.exp2((s - top) * SCALE2)
    total = jnp.sum(p, axis=0, keepdims=True)
    acc = mm(part(2, i), p.astype(BF))

    def step(j, carry):
        top, total, acc = carry
        s = scores(j)
        new = jnp.maximum(top, jnp.max(s, axis=0, keepdims=True))
        p = jnp.exp2((s - new) * SCALE2)
        keep = jnp.exp2((top - new) * SCALE2)
        total = total * keep + jnp.sum(p, axis=0, keepdims=True)
        acc = acc * keep + mm(part(2, j), p.astype(BF))
        return new, total, acc

    low = jnp.where(i * blk >= first_len, first_len // blk, 0)
    top, total, acc = lax.fori_loop(low, i, step, (top, total, acc))
    o_ref[0] = (acc / total).astype(BF)
    lse_ref[0] = top * SCALE2 + jnp.log2(total)


def attend(first_len, qkv):
    parts, _, rows = qkv.shape
    blk = min(512, rows)
    per = rows // blk
    count = parts * per
    return pl.pallas_call(
        partial(attend_kernel, blk, per),
        grid_spec=pltpu.PrefetchScalarGridSpec(
            num_scalar_prefetch=1,
            grid=(count,),
            in_specs=[pl.BlockSpec((parts, 3 * HD, rows), lambda i, n: (0, 0, 0))],
            out_specs=[
                pl.BlockSpec((1, HD, blk), lambda i, n: (i // per, 0, i % per)),
                pl.BlockSpec((1, 1, blk), lambda i, n: (i, 0, 0)),
            ],
            scratch_shapes=[pltpu.VMEM((parts * rows, 128), BF)],
        ),
        out_shape=[
            jax.ShapeDtypeStruct((parts, HD, rows), BF),
            jax.ShapeDtypeStruct((count, 1, blk), F32),
        ],
        compiler_params=pltpu.CompilerParams(vmem_limit_bytes=40 * 2**20),
        cost_estimate=pl.CostEstimate(
            flops=8 * (parts * rows) ** 2 * HD,
            bytes_accessed=4 * parts * rows * HD * 2,
            transcendentals=(parts * rows) ** 2 // 2,
        ),
        name="attend",
    )(first_len, qkv)


def back_kernel(
    blk, per, count, len_ref, qkv_ref, do_ref, o_ref, lse_ref, out_ref, k_s, v_s, dq_s, wide_s, both_s, delta_s, acc_s
):
    j = pl.program_id(0)
    first_len = len_ref[0]

    def part(which, i):
        return qkv_ref[i // per, HD * which : HD * (which + 1), pl.ds((i % per) * blk, blk)]

    def dout(i):
        return do_ref[i // per, :, pl.ds((i % per) * blk, blk)]

    @pl.when(j == 0)
    def _():
        def prepare(i, carry):
            at = pl.ds(pl.multiple_of(i * blk, blk), blk)
            fill_keys(k_s, i, part(1, i), first_len, blk)
            wide_s[:, at] = wide_query(part(0, i), i, first_len, blk)
            zero = jnp.zeros((blk, HD), F32)
            grad = dout(i).astype(F32)
            v_s[at, :] = jnp.concatenate([part(2, i).astype(F32).T, zero], axis=1).astype(BF)
            both_s[0, at, :] = jnp.concatenate([grad.T, zero], axis=1).astype(BF)
            both_s[1, at, :] = jnp.concatenate([zero, part(0, i).astype(F32).T], axis=1).astype(BF)
            held = o_ref[i // per, :, pl.ds((i % per) * blk, blk)].astype(F32)
            delta_s[i] = jnp.sum(held * grad, axis=0, keepdims=True)
            dq_s[:, at] = jnp.zeros((HD, blk), F32)
            return carry

        lax.fori_loop(0, count, prepare, 0)

    here = pl.ds(pl.multiple_of(j * blk, blk), blk)
    keys_t = part(1, j)
    values = v_s[here, 0:HD]

    def pair(i, diagonal):
        at = pl.ds(pl.multiple_of(i * blk, blk), blk)
        s = mm(k_s[here, :], wide_s[:, at])
        p = jnp.exp2(s * SCALE2 - lse_ref[i])
        if diagonal:
            p = jnp.where(causal(blk), p, 0.0)
        dp = mm(values, dout(i))
        ds = (p * (dp - delta_s[i])).astype(BF)
        dq_s[:, at] += mm(keys_t, ds)
        return mm(p.astype(BF), both_s[0, at, :]) + mm(ds, both_s[1, at, :])

    acc_s[...] = pair(j, True)

    def step(i, carry):
        acc_s[...] += pair(i, False)
        return carry

    high = jnp.where((j + 1) * blk <= first_len, (first_len + blk - 1) // blk, count)
    lax.fori_loop(j + 1, high, step, 0)
    both = acc_s[...].T
    out_ref[0, 0:HD, :] = (dq_s[:, here] * 0.125).astype(BF)
    out_ref[0, HD : 2 * HD, :] = (both[HD:, :] * 0.125).astype(BF)
    out_ref[0, 2 * HD :, :] = both[:HD, :].astype(BF)


def attend_back(first_len, qkv, do, o, lse):
    parts, _, rows = qkv.shape
    blk = min(512, rows)
    per = rows // blk
    count = parts * per
    whole = lambda j, n: (0, 0, 0)
    return pl.pallas_call(
        partial(back_kernel, blk, per, count),
        grid_spec=pltpu.PrefetchScalarGridSpec(
            num_scalar_prefetch=1,
            grid=(count,),
            in_specs=[
                pl.BlockSpec((parts, 3 * HD, rows), whole),
                pl.BlockSpec((parts, HD, rows), whole),
                pl.BlockSpec((parts, HD, rows), whole),
                pl.BlockSpec((count, 1, blk), whole),
            ],
            out_specs=pl.BlockSpec((1, 3 * HD, blk), lambda j, n: (j // per, 0, j % per)),
            scratch_shapes=[
                pltpu.VMEM((parts * rows, 128), BF),
                pltpu.VMEM((parts * rows, 128), BF),
                pltpu.VMEM((HD, parts * rows), F32),
                pltpu.VMEM((128, parts * rows), BF),
                pltpu.VMEM((2, parts * rows, 128), BF),
                pltpu.VMEM((count, 1, blk), F32),
                pltpu.VMEM((blk, 128), F32),
            ],
        ),
        out_shape=jax.ShapeDtypeStruct((parts, 3 * HD, rows), BF),
        compiler_params=pltpu.CompilerParams(vmem_limit_bytes=48 * 2**20),
        cost_estimate=pl.CostEstimate(
            flops=20 * (parts * rows) ** 2 * HD,
            bytes_accessed=8 * parts * rows * HD * 2,
            transcendentals=(parts * rows) ** 2 // 2,
        ),
        name="attend_back",
    )(first_len, qkv, do, o, lse)


def rotate(value, steps):
    count = lax.axis_size("mp")
    return lax.ppermute(value, "mp", [(s, (s + steps) % count) for s in range(count)])


def gather_rows(own):
    return jnp.concatenate([own] + [rotate(own, -r) for r in range(1, lax.axis_size("mp"))], axis=0)


def scatter_sum(quarters):
    total = quarters[0]
    for r in range(1, len(quarters)):
        total = total + rotate(quarters[r].astype(BF), r).astype(F32)
    return total


def roll_rows(value, start):
    twice = jnp.concatenate([value, value], axis=0)
    return lax.dynamic_slice_in_dim(twice, start, value.shape[0], 0)


def split_two(value):
    high = value.astype(BF)
    low = (value - high.astype(F32)).astype(BF)
    return jnp.concatenate([high, low], axis=1)


def body(
    tokens,
    cotangent,
    ln_gains,
    ln_biases,
    w_qkv,
    w_o,
    w_in,
    w_out,
    w_router,
    w_coef,
    w_up,
    w_down,
    routes,
    long_group,
):
    rows, width = tokens.shape
    mps, dps = lax.axis_size("mp"), lax.axis_size("dp")
    mine, position = lax.axis_index("mp"), lax.axis_index("dp")
    quarter = rows // mps
    start = mine * quarter
    heads_loc = w_qkv.shape[2] // HD
    experts = w_router.shape[1]
    capacity = max(2, 2 * rows // experts)
    slots = experts * capacity
    groups = [[g * GROUP + t for t in range(GROUP)] for g in range(dps // GROUP)]
    first_len = lax.dynamic_slice_in_dim(long_group, position // GROUP, 1, 0)
    chunks = 2
    step = width // chunks
    cuts = [slice(c * step, (c + 1) * step) for c in range(chunks)]

    def group_swap(value):
        return lax.all_to_all(value, "dp", 0, 0, axis_index_groups=groups, tiled=True)

    def expert_swap(value):
        wide = value.reshape(experts, capacity, value.shape[1])
        return lax.all_to_all(wide, "dp", 0, 0, tiled=True).reshape(value.shape)

    w_o_all = lax.all_gather(w_o, "mp", axis=0, tiled=True)

    x = tokens.astype(F32)
    a_r = layer_norm(x, ln_gains[0], ln_biases[0]).astype(BF)
    w_heads = w_qkv.reshape(width, 3, heads_loc, HD)
    qkv = ein("td,dche->hcet", a_r, w_heads).astype(BF).reshape(heads_loc, 3 * HD, rows)
    qkv = group_swap(qkv)

    route = roll_rows(routes, start)[:, 0]
    picked = (route[:, None] == jnp.arange(experts, dtype=jnp.int32)[None, :]).astype(jnp.int32)
    slot = jnp.sum((jnp.cumsum(picked, axis=0) - picked) * picked, axis=1)
    dest = route * capacity + slot
    spread = (jnp.arange(slots, dtype=jnp.int32)[:, None] == dest[None, :]).astype(BF)
    dy_b = roll_rows(cotangent, start)
    dy = dy_b.astype(F32)
    got_dy = expert_swap(mm(spread, dy_b).astype(BF))

    o_t, lse = attend(first_len, qkv)
    o_heads = group_swap(o_t).reshape(heads_loc * HD, rows)
    o_q = lax.all_to_all(o_heads, "mp", 1, 0, tiled=True)
    x_q = lax.dynamic_slice_in_dim(tokens, start, quarter, 0).astype(F32)
    h = x_q + ein("ft,fd->td", o_q, w_o_all)
    b, norm_two = jax.vjp(layer_norm, h, ln_gains[1], ln_biases[1])
    b_q = b.astype(BF)

    b_parts, got_parts = [], []
    for cut in cuts:
        part = gather_rows(b_q[:, cut])
        b_parts.append(part)
        got_parts.append(expert_swap(mm(spread, part).astype(BF)))
    b_r = jnp.concatenate(b_parts, axis=1)
    got = jnp.concatenate(got_parts, axis=1)

    up = mm(b_r, w_in)
    hidden, dense_pull = jax.vjp(gelu_tanh, up)
    hidden_r = hidden.astype(BF)
    dense = mm(hidden_r, w_out)
    coef = jax.nn.softmax(mm(b_r, w_coef), axis=-1)
    dense_grad = (coef[:, 0:1] * dy).astype(BF)
    d_up = dense_pull(ein("td,fd->tf", dense_grad, w_out))[0].astype(BF)
    along = coef[:, 0] * coef[:, 1] * jnp.sum(dy * dense, axis=1)
    d_lc = split_two(jnp.stack([along, -along], axis=1))
    w_coef_two = jnp.concatenate([w_coef, w_coef], axis=1)

    w_small = jnp.concatenate([w_router, w_coef], axis=1)
    logits = mm(got, w_small)
    probs = jax.nn.softmax(logits[:, :experts], axis=-1)
    coef_e = jax.nn.softmax(logits[:, experts:], axis=-1)
    own = (jnp.arange(experts, dtype=jnp.int32) == position).astype(F32)[None, :]
    gate = jnp.sum(probs * own, axis=-1)
    weight = (coef_e[:, 1] * gate)[:, None]
    got_dy_f = got_dy.astype(F32)
    d_y = (weight * got_dy_f).astype(BF)
    expert_up = mm(got, w_up[0])
    expert_hidden, expert_pull = jax.vjp(gelu_tanh, expert_up)
    expert_hidden_r = expert_hidden.astype(BF)
    y = mm(expert_hidden_r, w_down[0])
    along_e = jnp.sum(got_dy_f * y, axis=1)
    back_y = (weight * y).astype(BF)
    d_eu = expert_pull(ein("rd,fd->rf", d_y, w_down[0]))[0].astype(BF)
    d_lr = (gate * coef_e[:, 1] * along_e)[:, None] * (own - probs)
    along_c = coef_e[:, 0] * coef_e[:, 1] * gate * along_e
    d_small = split_two(jnp.concatenate([d_lr, -along_c[:, None], along_c[:, None]], axis=1))
    w_small_two = jnp.concatenate([w_small, w_small], axis=1)

    db_parts = []
    for cut in cuts:
        d_rows = ein("rf,df->rd", d_eu, w_up[0][cut]) + ein("rs,ds->rd", d_small, w_small_two[cut])
        back = expert_swap(d_rows.astype(BF))
        part = (
            ein("tf,df->td", d_up, w_in[cut])
            + ein("ts,ds->td", d_lc, w_coef_two[cut])
            + ein("st,sd->td", spread, back)
        )
        db_parts.append(scatter_sum([part[r * quarter : (r + 1) * quarter] for r in range(mps)]))
    db = jnp.concatenate(db_parts, axis=1)
    dh_norm, d_gain2, d_bias2 = norm_two(db)
    dh = dy[:quarter] + dh_norm
    dh_r = dh.astype(BF)
    do_q = ein("td,fd->ft", dh_r, w_o_all).astype(BF)
    do_heads = lax.all_to_all(do_q, "mp", 0, 1, tiled=True)
    do_t = group_swap(do_heads.reshape(heads_loc, HD, rows))
    d_qkv_t = attend_back(first_len, qkv, do_t, o_t, lse)

    back_tok = expert_swap(back_y)
    mix = coef[:, 0:1] * dense + ein("st,sd->td", spread, back_tok)
    out_q = h + scatter_sum([mix[r * quarter : (r + 1) * quarter] for r in range(mps)])
    output = roll_rows(gather_rows(out_q.astype(BF)), rows - start)

    grad_out = ein("tf,td->fd", hidden_r, dense_grad)
    grad_in = ein("td,tf->df", b_r, d_up)
    grad_down = ein("rf,rd->fd", expert_hidden_r, d_y)[None]
    grad_up = ein("rd,rf->df", got, d_eu)[None]
    grad_o = ein("ft,td->fd", o_q, dh_r)

    def shared(value, dim):
        return lax.psum_scatter(value.astype(BF), "dp", scatter_dimension=dim, tiled=True)

    grad_in = shared(grad_in, 0).astype(F32)
    grad_out = shared(grad_out, 1).astype(F32)
    grad_o = lax.psum_scatter(shared(grad_o, 1), "mp", scatter_dimension=0, tiled=True).astype(F32)
    wide_e = ein("rd,rs->ds", got, d_small)
    wide_t = ein("td,ts->ds", b_r, d_lc)
    small = wide_e[:, : experts + 2] + wide_e[:, experts + 2 :]
    small_t = wide_t[:, :2] + wide_t[:, 2:]
    small = small + jnp.concatenate([jnp.zeros((width, experts), F32), small_t], axis=1)
    small, norm_sums = lax.psum((small, jnp.stack([d_gain2, d_bias2])), ("dp", "mp"))
    share = width // dps
    small = lax.dynamic_slice_in_dim(small, position * share, share, 0)

    d_qkv_t = group_swap(d_qkv_t)
    d_heads = d_qkv_t.reshape(heads_loc, 3, HD, rows)
    grad_qkv = ein("td,hcet->dche", a_r, d_heads).reshape(width, 3, heads_loc * HD)
    grad_qkv = shared(grad_qkv, 0).astype(F32)
    d_a = roll_rows(ein("hcet,dche->td", d_heads, w_heads), start)
    d_a_q = scatter_sum([d_a[r * quarter : (r + 1) * quarter] for r in range(mps)])
    _, norm_one = jax.vjp(layer_norm, x_q, ln_gains[0], ln_biases[0])
    dx_norm, d_gain1, d_bias1 = norm_one(d_a_q)
    grad_tokens = roll_rows(gather_rows((dh + dx_norm).astype(BF)), rows - start)
    first_sums = lax.psum(jnp.stack([d_gain1, d_bias1]), ("dp", "mp"))
    sums = lax.dynamic_slice_in_dim(
        jnp.stack([first_sums, norm_sums], axis=1), position * share, share, 2
    )
    return (
        output,
        grad_tokens,
        sums[0],
        sums[1],
        grad_qkv,
        grad_o,
        grad_in,
        grad_out,
        small[:, :experts],
        small[:, experts:],
        grad_up,
        grad_down,
    )


def solution(mesh):
    in_specs = (
        P("dp", None),
        P("dp", None),
        P(),
        P(),
        P(None, None, "mp"),
        P("mp", None),
        P(None, "mp"),
        P("mp", None),
        P(),
        P(),
        P("dp", None, "mp"),
        P("dp", "mp", None),
        P("dp", None),
        P(),
    )
    out_specs = (
        P("dp", None),
        P("dp", None),
        P(None, "dp"),
        P(None, "dp"),
        P("dp", None, "mp"),
        P("mp", "dp"),
        P("dp", "mp"),
        P("mp", "dp"),
        P("dp", None),
        P("dp", None),
        P("dp", None, "mp"),
        P("dp", "mp", None),
    )
    return jax.shard_map(body, mesh=mesh, in_specs=in_specs, out_specs=out_specs, check_vma=False)
```

```python
from functools import partial

import jax
import jax.numpy as jnp
from jax import lax
from jax.experimental import pallas as pl
from jax.experimental.pallas import tpu as pltpu
from jax.sharding import PartitionSpec as P

HD = 64
GROUP = 4
CHUNKS = 2
HALVES = 2
EPS = 1e-05
LOG2E = 1.4426950408889634
SCALE2 = 0.125 * LOG2E
HIDE = -1e30
BF = jnp.bfloat16
F32 = jnp.float32


def layer_norm(v, gain, bias):
    mean = jnp.mean(v, axis=-1, keepdims=True)
    centred = v - mean
    var = jnp.mean(centred * centred, axis=-1, keepdims=True)
    return centred * lax.rsqrt(var + EPS) * gain + bias


def mm(a, b):
    return jnp.dot(a, b, preferred_element_type=F32)


def ein(spec, a, b):
    return jnp.einsum(spec, a, b, preferred_element_type=F32)


def fill_keys(k_s, place, keys, first_len, blk):
    rows = place * blk + lax.broadcasted_iota(jnp.int32, (blk, 128), 0)
    lane = lax.broadcasted_iota(jnp.int32, (blk, 128), 1)
    wide = jnp.concatenate([keys.astype(F32).T, jnp.zeros((blk, 128 - HD), F32)], axis=1)
    wide = jnp.where((lane == HD) & (rows < first_len), HIDE, wide)
    k_s[pl.ds(place * blk, blk), :] = wide.astype(BF)


def wide_query(query, place, first_len, blk):
    cols = place * blk + lax.broadcasted_iota(jnp.int32, (128 - HD, blk), 1)
    sub = lax.broadcasted_iota(jnp.int32, (128 - HD, blk), 0)
    extra = jnp.where((sub == 0) & (cols >= first_len), 1.0, 0.0)
    return jnp.concatenate([query, extra.astype(BF)], axis=0)


def causal(blk):
    keys = lax.broadcasted_iota(jnp.int32, (blk, blk), 0)
    queries = lax.broadcasted_iota(jnp.int32, (blk, blk), 1)
    return keys <= queries


def attend_kernel(blk, per, len_ref, qkv_ref, o_ref, lse_ref, k_s):
    i = pl.program_id(0)
    first_len = len_ref[0]

    def part(which, j):
        return qkv_ref[j // per, HD * which : HD * (which + 1), pl.ds((j % per) * blk, blk)]

    fill_keys(k_s, i, part(1, i), first_len, blk)
    query = wide_query(part(0, i), i, first_len, blk)

    def scores(j):
        return mm(k_s[pl.ds(pl.multiple_of(j * blk, blk), blk), :], query)

    s = jnp.where(causal(blk), scores(i), HIDE)
    top = jnp.max(s, axis=0, keepdims=True)
    p = jnp.exp2((s - top) * SCALE2)
    total = jnp.sum(p, axis=0, keepdims=True)
    acc = mm(part(2, i), p.astype(BF))

    def step(j, carry):
        top, total, acc = carry
        s = scores(j)
        new = jnp.maximum(top, jnp.max(s, axis=0, keepdims=True))
        p = jnp.exp2((s - new) * SCALE2)
        keep = jnp.exp2((top - new) * SCALE2)
        total = total * keep + jnp.sum(p, axis=0, keepdims=True)
        acc = acc * keep + mm(part(2, j), p.astype(BF))
        return new, total, acc

    low = jnp.where(i * blk >= first_len, first_len // blk, 0)
    top, total, acc = lax.fori_loop(low, i, step, (top, total, acc))
    o_ref[0] = (acc / total).astype(BF)
    lse_ref[0] = top * SCALE2 + jnp.log2(total)


def attend(first_len, qkv):
    parts, _, rows = qkv.shape
    blk = min(512, rows)
    per = rows // blk
    count = parts * per
    return pl.pallas_call(
        partial(attend_kernel, blk, per),
        grid_spec=pltpu.PrefetchScalarGridSpec(
            num_scalar_prefetch=1,
            grid=(count,),
            in_specs=[pl.BlockSpec((parts, 3 * HD, rows), lambda i, n: (0, 0, 0))],
            out_specs=[
                pl.BlockSpec((1, HD, blk), lambda i, n: (i // per, 0, i % per)),
                pl.BlockSpec((1, 1, blk), lambda i, n: (i, 0, 0)),
            ],
            scratch_shapes=[pltpu.VMEM((parts * rows, 128), BF)],
        ),
        out_shape=[
            jax.ShapeDtypeStruct((parts, HD, rows), BF),
            jax.ShapeDtypeStruct((count, 1, blk), F32),
        ],
        compiler_params=pltpu.CompilerParams(vmem_limit_bytes=40 * 2**20),
        cost_estimate=pl.CostEstimate(
            flops=8 * (parts * rows) ** 2 * HD,
            bytes_accessed=4 * parts * rows * HD * 2,
            transcendentals=(parts * rows) ** 2 // 2,
        ),
        name="attend",
    )(first_len, qkv)


def back_kernel(
    blk, per, count, len_ref, qkv_ref, do_ref, o_ref, lse_ref, out_ref, k_s, v_s, dq_s, wide_s, both_s, delta_s, acc_s
):
    j = pl.program_id(0)
    first_len = len_ref[0]

    def part(which, i):
        return qkv_ref[i // per, HD * which : HD * (which + 1), pl.ds((i % per) * blk, blk)]

    def dout(i):
        return do_ref[i // per, :, pl.ds((i % per) * blk, blk)]

    @pl.when(j == 0)
    def _():
        def prepare(i, carry):
            at = pl.ds(pl.multiple_of(i * blk, blk), blk)
            fill_keys(k_s, i, part(1, i), first_len, blk)
            wide_s[:, at] = wide_query(part(0, i), i, first_len, blk)
            zero = jnp.zeros((blk, HD), F32)
            grad = dout(i).astype(F32)
            v_s[at, :] = jnp.concatenate([part(2, i).astype(F32).T, zero], axis=1).astype(BF)
            both_s[0, at, :] = jnp.concatenate([grad.T, zero], axis=1).astype(BF)
            both_s[1, at, :] = jnp.concatenate([zero, part(0, i).astype(F32).T], axis=1).astype(BF)
            held = o_ref[i // per, :, pl.ds((i % per) * blk, blk)].astype(F32)
            delta_s[i] = jnp.sum(held * grad, axis=0, keepdims=True)
            dq_s[:, at] = jnp.zeros((HD, blk), F32)
            return carry

        lax.fori_loop(0, count, prepare, 0)

    here = pl.ds(pl.multiple_of(j * blk, blk), blk)
    keys_t = part(1, j)
    values = v_s[here, 0:HD]

    def pair(i, diagonal):
        at = pl.ds(pl.multiple_of(i * blk, blk), blk)
        s = mm(k_s[here, :], wide_s[:, at])
        p = jnp.exp2(s * SCALE2 - lse_ref[i])
        if diagonal:
            p = jnp.where(causal(blk), p, 0.0)
        dp = mm(values, dout(i))
        ds = (p * (dp - delta_s[i])).astype(BF)
        dq_s[:, at] += mm(keys_t, ds)
        return mm(p.astype(BF), both_s[0, at, :]) + mm(ds, both_s[1, at, :])

    acc_s[...] = pair(j, True)

    def step(i, carry):
        acc_s[...] += pair(i, False)
        return carry

    high = jnp.where((j + 1) * blk <= first_len, (first_len + blk - 1) // blk, count)
    lax.fori_loop(j + 1, high, step, 0)
    both = acc_s[...].T
    out_ref[0, 0:HD, :] = (dq_s[:, here] * 0.125).astype(BF)
    out_ref[0, HD : 2 * HD, :] = (both[HD:, :] * 0.125).astype(BF)
    out_ref[0, 2 * HD :, :] = both[:HD, :].astype(BF)


def attend_back(first_len, qkv, do, o, lse):
    parts, _, rows = qkv.shape
    blk = min(512, rows)
    per = rows // blk
    count = parts * per
    whole = lambda j, n: (0, 0, 0)
    return pl.pallas_call(
        partial(back_kernel, blk, per, count),
        grid_spec=pltpu.PrefetchScalarGridSpec(
            num_scalar_prefetch=1,
            grid=(count,),
            in_specs=[
                pl.BlockSpec((parts, 3 * HD, rows), whole),
                pl.BlockSpec((parts, HD, rows), whole),
                pl.BlockSpec((parts, HD, rows), whole),
                pl.BlockSpec((count, 1, blk), whole),
            ],
            out_specs=pl.BlockSpec((1, 3 * HD, blk), lambda j, n: (j // per, 0, j % per)),
            scratch_shapes=[
                pltpu.VMEM((parts * rows, 128), BF),
                pltpu.VMEM((parts * rows, 128), BF),
                pltpu.VMEM((HD, parts * rows), F32),
                pltpu.VMEM((128, parts * rows), BF),
                pltpu.VMEM((2, parts * rows, 128), BF),
                pltpu.VMEM((count, 1, blk), F32),
                pltpu.VMEM((blk, 128), F32),
            ],
        ),
        out_shape=jax.ShapeDtypeStruct((parts, 3 * HD, rows), BF),
        compiler_params=pltpu.CompilerParams(vmem_limit_bytes=48 * 2**20),
        cost_estimate=pl.CostEstimate(
            flops=20 * (parts * rows) ** 2 * HD,
            bytes_accessed=8 * parts * rows * HD * 2,
            transcendentals=(parts * rows) ** 2 // 2,
        ),
        name="attend_back",
    )(first_len, qkv, do, o, lse)


def dispatch_kernel(count, dest_ref, *refs):
    pieces, out_ref = refs[:count], refs[count]
    blk, rows = out_ref.shape[0], dest_ref.shape[1]
    i = pl.program_id(0)
    slot = i * blk + lax.broadcasted_iota(jnp.int32, (blk, rows), 0)
    spread = jnp.where(slot == dest_ref[...], 1.0, 0.0).astype(BF)
    each = rows // count
    total = mm(spread[:, :each], pieces[0][...])
    for r in range(1, count):
        total = total + mm(spread[:, r * each : (r + 1) * each], pieces[r][...])
    out_ref[...] = total.astype(BF)
    if count > 1:
        joined_ref = refs[count + 1]

        @pl.when(i == 0)
        def _():
            for r in range(count):
                joined_ref[r * each : (r + 1) * each, :] = pieces[r][...]


def dispatch(dest_row, pieces, slots):
    count, (each, width) = len(pieces), pieces[0].shape
    rows = count * each
    blk = min(256, slots)
    fixed = lambda i: (0, 0)
    out_specs = [pl.BlockSpec((blk, width), lambda i: (i, 0))]
    out_shape = [jax.ShapeDtypeStruct((slots, width), BF)]
    if count > 1:
        out_specs.append(pl.BlockSpec((rows, width), fixed))
        out_shape.append(jax.ShapeDtypeStruct((rows, width), BF))
    return pl.pallas_call(
        partial(dispatch_kernel, count),
        grid=(slots // blk,),
        in_specs=[pl.BlockSpec((1, rows), fixed)] + [pl.BlockSpec((each, width), fixed)] * count,
        out_specs=out_specs,
        out_shape=out_shape,
        compiler_params=pltpu.CompilerParams(vmem_limit_bytes=32 * 2**20),
        cost_estimate=pl.CostEstimate(
            flops=2 * slots * rows * width,
            bytes_accessed=2 * (slots + 2 * rows) * width,
            transcendentals=0,
        ),
        name="dispatch",
    )(dest_row, *pieces)


def combine_kernel(count, dest_ref, back_ref, base_ref, *outs):
    r = pl.program_id(0)
    rows, slots = dest_ref.shape[0], back_ref.shape[0]
    lane = lax.broadcasted_iota(jnp.int32, (rows, slots), 1)
    pick = jnp.where(lane == dest_ref[...], 1.0, 0.0).astype(BF)
    total = mm(pick, back_ref[...]) + base_ref[...]
    for k in range(count):

        @pl.when(r == k)
        def _():
            outs[k][...] = total.astype(outs[k].dtype)


def combine(dest_col, back, base, column, count):
    slots, width = back.shape
    rows = dest_col.shape[0] // count
    fixed = lambda r: (0, 0)
    return pl.pallas_call(
        partial(combine_kernel, count),
        grid=(count,),
        in_specs=[
            pl.BlockSpec((rows, 1), lambda r: (r, 0)),
            pl.BlockSpec((slots, width), fixed),
            pl.BlockSpec((rows, width), lambda r: (r, column)),
        ],
        out_specs=[pl.BlockSpec((rows, width), fixed)] * count,
        out_shape=[
            jax.ShapeDtypeStruct((rows, width), F32 if k == 0 else BF) for k in range(count)
        ],
        compiler_params=pltpu.CompilerParams(vmem_limit_bytes=40 * 2**20),
        cost_estimate=pl.CostEstimate(
            flops=2 * slots * rows * count * width,
            bytes_accessed=2 * slots * width + 7 * rows * count * width,
            transcendentals=0,
        ),
        name="combine",
    )(dest_col, back, base)


def mm_t(a, b):
    return lax.dot_general(a, b, (((1,), (1,)), ((), ())), preferred_element_type=F32)


def gelu_both(u):
    c = 0.7978845608028654
    square = u * u
    t = jnp.tanh(u * (c + (c * 0.044715) * square))
    half = 0.5 + 0.5 * t
    slope = half + (0.5 * u) * (1.0 - t * t) * (c + (3.0 * c * 0.044715) * square)
    return u * half, slope


def high_low(value):
    high = value.astype(BF)
    return high, (value - high.astype(F32)).astype(BF)


def two_coefs(logits, lane, experts):
    inside = (lane >= experts) & (lane < experts + 2)
    top = jnp.max(jnp.where(inside, logits, HIDE), axis=1, keepdims=True)
    e = jnp.where(inside, jnp.exp(logits - top), 0.0)
    e = e / jnp.sum(e, axis=1, keepdims=True)
    first = jnp.sum(jnp.where(lane == experts, e, 0.0), axis=1, keepdims=True)
    second = jnp.sum(jnp.where(lane == experts + 1, e, 0.0), axis=1, keepdims=True)
    return first, second


def small_back(d_small, parts, w_small_ref, small_ref, i):
    high, low = high_low(d_small)
    w_small = w_small_ref[...]
    high_t, low_t = high_low(d_small.T)

    @pl.when(i == 0)
    def _():
        small_ref[...] = jnp.zeros(small_ref.shape, F32)

    at = 0
    for part in parts:
        width = part.shape[1]
        small_ref[:, at : at + width] += mm(high_t, part) + mm(low_t, part)
        at += width
    return mm_t(high, w_small) + mm_t(low, w_small)


def expert_kernel(count, experts, place_ref, *refs):
    parts = [ref[...] for ref in refs[:count]]
    dy_ref, up_ref, down_ref, w_small_ref = refs[count : count + 4]
    outs = refs[count + 4 :]
    rows_ref, hid_ref, dy_out_ref, deu_ref, y_ref, small_ref = outs[:6]
    d_rows_refs = outs[6:]
    i = pl.program_id(0)
    step = parts[0].shape[1]
    up, logits, at = 0.0, 0.0, 0
    for part in parts:
        rows_ref[:, at : at + step] = part
        up = up + mm(part, up_ref[at : at + step, :])
        logits = logits + mm(part, w_small_ref[at : at + step, :])
        at += step
    lane = lax.broadcasted_iota(jnp.int32, logits.shape, 1)
    routed = lane < experts
    top = jnp.max(jnp.where(routed, logits, HIDE), axis=1, keepdims=True)
    probs = jnp.where(routed, jnp.exp(logits - top), 0.0)
    probs = probs / jnp.sum(probs, axis=1, keepdims=True)
    own = jnp.where(lane == place_ref[0], 1.0, 0.0)
    gate = jnp.sum(probs * own, axis=1, keepdims=True)
    first, second = two_coefs(logits, lane, experts)
    weight = second * gate
    dy = dy_ref[...].astype(F32)
    d_y = (weight * dy).astype(BF)
    dy_out_ref[...] = d_y
    d_hidden = mm_t(d_y, down_ref[...])
    hidden, slope = gelu_both(up)
    hidden = hidden.astype(BF)
    hid_ref[...] = hidden
    d_up = (d_hidden * slope).astype(BF)
    deu_ref[...] = d_up
    y = mm(hidden, down_ref[...])
    y_ref[...] = (weight * y).astype(BF)
    along = gate * jnp.sum(dy * y, axis=1, keepdims=True)
    mixed = first * second * along
    d_small = (second * along) * (own - probs)
    d_small = jnp.where(routed, d_small, 0.0)
    d_small = d_small + jnp.where(lane == experts + 1, mixed, 0.0)
    d_small = d_small - jnp.where(lane == experts, mixed, 0.0)
    d_rows = mm_t(d_up, up_ref[...]) + small_back(d_small, parts, w_small_ref, small_ref, i)
    for c in range(count):
        d_rows_refs[c][...] = d_rows[:, c * step : (c + 1) * step].astype(BF)


def expert_rows(place, parts, dy, w_up, w_down, w_small, experts):
    count, (rows, step) = len(parts), parts[0].shape
    width, hid = w_up.shape
    lanes = w_small.shape[1]
    blk = min(256, rows)
    fixed = lambda i, n: (0, 0)
    moving = lambda i, n: (i, 0)
    row_out = pl.BlockSpec((blk, width), moving)
    hid_out = pl.BlockSpec((blk, hid), moving)
    row_shape = jax.ShapeDtypeStruct((rows, width), BF)
    hid_shape = jax.ShapeDtypeStruct((rows, hid), BF)
    return pl.pallas_call(
        partial(expert_kernel, count, experts),
        grid_spec=pltpu.PrefetchScalarGridSpec(
            num_scalar_prefetch=1,
            grid=(rows // blk,),
            in_specs=[pl.BlockSpec((blk, step), moving)] * count
            + [
                pl.BlockSpec((blk, width), moving),
                pl.BlockSpec((width, hid), fixed),
                pl.BlockSpec((hid, width), fixed),
                pl.BlockSpec((width, lanes), fixed),
            ],
            out_specs=[row_out, hid_out, row_out, hid_out, row_out]
            + [pl.BlockSpec((lanes, width), fixed)]
            + [pl.BlockSpec((blk, step), moving)] * count,
        ),
        out_shape=[row_shape, hid_shape, row_shape, hid_shape, row_shape]
        + [jax.ShapeDtypeStruct((lanes, width), F32)]
        + [jax.ShapeDtypeStruct((rows, step), BF)] * count,
        compiler_params=pltpu.CompilerParams(vmem_limit_bytes=48 * 2**20),
        cost_estimate=pl.CostEstimate(
            flops=8 * rows * width * hid,
            bytes_accessed=14 * rows * width + 4 * width * hid,
            transcendentals=rows * hid,
        ),
        name="expert_rows",
    )(place, *parts, dy, w_up, w_down, w_small)


def dense_kernel(count, experts, *refs):
    parts = [ref[...] for ref in refs[:count]]
    dy_ref, in_ref, out_ref, w_small_ref = refs[count : count + 4]
    rows_ref, hid_ref, grad_ref, d_up_ref, mix_ref, db_ref, small_ref = refs[count + 4 :]
    i = pl.program_id(0)
    step = parts[0].shape[1]
    up, logits, at = 0.0, 0.0, 0
    for part in parts:
        rows_ref[:, at : at + step] = part
        up = up + mm(part, in_ref[at : at + step, :])
        logits = logits + mm(part, w_small_ref[at : at + step, :])
        at += step
    lane = lax.broadcasted_iota(jnp.int32, logits.shape, 1)
    first, second = two_coefs(logits, lane, experts)
    dy = dy_ref[...].astype(F32)
    grad = (first * dy).astype(BF)
    grad_ref[...] = grad
    d_hidden = mm_t(grad, out_ref[...])
    hidden, slope = gelu_both(up)
    hidden = hidden.astype(BF)
    hid_ref[...] = hidden
    d_up = (d_hidden * slope).astype(BF)
    d_up_ref[...] = d_up
    dense = mm(hidden, out_ref[...])
    mix_ref[...] = first * dense
    mixed = first * second * jnp.sum(dy * dense, axis=1, keepdims=True)
    d_small = jnp.where(lane == experts, mixed, 0.0) - jnp.where(lane == experts + 1, mixed, 0.0)
    db_ref[...] = mm_t(d_up, in_ref[...]) + small_back(d_small, parts, w_small_ref, small_ref, i)


def dense_rows(parts, dy, w_in, w_out, w_small, experts):
    count, (rows, step) = len(parts), parts[0].shape
    width, hid = w_in.shape
    lanes = w_small.shape[1]
    blk = min(256, rows)
    fixed = lambda i: (0, 0)
    moving = lambda i: (i, 0)
    row_out = pl.BlockSpec((blk, width), moving)
    hid_out = pl.BlockSpec((blk, hid), moving)
    return pl.pallas_call(
        partial(dense_kernel, count, experts),
        grid=(rows // blk,),
        in_specs=[pl.BlockSpec((blk, step), moving)] * count
        + [
            row_out,
            pl.BlockSpec((width, hid), fixed),
            pl.BlockSpec((hid, width), fixed),
            pl.BlockSpec((width, lanes), fixed),
        ],
        out_specs=[row_out, hid_out, row_out, hid_out, row_out, row_out]
        + [pl.BlockSpec((lanes, width), fixed)],
        out_shape=[
            jax.ShapeDtypeStruct((rows, width), BF),
            jax.ShapeDtypeStruct((rows, hid), BF),
            jax.ShapeDtypeStruct((rows, width), BF),
            jax.ShapeDtypeStruct((rows, hid), BF),
            jax.ShapeDtypeStruct((rows, width), F32),
            jax.ShapeDtypeStruct((rows, width), F32),
            jax.ShapeDtypeStruct((lanes, width), F32),
        ],
        compiler_params=pltpu.CompilerParams(vmem_limit_bytes=48 * 2**20),
        cost_estimate=pl.CostEstimate(
            flops=8 * rows * width * hid,
            bytes_accessed=18 * rows * width + 4 * width * hid,
            transcendentals=rows * hid,
        ),
        name="dense_rows",
    )(*parts, dy, w_in, w_out, w_small)


def project_kernel(count, mine_ref, grad_ref, w_ref, *outs):
    r = pl.program_id(0)
    total = mm(grad_ref[...].astype(F32).T.astype(BF), w_ref[...])
    for k in range(count):

        @pl.when(r == k)
        def _():
            outs[k][...] = total.astype(outs[k].dtype)


def project_back(mine, grads, w_t, count, part, parts):
    features, rows = grads.shape
    width = w_t.shape[1]
    blk = rows // (count * parts)
    fixed = lambda r, n: (0, 0)
    return pl.pallas_call(
        partial(project_kernel, count),
        grid_spec=pltpu.PrefetchScalarGridSpec(
            num_scalar_prefetch=1,
            grid=(count,),
            in_specs=[
                pl.BlockSpec((features, blk), lambda r, n: (0, ((n[0] + r) % count) * parts + part)),
                pl.BlockSpec((features, width), fixed),
            ],
            out_specs=[pl.BlockSpec((blk, width), fixed)] * count,
        ),
        out_shape=[
            jax.ShapeDtypeStruct((blk, width), F32 if k == 0 else BF) for k in range(count)
        ],
        compiler_params=pltpu.CompilerParams(vmem_limit_bytes=32 * 2**20),
        cost_estimate=pl.CostEstimate(
            flops=2 * features * blk * count * width,
            bytes_accessed=2 * features * (blk * count + width) + 3 * blk * count * width,
            transcendentals=0,
        ),
        name="project_back",
    )(mine, grads, w_t)


def rotate(value, steps):
    count = lax.axis_size("mp")
    return lax.ppermute(value, "mp", [(s, (s + steps) % count) for s in range(count)])


def gather_pieces(own):
    return [own] + [rotate(own, -r) for r in range(1, lax.axis_size("mp"))]


def scatter_sum(quarters):
    total = quarters[0]
    for r in range(1, len(quarters)):
        total = total + rotate(quarters[r], r).astype(F32)
    return total


def place_pieces(pieces, mine, rows):
    quarter = rows // len(pieces)
    out = jnp.zeros((rows, pieces[0].shape[1]), pieces[0].dtype)
    for r, piece in enumerate(pieces):
        at = ((mine + r) % len(pieces)) * quarter
        out = lax.dynamic_update_slice_in_dim(out, piece, at, 0)
    return out


def roll_rows(value, start):
    twice = jnp.concatenate([value, value], axis=0)
    return lax.dynamic_slice_in_dim(twice, start, value.shape[0], 0)


def sum_shares(value):
    count, width = value.shape
    dps = lax.axis_size("dp")
    parts = value.reshape(count, dps, width // dps).transpose(1, 0, 2)
    own = jnp.sum(lax.all_to_all(parts, "dp", 0, 0, tiled=True), axis=0)
    total = own
    for r in range(1, lax.axis_size("mp")):
        total = total + rotate(own, r)
    return total


def body(
    tokens,
    cotangent,
    ln_gains,
    ln_biases,
    w_qkv,
    w_o,
    w_in,
    w_out,
    w_router,
    w_coef,
    w_up,
    w_down,
    routes,
    long_group,
):
    rows, width = tokens.shape
    mps, dps = lax.axis_size("mp"), lax.axis_size("dp")
    mine, position = lax.axis_index("mp"), lax.axis_index("dp")
    quarter = rows // mps
    start = mine * quarter
    heads_loc = w_qkv.shape[2] // HD
    experts = w_router.shape[1]
    capacity = max(2, 2 * rows // experts)
    slots = experts * capacity
    groups = [[g * GROUP + t for t in range(GROUP)] for g in range(dps // GROUP)]
    first_len = lax.dynamic_slice_in_dim(long_group, position // GROUP, 1, 0)
    mine_s, position_s = mine.reshape(1), position.reshape(1)
    step = width // CHUNKS
    barrier = lax.optimization_barrier

    def group_swap(value):
        return lax.all_to_all(value, "dp", 0, 0, axis_index_groups=groups, tiled=True)

    def expert_swap(value):
        wide = value.reshape(experts, capacity, value.shape[1])
        return lax.all_to_all(wide, "dp", 0, 0, tiled=True).reshape(value.shape)

    w_o_all = lax.all_gather(w_o, "mp", axis=0, tiled=True)

    x = tokens.astype(F32)
    a_r = layer_norm(x, ln_gains[0], ln_biases[0]).astype(BF)
    w_heads = w_qkv.reshape(width, 3, heads_loc, HD).transpose(2, 1, 3, 0)
    w_heads = w_heads.reshape(heads_loc * 3 * HD, width)
    qkv = mm_t(w_heads, a_r).astype(BF).reshape(heads_loc, 3 * HD, rows)
    qkv = group_swap(qkv)

    route = roll_rows(routes, start)[:, 0]
    picked = (route[:, None] == jnp.arange(experts, dtype=jnp.int32)[None, :]).astype(jnp.int32)
    slot = jnp.sum((jnp.cumsum(picked, axis=0) - picked) * picked, axis=1)
    dest = route * capacity + slot
    dest_row, dest_col = dest[None, :], dest[:, None]
    dy_b = roll_rows(cotangent, start)
    send_dy = dispatch(dest_row, [dy_b], slots)[0]
    qkv, send_dy = barrier((qkv, send_dy))
    got_dy = expert_swap(send_dy)

    o_t, lse = attend(first_len, qkv)
    o_heads = group_swap(o_t).reshape(heads_loc * HD, rows)
    o_q = lax.all_to_all(o_heads, "mp", 1, 0, tiled=True)
    x_q = lax.dynamic_slice_in_dim(tokens, start, quarter, 0).astype(F32)
    h = x_q + ein("ft,fd->td", o_q, w_o_all)
    b, norm_two = jax.vjp(layer_norm, h, ln_gains[1], ln_biases[1])
    b_q, got_dy = barrier((b.astype(BF), got_dy))

    b_parts, sends = [], []
    for c in range(CHUNKS):
        send, joined = dispatch(dest_row, gather_pieces(b_q[:, c * step : (c + 1) * step]), slots)
        sends.append(send)
        b_parts.append(joined)
    got_parts = [expert_swap(send) for send in sends]
    b_parts = list(barrier(tuple(b_parts) + tuple(sends))[:CHUNKS])
    lanes = -(-(experts + 2) // 128) * 128
    w_small = jnp.concatenate(
        [w_router, w_coef, jnp.zeros((width, lanes - experts - 2), BF)], axis=1
    )
    b_r, hidden, dense_grad, d_up, mix_base, db_base, small_t = dense_rows(
        b_parts, dy_b, w_in, w_out, w_small, experts
    )

    def shared(value, dim):
        return lax.psum_scatter(value.astype(BF), "dp", scatter_dimension=dim, tiled=True)

    grad_out = shared(ein("tf,td->fd", hidden, dense_grad), 1).astype(F32)
    grad_in = shared(ein("td,tf->df", b_r, d_up), 0).astype(F32)

    got, hidden_e, d_y, d_eu, back_y, small_e, *d_rows = expert_rows(
        position_s, got_parts, got_dy, w_up[0], w_down[0], w_small, experts
    )

    backs = [expert_swap(part) for part in d_rows]
    back_y = barrier((back_y, backs[-1]))[0]
    back_tok = expert_swap(back_y)
    db = []
    for c in range(CHUNKS):
        db.append(scatter_sum(combine(dest_col, backs[c], db_base, c, mps)))
    db = jnp.concatenate(db, axis=1)
    dh_norm, d_gain2, d_bias2 = norm_two(db)
    dh = dy_b[:quarter].astype(F32) + dh_norm
    dh_r = dh.astype(BF)
    do_q = mm_t(w_o_all, dh_r).astype(BF)
    do_heads = lax.all_to_all(do_q, "mp", 0, 1, tiled=True)
    do_t = group_swap(do_heads.reshape(heads_loc, HD, rows))
    grad_o = shared(ein("ft,td->fd", o_q, dh_r), 1)
    small = small_e[: experts + 2] + small_t[: experts + 2]
    small = sum_shares(jnp.concatenate([small, d_gain2[None], d_bias2[None]], axis=0))

    mix = combine(dest_col, back_tok, mix_base, 0, mps)
    do_t, *mix = barrier((do_t, *mix))
    d_qkv_t = attend_back(first_len, qkv, do_t, o_t, lse)
    out_q = (h + scatter_sum(mix)).astype(BF)
    output = place_pieces(gather_pieces(out_q), mine, rows)

    d_qkv_t, hidden_e, d_y, d_eu, got = barrier((d_qkv_t, hidden_e, d_y, d_eu, got))
    grad_down = ein("rf,rd->fd", hidden_e, d_y)[None]
    grad_up = ein("rd,rf->df", got, d_eu)[None]

    d_heads = group_swap(d_qkv_t).reshape(heads_loc * 3 * HD, rows)
    d_a = [project_back(mine_s, d_heads, w_heads, mps, part, HALVES) for part in range(HALVES)]
    grad_qkv = ein("td,ft->df", a_r, d_heads)
    grad_qkv = shared(grad_qkv, 0).astype(F32)
    grad_qkv = grad_qkv.reshape(width // dps, heads_loc, 3, HD).transpose(0, 2, 1, 3)
    grad_qkv = grad_qkv.reshape(width // dps, 3, heads_loc * HD)
    grad_o = lax.psum_scatter(grad_o, "mp", scatter_dimension=0, tiled=True).astype(F32)
    half = quarter // HALVES
    sums, grad_pieces = 0.0, []
    for part in range(HALVES):
        cut = slice(part * half, (part + 1) * half)
        _, norm_one = jax.vjp(layer_norm, x_q[cut], ln_gains[0], ln_biases[0])
        dx_norm, d_gain1, d_bias1 = norm_one(scatter_sum(d_a[part]))
        sums = sums + jnp.stack([d_gain1, d_bias1])
        grad_pieces.append(gather_pieces((dh[cut] + dx_norm).astype(BF)))
    grad_tokens = jnp.zeros((rows, width), BF)
    for part in range(HALVES):
        for r in range(mps):
            at = ((mine + r) % mps) * quarter + part * half
            grad_tokens = lax.dynamic_update_slice_in_dim(grad_tokens, grad_pieces[part][r], at, 0)
    sums = sum_shares(sums)
    small_out = small[: experts + 2].T
    return (
        output,
        grad_tokens,
        jnp.stack([sums[0], small[experts + 2]]),
        jnp.stack([sums[1], small[experts + 3]]),
        grad_qkv,
        grad_o,
        grad_in,
        grad_out,
        small_out[:, :experts],
        small_out[:, experts:],
        grad_up,
        grad_down,
    )


def solution(mesh):
    in_specs = (
        P("dp", None),
        P("dp", None),
        P(),
        P(),
        P(None, None, "mp"),
        P("mp", None),
        P(None, "mp"),
        P("mp", None),
        P(),
        P(),
        P("dp", None, "mp"),
        P("dp", "mp", None),
        P("dp", None),
        P(),
    )
    out_specs = (
        P("dp", None),
        P("dp", None),
        P(None, "dp"),
        P(None, "dp"),
        P("dp", None, "mp"),
        P("mp", "dp"),
        P("dp", "mp"),
        P("mp", "dp"),
        P("dp", None),
        P("dp", None),
        P("dp", None, "mp"),
        P("dp", "mp", None),
    )
    return jax.shard_map(body, mesh=mesh, in_specs=in_specs, out_specs=out_specs, check_vma=False)
```

```python
from functools import partial

import jax
import jax.numpy as jnp
from jax import lax
from jax.experimental import pallas as pl
from jax.experimental.pallas import tpu as pltpu
from jax.sharding import PartitionSpec as P

HD = 64
GROUP = 4
CHUNKS = 2
HALVES = 2
EPS = 1e-05
LOG2E = 1.4426950408889634
SCALE2 = 0.125 * LOG2E
HIDE = -1e30
BF = jnp.bfloat16
F32 = jnp.float32
LIGHT = pl.CostEstimate(flops=1 << 20, bytes_accessed=1 << 20, transcendentals=0)


def layer_norm(v, gain, bias):
    mean = jnp.mean(v, axis=-1, keepdims=True)
    centred = v - mean
    var = jnp.mean(centred * centred, axis=-1, keepdims=True)
    return centred * lax.rsqrt(var + EPS) * gain + bias


def mm(a, b):
    return jnp.dot(a, b, preferred_element_type=F32)


def ein(spec, a, b):
    return jnp.einsum(spec, a, b, preferred_element_type=F32)


def fill_keys(k_s, place, keys, first_len, blk):
    rows = place * blk + lax.broadcasted_iota(jnp.int32, (blk, 128), 0)
    lane = lax.broadcasted_iota(jnp.int32, (blk, 128), 1)
    wide = jnp.concatenate([keys.astype(F32).T, jnp.zeros((blk, 128 - HD), F32)], axis=1)
    wide = jnp.where((lane == HD) & (rows < first_len), HIDE, wide)
    k_s[pl.ds(place * blk, blk), :] = wide.astype(BF)


def wide_query(query, place, first_len, blk):
    cols = place * blk + lax.broadcasted_iota(jnp.int32, (128 - HD, blk), 1)
    sub = lax.broadcasted_iota(jnp.int32, (128 - HD, blk), 0)
    extra = jnp.where((sub == 0) & (cols >= first_len), 1.0, 0.0)
    return jnp.concatenate([query, extra.astype(BF)], axis=0)


def causal(blk):
    keys = lax.broadcasted_iota(jnp.int32, (blk, blk), 0)
    queries = lax.broadcasted_iota(jnp.int32, (blk, blk), 1)
    return keys <= queries


def attend_kernel(blk, per, len_ref, qkv_ref, o_ref, lse_ref, k_s):
    i = pl.program_id(0)
    first_len = len_ref[0]

    def part(which, j):
        return qkv_ref[j // per, HD * which : HD * (which + 1), pl.ds((j % per) * blk, blk)]

    fill_keys(k_s, i, part(1, i), first_len, blk)
    query = wide_query(part(0, i), i, first_len, blk)

    def scores(j):
        return mm(k_s[pl.ds(pl.multiple_of(j * blk, blk), blk), :], query)

    s = jnp.where(causal(blk), scores(i), HIDE)
    top = jnp.max(s, axis=0, keepdims=True)
    p = jnp.exp2((s - top) * SCALE2)
    total = jnp.sum(p, axis=0, keepdims=True)
    acc = mm(part(2, i), p.astype(BF))

    def step(j, carry):
        top, total, acc = carry
        s = scores(j)
        new = jnp.maximum(top, jnp.max(s, axis=0, keepdims=True))
        p = jnp.exp2((s - new) * SCALE2)
        keep = jnp.exp2((top - new) * SCALE2)
        total = total * keep + jnp.sum(p, axis=0, keepdims=True)
        acc = acc * keep + mm(part(2, j), p.astype(BF))
        return new, total, acc

    low = jnp.where(i * blk >= first_len, first_len // blk, 0)
    top, total, acc = lax.fori_loop(low, i, step, (top, total, acc))
    o_ref[0] = (acc / total).astype(BF)
    lse_ref[0] = top * SCALE2 + jnp.log2(total)


def attend(first_len, qkv):
    parts, _, rows = qkv.shape
    blk = min(512, rows)
    per = rows // blk
    count = parts * per
    return pl.pallas_call(
        partial(attend_kernel, blk, per),
        grid_spec=pltpu.PrefetchScalarGridSpec(
            num_scalar_prefetch=1,
            grid=(count,),
            in_specs=[pl.BlockSpec((parts, 3 * HD, rows), lambda i, n: (0, 0, 0))],
            out_specs=[
                pl.BlockSpec((1, HD, blk), lambda i, n: (i // per, 0, i % per)),
                pl.BlockSpec((1, 1, blk), lambda i, n: (i, 0, 0)),
            ],
            scratch_shapes=[pltpu.VMEM((parts * rows, 128), BF)],
        ),
        out_shape=[
            jax.ShapeDtypeStruct((parts, HD, rows), BF),
            jax.ShapeDtypeStruct((count, 1, blk), F32),
        ],
        compiler_params=pltpu.CompilerParams(vmem_limit_bytes=40 * 2**20),
        cost_estimate=LIGHT,
        name="attend",
    )(first_len, qkv)


def back_kernel(blk, per, first, count, len_ref, qkv_ref, do_ref, o_ref, lse_ref, *refs):
    if first:
        _, dq_in_ref = refs[:2]
        refs = refs[2:]
    out_ref, dq_ref, k_s, v_s, wide_s, both_s, delta_s, acc_s = refs
    at_first = pl.program_id(0) == 0
    j = first + pl.program_id(0)
    first_len = len_ref[0]

    def part(which, i):
        return qkv_ref[i // per, HD * which : HD * (which + 1), pl.ds((i % per) * blk, blk)]

    def dout(i):
        return do_ref[i // per, :, pl.ds((i % per) * blk, blk)]

    @pl.when(at_first)
    def _():
        dq_ref[...] = dq_in_ref[...] if first else jnp.zeros(dq_ref.shape, F32)

        def prepare(i, carry):
            at = pl.ds(pl.multiple_of(i * blk, blk), blk)
            fill_keys(k_s, i, part(1, i), first_len, blk)
            wide_s[:, at] = wide_query(part(0, i), i, first_len, blk)
            zero = jnp.zeros((blk, HD), F32)
            grad = dout(i).astype(F32)
            v_s[at, :] = jnp.concatenate([part(2, i).astype(F32).T, zero], axis=1).astype(BF)
            both_s[0, at, :] = jnp.concatenate([grad.T, zero], axis=1).astype(BF)
            both_s[1, at, :] = jnp.concatenate([zero, part(0, i).astype(F32).T], axis=1).astype(BF)
            held = o_ref[i // per, :, pl.ds((i % per) * blk, blk)].astype(F32)
            delta_s[i] = jnp.sum(held * grad, axis=0, keepdims=True)
            return carry

        lax.fori_loop(first, count, prepare, 0)

    here = pl.ds(pl.multiple_of(j * blk, blk), blk)
    keys_t = part(1, j)
    values = v_s[here, 0:HD]

    def pair(i, diagonal):
        at = pl.ds(pl.multiple_of(i * blk, blk), blk)
        s = mm(k_s[here, :], wide_s[:, at])
        p = jnp.exp2(s * SCALE2 - lse_ref[i])
        if diagonal:
            p = jnp.where(causal(blk), p, 0.0)
        dp = mm(values, dout(i))
        ds = (p * (dp - delta_s[i])).astype(BF)
        dq_ref[:, at] += mm(keys_t, ds)
        return mm(p.astype(BF), both_s[0, at, :]) + mm(ds, both_s[1, at, :])

    acc_s[...] = pair(j, True)

    def step(i, carry):
        acc_s[...] += pair(i, False)
        return carry

    high = jnp.where((j + 1) * blk <= first_len, (first_len + blk - 1) // blk, count)
    lax.fori_loop(j + 1, high, step, 0)
    both = acc_s[...].T
    out_ref[0, 0:HD, :] = (dq_ref[:, here] * 0.125).astype(BF)
    out_ref[0, HD : 2 * HD, :] = (both[HD:, :] * 0.125).astype(BF)
    out_ref[0, 2 * HD :, :] = both[:HD, :].astype(BF)


def attend_back(first_len, qkv, do, o, lse, before, first, last):
    parts, _, rows = qkv.shape
    blk = min(512, rows)
    per = rows // blk
    count = parts * per
    whole = lambda j, n: (0, 0, 0)
    flat = lambda j, n: (0, 0)
    dq_spec = pl.BlockSpec((HD, parts * rows), flat)
    return pl.pallas_call(
        partial(back_kernel, blk, per, first * per, count),
        grid_spec=pltpu.PrefetchScalarGridSpec(
            num_scalar_prefetch=1,
            grid=((last - first) * per,),
            in_specs=[
                pl.BlockSpec((parts, 3 * HD, rows), whole),
                pl.BlockSpec((parts, HD, rows), whole),
                pl.BlockSpec((parts, HD, rows), whole),
                pl.BlockSpec((count, 1, blk), whole),
            ]
            + ([pl.BlockSpec(memory_space=pl.ANY), dq_spec] if first else []),
            out_specs=[
                pl.BlockSpec((1, 3 * HD, blk), lambda j, n: (first + j // per, 0, j % per)),
                dq_spec,
            ],
            scratch_shapes=[
                pltpu.VMEM((parts * rows, 128), BF),
                pltpu.VMEM((parts * rows, 128), BF),
                pltpu.VMEM((128, parts * rows), BF),
                pltpu.VMEM((2, parts * rows, 128), BF),
                pltpu.VMEM((count, 1, blk), F32),
                pltpu.VMEM((blk, 128), F32),
            ],
        ),
        out_shape=[
            jax.ShapeDtypeStruct((parts, 3 * HD, rows), BF),
            jax.ShapeDtypeStruct((HD, parts * rows), F32),
        ],
        input_output_aliases={5: 0} if first else {},
        compiler_params=pltpu.CompilerParams(vmem_limit_bytes=48 * 2**20),
        cost_estimate=LIGHT,
        name="attend_back",
    )(first_len, qkv, do, o, lse, *(before if first else ()))


def in_order(mine, own, right, left, right_two, left_two):
    one = jnp.where(mine == 3, left_two, left)
    two = jnp.where(mine < 2, left_two, right_two)
    three = jnp.where(mine == 0, right_two, right)
    return own, one, two, three


def dispatch_kernel(count, mine_ref, dest_ref, *refs):
    pieces, out_ref = [ref[...] for ref in refs[:count]], refs[count]
    blk, rows = out_ref.shape[0], dest_ref.shape[1]
    i = pl.program_id(0)
    slot = i * blk + lax.broadcasted_iota(jnp.int32, (blk, rows), 0)
    spread = jnp.where(slot == dest_ref[...], 1.0, 0.0).astype(BF)
    if count > 1:
        pieces = in_order(mine_ref[0], *pieces)
        joined_ref = refs[count + 1]
    total, at = 0.0, 0
    for piece in pieces:
        each = piece.shape[0]
        total = total + mm(spread[:, at : at + each], piece)
        if count > 1:

            @pl.when(i == 0)
            def _():
                joined_ref[at : at + each, :] = piece

        at += each
    out_ref[...] = total.astype(BF)


def dispatch(mine, dest_row, pieces, slots):
    count, (each, width) = len(pieces), pieces[0].shape
    rows = dest_row.shape[1]
    blk = min(256, slots)
    fixed = lambda i, n: (0, 0)
    out_specs = [pl.BlockSpec((blk, width), lambda i, n: (i, 0))]
    out_shape = [jax.ShapeDtypeStruct((slots, width), BF)]
    if count > 1:
        out_specs.append(pl.BlockSpec((rows, width), fixed))
        out_shape.append(jax.ShapeDtypeStruct((rows, width), BF))
    return pl.pallas_call(
        partial(dispatch_kernel, count),
        grid_spec=pltpu.PrefetchScalarGridSpec(
            num_scalar_prefetch=1,
            grid=(slots // blk,),
            in_specs=[pl.BlockSpec((1, rows), fixed)]
            + [pl.BlockSpec((each, width), fixed)] * count,
            out_specs=out_specs,
        ),
        out_shape=out_shape,
        compiler_params=pltpu.CompilerParams(vmem_limit_bytes=32 * 2**20),
        cost_estimate=LIGHT,
        name="dispatch",
    )(mine, dest_row, *pieces)


def join_kernel(count, mine_ref, *refs):
    r, part = pl.program_id(0), pl.program_id(1)
    out_ref = refs[-1]
    for k in range(count):

        @pl.when(part == k)
        def _():
            pieces = in_order(mine_ref[0], *[ref[...] for ref in refs[5 * k : 5 * k + 5]])
            for place in range(4):

                @pl.when(r == place)
                def _():
                    out_ref[...] = pieces[place]


def join(mine, halves):
    count, (each, width) = len(halves), halves[0][0].shape
    fixed = lambda r, k, n: (0, 0)
    return pl.pallas_call(
        partial(join_kernel, count),
        grid_spec=pltpu.PrefetchScalarGridSpec(
            num_scalar_prefetch=1,
            grid=(4, count),
            in_specs=[pl.BlockSpec((each, width), fixed)] * (5 * count),
            out_specs=pl.BlockSpec((each, width), lambda r, k, n: (((n[0] + r) % 4) * count + k, 0)),
        ),
        out_shape=jax.ShapeDtypeStruct((4 * count * each, width), BF),
        compiler_params=pltpu.CompilerParams(vmem_limit_bytes=32 * 2**20),
        cost_estimate=LIGHT,
        name="join",
    )(mine, *[piece for half in halves for piece in half])


def write_shares(r, mine, total, own_ref, one_ref, three_ref, far_left_ref, far_right_ref):
    value = total.astype(BF)

    @pl.when(r == 0)
    def _():
        own_ref[...] = total

    @pl.when(r == 1)
    def _():
        one_ref[...] = value

    @pl.when(r == 3)
    def _():
        three_ref[...] = value

    @pl.when(r == jnp.where(mine == 0, 3, 2))
    def _():
        far_left_ref[...] = value

    @pl.when(r == jnp.where(mine == 3, 1, 2))
    def _():
        far_right_ref[...] = value


def share_shapes(rows, width):
    sent = jax.ShapeDtypeStruct((rows, width), BF)
    return [jax.ShapeDtypeStruct((rows, width), F32)] + [sent] * 4


def combine_kernel(mine_ref, dest_ref, back_ref, base_ref, *outs):
    rows, slots = dest_ref.shape[0], back_ref.shape[0]
    lane = lax.broadcasted_iota(jnp.int32, (rows, slots), 1)
    pick = jnp.where(lane == dest_ref[...], 1.0, 0.0).astype(BF)
    total = mm(pick, back_ref[...]) + base_ref[...]
    write_shares(pl.program_id(0), mine_ref[0], total, *outs)


def combine(mine, dest_col, back, base, column):
    slots, width = back.shape
    rows = dest_col.shape[0] // 4
    fixed = lambda r, n: (0, 0)
    return pl.pallas_call(
        combine_kernel,
        grid_spec=pltpu.PrefetchScalarGridSpec(
            num_scalar_prefetch=1,
            grid=(4,),
            in_specs=[
                pl.BlockSpec((rows, 1), lambda r, n: (r, 0)),
                pl.BlockSpec((slots, width), fixed),
                pl.BlockSpec((rows, width), lambda r, n: (r, column)),
            ],
            out_specs=[pl.BlockSpec((rows, width), fixed)] * 5,
        ),
        out_shape=share_shapes(rows, width),
        compiler_params=pltpu.CompilerParams(vmem_limit_bytes=40 * 2**20),
        cost_estimate=LIGHT,
        name="combine",
    )(mine, dest_col, back, base)


def mm_t(a, b):
    return lax.dot_general(a, b, (((1,), (1,)), ((), ())), preferred_element_type=F32)


def gelu_both(u):
    c = 0.7978845608028654
    square = u * u
    t = jnp.tanh(u * (c + (c * 0.044715) * square))
    half = 0.5 + 0.5 * t
    slope = half + (0.5 * u) * (1.0 - t * t) * (c + (3.0 * c * 0.044715) * square)
    return u * half, slope


def high_low(value):
    high = value.astype(BF)
    return high, (value - high.astype(F32)).astype(BF)


def two_coefs(logits, lane, experts):
    inside = (lane >= experts) & (lane < experts + 2)
    top = jnp.max(jnp.where(inside, logits, HIDE), axis=1, keepdims=True)
    e = jnp.where(inside, jnp.exp(logits - top), 0.0)
    e = e / jnp.sum(e, axis=1, keepdims=True)
    first = jnp.sum(jnp.where(lane == experts, e, 0.0), axis=1, keepdims=True)
    second = jnp.sum(jnp.where(lane == experts + 1, e, 0.0), axis=1, keepdims=True)
    return first, second


def small_back(d_small, parts, w_small_ref, small_ref, i):
    high, low = high_low(d_small)
    w_small = w_small_ref[...]
    high_t, low_t = high_low(d_small.T)

    @pl.when(i == 0)
    def _():
        small_ref[...] = jnp.zeros(small_ref.shape, F32)

    at = 0
    for part in parts:
        width = part.shape[1]
        small_ref[:, at : at + width] += mm(high_t, part) + mm(low_t, part)
        at += width
    return mm_t(high, w_small) + mm_t(low, w_small)


def expert_kernel(count, experts, place_ref, *refs):
    parts = [ref[...] for ref in refs[:count]]
    dy_ref, up_ref, down_ref, w_small_ref = refs[count : count + 4]
    outs = refs[count + 4 :]
    rows_ref, hid_ref, dy_out_ref, deu_ref, y_ref, small_ref = outs[:6]
    d_rows_refs = outs[6:]
    i = pl.program_id(0)
    step = parts[0].shape[1]
    up, logits, at = 0.0, 0.0, 0
    for part in parts:
        rows_ref[:, at : at + step] = part
        up = up + mm(part, up_ref[at : at + step, :])
        logits = logits + mm(part, w_small_ref[at : at + step, :])
        at += step
    lane = lax.broadcasted_iota(jnp.int32, logits.shape, 1)
    routed = lane < experts
    top = jnp.max(jnp.where(routed, logits, HIDE), axis=1, keepdims=True)
    probs = jnp.where(routed, jnp.exp(logits - top), 0.0)
    probs = probs / jnp.sum(probs, axis=1, keepdims=True)
    own = jnp.where(lane == place_ref[0], 1.0, 0.0)
    gate = jnp.sum(probs * own, axis=1, keepdims=True)
    first, second = two_coefs(logits, lane, experts)
    weight = second * gate
    dy = dy_ref[...].astype(F32)
    d_y = (weight * dy).astype(BF)
    dy_out_ref[...] = d_y
    d_hidden = mm_t(d_y, down_ref[...])
    hidden, slope = gelu_both(up)
    hidden = hidden.astype(BF)
    hid_ref[...] = hidden
    d_up = (d_hidden * slope).astype(BF)
    deu_ref[...] = d_up
    y = mm(hidden, down_ref[...])
    y_ref[...] = (weight * y).astype(BF)
    along = gate * jnp.sum(dy * y, axis=1, keepdims=True)
    mixed = first * second * along
    d_small = (second * along) * (own - probs)
    d_small = jnp.where(routed, d_small, 0.0)
    d_small = d_small + jnp.where(lane == experts + 1, mixed, 0.0)
    d_small = d_small - jnp.where(lane == experts, mixed, 0.0)
    d_rows = mm_t(d_up, up_ref[...]) + small_back(d_small, parts, w_small_ref, small_ref, i)
    for c in range(count):
        d_rows_refs[c][...] = d_rows[:, c * step : (c + 1) * step].astype(BF)


def expert_rows(place, parts, dy, w_up, w_down, w_small, experts):
    count, (rows, step) = len(parts), parts[0].shape
    width, hid = w_up.shape
    lanes = w_small.shape[1]
    blk = min(256, rows)
    fixed = lambda i, n: (0, 0)
    moving = lambda i, n: (i, 0)
    row_out = pl.BlockSpec((blk, width), moving)
    hid_out = pl.BlockSpec((blk, hid), moving)
    row_shape = jax.ShapeDtypeStruct((rows, width), BF)
    hid_shape = jax.ShapeDtypeStruct((rows, hid), BF)
    return pl.pallas_call(
        partial(expert_kernel, count, experts),
        grid_spec=pltpu.PrefetchScalarGridSpec(
            num_scalar_prefetch=1,
            grid=(rows // blk,),
            in_specs=[pl.BlockSpec((blk, step), moving)] * count
            + [
                pl.BlockSpec((blk, width), moving),
                pl.BlockSpec((width, hid), fixed),
                pl.BlockSpec((hid, width), fixed),
                pl.BlockSpec((width, lanes), fixed),
            ],
            out_specs=[row_out, hid_out, row_out, hid_out, row_out]
            + [pl.BlockSpec((lanes, width), fixed)]
            + [pl.BlockSpec((blk, step), moving)] * count,
        ),
        out_shape=[row_shape, hid_shape, row_shape, hid_shape, row_shape]
        + [jax.ShapeDtypeStruct((lanes, width), F32)]
        + [jax.ShapeDtypeStruct((rows, step), BF)] * count,
        compiler_params=pltpu.CompilerParams(vmem_limit_bytes=48 * 2**20),
        cost_estimate=LIGHT,
        name="expert_rows",
    )(place, *parts, dy, w_up, w_down, w_small)


def dense_kernel(count, experts, *refs):
    parts = [ref[...] for ref in refs[:count]]
    dy_ref, in_ref, out_ref, w_small_ref = refs[count : count + 4]
    rows_ref, hid_ref, grad_ref, d_up_ref, mix_ref, db_ref, small_ref = refs[count + 4 :]
    i = pl.program_id(0)
    step = parts[0].shape[1]
    up, logits, at = 0.0, 0.0, 0
    for part in parts:
        rows_ref[:, at : at + step] = part
        up = up + mm(part, in_ref[at : at + step, :])
        logits = logits + mm(part, w_small_ref[at : at + step, :])
        at += step
    lane = lax.broadcasted_iota(jnp.int32, logits.shape, 1)
    first, second = two_coefs(logits, lane, experts)
    dy = dy_ref[...].astype(F32)
    grad = (first * dy).astype(BF)
    grad_ref[...] = grad
    d_hidden = mm_t(grad, out_ref[...])
    hidden, slope = gelu_both(up)
    hidden = hidden.astype(BF)
    hid_ref[...] = hidden
    d_up = (d_hidden * slope).astype(BF)
    d_up_ref[...] = d_up
    dense = mm(hidden, out_ref[...])
    mix_ref[...] = first * dense
    mixed = first * second * jnp.sum(dy * dense, axis=1, keepdims=True)
    d_small = jnp.where(lane == experts, mixed, 0.0) - jnp.where(lane == experts + 1, mixed, 0.0)
    db_ref[...] = mm_t(d_up, in_ref[...]) + small_back(d_small, parts, w_small_ref, small_ref, i)


def dense_rows(parts, dy, w_in, w_out, w_small, experts):
    count, (rows, step) = len(parts), parts[0].shape
    width, hid = w_in.shape
    lanes = w_small.shape[1]
    blk = min(256, rows)
    fixed = lambda i: (0, 0)
    moving = lambda i: (i, 0)
    row_out = pl.BlockSpec((blk, width), moving)
    hid_out = pl.BlockSpec((blk, hid), moving)
    return pl.pallas_call(
        partial(dense_kernel, count, experts),
        grid=(rows // blk,),
        in_specs=[pl.BlockSpec((blk, step), moving)] * count
        + [
            row_out,
            pl.BlockSpec((width, hid), fixed),
            pl.BlockSpec((hid, width), fixed),
            pl.BlockSpec((width, lanes), fixed),
        ],
        out_specs=[row_out, hid_out, row_out, hid_out, row_out, row_out]
        + [pl.BlockSpec((lanes, width), fixed)],
        out_shape=[
            jax.ShapeDtypeStruct((rows, width), BF),
            jax.ShapeDtypeStruct((rows, hid), BF),
            jax.ShapeDtypeStruct((rows, width), BF),
            jax.ShapeDtypeStruct((rows, hid), BF),
            jax.ShapeDtypeStruct((rows, width), F32),
            jax.ShapeDtypeStruct((rows, width), F32),
            jax.ShapeDtypeStruct((lanes, width), F32),
        ],
        compiler_params=pltpu.CompilerParams(vmem_limit_bytes=48 * 2**20),
        cost_estimate=LIGHT,
        name="dense_rows",
    )(*parts, dy, w_in, w_out, w_small)


def project_kernel(mine_ref, grad_ref, w_ref, *outs):
    total = mm(grad_ref[...].astype(F32).T.astype(BF), w_ref[...])
    write_shares(pl.program_id(0), mine_ref[0], total, *outs)


def project_back(mine, grads, w_t, part, parts):
    features, rows = grads.shape
    width = w_t.shape[1]
    blk = rows // (4 * parts)
    fixed = lambda r, n: (0, 0)
    return pl.pallas_call(
        project_kernel,
        grid_spec=pltpu.PrefetchScalarGridSpec(
            num_scalar_prefetch=1,
            grid=(4,),
            in_specs=[
                pl.BlockSpec((features, blk), lambda r, n: (0, ((n[0] + r) % 4) * parts + part)),
                pl.BlockSpec((features, width), fixed),
            ],
            out_specs=[pl.BlockSpec((blk, width), fixed)] * 5,
        ),
        out_shape=share_shapes(blk, width),
        compiler_params=pltpu.CompilerParams(vmem_limit_bytes=32 * 2**20),
        cost_estimate=LIGHT,
        name="project_back",
    )(mine, grads, w_t)


def rotate(value, steps):
    count = lax.axis_size("mp")
    return lax.ppermute(value, "mp", [(s, (s + steps) % count) for s in range(count)])


def hop(value, *pairs):
    return lax.ppermute(value, "mp", pairs)


def gather_near(own):
    return hop(own, (0, 1), (1, 2), (2, 3)), hop(own, (1, 0), (2, 1), (3, 2))


def gather_far(own, came):
    right, left = came
    mine = lax.axis_index("mp")
    right_two = hop(jnp.where(mine == 3, own, right), (1, 2), (2, 3), (3, 0))
    left_two = hop(jnp.where(mine == 0, own, left), (1, 0), (2, 1), (0, 3))
    return own, right, left, right_two, left_two


def gather_pieces(own):
    return gather_far(own, gather_near(own))


def scatter_far(shares):
    _, _, _, far_left, far_right = shares
    return hop(far_left, (2, 1), (3, 2), (0, 3)), hop(far_right, (0, 1), (1, 2), (3, 0))


def scatter_near(shares, came):
    own, one, three, _, _ = shares
    from_right, from_left = came
    mine = lax.axis_index("mp")
    middle = (mine == 1) | (mine == 2)

    def add(share, extra):
        return (share.astype(F32) + jnp.where(middle, extra, 0).astype(F32)).astype(BF)

    near_right = hop(add(three, from_right), (1, 0), (2, 1), (3, 2))
    near_left = hop(add(one, from_left), (0, 1), (1, 2), (2, 3))
    ends = jnp.where(mine == 0, from_left, jnp.where(mine == 3, from_right, 0))
    return own + near_right.astype(F32) + near_left.astype(F32) + ends.astype(F32)


def scatter_sum(shares):
    return scatter_near(shares, scatter_far(shares))


def roll_rows(value, start):
    twice = jnp.concatenate([value, value], axis=0)
    return lax.dynamic_slice_in_dim(twice, start, value.shape[0], 0)


def sum_shares(value):
    count, width = value.shape
    dps = lax.axis_size("dp")
    parts = value.reshape(count, dps, width // dps).transpose(1, 0, 2)
    own = jnp.sum(lax.all_to_all(parts, "dp", 0, 0, tiled=True), axis=0)
    total = own
    for r in range(1, lax.axis_size("mp")):
        total = total + rotate(own, r)
    return total


def body(
    tokens,
    cotangent,
    ln_gains,
    ln_biases,
    w_qkv,
    w_o,
    w_in,
    w_out,
    w_router,
    w_coef,
    w_up,
    w_down,
    routes,
    long_group,
):
    rows, width = tokens.shape
    mps, dps = lax.axis_size("mp"), lax.axis_size("dp")
    mine, position = lax.axis_index("mp"), lax.axis_index("dp")
    quarter = rows // mps
    start = mine * quarter
    heads_loc = w_qkv.shape[2] // HD
    experts = w_router.shape[1]
    capacity = max(2, 2 * rows // experts)
    slots = experts * capacity
    groups = [[g * GROUP + t for t in range(GROUP)] for g in range(dps // GROUP)]
    first_len = lax.dynamic_slice_in_dim(long_group, position // GROUP, 1, 0)
    mine_s, position_s = mine.reshape(1), position.reshape(1)
    step = width // CHUNKS
    barrier = lax.optimization_barrier

    def group_swap(value):
        return lax.all_to_all(value, "dp", 0, 0, axis_index_groups=groups, tiled=True)

    def expert_swap(value):
        wide = value.reshape(experts, capacity, value.shape[1])
        return lax.all_to_all(wide, "dp", 0, 0, tiled=True).reshape(value.shape)

    w_o_all = lax.all_gather(w_o, "mp", axis=0, tiled=True)

    x = tokens.astype(F32)
    a_r = layer_norm(x, ln_gains[0], ln_biases[0]).astype(BF)
    w_heads = w_qkv.reshape(width, 3, heads_loc, HD).transpose(2, 1, 3, 0)
    w_heads = w_heads.reshape(heads_loc * 3 * HD, width)
    qkv = mm_t(w_heads, a_r).astype(BF).reshape(heads_loc, 3 * HD, rows)
    qkv = group_swap(qkv)

    route = roll_rows(routes, start)[:, 0]
    picked = (route[:, None] == jnp.arange(experts, dtype=jnp.int32)[None, :]).astype(jnp.int32)
    slot = jnp.sum((jnp.cumsum(picked, axis=0) - picked) * picked, axis=1)
    dest = route * capacity + slot
    dest_row, dest_col = dest[None, :], dest[:, None]
    dy_b = roll_rows(cotangent, start)
    send_dy = dispatch(mine_s, dest_row, [dy_b], slots)[0]
    qkv, send_dy = barrier((qkv, send_dy))
    got_dy = expert_swap(send_dy)

    o_t, lse = attend(first_len, qkv)
    o_t, w_o_all = barrier((o_t, w_o_all))
    o_heads = group_swap(o_t).reshape(heads_loc * HD, rows)
    o_q = lax.all_to_all(o_heads, "mp", 1, 0, tiled=True)
    o_q, got_dy = barrier((o_q, got_dy))
    x_q = lax.dynamic_slice_in_dim(tokens, start, quarter, 0).astype(F32)
    h = x_q + ein("ft,fd->td", o_q, w_o_all)
    b, norm_two = jax.vjp(layer_norm, h, ln_gains[1], ln_biases[1])
    b_q = b.astype(BF)

    b_parts, sends = [], []
    for c in range(CHUNKS):
        send, joined = dispatch(mine_s, dest_row, gather_pieces(b_q[:, c * step : (c + 1) * step]), slots)
        sends.append(send)
        b_parts.append(joined)
    got_parts = [expert_swap(send) for send in sends]
    b_parts = list(barrier(tuple(b_parts) + tuple(sends))[:CHUNKS])
    lanes = -(-(experts + 2) // 128) * 128
    w_small = jnp.concatenate(
        [w_router, w_coef, jnp.zeros((width, lanes - experts - 2), BF)], axis=1
    )
    b_r, hidden, dense_grad, d_up, mix_base, db_base, small_t = dense_rows(
        b_parts, dy_b, w_in, w_out, w_small, experts
    )

    def share(value):
        return lax.psum_scatter(value, "dp", scatter_dimension=0, tiled=True)

    got, hidden_e, d_y, d_eu, back_y, small_e, *d_rows = expert_rows(
        position_s, got_parts, got_dy, w_up[0], w_down[0], w_small, experts
    )

    b_r, hidden, dense_grad, d_up, *d_rows = barrier((b_r, hidden, dense_grad, d_up, *d_rows))
    grad_in = ein("td,tf->df", b_r, d_up).astype(BF)
    grad_out = ein("td,tf->df", dense_grad, hidden).astype(BF)
    backs = [expert_swap(part) for part in d_rows]
    back_y = barrier((back_y, backs[-1]))[0]
    back_tok = expert_swap(back_y)
    db = []
    for c in range(CHUNKS):
        db.append(scatter_sum(combine(mine_s, dest_col, backs[c], db_base, c)))
    db = jnp.concatenate(db, axis=1)
    dh_norm, d_gain2, d_bias2 = norm_two(db)
    dh = dy_b[:quarter].astype(F32) + dh_norm
    dh_r = dh.astype(BF)
    do_q = mm_t(w_o_all, dh_r).astype(BF)
    do_heads = lax.all_to_all(do_q, "mp", 0, 1, tiled=True)
    do_t = group_swap(do_heads.reshape(heads_loc, HD, rows))
    grad_o = ein("td,ft->df", dh_r, o_q).astype(BF)
    small = small_e[: experts + 2] + small_t[: experts + 2]
    small = sum_shares(jnp.concatenate([small, d_gain2[None], d_bias2[None]], axis=0))

    mix = combine(mine_s, dest_col, back_tok, mix_base, 0)
    summed, do_t, *mix = barrier(
        (jnp.concatenate([grad_in, grad_out, grad_o], axis=1), do_t, *mix)
    )
    summed = share(summed)
    far = scatter_far(mix)
    before = attend_back(first_len, qkv, do_t, o_t, lse, None, 0, 1)
    *before, far_right, far_left = barrier((*before, *far))
    out_q = (h + scatter_near(mix, (far_right, far_left))).astype(BF)
    before = attend_back(first_len, qkv, do_t, o_t, lse, before, 1, 2)
    *before, out_q = barrier((*before, out_q))
    near = gather_near(out_q)
    d_qkv_t, _ = attend_back(first_len, qkv, do_t, o_t, lse, before, 2, GROUP)
    d_qkv_t, *near = barrier((d_qkv_t, *near))
    output = join(mine_s, [gather_far(out_q, near)])

    d_qkv_t, hidden_e, d_y, d_eu, got = barrier((d_qkv_t, hidden_e, d_y, d_eu, got))
    grad_down = ein("rf,rd->fd", hidden_e, d_y)[None]
    grad_up = ein("rd,rf->df", got, d_eu)[None]

    d_heads = group_swap(d_qkv_t).reshape(heads_loc * 3 * HD, rows)
    d_a = [project_back(mine_s, d_heads, w_heads, part, HALVES) for part in range(HALVES)]
    grad_qkv, summed = barrier((ein("td,ft->df", a_r, d_heads).astype(BF), summed))
    grad_qkv = share(grad_qkv).astype(F32)
    own = width // dps
    grad_qkv = grad_qkv.reshape(own, heads_loc, 3, HD).transpose(0, 2, 1, 3)
    grad_qkv = grad_qkv.reshape(own, 3, heads_loc * HD)
    hid = w_in.shape[1]
    grad_in = summed[:, :hid].astype(F32)
    grad_out = summed[:, hid : 2 * hid].astype(F32).T
    grad_o = summed[:, 2 * hid :].reshape(own, mps, width // mps).transpose(1, 0, 2)
    grad_o = jnp.sum(lax.all_to_all(grad_o, "mp", 0, 0, tiled=True).astype(F32), axis=0).T
    half = quarter // HALVES
    sums, grad_pieces = 0.0, []
    for part in range(HALVES):
        cut = slice(part * half, (part + 1) * half)
        _, norm_one = jax.vjp(layer_norm, x_q[cut], ln_gains[0], ln_biases[0])
        dx_norm, d_gain1, d_bias1 = norm_one(scatter_sum(d_a[part]))
        sums = sums + jnp.stack([d_gain1, d_bias1])
        grad_pieces.append(gather_pieces((dh[cut] + dx_norm).astype(BF)))
    grad_tokens = join(mine_s, grad_pieces)
    sums = sum_shares(sums)
    small_out = small[: experts + 2].T
    return (
        output,
        grad_tokens,
        jnp.stack([sums[0], small[experts + 2]]),
        jnp.stack([sums[1], small[experts + 3]]),
        grad_qkv,
        grad_o,
        grad_in,
        grad_out,
        small_out[:, :experts],
        small_out[:, experts:],
        grad_up,
        grad_down,
    )


def solution(mesh):
    in_specs = (
        P("dp", None),
        P("dp", None),
        P(),
        P(),
        P(None, None, "mp"),
        P("mp", None),
        P(None, "mp"),
        P("mp", None),
        P(),
        P(),
        P("dp", None, "mp"),
        P("dp", "mp", None),
        P("dp", None),
        P(),
    )
    out_specs = (
        P("dp", None),
        P("dp", None),
        P(None, "dp"),
        P(None, "dp"),
        P("dp", None, "mp"),
        P("mp", "dp"),
        P("dp", "mp"),
        P("mp", "dp"),
        P("dp", None),
        P("dp", None),
        P("dp", None, "mp"),
        P("dp", "mp", None),
    )
    return jax.shard_map(body, mesh=mesh, in_specs=in_specs, out_specs=out_specs, check_vma=False)
```

```python
from functools import partial

import jax
import jax.numpy as jnp
from jax import lax
from jax.experimental import pallas as pl
from jax.experimental.pallas import tpu as pltpu
from jax.sharding import PartitionSpec as P

HD = 64
GROUP = 4
EPS = 1e-05
LOG2E = 1.4426950408889634
SCALE2 = 0.125 * LOG2E
HIDE = -1e30
BF = jnp.bfloat16
F32 = jnp.float32
LIGHT = pl.CostEstimate(flops=1 << 20, bytes_accessed=1 << 20, transcendentals=0)


def mm(a, b):
    return jnp.dot(a, b, preferred_element_type=F32)


def ein(spec, a, b):
    return jnp.einsum(spec, a, b, preferred_element_type=F32)


def call(kernel, name, prefetch, grid, in_specs, out_specs, out_shape, args, scratch=(), alias=None, vmem=48):
    return pl.pallas_call(
        kernel,
        grid_spec=pltpu.PrefetchScalarGridSpec(
            num_scalar_prefetch=1,
            grid=grid,
            in_specs=in_specs,
            out_specs=out_specs,
            scratch_shapes=list(scratch),
        ),
        out_shape=out_shape,
        input_output_aliases=alias or {},
        compiler_params=pltpu.CompilerParams(vmem_limit_bytes=vmem * 2**20),
        cost_estimate=LIGHT,
        name=name,
    )(prefetch, *args)


def fixed(shape):
    zeros = (0,) * len(shape)
    return pl.BlockSpec(shape, lambda *_: zeros)


def like(shape, dtype):
    return jax.ShapeDtypeStruct(shape, dtype)


def normalize(v):
    mean = jnp.mean(v, axis=-1, keepdims=True)
    centred = v - mean
    scale = lax.rsqrt(jnp.mean(centred * centred, axis=-1, keepdims=True) + EPS)
    return centred * scale, scale


def norm_back(grad, gain, normal, scale):
    g = grad * gain
    along = jnp.mean(g * normal, axis=-1, keepdims=True)
    return scale * (g - jnp.mean(g, axis=-1, keepdims=True) - normal * along)


def qkv_kernel(at_ref, x_ref, gain_ref, bias_ref, w_ref, a_ref, *outs):
    normal, _ = normalize(x_ref[...].astype(F32))
    a = (normal * gain_ref[...] + bias_ref[...]).astype(BF)
    a_ref[...] = a
    for s in range(GROUP):
        outs[s][...] = mm_t(w_ref[at_ref[0] ^ s], a).astype(BF)


def project(at, tokens, gain, bias, w_heads):
    rows, width = tokens.shape
    features = w_heads.shape[1]
    blk = min(256, rows)
    moving = pl.BlockSpec((blk, width), lambda i, n: (i, 0))
    return call(
        qkv_kernel,
        "project",
        at,
        (rows // blk,),
        [moving, fixed((1, width)), fixed((1, width)), fixed(w_heads.shape)],
        [moving] + [pl.BlockSpec((features, blk), lambda i, n: (0, i))] * GROUP,
        [like((rows, width), BF)] + [like((features, rows), BF)] * GROUP,
        (tokens, gain, bias, w_heads),
    )


def fill_keys(k_s, place, keys, first_len, blk):
    rows = place * blk + lax.broadcasted_iota(jnp.int32, (blk, 128), 0)
    lane = lax.broadcasted_iota(jnp.int32, (blk, 128), 1)
    wide = jnp.concatenate([keys.astype(F32).T, jnp.zeros((blk, 128 - HD), F32)], axis=1)
    wide = jnp.where((lane == HD) & (rows < first_len), HIDE, wide)
    k_s[pl.ds(place * blk, blk), :] = wide.astype(BF)


def wide_query(query, place, first_len, blk):
    cols = place * blk + lax.broadcasted_iota(jnp.int32, (128 - HD, blk), 1)
    sub = lax.broadcasted_iota(jnp.int32, (128 - HD, blk), 0)
    extra = jnp.where((sub == 0) & (cols >= first_len), 1.0, 0.0)
    return jnp.concatenate([query, extra.astype(BF)], axis=0)


def causal(blk):
    keys = lax.broadcasted_iota(jnp.int32, (blk, blk), 0)
    queries = lax.broadcasted_iota(jnp.int32, (blk, blk), 1)
    return keys <= queries


def attend_kernel(blk, per, at_ref, *refs):
    qkv_refs, o_refs = refs[:GROUP], refs[GROUP : 2 * GROUP]
    lse_ref, k_s, qkv_s = refs[2 * GROUP :]
    i = pl.program_id(0)
    place, first_len = at_ref[0], at_ref[3]

    @pl.when(i == 0)
    def _():
        for s in range(GROUP):
            qkv_s[place ^ s] = qkv_refs[s][...]

    def part(which, j):
        return qkv_s[j // per, HD * which : HD * (which + 1), pl.ds((j % per) * blk, blk)]

    fill_keys(k_s, i, part(1, i), first_len, blk)
    query = wide_query(part(0, i), i, first_len, blk)

    def scores(j):
        return mm(k_s[pl.ds(pl.multiple_of(j * blk, blk), blk), :], query)

    s = jnp.where(causal(blk), scores(i), HIDE)
    top = jnp.max(s, axis=0, keepdims=True)
    p = jnp.exp2((s - top) * SCALE2)
    total = jnp.sum(p, axis=0, keepdims=True)
    acc = mm(part(2, i), p.astype(BF))

    def step(j, carry):
        top, total, acc = carry
        s = scores(j)
        new = jnp.maximum(top, jnp.max(s, axis=0, keepdims=True))
        p = jnp.exp2((s - new) * SCALE2)
        keep = jnp.exp2((top - new) * SCALE2)
        total = total * keep + jnp.sum(p, axis=0, keepdims=True)
        acc = acc * keep + mm(part(2, j), p.astype(BF))
        return new, total, acc

    low = jnp.where(i * blk >= first_len, first_len // blk, 0)
    top, total, acc = lax.fori_loop(low, i, step, (top, total, acc))
    out = (acc / total).astype(BF)
    for s in range(GROUP):

        @pl.when((i // per) ^ place == s)
        def _():
            o_refs[s][:, pl.ds((i % per) * blk, blk)] = out

    lse_ref[0] = top * SCALE2 + jnp.log2(total)


def attend(at, qkv):
    features, rows = qkv[0].shape
    blk = min(512, rows)
    per = rows // blk
    count = GROUP * per
    return call(
        partial(attend_kernel, blk, per),
        "attend",
        at,
        (count,),
        [fixed((features, rows))] * GROUP,
        [fixed((HD, rows))] * GROUP + [pl.BlockSpec((1, 1, blk), lambda i, n: (i, 0, 0))],
        [like((HD, rows), BF)] * GROUP + [like((count, 1, blk), F32)],
        qkv,
        scratch=[pltpu.VMEM((GROUP * rows, 128), BF), pltpu.VMEM((GROUP, features, rows), BF)],
    )


def back_kernel(blk, per, first, count, at_ref, *refs):
    qkv_refs, do_refs, o_refs = refs[:GROUP], refs[GROUP : 2 * GROUP], refs[2 * GROUP : 3 * GROUP]
    lse_ref, refs = refs[3 * GROUP], refs[3 * GROUP + 1 :]
    if first:
        dq_in_ref, refs = refs[1], refs[2:]
    out_ref, dq_ref, k_s, kt_s, v_s, wide_s, dot_s, both_s, delta_s, acc_s = refs
    at_first = pl.program_id(0) == 0
    j = first + pl.program_id(0)
    place, first_len = at_ref[0], at_ref[3]

    @pl.when(at_first)
    def _():
        dq_ref[...] = dq_in_ref[...] if first else jnp.zeros(dq_ref.shape, F32)
        zero = jnp.zeros((blk, HD), F32)
        for s in range(GROUP):

            @pl.when((place ^ s) * per >= first)
            def _():
                for sub in range(per):
                    i = (place ^ s) * per + sub
                    at = pl.ds(pl.multiple_of(i * blk, blk), blk)
                    cut = slice(sub * blk, (sub + 1) * blk)
                    query = qkv_refs[s][0:HD, cut]
                    keys = qkv_refs[s][HD : 2 * HD, cut]
                    grad = do_refs[s][:, cut]
                    fill_keys(k_s, i, keys, first_len, blk)
                    kt_s[:, at] = keys
                    dot_s[:, at] = grad
                    wide_s[:, at] = wide_query(query, i, first_len, blk)
                    grad = grad.astype(F32)
                    values = qkv_refs[s][2 * HD :, cut].astype(F32)
                    v_s[at, :] = jnp.concatenate([values.T, zero], axis=1).astype(BF)
                    both_s[0, at, :] = jnp.concatenate([grad.T, zero], axis=1).astype(BF)
                    both_s[1, at, :] = jnp.concatenate([zero, query.astype(F32).T], axis=1).astype(BF)
                    held = o_refs[s][:, cut].astype(F32)
                    delta_s[i] = jnp.sum(held * grad, axis=0, keepdims=True)

    here = pl.ds(pl.multiple_of(j * blk, blk), blk)
    keys_t = kt_s[:, here]
    values = v_s[here, 0:HD]

    def pair(i, diagonal):
        at = pl.ds(pl.multiple_of(i * blk, blk), blk)
        s = mm(k_s[here, :], wide_s[:, at])
        p = jnp.exp2(s * SCALE2 - lse_ref[i])
        if diagonal:
            p = jnp.where(causal(blk), p, 0.0)
        dp = mm(values, dot_s[:, at])
        ds = (p * (dp - delta_s[i])).astype(BF)
        dq_ref[:, at] += mm(keys_t, ds)
        return mm(p.astype(BF), both_s[0, at, :]) + mm(ds, both_s[1, at, :])

    acc_s[...] = pair(j, True)

    def step(i, carry):
        acc_s[...] += pair(i, False)
        return carry

    high = jnp.where((j + 1) * blk <= first_len, (first_len + blk - 1) // blk, count)
    lax.fori_loop(j + 1, high, step, 0)
    both = acc_s[...].T
    out_ref[0, 0:HD, :] = (dq_ref[:, here] * 0.125).astype(BF)
    out_ref[0, HD : 2 * HD, :] = (both[HD:, :] * 0.125).astype(BF)
    out_ref[0, 2 * HD :, :] = both[:HD, :].astype(BF)


def attend_back(at, qkv, do, o, lse, before, first, last):
    features, rows = qkv[0].shape
    blk = min(512, rows)
    per = rows // blk
    count = GROUP * per
    dq_shape = (HD, GROUP * rows)
    carried = [pl.BlockSpec(memory_space=pl.ANY), fixed(dq_shape)] if first else []
    return call(
        partial(back_kernel, blk, per, first * per, count),
        "attend_back",
        at,
        ((last - first) * per,),
        [fixed((features, rows))] * GROUP
        + [fixed((HD, rows))] * (2 * GROUP)
        + [fixed((count, 1, blk))]
        + carried,
        [
            pl.BlockSpec((1, features, blk), lambda j, n: ((first + j // per) ^ n[0], 0, j % per)),
            fixed(dq_shape),
        ],
        [like((GROUP, features, rows), BF), like(dq_shape, F32)],
        (*qkv, *do, *o, lse, *(before if first else ())),
        scratch=[
            pltpu.VMEM((GROUP * rows, 128), BF),
            pltpu.VMEM((HD, GROUP * rows), BF),
            pltpu.VMEM((GROUP * rows, 128), BF),
            pltpu.VMEM((128, GROUP * rows), BF),
            pltpu.VMEM((HD, GROUP * rows), BF),
            pltpu.VMEM((2, GROUP * rows, 128), BF),
            pltpu.VMEM((count, 1, blk), F32),
            pltpu.VMEM((blk, 128), F32),
        ],
        alias={3 * GROUP + 2: 0} if first else None,
    )


def split_kernel(at_ref, *refs):
    ins, outs = refs[:GROUP], refs[GROUP:]
    cols = outs[0].shape[1]
    for r in range(4):
        lanes = pl.ds(pl.multiple_of(((at_ref[1] + r) % 4) * cols, cols), cols)
        for s in range(GROUP):
            head = pl.ds(pl.multiple_of((at_ref[0] ^ s) * HD, HD), HD)
            outs[r][head, :] = ins[s][:, lanes]


def split(at, heads):
    rows = heads[0].shape[1]
    shape = (GROUP * HD, rows // 4)
    return call(
        split_kernel,
        "split",
        at,
        (1,),
        [fixed((HD, rows))] * GROUP,
        [fixed(shape)] * 4,
        [like(shape, BF)] * 4,
        heads,
    )


def unsplit_kernel(at_ref, *refs):
    ins, outs = refs[:4], refs[4:]
    cols = ins[0].shape[1]
    for r in range(4):
        lanes = pl.ds(pl.multiple_of(((at_ref[1] + r) % 4) * cols, cols), cols)
        for s in range(GROUP):
            head = pl.ds(pl.multiple_of((at_ref[0] ^ s) * HD, HD), HD)
            outs[s][:, lanes] = ins[r][head, :]


def unsplit(at, pieces):
    shape = (HD, 4 * pieces[0].shape[1])
    return call(
        unsplit_kernel,
        "unsplit",
        at,
        (1,),
        [fixed(pieces[0].shape)] * 4,
        [fixed(shape)] * GROUP,
        [like(shape, BF)] * GROUP,
        pieces,
    )


def mid_kernel(at_ref, *refs):
    o_refs, w_refs = refs[:4], refs[4:8]
    x_ref, gain_ref, bias_ref, h_ref, b_ref = refs[8:]
    h = x_ref[...].astype(F32)
    for r in range(4):
        h = h + mm(o_refs[r][...].astype(F32).T.astype(BF), w_refs[r][...])
    h_ref[...] = h
    normal, _ = normalize(h)
    b_ref[...] = (normal * gain_ref[...] + bias_ref[...]).astype(BF)


def mid(at, o, w_o, tokens, gain, bias):
    features, quarter = o[0].shape
    width = tokens.shape[1]
    return call(
        mid_kernel,
        "mid",
        at,
        (1,),
        [fixed((features, quarter))] * 4
        + [fixed((features, width))] * 4
        + [pl.BlockSpec((quarter, width), lambda i, n: (n[1], 0))]
        + [fixed((1, width))] * 2,
        [fixed((quarter, width))] * 2,
        [like((quarter, width), F32), like((quarter, width), BF)],
        (*o, *w_o, tokens, gain, bias),
    )


def add_up(refs):
    total = refs[0][...]
    for ref in refs[1:]:
        total = total + ref[...].astype(F32)
    return total


def mid_back_kernel(count, at_ref, *refs):
    shares, refs = refs[: 4 * count], refs[4 * count :]
    w_refs = refs[:4]
    h_ref, dy_ref, gain_ref, dh_ref, low_ref, sums_ref = refs[4:10]
    do_refs = refs[10:]
    db = jnp.concatenate([add_up(shares[4 * c : 4 * c + 4]) for c in range(count)], axis=1)
    normal, scale = normalize(h_ref[...])
    dh = dy_ref[...].astype(F32) + norm_back(db, gain_ref[...], normal, scale)
    dh_ref[...] = dh
    low = dh.astype(BF)
    low_ref[...] = low
    sums_ref[0:1, :] = jnp.sum(db * normal, axis=0, keepdims=True)
    sums_ref[1:2, :] = jnp.sum(db, axis=0, keepdims=True)
    for r in range(4):
        do_refs[r][...] = mm_t(w_refs[r][...], low).astype(BF)


def mid_back(at, shares, w_o, h, dy, gain):
    count = len(shares)
    (features, width), quarter = w_o[0].shape, h.shape[0]
    each = shares[0][0].shape
    piece = (features, quarter)
    return call(
        partial(mid_back_kernel, count),
        "mid_back",
        at,
        (1,),
        [fixed(each)] * (4 * count)
        + [fixed((features, width))] * 4
        + [fixed((quarter, width))] * 2
        + [fixed((1, width))],
        [fixed((quarter, width))] * 2 + [fixed((2, width))] + [fixed(piece)] * 4,
        [like((quarter, width), F32), like((quarter, width), BF), like((2, width), F32)]
        + [like(piece, BF)] * 4,
        (*[part for share in shares for part in share], *w_o, h, dy, gain),
    )


def first_back_kernel(at_ref, *refs):
    shares = refs[:4]
    x_ref, dh_ref, gain_ref, out_ref, sums_ref = refs[4:]
    d_a = add_up(shares)
    normal, scale = normalize(x_ref[...].astype(F32))
    out_ref[...] = (dh_ref[...] + norm_back(d_a, gain_ref[...], normal, scale)).astype(BF)
    sums_ref[0:1, :] = jnp.sum(d_a * normal, axis=0, keepdims=True)
    sums_ref[1:2, :] = jnp.sum(d_a, axis=0, keepdims=True)


def first_back(at, shares, tokens, dh, gain):
    quarter, width = dh.shape
    return call(
        first_back_kernel,
        "first_back",
        at,
        (1,),
        [fixed((quarter, width))] * 4
        + [pl.BlockSpec((quarter, width), lambda i, n: (n[1], 0))]
        + [fixed((quarter, width)), fixed((1, width))],
        [fixed((quarter, width)), fixed((2, width))],
        [like((quarter, width), BF), like((2, width), F32)],
        (*shares, tokens, dh, gain),
    )


def in_order(mine, own, right, left, far, right_two, left_two):
    one = jnp.where(mine == 3, far, left)
    two = jnp.where(mine < 2, left_two, right_two)
    three = jnp.where(mine == 0, far, right)
    return own, one, two, three


def one_hot(slots, dest):
    return jnp.where(slots == dest, 1.0, 0.0).astype(BF)


def dispatch_kernel(at_ref, dest_ref, rows_ref, out_ref):
    blk, rows = out_ref.shape[0], dest_ref.shape[1]
    slot = pl.program_id(0) * blk + lax.broadcasted_iota(jnp.int32, (blk, rows), 0)
    out_ref[...] = mm(one_hot(slot, dest_ref[...]), rows_ref[...]).astype(BF)


def gather_dispatch_kernel(at_ref, dest_ref, *refs):
    pieces, out_ref, rows_ref = refs[:6], refs[6], refs[7]

    @pl.when(pl.program_id(0) == 0)
    def _():
        at = 0
        for piece in in_order(at_ref[1], *[ref[...] for ref in pieces]):
            rows_ref[at : at + piece.shape[0], :] = piece
            at += piece.shape[0]

    dispatch_kernel(at_ref, dest_ref, rows_ref, out_ref)


def dispatch(at, dest_row, pieces, slots):
    rows, width = dest_row.shape[1], pieces[0].shape[1]
    blk = min(256, slots)
    joined = len(pieces) > 1
    return call(
        gather_dispatch_kernel if joined else dispatch_kernel,
        "dispatch",
        at,
        (slots // blk,),
        [fixed((1, rows))] + [fixed(piece.shape) for piece in pieces],
        [pl.BlockSpec((blk, width), lambda i, n: (i, 0))] + [fixed((rows, width))] * joined,
        [like((slots, width), BF)] + [like((rows, width), BF)] * joined,
        (dest_row, *pieces),
    )


def join_kernel(at_ref, *refs):
    pieces, out_ref = refs[:6], refs[6]
    r = pl.program_id(0)
    for place, piece in enumerate(in_order(at_ref[1], *[ref[...] for ref in pieces])):

        @pl.when(r == place)
        def _():
            out_ref[...] = piece


def join(at, pieces):
    each, width = pieces[0].shape
    return call(
        join_kernel,
        "join",
        at,
        (4,),
        [fixed((each, width))] * 6,
        pl.BlockSpec((each, width), lambda r, n: ((n[1] + r) % 4, 0)),
        like((4 * each, width), BF),
        pieces,
    )


def write_shares(r, mine, total, own_ref, one_ref, two_ref, three_ref, end_ref):
    value = total.astype(BF)

    @pl.when(r == 0)
    def _():
        own_ref[...] = total

    @pl.when(r == 1)
    def _():
        one_ref[...] = value

    @pl.when(r == 2)
    def _():
        two_ref[...] = value

    @pl.when(r == 3)
    def _():
        three_ref[...] = value

    @pl.when(r == jnp.where(mine == 0, 3, 1))
    def _():
        end_ref[...] = value


def share_shapes(rows, width):
    return [like((rows, width), F32)] + [like((rows, width), BF)] * 4


def combine_kernel(count, at_ref, *refs):
    dests, backs = refs[:count], refs[count : 2 * count]
    base_ref, outs = refs[2 * count], refs[2 * count + 1 :]
    total = base_ref[...].astype(F32)
    for dest_ref, back_ref in zip(dests, backs):
        shape = (dest_ref.shape[0], back_ref.shape[0])
        lane = lax.broadcasted_iota(jnp.int32, shape, 1)
        total = total + mm(one_hot(lane, dest_ref[...]), back_ref[...])
    write_shares(pl.program_id(0), at_ref[1], total, *outs)


def combine(at, dests, backs, base, column, columns):
    count, (slots, width) = len(backs), backs[0].shape
    width, rows = width // columns, base.shape[0] // 4
    return call(
        partial(combine_kernel, count),
        "combine",
        at,
        (4,),
        [pl.BlockSpec((rows, 1), lambda r, n: (r, 0))] * count
        + [pl.BlockSpec((slots, width), lambda r, n: (0, column))] * count
        + [pl.BlockSpec((rows, width), lambda r, n: (r, column))],
        [fixed((rows, width))] * 5,
        share_shapes(rows, width),
        (*dests, *backs, base),
    )


def mm_t(a, b):
    return lax.dot_general(a, b, (((1,), (1,)), ((), ())), preferred_element_type=F32)


def gelu_both(u):
    c = 0.7978845608028654
    square = u * u
    t = jnp.tanh(u * (c + (c * 0.044715) * square))
    half = 0.5 + 0.5 * t
    slope = half + (0.5 * u) * (1.0 - t * t) * (c + (3.0 * c * 0.044715) * square)
    return u * half, slope


def high_low(value):
    high = value.astype(BF)
    return high, (value - high.astype(F32)).astype(BF)


def two_coefs(logits, lane, experts):
    inside = (lane >= experts) & (lane < experts + 2)
    top = jnp.max(jnp.where(inside, logits, HIDE), axis=1, keepdims=True)
    e = jnp.where(inside, jnp.exp(logits - top), 0.0)
    e = e / jnp.sum(e, axis=1, keepdims=True)
    first = jnp.sum(jnp.where(lane == experts, e, 0.0), axis=1, keepdims=True)
    second = jnp.sum(jnp.where(lane == experts + 1, e, 0.0), axis=1, keepdims=True)
    return first, second


def small_back(d_small, rows, w_small_ref, small_ref, i):
    high, low = high_low(d_small)
    w_small = w_small_ref[...]
    high_t, low_t = high_low(d_small.T)

    @pl.when(i == 0)
    def _():
        small_ref[...] = jnp.zeros(small_ref.shape, F32)

    small_ref[...] += mm(high_t, rows) + mm(low_t, rows)
    return mm_t(high, w_small) + mm_t(low, w_small)


def expert_kernel(experts, half, at_ref, rows_ref, dy_ref, up_ref, down_ref, w_small_ref, *outs):
    if half:
        outs = outs[4:]
    rows_out_ref, hid_ref, dy_out_ref, deu_ref, y_ref, d_rows_ref, small_ref = outs
    rows = rows_ref[...]
    rows_out_ref[...] = rows
    up = mm(rows, up_ref[...])
    logits = mm(rows, w_small_ref[...])
    lane = lax.broadcasted_iota(jnp.int32, logits.shape, 1)
    routed = lane < experts
    top = jnp.max(jnp.where(routed, logits, HIDE), axis=1, keepdims=True)
    probs = jnp.where(routed, jnp.exp(logits - top), 0.0)
    probs = probs / jnp.sum(probs, axis=1, keepdims=True)
    own = jnp.where(lane == at_ref[2], 1.0, 0.0)
    gate = jnp.sum(probs * own, axis=1, keepdims=True)
    first, second = two_coefs(logits, lane, experts)
    weight = second * gate
    dy = dy_ref[...].reshape(rows.shape).astype(F32)
    d_y = (weight * dy).astype(BF)
    dy_out_ref[...] = d_y
    d_hidden = mm_t(d_y, down_ref[...])
    hidden, slope = gelu_both(up)
    hidden = hidden.astype(BF)
    hid_ref[...] = hidden
    d_up = (d_hidden * slope).astype(BF)
    deu_ref[...] = d_up
    y = mm(hidden, down_ref[...])
    y_ref[...] = (weight * y).astype(BF)
    along = gate * jnp.sum(dy * y, axis=1, keepdims=True)
    mixed = first * second * along
    d_small = (second * along) * (own - probs)
    d_small = jnp.where(routed, d_small, 0.0)
    d_small = d_small + jnp.where(lane == experts + 1, mixed, 0.0)
    d_small = d_small - jnp.where(lane == experts, mixed, 0.0)
    d_rows = mm_t(d_up, up_ref[...]) + small_back(d_small, rows, w_small_ref, small_ref, pl.program_id(0))
    d_rows_ref[...] = d_rows.astype(BF)


def expert_rows(at, rows, dy, w_up, w_down, w_small, experts, half, before):
    count, width = rows.shape
    hid, lanes = w_up.shape[1], w_small.shape[1]
    blk = min(256, count)
    capacity = count // dy.shape[0]
    steps = count // blk
    moving = pl.BlockSpec((blk, width), lambda i, n: (i, 0))
    kept = [pl.BlockSpec((blk, size), lambda i, n: (i + half * steps, 0)) for size in (width, hid, width, hid)]
    return call(
        partial(expert_kernel, experts, half),
        "expert_rows",
        at,
        (steps,),
        [
            moving,
            pl.BlockSpec((blk // capacity, capacity, width), lambda i, n: (i, half, 0)),
            fixed((width, hid)),
            fixed((hid, width)),
            fixed((width, lanes)),
        ]
        + [pl.BlockSpec(memory_space=pl.ANY)] * (4 * half),
        kept + [moving, moving, fixed((lanes, width))],
        [like((2 * count, size), BF) for size in (width, hid, width, hid)]
        + [like((count, width), BF)] * 2
        + [like((lanes, width), F32)],
        (rows, dy, w_up, w_down, w_small, *before),
        alias={6 + k: k for k in range(4)} if half else None,
    )


def dense_kernel(experts, at_ref, rows_ref, dy_ref, in_ref, out_ref, w_small_ref, *outs):
    hid_ref, grad_ref, d_up_ref, mix_ref, db_ref, small_ref = outs
    rows = rows_ref[...]
    up = mm(rows, in_ref[...])
    logits = mm(rows, w_small_ref[...])
    lane = lax.broadcasted_iota(jnp.int32, logits.shape, 1)
    first, second = two_coefs(logits, lane, experts)
    dy = dy_ref[...].astype(F32)
    grad = (first * dy).astype(BF)
    grad_ref[...] = grad
    d_hidden = mm_t(grad, out_ref[...])
    hidden, slope = gelu_both(up)
    hidden = hidden.astype(BF)
    hid_ref[...] = hidden
    d_up = (d_hidden * slope).astype(BF)
    d_up_ref[...] = d_up
    dense = mm(hidden, out_ref[...])
    mix_ref[...] = first * dense
    mixed = first * second * jnp.sum(dy * dense, axis=1, keepdims=True)
    d_small = jnp.where(lane == experts, mixed, 0.0) - jnp.where(lane == experts + 1, mixed, 0.0)
    db_ref[...] = mm_t(d_up, in_ref[...]) + small_back(d_small, rows, w_small_ref, small_ref, pl.program_id(0))


def dense_rows(at, rows, dy, w_in, w_out, w_small, experts):
    (count, width), hid, lanes = rows.shape, w_in.shape[1], w_small.shape[1]
    blk = min(256, count)
    row_out = pl.BlockSpec((blk, width), lambda i, n: (i, 0))
    hid_out = pl.BlockSpec((blk, hid), lambda i, n: (i, 0))
    return call(
        partial(dense_kernel, experts),
        "dense_rows",
        at,
        (count // blk,),
        [row_out, row_out, fixed((width, hid)), fixed((hid, width)), fixed((width, lanes))],
        [hid_out, row_out, hid_out, row_out, row_out, fixed((lanes, width))],
        [
            like((count, hid), BF),
            like((count, width), BF),
            like((count, hid), BF),
            like((count, width), F32),
            like((count, width), F32),
            like((lanes, width), F32),
        ],
        (rows, dy, w_in, w_out, w_small),
    )


def turned(value):
    return value.astype(F32).T.astype(BF)


def dense_grads_kernel(at_ref, b_ref, d_up_ref, grad_ref, hid_ref, out_ref):
    width = d_up_ref.shape[1]
    out_ref[:, :width] = mm(turned(b_ref[...]), d_up_ref[...]).astype(BF)
    out_ref[:, width:] = mm(turned(grad_ref[...]), hid_ref[...]).astype(BF)


def dense_grads(at, b, d_up, grad, hidden):
    (rows, width), hid = b.shape, hidden.shape[1]
    blk = min(256, width)
    column = pl.BlockSpec((rows, blk), lambda i, n: (0, i))
    return call(
        dense_grads_kernel,
        "dense_grads",
        at,
        (width // blk,),
        [column, fixed((rows, hid)), column, fixed((rows, hid))],
        pl.BlockSpec((blk, 2 * hid), lambda i, n: (i, 0)),
        like((width, 2 * hid), BF),
        (b, d_up, grad, hidden),
    )


def qkv_grads_kernel(at_ref, *refs):
    grads, a_ref, out_ref = refs[:GROUP], refs[GROUP], refs[GROUP + 1]
    s = pl.program_id(0)
    for k in range(GROUP):

        @pl.when(s == k)
        def _():
            grad = grads[k][...]
            grad = grad[0] if k == 0 else grad
            out_ref[...] = mm(grad, a_ref[...]).astype(BF)


def qkv_grads(at, held, came, a):
    rows, width = a.shape
    features = held.shape[1]
    return call(
        qkv_grads_kernel,
        "qkv_grads",
        at,
        (GROUP,),
        [fixed((1, features, rows))] + [fixed((features, rows))] * 3 + [fixed((rows, width))],
        pl.BlockSpec((features, width), lambda s, n: (n[0] ^ s, 0)),
        like((GROUP * features, width), BF),
        (held, *came, a),
    )


def project_kernel(at_ref, *refs):
    grads, w_ref, outs = refs[:GROUP], refs[GROUP], refs[GROUP + 1 :]
    total = 0.0
    for s in range(GROUP):
        grad = grads[s][...]
        grad = grad[0] if s == 0 else grad
        total = total + mm(turned(grad), w_ref[at_ref[0] ^ s])
    write_shares(pl.program_id(0), at_ref[1], total, *outs)


def project_back(at, held, came, w_heads):
    _, features, rows = held.shape
    width = w_heads.shape[2]
    blk = rows // 4
    return call(
        project_kernel,
        "project_back",
        at,
        (4,),
        [pl.BlockSpec((1, features, blk), lambda r, n: (0, 0, (n[1] + r) % 4))]
        + [pl.BlockSpec((features, blk), lambda r, n: (0, (n[1] + r) % 4))] * 3
        + [fixed(w_heads.shape)],
        [fixed((blk, width))] * 5,
        share_shapes(blk, width),
        (held, *came, w_heads),
    )


def hop(value, *pairs):
    return lax.ppermute(value, "mp", pairs)


def rotate(value, steps):
    return hop(value, *[(s, (s + steps) % 4) for s in range(4)])


def gather_near(own):
    right = hop(own, (0, 1), (1, 2), (2, 3))
    left = hop(own, (1, 0), (2, 1), (3, 2))
    return own, right, left, hop(own, (0, 3), (3, 0))


def gather_far(near):
    _, right, left, _ = near
    return *near, hop(right, (1, 2), (2, 3)), hop(left, (1, 0), (2, 1))


def gather_pieces(own):
    return gather_far(gather_near(own))


def scatter_far(shares):
    _, _, two, _, end = shares
    return hop(two, (2, 1), (3, 2)), hop(two, (0, 1), (1, 2)), hop(end, (0, 3), (3, 0))


def scatter_near(shares, came):
    own, one, _, three, _ = shares
    from_right, from_left, from_end = came
    three = (three.astype(F32) + from_right.astype(F32)).astype(BF)
    one = (one.astype(F32) + from_left.astype(F32)).astype(BF)
    return own, hop(three, (1, 0), (2, 1), (3, 2)), hop(one, (0, 1), (1, 2), (2, 3)), from_end


def scatter_sum(shares):
    return scatter_near(shares, scatter_far(shares))


def group_swap(value, s):
    count = lax.axis_size("dp")
    return lax.ppermute(value, "dp", [(t, t ^ s) for t in range(count)])


def expert_swap(value, experts):
    wide = value.reshape(experts, value.shape[0] // experts, value.shape[1])
    return lax.all_to_all(wide, "dp", 0, 0, tiled=True).reshape(value.shape)


def roll_rows(value, start):
    twice = jnp.concatenate([value, value], axis=0)
    return lax.dynamic_slice_in_dim(twice, start, value.shape[0], 0)


def sum_shares(value):
    count, width = value.shape
    dps = lax.axis_size("dp")
    parts = value.reshape(count, dps, width // dps).transpose(1, 0, 2)
    own = jnp.sum(lax.all_to_all(parts, "dp", 0, 0, tiled=True), axis=0)
    total = own
    for r in range(1, lax.axis_size("mp")):
        total = total + rotate(own, r)
    return total


def dp_share(value, dim):
    return lax.psum_scatter(value, "dp", scatter_dimension=dim, tiled=True)


def body(
    tokens,
    cotangent,
    ln_gains,
    ln_biases,
    w_qkv,
    w_o,
    w_in,
    w_out,
    w_router,
    w_coef,
    w_up,
    w_down,
    routes,
    long_group,
):
    rows, width = tokens.shape
    dps = lax.axis_size("dp")
    mine, position = lax.axis_index("mp"), lax.axis_index("dp")
    quarter = rows // 4
    start = mine * quarter
    heads_loc = w_qkv.shape[2] // HD
    hid = w_in.shape[1]
    experts = w_router.shape[1]
    capacity = max(2, 2 * rows // experts)
    half = capacity // 2
    barrier = lax.optimization_barrier
    first_len = lax.dynamic_index_in_dim(long_group, position // GROUP, 0, keepdims=False)
    at = jnp.stack([position % GROUP, mine, position, first_len]).astype(jnp.int32)
    gains = [ln_gains[0:1], ln_gains[1:2]]
    biases = [ln_biases[0:1], ln_biases[1:2]]
    w_o_parts = [w_o] + [rotate(w_o, r) for r in (1, 2, 3)]

    w_heads = w_qkv.reshape(width, 3, heads_loc, HD).transpose(2, 1, 3, 0)
    w_heads = w_heads.reshape(heads_loc, 3 * HD, width)
    a_r, *qkv = project(at, tokens, gains[0], biases[0], w_heads)
    qkv = [qkv[0]] + [group_swap(qkv[s], s) for s in (1, 2, 3)]

    route = roll_rows(routes, start)[:, 0]
    picked = (route[:, None] == jnp.arange(experts, dtype=jnp.int32)[None, :]).astype(jnp.int32)
    slot = jnp.sum((jnp.cumsum(picked, axis=0) - picked) * picked, axis=1)
    dy_b = roll_rows(cotangent, start)
    send_dy = dispatch(at, (route * capacity + slot)[None, :], [dy_b], experts * capacity)[0]
    *qkv, send_dy = barrier((*qkv, send_dy))
    got_dy = expert_swap(send_dy, experts).reshape(experts, capacity, width)
    in_half = [slot < half, slot >= half]
    dests = [
        jnp.where(in_half[k], route * half + slot - k * half, -1).astype(jnp.int32) for k in (0, 1)
    ]

    *o_t, lse = attend(at, qkv)
    *o_t, w_1, w_2, w_3 = barrier((*o_t, *w_o_parts[1:]))
    w_o_parts = [w_o, w_1, w_2, w_3]
    o_heads = [o_t[0]] + [group_swap(o_t[s], s) for s in (1, 2, 3)]
    pieces = split(at, o_heads)
    o_q = [pieces[0]] + [rotate(pieces[r], r) for r in (1, 2, 3)]
    h, b_q = mid(at, o_q, w_o_parts, tokens, gains[1], biases[1])

    pieces = gather_pieces(b_q)
    lanes = -(-(experts + 2) // 128) * 128
    w_small = jnp.concatenate(
        [w_router, w_coef, jnp.zeros((width, lanes - experts - 2), BF)], axis=1
    )
    send_0, b_r = dispatch(at, dests[0][None, :], pieces, experts * half)
    send_0, got_dy = barrier((send_0, got_dy))
    got_0 = expert_swap(send_0, experts)
    send_1 = dispatch(at, dests[1][None, :], [b_r], experts * half)[0]
    got_1 = expert_swap(send_1, experts)
    b_r, send_1 = barrier((b_r, send_1))
    hidden, dense_grad, d_up, mix_base, db_base, small_t = dense_rows(
        at, b_r, dy_b, w_in, w_out, w_small, experts
    )
    got_0, db_base = barrier((got_0, db_base))

    *kept, y_0, d_rows_0, small_0 = expert_rows(
        at, got_0, got_dy, w_up[0], w_down[0], w_small, experts, 0, ()
    )
    back_0 = expert_swap(d_rows_0, experts)
    *kept, y_1, d_rows_1, small_1 = expert_rows(
        at, got_1, got_dy, w_up[0], w_down[0], w_small, experts, 1, kept
    )
    back_1 = expert_swap(d_rows_1, experts)
    d_rows_1, b_r = barrier((d_rows_1, b_r))
    grads = dense_grads(at, b_r, d_up, dense_grad, hidden)
    back_0, back_1, grads, y_0, y_1 = barrier((back_0, back_1, grads, y_0, y_1))
    grads = dp_share(grads, 0)
    tok_y = [expert_swap(y_0, experts), expert_swap(y_1, experts)]

    dest_cols = [dest[:, None] for dest in dests]
    shares = [combine(at, dest_cols, [back_0, back_1], db_base, c, 2) for c in (0, 1)]
    shares = [scatter_sum(share) for share in shares]
    dh, dh_r, sums_2, *do_q = mid_back(at, shares, w_o_parts, h, dy_b[:quarter], gains[1])
    do_heads = unsplit(at, [do_q[0]] + [rotate(do_q[r], -r) for r in (1, 2, 3)])
    do_t = [do_heads[0]] + [group_swap(do_heads[s], s) for s in (1, 2, 3)]
    small = small_0[: experts + 2] + small_1[: experts + 2] + small_t[: experts + 2]
    small = jnp.concatenate([small, sums_2], axis=0)

    mix = combine(at, dest_cols, tok_y, mix_base, 0, 1)
    *do_t, m_0, m_1, m_2, m_3, m_4 = barrier((*do_t, *mix))
    mix = (m_0, m_1, m_2, m_3, m_4)
    far = scatter_far(mix)
    before = attend_back(at, qkv, do_t, o_t, lse, None, 0, 1)
    *before, f_0, f_1, f_2 = barrier((*before, *far))
    addends = scatter_near(mix, (f_0, f_1, f_2))
    out_q = sum([part.astype(F32) for part in addends], h).astype(BF)
    before = attend_back(at, qkv, do_t, o_t, lse, before, 1, 2)
    *before, out_q = barrier((*before, out_q))
    near = gather_near(out_q)
    d_qkv, _ = attend_back(at, qkv, do_t, o_t, lse, before, 2, GROUP)
    d_qkv, *near = barrier((d_qkv, *near))
    output = join(at, gather_far(near))

    came = [group_swap(d_qkv[s], s) for s in (1, 2, 3)]
    d_qkv, *kept = barrier((d_qkv, *kept))
    got, hidden_e, d_y, d_eu = kept
    grad_down = ein("rf,rd->fd", hidden_e, d_y)
    *came, grad_down = barrier((*came, grad_down))
    shares = project_back(at, d_qkv, came, w_heads)
    far = scatter_far(shares)
    grad_qkv = qkv_grads(at, d_qkv, came, a_r)
    grad_qkv, grads = barrier((grad_qkv, grads))
    grad_qkv = dp_share(grad_qkv, 1).astype(F32)
    grad_up = ein("rd,rf->df", got, d_eu)
    f_0, f_1, f_2, grad_up = barrier((*far, grad_up))
    shares = scatter_near(shares, (f_0, f_1, f_2))
    grad_q, sums_1 = first_back(at, shares, tokens, dh, gains[0])
    grad_tokens = join(at, gather_pieces(grad_q))
    sums_1 = sum_shares(sums_1)
    small = sum_shares(small)

    own = width // dps
    grad_qkv = grad_qkv.reshape(heads_loc, 3, HD, own).transpose(3, 1, 0, 2)
    grad_qkv = grad_qkv.reshape(own, 3, heads_loc * HD)
    grad_in = grads[:, :hid].astype(F32)
    grad_out = grads[:, hid:].astype(F32).T
    o_rows = jnp.concatenate(o_q, axis=0)
    grad_o = dp_share(ein("ft,td->fd", o_rows, dh_r).astype(BF), 1)
    share = heads_loc * HD
    grad_o = sum(
        [rotate(grad_o[r * share : (r + 1) * share], -r).astype(F32) for r in (1, 2, 3)],
        grad_o[:share].astype(F32),
    )
    small_out = small[: experts + 2].T
    return (
        output,
        grad_tokens,
        jnp.stack([sums_1[0], small[experts + 2]]),
        jnp.stack([sums_1[1], small[experts + 3]]),
        grad_qkv,
        grad_o,
        grad_in,
        grad_out,
        small_out[:, :experts],
        small_out[:, experts:],
        grad_up[None],
        grad_down[None],
    )


def solution(mesh):
    in_specs = (
        P("dp", None),
        P("dp", None),
        P(),
        P(),
        P(None, None, "mp"),
        P("mp", None),
        P(None, "mp"),
        P("mp", None),
        P(),
        P(),
        P("dp", None, "mp"),
        P("dp", "mp", None),
        P("dp", None),
        P(),
    )
    out_specs = (
        P("dp", None),
        P("dp", None),
        P(None, "dp"),
        P(None, "dp"),
        P("dp", None, "mp"),
        P("mp", "dp"),
        P("dp", "mp"),
        P("mp", "dp"),
        P("dp", None),
        P("dp", None),
        P("dp", None, "mp"),
        P("dp", "mp", None),
    )
    return jax.shard_map(body, mesh=mesh, in_specs=in_specs, out_specs=out_specs, check_vma=False)
```

```python
from functools import partial

import jax
import jax.numpy as jnp
from jax import lax
from jax.experimental import pallas as pl
from jax.experimental.pallas import tpu as pltpu
from jax.sharding import PartitionSpec as P

HD = 64
GROUP = 4
EPS = 1e-05
LOG2E = 1.4426950408889634
SCALE2 = 0.125 * LOG2E
HIDE = -1e30
BF = jnp.bfloat16
F32 = jnp.float32
LIGHT = pl.CostEstimate(flops=1 << 20, bytes_accessed=1 << 20, transcendentals=0)


def mm(a, b):
    return jnp.dot(a, b, preferred_element_type=F32)


def ein(spec, a, b):
    return jnp.einsum(spec, a, b, preferred_element_type=F32)


def call(kernel, name, prefetch, grid, in_specs, out_specs, out_shape, args, scratch=(), alias=None, vmem=48):
    return pl.pallas_call(
        kernel,
        grid_spec=pltpu.PrefetchScalarGridSpec(
            num_scalar_prefetch=1,
            grid=grid,
            in_specs=in_specs,
            out_specs=out_specs,
            scratch_shapes=list(scratch),
        ),
        out_shape=out_shape,
        input_output_aliases=alias or {},
        compiler_params=pltpu.CompilerParams(vmem_limit_bytes=vmem * 2**20),
        cost_estimate=LIGHT,
        name=name,
    )(prefetch, *args)


def fixed(shape):
    zeros = (0,) * len(shape)
    return pl.BlockSpec(shape, lambda *_: zeros)


def like(shape, dtype):
    return jax.ShapeDtypeStruct(shape, dtype)


def normalize(v):
    mean = jnp.mean(v, axis=-1, keepdims=True)
    centred = v - mean
    scale = lax.rsqrt(jnp.mean(centred * centred, axis=-1, keepdims=True) + EPS)
    return centred * scale, scale


def norm_back(grad, gain, normal, scale):
    g = grad * gain
    along = jnp.mean(g * normal, axis=-1, keepdims=True)
    return scale * (g - jnp.mean(g, axis=-1, keepdims=True) - normal * along)


def qkv_kernel(at_ref, x_ref, gain_ref, bias_ref, w_ref, a_ref, *outs):
    normal, _ = normalize(x_ref[...].astype(F32))
    a = (normal * gain_ref[...] + bias_ref[...]).astype(BF)
    a_ref[...] = a
    for s in range(GROUP):
        outs[s][...] = mm_t(w_ref[at_ref[0] ^ s], a).astype(BF)


def project(at, tokens, gain, bias, w_heads):
    rows, width = tokens.shape
    features = w_heads.shape[1]
    blk = min(256, rows)
    moving = pl.BlockSpec((blk, width), lambda i, n: (i, 0))
    return call(
        qkv_kernel,
        "project",
        at,
        (rows // blk,),
        [moving, fixed((1, width)), fixed((1, width)), fixed(w_heads.shape)],
        [moving] + [pl.BlockSpec((features, blk), lambda i, n: (0, i))] * GROUP,
        [like((rows, width), BF)] + [like((features, rows), BF)] * GROUP,
        (tokens, gain, bias, w_heads),
    )


def fill_keys(k_s, place, keys, first_len, blk):
    rows = place * blk + lax.broadcasted_iota(jnp.int32, (blk, 128), 0)
    lane = lax.broadcasted_iota(jnp.int32, (blk, 128), 1)
    wide = jnp.concatenate([keys.astype(F32).T, jnp.zeros((blk, 128 - HD), F32)], axis=1)
    wide = jnp.where((lane == HD) & (rows < first_len), HIDE, wide)
    k_s[pl.ds(place * blk, blk), :] = wide.astype(BF)


def wide_query(query, place, first_len, blk):
    cols = place * blk + lax.broadcasted_iota(jnp.int32, (128 - HD, blk), 1)
    sub = lax.broadcasted_iota(jnp.int32, (128 - HD, blk), 0)
    extra = jnp.where((sub == 0) & (cols >= first_len), 1.0, 0.0)
    return jnp.concatenate([query, extra.astype(BF)], axis=0)


def causal(blk):
    keys = lax.broadcasted_iota(jnp.int32, (blk, blk), 0)
    queries = lax.broadcasted_iota(jnp.int32, (blk, blk), 1)
    return keys <= queries


def attend_kernel(blk, per, at_ref, *refs):
    qkv_refs, o_refs = refs[:GROUP], refs[GROUP : 2 * GROUP]
    lse_ref, k_s, qkv_s = refs[2 * GROUP :]
    i = pl.program_id(0)
    place, first_len = at_ref[0], at_ref[3]

    @pl.when(i == 0)
    def _():
        for s in range(GROUP):
            qkv_s[place ^ s] = qkv_refs[s][...]

    def part(which, j):
        return qkv_s[j // per, HD * which : HD * (which + 1), pl.ds((j % per) * blk, blk)]

    fill_keys(k_s, i, part(1, i), first_len, blk)
    query = wide_query(part(0, i), i, first_len, blk)

    def scores(j):
        return mm(k_s[pl.ds(pl.multiple_of(j * blk, blk), blk), :], query)

    s = jnp.where(causal(blk), scores(i), HIDE)
    top = jnp.max(s, axis=0, keepdims=True)
    p = jnp.exp2((s - top) * SCALE2)
    total = jnp.sum(p, axis=0, keepdims=True)
    acc = mm(part(2, i), p.astype(BF))

    def step(j, carry):
        top, total, acc = carry
        s = scores(j)
        new = jnp.maximum(top, jnp.max(s, axis=0, keepdims=True))
        p = jnp.exp2((s - new) * SCALE2)
        keep = jnp.exp2((top - new) * SCALE2)
        total = total * keep + jnp.sum(p, axis=0, keepdims=True)
        acc = acc * keep + mm(part(2, j), p.astype(BF))
        return new, total, acc

    low = jnp.where(i * blk >= first_len, first_len // blk, 0)
    top, total, acc = lax.fori_loop(low, i, step, (top, total, acc))
    out = (acc / total).astype(BF)
    for s in range(GROUP):

        @pl.when((i // per) ^ place == s)
        def _():
            o_refs[s][:, pl.ds((i % per) * blk, blk)] = out

    lse_ref[0] = top * SCALE2 + jnp.log2(total)


def attend(at, qkv):
    features, rows = qkv[0].shape
    blk = min(512, rows)
    per = rows // blk
    count = GROUP * per
    return call(
        partial(attend_kernel, blk, per),
        "attend",
        at,
        (count,),
        [fixed((features, rows))] * GROUP,
        [fixed((HD, rows))] * GROUP + [pl.BlockSpec((1, 1, blk), lambda i, n: (i, 0, 0))],
        [like((HD, rows), BF)] * GROUP + [like((count, 1, blk), F32)],
        qkv,
        scratch=[pltpu.VMEM((GROUP * rows, 128), BF), pltpu.VMEM((GROUP, features, rows), BF)],
    )


def back_kernel(blk, per, first, count, at_ref, *refs):
    qkv_refs, do_refs, o_refs = refs[:GROUP], refs[GROUP : 2 * GROUP], refs[2 * GROUP : 3 * GROUP]
    lse_ref, refs = refs[3 * GROUP], refs[3 * GROUP + 1 :]
    if first:
        dq_in_ref, refs = refs[1], refs[2:]
    out_ref, dq_ref, k_s, kt_s, v_s, wide_s, dot_s, both_s, delta_s, acc_s = refs
    at_first = pl.program_id(0) == 0
    j = first + pl.program_id(0)
    place, first_len = at_ref[0], at_ref[3]

    @pl.when(at_first)
    def _():
        dq_ref[...] = dq_in_ref[...] if first else jnp.zeros(dq_ref.shape, F32)
        zero = jnp.zeros((blk, HD), F32)
        for s in range(GROUP):

            @pl.when((place ^ s) * per >= first)
            def _():
                for sub in range(per):
                    i = (place ^ s) * per + sub
                    at = pl.ds(pl.multiple_of(i * blk, blk), blk)
                    cut = slice(sub * blk, (sub + 1) * blk)
                    query = qkv_refs[s][0:HD, cut]
                    keys = qkv_refs[s][HD : 2 * HD, cut]
                    grad = do_refs[s][:, cut]
                    fill_keys(k_s, i, keys, first_len, blk)
                    kt_s[:, at] = keys
                    dot_s[:, at] = grad
                    wide_s[:, at] = wide_query(query, i, first_len, blk)
                    grad = grad.astype(F32)
                    values = qkv_refs[s][2 * HD :, cut].astype(F32)
                    v_s[at, :] = jnp.concatenate([values.T, zero], axis=1).astype(BF)
                    both_s[0, at, :] = jnp.concatenate([grad.T, zero], axis=1).astype(BF)
                    both_s[1, at, :] = jnp.concatenate([zero, query.astype(F32).T], axis=1).astype(BF)
                    held = o_refs[s][:, cut].astype(F32)
                    delta_s[i] = jnp.sum(held * grad, axis=0, keepdims=True)

    here = pl.ds(pl.multiple_of(j * blk, blk), blk)
    keys_t = kt_s[:, here]
    values = v_s[here, 0:HD]

    def pair(i, diagonal):
        at = pl.ds(pl.multiple_of(i * blk, blk), blk)
        s = mm(k_s[here, :], wide_s[:, at])
        p = jnp.exp2(s * SCALE2 - lse_ref[i])
        if diagonal:
            p = jnp.where(causal(blk), p, 0.0)
        dp = mm(values, dot_s[:, at])
        ds = (p * (dp - delta_s[i])).astype(BF)
        dq_ref[:, at] += mm(keys_t, ds)
        return mm(p.astype(BF), both_s[0, at, :]) + mm(ds, both_s[1, at, :])

    acc_s[...] = pair(j, True)

    def step(i, carry):
        acc_s[...] += pair(i, False)
        return carry

    high = jnp.where((j + 1) * blk <= first_len, (first_len + blk - 1) // blk, count)
    lax.fori_loop(j + 1, high, step, 0)
    both = acc_s[...].T
    out_ref[0, 0:HD, :] = (dq_ref[:, here] * 0.125).astype(BF)
    out_ref[0, HD : 2 * HD, :] = (both[HD:, :] * 0.125).astype(BF)
    out_ref[0, 2 * HD :, :] = both[:HD, :].astype(BF)


def attend_back(at, qkv, do, o, lse, before, first, last):
    features, rows = qkv[0].shape
    blk = min(512, rows)
    per = rows // blk
    count = GROUP * per
    dq_shape = (HD, GROUP * rows)
    carried = [pl.BlockSpec(memory_space=pl.ANY), fixed(dq_shape)] if first else []
    return call(
        partial(back_kernel, blk, per, first * per, count),
        "attend_back",
        at,
        ((last - first) * per,),
        [fixed((features, rows))] * GROUP
        + [fixed((HD, rows))] * (2 * GROUP)
        + [fixed((count, 1, blk))]
        + carried,
        [
            pl.BlockSpec((1, features, blk), lambda j, n: ((first + j // per) ^ n[0], 0, j % per)),
            fixed(dq_shape),
        ],
        [like((GROUP, features, rows), BF), like(dq_shape, F32)],
        (*qkv, *do, *o, lse, *(before if first else ())),
        scratch=[
            pltpu.VMEM((GROUP * rows, 128), BF),
            pltpu.VMEM((HD, GROUP * rows), BF),
            pltpu.VMEM((GROUP * rows, 128), BF),
            pltpu.VMEM((128, GROUP * rows), BF),
            pltpu.VMEM((HD, GROUP * rows), BF),
            pltpu.VMEM((2, GROUP * rows, 128), BF),
            pltpu.VMEM((count, 1, blk), F32),
            pltpu.VMEM((blk, 128), F32),
        ],
        alias={3 * GROUP + 2: 0} if first else None,
    )


def split_kernel(at_ref, *refs):
    ins, outs = refs[:GROUP], refs[GROUP:]
    cols = outs[0].shape[1]
    for r in range(4):
        lanes = pl.ds(pl.multiple_of(((at_ref[1] + r) % 4) * cols, cols), cols)
        for s in range(GROUP):
            head = pl.ds(pl.multiple_of((at_ref[0] ^ s) * HD, HD), HD)
            outs[r][head, :] = ins[s][:, lanes]


def split(at, heads):
    rows = heads[0].shape[1]
    shape = (GROUP * HD, rows // 4)
    return call(
        split_kernel,
        "split",
        at,
        (1,),
        [fixed((HD, rows))] * GROUP,
        [fixed(shape)] * 4,
        [like(shape, BF)] * 4,
        heads,
    )


def unsplit_kernel(at_ref, *refs):
    ins, outs = refs[:4], refs[4:]
    cols = ins[0].shape[1]
    for r in range(4):
        lanes = pl.ds(pl.multiple_of(((at_ref[1] + r) % 4) * cols, cols), cols)
        for s in range(GROUP):
            head = pl.ds(pl.multiple_of((at_ref[0] ^ s) * HD, HD), HD)
            outs[s][:, lanes] = ins[r][head, :]


def unsplit(at, pieces):
    shape = (HD, 4 * pieces[0].shape[1])
    return call(
        unsplit_kernel,
        "unsplit",
        at,
        (1,),
        [fixed(pieces[0].shape)] * 4,
        [fixed(shape)] * GROUP,
        [like(shape, BF)] * GROUP,
        pieces,
    )


def heads_of(mine, r, features):
    return pl.ds(pl.multiple_of(((mine + 4 - r) % 4) * features, features), features)


def mid_kernel(at_ref, *refs):
    o_refs, (w_ref, x_ref, gain_ref, bias_ref, h_ref, b_ref) = refs[:4], refs[4:]
    h = x_ref[...].astype(F32)
    for r in range(4):
        rows = heads_of(at_ref[1], r, o_refs[r].shape[0])
        h = h + mm(o_refs[r][...].astype(F32).T.astype(BF), w_ref[rows, :])
    h_ref[...] = h
    normal, _ = normalize(h)
    b_ref[...] = (normal * gain_ref[...] + bias_ref[...]).astype(BF)


def mid(at, o, w_o, tokens, gain, bias):
    features, quarter = o[0].shape
    width = tokens.shape[1]
    return call(
        mid_kernel,
        "mid",
        at,
        (1,),
        [fixed((features, quarter))] * 4
        + [fixed(w_o.shape)]
        + [pl.BlockSpec((quarter, width), lambda i, n: (n[1], 0))]
        + [fixed((1, width))] * 2,
        [fixed((quarter, width))] * 2,
        [like((quarter, width), F32), like((quarter, width), BF)],
        (*o, w_o, tokens, gain, bias),
    )


def add_up(refs):
    total = refs[0][...]
    for ref in refs[1:]:
        total = total + ref[...].astype(F32)
    return total


def mid_back_kernel(at_ref, *refs):
    shares, (w_ref, h_ref, dy_ref, gain_ref, dh_ref, low_ref, sums_ref) = refs[:4], refs[4:11]
    do_refs = refs[11:]
    db = add_up(shares)
    normal, scale = normalize(h_ref[...])
    dh = dy_ref[...].astype(F32) + norm_back(db, gain_ref[...], normal, scale)
    dh_ref[...] = dh
    low = dh.astype(BF)
    low_ref[...] = low
    sums_ref[0:1, :] = jnp.sum(db * normal, axis=0, keepdims=True)
    sums_ref[1:2, :] = jnp.sum(db, axis=0, keepdims=True)
    for r in range(4):
        rows = heads_of(at_ref[1], r, do_refs[r].shape[0])
        do_refs[r][...] = mm_t(w_ref[rows, :], low).astype(BF)


def mid_back(at, shares, w_o, h, dy, gain):
    quarter, width = h.shape
    whole = fixed((quarter, width))
    piece = (w_o.shape[0] // 4, quarter)
    return call(
        mid_back_kernel,
        "mid_back",
        at,
        (1,),
        [whole] * 4 + [fixed(w_o.shape), whole, whole, fixed((1, width))],
        [whole] * 2 + [fixed((2, width))] + [fixed(piece)] * 4,
        [like((quarter, width), F32), like((quarter, width), BF), like((2, width), F32)]
        + [like(piece, BF)] * 4,
        (*shares, w_o, h, dy, gain),
    )


def first_back_kernel(at_ref, *refs):
    shares = refs[:4]
    x_ref, dh_ref, gain_ref, out_ref, sums_ref = refs[4:]
    d_a = add_up(shares)
    normal, scale = normalize(x_ref[...].astype(F32))
    out_ref[...] = (dh_ref[...] + norm_back(d_a, gain_ref[...], normal, scale)).astype(BF)
    sums_ref[0:1, :] = jnp.sum(d_a * normal, axis=0, keepdims=True)
    sums_ref[1:2, :] = jnp.sum(d_a, axis=0, keepdims=True)


def first_back(at, shares, tokens, dh, gain):
    quarter, width = dh.shape
    return call(
        first_back_kernel,
        "first_back",
        at,
        (1,),
        [fixed((quarter, width))] * 4
        + [pl.BlockSpec((quarter, width), lambda i, n: (n[1], 0))]
        + [fixed((quarter, width)), fixed((1, width))],
        [fixed((quarter, width)), fixed((2, width))],
        [like((quarter, width), BF), like((2, width), F32)],
        (*shares, tokens, dh, gain),
    )


def in_order(mine, own, right, left, far, right_two, left_two):
    one = jnp.where(mine == 3, far, left)
    two = jnp.where(mine < 2, left_two, right_two)
    three = jnp.where(mine == 0, far, right)
    return own, one, two, three


def one_hot(slots, dest):
    return jnp.where(slots == dest, 1.0, 0.0).astype(BF)


def dispatch_kernel(at_ref, dest_ref, rows_ref, out_ref):
    blk, rows = out_ref.shape[0], dest_ref.shape[1]
    slot = pl.program_id(0) * blk + lax.broadcasted_iota(jnp.int32, (blk, rows), 0)
    out_ref[...] = mm(one_hot(slot, dest_ref[...]), rows_ref[...]).astype(BF)


def gather_dispatch_kernel(at_ref, dest_ref, *refs):
    pieces, out_ref, rows_ref = refs[:6], refs[6], refs[7]

    @pl.when(pl.program_id(0) == 0)
    def _():
        at = 0
        for piece in in_order(at_ref[1], *[ref[...] for ref in pieces]):
            rows_ref[at : at + piece.shape[0], :] = piece
            at += piece.shape[0]

    dispatch_kernel(at_ref, dest_ref, rows_ref, out_ref)


def dispatch(at, dest_row, pieces, slots):
    rows, width = dest_row.shape[1], pieces[0].shape[1]
    blk = min(256, slots)
    joined = len(pieces) > 1
    return call(
        gather_dispatch_kernel if joined else dispatch_kernel,
        "dispatch",
        at,
        (slots // blk,),
        [fixed((1, rows))] + [fixed(piece.shape) for piece in pieces],
        [pl.BlockSpec((blk, width), lambda i, n: (i, 0))] + [fixed((rows, width))] * joined,
        [like((slots, width), BF)] + [like((rows, width), BF)] * joined,
        (dest_row, *pieces),
    )


def join_kernel(at_ref, *refs):
    pieces, out_ref = refs[:6], refs[6]
    r = pl.program_id(0)
    for place, piece in enumerate(in_order(at_ref[1], *[ref[...] for ref in pieces])):

        @pl.when(r == place)
        def _():
            out_ref[...] = piece


def join(at, pieces):
    each, width = pieces[0].shape
    return call(
        join_kernel,
        "join",
        at,
        (4,),
        [fixed((each, width))] * 6,
        pl.BlockSpec((each, width), lambda r, n: ((n[1] + r) % 4, 0)),
        like((4 * each, width), BF),
        pieces,
    )


def write_shares(r, mine, total, own_ref, one_ref, two_ref, three_ref, end_ref):
    value = total.astype(BF)

    @pl.when(r == 0)
    def _():
        own_ref[...] = total

    @pl.when(r == 1)
    def _():
        one_ref[...] = value

    @pl.when(r == 2)
    def _():
        two_ref[...] = value

    @pl.when(r == 3)
    def _():
        three_ref[...] = value

    @pl.when(r == jnp.where(mine == 0, 3, 1))
    def _():
        end_ref[...] = value


def share_shapes(rows, width):
    return [like((rows, width), F32)] + [like((rows, width), BF)] * 4


def combined(dests, backs, base_ref):
    total = base_ref[...].astype(F32)
    for dest_ref, back_ref in zip(dests, backs):
        shape = (dest_ref.shape[0], back_ref.shape[0])
        lane = lax.broadcasted_iota(jnp.int32, shape, 1)
        total = total + mm(one_hot(lane, dest_ref[...]), back_ref[...])
    return total


def combine_kernel(count, at_ref, *refs):
    total = combined(refs[:count], refs[count : 2 * count], refs[2 * count])
    write_shares(pl.program_id(0), at_ref[1], total, *refs[2 * count + 1 :])


def combine_whole_kernel(at_ref, dest_ref, back_ref, base_ref, h_ref, out_ref):
    total = combined([dest_ref], [back_ref], base_ref)
    own = jnp.where(pl.program_id(0) == 0, 1.0, 0.0)
    out_ref[...] = (total + own * h_ref[...]).astype(BF)


def combine(at, dests, backs, base, h=None):
    count, (slots, width) = len(backs), backs[0].shape
    rows = base.shape[0] // 4
    in_specs = (
        [pl.BlockSpec((rows, 1), lambda r, n: (r, 0))] * count
        + [fixed((slots, width))] * count
        + [pl.BlockSpec((rows, width), lambda r, n: (r, 0))]
    )
    if h is None:
        out_specs, shapes = [fixed((rows, width))] * 5, share_shapes(rows, width)
        kernel, args = partial(combine_kernel, count), (*dests, *backs, base)
    else:
        in_specs.append(fixed((rows, width)))
        out_specs = pl.BlockSpec((rows, width), lambda r, n: ((n[1] + r) % 4, 0))
        shapes = like(base.shape, BF)
        kernel, args = combine_whole_kernel, (*dests, *backs, base, h)
    return call(kernel, "combine", at, (4,), in_specs, out_specs, shapes, args)


def mm_t(a, b):
    return lax.dot_general(a, b, (((1,), (1,)), ((), ())), preferred_element_type=F32)


def gelu_both(u):
    c = 0.7978845608028654
    square = u * u
    t = jnp.tanh(u * (c + (c * 0.044715) * square))
    half = 0.5 + 0.5 * t
    slope = half + (0.5 * u) * (1.0 - t * t) * (c + (3.0 * c * 0.044715) * square)
    return u * half, slope


def high_low(value):
    high = value.astype(BF)
    return high, (value - high.astype(F32)).astype(BF)


def two_coefs(logits, lane, experts):
    inside = (lane >= experts) & (lane < experts + 2)
    top = jnp.max(jnp.where(inside, logits, HIDE), axis=1, keepdims=True)
    e = jnp.where(inside, jnp.exp(logits - top), 0.0)
    e = e / jnp.sum(e, axis=1, keepdims=True)
    first = jnp.sum(jnp.where(lane == experts, e, 0.0), axis=1, keepdims=True)
    second = jnp.sum(jnp.where(lane == experts + 1, e, 0.0), axis=1, keepdims=True)
    return first, second


def small_back(d_small, rows, w_small_ref, small_ref, i):
    high, low = high_low(d_small)
    w_small = w_small_ref[...]
    high_t, low_t = high_low(d_small.T)

    @pl.when(i == 0)
    def _():
        small_ref[...] = jnp.zeros(small_ref.shape, F32)

    small_ref[...] += mm(high_t, rows) + mm(low_t, rows)
    return mm_t(high, w_small) + mm_t(low, w_small)


def expert_kernel(experts, half, at_ref, rows_ref, dy_ref, up_ref, down_ref, w_small_ref, *outs):
    if half:
        outs = outs[5:]
    rows_out_ref, hid_ref, dy_out_ref, deu_ref, y_ref, d_rows_ref, small_ref = outs
    rows = rows_ref[...]
    rows_out_ref[...] = rows
    up = mm(rows, up_ref[...])
    logits = mm(rows, w_small_ref[...])
    lane = lax.broadcasted_iota(jnp.int32, logits.shape, 1)
    routed = lane < experts
    top = jnp.max(jnp.where(routed, logits, HIDE), axis=1, keepdims=True)
    probs = jnp.where(routed, jnp.exp(logits - top), 0.0)
    probs = probs / jnp.sum(probs, axis=1, keepdims=True)
    own = jnp.where(lane == at_ref[2], 1.0, 0.0)
    gate = jnp.sum(probs * own, axis=1, keepdims=True)
    first, second = two_coefs(logits, lane, experts)
    weight = second * gate
    dy = dy_ref[...].reshape(rows.shape).astype(F32)
    d_y = (weight * dy).astype(BF)
    dy_out_ref[...] = d_y
    d_hidden = mm_t(d_y, down_ref[...])
    hidden, slope = gelu_both(up)
    hidden = hidden.astype(BF)
    hid_ref[...] = hidden
    d_up = (d_hidden * slope).astype(BF)
    deu_ref[...] = d_up
    y = mm(hidden, down_ref[...])
    y_ref[...] = (weight * y).astype(BF).reshape(y_ref.shape)
    along = gate * jnp.sum(dy * y, axis=1, keepdims=True)
    mixed = first * second * along
    d_small = (second * along) * (own - probs)
    d_small = jnp.where(routed, d_small, 0.0)
    d_small = d_small + jnp.where(lane == experts + 1, mixed, 0.0)
    d_small = d_small - jnp.where(lane == experts, mixed, 0.0)
    d_rows = mm_t(d_up, up_ref[...]) + small_back(d_small, rows, w_small_ref, small_ref, pl.program_id(0))
    d_rows_ref[...] = d_rows.astype(BF)


def expert_rows(at, rows, dy, w_up, w_down, w_small, experts, half, before):
    count, width = rows.shape
    hid, lanes = w_up.shape[1], w_small.shape[1]
    blk = min(256, count)
    capacity = count // dy.shape[0]
    steps = count // blk
    moving = pl.BlockSpec((blk, width), lambda i, n: (i, 0))
    slots = pl.BlockSpec((blk // capacity, capacity, width), lambda i, n: (i, half, 0))
    kept = [pl.BlockSpec((blk, size), lambda i, n: (i + half * steps, 0)) for size in (width, hid, width, hid)]
    return call(
        partial(expert_kernel, experts, half),
        "expert_rows",
        at,
        (steps,),
        [
            moving,
            slots,
            fixed((width, hid)),
            fixed((hid, width)),
            fixed((width, lanes)),
        ]
        + [pl.BlockSpec(memory_space=pl.ANY)] * (5 * half),
        kept + [slots, moving, fixed((lanes, width))],
        [like((2 * count, size), BF) for size in (width, hid, width, hid)]
        + [like(dy.shape, BF), like((count, width), BF)]
        + [like((lanes, width), F32)],
        (rows, dy, w_up, w_down, w_small, *before),
        alias={6 + k: k for k in range(5)} if half else None,
    )


def dense_kernel(experts, at_ref, rows_ref, dy_ref, in_ref, out_ref, w_small_ref, *outs):
    hid_ref, grad_ref, d_up_ref, mix_ref, db_ref, small_ref = outs
    rows = rows_ref[...]
    up = mm(rows, in_ref[...])
    logits = mm(rows, w_small_ref[...])
    lane = lax.broadcasted_iota(jnp.int32, logits.shape, 1)
    first, second = two_coefs(logits, lane, experts)
    dy = dy_ref[...].astype(F32)
    grad = (first * dy).astype(BF)
    grad_ref[...] = grad
    d_hidden = mm_t(grad, out_ref[...])
    hidden, slope = gelu_both(up)
    hidden = hidden.astype(BF)
    hid_ref[...] = hidden
    d_up = (d_hidden * slope).astype(BF)
    d_up_ref[...] = d_up
    dense = mm(hidden, out_ref[...])
    mix_ref[...] = first * dense
    mixed = first * second * jnp.sum(dy * dense, axis=1, keepdims=True)
    d_small = jnp.where(lane == experts, mixed, 0.0) - jnp.where(lane == experts + 1, mixed, 0.0)
    db_ref[...] = mm_t(d_up, in_ref[...]) + small_back(d_small, rows, w_small_ref, small_ref, pl.program_id(0))


def dense_rows(at, rows, dy, w_in, w_out, w_small, experts):
    (count, width), hid, lanes = rows.shape, w_in.shape[1], w_small.shape[1]
    blk = min(256, count)
    row_out = pl.BlockSpec((blk, width), lambda i, n: (i, 0))
    hid_out = pl.BlockSpec((blk, hid), lambda i, n: (i, 0))
    return call(
        partial(dense_kernel, experts),
        "dense_rows",
        at,
        (count // blk,),
        [row_out, row_out, fixed((width, hid)), fixed((hid, width)), fixed((width, lanes))],
        [hid_out, row_out, hid_out, row_out, row_out, fixed((lanes, width))],
        [
            like((count, hid), BF),
            like((count, width), BF),
            like((count, hid), BF),
            like((count, width), F32),
            like((count, width), F32),
            like((lanes, width), F32),
        ],
        (rows, dy, w_in, w_out, w_small),
    )


def turned(value):
    return value.astype(F32).T.astype(BF)


def dense_grads_kernel(at_ref, b_ref, d_up_ref, grad_ref, hid_ref, out_ref):
    width = d_up_ref.shape[1]
    blk = out_ref.shape[1]
    parts = out_ref.shape[0]
    first = mm(turned(b_ref[...]), d_up_ref[...]).astype(BF)
    second = mm(turned(grad_ref[...]), hid_ref[...]).astype(BF)
    for k in range(parts):
        out_ref[k, :, :width] = first[k * blk : (k + 1) * blk]
        out_ref[k, :, width:] = second[k * blk : (k + 1) * blk]


def dense_grads(at, b, d_up, grad, hidden, parts):
    (rows, width), hid = b.shape, hidden.shape[1]
    blk = min(256, width)
    own = width // parts
    column = pl.BlockSpec((rows, blk), lambda i, n: (0, i))
    return call(
        dense_grads_kernel,
        "dense_grads",
        at,
        (width // blk,),
        [column, fixed((rows, hid)), column, fixed((rows, hid))],
        pl.BlockSpec((blk // own, own, 2 * hid), lambda i, n: (i, 0, 0)),
        like((parts, own, 2 * hid), BF),
        (b, d_up, grad, hidden),
    )


def attention_grads_kernel(at_ref, *refs):
    grads, o_refs = refs[:GROUP], refs[GROUP : GROUP + 4]
    a_ref, dh_ref, out_ref = refs[GROUP + 4 :]
    heads, features = GROUP * HD, grads[1].shape[0]
    for k in range(GROUP):
        rows = pl.ds(pl.multiple_of((at_ref[0] ^ k) * features, features), features)
        grad = grads[k][...]
        grad = grad[0] if k == 0 else grad
        out_ref[rows, :] = mm(grad, a_ref[...]).astype(BF)
    for r in range(4):
        rows = pl.ds(pl.multiple_of(GROUP * features + ((at_ref[1] + 4 - r) % 4) * heads, heads), heads)
        out_ref[rows, :] = mm(o_refs[r][...], dh_ref[...]).astype(BF)


def attention_grads(at, held, came, o, a, dh):
    rows, width = a.shape
    features = held.shape[1]
    height = GROUP * features + 4 * o[0].shape[0]
    blk = min(256, width)
    column = lambda i, n: (0, i)
    return call(
        attention_grads_kernel,
        "attention_grads",
        at,
        (width // blk,),
        [fixed((1, features, rows))]
        + [fixed((features, rows))] * 3
        + [fixed(o[0].shape)] * 4
        + [pl.BlockSpec((rows, blk), column), pl.BlockSpec((dh.shape[0], blk), column)],
        pl.BlockSpec((height, blk), column),
        like((height, width), BF),
        (held, *came, *o, a, dh),
    )


def project_kernel(at_ref, *refs):
    grads, w_ref, outs = refs[:GROUP], refs[GROUP], refs[GROUP + 1 :]
    total = 0.0
    for s in range(GROUP):
        grad = grads[s][...]
        grad = grad[0] if s == 0 else grad
        total = total + mm(turned(grad), w_ref[at_ref[0] ^ s])
    write_shares(pl.program_id(0), at_ref[1], total, *outs)


def project_back(at, held, came, w_heads):
    _, features, rows = held.shape
    width = w_heads.shape[2]
    blk = rows // 4
    return call(
        project_kernel,
        "project_back",
        at,
        (4,),
        [pl.BlockSpec((1, features, blk), lambda r, n: (0, 0, (n[1] + r) % 4))]
        + [pl.BlockSpec((features, blk), lambda r, n: (0, (n[1] + r) % 4))] * 3
        + [fixed(w_heads.shape)],
        [fixed((blk, width))] * 5,
        share_shapes(blk, width),
        (held, *came, w_heads),
    )


def hop(value, *pairs):
    return lax.ppermute(value, "mp", pairs)


def rotate(value, steps):
    return hop(value, *[(s, (s + steps) % 4) for s in range(4)])


def gather_near(own):
    right = hop(own, (0, 1), (1, 2), (2, 3))
    left = hop(own, (1, 0), (2, 1), (3, 2))
    return own, right, left, hop(own, (0, 3), (3, 0))


def gather_far(near):
    _, right, left, _ = near
    return *near, hop(right, (1, 2), (2, 3)), hop(left, (1, 0), (2, 1))


def gather_pieces(own):
    return gather_far(gather_near(own))


def scatter_far(shares):
    _, _, two, _, end = shares
    return hop(two, (2, 1), (3, 2)), hop(two, (0, 1), (1, 2)), hop(end, (0, 3), (3, 0))


def scatter_near(shares, came):
    own, one, _, three, _ = shares
    from_right, from_left, from_end = came
    three = (three.astype(F32) + from_right.astype(F32)).astype(BF)
    one = (one.astype(F32) + from_left.astype(F32)).astype(BF)
    return own, hop(three, (1, 0), (2, 1), (3, 2)), hop(one, (0, 1), (1, 2), (2, 3)), from_end


def scatter_sum(shares):
    return scatter_near(shares, scatter_far(shares))


def group_swap(value, s):
    count = lax.axis_size("dp")
    return lax.ppermute(value, "dp", [(t, t ^ s) for t in range(count)])


def expert_swap(value, experts):
    wide = value.reshape(experts, value.shape[0] // experts, value.shape[1])
    return lax.all_to_all(wide, "dp", 0, 0, tiled=True).reshape(value.shape)


def roll_rows(value, start):
    twice = jnp.concatenate([value, value], axis=0)
    return lax.dynamic_slice_in_dim(twice, start, value.shape[0], 0)


def sum_shares(value):
    count, width = value.shape
    dps = lax.axis_size("dp")
    parts = value.reshape(count, dps, width // dps).transpose(1, 0, 2)
    own = jnp.sum(lax.all_to_all(parts, "dp", 0, 0, tiled=True), axis=0)
    total = own
    for r in range(1, lax.axis_size("mp")):
        total = total + rotate(own, r)
    return total


def dp_halving(value):
    position = lax.axis_index("dp")
    bit = 1
    while value.shape[0] > 1:
        pairs = value.reshape(value.shape[0] // 2, 2, *value.shape[1:])
        own = (position // bit) % 2
        keep = lax.dynamic_index_in_dim(pairs, own, 1, keepdims=False)
        give = lax.dynamic_index_in_dim(pairs, 1 - own, 1, keepdims=False)
        value = (keep.astype(F32) + group_swap(give, bit).astype(F32)).astype(BF)
        bit *= 2
    return value[0]


def dp_share(value, dim):
    return lax.psum_scatter(value, "dp", scatter_dimension=dim, tiled=True)


def body(
    tokens,
    cotangent,
    ln_gains,
    ln_biases,
    w_qkv,
    w_o,
    w_in,
    w_out,
    w_router,
    w_coef,
    w_up,
    w_down,
    routes,
    long_group,
):
    rows, width = tokens.shape
    dps = lax.axis_size("dp")
    mine, position = lax.axis_index("mp"), lax.axis_index("dp")
    quarter = rows // 4
    start = mine * quarter
    heads_loc = w_qkv.shape[2] // HD
    hid = w_in.shape[1]
    experts = w_router.shape[1]
    capacity = max(2, 2 * rows // experts)
    half = capacity // 2
    barrier = lax.optimization_barrier
    first_len = lax.dynamic_index_in_dim(long_group, position // GROUP, 0, keepdims=False)
    at = jnp.stack([position % GROUP, mine, position, first_len]).astype(jnp.int32)
    gains = [ln_gains[0:1], ln_gains[1:2]]
    biases = [ln_biases[0:1], ln_biases[1:2]]
    w_o_all = lax.all_gather(w_o, "mp", axis=0, tiled=True)

    w_heads = w_qkv.reshape(width, 3, heads_loc, HD).transpose(2, 1, 3, 0)
    w_heads = w_heads.reshape(heads_loc, 3 * HD, width)
    a_r, *qkv = project(at, tokens, gains[0], biases[0], w_heads)
    qkv = [qkv[0]] + [group_swap(qkv[s], s) for s in (1, 2, 3)]

    route = roll_rows(routes, start)[:, 0]
    picked = (route[:, None] == jnp.arange(experts, dtype=jnp.int32)[None, :]).astype(jnp.int32)
    slot = jnp.sum((jnp.cumsum(picked, axis=0) - picked) * picked, axis=1)
    dy_b = roll_rows(cotangent, start)
    send_dy = dispatch(at, (route * capacity + slot)[None, :], [dy_b], experts * capacity)[0]
    *qkv, send_dy = barrier((*qkv, send_dy))
    got_dy = expert_swap(send_dy, experts).reshape(experts, capacity, width)
    in_half = [slot < half, slot >= half]
    dests = [
        jnp.where(in_half[k], route * half + slot - k * half, -1).astype(jnp.int32) for k in (0, 1)
    ]

    *o_t, lse = attend(at, qkv)
    *o_t, w_o_all = barrier((*o_t, w_o_all))
    o_heads = [o_t[0]] + [group_swap(o_t[s], s) for s in (1, 2, 3)]
    pieces = split(at, o_heads)
    o_q = [pieces[0]] + [rotate(pieces[r], r) for r in (1, 2, 3)]
    h, b_q = mid(at, o_q, w_o_all, tokens, gains[1], biases[1])

    pieces = gather_pieces(b_q)
    lanes = -(-(experts + 2) // 128) * 128
    w_small = jnp.concatenate(
        [w_router, w_coef, jnp.zeros((width, lanes - experts - 2), BF)], axis=1
    )
    send_0, b_r = dispatch(at, dests[0][None, :], pieces, experts * half)
    send_0, got_dy = barrier((send_0, got_dy))
    got_0 = expert_swap(send_0, experts)
    send_1 = dispatch(at, dests[1][None, :], [b_r], experts * half)[0]
    b_r, send_1 = barrier((b_r, send_1))
    hidden, dense_grad, d_up, mix_base, db_base, small_t = dense_rows(
        at, b_r, dy_b, w_in, w_out, w_small, experts
    )
    send_1, got_0, db_base = barrier((send_1, got_0, db_base))
    got_1 = expert_swap(send_1, experts)

    *kept, d_rows_0, small_0 = expert_rows(
        at, got_0, got_dy, w_up[0], w_down[0], w_small, experts, 0, ()
    )
    back_0 = expert_swap(d_rows_0, experts)
    *kept, d_rows_1, small_1 = expert_rows(
        at, got_1, got_dy, w_up[0], w_down[0], w_small, experts, 1, kept
    )
    got, hidden_e, d_y, d_eu, back_y = kept
    back_1 = expert_swap(d_rows_1, experts)
    d_rows_1, b_r = barrier((d_rows_1, b_r))
    grads = dense_grads(at, b_r, d_up, dense_grad, hidden, dps)
    back_0, back_1, grads, back_y = barrier((back_0, back_1, grads, back_y))

    dest_cols = [dest[:, None] for dest in dests]
    shares = combine(at, dest_cols, [back_0, back_1], db_base)
    *shares, back_y, grads = barrier((*shares, back_y, grads))
    tok_y = expert_swap(back_y.reshape(experts * capacity, width), experts)
    shares = scatter_sum(shares)
    dh, dh_r, sums_2, *do_q = mid_back(at, shares, w_o_all, h, dy_b[:quarter], gains[1])
    do_heads = unsplit(at, [do_q[0]] + [rotate(do_q[r], -r) for r in (1, 2, 3)])
    do_t = [do_heads[0]] + [group_swap(do_heads[s], s) for s in (1, 2, 3)]
    grads = dp_halving(grads)

    mix = combine(at, [(route * capacity + slot)[:, None]], [tok_y], mix_base, h)
    *do_t, mix, grads = barrier((*do_t, mix, grads))
    output = lax.psum(mix, "mp")
    d_qkv, _ = attend_back(at, qkv, do_t, o_t, lse, None, 0, GROUP)

    came = [group_swap(d_qkv[s], s) for s in (1, 2, 3)]
    d_qkv, got, hidden_e, d_y, d_eu = barrier((d_qkv, got, hidden_e, d_y, d_eu))
    grad_down = ein("rf,rd->fd", hidden_e, d_y)
    *came, grad_down = barrier((*came, grad_down))
    shares = project_back(at, d_qkv, came, w_heads)
    far = scatter_far(shares)
    grads_a = attention_grads(at, d_qkv, came, o_q, a_r, dh_r)
    grads_a, output = barrier((grads_a, output))
    grads_a = dp_share(grads_a, 1).astype(F32)
    grad_up = ein("rd,rf->df", got, d_eu)
    f_0, f_1, f_2, grad_up = barrier((*far, grad_up))
    shares = scatter_near(shares, (f_0, f_1, f_2))
    grad_q, sums_1 = first_back(at, shares, tokens, dh, gains[0])
    grad_tokens = join(at, gather_pieces(grad_q))
    small = small_0[: experts + 2] + small_1[: experts + 2] + small_t[: experts + 2]
    small = sum_shares(jnp.concatenate([small, sums_2, sums_1], axis=0))

    own, features = width // dps, 3 * heads_loc * HD
    grad_qkv = grads_a[:features].reshape(heads_loc, 3, HD, own).transpose(3, 1, 0, 2)
    grad_qkv = grad_qkv.reshape(own, 3, heads_loc * HD)
    grad_in = grads[:, :hid].astype(F32)
    grad_out = grads[:, hid:].astype(F32).T
    grad_o = grads_a[features:].astype(BF).reshape(4, heads_loc * HD, own)
    grad_o = jnp.sum(lax.all_to_all(grad_o, "mp", 0, 0, tiled=True).astype(F32), axis=0)
    small_out = small[: experts + 2].T
    return (
        output,
        grad_tokens,
        jnp.stack([small[experts + 4], small[experts + 2]]),
        jnp.stack([small[experts + 5], small[experts + 3]]),
        grad_qkv,
        grad_o,
        grad_in,
        grad_out,
        small_out[:, :experts],
        small_out[:, experts:],
        grad_up[None],
        grad_down[None],
    )


def solution(mesh):
    in_specs = (
        P("dp", None),
        P("dp", None),
        P(),
        P(),
        P(None, None, "mp"),
        P("mp", None),
        P(None, "mp"),
        P("mp", None),
        P(),
        P(),
        P("dp", None, "mp"),
        P("dp", "mp", None),
        P("dp", None),
        P(),
    )
    out_specs = (
        P("dp", None),
        P("dp", None),
        P(None, "dp"),
        P(None, "dp"),
        P("dp", None, "mp"),
        P("mp", "dp"),
        P("dp", "mp"),
        P("mp", "dp"),
        P("dp", None),
        P("dp", None),
        P("dp", None, "mp"),
        P("dp", "mp", None),
    )
    return jax.shard_map(body, mesh=mesh, in_specs=in_specs, out_specs=out_specs, check_vma=False)
```

```python
from functools import partial

import jax
import jax.numpy as jnp
from jax import lax
from jax.experimental import pallas as pl
from jax.experimental.pallas import tpu as pltpu
from jax.sharding import PartitionSpec as P

HD = 64
GROUP = 4
EPS = 1e-05
LOG2E = 1.4426950408889634
SCALE2 = 0.125 * LOG2E
HIDE = -1e30
BF = jnp.bfloat16
F32 = jnp.float32
LIGHT = pl.CostEstimate(flops=1 << 20, bytes_accessed=1 << 20, transcendentals=0)


def mm(a, b):
    return jnp.dot(a, b, preferred_element_type=F32)


def ein(spec, a, b):
    return jnp.einsum(spec, a, b, preferred_element_type=F32)


def call(kernel, name, prefetch, grid, in_specs, out_specs, out_shape, args, scratch=(), alias=None, vmem=60):
    return pl.pallas_call(
        kernel,
        grid_spec=pltpu.PrefetchScalarGridSpec(
            num_scalar_prefetch=1,
            grid=grid,
            in_specs=in_specs,
            out_specs=out_specs,
            scratch_shapes=list(scratch),
        ),
        out_shape=out_shape,
        input_output_aliases=alias or {},
        compiler_params=pltpu.CompilerParams(vmem_limit_bytes=vmem * 2**20),
        cost_estimate=LIGHT,
        name=name,
    )(prefetch, *args)


def fixed(shape):
    zeros = (0,) * len(shape)
    return pl.BlockSpec(shape, lambda *_: zeros)


def like(shape, dtype):
    return jax.ShapeDtypeStruct(shape, dtype)


def normalize(v):
    mean = jnp.mean(v, axis=-1, keepdims=True)
    centred = v - mean
    scale = lax.rsqrt(jnp.mean(centred * centred, axis=-1, keepdims=True) + EPS)
    return centred * scale, scale


def norm_back(grad, gain, normal, scale):
    g = grad * gain
    along = jnp.mean(g * normal, axis=-1, keepdims=True)
    return scale * (g - jnp.mean(g, axis=-1, keepdims=True) - normal * along)


def qkv_kernel(at_ref, x_ref, gain_ref, bias_ref, w_ref, a_ref, *outs):
    normal, _ = normalize(x_ref[...].astype(F32))
    a = (normal * gain_ref[...] + bias_ref[...]).astype(BF)
    a_ref[...] = a
    for s in range(GROUP):
        outs[s][...] = mm_t(w_ref[at_ref[0] ^ s], a).astype(BF)


def project(at, tokens, gain, bias, w_heads):
    rows, width = tokens.shape
    features = w_heads.shape[1]
    blk = min(256, rows)
    moving = pl.BlockSpec((blk, width), lambda i, n: (i, 0))
    return call(
        qkv_kernel,
        "project",
        at,
        (rows // blk,),
        [moving, fixed((1, width)), fixed((1, width)), fixed(w_heads.shape)],
        [moving] + [pl.BlockSpec((features, blk), lambda i, n: (0, i))] * GROUP,
        [like((rows, width), BF)] + [like((features, rows), BF)] * GROUP,
        (tokens, gain, bias, w_heads),
    )


def fill_keys(k_s, place, keys, first_len, blk):
    rows = place * blk + lax.broadcasted_iota(jnp.int32, (blk, 128), 0)
    lane = lax.broadcasted_iota(jnp.int32, (blk, 128), 1)
    wide = jnp.concatenate([keys.astype(F32).T, jnp.zeros((blk, 128 - HD), F32)], axis=1)
    wide = jnp.where((lane == HD) & (rows < first_len), HIDE, wide)
    k_s[pl.ds(place * blk, blk), :] = wide.astype(BF)


def wide_query(query, place, first_len, blk):
    cols = place * blk + lax.broadcasted_iota(jnp.int32, (128 - HD, blk), 1)
    sub = lax.broadcasted_iota(jnp.int32, (128 - HD, blk), 0)
    extra = jnp.where((sub == 0) & (cols >= first_len), 1.0, 0.0)
    return jnp.concatenate([query, extra.astype(BF)], axis=0)


def causal(blk):
    keys = lax.broadcasted_iota(jnp.int32, (blk, blk), 0)
    queries = lax.broadcasted_iota(jnp.int32, (blk, blk), 1)
    return keys <= queries


def attend_kernel(blk, per, at_ref, *refs):
    qkv_refs, o_refs = refs[:GROUP], refs[GROUP : 2 * GROUP]
    lse_ref, k_s, qkv_s = refs[2 * GROUP :]
    i = pl.program_id(0)
    place, first_len = at_ref[0], at_ref[3]

    @pl.when(i == 0)
    def _():
        for s in range(GROUP):
            qkv_s[place ^ s] = qkv_refs[s][...]

    def part(which, j):
        return qkv_s[j // per, HD * which : HD * (which + 1), pl.ds((j % per) * blk, blk)]

    fill_keys(k_s, i, part(1, i), first_len, blk)
    query = wide_query(part(0, i), i, first_len, blk)

    def scores(j):
        return mm(k_s[pl.ds(pl.multiple_of(j * blk, blk), blk), :], query)

    s = jnp.where(causal(blk), scores(i), HIDE)
    top = jnp.max(s, axis=0, keepdims=True)
    p = jnp.exp2((s - top) * SCALE2)
    total = jnp.sum(p, axis=0, keepdims=True)
    acc = mm(part(2, i), p.astype(BF))

    def step(j, carry):
        top, total, acc = carry
        s = scores(j)
        new = jnp.maximum(top, jnp.max(s, axis=0, keepdims=True))
        p = jnp.exp2((s - new) * SCALE2)
        keep = jnp.exp2((top - new) * SCALE2)
        total = total * keep + jnp.sum(p, axis=0, keepdims=True)
        acc = acc * keep + mm(part(2, j), p.astype(BF))
        return new, total, acc

    low = jnp.where(i * blk >= first_len, first_len // blk, 0)
    top, total, acc = lax.fori_loop(low, i, step, (top, total, acc))
    out = (acc / total).astype(BF)
    for s in range(GROUP):

        @pl.when((i // per) ^ place == s)
        def _():
            o_refs[s][:, pl.ds((i % per) * blk, blk)] = out

    lse_ref[0] = top * SCALE2 + jnp.log2(total)


def attend(at, qkv):
    features, rows = qkv[0].shape
    blk = min(512, rows)
    per = rows // blk
    count = GROUP * per
    return call(
        partial(attend_kernel, blk, per),
        "attend",
        at,
        (count,),
        [fixed((features, rows))] * GROUP,
        [fixed((HD, rows))] * GROUP + [pl.BlockSpec((1, 1, blk), lambda i, n: (i, 0, 0))],
        [like((HD, rows), BF)] * GROUP + [like((count, 1, blk), F32)],
        qkv,
        scratch=[pltpu.VMEM((GROUP * rows, 128), BF), pltpu.VMEM((GROUP, features, rows), BF)],
    )


def back_kernel(blk, per, first, count, at_ref, *refs):
    qkv_refs, do_refs, o_refs = refs[:GROUP], refs[GROUP : 2 * GROUP], refs[2 * GROUP : 3 * GROUP]
    lse_ref, refs = refs[3 * GROUP], refs[3 * GROUP + 1 :]
    if first:
        dq_in_ref, refs = refs[1], refs[2:]
    out_ref, dq_ref, k_s, kt_s, v_s, wide_s, dot_s, both_s, delta_s, acc_s = refs
    at_first = pl.program_id(0) == 0
    j = first + pl.program_id(0)
    place, first_len = at_ref[0], at_ref[3]

    @pl.when(at_first)
    def _():
        dq_ref[...] = dq_in_ref[...] if first else jnp.zeros(dq_ref.shape, F32)
        zero = jnp.zeros((blk, HD), F32)
        for s in range(GROUP):

            @pl.when((place ^ s) * per >= first)
            def _():
                for sub in range(per):
                    i = (place ^ s) * per + sub
                    at = pl.ds(pl.multiple_of(i * blk, blk), blk)
                    cut = slice(sub * blk, (sub + 1) * blk)
                    query = qkv_refs[s][0:HD, cut]
                    keys = qkv_refs[s][HD : 2 * HD, cut]
                    grad = do_refs[s][:, cut]
                    fill_keys(k_s, i, keys, first_len, blk)
                    kt_s[:, at] = keys
                    dot_s[:, at] = grad
                    wide_s[:, at] = wide_query(query, i, first_len, blk)
                    grad = grad.astype(F32)
                    values = qkv_refs[s][2 * HD :, cut].astype(F32)
                    v_s[at, :] = jnp.concatenate([values.T, zero], axis=1).astype(BF)
                    both_s[0, at, :] = jnp.concatenate([grad.T, zero], axis=1).astype(BF)
                    both_s[1, at, :] = jnp.concatenate([zero, query.astype(F32).T], axis=1).astype(BF)
                    held = o_refs[s][:, cut].astype(F32)
                    delta_s[i] = jnp.sum(held * grad, axis=0, keepdims=True)

    here = pl.ds(pl.multiple_of(j * blk, blk), blk)
    keys_t = kt_s[:, here]
    values = v_s[here, 0:HD]

    def pair(i, diagonal):
        at = pl.ds(pl.multiple_of(i * blk, blk), blk)
        s = mm(k_s[here, :], wide_s[:, at])
        p = jnp.exp2(s * SCALE2 - lse_ref[i])
        if diagonal:
            p = jnp.where(causal(blk), p, 0.0)
        dp = mm(values, dot_s[:, at])
        ds = (p * (dp - delta_s[i])).astype(BF)
        dq_ref[:, at] += mm(keys_t, ds)
        return mm(p.astype(BF), both_s[0, at, :]) + mm(ds, both_s[1, at, :])

    acc_s[...] = pair(j, True)

    def step(i, carry):
        acc_s[...] += pair(i, False)
        return carry

    high = jnp.where((j + 1) * blk <= first_len, (first_len + blk - 1) // blk, count)
    lax.fori_loop(j + 1, high, step, 0)
    both = acc_s[...].T
    out_ref[0, 0:HD, :] = (dq_ref[:, here] * 0.125).astype(BF)
    out_ref[0, HD : 2 * HD, :] = (both[HD:, :] * 0.125).astype(BF)
    out_ref[0, 2 * HD :, :] = both[:HD, :].astype(BF)


def attend_back(at, qkv, do, o, lse, before, first, last):
    features, rows = qkv[0].shape
    blk = min(512, rows)
    per = rows // blk
    count = GROUP * per
    dq_shape = (HD, GROUP * rows)
    carried = [pl.BlockSpec(memory_space=pl.ANY), fixed(dq_shape)] if first else []
    return call(
        partial(back_kernel, blk, per, first * per, count),
        "attend_back",
        at,
        ((last - first) * per,),
        [fixed((features, rows))] * GROUP
        + [fixed((HD, rows))] * (2 * GROUP)
        + [fixed((count, 1, blk))]
        + carried,
        [
            pl.BlockSpec((1, features, blk), lambda j, n: ((first + j // per) ^ n[0], 0, j % per)),
            fixed(dq_shape),
        ],
        [like((GROUP, features, rows), BF), like(dq_shape, F32)],
        (*qkv, *do, *o, lse, *(before if first else ())),
        scratch=[
            pltpu.VMEM((GROUP * rows, 128), BF),
            pltpu.VMEM((HD, GROUP * rows), BF),
            pltpu.VMEM((GROUP * rows, 128), BF),
            pltpu.VMEM((128, GROUP * rows), BF),
            pltpu.VMEM((HD, GROUP * rows), BF),
            pltpu.VMEM((2, GROUP * rows, 128), BF),
            pltpu.VMEM((count, 1, blk), F32),
            pltpu.VMEM((blk, 128), F32),
        ],
        alias={3 * GROUP + 2: 0} if first else None,
    )


def split_kernel(at_ref, *refs):
    ins, outs = refs[:GROUP], refs[GROUP:]
    cols = outs[0].shape[1]
    for r in range(4):
        lanes = pl.ds(pl.multiple_of(((at_ref[1] + r) % 4) * cols, cols), cols)
        for s in range(GROUP):
            head = pl.ds(pl.multiple_of((at_ref[0] ^ s) * HD, HD), HD)
            outs[r][head, :] = ins[s][:, lanes]


def split(at, heads):
    rows = heads[0].shape[1]
    shape = (GROUP * HD, rows // 4)
    return call(
        split_kernel,
        "split",
        at,
        (1,),
        [fixed((HD, rows))] * GROUP,
        [fixed(shape)] * 4,
        [like(shape, BF)] * 4,
        heads,
    )


def unsplit_kernel(at_ref, *refs):
    ins, outs = refs[:4], refs[4:]
    cols = ins[0].shape[1]
    for r in range(4):
        lanes = pl.ds(pl.multiple_of(((at_ref[1] + r) % 4) * cols, cols), cols)
        for s in range(GROUP):
            head = pl.ds(pl.multiple_of((at_ref[0] ^ s) * HD, HD), HD)
            outs[s][:, lanes] = ins[r][head, :]


def unsplit(at, pieces):
    shape = (HD, 4 * pieces[0].shape[1])
    return call(
        unsplit_kernel,
        "unsplit",
        at,
        (1,),
        [fixed(pieces[0].shape)] * 4,
        [fixed(shape)] * GROUP,
        [like(shape, BF)] * GROUP,
        pieces,
    )


def heads_of(mine, r, features):
    return pl.ds(pl.multiple_of(((mine + 4 - r) % 4) * features, features), features)


def mid_kernel(at_ref, *refs):
    o_refs, (w_ref, x_ref, gain_ref, bias_ref, h_ref, b_ref) = refs[:4], refs[4:]
    h = x_ref[...].astype(F32)
    for r in range(4):
        rows = heads_of(at_ref[1], r, o_refs[r].shape[0])
        h = h + mm(o_refs[r][...].astype(F32).T.astype(BF), w_ref[rows, :])
    h_ref[...] = h
    normal, _ = normalize(h)
    b_ref[...] = (normal * gain_ref[...] + bias_ref[...]).astype(BF)


def mid(at, o, w_o, tokens, gain, bias):
    features, quarter = o[0].shape
    width = tokens.shape[1]
    return call(
        mid_kernel,
        "mid",
        at,
        (1,),
        [fixed((features, quarter))] * 4
        + [fixed(w_o.shape)]
        + [pl.BlockSpec((quarter, width), lambda i, n: (n[1], 0))]
        + [fixed((1, width))] * 2,
        [fixed((quarter, width))] * 2,
        [like((quarter, width), F32), like((quarter, width), BF)],
        (*o, w_o, tokens, gain, bias),
    )


def add_up(refs):
    total = refs[0][...]
    for ref in refs[1:]:
        total = total + ref[...].astype(F32)
    return total


def mid_back_kernel(at_ref, *refs):
    shares, (w_ref, h_ref, dy_ref, gain_ref, dh_ref, low_ref, sums_ref) = refs[:4], refs[4:11]
    do_refs = refs[11:]
    db = add_up(shares)
    normal, scale = normalize(h_ref[...])
    dh = dy_ref[...].astype(F32) + norm_back(db, gain_ref[...], normal, scale)
    dh_ref[...] = dh
    low = dh.astype(BF)
    low_ref[...] = low
    sums_ref[0:1, :] = jnp.sum(db * normal, axis=0, keepdims=True)
    sums_ref[1:2, :] = jnp.sum(db, axis=0, keepdims=True)
    for r in range(4):
        rows = heads_of(at_ref[1], r, do_refs[r].shape[0])
        do_refs[r][...] = mm_t(w_ref[rows, :], low).astype(BF)


def mid_back(at, shares, w_o, h, dy, gain):
    quarter, width = h.shape
    whole = fixed((quarter, width))
    piece = (w_o.shape[0] // 4, quarter)
    return call(
        mid_back_kernel,
        "mid_back",
        at,
        (1,),
        [whole] * 4 + [fixed(w_o.shape), whole, whole, fixed((1, width))],
        [whole] * 2 + [fixed((2, width))] + [fixed(piece)] * 4,
        [like((quarter, width), F32), like((quarter, width), BF), like((2, width), F32)]
        + [like(piece, BF)] * 4,
        (*shares, w_o, h, dy, gain),
    )


def first_back_kernel(at_ref, *refs):
    shares = refs[:4]
    x_ref, dh_ref, gain_ref, out_ref, sums_ref = refs[4:]
    d_a = add_up(shares)
    normal, scale = normalize(x_ref[...].astype(F32))
    out_ref[...] = (dh_ref[...] + norm_back(d_a, gain_ref[...], normal, scale)).astype(BF)
    sums_ref[0:1, :] = jnp.sum(d_a * normal, axis=0, keepdims=True)
    sums_ref[1:2, :] = jnp.sum(d_a, axis=0, keepdims=True)


def first_back(at, shares, tokens, dh, gain):
    quarter, width = dh.shape
    return call(
        first_back_kernel,
        "first_back",
        at,
        (1,),
        [fixed((quarter, width))] * 4
        + [pl.BlockSpec((quarter, width), lambda i, n: (n[1], 0))]
        + [fixed((quarter, width)), fixed((1, width))],
        [fixed((quarter, width)), fixed((2, width))],
        [like((quarter, width), BF), like((2, width), F32)],
        (*shares, tokens, dh, gain),
    )


def in_order(mine, own, right, left, far, right_two, left_two):
    one = jnp.where(mine == 3, far, left)
    two = jnp.where(mine < 2, left_two, right_two)
    three = jnp.where(mine == 0, far, right)
    return own, one, two, three


def one_hot(slots, dest):
    return jnp.where(slots == dest, 1.0, 0.0).astype(BF)


def dispatch_kernel(at_ref, dest_ref, rows_ref, out_ref):
    blk, rows = out_ref.shape[0], dest_ref.shape[1]
    slot = pl.program_id(0) * blk + lax.broadcasted_iota(jnp.int32, (blk, rows), 0)
    out_ref[...] = mm(one_hot(slot, dest_ref[...]), rows_ref[...]).astype(BF)


def gather_dispatch_kernel(at_ref, dest_ref, *refs):
    pieces, out_ref, rows_ref = refs[:6], refs[6], refs[7]

    @pl.when(pl.program_id(0) == 0)
    def _():
        at = 0
        for piece in in_order(at_ref[1], *[ref[...] for ref in pieces]):
            rows_ref[at : at + piece.shape[0], :] = piece
            at += piece.shape[0]

    dispatch_kernel(at_ref, dest_ref, rows_ref, out_ref)


def dispatch(at, dest_row, pieces, slots):
    rows, width = dest_row.shape[1], pieces[0].shape[1]
    blk = min(256, slots)
    joined = len(pieces) > 1
    return call(
        gather_dispatch_kernel if joined else dispatch_kernel,
        "dispatch",
        at,
        (slots // blk,),
        [fixed((1, rows))] + [fixed(piece.shape) for piece in pieces],
        [pl.BlockSpec((blk, width), lambda i, n: (i, 0))] + [fixed((rows, width))] * joined,
        [like((slots, width), BF)] + [like((rows, width), BF)] * joined,
        (dest_row, *pieces),
    )


def join_kernel(at_ref, *refs):
    pieces, out_ref = refs[:6], refs[6]
    r = pl.program_id(0)
    for place, piece in enumerate(in_order(at_ref[1], *[ref[...] for ref in pieces])):

        @pl.when(r == place)
        def _():
            out_ref[...] = piece


def join(at, pieces):
    each, width = pieces[0].shape
    return call(
        join_kernel,
        "join",
        at,
        (4,),
        [fixed((each, width))] * 6,
        pl.BlockSpec((each, width), lambda r, n: ((n[1] + r) % 4, 0)),
        like((4 * each, width), BF),
        pieces,
    )


def write_shares(r, mine, total, own_ref, one_ref, two_ref, three_ref, end_ref):
    value = total.astype(BF)

    @pl.when(r == 0)
    def _():
        own_ref[...] = total

    @pl.when(r == 1)
    def _():
        one_ref[...] = value

    @pl.when(r == 2)
    def _():
        two_ref[...] = value

    @pl.when(r == 3)
    def _():
        three_ref[...] = value

    @pl.when(r == jnp.where(mine == 0, 3, 1))
    def _():
        end_ref[...] = value


def share_shapes(rows, width):
    return [like((rows, width), F32)] + [like((rows, width), BF)] * 4


def combined(dests, backs, base_ref):
    total = base_ref[...].astype(F32)
    for dest_ref, back_ref in zip(dests, backs):
        shape = (dest_ref.shape[0], back_ref.shape[0])
        lane = lax.broadcasted_iota(jnp.int32, shape, 1)
        total = total + mm(one_hot(lane, dest_ref[...]), back_ref[...])
    return total


def combine_kernel(count, at_ref, *refs):
    total = combined(refs[:count], refs[count : 2 * count], refs[2 * count])
    write_shares(pl.program_id(0), at_ref[1], total, *refs[2 * count + 1 :])


def combine_whole_kernel(at_ref, dest_ref, back_ref, base_ref, h_ref, out_ref):
    total = combined([dest_ref], [back_ref], base_ref)
    own = jnp.where(pl.program_id(0) == 0, 1.0, 0.0)
    out_ref[...] = (total + own * h_ref[...]).astype(BF)


def combine(at, dests, backs, base, h=None):
    count, (slots, width) = len(backs), backs[0].shape
    rows = base.shape[0] // 4
    in_specs = (
        [pl.BlockSpec((rows, 1), lambda r, n: (r, 0))] * count
        + [fixed((slots, width))] * count
        + [pl.BlockSpec((rows, width), lambda r, n: (r, 0))]
    )
    if h is None:
        out_specs, shapes = [fixed((rows, width))] * 5, share_shapes(rows, width)
        kernel, args = partial(combine_kernel, count), (*dests, *backs, base)
    else:
        in_specs.append(fixed((rows, width)))
        out_specs = pl.BlockSpec((rows, width), lambda r, n: ((n[1] + r) % 4, 0))
        shapes = like(base.shape, BF)
        kernel, args = combine_whole_kernel, (*dests, *backs, base, h)
    return call(kernel, "combine", at, (4,), in_specs, out_specs, shapes, args)


def mm_t(a, b):
    return lax.dot_general(a, b, (((1,), (1,)), ((), ())), preferred_element_type=F32)


def gelu_both(u):
    c = 0.7978845608028654
    square = u * u
    t = jnp.tanh(u * (c + (c * 0.044715) * square))
    half = 0.5 + 0.5 * t
    slope = half + (0.5 * u) * (1.0 - t * t) * (c + (3.0 * c * 0.044715) * square)
    return u * half, slope


def high_low(value):
    high = value.astype(BF)
    return high, (value - high.astype(F32)).astype(BF)


def two_coefs(logits, lane, experts):
    inside = (lane >= experts) & (lane < experts + 2)
    top = jnp.max(jnp.where(inside, logits, HIDE), axis=1, keepdims=True)
    e = jnp.where(inside, jnp.exp(logits - top), 0.0)
    e = e / jnp.sum(e, axis=1, keepdims=True)
    first = jnp.sum(jnp.where(lane == experts, e, 0.0), axis=1, keepdims=True)
    second = jnp.sum(jnp.where(lane == experts + 1, e, 0.0), axis=1, keepdims=True)
    return first, second


def small_back(d_small, rows, w_small_ref, small_ref, i):
    high, low = high_low(d_small)
    w_small = w_small_ref[...]
    high_t, low_t = high_low(d_small.T)

    @pl.when(i == 0)
    def _():
        small_ref[...] = jnp.zeros(small_ref.shape, F32)

    small_ref[...] += mm(high_t, rows) + mm(low_t, rows)
    return mm_t(high, w_small) + mm_t(low, w_small)


def expert_kernel(experts, half, at_ref, rows_ref, dy_ref, up_ref, down_ref, w_small_ref, *outs):
    if half:
        outs = outs[5:]
    rows_out_ref, hid_ref, dy_out_ref, deu_ref, y_ref, d_rows_ref, small_ref = outs
    rows = rows_ref[...]
    rows_out_ref[...] = rows
    up = mm(rows, up_ref[...])
    logits = mm(rows, w_small_ref[...])
    lane = lax.broadcasted_iota(jnp.int32, logits.shape, 1)
    routed = lane < experts
    top = jnp.max(jnp.where(routed, logits, HIDE), axis=1, keepdims=True)
    probs = jnp.where(routed, jnp.exp(logits - top), 0.0)
    probs = probs / jnp.sum(probs, axis=1, keepdims=True)
    own = jnp.where(lane == at_ref[2], 1.0, 0.0)
    gate = jnp.sum(probs * own, axis=1, keepdims=True)
    first, second = two_coefs(logits, lane, experts)
    weight = second * gate
    dy = dy_ref[...].reshape(rows.shape).astype(F32)
    d_y = (weight * dy).astype(BF)
    dy_out_ref[...] = d_y
    d_hidden = mm_t(d_y, down_ref[...])
    hidden, slope = gelu_both(up)
    hidden = hidden.astype(BF)
    hid_ref[...] = hidden
    d_up = (d_hidden * slope).astype(BF)
    deu_ref[...] = d_up
    y = mm(hidden, down_ref[...])
    y_ref[...] = (weight * y).astype(BF).reshape(y_ref.shape)
    along = gate * jnp.sum(dy * y, axis=1, keepdims=True)
    mixed = first * second * along
    d_small = (second * along) * (own - probs)
    d_small = jnp.where(routed, d_small, 0.0)
    d_small = d_small + jnp.where(lane == experts + 1, mixed, 0.0)
    d_small = d_small - jnp.where(lane == experts, mixed, 0.0)
    d_rows = mm_t(d_up, up_ref[...]) + small_back(d_small, rows, w_small_ref, small_ref, pl.program_id(0))
    d_rows_ref[...] = d_rows.astype(BF)


def expert_rows(at, rows, dy, w_up, w_down, w_small, experts, half, before):
    count, width = rows.shape
    hid, lanes = w_up.shape[1], w_small.shape[1]
    blk = min(256, count)
    capacity = count // dy.shape[0]
    steps = count // blk
    moving = pl.BlockSpec((blk, width), lambda i, n: (i, 0))
    slots = pl.BlockSpec((blk // capacity, capacity, width), lambda i, n: (i, half, 0))
    kept = [pl.BlockSpec((blk, size), lambda i, n: (i + half * steps, 0)) for size in (width, hid, width, hid)]
    return call(
        partial(expert_kernel, experts, half),
        "expert_rows",
        at,
        (steps,),
        [
            moving,
            slots,
            fixed((width, hid)),
            fixed((hid, width)),
            fixed((width, lanes)),
        ]
        + [pl.BlockSpec(memory_space=pl.ANY)] * (5 * half),
        kept + [slots, moving, fixed((lanes, width))],
        [like((2 * count, size), BF) for size in (width, hid, width, hid)]
        + [like(dy.shape, BF), like((count, width), BF)]
        + [like((lanes, width), F32)],
        (rows, dy, w_up, w_down, w_small, *before),
        alias={6 + k: k for k in range(5)} if half else None,
    )


def dense_kernel(experts, at_ref, rows_ref, dy_ref, in_ref, out_ref, w_small_ref, *outs):
    hid_ref, grad_ref, d_up_ref, mix_ref, db_ref, small_ref = outs
    rows = rows_ref[...]
    up = mm(rows, in_ref[...])
    logits = mm(rows, w_small_ref[...])
    lane = lax.broadcasted_iota(jnp.int32, logits.shape, 1)
    first, second = two_coefs(logits, lane, experts)
    dy = dy_ref[...].astype(F32)
    grad = (first * dy).astype(BF)
    grad_ref[...] = grad
    d_hidden = mm_t(grad, out_ref[...])
    hidden, slope = gelu_both(up)
    hidden = hidden.astype(BF)
    hid_ref[...] = hidden
    d_up = (d_hidden * slope).astype(BF)
    d_up_ref[...] = d_up
    dense = mm(hidden, out_ref[...])
    mix_ref[...] = first * dense
    mixed = first * second * jnp.sum(dy * dense, axis=1, keepdims=True)
    d_small = jnp.where(lane == experts, mixed, 0.0) - jnp.where(lane == experts + 1, mixed, 0.0)
    db_ref[...] = mm_t(d_up, in_ref[...]) + small_back(d_small, rows, w_small_ref, small_ref, pl.program_id(0))


def dense_rows(at, rows, dy, w_in, w_out, w_small, experts):
    (count, width), hid, lanes = rows.shape, w_in.shape[1], w_small.shape[1]
    blk = min(256, count)
    row_out = pl.BlockSpec((blk, width), lambda i, n: (i, 0))
    hid_out = pl.BlockSpec((blk, hid), lambda i, n: (i, 0))
    return call(
        partial(dense_kernel, experts),
        "dense_rows",
        at,
        (count // blk,),
        [row_out, row_out, fixed((width, hid)), fixed((hid, width)), fixed((width, lanes))],
        [hid_out, row_out, hid_out, row_out, row_out, fixed((lanes, width))],
        [
            like((count, hid), BF),
            like((count, width), BF),
            like((count, hid), BF),
            like((count, width), F32),
            like((count, width), F32),
            like((lanes, width), F32),
        ],
        (rows, dy, w_in, w_out, w_small),
    )


def turned(value):
    return value.astype(F32).T.astype(BF)


def dense_grads_kernel(at_ref, b_ref, d_up_ref, grad_ref, hid_ref, out_ref):
    width = d_up_ref.shape[1]
    blk = out_ref.shape[1]
    parts = out_ref.shape[0]
    first = mm(turned(b_ref[...]), d_up_ref[...]).astype(BF)
    second = mm(turned(grad_ref[...]), hid_ref[...]).astype(BF)
    for k in range(parts):
        out_ref[k, :, :width] = first[k * blk : (k + 1) * blk]
        out_ref[k, :, width:] = second[k * blk : (k + 1) * blk]


def dense_grads(at, b, d_up, grad, hidden, parts):
    (rows, width), hid = b.shape, hidden.shape[1]
    blk = min(256, width)
    own = width // parts
    column = pl.BlockSpec((rows, blk), lambda i, n: (0, i))
    return call(
        dense_grads_kernel,
        "dense_grads",
        at,
        (width // blk,),
        [column, fixed((rows, hid)), column, fixed((rows, hid))],
        pl.BlockSpec((blk // own, own, 2 * hid), lambda i, n: (i, 0, 0)),
        like((parts, own, 2 * hid), BF),
        (b, d_up, grad, hidden),
    )


def attention_grads_kernel(at_ref, *refs):
    grads, o_refs = refs[:GROUP], refs[GROUP : GROUP + 4]
    a_ref, dh_ref, out_ref, all_s = refs[GROUP + 4 :]
    heads, features = GROUP * HD, grads[1].shape[0]
    for k in range(GROUP):
        rows = pl.ds(pl.multiple_of((at_ref[0] ^ k) * features, features), features)
        grad = grads[k][...]
        grad = grad[0] if k == 0 else grad
        all_s[rows, :] = mm(grad, a_ref[...])
    for r in range(4):
        rows = pl.ds(pl.multiple_of(GROUP * features + ((at_ref[1] + 4 - r) % 4) * heads, heads), heads)
        all_s[rows, :] = mm(o_refs[r][...], dh_ref[...])
    out_ref[...] = all_s[...].T.astype(BF)


def attention_grads(at, held, came, o, a, dh):
    rows, width = a.shape
    features = held.shape[1]
    height = GROUP * features + 4 * o[0].shape[0]
    blk = min(256, width)
    column = lambda i, n: (0, i)
    return call(
        attention_grads_kernel,
        "attention_grads",
        at,
        (width // blk,),
        [fixed((1, features, rows))]
        + [fixed((features, rows))] * 3
        + [fixed(o[0].shape)] * 4
        + [pl.BlockSpec((rows, blk), column), pl.BlockSpec((dh.shape[0], blk), column)],
        pl.BlockSpec((blk, height), lambda i, n: (i, 0)),
        like((width, height), BF),
        (held, *came, *o, a, dh),
        scratch=[pltpu.VMEM((height, blk), F32)],
    )


def project_kernel(at_ref, *refs):
    grads, w_ref, outs = refs[:GROUP], refs[GROUP], refs[GROUP + 1 :]
    total = 0.0
    for s in range(GROUP):
        grad = grads[s][...]
        grad = grad[0] if s == 0 else grad
        total = total + mm(turned(grad), w_ref[at_ref[0] ^ s])
    write_shares(pl.program_id(0), at_ref[1], total, *outs)


def project_back(at, held, came, w_heads):
    _, features, rows = held.shape
    width = w_heads.shape[2]
    blk = rows // 4
    return call(
        project_kernel,
        "project_back",
        at,
        (4,),
        [pl.BlockSpec((1, features, blk), lambda r, n: (0, 0, (n[1] + r) % 4))]
        + [pl.BlockSpec((features, blk), lambda r, n: (0, (n[1] + r) % 4))] * 3
        + [fixed(w_heads.shape)],
        [fixed((blk, width))] * 5,
        share_shapes(blk, width),
        (held, *came, w_heads),
    )


def hop(value, *pairs):
    return lax.ppermute(value, "mp", pairs)


def rotate(value, steps):
    return hop(value, *[(s, (s + steps) % 4) for s in range(4)])


def gather_near(own):
    right = hop(own, (0, 1), (1, 2), (2, 3))
    left = hop(own, (1, 0), (2, 1), (3, 2))
    return own, right, left, hop(own, (0, 3), (3, 0))


def gather_far(near):
    _, right, left, _ = near
    return *near, hop(right, (1, 2), (2, 3)), hop(left, (1, 0), (2, 1))


def gather_pieces(own):
    return gather_far(gather_near(own))


def scatter_far(shares):
    _, _, two, _, end = shares
    return hop(two, (2, 1), (3, 2)), hop(two, (0, 1), (1, 2)), hop(end, (0, 3), (3, 0))


def scatter_near(shares, came):
    own, one, _, three, _ = shares
    from_right, from_left, from_end = came
    three = (three.astype(F32) + from_right.astype(F32)).astype(BF)
    one = (one.astype(F32) + from_left.astype(F32)).astype(BF)
    return own, hop(three, (1, 0), (2, 1), (3, 2)), hop(one, (0, 1), (1, 2), (2, 3)), from_end


def scatter_sum(shares):
    return scatter_near(shares, scatter_far(shares))


def group_swap(value, s):
    count = lax.axis_size("dp")
    return lax.ppermute(value, "dp", [(t, t ^ s) for t in range(count)])


def expert_swap(value, experts):
    wide = value.reshape(experts, value.shape[0] // experts, value.shape[1])
    return lax.all_to_all(wide, "dp", 0, 0, tiled=True).reshape(value.shape)


def roll_rows(value, start):
    twice = jnp.concatenate([value, value], axis=0)
    return lax.dynamic_slice_in_dim(twice, start, value.shape[0], 0)


def sum_shares(value):
    count, width = value.shape
    dps = lax.axis_size("dp")
    parts = value.reshape(count, dps, width // dps).transpose(1, 0, 2)
    own = jnp.sum(lax.all_to_all(parts, "dp", 0, 0, tiled=True), axis=0)
    total = own
    for r in range(1, lax.axis_size("mp")):
        total = total + rotate(own, r)
    return total


def halve(value, bit):
    pairs = value.reshape(value.shape[0] // 2, 2, *value.shape[1:])
    own = (lax.axis_index("dp") // bit) % 2
    keep = lax.dynamic_index_in_dim(pairs, own, 1, keepdims=False)
    return keep, lax.dynamic_index_in_dim(pairs, 1 - own, 1, keepdims=False)


def add_halves(keep, came):
    return (keep.astype(F32) + came.astype(F32)).astype(BF)


def body(
    tokens,
    cotangent,
    ln_gains,
    ln_biases,
    w_qkv,
    w_o,
    w_in,
    w_out,
    w_router,
    w_coef,
    w_up,
    w_down,
    routes,
    long_group,
):
    rows, width = tokens.shape
    dps = lax.axis_size("dp")
    mine, position = lax.axis_index("mp"), lax.axis_index("dp")
    quarter = rows // 4
    start = mine * quarter
    heads_loc = w_qkv.shape[2] // HD
    hid = w_in.shape[1]
    experts = w_router.shape[1]
    capacity = max(2, 2 * rows // experts)
    half = capacity // 2
    barrier = lax.optimization_barrier
    first_len = lax.dynamic_index_in_dim(long_group, position // GROUP, 0, keepdims=False)
    at = jnp.stack([position % GROUP, mine, position, first_len]).astype(jnp.int32)
    gains = [ln_gains[0:1], ln_gains[1:2]]
    biases = [ln_biases[0:1], ln_biases[1:2]]
    w_o_all = lax.all_gather(w_o, "mp", axis=0, tiled=True)

    w_heads = w_qkv.reshape(width, 3, heads_loc, HD).transpose(2, 1, 3, 0)
    w_heads = w_heads.reshape(heads_loc, 3 * HD, width)
    a_r, *qkv = project(at, tokens, gains[0], biases[0], w_heads)
    qkv = [qkv[0]] + [group_swap(qkv[s], s) for s in (1, 2, 3)]

    route = roll_rows(routes, start)[:, 0]
    picked = (route[:, None] == jnp.arange(experts, dtype=jnp.int32)[None, :]).astype(jnp.int32)
    slot = jnp.sum((jnp.cumsum(picked, axis=0) - picked) * picked, axis=1)
    dy_b = roll_rows(cotangent, start)
    send_dy = dispatch(at, (route * capacity + slot)[None, :], [dy_b], experts * capacity)[0]
    *qkv, send_dy = barrier((*qkv, send_dy))
    in_half = [slot < half, slot >= half]
    dests = [
        jnp.where(in_half[k], route * half + slot - k * half, -1).astype(jnp.int32) for k in (0, 1)
    ]

    *o_t, lse = attend(at, qkv)
    *o_t, w_o_all = barrier((*o_t, w_o_all))
    o_heads = [o_t[0]] + [group_swap(o_t[s], s) for s in (1, 2, 3)]
    *o_heads, send_dy = barrier((*o_heads, send_dy))
    got_dy = expert_swap(send_dy, experts).reshape(experts, capacity, width)
    pieces = split(at, o_heads)
    o_q = [pieces[0]] + [rotate(pieces[r], r) for r in (1, 2, 3)]
    h, b_q = mid(at, o_q, w_o_all, tokens, gains[1], biases[1])

    pieces = gather_pieces(b_q)
    lanes = -(-(experts + 2) // 128) * 128
    w_small = jnp.concatenate(
        [w_router, w_coef, jnp.zeros((width, lanes - experts - 2), BF)], axis=1
    )
    send_0, b_r = dispatch(at, dests[0][None, :], pieces, experts * half)
    send_0, got_dy = barrier((send_0, got_dy))
    got_0 = expert_swap(send_0, experts)
    send_1 = dispatch(at, dests[1][None, :], [b_r], experts * half)[0]
    b_r, send_1 = barrier((b_r, send_1))
    hidden, dense_grad, d_up, mix_base, db_base, small_t = dense_rows(
        at, b_r, dy_b, w_in, w_out, w_small, experts
    )
    send_1, got_0, db_base = barrier((send_1, got_0, db_base))
    got_1 = expert_swap(send_1, experts)

    *kept, d_rows_0, small_0 = expert_rows(
        at, got_0, got_dy, w_up[0], w_down[0], w_small, experts, 0, ()
    )
    back_0 = expert_swap(d_rows_0, experts)
    *kept, d_rows_1, small_1 = expert_rows(
        at, got_1, got_dy, w_up[0], w_down[0], w_small, experts, 1, kept
    )
    got, hidden_e, d_y, d_eu, back_y = kept
    back_1 = expert_swap(d_rows_1, experts)
    d_rows_1, b_r = barrier((d_rows_1, b_r))
    grads = dense_grads(at, b_r, d_up, dense_grad, hidden, dps)
    back_0, back_1, grads, back_y = barrier((back_0, back_1, grads, back_y))

    dest_cols = [dest[:, None] for dest in dests]
    shares = combine(at, dest_cols, [back_0, back_1], db_base)
    *shares, back_y, grads = barrier((*shares, back_y, grads))
    tok_y = expert_swap(back_y.reshape(experts * capacity, width), experts)
    shares = scatter_sum(shares)
    dh, dh_r, sums_2, *do_q = mid_back(at, shares, w_o_all, h, dy_b[:quarter], gains[1])
    do_heads = unsplit(at, [do_q[0]] + [rotate(do_q[r], -r) for r in (1, 2, 3)])
    do_t = [do_heads[0]] + [group_swap(do_heads[s], s) for s in (1, 2, 3)]
    keep_1, give = halve(grads, 1)
    came_1 = group_swap(give, 1)

    mix = combine(at, [(route * capacity + slot)[:, None]], [tok_y], mix_base, h)
    keep_2, give = halve(add_halves(keep_1, came_1), 2)
    *do_t, mix, keep_2, give = barrier((*do_t, mix, keep_2, give))
    output = lax.psum(mix, "mp")
    came_2 = group_swap(give, 2)
    d_qkv, _ = attend_back(at, qkv, do_t, o_t, lse, None, 0, GROUP)
    d_qkv, keep_2, came_2 = barrier((d_qkv, keep_2, came_2))

    came = [group_swap(d_qkv[s], s) for s in (1, 2, 3)]
    d_qkv, got, hidden_e, d_y, d_eu = barrier((d_qkv, got, hidden_e, d_y, d_eu))
    grad_down = ein("rf,rd->fd", hidden_e, d_y)
    *came, grad_down = barrier((*came, grad_down))
    shares = project_back(at, d_qkv, came, w_heads)
    d_qkv, *shares = barrier((d_qkv, *shares))
    far = scatter_far(shares)
    grads_a = attention_grads(at, d_qkv, came, o_q, a_r, dh_r)
    grads_a, output = barrier((grads_a, output))
    grads_a = lax.psum_scatter(grads_a, "dp", scatter_dimension=0, tiled=True).T.astype(F32)
    grads = add_halves(keep_2, came_2)
    bit = 4
    while bit < dps:
        keep, give = halve(grads, bit)
        grads = add_halves(keep, group_swap(give, bit))
        bit *= 2
    grads = grads[0]
    grad_up = ein("rd,rf->df", got, d_eu)
    f_0, f_1, f_2, grad_up = barrier((*far, grad_up))
    shares = scatter_near(shares, (f_0, f_1, f_2))
    grad_q, sums_1 = first_back(at, shares, tokens, dh, gains[0])
    near = gather_near(grad_q)
    sums_1, right, left = barrier((sums_1, near[1], near[2]))
    grad_tokens = join(at, gather_far((near[0], right, left, near[3])))
    small = small_0[: experts + 2] + small_1[: experts + 2] + small_t[: experts + 2]
    small = sum_shares(jnp.concatenate([small, sums_2, sums_1], axis=0))

    own, features = width // dps, 3 * heads_loc * HD
    grad_qkv = grads_a[:features].reshape(heads_loc, 3, HD, own).transpose(3, 1, 0, 2)
    grad_qkv = grad_qkv.reshape(own, 3, heads_loc * HD)
    grad_in = grads[:, :hid].astype(F32)
    grad_out = grads[:, hid:].astype(F32).T
    grad_o = grads_a[features:].astype(BF).reshape(4, heads_loc * HD, own)
    grad_o = jnp.sum(lax.all_to_all(grad_o, "mp", 0, 0, tiled=True).astype(F32), axis=0)
    small_out = small[: experts + 2].T
    return (
        output,
        grad_tokens,
        jnp.stack([small[experts + 4], small[experts + 2]]),
        jnp.stack([small[experts + 5], small[experts + 3]]),
        grad_qkv,
        grad_o,
        grad_in,
        grad_out,
        small_out[:, :experts],
        small_out[:, experts:],
        grad_up[None],
        grad_down[None],
    )


def solution(mesh):
    in_specs = (
        P("dp", None),
        P("dp", None),
        P(),
        P(),
        P(None, None, "mp"),
        P("mp", None),
        P(None, "mp"),
        P("mp", None),
        P(),
        P(),
        P("dp", None, "mp"),
        P("dp", "mp", None),
        P("dp", None),
        P(),
    )
    out_specs = (
        P("dp", None),
        P("dp", None),
        P(None, "dp"),
        P(None, "dp"),
        P("dp", None, "mp"),
        P("mp", "dp"),
        P("dp", "mp"),
        P("mp", "dp"),
        P("dp", None),
        P("dp", None),
        P("dp", None, "mp"),
        P("dp", "mp", None),
    )
    return jax.shard_map(body, mesh=mesh, in_specs=in_specs, out_specs=out_specs, check_vma=False)
```

```python
from functools import partial

import jax
import jax.numpy as jnp
from jax import lax
from jax.experimental import pallas as pl
from jax.experimental.pallas import tpu as pltpu
from jax.sharding import PartitionSpec as P

HD = 64
GROUP = 4
EPS = 1e-05
LOG2E = 1.4426950408889634
SCALE2 = 0.125 * LOG2E
HIDE = -1e30
BF = jnp.bfloat16
F32 = jnp.float32
LIGHT = pl.CostEstimate(flops=1 << 20, bytes_accessed=1 << 20, transcendentals=0)


def mm(a, b):
    return jnp.dot(a, b, preferred_element_type=F32)


def ein(spec, a, b):
    return jnp.einsum(spec, a, b, preferred_element_type=F32)


def call(kernel, name, prefetch, grid, in_specs, out_specs, out_shape, args, scratch=(), alias=None, vmem=48):
    return pl.pallas_call(
        kernel,
        grid_spec=pltpu.PrefetchScalarGridSpec(
            num_scalar_prefetch=1,
            grid=grid,
            in_specs=in_specs,
            out_specs=out_specs,
            scratch_shapes=list(scratch),
        ),
        out_shape=out_shape,
        input_output_aliases=alias or {},
        compiler_params=pltpu.CompilerParams(vmem_limit_bytes=vmem * 2**20),
        cost_estimate=LIGHT,
        name=name,
    )(prefetch, *args)


def fixed(shape):
    zeros = (0,) * len(shape)
    return pl.BlockSpec(shape, lambda *_: zeros)


def like(shape, dtype):
    return jax.ShapeDtypeStruct(shape, dtype)


def normalize(v):
    mean = jnp.mean(v, axis=-1, keepdims=True)
    centred = v - mean
    scale = lax.rsqrt(jnp.mean(centred * centred, axis=-1, keepdims=True) + EPS)
    return centred * scale, scale


def norm_back(grad, gain, normal, scale):
    g = grad * gain
    along = jnp.mean(g * normal, axis=-1, keepdims=True)
    return scale * (g - jnp.mean(g, axis=-1, keepdims=True) - normal * along)


def qkv_kernel(at_ref, x_ref, gain_ref, bias_ref, w_ref, a_ref, *outs):
    normal, _ = normalize(x_ref[...].astype(F32))
    a = (normal * gain_ref[...] + bias_ref[...]).astype(BF)
    a_ref[...] = a
    for s in range(GROUP):
        outs[s][...] = mm_t(w_ref[at_ref[0] ^ s], a).astype(BF)


def project(at, tokens, gain, bias, w_heads):
    rows, width = tokens.shape
    features = w_heads.shape[1]
    blk = min(256, rows)
    moving = pl.BlockSpec((blk, width), lambda i, n: (i, 0))
    return call(
        qkv_kernel,
        "project",
        at,
        (rows // blk,),
        [moving, fixed((1, width)), fixed((1, width)), fixed(w_heads.shape)],
        [moving] + [pl.BlockSpec((features, blk), lambda i, n: (0, i))] * GROUP,
        [like((rows, width), BF)] + [like((features, rows), BF)] * GROUP,
        (tokens, gain, bias, w_heads),
    )


def fill_keys(k_s, place, keys, first_len, blk):
    rows = place * blk + lax.broadcasted_iota(jnp.int32, (blk, 128), 0)
    lane = lax.broadcasted_iota(jnp.int32, (blk, 128), 1)
    wide = jnp.concatenate([keys.astype(F32).T, jnp.zeros((blk, 128 - HD), F32)], axis=1)
    wide = jnp.where((lane == HD) & (rows < first_len), HIDE, wide)
    k_s[pl.ds(place * blk, blk), :] = wide.astype(BF)


def wide_query(query, place, first_len, blk):
    cols = place * blk + lax.broadcasted_iota(jnp.int32, (128 - HD, blk), 1)
    sub = lax.broadcasted_iota(jnp.int32, (128 - HD, blk), 0)
    extra = jnp.where((sub == 0) & (cols >= first_len), 1.0, 0.0)
    return jnp.concatenate([query, extra.astype(BF)], axis=0)


def causal(blk):
    keys = lax.broadcasted_iota(jnp.int32, (blk, blk), 0)
    queries = lax.broadcasted_iota(jnp.int32, (blk, blk), 1)
    return keys <= queries


def attend_kernel(blk, per, at_ref, *refs):
    qkv_refs, o_refs = refs[:GROUP], refs[GROUP : 2 * GROUP]
    lse_ref, k_s, qkv_s = refs[2 * GROUP :]
    i = pl.program_id(0)
    place, first_len = at_ref[0], at_ref[3]

    @pl.when(i == 0)
    def _():
        for s in range(GROUP):
            qkv_s[place ^ s] = qkv_refs[s][...]

    def part(which, j):
        return qkv_s[j // per, HD * which : HD * (which + 1), pl.ds((j % per) * blk, blk)]

    fill_keys(k_s, i, part(1, i), first_len, blk)
    query = wide_query(part(0, i), i, first_len, blk)

    def scores(j):
        return mm(k_s[pl.ds(pl.multiple_of(j * blk, blk), blk), :], query)

    s = jnp.where(causal(blk), scores(i), HIDE)
    top = jnp.max(s, axis=0, keepdims=True)
    p = jnp.exp2((s - top) * SCALE2)
    total = jnp.sum(p, axis=0, keepdims=True)
    acc = mm(part(2, i), p.astype(BF))

    def step(j, carry):
        top, total, acc = carry
        s = scores(j)
        new = jnp.maximum(top, jnp.max(s, axis=0, keepdims=True))
        p = jnp.exp2((s - new) * SCALE2)
        keep = jnp.exp2((top - new) * SCALE2)
        total = total * keep + jnp.sum(p, axis=0, keepdims=True)
        acc = acc * keep + mm(part(2, j), p.astype(BF))
        return new, total, acc

    low = jnp.where(i * blk >= first_len, first_len // blk, 0)
    top, total, acc = lax.fori_loop(low, i, step, (top, total, acc))
    out = (acc / total).astype(BF)
    for s in range(GROUP):

        @pl.when((i // per) ^ place == s)
        def _():
            o_refs[s][:, pl.ds((i % per) * blk, blk)] = out

    lse_ref[0] = top * SCALE2 + jnp.log2(total)


def attend(at, qkv):
    features, rows = qkv[0].shape
    blk = min(512, rows)
    per = rows // blk
    count = GROUP * per
    return call(
        partial(attend_kernel, blk, per),
        "attend",
        at,
        (count,),
        [fixed((features, rows))] * GROUP,
        [fixed((HD, rows))] * GROUP + [pl.BlockSpec((1, 1, blk), lambda i, n: (i, 0, 0))],
        [like((HD, rows), BF)] * GROUP + [like((count, 1, blk), F32)],
        qkv,
        scratch=[pltpu.VMEM((GROUP * rows, 128), BF), pltpu.VMEM((GROUP, features, rows), BF)],
    )


def back_kernel(blk, per, first, count, at_ref, *refs):
    qkv_refs, do_refs, o_refs = refs[:GROUP], refs[GROUP : 2 * GROUP], refs[2 * GROUP : 3 * GROUP]
    lse_ref, refs = refs[3 * GROUP], refs[3 * GROUP + 1 :]
    if first:
        dq_in_ref, refs = refs[1], refs[2:]
    out_ref, dq_ref, k_s, kt_s, v_s, wide_s, dot_s, both_s, delta_s, acc_s = refs
    at_first = pl.program_id(0) == 0
    j = first + pl.program_id(0)
    place, first_len = at_ref[0], at_ref[3]

    @pl.when(at_first)
    def _():
        dq_ref[...] = dq_in_ref[...] if first else jnp.zeros(dq_ref.shape, F32)
        zero = jnp.zeros((blk, HD), F32)
        for s in range(GROUP):

            @pl.when((place ^ s) * per >= first)
            def _():
                for sub in range(per):
                    i = (place ^ s) * per + sub
                    at = pl.ds(pl.multiple_of(i * blk, blk), blk)
                    cut = slice(sub * blk, (sub + 1) * blk)
                    query = qkv_refs[s][0:HD, cut]
                    keys = qkv_refs[s][HD : 2 * HD, cut]
                    grad = do_refs[s][:, cut]
                    fill_keys(k_s, i, keys, first_len, blk)
                    kt_s[:, at] = keys
                    dot_s[:, at] = grad
                    wide_s[:, at] = wide_query(query, i, first_len, blk)
                    grad = grad.astype(F32)
                    values = qkv_refs[s][2 * HD :, cut].astype(F32)
                    v_s[at, :] = jnp.concatenate([values.T, zero], axis=1).astype(BF)
                    both_s[0, at, :] = jnp.concatenate([grad.T, zero], axis=1).astype(BF)
                    both_s[1, at, :] = jnp.concatenate([zero, query.astype(F32).T], axis=1).astype(BF)
                    held = o_refs[s][:, cut].astype(F32)
                    delta_s[i] = jnp.sum(held * grad, axis=0, keepdims=True)

    here = pl.ds(pl.multiple_of(j * blk, blk), blk)
    keys_t = kt_s[:, here]
    values = v_s[here, 0:HD]

    def pair(i, diagonal):
        at = pl.ds(pl.multiple_of(i * blk, blk), blk)
        s = mm(k_s[here, :], wide_s[:, at])
        p = jnp.exp2(s * SCALE2 - lse_ref[i])
        if diagonal:
            p = jnp.where(causal(blk), p, 0.0)
        dp = mm(values, dot_s[:, at])
        ds = (p * (dp - delta_s[i])).astype(BF)
        dq_ref[:, at] += mm(keys_t, ds)
        return mm(p.astype(BF), both_s[0, at, :]) + mm(ds, both_s[1, at, :])

    acc_s[...] = pair(j, True)

    def step(i, carry):
        acc_s[...] += pair(i, False)
        return carry

    high = jnp.where((j + 1) * blk <= first_len, (first_len + blk - 1) // blk, count)
    lax.fori_loop(j + 1, high, step, 0)
    both = acc_s[...].T
    out_ref[0, 0:HD, :] = (dq_ref[:, here] * 0.125).astype(BF)
    out_ref[0, HD : 2 * HD, :] = (both[HD:, :] * 0.125).astype(BF)
    out_ref[0, 2 * HD :, :] = both[:HD, :].astype(BF)


def attend_back(at, qkv, do, o, lse, before, first, last):
    features, rows = qkv[0].shape
    blk = min(512, rows)
    per = rows // blk
    count = GROUP * per
    dq_shape = (HD, GROUP * rows)
    carried = [pl.BlockSpec(memory_space=pl.ANY), fixed(dq_shape)] if first else []
    return call(
        partial(back_kernel, blk, per, first * per, count),
        "attend_back",
        at,
        ((last - first) * per,),
        [fixed((features, rows))] * GROUP
        + [fixed((HD, rows))] * (2 * GROUP)
        + [fixed((count, 1, blk))]
        + carried,
        [
            pl.BlockSpec((1, features, blk), lambda j, n: ((first + j // per) ^ n[0], 0, j % per)),
            fixed(dq_shape),
        ],
        [like((GROUP, features, rows), BF), like(dq_shape, F32)],
        (*qkv, *do, *o, lse, *(before if first else ())),
        scratch=[
            pltpu.VMEM((GROUP * rows, 128), BF),
            pltpu.VMEM((HD, GROUP * rows), BF),
            pltpu.VMEM((GROUP * rows, 128), BF),
            pltpu.VMEM((128, GROUP * rows), BF),
            pltpu.VMEM((HD, GROUP * rows), BF),
            pltpu.VMEM((2, GROUP * rows, 128), BF),
            pltpu.VMEM((count, 1, blk), F32),
            pltpu.VMEM((blk, 128), F32),
        ],
        alias={3 * GROUP + 2: 0} if first else None,
    )


def split_kernel(at_ref, *refs):
    ins, outs = refs[:GROUP], refs[GROUP:]
    cols = outs[0].shape[1]
    for r in range(4):
        lanes = pl.ds(pl.multiple_of(((at_ref[1] + r) % 4) * cols, cols), cols)
        for s in range(GROUP):
            head = pl.ds(pl.multiple_of((at_ref[0] ^ s) * HD, HD), HD)
            outs[r][head, :] = ins[s][:, lanes]


def split(at, heads):
    rows = heads[0].shape[1]
    shape = (GROUP * HD, rows // 4)
    return call(
        split_kernel,
        "split",
        at,
        (1,),
        [fixed((HD, rows))] * GROUP,
        [fixed(shape)] * 4,
        [like(shape, BF)] * 4,
        heads,
    )


def unsplit_kernel(at_ref, *refs):
    ins, outs = refs[:4], refs[4:]
    cols = ins[0].shape[1]
    for r in range(4):
        lanes = pl.ds(pl.multiple_of(((at_ref[1] + r) % 4) * cols, cols), cols)
        for s in range(GROUP):
            head = pl.ds(pl.multiple_of((at_ref[0] ^ s) * HD, HD), HD)
            outs[s][:, lanes] = ins[r][head, :]


def unsplit(at, pieces):
    shape = (HD, 4 * pieces[0].shape[1])
    return call(
        unsplit_kernel,
        "unsplit",
        at,
        (1,),
        [fixed(pieces[0].shape)] * 4,
        [fixed(shape)] * GROUP,
        [like(shape, BF)] * GROUP,
        pieces,
    )


def heads_of(mine, r, features):
    return pl.ds(pl.multiple_of(((mine + 4 - r) % 4) * features, features), features)


def mid_kernel(at_ref, *refs):
    o_refs, (w_ref, x_ref, gain_ref, bias_ref, h_ref, b_ref) = refs[:4], refs[4:]
    h = x_ref[...].astype(F32)
    for r in range(4):
        rows = heads_of(at_ref[1], r, o_refs[r].shape[0])
        h = h + mm(o_refs[r][...].astype(F32).T.astype(BF), w_ref[rows, :])
    h_ref[...] = h
    normal, _ = normalize(h)
    b_ref[...] = (normal * gain_ref[...] + bias_ref[...]).astype(BF)


def mid(at, o, w_o, tokens, gain, bias):
    features, quarter = o[0].shape
    width = tokens.shape[1]
    return call(
        mid_kernel,
        "mid",
        at,
        (1,),
        [fixed((features, quarter))] * 4
        + [fixed(w_o.shape)]
        + [pl.BlockSpec((quarter, width), lambda i, n: (n[1], 0))]
        + [fixed((1, width))] * 2,
        [fixed((quarter, width))] * 2,
        [like((quarter, width), F32), like((quarter, width), BF)],
        (*o, w_o, tokens, gain, bias),
    )


def add_up(refs):
    total = refs[0][...]
    for ref in refs[1:]:
        total = total + ref[...].astype(F32)
    return total


def mid_back_kernel(at_ref, *refs):
    shares, (w_ref, h_ref, dy_ref, gain_ref, dh_ref, low_ref, sums_ref) = refs[:4], refs[4:11]
    do_refs = refs[11:]
    db = add_up(shares)
    normal, scale = normalize(h_ref[...])
    dh = dy_ref[...].astype(F32) + norm_back(db, gain_ref[...], normal, scale)
    dh_ref[...] = dh
    low = dh.astype(BF)
    low_ref[...] = low
    sums_ref[0:1, :] = jnp.sum(db * normal, axis=0, keepdims=True)
    sums_ref[1:2, :] = jnp.sum(db, axis=0, keepdims=True)
    for r in range(4):
        rows = heads_of(at_ref[1], r, do_refs[r].shape[0])
        do_refs[r][...] = mm_t(w_ref[rows, :], low).astype(BF)


def mid_back(at, shares, w_o, h, dy, gain):
    quarter, width = h.shape
    whole = fixed((quarter, width))
    piece = (w_o.shape[0] // 4, quarter)
    return call(
        mid_back_kernel,
        "mid_back",
        at,
        (1,),
        [whole] * 4 + [fixed(w_o.shape), whole, whole, fixed((1, width))],
        [whole] * 2 + [fixed((2, width))] + [fixed(piece)] * 4,
        [like((quarter, width), F32), like((quarter, width), BF), like((2, width), F32)]
        + [like(piece, BF)] * 4,
        (*shares, w_o, h, dy, gain),
    )


def first_back_kernel(at_ref, *refs):
    shares = refs[:4]
    x_ref, dh_ref, gain_ref, out_ref = refs[4:]
    d_a = add_up(shares)
    normal, scale = normalize(x_ref[...].astype(F32))
    out_ref[...] = (dh_ref[...] + norm_back(d_a, gain_ref[...], normal, scale)).astype(BF)


def first_back(at, shares, tokens, dh, gain):
    quarter, width = dh.shape
    return call(
        first_back_kernel,
        "first_back",
        at,
        (1,),
        [fixed((quarter, width))] * 4
        + [pl.BlockSpec((quarter, width), lambda i, n: (n[1], 0))]
        + [fixed((quarter, width)), fixed((1, width))],
        fixed((quarter, width)),
        like((quarter, width), BF),
        (*shares, tokens, dh, gain),
    )


def in_order(mine, own, right, left, far, right_two, left_two):
    one = jnp.where(mine == 3, far, left)
    two = jnp.where(mine < 2, left_two, right_two)
    three = jnp.where(mine == 0, far, right)
    return own, one, two, three


def one_hot(slots, dest):
    return jnp.where(slots == dest, 1.0, 0.0).astype(BF)


def dispatch_kernel(joined, at_ref, dest_ref, *refs):
    pieces, out_ref, spread_s = refs[:joined], refs[joined], refs[-1]
    blk, rows = min(256, spread_s.shape[0]), dest_ref.shape[1]

    @pl.when(pl.program_id(0) == 0)
    def _():
        slot = lax.broadcasted_iota(jnp.int32, (blk, rows), 0)
        for start in range(0, spread_s.shape[0], blk):
            spread_s[start : start + blk, :] = one_hot(slot + start, dest_ref[...])

    if joined == 1:
        rows_ref = pieces[0]
    else:
        rows_ref = refs[joined + 1]
        start = 0
        for piece in in_order(at_ref[1], *[ref[...] for ref in pieces]):
            rows_ref[start : start + piece.shape[0], :] = piece
            start += piece.shape[0]
    out_ref[...] = mm(spread_s[...], rows_ref[...]).astype(BF)


def columns(rows, width):
    return pl.BlockSpec((rows, width), lambda i, n: (0, i))


def dispatch(at, dest_row, pieces, slots):
    rows, width = dest_row.shape[1], pieces[0].shape[1]
    blk = min(256, width)
    joined = len(pieces) > 1
    return call(
        partial(dispatch_kernel, len(pieces)),
        "dispatch",
        at,
        (width // blk,),
        [fixed((1, rows))] + [columns(piece.shape[0], blk) for piece in pieces],
        [columns(slots, blk)] + [columns(rows, blk)] * joined,
        [like((slots, width), BF)] + [like((rows, width), BF)] * joined,
        (dest_row, *pieces),
        scratch=[pltpu.VMEM((slots, rows), BF)],
    )


def join_kernel(at_ref, *refs):
    pieces, out_ref = refs[:6], refs[6]
    r = pl.program_id(0)
    for place, piece in enumerate(in_order(at_ref[1], *[ref[...] for ref in pieces])):

        @pl.when(r == place)
        def _():
            out_ref[...] = piece


def join(at, pieces):
    each, width = pieces[0].shape
    return call(
        join_kernel,
        "join",
        at,
        (4,),
        [fixed((each, width))] * 6,
        pl.BlockSpec((each, width), lambda r, n: ((n[1] + r) % 4, 0)),
        like((4 * each, width), BF),
        pieces,
    )


def write_shares(mine, total, own_ref, one_ref, two_ref, three_ref, end_ref):
    rows = own_ref.shape[0]
    own_ref[...] = total[:rows]
    one, two, three = [total[r * rows : (r + 1) * rows].astype(BF) for r in (1, 2, 3)]
    one_ref[...] = one
    two_ref[...] = two
    three_ref[...] = three
    end_ref[...] = jnp.where(mine == 0, three, one)


def share_shapes(rows, width):
    return [like((rows, width), F32)] + [like((rows, width), BF)] * 4


def combine_kernel(count, whole, at_ref, *refs):
    dests, backs = refs[:count], refs[count : 2 * count]
    base_ref, refs, pick_s = refs[2 * count], refs[2 * count + 1 : -1], refs[-1]
    rows, slots = base_ref.shape[0], backs[0].shape[0]
    blk = rows // 4

    @pl.when(pl.program_id(0) == 0)
    def _():
        lane = lax.broadcasted_iota(jnp.int32, (blk, slots), 1)
        for k in range(count):
            for start in range(0, rows, blk):
                dest = dests[k][start : start + blk, :]
                pick_s[start : start + blk, k * slots : (k + 1) * slots] = one_hot(lane, dest)

    total = base_ref[...].astype(F32)
    for k in range(count):
        total = total + mm(pick_s[:, k * slots : (k + 1) * slots], backs[k][...])
    mine = at_ref[1]
    if whole:
        h_ref, out_ref = refs
        for r in range(4):
            part = total[r * blk : (r + 1) * blk]
            if r == 0:
                part = part + h_ref[...]
            place = pl.ds(pl.multiple_of(((mine + r) % 4) * blk, blk), blk)
            out_ref[place, :] = part.astype(BF)
    else:
        write_shares(mine, total, *refs)


def combine(at, dests, backs, base, h=None):
    count, (slots, width), rows = len(backs), backs[0].shape, base.shape[0]
    blk = min(256, width)
    whole = h is not None
    quarter = columns(rows // 4, blk)
    return call(
        partial(combine_kernel, count, whole),
        "combine",
        at,
        (width // blk,),
        [fixed((rows, 1))] * count
        + [columns(slots, blk)] * count
        + [columns(rows, blk)]
        + [quarter] * whole,
        columns(rows, blk) if whole else [quarter] * 5,
        like(base.shape, BF) if whole else share_shapes(rows // 4, width),
        (*dests, *backs, base) + ((h,) if whole else ()),
        scratch=[pltpu.VMEM((rows, count * slots), BF)],
    )


def mm_t(a, b):
    return lax.dot_general(a, b, (((1,), (1,)), ((), ())), preferred_element_type=F32)


def gelu_both(u):
    c = 0.7978845608028654
    square = u * u
    t = jnp.tanh(u * (c + (c * 0.044715) * square))
    half = 0.5 + 0.5 * t
    slope = half + (0.5 * u) * (1.0 - t * t) * (c + (3.0 * c * 0.044715) * square)
    return u * half, slope


def high_low(value):
    high = value.astype(BF)
    return high, (value - high.astype(F32)).astype(BF)


def two_coefs(logits, lane, experts):
    inside = (lane >= experts) & (lane < experts + 2)
    top = jnp.max(jnp.where(inside, logits, HIDE), axis=1, keepdims=True)
    e = jnp.where(inside, jnp.exp(logits - top), 0.0)
    e = e / jnp.sum(e, axis=1, keepdims=True)
    first = jnp.sum(jnp.where(lane == experts, e, 0.0), axis=1, keepdims=True)
    second = jnp.sum(jnp.where(lane == experts + 1, e, 0.0), axis=1, keepdims=True)
    return first, second


def small_back(d_small, rows, w_small_ref, small_ref, i):
    high, low = high_low(d_small)
    w_small = w_small_ref[...]
    high_t, low_t = high_low(d_small.T)

    @pl.when(i == 0)
    def _():
        small_ref[...] = jnp.zeros(small_ref.shape, F32)

    small_ref[...] += mm(high_t, rows) + mm(low_t, rows)
    return mm_t(high, w_small) + mm_t(low, w_small)


def expert_kernel(experts, half, at_ref, rows_ref, dy_ref, up_ref, down_ref, w_small_ref, *outs):
    if half:
        outs = outs[5:]
    rows_out_ref, hid_ref, dy_out_ref, deu_ref, y_ref, d_rows_ref, small_ref = outs
    rows = rows_ref[...]
    rows_out_ref[...] = rows
    up = mm(rows, up_ref[...])
    logits = mm(rows, w_small_ref[...])
    lane = lax.broadcasted_iota(jnp.int32, logits.shape, 1)
    routed = lane < experts
    top = jnp.max(jnp.where(routed, logits, HIDE), axis=1, keepdims=True)
    probs = jnp.where(routed, jnp.exp(logits - top), 0.0)
    probs = probs / jnp.sum(probs, axis=1, keepdims=True)
    own = jnp.where(lane == at_ref[2], 1.0, 0.0)
    gate = jnp.sum(probs * own, axis=1, keepdims=True)
    first, second = two_coefs(logits, lane, experts)
    weight = second * gate
    dy = dy_ref[...].reshape(rows.shape).astype(F32)
    d_y = (weight * dy).astype(BF)
    dy_out_ref[...] = d_y
    d_hidden = mm_t(d_y, down_ref[...])
    hidden, slope = gelu_both(up)
    hidden = hidden.astype(BF)
    hid_ref[...] = hidden
    d_up = (d_hidden * slope).astype(BF)
    deu_ref[...] = d_up
    y = mm(hidden, down_ref[...])
    y_ref[...] = (weight * y).astype(BF).reshape(y_ref.shape)
    along = gate * jnp.sum(dy * y, axis=1, keepdims=True)
    mixed = first * second * along
    d_small = (second * along) * (own - probs)
    d_small = jnp.where(routed, d_small, 0.0)
    d_small = d_small + jnp.where(lane == experts + 1, mixed, 0.0)
    d_small = d_small - jnp.where(lane == experts, mixed, 0.0)
    d_rows = mm_t(d_up, up_ref[...]) + small_back(d_small, rows, w_small_ref, small_ref, pl.program_id(0))
    d_rows_ref[...] = d_rows.astype(BF)


def expert_rows(at, rows, dy, w_up, w_down, w_small, experts, half, before):
    count, width = rows.shape
    hid, lanes = w_up.shape[1], w_small.shape[1]
    blk = min(512, count)
    capacity = count // dy.shape[0]
    steps = count // blk
    moving = pl.BlockSpec((blk, width), lambda i, n: (i, 0))
    slots = pl.BlockSpec((blk // capacity, capacity, width), lambda i, n: (i, half, 0))
    kept = [pl.BlockSpec((blk, size), lambda i, n: (i + half * steps, 0)) for size in (width, hid, width, hid)]
    return call(
        partial(expert_kernel, experts, half),
        "expert_rows",
        at,
        (steps,),
        [
            moving,
            slots,
            fixed((width, hid)),
            fixed((hid, width)),
            fixed((width, lanes)),
        ]
        + [pl.BlockSpec(memory_space=pl.ANY)] * (5 * half),
        kept + [slots, moving, fixed((lanes, width))],
        [like((2 * count, size), BF) for size in (width, hid, width, hid)]
        + [like(dy.shape, BF), like((count, width), BF)]
        + [like((lanes, width), F32)],
        (rows, dy, w_up, w_down, w_small, *before),
        alias={6 + k: k for k in range(5)} if half else None,
        vmem=56,
    )


def dense_kernel(experts, at_ref, rows_ref, dy_ref, in_ref, out_ref, w_small_ref, *outs):
    hid_ref, grad_ref, d_up_ref, mix_ref, db_ref, small_ref = outs
    rows = rows_ref[...]
    up = mm(rows, in_ref[...])
    logits = mm(rows, w_small_ref[...])
    lane = lax.broadcasted_iota(jnp.int32, logits.shape, 1)
    first, second = two_coefs(logits, lane, experts)
    dy = dy_ref[...].astype(F32)
    grad = (first * dy).astype(BF)
    grad_ref[...] = grad
    d_hidden = mm_t(grad, out_ref[...])
    hidden, slope = gelu_both(up)
    hidden = hidden.astype(BF)
    hid_ref[...] = hidden
    d_up = (d_hidden * slope).astype(BF)
    d_up_ref[...] = d_up
    dense = mm(hidden, out_ref[...])
    mix_ref[...] = first * dense
    mixed = first * second * jnp.sum(dy * dense, axis=1, keepdims=True)
    d_small = jnp.where(lane == experts, mixed, 0.0) - jnp.where(lane == experts + 1, mixed, 0.0)
    db_ref[...] = mm_t(d_up, in_ref[...]) + small_back(d_small, rows, w_small_ref, small_ref, pl.program_id(0))


def dense_rows(at, rows, dy, w_in, w_out, w_small, experts):
    (count, width), hid, lanes = rows.shape, w_in.shape[1], w_small.shape[1]
    blk = min(512, count)
    row_out = pl.BlockSpec((blk, width), lambda i, n: (i, 0))
    hid_out = pl.BlockSpec((blk, hid), lambda i, n: (i, 0))
    return call(
        partial(dense_kernel, experts),
        "dense_rows",
        at,
        (count // blk,),
        [row_out, row_out, fixed((width, hid)), fixed((hid, width)), fixed((width, lanes))],
        [hid_out, row_out, hid_out, row_out, row_out, fixed((lanes, width))],
        [
            like((count, hid), BF),
            like((count, width), BF),
            like((count, hid), BF),
            like((count, width), F32),
            like((count, width), F32),
            like((lanes, width), F32),
        ],
        (rows, dy, w_in, w_out, w_small),
        vmem=56,
    )


def turned(value):
    return value.astype(F32).T.astype(BF)


def dense_grads_kernel(at_ref, b_ref, d_up_ref, grad_ref, hid_ref, out_ref):
    width = d_up_ref.shape[1]
    blk = out_ref.shape[1]
    parts = out_ref.shape[0]
    first = mm(turned(b_ref[...]), d_up_ref[...]).astype(BF)
    second = mm(turned(grad_ref[...]), hid_ref[...]).astype(BF)
    for k in range(parts):
        out_ref[k, :, :width] = first[k * blk : (k + 1) * blk]
        out_ref[k, :, width:] = second[k * blk : (k + 1) * blk]


def dense_grads(at, b, d_up, grad, hidden, parts):
    (rows, width), hid = b.shape, hidden.shape[1]
    blk = min(256, width)
    own = width // parts
    column = pl.BlockSpec((rows, blk), lambda i, n: (0, i))
    return call(
        dense_grads_kernel,
        "dense_grads",
        at,
        (width // blk,),
        [column, fixed((rows, hid)), column, fixed((rows, hid))],
        pl.BlockSpec((blk // own, own, 2 * hid), lambda i, n: (i, 0, 0)),
        like((parts, own, 2 * hid), BF),
        (b, d_up, grad, hidden),
    )


def attention_grads_kernel(experts, at_ref, *refs):
    grads, o_refs, refs = refs[:GROUP], refs[GROUP : GROUP + 4], refs[GROUP + 4 :]
    a_ref, dh_ref, w_ref, gain_ref, bias_ref, sums_ref = refs[:6]
    small_refs, (out_ref, all_s) = refs[6:-2], refs[-2:]
    heads, features = GROUP * HD, grads[1].shape[0]
    products, plain = 0.0, 0.0
    for k in range(GROUP):
        head = at_ref[0] ^ k
        rows = pl.ds(pl.multiple_of(head * features, features), features)
        grad = grads[k][...]
        grad = grad[0] if k == 0 else grad
        weight = w_ref[head].astype(F32)
        total = mm(grad, a_ref[...])
        all_s[rows, :] = total
        each = jnp.sum(grad.astype(F32), axis=1, keepdims=True)
        products = products + jnp.sum(total * weight, axis=0, keepdims=True)
        plain = plain + jnp.sum(each * weight, axis=0, keepdims=True)
    first = GROUP * features
    for r in range(4):
        rows = pl.ds(pl.multiple_of(first + ((at_ref[1] + 4 - r) % 4) * heads, heads), heads)
        all_s[rows, :] = mm(o_refs[r][...], dh_ref[...])
    first += 4 * heads
    small = add_up(small_refs)
    row = lax.broadcasted_iota(jnp.int32, small.shape, 0)
    d_gain = (products - bias_ref[...] * plain) / gain_ref[...]
    for k, sums in enumerate((sums_ref[0:1, :], sums_ref[1:2, :], d_gain, plain)):
        small = jnp.where(row == experts + 2 + k, sums, small)
    all_s[first:, :] = small
    out_ref[...] = all_s[...].T.astype(BF)


def attention_grads(at, held, came, o, a, dh, w_heads, gain, bias, sums, small, experts):
    rows, width = a.shape
    features, lanes = held.shape[1], small[0].shape[0]
    height = GROUP * features + 4 * o[0].shape[0] + lanes
    blk = min(256, width)
    return call(
        partial(attention_grads_kernel, experts),
        "attention_grads",
        at,
        (width // blk,),
        [fixed((1, features, rows))]
        + [fixed((features, rows))] * 3
        + [fixed(o[0].shape)] * 4
        + [columns(rows, blk), columns(dh.shape[0], blk)]
        + [pl.BlockSpec((GROUP, features, blk), lambda i, n: (0, 0, i))]
        + [columns(1, blk)] * 2
        + [columns(2, blk)]
        + [columns(lanes, blk)] * len(small),
        pl.BlockSpec((blk, height), lambda i, n: (i, 0)),
        like((width, height), BF),
        (held, *came, *o, a, dh, w_heads, gain, bias, sums, *small),
        scratch=[pltpu.VMEM((height, blk), F32)],
    )


def project_kernel(at_ref, *refs):
    grads, w_ref, outs, turned_s = refs[:GROUP], refs[GROUP], refs[GROUP + 1 : -1], refs[-1]
    rows = turned_s.shape[1]
    blk = rows // 4

    @pl.when(pl.program_id(0) == 0)
    def _():
        for s in range(GROUP):
            for r in range(4):
                lanes = pl.ds(pl.multiple_of(((at_ref[1] + r) % 4) * blk, blk), blk)
                grad = grads[s][0, :, lanes] if s == 0 else grads[s][:, lanes]
                turned_s[s, r * blk : (r + 1) * blk, :] = turned(grad)

    total = 0.0
    for s in range(GROUP):
        total = total + mm(turned_s[s], w_ref[at_ref[0] ^ s])
    write_shares(at_ref[1], total, *outs)


def project_back(at, held, came, w_heads):
    _, features, rows = held.shape
    width = w_heads.shape[2]
    blk = min(256, width)
    return call(
        project_kernel,
        "project_back",
        at,
        (width // blk,),
        [fixed((1, features, rows))]
        + [fixed((features, rows))] * 3
        + [pl.BlockSpec((GROUP, features, blk), lambda i, n: (0, 0, i))],
        [columns(rows // 4, blk)] * 5,
        share_shapes(rows // 4, width),
        (held, *came, w_heads),
        scratch=[pltpu.VMEM((GROUP, rows, features), BF)],
    )


def hop(value, *pairs):
    return lax.ppermute(value, "mp", pairs)


def rotate(value, steps):
    return hop(value, *[(s, (s + steps) % 4) for s in range(4)])


def gather_near(own):
    right = hop(own, (0, 1), (1, 2), (2, 3))
    left = hop(own, (1, 0), (2, 1), (3, 2))
    return own, right, left, hop(own, (0, 3), (3, 0))


def gather_far(near):
    _, right, left, _ = near
    return *near, hop(right, (1, 2), (2, 3)), hop(left, (1, 0), (2, 1))


def gather_pieces(own):
    return gather_far(gather_near(own))


def scatter_far(shares):
    _, _, two, _, end = shares
    return hop(two, (2, 1), (3, 2)), hop(two, (0, 1), (1, 2)), hop(end, (0, 3), (3, 0))


def scatter_near(shares, came):
    own, one, _, three, _ = shares
    from_right, from_left, from_end = came
    three = (three.astype(F32) + from_right.astype(F32)).astype(BF)
    one = (one.astype(F32) + from_left.astype(F32)).astype(BF)
    return own, hop(three, (1, 0), (2, 1), (3, 2)), hop(one, (0, 1), (1, 2), (2, 3)), from_end


def group_swap(value, s):
    count = lax.axis_size("dp")
    return lax.ppermute(value, "dp", [(t, t ^ s) for t in range(count)])


def expert_swap(value, experts):
    wide = value.reshape(experts, value.shape[0] // experts, value.shape[1])
    return lax.all_to_all(wide, "dp", 0, 0, tiled=True).reshape(value.shape)


def roll_rows(value, start):
    twice = jnp.concatenate([value, value], axis=0)
    return lax.dynamic_slice_in_dim(twice, start, value.shape[0], 0)


def halve(value, bit):
    pairs = value.reshape(value.shape[0] // 2, 2, *value.shape[1:])
    own = (lax.axis_index("dp") // bit) % 2
    keep = lax.dynamic_index_in_dim(pairs, own, 1, keepdims=False)
    return keep, lax.dynamic_index_in_dim(pairs, 1 - own, 1, keepdims=False)


def add_halves(keep, came):
    return (keep.astype(F32) + came.astype(F32)).astype(BF)


def body(
    tokens,
    cotangent,
    ln_gains,
    ln_biases,
    w_qkv,
    w_o,
    w_in,
    w_out,
    w_router,
    w_coef,
    w_up,
    w_down,
    routes,
    long_group,
):
    rows, width = tokens.shape
    dps = lax.axis_size("dp")
    mine, position = lax.axis_index("mp"), lax.axis_index("dp")
    quarter = rows // 4
    start = mine * quarter
    heads_loc = w_qkv.shape[2] // HD
    hid = w_in.shape[1]
    experts = w_router.shape[1]
    capacity = max(2, 2 * rows // experts)
    half = capacity // 2
    barrier = lax.optimization_barrier
    first_len = lax.dynamic_index_in_dim(long_group, position // GROUP, 0, keepdims=False)
    at = jnp.stack([position % GROUP, mine, position, first_len]).astype(jnp.int32)
    gains = [ln_gains[0:1], ln_gains[1:2]]
    biases = [ln_biases[0:1], ln_biases[1:2]]
    w_o_all = lax.all_gather(w_o, "mp", axis=0, tiled=True)

    w_heads = w_qkv.reshape(width, 3, heads_loc, HD).transpose(2, 1, 3, 0)
    w_heads = w_heads.reshape(heads_loc, 3 * HD, width)
    a_r, *qkv = project(at, tokens, gains[0], biases[0], w_heads)
    qkv = [qkv[0]] + [group_swap(qkv[s], s) for s in (1, 2, 3)]

    route = roll_rows(routes, start)[:, 0]
    picked = (route[:, None] == jnp.arange(experts, dtype=jnp.int32)[None, :]).astype(jnp.int32)
    slot = jnp.sum((jnp.cumsum(picked, axis=0) - picked) * picked, axis=1)
    dy_b = roll_rows(cotangent, start)
    send_dy = dispatch(at, (route * capacity + slot)[None, :], [dy_b], experts * capacity)[0]
    *qkv, send_dy = barrier((*qkv, send_dy))
    in_half = [slot < half, slot >= half]
    dests = [
        jnp.where(in_half[k], route * half + slot - k * half, -1).astype(jnp.int32) for k in (0, 1)
    ]

    *o_t, lse = attend(at, qkv)
    *o_t, w_o_all = barrier((*o_t, w_o_all))
    o_heads = [o_t[0]] + [group_swap(o_t[s], s) for s in (1, 2, 3)]
    pieces = split(at, o_heads)
    o_q = [pieces[0]] + [rotate(pieces[r], r) for r in (1, 2, 3)]
    o_q[1], send_dy = barrier((o_q[1], send_dy))
    got_dy = expert_swap(send_dy, experts).reshape(experts, capacity, width)
    h, b_q = mid(at, o_q, w_o_all, tokens, gains[1], biases[1])

    pieces = gather_pieces(b_q)
    lanes = -(-(experts + 2) // 128) * 128
    w_small = jnp.concatenate(
        [w_router, w_coef, jnp.zeros((width, lanes - experts - 2), BF)], axis=1
    )
    send_0, b_r = dispatch(at, dests[0][None, :], pieces, experts * half)
    send_0, got_dy = barrier((send_0, got_dy))
    got_0 = expert_swap(send_0, experts)
    send_1 = dispatch(at, dests[1][None, :], [b_r], experts * half)[0]
    b_r, send_1 = barrier((b_r, send_1))
    hidden, dense_grad, d_up, mix_base, db_base, small_t = dense_rows(
        at, b_r, dy_b, w_in, w_out, w_small, experts
    )
    send_1, got_0, db_base = barrier((send_1, got_0, db_base))
    got_1 = expert_swap(send_1, experts)

    *kept, d_rows_0, small_0 = expert_rows(
        at, got_0, got_dy, w_up[0], w_down[0], w_small, experts, 0, ()
    )
    back_0 = expert_swap(d_rows_0, experts)
    *kept, d_rows_1, small_1 = expert_rows(
        at, got_1, got_dy, w_up[0], w_down[0], w_small, experts, 1, kept
    )
    got, hidden_e, d_y, d_eu, back_y = kept
    back_1 = expert_swap(d_rows_1, experts)
    d_rows_1, b_r = barrier((d_rows_1, b_r))
    grads = dense_grads(at, b_r, d_up, dense_grad, hidden, dps)
    back_0, back_1, grads, back_y = barrier((back_0, back_1, grads, back_y))

    dest_cols = [dest[:, None] for dest in dests]
    shares = combine(at, dest_cols, [back_0, back_1], db_base)
    far = scatter_far(shares)
    f_0, back_y, grads = barrier((far[0], back_y, grads))
    tok_y = expert_swap(back_y.reshape(experts * capacity, width), experts)
    shares = scatter_near(shares, (f_0, far[1], far[2]))
    dh, dh_r, sums_2, *do_q = mid_back(at, shares, w_o_all, h, dy_b[:quarter], gains[1])
    do_heads = unsplit(at, [do_q[0]] + [rotate(do_q[r], -r) for r in (1, 2, 3)])
    do_t = [do_heads[0]] + [group_swap(do_heads[s], s) for s in (1, 2, 3)]
    keep_1, give = halve(grads, 1)
    came_1 = group_swap(give, 1)

    mix = combine(at, [(route * capacity + slot)[:, None]], [tok_y], mix_base, h)
    keep_2, give = halve(add_halves(keep_1, came_1), 2)
    *do_t, mix, keep_2, give = barrier((*do_t, mix, keep_2, give))
    output = lax.psum(mix, "mp")
    came_2 = group_swap(give, 2)
    d_qkv, _ = attend_back(at, qkv, do_t, o_t, lse, None, 0, GROUP)
    d_qkv, keep_2, came_2 = barrier((d_qkv, keep_2, came_2))

    came = [group_swap(d_qkv[s], s) for s in (1, 2, 3)]
    d_qkv, got, hidden_e, d_y, d_eu = barrier((d_qkv, got, hidden_e, d_y, d_eu))
    grad_down = ein("rf,rd->fd", hidden_e, d_y)
    *came, grad_down = barrier((*came, grad_down))
    shares = project_back(at, d_qkv, came, w_heads)
    far = scatter_far(shares)
    grad_up = ein("rd,rf->df", got, d_eu)
    f_0, d_qkv, grad_up = barrier((far[0], d_qkv, grad_up))
    grads_a = attention_grads(
        at, d_qkv, came, o_q, a_r, dh_r, w_heads, gains[0], biases[0], sums_2, (small_0, small_1, small_t), experts
    )
    grads_a, output = barrier((grads_a, output))
    grads_a = lax.psum_scatter(grads_a, "dp", scatter_dimension=0, tiled=True).T
    grads = add_halves(keep_2, came_2)
    bit = 4
    while bit < dps:
        keep, give = halve(grads, bit)
        grads = add_halves(keep, group_swap(give, bit))
        bit *= 2
    grads = grads[0]
    shares = scatter_near(shares, (f_0, far[1], far[2]))
    grad_q = first_back(at, shares, tokens, dh, gains[0])
    grad_tokens = join(at, gather_pieces(grad_q))

    own, heads = width // dps, heads_loc * HD
    grad_qkv = grads_a[: 3 * heads].astype(F32).reshape(heads_loc, 3, HD, own).transpose(3, 1, 0, 2)
    grad_qkv = grad_qkv.reshape(own, 3, heads)
    grad_in = grads[:, :hid].astype(F32)
    grad_out = grads[:, hid:].astype(F32).T
    rest = grads_a[3 * heads : 7 * heads].reshape(4, heads, own)
    small = jnp.broadcast_to(grads_a[7 * heads :], (4, lanes, own))
    rest = lax.all_to_all(jnp.concatenate([rest, small], axis=1), "mp", 0, 0, tiled=True)
    rest = jnp.sum(rest.astype(F32), axis=0)
    grad_o, small = rest[:heads], rest[heads:]
    small_out = small[: experts + 2].T
    return (
        output,
        grad_tokens,
        jnp.stack([small[experts + 4], small[experts + 2]]),
        jnp.stack([small[experts + 5], small[experts + 3]]),
        grad_qkv,
        grad_o,
        grad_in,
        grad_out,
        small_out[:, :experts],
        small_out[:, experts:],
        grad_up[None],
        grad_down[None],
    )


def solution(mesh):
    in_specs = (
        P("dp", None),
        P("dp", None),
        P(),
        P(),
        P(None, None, "mp"),
        P("mp", None),
        P(None, "mp"),
        P("mp", None),
        P(),
        P(),
        P("dp", None, "mp"),
        P("dp", "mp", None),
        P("dp", None),
        P(),
    )
    out_specs = (
        P("dp", None),
        P("dp", None),
        P(None, "dp"),
        P(None, "dp"),
        P("dp", None, "mp"),
        P("mp", "dp"),
        P("dp", "mp"),
        P("mp", "dp"),
        P("dp", None),
        P("dp", None),
        P("dp", None, "mp"),
        P("dp", "mp", None),
    )
    return jax.shard_map(body, mesh=mesh, in_specs=in_specs, out_specs=out_specs, check_vma=False)
```

```python
from functools import partial

import jax
import jax.numpy as jnp
from jax import lax
from jax.experimental import pallas as pl
from jax.experimental.pallas import tpu as pltpu
from jax.sharding import PartitionSpec as P

HD = 64
GROUP = 4
EPS = 1e-05
LOG2E = 1.4426950408889634
SCALE2 = 0.125 * LOG2E
HIDE = -1e30
BF = jnp.bfloat16
F32 = jnp.float32
LIGHT = pl.CostEstimate(flops=1 << 20, bytes_accessed=1 << 20, transcendentals=0)


def mm(a, b):
    return jnp.dot(a, b, preferred_element_type=F32)


def ein(spec, a, b):
    return jnp.einsum(spec, a, b, preferred_element_type=F32)


def call(kernel, name, prefetch, grid, in_specs, out_specs, out_shape, args, scratch=(), alias=None, vmem=48):
    return pl.pallas_call(
        kernel,
        grid_spec=pltpu.PrefetchScalarGridSpec(
            num_scalar_prefetch=1,
            grid=grid,
            in_specs=in_specs,
            out_specs=out_specs,
            scratch_shapes=list(scratch),
        ),
        out_shape=out_shape,
        input_output_aliases=alias or {},
        compiler_params=pltpu.CompilerParams(vmem_limit_bytes=vmem * 2**20),
        cost_estimate=LIGHT,
        name=name,
    )(prefetch, *args)


def fixed(shape):
    zeros = (0,) * len(shape)
    return pl.BlockSpec(shape, lambda *_: zeros)


def like(shape, dtype):
    return jax.ShapeDtypeStruct(shape, dtype)


def normalize(v):
    mean = jnp.mean(v, axis=-1, keepdims=True)
    centred = v - mean
    scale = lax.rsqrt(jnp.mean(centred * centred, axis=-1, keepdims=True) + EPS)
    return centred * scale, scale


def norm_back(grad, gain, normal, scale):
    g = grad * gain
    along = jnp.mean(g * normal, axis=-1, keepdims=True)
    return scale * (g - jnp.mean(g, axis=-1, keepdims=True) - normal * along)


def qkv_kernel(at_ref, x_ref, gain_ref, bias_ref, w_ref, a_ref, *outs):
    normal, _ = normalize(x_ref[...].astype(F32))
    a = (normal * gain_ref[...] + bias_ref[...]).astype(BF)
    a_ref[...] = a
    for s in range(GROUP):
        outs[s][...] = mm_t(w_ref[at_ref[0] ^ s], a).astype(BF)


def project(at, tokens, gain, bias, w_heads):
    rows, width = tokens.shape
    features = w_heads.shape[1]
    blk = min(256, rows)
    moving = pl.BlockSpec((blk, width), lambda i, n: (i, 0))
    return call(
        qkv_kernel,
        "project",
        at,
        (rows // blk,),
        [moving, fixed((1, width)), fixed((1, width)), fixed(w_heads.shape)],
        [moving] + [pl.BlockSpec((features, blk), lambda i, n: (0, i))] * GROUP,
        [like((rows, width), BF)] + [like((features, rows), BF)] * GROUP,
        (tokens, gain, bias, w_heads),
    )


def fill_keys(k_s, place, keys, first_len, blk):
    rows = place * blk + lax.broadcasted_iota(jnp.int32, (blk, 128), 0)
    lane = lax.broadcasted_iota(jnp.int32, (blk, 128), 1)
    wide = jnp.concatenate([keys.astype(F32).T, jnp.zeros((blk, 128 - HD), F32)], axis=1)
    wide = jnp.where((lane == HD) & (rows < first_len), HIDE, wide)
    k_s[pl.ds(place * blk, blk), :] = wide.astype(BF)


def wide_query(query, place, first_len, blk):
    cols = place * blk + lax.broadcasted_iota(jnp.int32, (128 - HD, blk), 1)
    sub = lax.broadcasted_iota(jnp.int32, (128 - HD, blk), 0)
    extra = jnp.where((sub == 0) & (cols >= first_len), 1.0, 0.0)
    return jnp.concatenate([query, extra.astype(BF)], axis=0)


def causal(blk):
    keys = lax.broadcasted_iota(jnp.int32, (blk, blk), 0)
    queries = lax.broadcasted_iota(jnp.int32, (blk, blk), 1)
    return keys <= queries


def attend_kernel(blk, per, at_ref, *refs):
    qkv_refs, o_refs = refs[:GROUP], refs[GROUP : 2 * GROUP]
    lse_ref, k_s, qkv_s = refs[2 * GROUP :]
    i = pl.program_id(0)
    place, first_len = at_ref[0], at_ref[3]

    @pl.when(i == 0)
    def _():
        for s in range(GROUP):
            qkv_s[place ^ s] = qkv_refs[s][...]

    def part(which, j):
        return qkv_s[j // per, HD * which : HD * (which + 1), pl.ds((j % per) * blk, blk)]

    fill_keys(k_s, i, part(1, i), first_len, blk)
    query = wide_query(part(0, i), i, first_len, blk)

    def scores(j):
        return mm(k_s[pl.ds(pl.multiple_of(j * blk, blk), blk), :], query)

    s = jnp.where(causal(blk), scores(i), HIDE)
    top = jnp.max(s, axis=0, keepdims=True)
    p = jnp.exp2((s - top) * SCALE2)
    total = jnp.sum(p, axis=0, keepdims=True)
    acc = mm(part(2, i), p.astype(BF))

    def step(j, carry):
        top, total, acc = carry
        s = scores(j)
        new = jnp.maximum(top, jnp.max(s, axis=0, keepdims=True))
        p = jnp.exp2((s - new) * SCALE2)
        keep = jnp.exp2((top - new) * SCALE2)
        total = total * keep + jnp.sum(p, axis=0, keepdims=True)
        acc = acc * keep + mm(part(2, j), p.astype(BF))
        return new, total, acc

    low = jnp.where(i * blk >= first_len, first_len // blk, 0)
    top, total, acc = lax.fori_loop(low, i, step, (top, total, acc))
    out = (acc / total).astype(BF)
    for s in range(GROUP):

        @pl.when((i // per) ^ place == s)
        def _():
            o_refs[s][:, pl.ds((i % per) * blk, blk)] = out

    lse_ref[0] = top * SCALE2 + jnp.log2(total)


def attend(at, qkv):
    features, rows = qkv[0].shape
    blk = min(512, rows)
    per = rows // blk
    count = GROUP * per
    return call(
        partial(attend_kernel, blk, per),
        "attend",
        at,
        (count,),
        [fixed((features, rows))] * GROUP,
        [fixed((HD, rows))] * GROUP + [pl.BlockSpec((1, 1, blk), lambda i, n: (i, 0, 0))],
        [like((HD, rows), BF)] * GROUP + [like((count, 1, blk), F32)],
        qkv,
        scratch=[pltpu.VMEM((GROUP * rows, 128), BF), pltpu.VMEM((GROUP, features, rows), BF)],
    )


def back_kernel(blk, per, first, count, at_ref, *refs):
    qkv_refs, do_refs, o_refs = refs[:GROUP], refs[GROUP : 2 * GROUP], refs[2 * GROUP : 3 * GROUP]
    lse_ref, refs = refs[3 * GROUP], refs[3 * GROUP + 1 :]
    if first:
        dq_in_ref, refs = refs[1], refs[2:]
    out_ref, dq_ref, k_s, kt_s, v_s, wide_s, dot_s, both_s, delta_s, acc_s = refs
    at_first = pl.program_id(0) == 0
    j = first + pl.program_id(0)
    place, first_len = at_ref[0], at_ref[3]

    @pl.when(at_first)
    def _():
        dq_ref[...] = dq_in_ref[...] if first else jnp.zeros(dq_ref.shape, F32)
        zero = jnp.zeros((blk, HD), F32)
        for s in range(GROUP):

            @pl.when((place ^ s) * per >= first)
            def _():
                for sub in range(per):
                    i = (place ^ s) * per + sub
                    at = pl.ds(pl.multiple_of(i * blk, blk), blk)
                    cut = slice(sub * blk, (sub + 1) * blk)
                    query = qkv_refs[s][0:HD, cut]
                    keys = qkv_refs[s][HD : 2 * HD, cut]
                    grad = do_refs[s][:, cut]
                    fill_keys(k_s, i, keys, first_len, blk)
                    kt_s[:, at] = keys
                    dot_s[:, at] = grad
                    wide_s[:, at] = wide_query(query, i, first_len, blk)
                    grad = grad.astype(F32)
                    values = qkv_refs[s][2 * HD :, cut].astype(F32)
                    v_s[at, :] = jnp.concatenate([values.T, zero], axis=1).astype(BF)
                    both_s[0, at, :] = jnp.concatenate([grad.T, zero], axis=1).astype(BF)
                    both_s[1, at, :] = jnp.concatenate([zero, query.astype(F32).T], axis=1).astype(BF)
                    held = o_refs[s][:, cut].astype(F32)
                    delta_s[i] = jnp.sum(held * grad, axis=0, keepdims=True)

    here = pl.ds(pl.multiple_of(j * blk, blk), blk)
    keys_t = kt_s[:, here]
    values = v_s[here, 0:HD]

    def pair(i, diagonal):
        at = pl.ds(pl.multiple_of(i * blk, blk), blk)
        s = mm(k_s[here, :], wide_s[:, at])
        p = jnp.exp2(s * SCALE2 - lse_ref[i])
        if diagonal:
            p = jnp.where(causal(blk), p, 0.0)
        dp = mm(values, dot_s[:, at])
        ds = (p * (dp - delta_s[i])).astype(BF)
        dq_ref[:, at] += mm(keys_t, ds)
        return mm(p.astype(BF), both_s[0, at, :]) + mm(ds, both_s[1, at, :])

    acc_s[...] = pair(j, True)

    def step(i, carry):
        acc_s[...] += pair(i, False)
        return carry

    high = jnp.where((j + 1) * blk <= first_len, (first_len + blk - 1) // blk, count)
    lax.fori_loop(j + 1, high, step, 0)
    both = acc_s[...].T
    out_ref[0, 0:HD, :] = (dq_ref[:, here] * 0.125).astype(BF)
    out_ref[0, HD : 2 * HD, :] = (both[HD:, :] * 0.125).astype(BF)
    out_ref[0, 2 * HD :, :] = both[:HD, :].astype(BF)


def attend_back(at, qkv, do, o, lse, before, first, last):
    features, rows = qkv[0].shape
    blk = min(512, rows)
    per = rows // blk
    count = GROUP * per
    dq_shape = (HD, GROUP * rows)
    carried = [pl.BlockSpec(memory_space=pl.ANY), fixed(dq_shape)] if first else []
    return call(
        partial(back_kernel, blk, per, first * per, count),
        "attend_back",
        at,
        ((last - first) * per,),
        [fixed((features, rows))] * GROUP
        + [fixed((HD, rows))] * (2 * GROUP)
        + [fixed((count, 1, blk))]
        + carried,
        [
            pl.BlockSpec((1, features, blk), lambda j, n: ((first + j // per) ^ n[0], 0, j % per)),
            fixed(dq_shape),
        ],
        [like((GROUP, features, rows), BF), like(dq_shape, F32)],
        (*qkv, *do, *o, lse, *(before if first else ())),
        scratch=[
            pltpu.VMEM((GROUP * rows, 128), BF),
            pltpu.VMEM((HD, GROUP * rows), BF),
            pltpu.VMEM((GROUP * rows, 128), BF),
            pltpu.VMEM((128, GROUP * rows), BF),
            pltpu.VMEM((HD, GROUP * rows), BF),
            pltpu.VMEM((2, GROUP * rows, 128), BF),
            pltpu.VMEM((count, 1, blk), F32),
            pltpu.VMEM((blk, 128), F32),
        ],
        alias={3 * GROUP + 2: 0} if first else None,
    )


def split_kernel(at_ref, *refs):
    ins, outs = refs[:GROUP], refs[GROUP:]
    cols = outs[0].shape[1]
    for r in range(4):
        lanes = pl.ds(pl.multiple_of(((at_ref[1] + r) % 4) * cols, cols), cols)
        for s in range(GROUP):
            head = pl.ds(pl.multiple_of((at_ref[0] ^ s) * HD, HD), HD)
            outs[r][head, :] = ins[s][:, lanes]


def split(at, heads):
    rows = heads[0].shape[1]
    shape = (GROUP * HD, rows // 4)
    return call(
        split_kernel,
        "split",
        at,
        (1,),
        [fixed((HD, rows))] * GROUP,
        [fixed(shape)] * 4,
        [like(shape, BF)] * 4,
        heads,
    )


def unsplit_kernel(at_ref, *refs):
    ins, outs = refs[:4], refs[4:]
    cols = ins[0].shape[1]
    for r in range(4):
        lanes = pl.ds(pl.multiple_of(((at_ref[1] + r) % 4) * cols, cols), cols)
        for s in range(GROUP):
            head = pl.ds(pl.multiple_of((at_ref[0] ^ s) * HD, HD), HD)
            outs[s][:, lanes] = ins[r][head, :]


def unsplit(at, pieces):
    shape = (HD, 4 * pieces[0].shape[1])
    return call(
        unsplit_kernel,
        "unsplit",
        at,
        (1,),
        [fixed(pieces[0].shape)] * 4,
        [fixed(shape)] * GROUP,
        [like(shape, BF)] * GROUP,
        pieces,
    )


def heads_of(mine, r, features):
    return pl.ds(pl.multiple_of(((mine + 4 - r) % 4) * features, features), features)


def mid_kernel(at_ref, *refs):
    o_refs, (w_ref, x_ref, gain_ref, bias_ref, h_ref, b_ref) = refs[:4], refs[4:]
    h = x_ref[...].astype(F32)
    for r in range(4):
        rows = heads_of(at_ref[1], r, o_refs[r].shape[0])
        h = h + mm(o_refs[r][...].astype(F32).T.astype(BF), w_ref[rows, :])
    h_ref[...] = h
    normal, _ = normalize(h)
    b_ref[...] = (normal * gain_ref[...] + bias_ref[...]).astype(BF)


def mid(at, o, w_o, tokens, gain, bias):
    features, quarter = o[0].shape
    width = tokens.shape[1]
    return call(
        mid_kernel,
        "mid",
        at,
        (1,),
        [fixed((features, quarter))] * 4
        + [fixed(w_o.shape)]
        + [pl.BlockSpec((quarter, width), lambda i, n: (n[1], 0))]
        + [fixed((1, width))] * 2,
        [fixed((quarter, width))] * 2,
        [like((quarter, width), F32), like((quarter, width), BF)],
        (*o, w_o, tokens, gain, bias),
    )


def add_up(refs):
    total = refs[0][...]
    for ref in refs[1:]:
        total = total + ref[...].astype(F32)
    return total


def mid_back_kernel(at_ref, *refs):
    shares, (w_ref, h_ref, dy_ref, gain_ref, dh_ref, low_ref, sums_ref) = refs[:4], refs[4:11]
    do_refs = refs[11:]
    db = add_up(shares)
    normal, scale = normalize(h_ref[...])
    dh = dy_ref[...].astype(F32) + norm_back(db, gain_ref[...], normal, scale)
    dh_ref[...] = dh
    low = dh.astype(BF)
    low_ref[...] = low
    sums_ref[0:1, :] = jnp.sum(db * normal, axis=0, keepdims=True)
    sums_ref[1:2, :] = jnp.sum(db, axis=0, keepdims=True)
    for r in range(4):
        rows = heads_of(at_ref[1], r, do_refs[r].shape[0])
        do_refs[r][...] = mm_t(w_ref[rows, :], low).astype(BF)


def mid_back(at, shares, w_o, h, dy, gain):
    quarter, width = h.shape
    whole = fixed((quarter, width))
    piece = (w_o.shape[0] // 4, quarter)
    return call(
        mid_back_kernel,
        "mid_back",
        at,
        (1,),
        [whole] * 4 + [fixed(w_o.shape), whole, whole, fixed((1, width))],
        [whole] * 2 + [fixed((2, width))] + [fixed(piece)] * 4,
        [like((quarter, width), F32), like((quarter, width), BF), like((2, width), F32)]
        + [like(piece, BF)] * 4,
        (*shares, w_o, h, dy, gain),
    )


def first_back_kernel(at_ref, *refs):
    shares = refs[:4]
    x_ref, dh_ref, gain_ref, out_ref = refs[4:]
    d_a = add_up(shares)
    normal, scale = normalize(x_ref[...].astype(F32))
    out_ref[...] = (dh_ref[...] + norm_back(d_a, gain_ref[...], normal, scale)).astype(BF)


def first_back(at, shares, tokens, dh, gain):
    quarter, width = dh.shape
    return call(
        first_back_kernel,
        "first_back",
        at,
        (1,),
        [fixed((quarter, width))] * 4
        + [pl.BlockSpec((quarter, width), lambda i, n: (n[1], 0))]
        + [fixed((quarter, width)), fixed((1, width))],
        fixed((quarter, width)),
        like((quarter, width), BF),
        (*shares, tokens, dh, gain),
    )


def in_order(mine, own, right, left, far, right_two, left_two):
    one = jnp.where(mine == 3, far, left)
    two = jnp.where(mine < 2, left_two, right_two)
    three = jnp.where(mine == 0, far, right)
    return own, one, two, three


def one_hot(slots, dest):
    return jnp.where(slots == dest, 1.0, 0.0).astype(BF)


def dispatch_kernel(joined, at_ref, dest_ref, *refs):
    pieces, out_ref, spread_s = refs[:joined], refs[joined], refs[-1]
    blk, rows = min(256, spread_s.shape[0]), dest_ref.shape[1]

    @pl.when(pl.program_id(0) == 0)
    def _():
        slot = lax.broadcasted_iota(jnp.int32, (blk, rows), 0)
        for start in range(0, spread_s.shape[0], blk):
            spread_s[start : start + blk, :] = one_hot(slot + start, dest_ref[...])

    if joined == 1:
        rows_ref = pieces[0]
    else:
        rows_ref = refs[joined + 1]
        start = 0
        for piece in in_order(at_ref[1], *[ref[...] for ref in pieces]):
            rows_ref[start : start + piece.shape[0], :] = piece
            start += piece.shape[0]
    out_ref[...] = mm(spread_s[...], rows_ref[...]).astype(BF)


def columns(rows, width):
    return pl.BlockSpec((rows, width), lambda i, n: (0, i))


def dispatch(at, dest_row, pieces, slots):
    rows, width = dest_row.shape[1], pieces[0].shape[1]
    blk = min(256, width)
    joined = len(pieces) > 1
    return call(
        partial(dispatch_kernel, len(pieces)),
        "dispatch",
        at,
        (width // blk,),
        [fixed((1, rows))] + [columns(piece.shape[0], blk) for piece in pieces],
        [columns(slots, blk)] + [columns(rows, blk)] * joined,
        [like((slots, width), BF)] + [like((rows, width), BF)] * joined,
        (dest_row, *pieces),
        scratch=[pltpu.VMEM((slots, rows), BF)],
    )


def join_kernel(at_ref, *refs):
    pieces, out_ref = refs[:6], refs[6]
    r = pl.program_id(0)
    for place, piece in enumerate(in_order(at_ref[1], *[ref[...] for ref in pieces])):

        @pl.when(r == place)
        def _():
            out_ref[...] = piece


def join(at, pieces):
    each, width = pieces[0].shape
    return call(
        join_kernel,
        "join",
        at,
        (4,),
        [fixed((each, width))] * 6,
        pl.BlockSpec((each, width), lambda r, n: ((n[1] + r) % 4, 0)),
        like((4 * each, width), BF),
        pieces,
    )


def write_shares(mine, total, own_ref, one_ref, two_ref, three_ref, end_ref):
    rows = own_ref.shape[0]
    own_ref[...] = total[:rows]
    one, two, three = [total[r * rows : (r + 1) * rows].astype(BF) for r in (1, 2, 3)]
    one_ref[...] = one
    two_ref[...] = two
    three_ref[...] = three
    end_ref[...] = jnp.where(mine == 0, three, one)


def share_shapes(rows, width):
    return [like((rows, width), F32)] + [like((rows, width), BF)] * 4


def combine_kernel(count, whole, at_ref, *refs):
    dests, backs = refs[:count], refs[count : 2 * count]
    base_ref, refs, pick_s = refs[2 * count], refs[2 * count + 1 : -1], refs[-1]
    rows, slots = base_ref.shape[0], backs[0].shape[0]
    blk = rows // 4

    @pl.when(pl.program_id(0) == 0)
    def _():
        lane = lax.broadcasted_iota(jnp.int32, (blk, slots), 1)
        for k in range(count):
            for start in range(0, rows, blk):
                dest = dests[k][start : start + blk, :]
                pick_s[start : start + blk, k * slots : (k + 1) * slots] = one_hot(lane, dest)

    total = base_ref[...].astype(F32)
    for k in range(count):
        total = total + mm(pick_s[:, k * slots : (k + 1) * slots], backs[k][...])
    mine = at_ref[1]
    if whole:
        h_ref, out_ref = refs
        for r in range(4):
            part = total[r * blk : (r + 1) * blk]
            if r == 0:
                part = part + h_ref[...]
            place = pl.ds(pl.multiple_of(((mine + r) % 4) * blk, blk), blk)
            out_ref[place, :] = part.astype(BF)
    else:
        write_shares(mine, total, *refs)


def combine(at, dests, backs, base, h=None):
    count, (slots, width), rows = len(backs), backs[0].shape, base.shape[0]
    blk = min(256, width)
    whole = h is not None
    quarter = columns(rows // 4, blk)
    return call(
        partial(combine_kernel, count, whole),
        "combine",
        at,
        (width // blk,),
        [fixed((rows, 1))] * count
        + [columns(slots, blk)] * count
        + [columns(rows, blk)]
        + [quarter] * whole,
        columns(rows, blk) if whole else [quarter] * 5,
        like(base.shape, BF) if whole else share_shapes(rows // 4, width),
        (*dests, *backs, base) + ((h,) if whole else ()),
        scratch=[pltpu.VMEM((rows, count * slots), BF)],
    )


def mm_t(a, b):
    return lax.dot_general(a, b, (((1,), (1,)), ((), ())), preferred_element_type=F32)


def gelu_both(u):
    c = 0.7978845608028654
    square = u * u
    t = jnp.tanh(u * (c + (c * 0.044715) * square))
    half = 0.5 + 0.5 * t
    slope = half + (0.5 * u) * (1.0 - t * t) * (c + (3.0 * c * 0.044715) * square)
    return u * half, slope


def high_low(value):
    high = value.astype(BF)
    return high, (value - high.astype(F32)).astype(BF)


def two_coefs(logits, lane, experts):
    inside = (lane >= experts) & (lane < experts + 2)
    top = jnp.max(jnp.where(inside, logits, HIDE), axis=1, keepdims=True)
    e = jnp.where(inside, jnp.exp(logits - top), 0.0)
    e = e / jnp.sum(e, axis=1, keepdims=True)
    first = jnp.sum(jnp.where(lane == experts, e, 0.0), axis=1, keepdims=True)
    second = jnp.sum(jnp.where(lane == experts + 1, e, 0.0), axis=1, keepdims=True)
    return first, second


def small_back(d_small, rows, w_small_ref, small_ref, i):
    high, low = high_low(d_small)
    w_small = w_small_ref[...]
    high_t, low_t = high_low(d_small.T)

    @pl.when(i == 0)
    def _():
        small_ref[...] = jnp.zeros(small_ref.shape, F32)

    small_ref[...] += mm(high_t, rows) + mm(low_t, rows)
    return mm_t(high, w_small) + mm_t(low, w_small)


def expert_kernel(experts, half, at_ref, rows_ref, dy_ref, up_ref, down_ref, w_small_ref, *outs):
    if half:
        outs = outs[5:]
    rows_out_ref, hid_ref, dy_out_ref, deu_ref, y_ref, d_rows_ref, small_ref = outs
    rows = rows_ref[...]
    rows_out_ref[...] = rows
    up = mm(rows, up_ref[...])
    logits = mm(rows, w_small_ref[...])
    lane = lax.broadcasted_iota(jnp.int32, logits.shape, 1)
    routed = lane < experts
    top = jnp.max(jnp.where(routed, logits, HIDE), axis=1, keepdims=True)
    probs = jnp.where(routed, jnp.exp(logits - top), 0.0)
    probs = probs / jnp.sum(probs, axis=1, keepdims=True)
    own = jnp.where(lane == at_ref[2], 1.0, 0.0)
    gate = jnp.sum(probs * own, axis=1, keepdims=True)
    first, second = two_coefs(logits, lane, experts)
    weight = second * gate
    dy = dy_ref[...].reshape(rows.shape).astype(F32)
    d_y = (weight * dy).astype(BF)
    dy_out_ref[...] = d_y
    d_hidden = mm_t(d_y, down_ref[...])
    hidden, slope = gelu_both(up)
    hidden = hidden.astype(BF)
    hid_ref[...] = hidden
    d_up = (d_hidden * slope).astype(BF)
    deu_ref[...] = d_up
    y = mm(hidden, down_ref[...])
    y_ref[...] = (weight * y).astype(BF).reshape(y_ref.shape)
    along = gate * jnp.sum(dy * y, axis=1, keepdims=True)
    mixed = first * second * along
    d_small = (second * along) * (own - probs)
    d_small = jnp.where(routed, d_small, 0.0)
    d_small = d_small + jnp.where(lane == experts + 1, mixed, 0.0)
    d_small = d_small - jnp.where(lane == experts, mixed, 0.0)
    d_rows = mm_t(d_up, up_ref[...]) + small_back(d_small, rows, w_small_ref, small_ref, pl.program_id(0))
    d_rows_ref[...] = d_rows.astype(BF)


def expert_rows(at, rows, dy, w_up, w_down, w_small, experts, half, before):
    count, width = rows.shape
    hid, lanes = w_up.shape[1], w_small.shape[1]
    blk = min(512, count)
    capacity = count // dy.shape[0]
    steps = count // blk
    moving = pl.BlockSpec((blk, width), lambda i, n: (i, 0))
    slots = pl.BlockSpec((blk // capacity, capacity, width), lambda i, n: (i, half, 0))
    kept = [pl.BlockSpec((blk, size), lambda i, n: (i + half * steps, 0)) for size in (width, hid, width, hid)]
    return call(
        partial(expert_kernel, experts, half),
        "expert_rows",
        at,
        (steps,),
        [
            moving,
            slots,
            fixed((width, hid)),
            fixed((hid, width)),
            fixed((width, lanes)),
        ]
        + [pl.BlockSpec(memory_space=pl.ANY)] * (5 * half),
        kept + [slots, moving, fixed((lanes, width))],
        [like((2 * count, size), BF) for size in (width, hid, width, hid)]
        + [like(dy.shape, BF), like((count, width), BF)]
        + [like((lanes, width), F32)],
        (rows, dy, w_up, w_down, w_small, *before),
        alias={6 + k: k for k in range(5)} if half else None,
        vmem=56,
    )


def dense_kernel(experts, at_ref, rows_ref, dy_ref, in_ref, out_ref, w_small_ref, *outs):
    hid_ref, grad_ref, d_up_ref, mix_ref, db_ref, small_ref = outs
    rows = rows_ref[...]
    up = mm(rows, in_ref[...])
    logits = mm(rows, w_small_ref[...])
    lane = lax.broadcasted_iota(jnp.int32, logits.shape, 1)
    first, second = two_coefs(logits, lane, experts)
    dy = dy_ref[...].astype(F32)
    grad = (first * dy).astype(BF)
    grad_ref[...] = grad
    d_hidden = mm_t(grad, out_ref[...])
    hidden, slope = gelu_both(up)
    hidden = hidden.astype(BF)
    hid_ref[...] = hidden
    d_up = (d_hidden * slope).astype(BF)
    d_up_ref[...] = d_up
    dense = mm(hidden, out_ref[...])
    mix_ref[...] = first * dense
    mixed = first * second * jnp.sum(dy * dense, axis=1, keepdims=True)
    d_small = jnp.where(lane == experts, mixed, 0.0) - jnp.where(lane == experts + 1, mixed, 0.0)
    db_ref[...] = mm_t(d_up, in_ref[...]) + small_back(d_small, rows, w_small_ref, small_ref, pl.program_id(0))


def dense_rows(at, rows, dy, w_in, w_out, w_small, experts):
    (count, width), hid, lanes = rows.shape, w_in.shape[1], w_small.shape[1]
    blk = min(512, count)
    row_out = pl.BlockSpec((blk, width), lambda i, n: (i, 0))
    hid_out = pl.BlockSpec((blk, hid), lambda i, n: (i, 0))
    return call(
        partial(dense_kernel, experts),
        "dense_rows",
        at,
        (count // blk,),
        [row_out, row_out, fixed((width, hid)), fixed((hid, width)), fixed((width, lanes))],
        [hid_out, row_out, hid_out, row_out, row_out, fixed((lanes, width))],
        [
            like((count, hid), BF),
            like((count, width), BF),
            like((count, hid), BF),
            like((count, width), F32),
            like((count, width), F32),
            like((lanes, width), F32),
        ],
        (rows, dy, w_in, w_out, w_small),
        vmem=56,
    )


def turned(value):
    return value.astype(F32).T.astype(BF)


def dense_grads_kernel(at_ref, b_ref, d_up_ref, grad_ref, hid_ref, keep_ref, give_ref):
    width = d_up_ref.shape[1]
    first = mm(turned(b_ref[...]), d_up_ref[...]).astype(BF)
    second = mm(turned(grad_ref[...]), hid_ref[...]).astype(BF)
    half = pl.num_programs(0) // 2
    for side, ref in ((0, keep_ref), (1, give_ref)):

        @pl.when(pl.program_id(0) // half == side)
        def _():
            ref[0, :, :width] = first
            ref[0, :, width:] = second


def dense_grads(at, b, d_up, grad, hidden, parts):
    (rows, width), hid = b.shape, hidden.shape[1]
    own, half, bits = width // parts, parts // 2, parts.bit_length() - 1

    def part(q, n):
        turned_q = sum([((q // 2**k) % 2) * 2 ** (bits - 1 - k) for k in range(bits)])
        return turned_q ^ n[2]

    column = pl.BlockSpec((rows, own), lambda q, n: (0, part(q, n)))
    shape = (1, own, 2 * hid)
    return call(
        dense_grads_kernel,
        "dense_grads",
        at,
        (parts,),
        [column, fixed((rows, hid)), column, fixed((rows, hid))],
        [
            pl.BlockSpec(shape, lambda q, n: (jnp.minimum(q, half - 1), 0, 0)),
            pl.BlockSpec(shape, lambda q, n: (jnp.maximum(q - half, 0), 0, 0)),
        ],
        [like((half, own, 2 * hid), BF)] * 2,
        (b, d_up, grad, hidden),
    )


def attention_grads_kernel(experts, at_ref, *refs):
    grads, o_refs, refs = refs[:GROUP], refs[GROUP : GROUP + 4], refs[GROUP + 4 :]
    a_ref, dh_ref, w_ref, gain_ref, bias_ref, sums_ref = refs[:6]
    small_refs, (out_ref, all_s) = refs[6:-2], refs[-2:]
    heads, features = GROUP * HD, grads[1].shape[0]
    products, plain = 0.0, 0.0
    for k in range(GROUP):
        head = at_ref[0] ^ k
        rows = pl.ds(pl.multiple_of(head * features, features), features)
        grad = grads[k][...]
        grad = grad[0] if k == 0 else grad
        weight = w_ref[head].astype(F32)
        total = mm(grad, a_ref[...])
        all_s[rows, :] = total
        each = jnp.sum(grad.astype(F32), axis=1, keepdims=True)
        products = products + jnp.sum(total * weight, axis=0, keepdims=True)
        plain = plain + jnp.sum(each * weight, axis=0, keepdims=True)
    first = GROUP * features
    for r in range(4):
        rows = pl.ds(pl.multiple_of(first + ((at_ref[1] + 4 - r) % 4) * heads, heads), heads)
        all_s[rows, :] = mm(o_refs[r][...], dh_ref[...])
    first += 4 * heads
    small = add_up(small_refs)
    row = lax.broadcasted_iota(jnp.int32, small.shape, 0)
    d_gain = (products - bias_ref[...] * plain) / gain_ref[...]
    for k, sums in enumerate((sums_ref[0:1, :], sums_ref[1:2, :], d_gain, plain)):
        small = jnp.where(row == experts + 2 + k, sums, small)
    all_s[first:, :] = small
    out_ref[...] = all_s[...].T.astype(BF)


def attention_grads(at, held, came, o, a, dh, w_heads, gain, bias, sums, small, experts):
    rows, width = a.shape
    features, lanes = held.shape[1], small[0].shape[0]
    height = GROUP * features + 4 * o[0].shape[0] + lanes
    blk = min(256, width)
    return call(
        partial(attention_grads_kernel, experts),
        "attention_grads",
        at,
        (width // blk,),
        [fixed((1, features, rows))]
        + [fixed((features, rows))] * 3
        + [fixed(o[0].shape)] * 4
        + [columns(rows, blk), columns(dh.shape[0], blk)]
        + [pl.BlockSpec((GROUP, features, blk), lambda i, n: (0, 0, i))]
        + [columns(1, blk)] * 2
        + [columns(2, blk)]
        + [columns(lanes, blk)] * len(small),
        pl.BlockSpec((blk, height), lambda i, n: (i, 0)),
        like((width, height), BF),
        (held, *came, *o, a, dh, w_heads, gain, bias, sums, *small),
        scratch=[pltpu.VMEM((height, blk), F32)],
    )


def project_kernel(at_ref, *refs):
    grads, w_ref, outs, turned_s = refs[:GROUP], refs[GROUP], refs[GROUP + 1 : -1], refs[-1]
    rows = turned_s.shape[1]
    blk = rows // 4

    @pl.when(pl.program_id(0) == 0)
    def _():
        for s in range(GROUP):
            for r in range(4):
                lanes = pl.ds(pl.multiple_of(((at_ref[1] + r) % 4) * blk, blk), blk)
                grad = grads[s][0, :, lanes] if s == 0 else grads[s][:, lanes]
                turned_s[s, r * blk : (r + 1) * blk, :] = turned(grad)

    total = 0.0
    for s in range(GROUP):
        total = total + mm(turned_s[s], w_ref[at_ref[0] ^ s])
    write_shares(at_ref[1], total, *outs)


def project_back(at, held, came, w_heads):
    _, features, rows = held.shape
    width = w_heads.shape[2]
    blk = min(256, width)
    return call(
        project_kernel,
        "project_back",
        at,
        (width // blk,),
        [fixed((1, features, rows))]
        + [fixed((features, rows))] * 3
        + [pl.BlockSpec((GROUP, features, blk), lambda i, n: (0, 0, i))],
        [columns(rows // 4, blk)] * 5,
        share_shapes(rows // 4, width),
        (held, *came, w_heads),
        scratch=[pltpu.VMEM((GROUP, rows, features), BF)],
    )


def hop(value, *pairs):
    return lax.ppermute(value, "mp", pairs)


def rotate(value, steps):
    return hop(value, *[(s, (s + steps) % 4) for s in range(4)])


def gather_near(own):
    right = hop(own, (0, 1), (1, 2), (2, 3))
    left = hop(own, (1, 0), (2, 1), (3, 2))
    return own, right, left, hop(own, (0, 3), (3, 0))


def gather_far(near):
    _, right, left, _ = near
    return *near, hop(right, (1, 2), (2, 3)), hop(left, (1, 0), (2, 1))


def gather_pieces(own):
    return gather_far(gather_near(own))


def scatter_far(shares):
    _, _, two, _, end = shares
    return hop(two, (2, 1), (3, 2)), hop(two, (0, 1), (1, 2)), hop(end, (0, 3), (3, 0))


def scatter_near(shares, came):
    own, one, _, three, _ = shares
    from_right, from_left, from_end = came
    three = (three.astype(F32) + from_right.astype(F32)).astype(BF)
    one = (one.astype(F32) + from_left.astype(F32)).astype(BF)
    return own, hop(three, (1, 0), (2, 1), (3, 2)), hop(one, (0, 1), (1, 2), (2, 3)), from_end


def group_swap(value, s):
    count = lax.axis_size("dp")
    return lax.ppermute(value, "dp", [(t, t ^ s) for t in range(count)])


def expert_swap(value, experts):
    wide = value.reshape(experts, value.shape[0] // experts, value.shape[1])
    return lax.all_to_all(wide, "dp", 0, 0, tiled=True).reshape(value.shape)


def roll_rows(value, start):
    twice = jnp.concatenate([value, value], axis=0)
    return lax.dynamic_slice_in_dim(twice, start, value.shape[0], 0)


def add_halves(keep, came):
    return (keep.astype(F32) + came.astype(F32)).astype(BF)


def body(
    tokens,
    cotangent,
    ln_gains,
    ln_biases,
    w_qkv,
    w_o,
    w_in,
    w_out,
    w_router,
    w_coef,
    w_up,
    w_down,
    routes,
    long_group,
):
    rows, width = tokens.shape
    dps = lax.axis_size("dp")
    mine, position = lax.axis_index("mp"), lax.axis_index("dp")
    quarter = rows // 4
    start = mine * quarter
    heads_loc = w_qkv.shape[2] // HD
    hid = w_in.shape[1]
    experts = w_router.shape[1]
    capacity = max(2, 2 * rows // experts)
    half = capacity // 2
    barrier = lax.optimization_barrier
    first_len = lax.dynamic_index_in_dim(long_group, position // GROUP, 0, keepdims=False)
    at = jnp.stack([position % GROUP, mine, position, first_len]).astype(jnp.int32)
    gains = [ln_gains[0:1], ln_gains[1:2]]
    biases = [ln_biases[0:1], ln_biases[1:2]]
    w_o_all = lax.all_gather(w_o, "mp", axis=0, tiled=True)

    w_heads = w_qkv.reshape(width, 3, heads_loc, HD).transpose(2, 1, 3, 0)
    w_heads = w_heads.reshape(heads_loc, 3 * HD, width)
    a_r, *qkv = project(at, tokens, gains[0], biases[0], w_heads)
    qkv = [qkv[0]] + [group_swap(qkv[s], s) for s in (1, 2, 3)]

    route = roll_rows(routes, start)[:, 0]
    picked = (route[:, None] == jnp.arange(experts, dtype=jnp.int32)[None, :]).astype(jnp.int32)
    slot = jnp.sum((jnp.cumsum(picked, axis=0) - picked) * picked, axis=1)
    dy_b = roll_rows(cotangent, start)
    send_dy = dispatch(at, (route * capacity + slot)[None, :], [dy_b], experts * capacity)[0]
    *qkv, send_dy = barrier((*qkv, send_dy))
    in_half = [slot < half, slot >= half]
    dests = [
        jnp.where(in_half[k], route * half + slot - k * half, -1).astype(jnp.int32) for k in (0, 1)
    ]

    *o_t, lse = attend(at, qkv)
    *o_t, w_o_all = barrier((*o_t, w_o_all))
    o_heads = [o_t[0]] + [group_swap(o_t[s], s) for s in (1, 2, 3)]
    pieces = split(at, o_heads)
    o_q = [pieces[0]] + [rotate(pieces[r], r) for r in (1, 2, 3)]
    lanes = -(-(experts + 2) // 128) * 128
    w_small = jnp.concatenate(
        [w_router, w_coef, jnp.zeros((width, lanes - experts - 2), BF)], axis=1
    )
    *o_q, send_dy, w_small = barrier((*o_q, send_dy, w_small))
    got_dy = expert_swap(send_dy, experts).reshape(experts, capacity, width)
    h, b_q = mid(at, o_q, w_o_all, tokens, gains[1], biases[1])

    pieces = gather_pieces(b_q)
    send_0, b_r = dispatch(at, dests[0][None, :], pieces, experts * half)
    send_0, got_dy = barrier((send_0, got_dy))
    got_0 = expert_swap(send_0, experts)
    send_1 = dispatch(at, dests[1][None, :], [b_r], experts * half)[0]
    b_r, send_1 = barrier((b_r, send_1))
    hidden, dense_grad, d_up, mix_base, db_base, small_t = dense_rows(
        at, b_r, dy_b, w_in, w_out, w_small, experts
    )
    send_1, got_0, db_base = barrier((send_1, got_0, db_base))
    got_1 = expert_swap(send_1, experts)

    *kept, d_rows_0, small_0 = expert_rows(
        at, got_0, got_dy, w_up[0], w_down[0], w_small, experts, 0, ()
    )
    back_0 = expert_swap(d_rows_0, experts)
    *kept, d_rows_1, small_1 = expert_rows(
        at, got_1, got_dy, w_up[0], w_down[0], w_small, experts, 1, kept
    )
    got, hidden_e, d_y, d_eu, back_y = kept
    back_1 = expert_swap(d_rows_1, experts)
    d_rows_1, b_r = barrier((d_rows_1, b_r))
    halving = width == dps * 128
    if halving:
        grads = dense_grads(at, b_r, d_up, dense_grad, hidden, dps)
    else:
        grads = [ein("td,tf->df", b_r, d_up).astype(BF), ein("td,tf->df", dense_grad, hidden).astype(BF)]
    back_0, back_1, back_y, *grads = barrier((back_0, back_1, back_y, *grads))

    dest_cols = [dest[:, None] for dest in dests]
    shares = combine(at, dest_cols, [back_0, back_1], db_base)
    far = scatter_far(shares)
    *far, back_y, g_0, g_1 = barrier((*far, back_y, *grads))
    grads = [g_0, g_1]
    tok_y = expert_swap(back_y.reshape(experts * capacity, width), experts)
    shares = scatter_near(shares, far)
    dh, dh_r, sums_2, *do_q = mid_back(at, shares, w_o_all, h, dy_b[:quarter], gains[1])
    do_q = [do_q[0]] + [rotate(do_q[r], -r) for r in (1, 2, 3)]

    mix = combine(at, [(route * capacity + slot)[:, None]], [tok_y], mix_base, h)
    *do_q, mix = barrier((*do_q, mix))
    output = lax.psum(mix, "mp")
    do_heads = unsplit(at, do_q)
    do_t = [do_heads[0]] + [group_swap(do_heads[s], s) for s in (1, 2, 3)]
    if halving:
        came_1 = group_swap(grads[1], 1)
        half = dps // 4
        give = add_halves(grads[0][half:], came_1[half:])
        *do_t, give = barrier((*do_t, give))
        came_2 = group_swap(give, 2)
    d_qkv, _ = attend_back(at, qkv, do_t, o_t, lse, None, 0, GROUP)
    if halving:
        keep = add_halves(grads[0][:half], came_1[:half])
        d_qkv, came_2, keep = barrier((d_qkv, came_2, keep))
        grads = add_halves(keep, came_2)
        bit = 4
        while bit < dps:
            half = grads.shape[0] // 2
            grads = add_halves(grads[:half], group_swap(grads[half:], bit))
            bit *= 2
        grads = [grads[0][:, :hid], grads[0][:, hid:]]
    else:
        grads = [lax.psum_scatter(grad, "dp", scatter_dimension=0, tiled=True) for grad in grads]

    came = [group_swap(d_qkv[s], s) for s in (1, 2, 3)]
    d_qkv, got, hidden_e, d_y, d_eu = barrier((d_qkv, got, hidden_e, d_y, d_eu))
    grad_down = ein("rf,rd->fd", hidden_e, d_y)
    *came, grad_down = barrier((*came, grad_down))
    grads_a = attention_grads(
        at, d_qkv, came, o_q, a_r, dh_r, w_heads, gains[0], biases[0], sums_2, (small_0, small_1, small_t), experts
    )
    d_qkv, grads_a = barrier((d_qkv, grads_a))
    shares = project_back(at, d_qkv, came, w_heads)
    far = scatter_far(shares)
    grads_a, output = barrier((grads_a, output))
    grads_a = lax.psum_scatter(grads_a, "dp", scatter_dimension=0, tiled=True).T
    grad_up = ein("rd,rf->df", got, d_eu)
    *far, grad_up = barrier((*far, grad_up))
    shares = scatter_near(shares, far)
    grad_q = first_back(at, shares, tokens, dh, gains[0])
    pieces = gather_pieces(grad_q)

    own, heads = width // dps, heads_loc * HD
    grad_qkv = grads_a[: 3 * heads].astype(F32).reshape(heads_loc, 3, HD, own).transpose(3, 1, 0, 2)
    grad_qkv = grad_qkv.reshape(own, 3, heads)
    grad_in = grads[0].astype(F32)
    grad_out = grads[1].astype(F32).T
    rest = grads_a[3 * heads : 7 * heads].reshape(4, heads, own)
    small = jnp.broadcast_to(grads_a[7 * heads :], (4, lanes, own))
    rest = lax.all_to_all(jnp.concatenate([rest, small], axis=1), "mp", 0, 0, tiled=True)
    rest = jnp.sum(rest.astype(F32), axis=0)
    grad_in, grad_out, grad_qkv, rest, *pieces = barrier((grad_in, grad_out, grad_qkv, rest, *pieces))
    grad_tokens = join(at, pieces)
    grad_o, small = rest[:heads], rest[heads:]
    small_out = small[: experts + 2].T
    return (
        output,
        grad_tokens,
        jnp.stack([small[experts + 4], small[experts + 2]]),
        jnp.stack([small[experts + 5], small[experts + 3]]),
        grad_qkv,
        grad_o,
        grad_in,
        grad_out,
        small_out[:, :experts],
        small_out[:, experts:],
        grad_up[None],
        grad_down[None],
    )


def solution(mesh):
    in_specs = (
        P("dp", None),
        P("dp", None),
        P(),
        P(),
        P(None, None, "mp"),
        P("mp", None),
        P(None, "mp"),
        P("mp", None),
        P(),
        P(),
        P("dp", None, "mp"),
        P("dp", "mp", None),
        P("dp", None),
        P(),
    )
    out_specs = (
        P("dp", None),
        P("dp", None),
        P(None, "dp"),
        P(None, "dp"),
        P("dp", None, "mp"),
        P("mp", "dp"),
        P("dp", "mp"),
        P("mp", "dp"),
        P("dp", None),
        P("dp", None),
        P("dp", None, "mp"),
        P("dp", "mp", None),
    )
    return jax.shard_map(body, mesh=mesh, in_specs=in_specs, out_specs=out_specs, check_vma=False)
```

```python
from functools import partial

import jax
import jax.numpy as jnp
from jax import lax
from jax.experimental import pallas as pl
from jax.experimental.pallas import tpu as pltpu
from jax.sharding import PartitionSpec as P

HD = 64
GROUP = 4
EPS = 1e-05
LOG2E = 1.4426950408889634
SCALE2 = 0.125 * LOG2E
HIDE = -1e30
BF = jnp.bfloat16
F32 = jnp.float32
LIGHT = pl.CostEstimate(flops=1 << 20, bytes_accessed=1 << 20, transcendentals=0)


def mm(a, b):
    return jnp.dot(a, b, preferred_element_type=F32)


def ein(spec, a, b):
    return jnp.einsum(spec, a, b, preferred_element_type=F32)


def call(kernel, name, prefetch, grid, in_specs, out_specs, out_shape, args, scratch=(), alias=None, vmem=48):
    return pl.pallas_call(
        kernel,
        grid_spec=pltpu.PrefetchScalarGridSpec(
            num_scalar_prefetch=1,
            grid=grid,
            in_specs=in_specs,
            out_specs=out_specs,
            scratch_shapes=list(scratch),
        ),
        out_shape=out_shape,
        input_output_aliases=alias or {},
        compiler_params=pltpu.CompilerParams(vmem_limit_bytes=vmem * 2**20),
        cost_estimate=LIGHT,
        name=name,
    )(prefetch, *args)


def fixed(shape):
    zeros = (0,) * len(shape)
    return pl.BlockSpec(shape, lambda *_: zeros)


def like(shape, dtype):
    return jax.ShapeDtypeStruct(shape, dtype)


def normalize(v):
    mean = jnp.mean(v, axis=-1, keepdims=True)
    centred = v - mean
    scale = lax.rsqrt(jnp.mean(centred * centred, axis=-1, keepdims=True) + EPS)
    return centred * scale, scale


def norm_back(grad, gain, normal, scale):
    g = grad * gain
    along = jnp.mean(g * normal, axis=-1, keepdims=True)
    return scale * (g - jnp.mean(g, axis=-1, keepdims=True) - normal * along)


def qkv_kernel(at_ref, x_ref, gain_ref, bias_ref, w_ref, a_ref, *outs):
    normal, _ = normalize(x_ref[...].astype(F32))
    a = (normal * gain_ref[...] + bias_ref[...]).astype(BF)
    a_ref[...] = a
    for s in range(GROUP):
        outs[s][...] = mm_t(w_ref[at_ref[0] ^ s], a).astype(BF)


def project(at, tokens, gain, bias, w_heads):
    rows, width = tokens.shape
    features = w_heads.shape[1]
    blk = min(256, rows)
    moving = pl.BlockSpec((blk, width), lambda i, n: (i, 0))
    return call(
        qkv_kernel,
        "project",
        at,
        (rows // blk,),
        [moving, fixed((1, width)), fixed((1, width)), fixed(w_heads.shape)],
        [moving] + [pl.BlockSpec((features, blk), lambda i, n: (0, i))] * GROUP,
        [like((rows, width), BF)] + [like((features, rows), BF)] * GROUP,
        (tokens, gain, bias, w_heads),
    )


def fill_keys(k_s, place, keys, first_len, blk):
    rows = place * blk + lax.broadcasted_iota(jnp.int32, (blk, 128), 0)
    lane = lax.broadcasted_iota(jnp.int32, (blk, 128), 1)
    wide = jnp.concatenate([keys.astype(F32).T, jnp.zeros((blk, 128 - HD), F32)], axis=1)
    wide = jnp.where((lane == HD) & (rows < first_len), HIDE, wide)
    k_s[pl.ds(place * blk, blk), :] = wide.astype(BF)


def wide_query(query, place, first_len, blk):
    cols = place * blk + lax.broadcasted_iota(jnp.int32, (128 - HD, blk), 1)
    sub = lax.broadcasted_iota(jnp.int32, (128 - HD, blk), 0)
    extra = jnp.where((sub == 0) & (cols >= first_len), 1.0, 0.0)
    return jnp.concatenate([query, extra.astype(BF)], axis=0)


def causal(blk):
    keys = lax.broadcasted_iota(jnp.int32, (blk, blk), 0)
    queries = lax.broadcasted_iota(jnp.int32, (blk, blk), 1)
    return keys <= queries


def attend_kernel(blk, per, at_ref, *refs):
    qkv_refs, o_refs = refs[:GROUP], refs[GROUP : 2 * GROUP]
    lse_ref, k_s, qkv_s = refs[2 * GROUP :]
    i = pl.program_id(0)
    place, first_len = at_ref[0], at_ref[3]

    @pl.when(i == 0)
    def _():
        for s in range(GROUP):
            qkv_s[place ^ s] = qkv_refs[s][...]

    def part(which, j):
        return qkv_s[j // per, HD * which : HD * (which + 1), pl.ds((j % per) * blk, blk)]

    fill_keys(k_s, i, part(1, i), first_len, blk)
    query = wide_query(part(0, i), i, first_len, blk)

    def scores(j):
        return mm(k_s[pl.ds(pl.multiple_of(j * blk, blk), blk), :], query)

    s = jnp.where(causal(blk), scores(i), HIDE)
    top = jnp.max(s, axis=0, keepdims=True)
    p = jnp.exp2((s - top) * SCALE2)
    total = jnp.sum(p, axis=0, keepdims=True)
    acc = mm(part(2, i), p.astype(BF))

    def steps(blocks, carry):
        top, total, acc = carry
        s = [scores(j) for j in blocks]
        new = top
        for one in s:
            new = jnp.maximum(new, jnp.max(one, axis=0, keepdims=True))
        keep = jnp.exp2((top - new) * SCALE2)
        total, acc = total * keep, acc * keep
        for j, one in zip(blocks, s):
            p = jnp.exp2((one - new) * SCALE2)
            total = total + jnp.sum(p, axis=0, keepdims=True)
            acc = acc + mm(part(2, j), p.astype(BF))
        return new, total, acc

    low = jnp.where(i * blk >= first_len, first_len // blk, 0)
    pairs = (i - low) // 2
    carry = lax.fori_loop(
        0, pairs, lambda t, c: steps([low + 2 * t, low + 2 * t + 1], c), (top, total, acc)
    )
    top, total, acc = lax.fori_loop(low + 2 * pairs, i, lambda j, c: steps([j], c), carry)
    out = (acc / total).astype(BF)
    for s in range(GROUP):

        @pl.when((i // per) ^ place == s)
        def _():
            o_refs[s][:, pl.ds((i % per) * blk, blk)] = out

    lse_ref[0] = top * SCALE2 + jnp.log2(total)


def attend(at, qkv):
    features, rows = qkv[0].shape
    blk = min(512, rows)
    per = rows // blk
    count = GROUP * per
    return call(
        partial(attend_kernel, blk, per),
        "attend",
        at,
        (count,),
        [fixed((features, rows))] * GROUP,
        [fixed((HD, rows))] * GROUP + [pl.BlockSpec((1, 1, blk), lambda i, n: (i, 0, 0))],
        [like((HD, rows), BF)] * GROUP + [like((count, 1, blk), F32)],
        qkv,
        scratch=[pltpu.VMEM((GROUP * rows, 128), BF), pltpu.VMEM((GROUP, features, rows), BF)],
    )


def back_kernel(blk, per, first, count, at_ref, *refs):
    qkv_refs, do_refs, o_refs = refs[:GROUP], refs[GROUP : 2 * GROUP], refs[2 * GROUP : 3 * GROUP]
    lse_ref, refs = refs[3 * GROUP], refs[3 * GROUP + 1 :]
    if first:
        dq_in_ref, refs = refs[1], refs[2:]
    out_ref, dq_ref, k_s, kt_s, v_s, wide_s, dot_s, both_s, delta_s, acc_s = refs
    at_first = pl.program_id(0) == 0
    j = first + pl.program_id(0)
    place, first_len = at_ref[0], at_ref[3]

    @pl.when(at_first)
    def _():
        dq_ref[...] = dq_in_ref[...] if first else jnp.zeros(dq_ref.shape, F32)
        zero = jnp.zeros((blk, HD), F32)
        for s in range(GROUP):

            @pl.when((place ^ s) * per >= first)
            def _():
                for sub in range(per):
                    i = (place ^ s) * per + sub
                    at = pl.ds(pl.multiple_of(i * blk, blk), blk)
                    cut = slice(sub * blk, (sub + 1) * blk)
                    query = qkv_refs[s][0:HD, cut]
                    keys = qkv_refs[s][HD : 2 * HD, cut]
                    grad = do_refs[s][:, cut]
                    fill_keys(k_s, i, keys, first_len, blk)
                    kt_s[:, at] = keys
                    dot_s[:, at] = grad
                    wide_s[:, at] = wide_query(query, i, first_len, blk)
                    grad = grad.astype(F32)
                    values = qkv_refs[s][2 * HD :, cut].astype(F32)
                    v_s[at, :] = jnp.concatenate([values.T, zero], axis=1).astype(BF)
                    both_s[0, at, :] = jnp.concatenate([grad.T, zero], axis=1).astype(BF)
                    both_s[1, at, :] = jnp.concatenate([zero, query.astype(F32).T], axis=1).astype(BF)
                    held = o_refs[s][:, cut].astype(F32)
                    delta_s[i] = jnp.sum(held * grad, axis=0, keepdims=True)

    here = pl.ds(pl.multiple_of(j * blk, blk), blk)
    keys_t = kt_s[:, here]
    values = v_s[here, 0:HD]

    def pair(i, diagonal):
        at = pl.ds(pl.multiple_of(i * blk, blk), blk)
        s = mm(k_s[here, :], wide_s[:, at])
        p = jnp.exp2(s * SCALE2 - lse_ref[i])
        if diagonal:
            p = jnp.where(causal(blk), p, 0.0)
        dp = mm(values, dot_s[:, at])
        ds = (p * (dp - delta_s[i])).astype(BF)
        return mm(p.astype(BF), both_s[0, at, :]) + mm(ds, both_s[1, at, :]), mm(keys_t, ds)

    acc_s[...], dq = pair(j, True)
    dq_ref[:, here] += dq

    def step_two(t, carry):
        i = j + 1 + 2 * t
        (kv_0, dq_0), (kv_1, dq_1) = pair(i, False), pair(i + 1, False)
        acc_s[...] += kv_0 + kv_1
        at = pl.ds(pl.multiple_of(i * blk, blk), 2 * blk)
        dq_ref[:, at] += jnp.concatenate([dq_0, dq_1], axis=1)
        return carry

    def step(i, carry):
        kv, dq = pair(i, False)
        acc_s[...] += kv
        dq_ref[:, pl.ds(pl.multiple_of(i * blk, blk), blk)] += dq
        return carry

    high = jnp.where((j + 1) * blk <= first_len, (first_len + blk - 1) // blk, count)
    pairs = (high - j - 1) // 2
    lax.fori_loop(0, pairs, step_two, 0)
    lax.fori_loop(j + 1 + 2 * pairs, high, step, 0)
    both = acc_s[...].T
    out_ref[0, 0:HD, :] = (dq_ref[:, here] * 0.125).astype(BF)
    out_ref[0, HD : 2 * HD, :] = (both[HD:, :] * 0.125).astype(BF)
    out_ref[0, 2 * HD :, :] = both[:HD, :].astype(BF)


def attend_back(at, qkv, do, o, lse, before, first, last):
    features, rows = qkv[0].shape
    blk = min(512, rows)
    per = rows // blk
    count = GROUP * per
    dq_shape = (HD, GROUP * rows)
    carried = [pl.BlockSpec(memory_space=pl.ANY), fixed(dq_shape)] if first else []
    return call(
        partial(back_kernel, blk, per, first * per, count),
        "attend_back",
        at,
        ((last - first) * per,),
        [fixed((features, rows))] * GROUP
        + [fixed((HD, rows))] * (2 * GROUP)
        + [fixed((count, 1, blk))]
        + carried,
        [
            pl.BlockSpec((1, features, blk), lambda j, n: ((first + j // per) ^ n[0], 0, j % per)),
            fixed(dq_shape),
        ],
        [like((GROUP, features, rows), BF), like(dq_shape, F32)],
        (*qkv, *do, *o, lse, *(before if first else ())),
        scratch=[
            pltpu.VMEM((GROUP * rows, 128), BF),
            pltpu.VMEM((HD, GROUP * rows), BF),
            pltpu.VMEM((GROUP * rows, 128), BF),
            pltpu.VMEM((128, GROUP * rows), BF),
            pltpu.VMEM((HD, GROUP * rows), BF),
            pltpu.VMEM((2, GROUP * rows, 128), BF),
            pltpu.VMEM((count, 1, blk), F32),
            pltpu.VMEM((blk, 128), F32),
        ],
        alias={3 * GROUP + 2: 0} if first else None,
    )


def split_kernel(at_ref, *refs):
    ins, outs = refs[:GROUP], refs[GROUP:]
    cols = outs[0].shape[1]
    for r in range(4):
        lanes = pl.ds(pl.multiple_of(((at_ref[1] + r) % 4) * cols, cols), cols)
        for s in range(GROUP):
            head = pl.ds(pl.multiple_of((at_ref[0] ^ s) * HD, HD), HD)
            outs[r][head, :] = ins[s][:, lanes]


def split(at, heads):
    rows = heads[0].shape[1]
    shape = (GROUP * HD, rows // 4)
    return call(
        split_kernel,
        "split",
        at,
        (1,),
        [fixed((HD, rows))] * GROUP,
        [fixed(shape)] * 4,
        [like(shape, BF)] * 4,
        heads,
    )


def unsplit_kernel(at_ref, *refs):
    ins, outs = refs[:4], refs[4:]
    cols = ins[0].shape[1]
    for r in range(4):
        lanes = pl.ds(pl.multiple_of(((at_ref[1] + r) % 4) * cols, cols), cols)
        for s in range(GROUP):
            head = pl.ds(pl.multiple_of((at_ref[0] ^ s) * HD, HD), HD)
            outs[s][:, lanes] = ins[r][head, :]


def unsplit(at, pieces):
    shape = (HD, 4 * pieces[0].shape[1])
    return call(
        unsplit_kernel,
        "unsplit",
        at,
        (1,),
        [fixed(pieces[0].shape)] * 4,
        [fixed(shape)] * GROUP,
        [like(shape, BF)] * GROUP,
        pieces,
    )


def heads_of(mine, r, features):
    return pl.ds(pl.multiple_of(((mine + 4 - r) % 4) * features, features), features)


def mid_kernel(at_ref, *refs):
    o_refs, (w_ref, x_ref, gain_ref, bias_ref, h_ref, b_ref) = refs[:4], refs[4:]
    h = x_ref[...].astype(F32)
    for r in range(4):
        rows = heads_of(at_ref[1], r, o_refs[r].shape[0])
        h = h + mm(o_refs[r][...].astype(F32).T.astype(BF), w_ref[rows, :])
    h_ref[...] = h
    normal, _ = normalize(h)
    b_ref[...] = (normal * gain_ref[...] + bias_ref[...]).astype(BF)


def mid(at, o, w_o, tokens, gain, bias):
    features, quarter = o[0].shape
    width = tokens.shape[1]
    return call(
        mid_kernel,
        "mid",
        at,
        (1,),
        [fixed((features, quarter))] * 4
        + [fixed(w_o.shape)]
        + [pl.BlockSpec((quarter, width), lambda i, n: (n[1], 0))]
        + [fixed((1, width))] * 2,
        [fixed((quarter, width))] * 2,
        [like((quarter, width), F32), like((quarter, width), BF)],
        (*o, w_o, tokens, gain, bias),
    )


def add_up(refs):
    total = refs[0][...]
    for ref in refs[1:]:
        total = total + ref[...].astype(F32)
    return total


def mid_back_kernel(at_ref, *refs):
    shares, (w_ref, h_ref, dy_ref, gain_ref, dh_ref, low_ref, sums_ref) = refs[:4], refs[4:11]
    do_refs = refs[11:]
    db = add_up(shares)
    normal, scale = normalize(h_ref[...])
    dh = dy_ref[...].astype(F32) + norm_back(db, gain_ref[...], normal, scale)
    dh_ref[...] = dh
    low = dh.astype(BF)
    low_ref[...] = low
    sums_ref[0:1, :] = jnp.sum(db * normal, axis=0, keepdims=True)
    sums_ref[1:2, :] = jnp.sum(db, axis=0, keepdims=True)
    for r in range(4):
        rows = heads_of(at_ref[1], r, do_refs[r].shape[0])
        do_refs[r][...] = mm_t(w_ref[rows, :], low).astype(BF)


def mid_back(at, shares, w_o, h, dy, gain):
    quarter, width = h.shape
    whole = fixed((quarter, width))
    piece = (w_o.shape[0] // 4, quarter)
    return call(
        mid_back_kernel,
        "mid_back",
        at,
        (1,),
        [whole] * 4 + [fixed(w_o.shape), whole, whole, fixed((1, width))],
        [whole] * 2 + [fixed((2, width))] + [fixed(piece)] * 4,
        [like((quarter, width), F32), like((quarter, width), BF), like((2, width), F32)]
        + [like(piece, BF)] * 4,
        (*shares, w_o, h, dy, gain),
    )


def first_back_kernel(at_ref, *refs):
    shares = refs[:4]
    x_ref, dh_ref, gain_ref, out_ref = refs[4:]
    d_a = add_up(shares)
    normal, scale = normalize(x_ref[...].astype(F32))
    out_ref[...] = (dh_ref[...] + norm_back(d_a, gain_ref[...], normal, scale)).astype(BF)


def first_back(at, shares, tokens, dh, gain):
    quarter, width = dh.shape
    return call(
        first_back_kernel,
        "first_back",
        at,
        (1,),
        [fixed((quarter, width))] * 4
        + [pl.BlockSpec((quarter, width), lambda i, n: (n[1], 0))]
        + [fixed((quarter, width)), fixed((1, width))],
        fixed((quarter, width)),
        like((quarter, width), BF),
        (*shares, tokens, dh, gain),
    )


def in_order(mine, own, right, left, far, right_two, left_two):
    one = jnp.where(mine == 3, far, left)
    two = jnp.where(mine < 2, left_two, right_two)
    three = jnp.where(mine == 0, far, right)
    return own, one, two, three


def one_hot(slots, dest):
    return jnp.where(slots == dest, 1.0, 0.0).astype(BF)


def dispatch_kernel(joined, at_ref, dest_ref, *refs):
    pieces, out_ref, spread_s = refs[:joined], refs[joined], refs[-1]
    blk, rows = min(256, spread_s.shape[0]), dest_ref.shape[1]

    @pl.when(pl.program_id(0) == 0)
    def _():
        slot = lax.broadcasted_iota(jnp.int32, (blk, rows), 0)
        for start in range(0, spread_s.shape[0], blk):
            spread_s[start : start + blk, :] = one_hot(slot + start, dest_ref[...])

    if joined == 1:
        rows_ref = pieces[0]
    else:
        rows_ref = refs[joined + 1]
        start = 0
        for piece in in_order(at_ref[1], *[ref[...] for ref in pieces]):
            rows_ref[start : start + piece.shape[0], :] = piece
            start += piece.shape[0]
    out_ref[...] = mm(spread_s[...], rows_ref[...]).astype(BF)


def columns(rows, width):
    return pl.BlockSpec((rows, width), lambda i, n: (0, i))


def dispatch(at, dest_row, pieces, slots):
    rows, width = dest_row.shape[1], pieces[0].shape[1]
    blk = min(256, width)
    joined = len(pieces) > 1
    return call(
        partial(dispatch_kernel, len(pieces)),
        "dispatch",
        at,
        (width // blk,),
        [fixed((1, rows))] + [columns(piece.shape[0], blk) for piece in pieces],
        [columns(slots, blk)] + [columns(rows, blk)] * joined,
        [like((slots, width), BF)] + [like((rows, width), BF)] * joined,
        (dest_row, *pieces),
        scratch=[pltpu.VMEM((slots, rows), BF)],
    )


def join_kernel(at_ref, *refs):
    pieces, out_ref = refs[:6], refs[6]
    r = pl.program_id(0)
    for place, piece in enumerate(in_order(at_ref[1], *[ref[...] for ref in pieces])):

        @pl.when(r == place)
        def _():
            out_ref[...] = piece


def join(at, pieces):
    each, width = pieces[0].shape
    return call(
        join_kernel,
        "join",
        at,
        (4,),
        [fixed((each, width))] * 6,
        pl.BlockSpec((each, width), lambda r, n: ((n[1] + r) % 4, 0)),
        like((4 * each, width), BF),
        pieces,
    )


def write_shares(mine, total, own_ref, one_ref, two_ref, three_ref, end_ref):
    rows = own_ref.shape[0]
    own_ref[...] = total[:rows]
    one, two, three = [total[r * rows : (r + 1) * rows].astype(BF) for r in (1, 2, 3)]
    one_ref[...] = one
    two_ref[...] = two
    three_ref[...] = three
    end_ref[...] = jnp.where(mine == 0, three, one)


def share_shapes(rows, width):
    return [like((rows, width), F32)] + [like((rows, width), BF)] * 4


def combine_kernel(count, whole, at_ref, *refs):
    dests, backs = refs[:count], refs[count : 2 * count]
    base_ref, refs, pick_s = refs[2 * count], refs[2 * count + 1 : -1], refs[-1]
    rows, slots = base_ref.shape[0], backs[0].shape[0]
    blk = rows // 4

    @pl.when(pl.program_id(0) == 0)
    def _():
        lane = lax.broadcasted_iota(jnp.int32, (blk, slots), 1)
        for k in range(count):
            for start in range(0, rows, blk):
                dest = dests[k][start : start + blk, :]
                pick_s[start : start + blk, k * slots : (k + 1) * slots] = one_hot(lane, dest)

    total = base_ref[...].astype(F32)
    for k in range(count):
        total = total + mm(pick_s[:, k * slots : (k + 1) * slots], backs[k][...])
    mine = at_ref[1]
    if whole:
        h_ref, out_ref = refs
        for r in range(4):
            part = total[r * blk : (r + 1) * blk]
            if r == 0:
                part = part + h_ref[...]
            place = pl.ds(pl.multiple_of(((mine + r) % 4) * blk, blk), blk)
            out_ref[place, :] = part.astype(BF)
    else:
        write_shares(mine, total, *refs)


def combine(at, dests, backs, base, h=None):
    count, (slots, width), rows = len(backs), backs[0].shape, base.shape[0]
    blk = min(256, width)
    whole = h is not None
    quarter = columns(rows // 4, blk)
    return call(
        partial(combine_kernel, count, whole),
        "combine",
        at,
        (width // blk,),
        [fixed((rows, 1))] * count
        + [columns(slots, blk)] * count
        + [columns(rows, blk)]
        + [quarter] * whole,
        columns(rows, blk) if whole else [quarter] * 5,
        like(base.shape, BF) if whole else share_shapes(rows // 4, width),
        (*dests, *backs, base) + ((h,) if whole else ()),
        scratch=[pltpu.VMEM((rows, count * slots), BF)],
    )


def mm_t(a, b):
    return lax.dot_general(a, b, (((1,), (1,)), ((), ())), preferred_element_type=F32)


def gelu_both(u):
    c = 0.7978845608028654
    square = u * u
    t = jnp.tanh(u * (c + (c * 0.044715) * square))
    half = 0.5 + 0.5 * t
    slope = half + (0.5 * u) * (1.0 - t * t) * (c + (3.0 * c * 0.044715) * square)
    return u * half, slope


def high_low(value):
    high = value.astype(BF)
    return high, (value - high.astype(F32)).astype(BF)


def two_coefs(logits, lane, experts):
    inside = (lane >= experts) & (lane < experts + 2)
    top = jnp.max(jnp.where(inside, logits, HIDE), axis=1, keepdims=True)
    e = jnp.where(inside, jnp.exp(logits - top), 0.0)
    e = e / jnp.sum(e, axis=1, keepdims=True)
    first = jnp.sum(jnp.where(lane == experts, e, 0.0), axis=1, keepdims=True)
    second = jnp.sum(jnp.where(lane == experts + 1, e, 0.0), axis=1, keepdims=True)
    return first, second


def small_back(d_small, rows, w_small_ref, small_ref, i):
    high, low = high_low(d_small)
    w_small = w_small_ref[...]
    high_t, low_t = high_low(d_small.T)

    @pl.when(i == 0)
    def _():
        small_ref[...] = jnp.zeros(small_ref.shape, F32)

    small_ref[...] += mm(high_t, rows) + mm(low_t, rows)
    return mm_t(high, w_small) + mm_t(low, w_small)


def expert_kernel(experts, half, at_ref, rows_ref, dy_ref, up_ref, down_ref, w_small_ref, *outs):
    if half:
        outs = outs[5:]
    rows_out_ref, hid_ref, dy_out_ref, deu_ref, y_ref, d_rows_ref, small_ref = outs
    rows = rows_ref[...]
    rows_out_ref[...] = rows
    up = mm(rows, up_ref[...])
    logits = mm(rows, w_small_ref[...])
    lane = lax.broadcasted_iota(jnp.int32, logits.shape, 1)
    routed = lane < experts
    top = jnp.max(jnp.where(routed, logits, HIDE), axis=1, keepdims=True)
    probs = jnp.where(routed, jnp.exp(logits - top), 0.0)
    probs = probs / jnp.sum(probs, axis=1, keepdims=True)
    own = jnp.where(lane == at_ref[2], 1.0, 0.0)
    gate = jnp.sum(probs * own, axis=1, keepdims=True)
    first, second = two_coefs(logits, lane, experts)
    weight = second * gate
    dy = dy_ref[...].reshape(rows.shape).astype(F32)
    d_y = (weight * dy).astype(BF)
    dy_out_ref[...] = d_y
    d_hidden = mm_t(d_y, down_ref[...])
    hidden, slope = gelu_both(up)
    hidden = hidden.astype(BF)
    hid_ref[...] = hidden
    d_up = (d_hidden * slope).astype(BF)
    deu_ref[...] = d_up
    y = mm(hidden, down_ref[...])
    y_ref[...] = (weight * y).astype(BF).reshape(y_ref.shape)
    along = gate * jnp.sum(dy * y, axis=1, keepdims=True)
    mixed = first * second * along
    d_small = (second * along) * (own - probs)
    d_small = jnp.where(routed, d_small, 0.0)
    d_small = d_small + jnp.where(lane == experts + 1, mixed, 0.0)
    d_small = d_small - jnp.where(lane == experts, mixed, 0.0)
    d_rows = mm_t(d_up, up_ref[...]) + small_back(d_small, rows, w_small_ref, small_ref, pl.program_id(0))
    d_rows_ref[...] = d_rows.astype(BF)


def expert_rows(at, rows, dy, w_up, w_down, w_small, experts, half, before):
    count, width = rows.shape
    hid, lanes = w_up.shape[1], w_small.shape[1]
    blk = min(512, count)
    capacity = count // dy.shape[0]
    steps = count // blk
    moving = pl.BlockSpec((blk, width), lambda i, n: (i, 0))
    slots = pl.BlockSpec((blk // capacity, capacity, width), lambda i, n: (i, half, 0))
    kept = [pl.BlockSpec((blk, size), lambda i, n: (i + half * steps, 0)) for size in (width, hid, width, hid)]
    return call(
        partial(expert_kernel, experts, half),
        "expert_rows",
        at,
        (steps,),
        [
            moving,
            slots,
            fixed((width, hid)),
            fixed((hid, width)),
            fixed((width, lanes)),
        ]
        + [pl.BlockSpec(memory_space=pl.ANY)] * (5 * half),
        kept + [slots, moving, fixed((lanes, width))],
        [like((2 * count, size), BF) for size in (width, hid, width, hid)]
        + [like(dy.shape, BF), like((count, width), BF)]
        + [like((lanes, width), F32)],
        (rows, dy, w_up, w_down, w_small, *before),
        alias={6 + k: k for k in range(5)} if half else None,
        vmem=56,
    )


def dense_kernel(experts, at_ref, rows_ref, dy_ref, in_ref, out_ref, w_small_ref, *outs):
    hid_ref, grad_ref, d_up_ref, mix_ref, db_ref, small_ref = outs
    rows = rows_ref[...]
    up = mm(rows, in_ref[...])
    logits = mm(rows, w_small_ref[...])
    lane = lax.broadcasted_iota(jnp.int32, logits.shape, 1)
    first, second = two_coefs(logits, lane, experts)
    dy = dy_ref[...].astype(F32)
    grad = (first * dy).astype(BF)
    grad_ref[...] = grad
    d_hidden = mm_t(grad, out_ref[...])
    hidden, slope = gelu_both(up)
    hidden = hidden.astype(BF)
    hid_ref[...] = hidden
    d_up = (d_hidden * slope).astype(BF)
    d_up_ref[...] = d_up
    dense = mm(hidden, out_ref[...])
    mix_ref[...] = first * dense
    mixed = first * second * jnp.sum(dy * dense, axis=1, keepdims=True)
    d_small = jnp.where(lane == experts, mixed, 0.0) - jnp.where(lane == experts + 1, mixed, 0.0)
    db_ref[...] = mm_t(d_up, in_ref[...]) + small_back(d_small, rows, w_small_ref, small_ref, pl.program_id(0))


def dense_rows(at, rows, dy, w_in, w_out, w_small, experts):
    (count, width), hid, lanes = rows.shape, w_in.shape[1], w_small.shape[1]
    blk = min(512, count)
    row_out = pl.BlockSpec((blk, width), lambda i, n: (i, 0))
    hid_out = pl.BlockSpec((blk, hid), lambda i, n: (i, 0))
    return call(
        partial(dense_kernel, experts),
        "dense_rows",
        at,
        (count // blk,),
        [row_out, row_out, fixed((width, hid)), fixed((hid, width)), fixed((width, lanes))],
        [hid_out, row_out, hid_out, row_out, row_out, fixed((lanes, width))],
        [
            like((count, hid), BF),
            like((count, width), BF),
            like((count, hid), BF),
            like((count, width), F32),
            like((count, width), F32),
            like((lanes, width), F32),
        ],
        (rows, dy, w_in, w_out, w_small),
        vmem=56,
    )


def turned(value):
    return value.astype(F32).T.astype(BF)


def dense_grads_kernel(at_ref, b_ref, d_up_ref, grad_ref, hid_ref, keep_ref, give_ref):
    width = d_up_ref.shape[1]
    first = mm(turned(b_ref[...]), d_up_ref[...]).astype(BF)
    second = mm(turned(grad_ref[...]), hid_ref[...]).astype(BF)
    half = pl.num_programs(0) // 2
    for side, ref in ((0, keep_ref), (1, give_ref)):

        @pl.when(pl.program_id(0) // half == side)
        def _():
            ref[0, :, :width] = first
            ref[0, :, width:] = second


def dense_grads(at, b, d_up, grad, hidden, parts):
    (rows, width), hid = b.shape, hidden.shape[1]
    own, half, bits = width // parts, parts // 2, parts.bit_length() - 1

    def part(q, n):
        turned_q = sum([((q // 2**k) % 2) * 2 ** (bits - 1 - k) for k in range(bits)])
        return turned_q ^ n[2]

    column = pl.BlockSpec((rows, own), lambda q, n: (0, part(q, n)))
    shape = (1, own, 2 * hid)
    return call(
        dense_grads_kernel,
        "dense_grads",
        at,
        (parts,),
        [column, fixed((rows, hid)), column, fixed((rows, hid))],
        [
            pl.BlockSpec(shape, lambda q, n: (jnp.minimum(q, half - 1), 0, 0)),
            pl.BlockSpec(shape, lambda q, n: (jnp.maximum(q - half, 0), 0, 0)),
        ],
        [like((half, own, 2 * hid), BF)] * 2,
        (b, d_up, grad, hidden),
    )


def attention_grads_kernel(experts, at_ref, *refs):
    grads, o_refs, refs = refs[:GROUP], refs[GROUP : GROUP + 4], refs[GROUP + 4 :]
    a_ref, dh_ref, w_ref, gain_ref, bias_ref, sums_ref = refs[:6]
    small_refs, (out_ref, all_s) = refs[6:-2], refs[-2:]
    heads, features = GROUP * HD, grads[1].shape[0]
    products, plain = 0.0, 0.0
    for k in range(GROUP):
        head = at_ref[0] ^ k
        rows = pl.ds(pl.multiple_of(head * features, features), features)
        grad = grads[k][...]
        grad = grad[0] if k == 0 else grad
        weight = w_ref[head].astype(F32)
        total = mm(grad, a_ref[...])
        all_s[rows, :] = total
        each = jnp.sum(grad.astype(F32), axis=1, keepdims=True)
        products = products + jnp.sum(total * weight, axis=0, keepdims=True)
        plain = plain + jnp.sum(each * weight, axis=0, keepdims=True)
    first = GROUP * features
    for r in range(4):
        rows = pl.ds(pl.multiple_of(first + ((at_ref[1] + 4 - r) % 4) * heads, heads), heads)
        all_s[rows, :] = mm(o_refs[r][...], dh_ref[...])
    first += 4 * heads
    small = add_up(small_refs)
    row = lax.broadcasted_iota(jnp.int32, small.shape, 0)
    d_gain = (products - bias_ref[...] * plain) / gain_ref[...]
    for k, sums in enumerate((sums_ref[0:1, :], sums_ref[1:2, :], d_gain, plain)):
        small = jnp.where(row == experts + 2 + k, sums, small)
    all_s[first:, :] = small
    out_ref[...] = all_s[...].T.astype(BF)


def attention_grads(at, held, came, o, a, dh, w_heads, gain, bias, sums, small, experts):
    rows, width = a.shape
    features, lanes = held.shape[1], small[0].shape[0]
    height = GROUP * features + 4 * o[0].shape[0] + lanes
    blk = min(256, width)
    return call(
        partial(attention_grads_kernel, experts),
        "attention_grads",
        at,
        (width // blk,),
        [fixed((1, features, rows))]
        + [fixed((features, rows))] * 3
        + [fixed(o[0].shape)] * 4
        + [columns(rows, blk), columns(dh.shape[0], blk)]
        + [pl.BlockSpec((GROUP, features, blk), lambda i, n: (0, 0, i))]
        + [columns(1, blk)] * 2
        + [columns(2, blk)]
        + [columns(lanes, blk)] * len(small),
        pl.BlockSpec((blk, height), lambda i, n: (i, 0)),
        like((width, height), BF),
        (held, *came, *o, a, dh, w_heads, gain, bias, sums, *small),
        scratch=[pltpu.VMEM((height, blk), F32)],
    )


def project_kernel(at_ref, *refs):
    grads, w_ref, outs, turned_s = refs[:GROUP], refs[GROUP], refs[GROUP + 1 : -1], refs[-1]
    rows = turned_s.shape[1]
    blk = rows // 4

    @pl.when(pl.program_id(0) == 0)
    def _():
        for s in range(GROUP):
            for r in range(4):
                lanes = pl.ds(pl.multiple_of(((at_ref[1] + r) % 4) * blk, blk), blk)
                grad = grads[s][0, :, lanes] if s == 0 else grads[s][:, lanes]
                turned_s[s, r * blk : (r + 1) * blk, :] = turned(grad)

    total = 0.0
    for s in range(GROUP):
        total = total + mm(turned_s[s], w_ref[at_ref[0] ^ s])
    write_shares(at_ref[1], total, *outs)


def project_back(at, held, came, w_heads):
    _, features, rows = held.shape
    width = w_heads.shape[2]
    blk = min(256, width)
    return call(
        project_kernel,
        "project_back",
        at,
        (width // blk,),
        [fixed((1, features, rows))]
        + [fixed((features, rows))] * 3
        + [pl.BlockSpec((GROUP, features, blk), lambda i, n: (0, 0, i))],
        [columns(rows // 4, blk)] * 5,
        share_shapes(rows // 4, width),
        (held, *came, w_heads),
        scratch=[pltpu.VMEM((GROUP, rows, features), BF)],
    )


def hop(value, *pairs):
    return lax.ppermute(value, "mp", pairs)


def rotate(value, steps):
    return hop(value, *[(s, (s + steps) % 4) for s in range(4)])


def gather_near(own):
    right = hop(own, (0, 1), (1, 2), (2, 3))
    left = hop(own, (1, 0), (2, 1), (3, 2))
    return own, right, left, hop(own, (0, 3), (3, 0))


def gather_far(near):
    _, right, left, _ = near
    return *near, hop(right, (1, 2), (2, 3)), hop(left, (1, 0), (2, 1))


def gather_pieces(own):
    return gather_far(gather_near(own))


def scatter_far(shares):
    _, _, two, _, end = shares
    return hop(two, (2, 1), (3, 2)), hop(two, (0, 1), (1, 2)), hop(end, (0, 3), (3, 0))


def scatter_near(shares, came):
    own, one, _, three, _ = shares
    from_right, from_left, from_end = came
    three = (three.astype(F32) + from_right.astype(F32)).astype(BF)
    one = (one.astype(F32) + from_left.astype(F32)).astype(BF)
    return own, hop(three, (1, 0), (2, 1), (3, 2)), hop(one, (0, 1), (1, 2), (2, 3)), from_end


def group_swap(value, s):
    count = lax.axis_size("dp")
    return lax.ppermute(value, "dp", [(t, t ^ s) for t in range(count)])


def expert_swap(value, experts):
    wide = value.reshape(experts, value.shape[0] // experts, value.shape[1])
    return lax.all_to_all(wide, "dp", 0, 0, tiled=True).reshape(value.shape)


def roll_rows(value, start):
    twice = jnp.concatenate([value, value], axis=0)
    return lax.dynamic_slice_in_dim(twice, start, value.shape[0], 0)


def add_halves(keep, came):
    return (keep.astype(F32) + came.astype(F32)).astype(BF)


def body(
    tokens,
    cotangent,
    ln_gains,
    ln_biases,
    w_qkv,
    w_o,
    w_in,
    w_out,
    w_router,
    w_coef,
    w_up,
    w_down,
    routes,
    long_group,
):
    rows, width = tokens.shape
    dps = lax.axis_size("dp")
    mine, position = lax.axis_index("mp"), lax.axis_index("dp")
    quarter = rows // 4
    start = mine * quarter
    heads_loc = w_qkv.shape[2] // HD
    hid = w_in.shape[1]
    experts = w_router.shape[1]
    capacity = max(2, 2 * rows // experts)
    half = capacity // 2
    barrier = lax.optimization_barrier
    first_len = lax.dynamic_index_in_dim(long_group, position // GROUP, 0, keepdims=False)
    at = jnp.stack([position % GROUP, mine, position, first_len]).astype(jnp.int32)
    gains = [ln_gains[0:1], ln_gains[1:2]]
    biases = [ln_biases[0:1], ln_biases[1:2]]
    w_o_all = lax.all_gather(w_o, "mp", axis=0, tiled=True)

    w_heads = w_qkv.reshape(width, 3, heads_loc, HD).transpose(2, 1, 3, 0)
    w_heads = w_heads.reshape(heads_loc, 3 * HD, width)
    a_r, *qkv = project(at, tokens, gains[0], biases[0], w_heads)
    qkv = [qkv[0]] + [group_swap(qkv[s], s) for s in (1, 2, 3)]

    route = roll_rows(routes, start)[:, 0]
    picked = (route[:, None] == jnp.arange(experts, dtype=jnp.int32)[None, :]).astype(jnp.int32)
    slot = jnp.sum((jnp.cumsum(picked, axis=0) - picked) * picked, axis=1)
    dy_b = roll_rows(cotangent, start)
    send_dy = dispatch(at, (route * capacity + slot)[None, :], [dy_b], experts * capacity)[0]
    *qkv, send_dy = barrier((*qkv, send_dy))
    in_half = [slot < half, slot >= half]
    dests = [
        jnp.where(in_half[k], route * half + slot - k * half, -1).astype(jnp.int32) for k in (0, 1)
    ]

    *o_t, lse = attend(at, qkv)
    *o_t, w_o_all = barrier((*o_t, w_o_all))
    o_heads = [o_t[0]] + [group_swap(o_t[s], s) for s in (1, 2, 3)]
    pieces = split(at, o_heads)
    o_q = [pieces[0]] + [rotate(pieces[r], r) for r in (1, 2, 3)]
    lanes = -(-(experts + 2) // 128) * 128
    w_small = jnp.concatenate(
        [w_router, w_coef, jnp.zeros((width, lanes - experts - 2), BF)], axis=1
    )
    *o_q, send_dy, w_small = barrier((*o_q, send_dy, w_small))
    got_dy = expert_swap(send_dy, experts).reshape(experts, capacity, width)
    h, b_q = mid(at, o_q, w_o_all, tokens, gains[1], biases[1])

    pieces = gather_pieces(b_q)
    send_0, b_r = dispatch(at, dests[0][None, :], pieces, experts * half)
    send_0, got_dy = barrier((send_0, got_dy))
    got_0 = expert_swap(send_0, experts)
    send_1 = dispatch(at, dests[1][None, :], [b_r], experts * half)[0]
    b_r, send_1 = barrier((b_r, send_1))
    hidden, dense_grad, d_up, mix_base, db_base, small_t = dense_rows(
        at, b_r, dy_b, w_in, w_out, w_small, experts
    )
    send_1, got_0, db_base = barrier((send_1, got_0, db_base))
    got_1 = expert_swap(send_1, experts)

    *kept, d_rows_0, small_0 = expert_rows(
        at, got_0, got_dy, w_up[0], w_down[0], w_small, experts, 0, ()
    )
    back_0 = expert_swap(d_rows_0, experts)
    *kept, d_rows_1, small_1 = expert_rows(
        at, got_1, got_dy, w_up[0], w_down[0], w_small, experts, 1, kept
    )
    got, hidden_e, d_y, d_eu, back_y = kept
    back_1 = expert_swap(d_rows_1, experts)
    d_rows_1, b_r = barrier((d_rows_1, b_r))
    halving = width == dps * 128
    if halving:
        grads = dense_grads(at, b_r, d_up, dense_grad, hidden, dps)
    else:
        grads = [ein("td,tf->df", b_r, d_up).astype(BF), ein("td,tf->df", dense_grad, hidden).astype(BF)]
    back_0, back_1, back_y, *grads = barrier((back_0, back_1, back_y, *grads))

    dest_cols = [dest[:, None] for dest in dests]
    tok_y = expert_swap(back_y.reshape(experts * capacity, width), experts)
    shares = combine(at, dest_cols, [back_0, back_1], db_base)
    far = scatter_far(shares)
    *far, g_0, g_1 = barrier((*far, *grads))
    grads = [g_0, g_1]
    shares = scatter_near(shares, far)
    dh, dh_r, sums_2, *do_q = mid_back(at, shares, w_o_all, h, dy_b[:quarter], gains[1])
    do_q = [do_q[0]] + [rotate(do_q[r], -r) for r in (1, 2, 3)]

    mix = combine(at, [(route * capacity + slot)[:, None]], [tok_y], mix_base, h)
    *do_q, mix = barrier((*do_q, mix))
    output = lax.psum(mix, "mp")
    do_heads = unsplit(at, do_q)
    do_t = [do_heads[0]] + [group_swap(do_heads[s], s) for s in (1, 2, 3)]
    if halving:
        came_1 = group_swap(grads[1], 1)
        half = dps // 4
        give = add_halves(grads[0][half:], came_1[half:])
        *do_t, give = barrier((*do_t, give))
        came_2 = group_swap(give, 2)
    d_qkv, _ = attend_back(at, qkv, do_t, o_t, lse, None, 0, GROUP)
    if halving:
        keep = add_halves(grads[0][:half], came_1[:half])
        d_qkv, came_2, keep = barrier((d_qkv, came_2, keep))
        grads = add_halves(keep, came_2)
        bit = 4
        while bit < dps:
            half = grads.shape[0] // 2
            grads = add_halves(grads[:half], group_swap(grads[half:], bit))
            bit *= 2
        grads = [grads[0][:, :hid], grads[0][:, hid:]]
    else:
        grads = [lax.psum_scatter(grad, "dp", scatter_dimension=0, tiled=True) for grad in grads]

    came = [group_swap(d_qkv[s], s) for s in (1, 2, 3)]
    d_qkv, got, hidden_e, d_y, d_eu = barrier((d_qkv, got, hidden_e, d_y, d_eu))
    grad_down = ein("rf,rd->fd", hidden_e, d_y)
    *came, grad_down = barrier((*came, grad_down))
    grads_a = attention_grads(
        at, d_qkv, came, o_q, a_r, dh_r, w_heads, gains[0], biases[0], sums_2, (small_0, small_1, small_t), experts
    )
    d_qkv, grads_a = barrier((d_qkv, grads_a))
    shares = project_back(at, d_qkv, came, w_heads)
    far = scatter_far(shares)
    grads_a, output = barrier((grads_a, output))
    grads_a = lax.psum_scatter(grads_a, "dp", scatter_dimension=0, tiled=True).T
    grad_up = ein("rd,rf->df", got, d_eu)
    *far, grad_up = barrier((*far, grad_up))
    shares = scatter_near(shares, far)
    grad_q = first_back(at, shares, tokens, dh, gains[0])
    grad_tokens = join(at, gather_pieces(grad_q))

    own, heads = width // dps, heads_loc * HD
    grad_qkv = grads_a[: 3 * heads].astype(F32).reshape(heads_loc, 3, HD, own).transpose(3, 1, 0, 2)
    grad_qkv = grad_qkv.reshape(own, 3, heads)
    grad_in = grads[0].astype(F32)
    grad_out = grads[1].astype(F32).T
    rest = grads_a[3 * heads : 7 * heads].reshape(4, heads, own)
    small = jnp.broadcast_to(grads_a[7 * heads :], (4, lanes, own))
    rest = lax.all_to_all(jnp.concatenate([rest, small], axis=1), "mp", 0, 0, tiled=True)
    rest = jnp.sum(rest.astype(F32), axis=0)
    grad_o, small = rest[:heads], rest[heads:]
    small_out = small[: experts + 2].T
    return (
        output,
        grad_tokens,
        jnp.stack([small[experts + 4], small[experts + 2]]),
        jnp.stack([small[experts + 5], small[experts + 3]]),
        grad_qkv,
        grad_o,
        grad_in,
        grad_out,
        small_out[:, :experts],
        small_out[:, experts:],
        grad_up[None],
        grad_down[None],
    )


def solution(mesh):
    in_specs = (
        P("dp", None),
        P("dp", None),
        P(),
        P(),
        P(None, None, "mp"),
        P("mp", None),
        P(None, "mp"),
        P("mp", None),
        P(),
        P(),
        P("dp", None, "mp"),
        P("dp", "mp", None),
        P("dp", None),
        P(),
    )
    out_specs = (
        P("dp", None),
        P("dp", None),
        P(None, "dp"),
        P(None, "dp"),
        P("dp", None, "mp"),
        P("mp", "dp"),
        P("dp", "mp"),
        P("mp", "dp"),
        P("dp", None),
        P("dp", None),
        P("dp", None, "mp"),
        P("dp", "mp", None),
    )
    return jax.shard_map(body, mesh=mesh, in_specs=in_specs, out_specs=out_specs, check_vma=False)
```

```python
from functools import partial

import jax
import jax.numpy as jnp
from jax import lax
from jax.experimental import pallas as pl
from jax.experimental.pallas import tpu as pltpu
from jax.sharding import PartitionSpec as P

HD = 64
GROUP = 4
EPS = 1e-05
LOG2E = 1.4426950408889634
SCALE2 = 0.125 * LOG2E
HIDE = -1e30
BF = jnp.bfloat16
F32 = jnp.float32
LIGHT = pl.CostEstimate(flops=1 << 20, bytes_accessed=1 << 20, transcendentals=0)


def mm(a, b):
    return jnp.dot(a, b, preferred_element_type=F32)


def ein(spec, a, b):
    return jnp.einsum(spec, a, b, preferred_element_type=F32)


def call(kernel, name, prefetch, grid, in_specs, out_specs, out_shape, args, scratch=(), alias=None, vmem=48):
    return pl.pallas_call(
        kernel,
        grid_spec=pltpu.PrefetchScalarGridSpec(
            num_scalar_prefetch=1,
            grid=grid,
            in_specs=in_specs,
            out_specs=out_specs,
            scratch_shapes=list(scratch),
        ),
        out_shape=out_shape,
        input_output_aliases=alias or {},
        compiler_params=pltpu.CompilerParams(vmem_limit_bytes=vmem * 2**20),
        cost_estimate=LIGHT,
        name=name,
    )(prefetch, *args)


def fixed(shape):
    zeros = (0,) * len(shape)
    return pl.BlockSpec(shape, lambda *_: zeros)


def like(shape, dtype):
    return jax.ShapeDtypeStruct(shape, dtype)


def normalize(v):
    mean = jnp.mean(v, axis=-1, keepdims=True)
    centred = v - mean
    scale = lax.rsqrt(jnp.mean(centred * centred, axis=-1, keepdims=True) + EPS)
    return centred * scale, scale


def norm_back(grad, gain, normal, scale):
    g = grad * gain
    along = jnp.mean(g * normal, axis=-1, keepdims=True)
    return scale * (g - jnp.mean(g, axis=-1, keepdims=True) - normal * along)


def qkv_kernel(at_ref, x_ref, gain_ref, bias_ref, w_ref, a_ref, *outs):
    normal, _ = normalize(x_ref[...].astype(F32))
    a = (normal * gain_ref[...] + bias_ref[...]).astype(BF)
    a_ref[...] = a
    for s in range(GROUP):
        outs[s][...] = mm_t(w_ref[at_ref[0] ^ s], a).astype(BF)


def project(at, tokens, gain, bias, w_heads):
    rows, width = tokens.shape
    features = w_heads.shape[1]
    blk = min(256, rows)
    moving = pl.BlockSpec((blk, width), lambda i, n: (i, 0))
    return call(
        qkv_kernel,
        "project",
        at,
        (rows // blk,),
        [moving, fixed((1, width)), fixed((1, width)), fixed(w_heads.shape)],
        [moving] + [pl.BlockSpec((features, blk), lambda i, n: (0, i))] * GROUP,
        [like((rows, width), BF)] + [like((features, rows), BF)] * GROUP,
        (tokens, gain, bias, w_heads),
    )


def fill_keys(k_s, place, keys, first_len, blk):
    rows = place * blk + lax.broadcasted_iota(jnp.int32, (blk, 128), 0)
    lane = lax.broadcasted_iota(jnp.int32, (blk, 128), 1)
    wide = jnp.concatenate([keys.astype(F32).T, jnp.zeros((blk, 128 - HD), F32)], axis=1)
    wide = jnp.where((lane == HD) & (rows < first_len), HIDE, wide)
    k_s[pl.ds(place * blk, blk), :] = wide.astype(BF)


def wide_query(query, place, first_len, blk):
    cols = place * blk + lax.broadcasted_iota(jnp.int32, (128 - HD, blk), 1)
    sub = lax.broadcasted_iota(jnp.int32, (128 - HD, blk), 0)
    extra = jnp.where((sub == 0) & (cols >= first_len), 1.0, 0.0)
    return jnp.concatenate([query, extra.astype(BF)], axis=0)


def causal(blk):
    keys = lax.broadcasted_iota(jnp.int32, (blk, blk), 0)
    queries = lax.broadcasted_iota(jnp.int32, (blk, blk), 1)
    return keys <= queries


def attend_kernel(blk, per, at_ref, *refs):
    qkv_refs, o_refs = refs[:GROUP], refs[GROUP : 2 * GROUP]
    lse_ref, k_s, qkv_s = refs[2 * GROUP :]
    i = pl.program_id(0)
    place, first_len = at_ref[0], at_ref[3]

    @pl.when(i == 0)
    def _():
        for s in range(GROUP):
            qkv_s[place ^ s] = qkv_refs[s][...]

    def part(which, j):
        return qkv_s[j // per, HD * which : HD * (which + 1), pl.ds((j % per) * blk, blk)]

    fill_keys(k_s, i, part(1, i), first_len, blk)
    query = wide_query(part(0, i), i, first_len, blk)

    def scores(j):
        return mm(k_s[pl.ds(pl.multiple_of(j * blk, blk), blk), :], query)

    s = jnp.where(causal(blk), scores(i), HIDE)
    top = jnp.max(s, axis=0, keepdims=True)
    p = jnp.exp2((s - top) * SCALE2)
    total = jnp.sum(p, axis=0, keepdims=True)
    acc = mm(part(2, i), p.astype(BF))

    def steps(blocks, carry):
        top, total, acc = carry
        s = [scores(j) for j in blocks]
        new = top
        for one in s:
            new = jnp.maximum(new, jnp.max(one, axis=0, keepdims=True))
        keep = jnp.exp2((top - new) * SCALE2)
        total, acc = total * keep, acc * keep
        for j, one in zip(blocks, s):
            p = jnp.exp2((one - new) * SCALE2)
            total = total + jnp.sum(p, axis=0, keepdims=True)
            acc = acc + mm(part(2, j), p.astype(BF))
        return new, total, acc

    low = jnp.where(i * blk >= first_len, first_len // blk, 0)
    pairs = (i - low) // 2
    carry = lax.fori_loop(
        0, pairs, lambda t, c: steps([low + 2 * t, low + 2 * t + 1], c), (top, total, acc)
    )
    top, total, acc = lax.fori_loop(low + 2 * pairs, i, lambda j, c: steps([j], c), carry)
    out = (acc / total).astype(BF)
    for s in range(GROUP):

        @pl.when((i // per) ^ place == s)
        def _():
            o_refs[s][:, pl.ds((i % per) * blk, blk)] = out

    lse_ref[0] = top * SCALE2 + jnp.log2(total)


def attend(at, qkv):
    features, rows = qkv[0].shape
    blk = min(512, rows)
    per = rows // blk
    count = GROUP * per
    return call(
        partial(attend_kernel, blk, per),
        "attend",
        at,
        (count,),
        [fixed((features, rows))] * GROUP,
        [fixed((HD, rows))] * GROUP + [pl.BlockSpec((1, 1, blk), lambda i, n: (i, 0, 0))],
        [like((HD, rows), BF)] * GROUP + [like((count, 1, blk), F32)],
        qkv,
        scratch=[pltpu.VMEM((GROUP * rows, 128), BF), pltpu.VMEM((GROUP, features, rows), BF)],
    )


def back_kernel(blk, per, count, at_ref, *refs):
    qkv_refs, do_refs, o_refs = refs[:GROUP], refs[GROUP : 2 * GROUP], refs[2 * GROUP : 3 * GROUP]
    lse_ref, refs = refs[3 * GROUP], refs[3 * GROUP + 1 :]
    out_refs, refs = refs[:GROUP], refs[GROUP:]
    dq_ref, out_ref, k_s, kt_s, v_s, wide_s, dot_s, both_s, delta_s, acc_s = refs
    j = pl.program_id(0)
    place, first_len = at_ref[0], at_ref[3]

    @pl.when(j == 0)
    def _():
        dq_ref[...] = jnp.zeros(dq_ref.shape, F32)
        zero = jnp.zeros((blk, HD), F32)
        for s in range(GROUP):
            for sub in range(per):
                i = (place ^ s) * per + sub
                at = pl.ds(pl.multiple_of(i * blk, blk), blk)
                cut = slice(sub * blk, (sub + 1) * blk)
                query = qkv_refs[s][0:HD, cut]
                keys = qkv_refs[s][HD : 2 * HD, cut]
                grad = do_refs[s][:, cut]
                fill_keys(k_s, i, keys, first_len, blk)
                kt_s[:, at] = keys
                dot_s[:, at] = grad
                wide_s[:, at] = wide_query(query, i, first_len, blk)
                grad = grad.astype(F32)
                values = qkv_refs[s][2 * HD :, cut].astype(F32)
                v_s[at, :] = jnp.concatenate([values.T, zero], axis=1).astype(BF)
                both_s[0, at, :] = jnp.concatenate([grad.T, zero], axis=1).astype(BF)
                both_s[1, at, :] = jnp.concatenate([zero, query.astype(F32).T], axis=1).astype(BF)
                held = o_refs[s][:, cut].astype(F32)
                delta_s[i] = jnp.sum(held * grad, axis=0, keepdims=True)

    here = pl.ds(pl.multiple_of(j * blk, blk), blk)
    keys_t = kt_s[:, here]
    values = v_s[here, 0:HD]

    def pair(i, diagonal):
        at = pl.ds(pl.multiple_of(i * blk, blk), blk)
        s = mm(k_s[here, :], wide_s[:, at])
        p = jnp.exp2(s * SCALE2 - lse_ref[i])
        if diagonal:
            p = jnp.where(causal(blk), p, 0.0)
        dp = mm(values, dot_s[:, at])
        ds = (p * (dp - delta_s[i])).astype(BF)
        return mm(p.astype(BF), both_s[0, at, :]) + mm(ds, both_s[1, at, :]), mm(keys_t, ds)

    acc_s[...], dq = pair(j, True)
    dq_ref[:, here] += dq

    def step_two(t, carry):
        i = j + 1 + 2 * t
        (kv_0, dq_0), (kv_1, dq_1) = pair(i, False), pair(i + 1, False)
        acc_s[...] += kv_0 + kv_1
        at = pl.ds(pl.multiple_of(i * blk, blk), 2 * blk)
        dq_ref[:, at] += jnp.concatenate([dq_0, dq_1], axis=1)
        return carry

    def step(i, carry):
        kv, dq = pair(i, False)
        acc_s[...] += kv
        dq_ref[:, pl.ds(pl.multiple_of(i * blk, blk), blk)] += dq
        return carry

    high = jnp.where((j + 1) * blk <= first_len, (first_len + blk - 1) // blk, count)
    pairs = (high - j - 1) // 2
    lax.fori_loop(0, pairs, step_two, 0)
    lax.fori_loop(j + 1 + 2 * pairs, high, step, 0)
    both = acc_s[...].T
    out_ref[0:HD, :] = (dq_ref[:, here] * 0.125).astype(BF)
    out_ref[HD : 2 * HD, :] = (both[HD:, :] * 0.125).astype(BF)
    out_ref[2 * HD :, :] = both[:HD, :].astype(BF)
    for s in range(GROUP):

        @pl.when((j // per) ^ place == s)
        def _():
            out_refs[s][:, pl.ds(pl.multiple_of((j % per) * blk, blk), blk)] = out_ref[...]


def attend_back(at, qkv, do, o, lse):
    features, rows = qkv[0].shape
    blk = min(512, rows)
    per = rows // blk
    count = GROUP * per
    return call(
        partial(back_kernel, blk, per, count),
        "attend_back",
        at,
        (count,),
        [fixed((features, rows))] * GROUP
        + [fixed((HD, rows))] * (2 * GROUP)
        + [fixed((count, 1, blk))],
        [fixed((features, rows))] * GROUP,
        [like((features, rows), BF)] * GROUP,
        (*qkv, *do, *o, lse),
        scratch=[
            pltpu.VMEM((HD, GROUP * rows), F32),
            pltpu.VMEM((features, blk), BF),
            pltpu.VMEM((GROUP * rows, 128), BF),
            pltpu.VMEM((HD, GROUP * rows), BF),
            pltpu.VMEM((GROUP * rows, 128), BF),
            pltpu.VMEM((128, GROUP * rows), BF),
            pltpu.VMEM((HD, GROUP * rows), BF),
            pltpu.VMEM((2, GROUP * rows, 128), BF),
            pltpu.VMEM((count, 1, blk), F32),
            pltpu.VMEM((blk, 128), F32),
        ],
    )


def stack_kernel(at_ref, *refs):
    ins, out_ref = refs[:GROUP], refs[GROUP]
    for s in range(GROUP):
        head = pl.ds(pl.multiple_of((at_ref[0] ^ s) * HD, HD), HD)
        out_ref[head, :] = ins[s][...]


def stack(at, heads):
    rows = heads[0].shape[1]
    return call(
        stack_kernel,
        "stack",
        at,
        (1,),
        [fixed((HD, rows))] * GROUP,
        fixed((GROUP * HD, rows)),
        like((GROUP * HD, rows), BF),
        heads,
    )


def unsplit_kernel(at_ref, *refs):
    ins, outs = refs[:4], refs[4:]
    cols = ins[0].shape[1]
    for r in range(4):
        lanes = pl.ds(pl.multiple_of(((at_ref[1] + r) % 4) * cols, cols), cols)
        for s in range(GROUP):
            head = pl.ds(pl.multiple_of((at_ref[0] ^ s) * HD, HD), HD)
            outs[s][:, lanes] = ins[r][head, :]


def unsplit(at, pieces):
    shape = (HD, 4 * pieces[0].shape[1])
    return call(
        unsplit_kernel,
        "unsplit",
        at,
        (1,),
        [fixed(pieces[0].shape)] * 4,
        [fixed(shape)] * GROUP,
        [like(shape, BF)] * GROUP,
        pieces,
    )


def heads_of(mine, r, features):
    return pl.ds(pl.multiple_of(((mine + 4 - r) % 4) * features, features), features)


def mid_kernel(at_ref, *refs):
    pieces, (w_ref, x_ref, gain_ref, bias_ref, h_ref, b_ref) = refs[:6], refs[6:]
    h = x_ref[...].astype(F32)
    for r, piece in enumerate(in_order(at_ref[1], *[ref[...] for ref in pieces])):
        rows = heads_of(at_ref[1], 4 - r, piece.shape[0])
        h = h + mm(turned(piece), w_ref[rows, :])

    @pl.when(pl.program_id(0) == 0)
    def _():
        h_ref[...] = h

    normal, _ = normalize(h)
    b_ref[...] = (normal * gain_ref[...] + bias_ref[...]).astype(BF)


def mid(at, pieces, w_o, tokens, gain, bias):
    features, rows = pieces[0].shape
    width, quarter = tokens.shape[1], rows // 4
    return call(
        mid_kernel,
        "mid",
        at,
        (4,),
        [pl.BlockSpec((features, quarter), lambda q, n: (0, (n[1] + q) % 4))] * 6
        + [fixed(w_o.shape)]
        + [pl.BlockSpec((quarter, width), lambda q, n: ((n[1] + q) % 4, 0))]
        + [fixed((1, width))] * 2,
        [fixed((quarter, width)), pl.BlockSpec((quarter, width), lambda q, n: (q, 0))],
        [like((quarter, width), F32), like((rows, width), BF)],
        (*pieces, w_o, tokens, gain, bias),
    )


def add_up(refs):
    total = refs[0][...]
    for ref in refs[1:]:
        total = total + ref[...].astype(F32)
    return total


def mid_back_kernel(at_ref, *refs):
    shares, (w_ref, h_ref, dy_ref, gain_ref, dh_ref, low_ref, sums_ref) = refs[:4], refs[4:11]
    do_refs = refs[11:]
    db = add_up(shares)
    normal, scale = normalize(h_ref[...])
    dh = dy_ref[...].astype(F32) + norm_back(db, gain_ref[...], normal, scale)
    dh_ref[...] = dh
    low = dh.astype(BF)
    low_ref[...] = low
    sums_ref[0:1, :] = jnp.sum(db * normal, axis=0, keepdims=True)
    sums_ref[1:2, :] = jnp.sum(db, axis=0, keepdims=True)
    for r in range(4):
        rows = heads_of(at_ref[1], r, do_refs[r].shape[0])
        do_refs[r][...] = mm_t(w_ref[rows, :], low).astype(BF)


def mid_back(at, shares, w_o, h, dy, gain):
    quarter, width = h.shape
    whole = fixed((quarter, width))
    piece = (w_o.shape[0] // 4, quarter)
    return call(
        mid_back_kernel,
        "mid_back",
        at,
        (1,),
        [whole] * 4 + [fixed(w_o.shape), whole, whole, fixed((1, width))],
        [whole] * 2 + [fixed((2, width))] + [fixed(piece)] * 4,
        [like((quarter, width), F32), like((quarter, width), BF), like((2, width), F32)]
        + [like(piece, BF)] * 4,
        (*shares, w_o, h, dy, gain),
    )


def cut_rows_kernel(at_ref, *refs):
    ins, outs = refs[:2], refs[2:]
    cols = outs[0].shape[2]
    for r in range(4):
        lanes = pl.ds(pl.multiple_of(((at_ref[1] + r) % 4) * cols, cols), cols)
        for k in range(2):
            outs[r][k] = ins[k][:, lanes]


def cut_rows(at, grads):
    features, rows = grads[0].shape
    shape = (2, features, rows // 4)
    return call(
        cut_rows_kernel,
        "cut_rows",
        at,
        (1,),
        [fixed((features, rows))] * 2,
        [fixed(shape)] * 4,
        [like(shape, BF)] * 4,
        grads,
    )


def first_back_kernel(at_ref, *refs):
    pieces, (w_ref, x_ref, dh_ref, gain_ref, out_ref, sum_s) = refs[:8], refs[8:]
    i = pl.program_id(0)
    total = 0.0
    for batch in range(2):
        piece = pieces[4 * batch][...]
        for r in range(1, 4):
            piece = jnp.where(i == r, pieces[4 * batch + r][...], piece)
        for k in range(2):
            total = total + mm(turned(piece[k]), w_ref[at_ref[0] ^ (2 * batch + k)])

    @pl.when(i == 0)
    def _():
        sum_s[...] = total

    @pl.when(i > 0)
    def _():
        sum_s[...] += total

    @pl.when(i == 3)
    def _():
        normal, scale = normalize(x_ref[...].astype(F32))
        grad = norm_back(sum_s[...], gain_ref[...], normal, scale)
        out_ref[...] = (dh_ref[...] + grad).astype(BF)


def first_back(at, near, far, w_heads, tokens, dh, gain):
    quarter, width = dh.shape
    shape = near[0].shape
    heads, features, _ = w_heads.shape
    own = lambda r, n: (n[1], 0)
    return call(
        first_back_kernel,
        "first_back",
        at,
        (4,),
        [fixed(shape)] * 8
        + [pl.BlockSpec((heads // 4, features, width), lambda r, n: ((n[1] + 4 - r) % 4, 0, 0))]
        + [pl.BlockSpec((quarter, width), own)]
        + [fixed((quarter, width)), fixed((1, width))],
        fixed((quarter, width)),
        like((quarter, width), BF),
        (*near, *far, w_heads, tokens, dh, gain),
        scratch=[pltpu.VMEM((quarter, width), F32)],
    )


def in_order(mine, own, right, left, far, right_two, left_two):
    one = jnp.where(mine == 3, far, left)
    two = jnp.where(mine < 2, left_two, right_two)
    three = jnp.where(mine == 0, far, right)
    return own, one, two, three


def one_hot(slots, dest):
    return jnp.where(slots == dest, 1.0, 0.0).astype(BF)


def dispatch_kernel(at_ref, dest_ref, rows_ref, out_ref, spread_s):
    blk, rows = min(256, spread_s.shape[0]), dest_ref.shape[1]

    @pl.when(pl.program_id(0) == 0)
    def _():
        slot = lax.broadcasted_iota(jnp.int32, (blk, rows), 0)
        for start in range(0, spread_s.shape[0], blk):
            spread_s[start : start + blk, :] = one_hot(slot + start, dest_ref[...])

    out_ref[...] = mm(spread_s[...], rows_ref[...]).astype(BF)


def columns(rows, width):
    return pl.BlockSpec((rows, width), lambda i, n: (0, i))


def dispatch(at, dest_row, values, slots):
    rows, width = values.shape
    blk = min(256, width)
    return call(
        dispatch_kernel,
        "dispatch",
        at,
        (width // blk,),
        [fixed((1, rows)), columns(rows, blk)],
        columns(slots, blk),
        like((slots, width), BF),
        (dest_row, values),
        scratch=[pltpu.VMEM((slots, rows), BF)],
    )


def join_kernel(at_ref, *refs):
    pieces, out_ref = refs[:6], refs[6]
    r = pl.program_id(0)
    for place, piece in enumerate(in_order(at_ref[1], *[ref[...] for ref in pieces])):

        @pl.when(r == place)
        def _():
            out_ref[...] = piece


def join(at, pieces):
    each, width = pieces[0].shape
    return call(
        join_kernel,
        "join",
        at,
        (4,),
        [fixed((each, width))] * 6,
        pl.BlockSpec((each, width), lambda r, n: ((n[1] + r) % 4, 0)),
        like((4 * each, width), BF),
        pieces,
    )


def write_shares(mine, total, own_ref, one_ref, two_ref, three_ref, end_ref):
    rows = own_ref.shape[0]
    own_ref[...] = total[:rows]
    one, two, three = [total[r * rows : (r + 1) * rows].astype(BF) for r in (1, 2, 3)]
    one_ref[...] = one
    two_ref[...] = two
    three_ref[...] = three
    end_ref[...] = jnp.where(mine == 0, three, one)


def share_shapes(rows, width):
    return [like((rows, width), F32)] + [like((rows, width), BF)] * 4


def combine_kernel(count, whole, at_ref, *refs):
    dests, backs = refs[:count], refs[count : 2 * count]
    base_ref, refs, pick_s = refs[2 * count], refs[2 * count + 1 : -1], refs[-1]
    rows, slots = base_ref.shape[0], backs[0].shape[0]
    blk = rows // 4

    @pl.when(pl.program_id(0) == 0)
    def _():
        lane = lax.broadcasted_iota(jnp.int32, (blk, slots), 1)
        for k in range(count):
            for start in range(0, rows, blk):
                dest = dests[k][start : start + blk, :]
                pick_s[start : start + blk, k * slots : (k + 1) * slots] = one_hot(lane, dest)

    total = base_ref[...].astype(F32)
    for k in range(count):
        total = total + mm(pick_s[:, k * slots : (k + 1) * slots], backs[k][...])
    mine = at_ref[1]
    if whole:
        h_ref, out_ref = refs
        for r in range(4):
            part = total[r * blk : (r + 1) * blk]
            if r == 0:
                part = part + h_ref[...]
            place = pl.ds(pl.multiple_of(((mine + r) % 4) * blk, blk), blk)
            out_ref[place, :] = part.astype(BF)
    else:
        write_shares(mine, total, *refs)


def combine(at, dests, backs, base, h=None):
    count, (slots, width), rows = len(backs), backs[0].shape, base.shape[0]
    blk = min(256, width)
    whole = h is not None
    quarter = columns(rows // 4, blk)
    return call(
        partial(combine_kernel, count, whole),
        "combine",
        at,
        (width // blk,),
        [fixed((rows, 1))] * count
        + [columns(slots, blk)] * count
        + [columns(rows, blk)]
        + [quarter] * whole,
        columns(rows, blk) if whole else [quarter] * 5,
        like(base.shape, BF) if whole else share_shapes(rows // 4, width),
        (*dests, *backs, base) + ((h,) if whole else ()),
        scratch=[pltpu.VMEM((rows, count * slots), BF)],
    )


def mm_t(a, b):
    return lax.dot_general(a, b, (((1,), (1,)), ((), ())), preferred_element_type=F32)


def gelu_both(u):
    c = 0.7978845608028654
    square = u * u
    t = jnp.tanh(u * (c + (c * 0.044715) * square))
    half = 0.5 + 0.5 * t
    slope = half + (0.5 * u) * (1.0 - t * t) * (c + (3.0 * c * 0.044715) * square)
    return u * half, slope


def high_low(value):
    high = value.astype(BF)
    return high, (value - high.astype(F32)).astype(BF)


def two_coefs(logits, lane, experts):
    inside = (lane >= experts) & (lane < experts + 2)
    top = jnp.max(jnp.where(inside, logits, HIDE), axis=1, keepdims=True)
    e = jnp.where(inside, jnp.exp(logits - top), 0.0)
    e = e / jnp.sum(e, axis=1, keepdims=True)
    first = jnp.sum(jnp.where(lane == experts, e, 0.0), axis=1, keepdims=True)
    second = jnp.sum(jnp.where(lane == experts + 1, e, 0.0), axis=1, keepdims=True)
    return first, second


def small_back(d_small, rows, w_small_ref, small_ref, i):
    high, low = high_low(d_small)
    w_small = w_small_ref[...]
    high_t, low_t = high_low(d_small.T)

    @pl.when(i == 0)
    def _():
        small_ref[...] = jnp.zeros(small_ref.shape, F32)

    small_ref[...] += mm(high_t, rows) + mm(low_t, rows)
    return mm_t(high, w_small) + mm_t(low, w_small)


def expert_kernel(experts, half, at_ref, rows_ref, dy_ref, up_ref, down_ref, w_small_ref, *outs):
    if half:
        outs = outs[5:]
    rows_out_ref, hid_ref, dy_out_ref, deu_ref, y_ref, d_rows_ref, small_ref = outs
    rows = rows_ref[...]
    rows_out_ref[...] = rows
    up = mm(rows, up_ref[...])
    logits = mm(rows, w_small_ref[...])
    lane = lax.broadcasted_iota(jnp.int32, logits.shape, 1)
    routed = lane < experts
    top = jnp.max(jnp.where(routed, logits, HIDE), axis=1, keepdims=True)
    probs = jnp.where(routed, jnp.exp(logits - top), 0.0)
    probs = probs / jnp.sum(probs, axis=1, keepdims=True)
    own = jnp.where(lane == at_ref[2], 1.0, 0.0)
    gate = jnp.sum(probs * own, axis=1, keepdims=True)
    first, second = two_coefs(logits, lane, experts)
    weight = second * gate
    dy = dy_ref[...].reshape(rows.shape).astype(F32)
    d_y = (weight * dy).astype(BF)
    dy_out_ref[...] = d_y
    d_hidden = mm_t(d_y, down_ref[...])
    hidden, slope = gelu_both(up)
    hidden = hidden.astype(BF)
    hid_ref[...] = hidden
    d_up = (d_hidden * slope).astype(BF)
    deu_ref[...] = d_up
    y = mm(hidden, down_ref[...])
    y_ref[...] = (weight * y).astype(BF).reshape(y_ref.shape)
    along = gate * jnp.sum(dy * y, axis=1, keepdims=True)
    mixed = first * second * along
    d_small = (second * along) * (own - probs)
    d_small = jnp.where(routed, d_small, 0.0)
    d_small = d_small + jnp.where(lane == experts + 1, mixed, 0.0)
    d_small = d_small - jnp.where(lane == experts, mixed, 0.0)
    d_rows = mm_t(d_up, up_ref[...]) + small_back(d_small, rows, w_small_ref, small_ref, pl.program_id(0))
    d_rows_ref[...] = d_rows.astype(BF)


def expert_rows(at, rows, dy, w_up, w_down, w_small, experts, half, before):
    count, width = rows.shape
    hid, lanes = w_up.shape[1], w_small.shape[1]
    blk = min(512, count)
    capacity = count // dy.shape[0]
    steps = count // blk
    moving = pl.BlockSpec((blk, width), lambda i, n: (i, 0))
    slots = pl.BlockSpec((blk // capacity, capacity, width), lambda i, n: (i, half, 0))
    kept = [pl.BlockSpec((blk, size), lambda i, n: (i + half * steps, 0)) for size in (width, hid, width, hid)]
    return call(
        partial(expert_kernel, experts, half),
        "expert_rows",
        at,
        (steps,),
        [
            moving,
            slots,
            fixed((width, hid)),
            fixed((hid, width)),
            fixed((width, lanes)),
        ]
        + [pl.BlockSpec(memory_space=pl.ANY)] * (5 * half),
        kept + [slots, moving, fixed((lanes, width))],
        [like((2 * count, size), BF) for size in (width, hid, width, hid)]
        + [like(dy.shape, BF), like((count, width), BF)]
        + [like((lanes, width), F32)],
        (rows, dy, w_up, w_down, w_small, *before),
        alias={6 + k: k for k in range(5)} if half else None,
        vmem=56,
    )


def dense_kernel(experts, at_ref, rows_ref, dy_ref, in_ref, out_ref, w_small_ref, *outs):
    hid_ref, grad_ref, d_up_ref, mix_ref, db_ref, small_ref = outs
    rows = rows_ref[...]
    up = mm(rows, in_ref[...])
    logits = mm(rows, w_small_ref[...])
    lane = lax.broadcasted_iota(jnp.int32, logits.shape, 1)
    first, second = two_coefs(logits, lane, experts)
    dy = dy_ref[...].astype(F32)
    grad = (first * dy).astype(BF)
    grad_ref[...] = grad
    d_hidden = mm_t(grad, out_ref[...])
    hidden, slope = gelu_both(up)
    hidden = hidden.astype(BF)
    hid_ref[...] = hidden
    d_up = (d_hidden * slope).astype(BF)
    d_up_ref[...] = d_up
    dense = mm(hidden, out_ref[...])
    mix_ref[...] = first * dense
    mixed = first * second * jnp.sum(dy * dense, axis=1, keepdims=True)
    d_small = jnp.where(lane == experts, mixed, 0.0) - jnp.where(lane == experts + 1, mixed, 0.0)
    db_ref[...] = mm_t(d_up, in_ref[...]) + small_back(d_small, rows, w_small_ref, small_ref, pl.program_id(0))


def dense_rows(at, rows, dy, w_in, w_out, w_small, experts):
    (count, width), hid, lanes = rows.shape, w_in.shape[1], w_small.shape[1]
    blk = min(512, count)
    row_out = pl.BlockSpec((blk, width), lambda i, n: (i, 0))
    hid_out = pl.BlockSpec((blk, hid), lambda i, n: (i, 0))
    return call(
        partial(dense_kernel, experts),
        "dense_rows",
        at,
        (count // blk,),
        [row_out, row_out, fixed((width, hid)), fixed((hid, width)), fixed((width, lanes))],
        [hid_out, row_out, hid_out, row_out, row_out, fixed((lanes, width))],
        [
            like((count, hid), BF),
            like((count, width), BF),
            like((count, hid), BF),
            like((count, width), F32),
            like((count, width), F32),
            like((lanes, width), F32),
        ],
        (rows, dy, w_in, w_out, w_small),
        vmem=56,
    )


def turned(value):
    return value.astype(F32).T.astype(BF)


def dense_grads_kernel(at_ref, b_ref, d_up_ref, grad_ref, hid_ref, keep_ref, give_ref):
    width = d_up_ref.shape[1]
    first = mm(turned(b_ref[...]), d_up_ref[...]).astype(BF)
    second = mm(turned(grad_ref[...]), hid_ref[...]).astype(BF)
    half = pl.num_programs(0) // 2
    for side, ref in ((0, keep_ref), (1, give_ref)):

        @pl.when(pl.program_id(0) // half == side)
        def _():
            ref[0, :, :width] = first
            ref[0, :, width:] = second


def dense_grads(at, b, d_up, grad, hidden, parts):
    (rows, width), hid = b.shape, hidden.shape[1]
    own, half, bits = width // parts, parts // 2, parts.bit_length() - 1

    def part(q, n):
        turned_q = sum([((q // 2**k) % 2) * 2 ** (bits - 1 - k) for k in range(bits)])
        return turned_q ^ n[2]

    column = pl.BlockSpec((rows, own), lambda q, n: (0, part(q, n)))
    shape = (1, own, 2 * hid)
    return call(
        dense_grads_kernel,
        "dense_grads",
        at,
        (parts,),
        [column, fixed((rows, hid)), column, fixed((rows, hid))],
        [
            pl.BlockSpec(shape, lambda q, n: (jnp.minimum(q, half - 1), 0, 0)),
            pl.BlockSpec(shape, lambda q, n: (jnp.maximum(q - half, 0), 0, 0)),
        ],
        [like((half, own, 2 * hid), BF)] * 2,
        (b, d_up, grad, hidden),
    )


def attention_grads_kernel(experts, at_ref, *refs):
    grads, o_refs, refs = refs[:GROUP], refs[GROUP : GROUP + 6], refs[GROUP + 6 :]
    a_ref, dh_ref, w_ref, gain_ref, bias_ref, sums_ref = refs[:6]
    small_refs, (out_ref, all_s) = refs[6:-2], refs[-2:]
    heads, features = GROUP * HD, grads[1].shape[0]
    products, plain = 0.0, 0.0
    for k in range(GROUP):
        head = at_ref[0] ^ k
        rows = pl.ds(pl.multiple_of(head * features, features), features)
        grad = grads[k][...]
        weight = w_ref[head].astype(F32)
        total = mm(grad, a_ref[...])
        all_s[rows, :] = total
        each = jnp.sum(grad.astype(F32), axis=1, keepdims=True)
        products = products + jnp.sum(total * weight, axis=0, keepdims=True)
        plain = plain + jnp.sum(each * weight, axis=0, keepdims=True)
    first = GROUP * features
    for r, piece in enumerate(in_order(at_ref[1], *[ref[...] for ref in o_refs])):
        rows = pl.ds(pl.multiple_of(first + ((at_ref[1] + r) % 4) * heads, heads), heads)
        all_s[rows, :] = mm(piece, dh_ref[...])
    first += 4 * heads
    small = add_up(small_refs)
    row = lax.broadcasted_iota(jnp.int32, small.shape, 0)
    d_gain = (products - bias_ref[...] * plain) / gain_ref[...]
    for k, sums in enumerate((sums_ref[0:1, :], sums_ref[1:2, :], d_gain, plain)):
        small = jnp.where(row == experts + 2 + k, sums, small)
    all_s[first:, :] = small
    out_ref[...] = all_s[...].T.astype(BF)


def attention_grads(at, grads, o, a, dh, w_heads, gain, bias, sums, small, experts):
    rows, width = a.shape
    features, lanes = grads[0].shape[0], small[0].shape[0]
    piece = pl.BlockSpec((o[0].shape[0], dh.shape[0]), lambda i, n: (0, n[1]))
    height = GROUP * features + 4 * o[0].shape[0] + lanes
    blk = min(256, width)
    return call(
        partial(attention_grads_kernel, experts),
        "attention_grads",
        at,
        (width // blk,),
        [fixed((features, rows))] * GROUP
        + [piece] * 6
        + [columns(rows, blk), columns(dh.shape[0], blk)]
        + [pl.BlockSpec((GROUP, features, blk), lambda i, n: (0, 0, i))]
        + [columns(1, blk)] * 2
        + [columns(2, blk)]
        + [columns(lanes, blk)] * len(small),
        pl.BlockSpec((blk, height), lambda i, n: (i, 0)),
        like((width, height), BF),
        (*grads, *o, a, dh, w_heads, gain, bias, sums, *small),
        scratch=[pltpu.VMEM((height, blk), F32)],
    )


def hop(value, *pairs):
    return lax.ppermute(value, "mp", pairs)


def rotate(value, steps):
    return hop(value, *[(s, (s + steps) % 4) for s in range(4)])


def gather_near(own):
    right = hop(own, (0, 1), (1, 2), (2, 3))
    left = hop(own, (1, 0), (2, 1), (3, 2))
    return own, right, left, hop(own, (0, 3), (3, 0))


def gather_far(near):
    _, right, left, _ = near
    return *near, hop(right, (1, 2), (2, 3)), hop(left, (1, 0), (2, 1))


def gather_pieces(own):
    return gather_far(gather_near(own))


def scatter_far(shares):
    _, _, two, _, end = shares
    return hop(two, (2, 1), (3, 2)), hop(two, (0, 1), (1, 2)), hop(end, (0, 3), (3, 0))


def scatter_near(shares, came):
    own, one, _, three, _ = shares
    from_right, from_left, from_end = came
    three = (three.astype(F32) + from_right.astype(F32)).astype(BF)
    one = (one.astype(F32) + from_left.astype(F32)).astype(BF)
    return own, hop(three, (1, 0), (2, 1), (3, 2)), hop(one, (0, 1), (1, 2), (2, 3)), from_end


def group_swap(value, s):
    count = lax.axis_size("dp")
    return lax.ppermute(value, "dp", [(t, t ^ s) for t in range(count)])


def expert_swap(value, experts):
    wide = value.reshape(experts, value.shape[0] // experts, value.shape[1])
    return lax.all_to_all(wide, "dp", 0, 0, tiled=True).reshape(value.shape)


def roll_rows(value, start):
    twice = jnp.concatenate([value, value], axis=0)
    return lax.dynamic_slice_in_dim(twice, start, value.shape[0], 0)


def add_halves(keep, came):
    return (keep.astype(F32) + came.astype(F32)).astype(BF)


def body(
    tokens,
    cotangent,
    ln_gains,
    ln_biases,
    w_qkv,
    w_o,
    w_in,
    w_out,
    w_router,
    w_coef,
    w_up,
    w_down,
    routes,
    long_group,
):
    rows, width = tokens.shape
    dps = lax.axis_size("dp")
    mine, position = lax.axis_index("mp"), lax.axis_index("dp")
    quarter = rows // 4
    start = mine * quarter
    heads_loc = w_qkv.shape[2] // HD
    hid = w_in.shape[1]
    experts = w_router.shape[1]
    capacity = max(2, 2 * rows // experts)
    half = capacity // 2
    barrier = lax.optimization_barrier
    first_len = lax.dynamic_index_in_dim(long_group, position // GROUP, 0, keepdims=False)
    at = jnp.stack([position % GROUP, mine, position, first_len]).astype(jnp.int32)
    gains = [ln_gains[0:1], ln_gains[1:2]]
    biases = [ln_biases[0:1], ln_biases[1:2]]
    w_o_all = lax.all_gather(w_o, "mp", axis=0, tiled=True)

    w_heads = w_qkv.reshape(width, 3, heads_loc, HD).transpose(2, 1, 3, 0)
    w_heads = w_heads.reshape(heads_loc, 3 * HD, width)
    a_r, *qkv = project(at, tokens, gains[0], biases[0], w_heads)
    qkv = [qkv[0]] + [group_swap(qkv[s], s) for s in (1, 2, 3)]

    route = roll_rows(routes, start)[:, 0]
    picked = (route[:, None] == jnp.arange(experts, dtype=jnp.int32)[None, :]).astype(jnp.int32)
    slot = jnp.sum((jnp.cumsum(picked, axis=0) - picked) * picked, axis=1)
    dy_b = roll_rows(cotangent, start)
    send_dy = dispatch(at, (route * capacity + slot)[None, :], dy_b, experts * capacity)
    *qkv, send_dy = barrier((*qkv, send_dy))
    in_half = [slot < half, slot >= half]
    dests = [
        jnp.where(in_half[k], route * half + slot - k * half, -1).astype(jnp.int32) for k in (0, 1)
    ]

    *o_t, lse = attend(at, qkv)
    *o_t, w_o_all = barrier((*o_t, w_o_all))
    o_heads = [o_t[0]] + [group_swap(o_t[s], s) for s in (1, 2, 3)]
    lanes = -(-(experts + 2) // 128) * 128
    w_small = jnp.concatenate(
        [w_router, w_coef, jnp.zeros((width, lanes - experts - 2), BF)], axis=1
    )
    *o_heads, send_dy, w_small = barrier((*o_heads, send_dy, w_small))
    got_dy = expert_swap(send_dy, experts).reshape(experts, capacity, width)
    o_pieces = gather_pieces(stack(at, o_heads))
    h, b_r = mid(at, o_pieces, w_o_all, tokens, gains[1], biases[1])

    b_r, w_heads = barrier((b_r, w_heads))
    w_heads_all = lax.all_gather(w_heads, "mp", axis=0, tiled=True)
    send_0 = dispatch(at, dests[0][None, :], b_r, experts * half)
    send_0, got_dy = barrier((send_0, got_dy))
    got_0 = expert_swap(send_0, experts)
    send_1 = dispatch(at, dests[1][None, :], b_r, experts * half)
    b_r, send_1 = barrier((b_r, send_1))
    hidden, dense_grad, d_up, mix_base, db_base, small_t = dense_rows(
        at, b_r, dy_b, w_in, w_out, w_small, experts
    )
    send_1, got_0, db_base = barrier((send_1, got_0, db_base))
    got_1 = expert_swap(send_1, experts)

    *kept, d_rows_0, small_0 = expert_rows(
        at, got_0, got_dy, w_up[0], w_down[0], w_small, experts, 0, ()
    )
    back_0 = expert_swap(d_rows_0, experts)
    *kept, d_rows_1, small_1 = expert_rows(
        at, got_1, got_dy, w_up[0], w_down[0], w_small, experts, 1, kept
    )
    got, hidden_e, d_y, d_eu, back_y = kept
    back_1 = expert_swap(d_rows_1, experts)
    back_1, w_heads_all = barrier((back_1, w_heads_all))
    d_rows_1, b_r = barrier((d_rows_1, b_r))
    halving = width == dps * 128
    if halving:
        grads = dense_grads(at, b_r, d_up, dense_grad, hidden, dps)
    else:
        grads = [ein("td,tf->df", b_r, d_up).astype(BF), ein("td,tf->df", dense_grad, hidden).astype(BF)]
    back_0, back_1, back_y, *grads = barrier((back_0, back_1, back_y, *grads))

    dest_cols = [dest[:, None] for dest in dests]
    tok_y = expert_swap(back_y.reshape(experts * capacity, width), experts)
    shares = combine(at, dest_cols, [back_0, back_1], db_base)
    far = scatter_far(shares)
    *far, g_0, g_1 = barrier((*far, *grads))
    grads = [g_0, g_1]
    shares = scatter_near(shares, far)

    mix = combine(at, [(route * capacity + slot)[:, None]], [tok_y], mix_base, h)
    *shares, mix = barrier((*shares, mix))
    output = lax.psum(mix, "mp")
    dh, dh_r, sums_2, *do_q = mid_back(at, shares, w_o_all, h, dy_b[:quarter], gains[1])
    do_q = [do_q[0]] + [rotate(do_q[r], -r) for r in (1, 2, 3)]
    do_heads = unsplit(at, do_q)
    do_t = [do_heads[0]] + [group_swap(do_heads[s], s) for s in (1, 2, 3)]
    if halving:
        came_1 = group_swap(grads[1], 1)
        half = dps // 4
        give = add_halves(grads[0][half:], came_1[half:])
        *do_t, give = barrier((*do_t, give))
        came_2 = group_swap(give, 2)
    d_qkv = attend_back(at, qkv, do_t, o_t, lse)
    if halving:
        keep = add_halves(grads[0][:half], came_1[:half])
        *d_qkv, came_2, keep = barrier((*d_qkv, came_2, keep))
        grads = add_halves(keep, came_2)
        bit = 4
        while bit < dps:
            half = grads.shape[0] // 2
            grads = add_halves(grads[:half], group_swap(grads[half:], bit))
            bit *= 2
        grads = [grads[0][:, :hid], grads[0][:, hid:]]
    else:
        grads = [lax.psum_scatter(grad, "dp", scatter_dimension=0, tiled=True) for grad in grads]

    d_own, got, hidden_e, d_y, d_eu = barrier((d_qkv[0], got, hidden_e, d_y, d_eu))
    d_qkv = [d_own] + [group_swap(d_qkv[s], s) for s in (1, 2, 3)]
    near = cut_rows(at, d_qkv[:2])
    near = [near[0]] + [rotate(near[r], r) for r in (1, 2, 3)]
    far = cut_rows(at, d_qkv[2:])
    grad_down = ein("rf,rd->fd", hidden_e, d_y)
    tied = barrier((*near, *far, *d_qkv, grad_down))
    near, far, d_qkv, grad_down = tied[:4], tied[4:8], tied[8:12], tied[12]
    far = [far[0]] + [rotate(far[r], r) for r in (1, 2, 3)]
    grads_a = attention_grads(
        at, d_qkv, o_pieces, a_r, dh_r, w_heads, gains[0], biases[0], sums_2, (small_0, small_1, small_t), experts
    )
    grads_a, output = barrier((grads_a, output))
    grads_a = lax.psum_scatter(grads_a, "dp", scatter_dimension=0, tiled=True).T
    grad_up = ein("rd,rf->df", got, d_eu)
    *far, grad_up = barrier((*far, grad_up))
    grad_q = first_back(at, near, far, w_heads_all, tokens, dh, gains[0])
    grad_tokens = join(at, gather_pieces(grad_q))

    own, heads = width // dps, heads_loc * HD
    grad_qkv = grads_a[: 3 * heads].astype(F32).reshape(heads_loc, 3, HD, own).transpose(3, 1, 0, 2)
    grad_qkv = grad_qkv.reshape(own, 3, heads)
    grad_in = grads[0].astype(F32)
    grad_out = grads[1].astype(F32).T
    rest = grads_a[3 * heads : 7 * heads].reshape(4, heads, own)
    small = jnp.broadcast_to(grads_a[7 * heads :], (4, lanes, own))
    rest = lax.all_to_all(jnp.concatenate([rest, small], axis=1), "mp", 0, 0, tiled=True)
    rest = jnp.sum(rest.astype(F32), axis=0)
    grad_o, small = rest[:heads], rest[heads:]
    small_out = small[: experts + 2].T
    return (
        output,
        grad_tokens,
        jnp.stack([small[experts + 4], small[experts + 2]]),
        jnp.stack([small[experts + 5], small[experts + 3]]),
        grad_qkv,
        grad_o,
        grad_in,
        grad_out,
        small_out[:, :experts],
        small_out[:, experts:],
        grad_up[None],
        grad_down[None],
    )


def solution(mesh):
    in_specs = (
        P("dp", None),
        P("dp", None),
        P(),
        P(),
        P(None, None, "mp"),
        P("mp", None),
        P(None, "mp"),
        P("mp", None),
        P(),
        P(),
        P("dp", None, "mp"),
        P("dp", "mp", None),
        P("dp", None),
        P(),
    )
    out_specs = (
        P("dp", None),
        P("dp", None),
        P(None, "dp"),
        P(None, "dp"),
        P("dp", None, "mp"),
        P("mp", "dp"),
        P("dp", "mp"),
        P("mp", "dp"),
        P("dp", None),
        P("dp", None),
        P("dp", None, "mp"),
        P("dp", "mp", None),
    )
    return jax.shard_map(body, mesh=mesh, in_specs=in_specs, out_specs=out_specs, check_vma=False)
```

```python
from functools import partial

import jax
import jax.numpy as jnp
from jax import lax
from jax.experimental import pallas as pl
from jax.experimental.pallas import tpu as pltpu
from jax.sharding import PartitionSpec as P

HD = 64
GROUP = 4
EPS = 1e-05
LOG2E = 1.4426950408889634
SCALE2 = 0.125 * LOG2E
HIDE = -1e30
BF = jnp.bfloat16
F32 = jnp.float32
LIGHT = pl.CostEstimate(flops=1 << 20, bytes_accessed=1 << 20, transcendentals=0)


def mm(a, b):
    return jnp.dot(a, b, preferred_element_type=F32)


def ein(spec, a, b):
    return jnp.einsum(spec, a, b, preferred_element_type=F32)


def call(kernel, name, prefetch, grid, in_specs, out_specs, out_shape, args, scratch=(), alias=None, vmem=48):
    return pl.pallas_call(
        kernel,
        grid_spec=pltpu.PrefetchScalarGridSpec(
            num_scalar_prefetch=1,
            grid=grid,
            in_specs=in_specs,
            out_specs=out_specs,
            scratch_shapes=list(scratch),
        ),
        out_shape=out_shape,
        input_output_aliases=alias or {},
        compiler_params=pltpu.CompilerParams(vmem_limit_bytes=vmem * 2**20),
        cost_estimate=LIGHT,
        name=name,
    )(prefetch, *args)


def fixed(shape):
    zeros = (0,) * len(shape)
    return pl.BlockSpec(shape, lambda *_: zeros)


def like(shape, dtype):
    return jax.ShapeDtypeStruct(shape, dtype)


def normalize(v):
    mean = jnp.mean(v, axis=-1, keepdims=True)
    centred = v - mean
    scale = lax.rsqrt(jnp.mean(centred * centred, axis=-1, keepdims=True) + EPS)
    return centred * scale, scale


def norm_back(grad, gain, normal, scale):
    g = grad * gain
    along = jnp.mean(g * normal, axis=-1, keepdims=True)
    return scale * (g - jnp.mean(g, axis=-1, keepdims=True) - normal * along)


def qkv_kernel(at_ref, x_ref, gain_ref, bias_ref, w_ref, a_ref, *outs):
    normal, _ = normalize(x_ref[...].astype(F32))
    a = (normal * gain_ref[...] + bias_ref[...]).astype(BF)
    a_ref[...] = a
    for s in range(GROUP):
        outs[s][...] = mm_t(w_ref[at_ref[0] ^ s], a).astype(BF)


def project(at, tokens, gain, bias, w_heads):
    rows, width = tokens.shape
    features = w_heads.shape[1]
    blk = min(256, rows)
    moving = pl.BlockSpec((blk, width), lambda i, n: (i, 0))
    return call(
        qkv_kernel,
        "project",
        at,
        (rows // blk,),
        [moving, fixed((1, width)), fixed((1, width)), fixed(w_heads.shape)],
        [moving] + [pl.BlockSpec((features, blk), lambda i, n: (0, i))] * GROUP,
        [like((rows, width), BF)] + [like((features, rows), BF)] * GROUP,
        (tokens, gain, bias, w_heads),
    )


def fill_keys(k_s, place, keys, first_len, blk):
    rows = place * blk + lax.broadcasted_iota(jnp.int32, (blk, 128), 0)
    lane = lax.broadcasted_iota(jnp.int32, (blk, 128), 1)
    wide = jnp.concatenate([keys.astype(F32).T, jnp.zeros((blk, 128 - HD), F32)], axis=1)
    wide = jnp.where((lane == HD) & (rows < first_len), HIDE, wide)
    k_s[pl.ds(place * blk, blk), :] = wide.astype(BF)


def wide_query(query, place, first_len, blk):
    cols = place * blk + lax.broadcasted_iota(jnp.int32, (128 - HD, blk), 1)
    sub = lax.broadcasted_iota(jnp.int32, (128 - HD, blk), 0)
    extra = jnp.where((sub == 0) & (cols >= first_len), 1.0, 0.0)
    return jnp.concatenate([query, extra.astype(BF)], axis=0)


def causal(blk):
    keys = lax.broadcasted_iota(jnp.int32, (blk, blk), 0)
    queries = lax.broadcasted_iota(jnp.int32, (blk, blk), 1)
    return keys <= queries


def attend_kernel(blk, per, at_ref, *refs):
    qkv_refs, o_refs = refs[:GROUP], refs[GROUP : 2 * GROUP]
    lse_ref, k_s, qkv_s = refs[2 * GROUP :]
    i = pl.program_id(0)
    place, first_len = at_ref[0], at_ref[3]

    @pl.when(i == 0)
    def _():
        for s in range(GROUP):
            qkv_s[place ^ s] = qkv_refs[s][...]

    def part(which, j):
        return qkv_s[j // per, HD * which : HD * (which + 1), pl.ds((j % per) * blk, blk)]

    fill_keys(k_s, i, part(1, i), first_len, blk)
    query = wide_query(part(0, i), i, first_len, blk)

    def scores(j):
        return mm(k_s[pl.ds(pl.multiple_of(j * blk, blk), blk), :], query)

    s = jnp.where(causal(blk), scores(i), HIDE)
    top = jnp.max(s, axis=0, keepdims=True)
    p = jnp.exp2((s - top) * SCALE2)
    total = jnp.sum(p, axis=0, keepdims=True)
    acc = mm(part(2, i), p.astype(BF))

    def steps(blocks, carry):
        top, total, acc = carry
        s = [scores(j) for j in blocks]
        new = top
        for one in s:
            new = jnp.maximum(new, jnp.max(one, axis=0, keepdims=True))
        keep = jnp.exp2((top - new) * SCALE2)
        total, acc = total * keep, acc * keep
        for j, one in zip(blocks, s):
            p = jnp.exp2((one - new) * SCALE2)
            total = total + jnp.sum(p, axis=0, keepdims=True)
            acc = acc + mm(part(2, j), p.astype(BF))
        return new, total, acc

    low = jnp.where(i * blk >= first_len, first_len // blk, 0)
    pairs = (i - low) // 2
    carry = lax.fori_loop(
        0, pairs, lambda t, c: steps([low + 2 * t, low + 2 * t + 1], c), (top, total, acc)
    )
    top, total, acc = lax.fori_loop(low + 2 * pairs, i, lambda j, c: steps([j], c), carry)
    out = (acc / total).astype(BF)
    for s in range(GROUP):

        @pl.when((i // per) ^ place == s)
        def _():
            o_refs[s][:, pl.ds((i % per) * blk, blk)] = out

    lse_ref[0] = top * SCALE2 + jnp.log2(total)


def attend(at, qkv):
    features, rows = qkv[0].shape
    blk = min(512, rows)
    per = rows // blk
    count = GROUP * per
    return call(
        partial(attend_kernel, blk, per),
        "attend",
        at,
        (count,),
        [fixed((features, rows))] * GROUP,
        [fixed((HD, rows))] * GROUP + [pl.BlockSpec((1, 1, blk), lambda i, n: (i, 0, 0))],
        [like((HD, rows), BF)] * GROUP + [like((count, 1, blk), F32)],
        qkv,
        scratch=[pltpu.VMEM((GROUP * rows, 128), BF), pltpu.VMEM((GROUP, features, rows), BF)],
    )


def back_kernel(blk, per, first, count, at_ref, *refs):
    qkv_refs, do_refs, o_refs = refs[:GROUP], refs[GROUP : 2 * GROUP], refs[2 * GROUP : 3 * GROUP]
    lse_ref, refs = refs[3 * GROUP], refs[3 * GROUP + 1 :]
    if first:
        held_refs, dq_in_ref, refs = refs[:GROUP], refs[GROUP], refs[GROUP + 1 :]
    out_refs, refs = refs[:GROUP], refs[GROUP:]
    dq_ref, out_ref, k_s, kt_s, v_s, wide_s, dot_s, both_s, delta_s, acc_s = refs
    j = first + pl.program_id(0)
    place, first_len = at_ref[0], at_ref[3]

    def prepare(s, zero):
        for sub in range(per):
            i = (place ^ s) * per + sub
            at = pl.ds(pl.multiple_of(i * blk, blk), blk)
            cut = slice(sub * blk, (sub + 1) * blk)
            query = qkv_refs[s][0:HD, cut]
            keys = qkv_refs[s][HD : 2 * HD, cut]
            grad = do_refs[s][:, cut]
            fill_keys(k_s, i, keys, first_len, blk)
            kt_s[:, at] = keys
            dot_s[:, at] = grad
            wide_s[:, at] = wide_query(query, i, first_len, blk)
            grad = grad.astype(F32)
            values = qkv_refs[s][2 * HD :, cut].astype(F32)
            v_s[at, :] = jnp.concatenate([values.T, zero], axis=1).astype(BF)
            both_s[0, at, :] = jnp.concatenate([grad.T, zero], axis=1).astype(BF)
            both_s[1, at, :] = jnp.concatenate([zero, query.astype(F32).T], axis=1).astype(BF)
            held = o_refs[s][:, cut].astype(F32)
            delta_s[i] = jnp.sum(held * grad, axis=0, keepdims=True)

    @pl.when(j == first)
    def _():
        dq_ref[...] = dq_in_ref[...] if first else jnp.zeros(dq_ref.shape, F32)
        zero = jnp.zeros((blk, HD), F32)
        for s in range(GROUP):
            if first:

                @pl.when((place ^ s) * per < first)
                def _():
                    out_refs[s][...] = held_refs[s][...]

            @pl.when((place ^ s) * per >= first)
            def _():
                prepare(s, zero)

    here = pl.ds(pl.multiple_of(j * blk, blk), blk)
    keys_t = kt_s[:, here]
    values = v_s[here, 0:HD]

    def pair(i, diagonal):
        at = pl.ds(pl.multiple_of(i * blk, blk), blk)
        s = mm(k_s[here, :], wide_s[:, at])
        p = jnp.exp2(s * SCALE2 - lse_ref[i])
        if diagonal:
            p = jnp.where(causal(blk), p, 0.0)
        dp = mm(values, dot_s[:, at])
        ds = (p * (dp - delta_s[i])).astype(BF)
        return mm(p.astype(BF), both_s[0, at, :]) + mm(ds, both_s[1, at, :]), mm(keys_t, ds)

    acc_s[...], dq = pair(j, True)
    dq_ref[:, here] += dq

    def step_two(t, carry):
        i = j + 1 + 2 * t
        (kv_0, dq_0), (kv_1, dq_1) = pair(i, False), pair(i + 1, False)
        acc_s[...] += kv_0 + kv_1
        at = pl.ds(pl.multiple_of(i * blk, blk), 2 * blk)
        dq_ref[:, at] += jnp.concatenate([dq_0, dq_1], axis=1)
        return carry

    def step(i, carry):
        kv, dq = pair(i, False)
        acc_s[...] += kv
        dq_ref[:, pl.ds(pl.multiple_of(i * blk, blk), blk)] += dq
        return carry

    high = jnp.where((j + 1) * blk <= first_len, (first_len + blk - 1) // blk, count)
    pairs = (high - j - 1) // 2
    lax.fori_loop(0, pairs, step_two, 0)
    lax.fori_loop(j + 1 + 2 * pairs, high, step, 0)
    both = acc_s[...].T
    out_ref[0:HD, :] = (dq_ref[:, here] * 0.125).astype(BF)
    out_ref[HD : 2 * HD, :] = (both[HD:, :] * 0.125).astype(BF)
    out_ref[2 * HD :, :] = both[:HD, :].astype(BF)
    for s in range(GROUP):

        @pl.when((j // per) ^ place == s)
        def _():
            out_refs[s][:, pl.ds(pl.multiple_of((j % per) * blk, blk), blk)] = out_ref[...]


def attend_back(at, qkv, do, o, lse, before, first, last):
    features, rows = qkv[0].shape
    blk = min(512, rows)
    per = rows // blk
    count = GROUP * per
    whole, dq = fixed((features, rows)), (HD, GROUP * rows)
    return call(
        partial(back_kernel, blk, per, first * per, count),
        "attend_back",
        at,
        ((last - first) * per,),
        [whole] * GROUP
        + [fixed((HD, rows))] * (2 * GROUP)
        + [fixed((count, 1, blk))]
        + ([whole] * GROUP + [fixed(dq)] if first else []),
        [whole] * GROUP + [fixed(dq)],
        [like((features, rows), BF)] * GROUP + [like(dq, F32)],
        (*qkv, *do, *o, lse, *before),
        scratch=[
            pltpu.VMEM((features, blk), BF),
            pltpu.VMEM((GROUP * rows, 128), BF),
            pltpu.VMEM((HD, GROUP * rows), BF),
            pltpu.VMEM((GROUP * rows, 128), BF),
            pltpu.VMEM((128, GROUP * rows), BF),
            pltpu.VMEM((HD, GROUP * rows), BF),
            pltpu.VMEM((2, GROUP * rows, 128), BF),
            pltpu.VMEM((count, 1, blk), F32),
            pltpu.VMEM((blk, 128), F32),
        ],
    )


def stack_kernel(at_ref, *refs):
    ins, out_ref = refs[:GROUP], refs[GROUP]
    for s in range(GROUP):
        head = pl.ds(pl.multiple_of((at_ref[0] ^ s) * HD, HD), HD)
        out_ref[head, :] = ins[s][...]


def stack(at, heads):
    rows = heads[0].shape[1]
    return call(
        stack_kernel,
        "stack",
        at,
        (1,),
        [fixed((HD, rows))] * GROUP,
        fixed((GROUP * HD, rows)),
        like((GROUP * HD, rows), BF),
        heads,
    )


def unsplit_kernel(at_ref, *refs):
    ins, outs = refs[:4], refs[4:]
    cols = ins[0].shape[1]
    for r in range(4):
        lanes = pl.ds(pl.multiple_of(((at_ref[1] + r) % 4) * cols, cols), cols)
        for s in range(GROUP):
            head = pl.ds(pl.multiple_of((at_ref[0] ^ s) * HD, HD), HD)
            outs[s][:, lanes] = ins[r][head, :]


def unsplit(at, pieces):
    shape = (HD, 4 * pieces[0].shape[1])
    return call(
        unsplit_kernel,
        "unsplit",
        at,
        (1,),
        [fixed(pieces[0].shape)] * 4,
        [fixed(shape)] * GROUP,
        [like(shape, BF)] * GROUP,
        pieces,
    )


def heads_of(mine, r, features):
    return pl.ds(pl.multiple_of(((mine + 4 - r) % 4) * features, features), features)


def mid_kernel(at_ref, *refs):
    pieces, (w_ref, x_ref, gain_ref, bias_ref, h_ref, b_ref) = refs[:6], refs[6:]
    h = x_ref[...].astype(F32)
    for r, piece in enumerate(in_order(at_ref[1], *[ref[...] for ref in pieces])):
        rows = heads_of(at_ref[1], 4 - r, piece.shape[0])
        h = h + mm(turned(piece), w_ref[rows, :])

    @pl.when(pl.program_id(0) == 0)
    def _():
        h_ref[...] = h

    normal, _ = normalize(h)
    b_ref[...] = (normal * gain_ref[...] + bias_ref[...]).astype(BF)


def mid(at, pieces, w_o, tokens, gain, bias):
    features, rows = pieces[0].shape
    width, quarter = tokens.shape[1], rows // 4
    return call(
        mid_kernel,
        "mid",
        at,
        (4,),
        [pl.BlockSpec((features, quarter), lambda q, n: (0, (n[1] + q) % 4))] * 6
        + [fixed(w_o.shape)]
        + [pl.BlockSpec((quarter, width), lambda q, n: ((n[1] + q) % 4, 0))]
        + [fixed((1, width))] * 2,
        [fixed((quarter, width)), pl.BlockSpec((quarter, width), lambda q, n: (q, 0))],
        [like((quarter, width), F32), like((rows, width), BF)],
        (*pieces, w_o, tokens, gain, bias),
    )


def add_up(refs):
    total = refs[0][...]
    for ref in refs[1:]:
        total = total + ref[...].astype(F32)
    return total


def mid_back_kernel(at_ref, *refs):
    shares, (w_ref, h_ref, dy_ref, gain_ref, dh_ref, low_ref, sums_ref) = refs[:4], refs[4:11]
    do_refs = refs[11:]
    db = add_up(shares)
    normal, scale = normalize(h_ref[...])
    dh = dy_ref[...].astype(F32) + norm_back(db, gain_ref[...], normal, scale)
    dh_ref[...] = dh
    low = dh.astype(BF)
    low_ref[...] = low
    sums_ref[0:1, :] = jnp.sum(db * normal, axis=0, keepdims=True)
    sums_ref[1:2, :] = jnp.sum(db, axis=0, keepdims=True)
    for r in range(4):
        rows = heads_of(at_ref[1], r, do_refs[r].shape[0])
        do_refs[r][...] = mm_t(w_ref[rows, :], low).astype(BF)


def mid_back(at, shares, w_o, h, dy, gain):
    quarter, width = h.shape
    whole = fixed((quarter, width))
    piece = (w_o.shape[0] // 4, quarter)
    return call(
        mid_back_kernel,
        "mid_back",
        at,
        (1,),
        [whole] * 4 + [fixed(w_o.shape), whole, whole, fixed((1, width))],
        [whole] * 2 + [fixed((2, width))] + [fixed(piece)] * 4,
        [like((quarter, width), F32), like((quarter, width), BF), like((2, width), F32)]
        + [like(piece, BF)] * 4,
        (*shares, w_o, h, dy, gain),
    )


def cut_rows_kernel(at_ref, *refs):
    ins, outs = refs[:2], refs[2:]
    cols = outs[0].shape[2]
    for r in range(4):
        lanes = pl.ds(pl.multiple_of(((at_ref[1] + r) % 4) * cols, cols), cols)
        for k in range(2):
            outs[r][k] = ins[k][:, lanes]


def cut_rows(at, grads):
    features, rows = grads[0].shape
    shape = (2, features, rows // 4)
    return call(
        cut_rows_kernel,
        "cut_rows",
        at,
        (1,),
        [fixed((features, rows))] * 2,
        [fixed(shape)] * 4,
        [like(shape, BF)] * 4,
        grads,
    )


def first_back_kernel(at_ref, *refs):
    pieces, (w_ref, x_ref, dh_ref, gain_ref, out_ref, sum_s) = refs[:8], refs[8:]
    i = pl.program_id(0)
    total = 0.0
    for batch in range(2):
        piece = pieces[4 * batch][...]
        for r in range(1, 4):
            piece = jnp.where(i == r, pieces[4 * batch + r][...], piece)
        for k in range(2):
            total = total + mm(turned(piece[k]), w_ref[at_ref[0] ^ (2 * batch + k)])

    @pl.when(i == 0)
    def _():
        sum_s[...] = total

    @pl.when(i > 0)
    def _():
        sum_s[...] += total

    @pl.when(i == 3)
    def _():
        normal, scale = normalize(x_ref[...].astype(F32))
        grad = norm_back(sum_s[...], gain_ref[...], normal, scale)
        out_ref[...] = (dh_ref[...] + grad).astype(BF)


def first_back(at, near, far, w_heads, tokens, dh, gain):
    quarter, width = dh.shape
    shape = near[0].shape
    heads, features, _ = w_heads.shape
    own = lambda r, n: (n[1], 0)
    return call(
        first_back_kernel,
        "first_back",
        at,
        (4,),
        [fixed(shape)] * 8
        + [pl.BlockSpec((heads // 4, features, width), lambda r, n: ((n[1] + 4 - r) % 4, 0, 0))]
        + [pl.BlockSpec((quarter, width), own)]
        + [fixed((quarter, width)), fixed((1, width))],
        fixed((quarter, width)),
        like((quarter, width), BF),
        (*near, *far, w_heads, tokens, dh, gain),
        scratch=[pltpu.VMEM((quarter, width), F32)],
    )


def in_order(mine, own, right, left, far, right_two, left_two):
    one = jnp.where(mine == 3, far, left)
    two = jnp.where(mine < 2, left_two, right_two)
    three = jnp.where(mine == 0, far, right)
    return own, one, two, three


def one_hot(slots, dest):
    return jnp.where(slots == dest, 1.0, 0.0).astype(BF)


def dispatch_kernel(at_ref, dest_ref, rows_ref, out_ref, spread_s):
    blk, rows = min(256, spread_s.shape[0]), dest_ref.shape[1]

    @pl.when(pl.program_id(0) == 0)
    def _():
        slot = lax.broadcasted_iota(jnp.int32, (blk, rows), 0)
        for start in range(0, spread_s.shape[0], blk):
            spread_s[start : start + blk, :] = one_hot(slot + start, dest_ref[...])

    out_ref[...] = mm(spread_s[...], rows_ref[...]).astype(BF)


def columns(rows, width):
    return pl.BlockSpec((rows, width), lambda i, n: (0, i))


def dispatch(at, dest_row, values, slots):
    rows, width = values.shape
    blk = min(256, width)
    return call(
        dispatch_kernel,
        "dispatch",
        at,
        (width // blk,),
        [fixed((1, rows)), columns(rows, blk)],
        columns(slots, blk),
        like((slots, width), BF),
        (dest_row, values),
        scratch=[pltpu.VMEM((slots, rows), BF)],
    )


def join_kernel(at_ref, *refs):
    pieces, out_ref = refs[:6], refs[6]
    r = pl.program_id(0)
    for place, piece in enumerate(in_order(at_ref[1], *[ref[...] for ref in pieces])):

        @pl.when(r == place)
        def _():
            out_ref[...] = piece


def join(at, pieces):
    each, width = pieces[0].shape
    return call(
        join_kernel,
        "join",
        at,
        (4,),
        [fixed((each, width))] * 6,
        pl.BlockSpec((each, width), lambda r, n: ((n[1] + r) % 4, 0)),
        like((4 * each, width), BF),
        pieces,
    )


def write_shares(mine, total, own_ref, one_ref, two_ref, three_ref, end_ref):
    rows = own_ref.shape[0]
    own_ref[...] = total[:rows]
    one, two, three = [total[r * rows : (r + 1) * rows].astype(BF) for r in (1, 2, 3)]
    one_ref[...] = one
    two_ref[...] = two
    three_ref[...] = three
    end_ref[...] = jnp.where(mine == 0, three, one)


def share_shapes(rows, width):
    return [like((rows, width), F32)] + [like((rows, width), BF)] * 4


def combine_kernel(count, onto, at_ref, *refs):
    dests, backs = refs[:count], refs[count : 2 * count]
    base_ref, refs, pick_s = refs[2 * count], refs[2 * count + 1 : -1], refs[-1]
    rows, slots = base_ref.shape[0], backs[0].shape[0]
    blk = rows // 4

    @pl.when(pl.program_id(0) == 0)
    def _():
        lane = lax.broadcasted_iota(jnp.int32, (blk, slots), 1)
        for k in range(count):
            for start in range(0, rows, blk):
                dest = dests[k][start : start + blk, :]
                pick_s[start : start + blk, k * slots : (k + 1) * slots] = one_hot(lane, dest)

    total = base_ref[...].astype(F32)
    for k in range(count):
        total = total + mm(pick_s[:, k * slots : (k + 1) * slots], backs[k][...])
    write_shares(at_ref[1], total, *refs[onto:])
    if onto:
        refs[onto][...] += refs[0][...]


def combine(at, dests, backs, base, h=None):
    count, (slots, width), rows = len(backs), backs[0].shape, base.shape[0]
    blk = min(256, width)
    onto = int(h is not None)
    quarter = columns(rows // 4, blk)
    return call(
        partial(combine_kernel, count, onto),
        "combine",
        at,
        (width // blk,),
        [fixed((rows, 1))] * count
        + [columns(slots, blk)] * count
        + [columns(rows, blk)]
        + [quarter] * onto,
        [quarter] * 5,
        share_shapes(rows // 4, width),
        (*dests, *backs, base) + ((h,) if onto else ()),
        scratch=[pltpu.VMEM((rows, count * slots), BF)],
    )


def mm_t(a, b):
    return lax.dot_general(a, b, (((1,), (1,)), ((), ())), preferred_element_type=F32)


def gelu_both(u):
    c = 0.7978845608028654
    square = u * u
    t = jnp.tanh(u * (c + (c * 0.044715) * square))
    half = 0.5 + 0.5 * t
    slope = half + (0.5 * u) * (1.0 - t * t) * (c + (3.0 * c * 0.044715) * square)
    return u * half, slope


def high_low(value):
    high = value.astype(BF)
    return high, (value - high.astype(F32)).astype(BF)


def two_coefs(logits, lane, experts):
    inside = (lane >= experts) & (lane < experts + 2)
    top = jnp.max(jnp.where(inside, logits, HIDE), axis=1, keepdims=True)
    e = jnp.where(inside, jnp.exp(logits - top), 0.0)
    e = e / jnp.sum(e, axis=1, keepdims=True)
    first = jnp.sum(jnp.where(lane == experts, e, 0.0), axis=1, keepdims=True)
    second = jnp.sum(jnp.where(lane == experts + 1, e, 0.0), axis=1, keepdims=True)
    return first, second


def small_back(d_small, rows, w_small_ref, small_ref, i):
    high, low = high_low(d_small)
    w_small = w_small_ref[...]
    high_t, low_t = high_low(d_small.T)

    @pl.when(i == 0)
    def _():
        small_ref[...] = jnp.zeros(small_ref.shape, F32)

    small_ref[...] += mm(high_t, rows) + mm(low_t, rows)
    return mm_t(high, w_small) + mm_t(low, w_small)


def expert_kernel(experts, half, at_ref, rows_ref, dy_ref, up_ref, down_ref, w_small_ref, *outs):
    if half:
        outs = outs[5:]
    rows_out_ref, hid_ref, dy_out_ref, deu_ref, y_ref, d_rows_ref, small_ref = outs
    rows = rows_ref[...]
    rows_out_ref[...] = rows
    up = mm(rows, up_ref[...])
    logits = mm(rows, w_small_ref[...])
    lane = lax.broadcasted_iota(jnp.int32, logits.shape, 1)
    routed = lane < experts
    top = jnp.max(jnp.where(routed, logits, HIDE), axis=1, keepdims=True)
    probs = jnp.where(routed, jnp.exp(logits - top), 0.0)
    probs = probs / jnp.sum(probs, axis=1, keepdims=True)
    own = jnp.where(lane == at_ref[2], 1.0, 0.0)
    gate = jnp.sum(probs * own, axis=1, keepdims=True)
    first, second = two_coefs(logits, lane, experts)
    weight = second * gate
    dy = dy_ref[...].reshape(rows.shape).astype(F32)
    d_y = (weight * dy).astype(BF)
    dy_out_ref[...] = d_y
    d_hidden = mm_t(d_y, down_ref[...])
    hidden, slope = gelu_both(up)
    hidden = hidden.astype(BF)
    hid_ref[...] = hidden
    d_up = (d_hidden * slope).astype(BF)
    deu_ref[...] = d_up
    y = mm(hidden, down_ref[...])
    y_ref[...] = (weight * y).astype(BF).reshape(y_ref.shape)
    along = gate * jnp.sum(dy * y, axis=1, keepdims=True)
    mixed = first * second * along
    d_small = (second * along) * (own - probs)
    d_small = jnp.where(routed, d_small, 0.0)
    d_small = d_small + jnp.where(lane == experts + 1, mixed, 0.0)
    d_small = d_small - jnp.where(lane == experts, mixed, 0.0)
    d_rows = mm_t(d_up, up_ref[...]) + small_back(d_small, rows, w_small_ref, small_ref, pl.program_id(0))
    d_rows_ref[...] = d_rows.astype(BF)


def expert_rows(at, rows, dy, w_up, w_down, w_small, experts, half, before):
    count, width = rows.shape
    hid, lanes = w_up.shape[1], w_small.shape[1]
    blk = min(512, count)
    capacity = count // dy.shape[0]
    steps = count // blk
    moving = pl.BlockSpec((blk, width), lambda i, n: (i, 0))
    slots = pl.BlockSpec((blk // capacity, capacity, width), lambda i, n: (i, half, 0))
    kept = [pl.BlockSpec((blk, size), lambda i, n: (i + half * steps, 0)) for size in (width, hid, width, hid)]
    return call(
        partial(expert_kernel, experts, half),
        "expert_rows",
        at,
        (steps,),
        [
            moving,
            slots,
            fixed((width, hid)),
            fixed((hid, width)),
            fixed((width, lanes)),
        ]
        + [pl.BlockSpec(memory_space=pl.ANY)] * (5 * half),
        kept + [slots, moving, fixed((lanes, width))],
        [like((2 * count, size), BF) for size in (width, hid, width, hid)]
        + [like(dy.shape, BF), like((count, width), BF)]
        + [like((lanes, width), F32)],
        (rows, dy, w_up, w_down, w_small, *before),
        alias={6 + k: k for k in range(5)} if half else None,
        vmem=56,
    )


def dense_kernel(experts, at_ref, rows_ref, dy_ref, in_ref, out_ref, w_small_ref, *outs):
    hid_ref, grad_ref, d_up_ref, mix_ref, db_ref, small_ref = outs
    rows = rows_ref[...]
    up = mm(rows, in_ref[...])
    logits = mm(rows, w_small_ref[...])
    lane = lax.broadcasted_iota(jnp.int32, logits.shape, 1)
    first, second = two_coefs(logits, lane, experts)
    dy = dy_ref[...].astype(F32)
    grad = (first * dy).astype(BF)
    grad_ref[...] = grad
    d_hidden = mm_t(grad, out_ref[...])
    hidden, slope = gelu_both(up)
    hidden = hidden.astype(BF)
    hid_ref[...] = hidden
    d_up = (d_hidden * slope).astype(BF)
    d_up_ref[...] = d_up
    dense = mm(hidden, out_ref[...])
    mix_ref[...] = first * dense
    mixed = first * second * jnp.sum(dy * dense, axis=1, keepdims=True)
    d_small = jnp.where(lane == experts, mixed, 0.0) - jnp.where(lane == experts + 1, mixed, 0.0)
    db_ref[...] = mm_t(d_up, in_ref[...]) + small_back(d_small, rows, w_small_ref, small_ref, pl.program_id(0))


def dense_rows(at, rows, dy, w_in, w_out, w_small, experts):
    (count, width), hid, lanes = rows.shape, w_in.shape[1], w_small.shape[1]
    blk = min(512, count)
    row_out = pl.BlockSpec((blk, width), lambda i, n: (i, 0))
    hid_out = pl.BlockSpec((blk, hid), lambda i, n: (i, 0))
    return call(
        partial(dense_kernel, experts),
        "dense_rows",
        at,
        (count // blk,),
        [row_out, row_out, fixed((width, hid)), fixed((hid, width)), fixed((width, lanes))],
        [hid_out, row_out, hid_out, row_out, row_out, fixed((lanes, width))],
        [
            like((count, hid), BF),
            like((count, width), BF),
            like((count, hid), BF),
            like((count, width), F32),
            like((count, width), F32),
            like((lanes, width), F32),
        ],
        (rows, dy, w_in, w_out, w_small),
        vmem=56,
    )


def turned(value):
    return value.astype(F32).T.astype(BF)


def dense_grads_kernel(at_ref, b_ref, d_up_ref, grad_ref, hid_ref, keep_ref, give_ref):
    width = d_up_ref.shape[1]
    first = mm(turned(b_ref[...]), d_up_ref[...]).astype(BF)
    second = mm(turned(grad_ref[...]), hid_ref[...]).astype(BF)
    half = pl.num_programs(0) // 2
    for side, ref in ((0, keep_ref), (1, give_ref)):

        @pl.when(pl.program_id(0) // half == side)
        def _():
            ref[0, :, :width] = first
            ref[0, :, width:] = second


def dense_grads(at, b, d_up, grad, hidden, parts):
    (rows, width), hid = b.shape, hidden.shape[1]
    own, half, bits = width // parts, parts // 2, parts.bit_length() - 1

    def part(q, n):
        turned_q = sum([((q // 2**k) % 2) * 2 ** (bits - 1 - k) for k in range(bits)])
        return turned_q ^ n[2]

    column = pl.BlockSpec((rows, own), lambda q, n: (0, part(q, n)))
    shape = (1, own, 2 * hid)
    return call(
        dense_grads_kernel,
        "dense_grads",
        at,
        (parts,),
        [column, fixed((rows, hid)), column, fixed((rows, hid))],
        [
            pl.BlockSpec(shape, lambda q, n: (jnp.minimum(q, half - 1), 0, 0)),
            pl.BlockSpec(shape, lambda q, n: (jnp.maximum(q - half, 0), 0, 0)),
        ],
        [like((half, own, 2 * hid), BF)] * 2,
        (b, d_up, grad, hidden),
    )


def attention_grads_kernel(experts, at_ref, *refs):
    grads, o_refs, refs = refs[:GROUP], refs[GROUP : GROUP + 6], refs[GROUP + 6 :]
    a_ref, dh_ref, w_ref, gain_ref, bias_ref, sums_ref = refs[:6]
    small_refs, (out_ref, all_s) = refs[6:-2], refs[-2:]
    heads, features = GROUP * HD, grads[1].shape[0]
    products, plain = 0.0, 0.0
    for k in range(GROUP):
        head = at_ref[0] ^ k
        rows = pl.ds(pl.multiple_of(head * features, features), features)
        grad = grads[k][...]
        weight = w_ref[head].astype(F32)
        total = mm(grad, a_ref[...])
        all_s[rows, :] = total
        each = jnp.sum(grad.astype(F32), axis=1, keepdims=True)
        products = products + jnp.sum(total * weight, axis=0, keepdims=True)
        plain = plain + jnp.sum(each * weight, axis=0, keepdims=True)
    first = GROUP * features
    for r, piece in enumerate(in_order(at_ref[1], *[ref[...] for ref in o_refs])):
        rows = pl.ds(pl.multiple_of(first + ((at_ref[1] + r) % 4) * heads, heads), heads)
        all_s[rows, :] = mm(piece, dh_ref[...])
    first += 4 * heads
    small = add_up(small_refs)
    row = lax.broadcasted_iota(jnp.int32, small.shape, 0)
    d_gain = (products - bias_ref[...] * plain) / gain_ref[...]
    for k, sums in enumerate((sums_ref[0:1, :], sums_ref[1:2, :], d_gain, plain)):
        small = jnp.where(row == experts + 2 + k, sums, small)
    all_s[first:, :] = small
    out_ref[...] = all_s[...].T.astype(BF)


def attention_grads(at, grads, o, a, dh, w_heads, gain, bias, sums, small, experts):
    rows, width = a.shape
    features, lanes = grads[0].shape[0], small[0].shape[0]
    piece = pl.BlockSpec((o[0].shape[0], dh.shape[0]), lambda i, n: (0, n[1]))
    height = GROUP * features + 4 * o[0].shape[0] + lanes
    blk = min(256, width)
    return call(
        partial(attention_grads_kernel, experts),
        "attention_grads",
        at,
        (width // blk,),
        [fixed((features, rows))] * GROUP
        + [piece] * 6
        + [columns(rows, blk), columns(dh.shape[0], blk)]
        + [pl.BlockSpec((GROUP, features, blk), lambda i, n: (0, 0, i))]
        + [columns(1, blk)] * 2
        + [columns(2, blk)]
        + [columns(lanes, blk)] * len(small),
        pl.BlockSpec((blk, height), lambda i, n: (i, 0)),
        like((width, height), BF),
        (*grads, *o, a, dh, w_heads, gain, bias, sums, *small),
        scratch=[pltpu.VMEM((height, blk), F32)],
    )


def hop(value, *pairs):
    return lax.ppermute(value, "mp", pairs)


def rotate(value, steps):
    return hop(value, *[(s, (s + steps) % 4) for s in range(4)])


def gather_near(own):
    right = hop(own, (0, 1), (1, 2), (2, 3))
    left = hop(own, (1, 0), (2, 1), (3, 2))
    return own, right, left, hop(own, (0, 3), (3, 0))


def gather_far(near):
    _, right, left, _ = near
    return *near, hop(right, (1, 2), (2, 3)), hop(left, (1, 0), (2, 1))


def gather_pieces(own):
    return gather_far(gather_near(own))


def scatter_far(shares):
    _, _, two, _, end = shares
    return hop(two, (2, 1), (3, 2)), hop(two, (0, 1), (1, 2)), hop(end, (0, 3), (3, 0))


def scatter_near(shares, came):
    own, one, _, three, _ = shares
    from_right, from_left, from_end = came
    three = (three.astype(F32) + from_right.astype(F32)).astype(BF)
    one = (one.astype(F32) + from_left.astype(F32)).astype(BF)
    return own, hop(three, (1, 0), (2, 1), (3, 2)), hop(one, (0, 1), (1, 2), (2, 3)), from_end


def group_swap(value, s):
    count = lax.axis_size("dp")
    return lax.ppermute(value, "dp", [(t, t ^ s) for t in range(count)])


def expert_swap(value, experts):
    wide = value.reshape(experts, value.shape[0] // experts, value.shape[1])
    return lax.all_to_all(wide, "dp", 0, 0, tiled=True).reshape(value.shape)


def roll_rows(value, start):
    twice = jnp.concatenate([value, value], axis=0)
    return lax.dynamic_slice_in_dim(twice, start, value.shape[0], 0)


def add_halves(keep, came):
    return (keep.astype(F32) + came.astype(F32)).astype(BF)


def body(
    tokens,
    cotangent,
    ln_gains,
    ln_biases,
    w_qkv,
    w_o,
    w_in,
    w_out,
    w_router,
    w_coef,
    w_up,
    w_down,
    routes,
    long_group,
):
    rows, width = tokens.shape
    dps = lax.axis_size("dp")
    mine, position = lax.axis_index("mp"), lax.axis_index("dp")
    quarter = rows // 4
    start = mine * quarter
    heads_loc = w_qkv.shape[2] // HD
    hid = w_in.shape[1]
    experts = w_router.shape[1]
    capacity = max(2, 2 * rows // experts)
    half = capacity // 2
    barrier = lax.optimization_barrier
    first_len = lax.dynamic_index_in_dim(long_group, position // GROUP, 0, keepdims=False)
    at = jnp.stack([position % GROUP, mine, position, first_len]).astype(jnp.int32)
    gains = [ln_gains[0:1], ln_gains[1:2]]
    biases = [ln_biases[0:1], ln_biases[1:2]]
    w_o_all = lax.all_gather(w_o, "mp", axis=0, tiled=True)

    w_heads = w_qkv.reshape(width, 3, heads_loc, HD).transpose(2, 1, 3, 0)
    w_heads = w_heads.reshape(heads_loc, 3 * HD, width)
    a_r, *qkv = project(at, tokens, gains[0], biases[0], w_heads)
    qkv = [qkv[0]] + [group_swap(qkv[s], s) for s in (1, 2, 3)]

    route = roll_rows(routes, start)[:, 0]
    picked = (route[:, None] == jnp.arange(experts, dtype=jnp.int32)[None, :]).astype(jnp.int32)
    slot = jnp.sum((jnp.cumsum(picked, axis=0) - picked) * picked, axis=1)
    dy_b = roll_rows(cotangent, start)
    send_dy = dispatch(at, (route * capacity + slot)[None, :], dy_b, experts * capacity)
    *qkv, send_dy = barrier((*qkv, send_dy))
    in_half = [slot < half, slot >= half]
    dests = [
        jnp.where(in_half[k], route * half + slot - k * half, -1).astype(jnp.int32) for k in (0, 1)
    ]

    *o_t, lse = attend(at, qkv)
    *o_t, w_o_all = barrier((*o_t, w_o_all))
    o_heads = [o_t[0]] + [group_swap(o_t[s], s) for s in (1, 2, 3)]
    lanes = -(-(experts + 2) // 128) * 128
    w_small = jnp.concatenate(
        [w_router, w_coef, jnp.zeros((width, lanes - experts - 2), BF)], axis=1
    )
    *o_heads, send_dy, w_small = barrier((*o_heads, send_dy, w_small))
    got_dy = expert_swap(send_dy, experts).reshape(experts, capacity, width)
    o_pieces = gather_pieces(stack(at, o_heads))
    h, b_r = mid(at, o_pieces, w_o_all, tokens, gains[1], biases[1])

    b_r, w_rows = barrier((b_r, w_heads.reshape(-1, width)))
    w_near = gather_near(w_rows)
    send_0 = dispatch(at, dests[0][None, :], b_r, experts * half)
    send_0, got_dy = barrier((send_0, got_dy))
    got_0 = expert_swap(send_0, experts)
    send_1 = dispatch(at, dests[1][None, :], b_r, experts * half)
    b_r, send_1 = barrier((b_r, send_1))
    hidden, dense_grad, d_up, mix_base, db_base, small_t = dense_rows(
        at, b_r, dy_b, w_in, w_out, w_small, experts
    )
    send_1, got_0, db_base = barrier((send_1, got_0, db_base))
    got_1 = expert_swap(send_1, experts)

    *kept, d_rows_0, small_0 = expert_rows(
        at, got_0, got_dy, w_up[0], w_down[0], w_small, experts, 0, ()
    )
    back_0 = expert_swap(d_rows_0, experts)
    got_1, *w_near = barrier((got_1, *w_near))
    w_far = gather_far(w_near)
    *kept, d_rows_1, small_1 = expert_rows(
        at, got_1, got_dy, w_up[0], w_down[0], w_small, experts, 1, kept
    )
    got, hidden_e, d_y, d_eu, back_y = kept
    back_1 = expert_swap(d_rows_1, experts)
    d_rows_1, b_r = barrier((d_rows_1, b_r))
    halving = width == dps * 128
    if halving:
        grads = dense_grads(at, b_r, d_up, dense_grad, hidden, dps)
    else:
        grads = [ein("td,tf->df", b_r, d_up).astype(BF), ein("td,tf->df", dense_grad, hidden).astype(BF)]
    tied = barrier((back_0, back_1, back_y, *grads, *w_far))
    back_0, back_1, back_y, grads, w_far = *tied[:3], tied[3:5], tied[5:]

    dest_cols = [dest[:, None] for dest in dests]
    tok_y = expert_swap(back_y.reshape(experts * capacity, width), experts)
    shares = combine(at, dest_cols, [back_0, back_1], db_base)
    far = scatter_far(shares)
    w_heads_all = join(at, w_far).reshape(-1, *w_heads.shape[1:])
    *far, g_0, g_1, w_heads_all = barrier((*far, *grads, w_heads_all))
    grads = [g_0, g_1]
    shares = scatter_near(shares, far)

    mix = combine(at, [(route * capacity + slot)[:, None]], [tok_y], mix_base, h)
    tied = barrier((*shares, *mix))
    shares, mix = tied[:4], tied[4:]
    mix_far = scatter_far(mix)
    dh, dh_r, sums_2, *do_q = mid_back(at, shares, w_o_all, h, dy_b[:quarter], gains[1])
    do_q = [do_q[0]] + [rotate(do_q[r], -r) for r in (1, 2, 3)]
    do_heads = unsplit(at, do_q)
    do_t = [do_heads[0]] + [group_swap(do_heads[s], s) for s in (1, 2, 3)]
    if halving:
        came_1 = group_swap(grads[1], 1)
        half = dps // 4
        give = add_halves(grads[0][half:], came_1[half:])
        *do_t, give = barrier((*do_t, give))
        came_2 = group_swap(give, 2)
    addends = scatter_near(mix, mix_far)
    out_q = sum([part.astype(F32) for part in addends[1:]], addends[0]).astype(BF)
    *do_t, out_q = barrier((*do_t, out_q))
    out_near = gather_near(out_q)
    before = attend_back(at, qkv, do_t, o_t, lse, (), 0, 1)
    tied = barrier((*before, *out_near))
    before, out_near = tied[:5], tied[5:]
    out_far = gather_far(out_near)
    *d_qkv, _ = attend_back(at, qkv, do_t, o_t, lse, before, 1, GROUP)
    tied = barrier((*d_qkv, *out_far))
    d_qkv, out_far = tied[:4], tied[4:]
    output = join(at, out_far)
    if halving:
        keep = add_halves(grads[0][:half], came_1[:half])
        *d_qkv, came_2, keep = barrier((*d_qkv, came_2, keep))
        grads = add_halves(keep, came_2)
        bit = 4
        while bit < dps:
            half = grads.shape[0] // 2
            grads = add_halves(grads[:half], group_swap(grads[half:], bit))
            bit *= 2
        grads = [grads[0][:, :hid], grads[0][:, hid:]]
    else:
        grads = [lax.psum_scatter(grad, "dp", scatter_dimension=0, tiled=True) for grad in grads]

    d_own, got, hidden_e, d_y, d_eu = barrier((d_qkv[0], got, hidden_e, d_y, d_eu))
    d_qkv = [d_own] + [group_swap(d_qkv[s], s) for s in (1, 2, 3)]
    near = cut_rows(at, d_qkv[:2])
    near = [near[0]] + [rotate(near[r], r) for r in (1, 2, 3)]
    far = cut_rows(at, d_qkv[2:])
    grad_down = ein("rf,rd->fd", hidden_e, d_y)
    tied = barrier((*near, *far, *d_qkv, grad_down, output))
    near, far, d_qkv, (grad_down, output) = tied[:4], tied[4:8], tied[8:12], tied[12:]
    far = [far[0]] + [rotate(far[r], r) for r in (1, 2, 3)]
    grads_a = attention_grads(
        at, d_qkv, o_pieces, a_r, dh_r, w_heads, gains[0], biases[0], sums_2, (small_0, small_1, small_t), experts
    )
    grads_a = lax.psum_scatter(grads_a, "dp", scatter_dimension=0, tiled=True).T
    grad_up = ein("rd,rf->df", got, d_eu)
    *far, grad_up = barrier((*far, grad_up))
    grad_q = first_back(at, near, far, w_heads_all, tokens, dh, gains[0])
    grad_tokens = join(at, gather_pieces(grad_q))

    own, heads = width // dps, heads_loc * HD
    grad_qkv = grads_a[: 3 * heads].astype(F32).reshape(heads_loc, 3, HD, own).transpose(3, 1, 0, 2)
    grad_qkv = grad_qkv.reshape(own, 3, heads)
    grad_in = grads[0].astype(F32)
    grad_out = grads[1].astype(F32).T
    rest = grads_a[3 * heads : 7 * heads].reshape(4, heads, own)
    small = jnp.broadcast_to(grads_a[7 * heads :], (4, lanes, own))
    rest = lax.all_to_all(jnp.concatenate([rest, small], axis=1), "mp", 0, 0, tiled=True)
    rest = jnp.sum(rest.astype(F32), axis=0)
    grad_o, small = rest[:heads], rest[heads:]
    small_out = small[: experts + 2].T
    return (
        output,
        grad_tokens,
        jnp.stack([small[experts + 4], small[experts + 2]]),
        jnp.stack([small[experts + 5], small[experts + 3]]),
        grad_qkv,
        grad_o,
        grad_in,
        grad_out,
        small_out[:, :experts],
        small_out[:, experts:],
        grad_up[None],
        grad_down[None],
    )


def solution(mesh):
    in_specs = (
        P("dp", None),
        P("dp", None),
        P(),
        P(),
        P(None, None, "mp"),
        P("mp", None),
        P(None, "mp"),
        P("mp", None),
        P(),
        P(),
        P("dp", None, "mp"),
        P("dp", "mp", None),
        P("dp", None),
        P(),
    )
    out_specs = (
        P("dp", None),
        P("dp", None),
        P(None, "dp"),
        P(None, "dp"),
        P("dp", None, "mp"),
        P("mp", "dp"),
        P("dp", "mp"),
        P("mp", "dp"),
        P("dp", None),
        P("dp", None),
        P("dp", None, "mp"),
        P("dp", "mp", None),
    )
    return jax.shard_map(body, mesh=mesh, in_specs=in_specs, out_specs=out_specs, check_vma=False)
```

```python
from functools import partial

import jax
import jax.numpy as jnp
from jax import lax
from jax.experimental import pallas as pl
from jax.experimental.pallas import tpu as pltpu
from jax.sharding import PartitionSpec as P

HD = 64
GROUP = 4
EPS = 1e-05
LOG2E = 1.4426950408889634
SCALE2 = 0.125 * LOG2E
HIDE = -1e30
BF = jnp.bfloat16
F32 = jnp.float32
LIGHT = pl.CostEstimate(flops=1 << 20, bytes_accessed=1 << 20, transcendentals=0)


def mm(a, b):
    return jnp.dot(a, b, preferred_element_type=F32)


def ein(spec, a, b):
    return jnp.einsum(spec, a, b, preferred_element_type=F32)


def call(kernel, name, prefetch, grid, in_specs, out_specs, out_shape, args, scratch=(), alias=None, vmem=48):
    return pl.pallas_call(
        kernel,
        grid_spec=pltpu.PrefetchScalarGridSpec(
            num_scalar_prefetch=1,
            grid=grid,
            in_specs=in_specs,
            out_specs=out_specs,
            scratch_shapes=list(scratch),
        ),
        out_shape=out_shape,
        input_output_aliases=alias or {},
        compiler_params=pltpu.CompilerParams(vmem_limit_bytes=vmem * 2**20),
        cost_estimate=LIGHT,
        name=name,
    )(prefetch, *args)


def fixed(shape):
    zeros = (0,) * len(shape)
    return pl.BlockSpec(shape, lambda *_: zeros)


def like(shape, dtype):
    return jax.ShapeDtypeStruct(shape, dtype)


def normalize(v):
    mean = jnp.mean(v, axis=-1, keepdims=True)
    centred = v - mean
    scale = lax.rsqrt(jnp.mean(centred * centred, axis=-1, keepdims=True) + EPS)
    return centred * scale, scale


def norm_back(grad, gain, normal, scale):
    g = grad * gain
    along = jnp.mean(g * normal, axis=-1, keepdims=True)
    return scale * (g - jnp.mean(g, axis=-1, keepdims=True) - normal * along)


def qkv_kernel(at_ref, x_ref, gain_ref, bias_ref, w_ref, a_ref, *outs):
    normal, _ = normalize(x_ref[...].astype(F32))
    a = (normal * gain_ref[...] + bias_ref[...]).astype(BF)
    a_ref[...] = a
    for s in range(GROUP):
        outs[s][...] = mm_t(w_ref[at_ref[0] ^ s], a).astype(BF)


def project(at, tokens, gain, bias, w_heads):
    rows, width = tokens.shape
    features = w_heads.shape[1]
    blk = min(256, rows)
    moving = pl.BlockSpec((blk, width), lambda i, n: (i, 0))
    return call(
        qkv_kernel,
        "project",
        at,
        (rows // blk,),
        [moving, fixed((1, width)), fixed((1, width)), fixed(w_heads.shape)],
        [moving] + [pl.BlockSpec((features, blk), lambda i, n: (0, i))] * GROUP,
        [like((rows, width), BF)] + [like((features, rows), BF)] * GROUP,
        (tokens, gain, bias, w_heads),
    )


def fill_keys(k_s, place, keys, first_len, blk):
    rows = place * blk + lax.broadcasted_iota(jnp.int32, (blk, 128), 0)
    lane = lax.broadcasted_iota(jnp.int32, (blk, 128), 1)
    wide = jnp.concatenate([keys.astype(F32).T, jnp.zeros((blk, 128 - HD), F32)], axis=1)
    wide = jnp.where((lane == HD) & (rows < first_len), HIDE, wide)
    k_s[pl.ds(place * blk, blk), :] = wide.astype(BF)


def wide_query(query, place, first_len, blk):
    cols = place * blk + lax.broadcasted_iota(jnp.int32, (128 - HD, blk), 1)
    sub = lax.broadcasted_iota(jnp.int32, (128 - HD, blk), 0)
    extra = jnp.where((sub == 0) & (cols >= first_len), 1.0, 0.0)
    return jnp.concatenate([query, extra.astype(BF)], axis=0)


def causal(blk):
    keys = lax.broadcasted_iota(jnp.int32, (blk, blk), 0)
    queries = lax.broadcasted_iota(jnp.int32, (blk, blk), 1)
    return keys <= queries


def attend_kernel(blk, per, at_ref, *refs):
    qkv_refs, o_refs = refs[:GROUP], refs[GROUP : 2 * GROUP]
    lse_ref, k_s, qkv_s = refs[2 * GROUP :]
    i = pl.program_id(0)
    place, first_len = at_ref[0], at_ref[3]

    @pl.when(i == 0)
    def _():
        for s in range(GROUP):
            qkv_s[place ^ s] = qkv_refs[s][...]

    def part(which, j):
        return qkv_s[j // per, HD * which : HD * (which + 1), pl.ds((j % per) * blk, blk)]

    fill_keys(k_s, i, part(1, i), first_len, blk)
    query = wide_query(part(0, i), i, first_len, blk)

    def scores(j):
        return mm(k_s[pl.ds(pl.multiple_of(j * blk, blk), blk), :], query)

    s = jnp.where(causal(blk), scores(i), HIDE)
    top = jnp.max(s, axis=0, keepdims=True)
    p = jnp.exp2((s - top) * SCALE2)
    total = jnp.sum(p, axis=0, keepdims=True)
    acc = mm(part(2, i), p.astype(BF))

    def steps(blocks, carry):
        top, total, acc = carry
        s = [scores(j) for j in blocks]
        new = top
        for one in s:
            new = jnp.maximum(new, jnp.max(one, axis=0, keepdims=True))
        keep = jnp.exp2((top - new) * SCALE2)
        total, acc = total * keep, acc * keep
        for j, one in zip(blocks, s):
            p = jnp.exp2((one - new) * SCALE2)
            total = total + jnp.sum(p, axis=0, keepdims=True)
            acc = acc + mm(part(2, j), p.astype(BF))
        return new, total, acc

    low = jnp.where(i * blk >= first_len, first_len // blk, 0)
    pairs = (i - low) // 2
    carry = lax.fori_loop(
        0, pairs, lambda t, c: steps([low + 2 * t, low + 2 * t + 1], c), (top, total, acc)
    )
    top, total, acc = lax.fori_loop(low + 2 * pairs, i, lambda j, c: steps([j], c), carry)
    out = (acc / total).astype(BF)
    for s in range(GROUP):

        @pl.when((i // per) ^ place == s)
        def _():
            o_refs[s][:, pl.ds((i % per) * blk, blk)] = out

    lse_ref[0] = top * SCALE2 + jnp.log2(total)


def attend(at, qkv):
    features, rows = qkv[0].shape
    blk = min(512, rows)
    per = rows // blk
    count = GROUP * per
    return call(
        partial(attend_kernel, blk, per),
        "attend",
        at,
        (count,),
        [fixed((features, rows))] * GROUP,
        [fixed((HD, rows))] * GROUP + [pl.BlockSpec((1, 1, blk), lambda i, n: (i, 0, 0))],
        [like((HD, rows), BF)] * GROUP + [like((count, 1, blk), F32)],
        qkv,
        scratch=[pltpu.VMEM((GROUP * rows, 128), BF), pltpu.VMEM((GROUP, features, rows), BF)],
    )


def back_kernel(blk, per, count, at_ref, *refs):
    qkv_refs, do_refs, o_refs = refs[:GROUP], refs[GROUP : 2 * GROUP], refs[2 * GROUP : 3 * GROUP]
    lse_ref, refs = refs[3 * GROUP], refs[3 * GROUP + 1 :]
    out_refs, refs = refs[:GROUP], refs[GROUP:]
    dq_ref, out_ref, k_s, kt_s, v_s, wide_s, dot_s, both_s, delta_s, acc_s = refs
    j = pl.program_id(0)
    place, first_len = at_ref[0], at_ref[3]

    @pl.when(j == 0)
    def _():
        dq_ref[...] = jnp.zeros(dq_ref.shape, F32)
        zero = jnp.zeros((blk, HD), F32)
        for s in range(GROUP):
            for sub in range(per):
                i = (place ^ s) * per + sub
                at = pl.ds(pl.multiple_of(i * blk, blk), blk)
                cut = slice(sub * blk, (sub + 1) * blk)
                query = qkv_refs[s][0:HD, cut]
                keys = qkv_refs[s][HD : 2 * HD, cut]
                grad = do_refs[s][:, cut]
                fill_keys(k_s, i, keys, first_len, blk)
                kt_s[:, at] = keys
                dot_s[:, at] = grad
                wide_s[:, at] = wide_query(query, i, first_len, blk)
                grad = grad.astype(F32)
                values = qkv_refs[s][2 * HD :, cut].astype(F32)
                v_s[at, :] = jnp.concatenate([values.T, zero], axis=1).astype(BF)
                both_s[0, at, :] = jnp.concatenate([grad.T, zero], axis=1).astype(BF)
                both_s[1, at, :] = jnp.concatenate([zero, query.astype(F32).T], axis=1).astype(BF)
                held = o_refs[s][:, cut].astype(F32)
                delta_s[i] = jnp.sum(held * grad, axis=0, keepdims=True)

    here = pl.ds(pl.multiple_of(j * blk, blk), blk)
    keys_t = kt_s[:, here]
    values = v_s[here, 0:HD]

    def pair(i, diagonal):
        at = pl.ds(pl.multiple_of(i * blk, blk), blk)
        s = mm(k_s[here, :], wide_s[:, at])
        p = jnp.exp2(s * SCALE2 - lse_ref[i])
        if diagonal:
            p = jnp.where(causal(blk), p, 0.0)
        dp = mm(values, dot_s[:, at])
        ds = (p * (dp - delta_s[i])).astype(BF)
        return mm(p.astype(BF), both_s[0, at, :]) + mm(ds, both_s[1, at, :]), mm(keys_t, ds)

    acc_s[...], dq = pair(j, True)
    dq_ref[:, here] += dq

    def step_two(t, carry):
        i = j + 1 + 2 * t
        (kv_0, dq_0), (kv_1, dq_1) = pair(i, False), pair(i + 1, False)
        acc_s[...] += kv_0 + kv_1
        at = pl.ds(pl.multiple_of(i * blk, blk), 2 * blk)
        dq_ref[:, at] += jnp.concatenate([dq_0, dq_1], axis=1)
        return carry

    def step(i, carry):
        kv, dq = pair(i, False)
        acc_s[...] += kv
        dq_ref[:, pl.ds(pl.multiple_of(i * blk, blk), blk)] += dq
        return carry

    high = jnp.where((j + 1) * blk <= first_len, (first_len + blk - 1) // blk, count)
    pairs = (high - j - 1) // 2
    lax.fori_loop(0, pairs, step_two, 0)
    lax.fori_loop(j + 1 + 2 * pairs, high, step, 0)
    both = acc_s[...].T
    out_ref[0:HD, :] = (dq_ref[:, here] * 0.125).astype(BF)
    out_ref[HD : 2 * HD, :] = (both[HD:, :] * 0.125).astype(BF)
    out_ref[2 * HD :, :] = both[:HD, :].astype(BF)
    for s in range(GROUP):

        @pl.when((j // per) ^ place == s)
        def _():
            out_refs[s][:, pl.ds(pl.multiple_of((j % per) * blk, blk), blk)] = out_ref[...]


def attend_back(at, qkv, do, o, lse):
    features, rows = qkv[0].shape
    blk = min(512, rows)
    per = rows // blk
    count = GROUP * per
    return call(
        partial(back_kernel, blk, per, count),
        "attend_back",
        at,
        (count,),
        [fixed((features, rows))] * GROUP
        + [fixed((HD, rows))] * (2 * GROUP)
        + [fixed((count, 1, blk))],
        [fixed((features, rows))] * GROUP,
        [like((features, rows), BF)] * GROUP,
        (*qkv, *do, *o, lse),
        scratch=[
            pltpu.VMEM((HD, GROUP * rows), F32),
            pltpu.VMEM((features, blk), BF),
            pltpu.VMEM((GROUP * rows, 128), BF),
            pltpu.VMEM((HD, GROUP * rows), BF),
            pltpu.VMEM((GROUP * rows, 128), BF),
            pltpu.VMEM((128, GROUP * rows), BF),
            pltpu.VMEM((HD, GROUP * rows), BF),
            pltpu.VMEM((2, GROUP * rows, 128), BF),
            pltpu.VMEM((count, 1, blk), F32),
            pltpu.VMEM((blk, 128), F32),
        ],
    )


def stack_kernel(at_ref, pos_ref, *refs):
    ins, out_ref, all_s = refs[:GROUP], refs[GROUP], refs[GROUP + 1]
    for s in range(GROUP):
        head = pl.ds(pl.multiple_of((at_ref[0] ^ s) * HD, HD), HD)
        all_s[head, :] = ins[s][...]
    rows = all_s.shape[1]
    lane = lax.broadcasted_iota(jnp.int32, (rows, rows), 1)
    out_ref[...] = mm(all_s[...], one_hot(lane, pos_ref[...])).astype(BF)


def stack(at, pos_col, heads):
    rows = heads[0].shape[1]
    shape = (GROUP * HD, rows)
    return call(
        stack_kernel,
        "stack",
        at,
        (1,),
        [fixed((rows, 1))] + [fixed((HD, rows))] * GROUP,
        fixed(shape),
        like(shape, BF),
        (pos_col, *heads),
        scratch=[pltpu.VMEM(shape, BF)],
    )


def unsplit_kernel(at_ref, pos_ref, *refs):
    ins, outs = refs[:4], refs[4:]
    quarter, rows = ins[0].shape[1], pos_ref.shape[1]
    sub = lax.broadcasted_iota(jnp.int32, (quarter, rows), 0)
    total = 0.0
    for r in range(4):
        total = total + mm(ins[r][...], one_hot(sub + r * quarter, pos_ref[...]))
    total = total.astype(BF)
    for s in range(GROUP):
        for t in range(GROUP):

            @pl.when((at_ref[0] ^ s) == t)
            def _():
                outs[s][...] = total[t * HD : (t + 1) * HD, :]


def unsplit(at, pos_row, pieces):
    shape = (HD, 4 * pieces[0].shape[1])
    return call(
        unsplit_kernel,
        "unsplit",
        at,
        (1,),
        [fixed(pos_row.shape)] + [fixed(pieces[0].shape)] * 4,
        [fixed(shape)] * GROUP,
        [like(shape, BF)] * GROUP,
        (pos_row, *pieces),
    )


def heads_of(mine, r, features):
    return pl.ds(pl.multiple_of(((mine + 4 - r) % 4) * features, features), features)


def mid_kernel(at_ref, *refs):
    pieces, (w_ref, x_ref, gain_ref, bias_ref, h_ref, b_ref) = refs[:6], refs[6:]
    h = x_ref[...].astype(F32)
    for r, piece in enumerate(in_order(at_ref[1], *[ref[...] for ref in pieces])):
        rows = heads_of(at_ref[1], 4 - r, piece.shape[0])
        h = h + mm(turned(piece), w_ref[rows, :])

    @pl.when(pl.program_id(0) == 0)
    def _():
        h_ref[...] = h

    normal, _ = normalize(h)
    b_ref[...] = (normal * gain_ref[...] + bias_ref[...]).astype(BF)


def mid(at, pieces, w_o, tokens, gain, bias):
    features, rows = pieces[0].shape
    width, quarter = tokens.shape[1], rows // 4
    return call(
        mid_kernel,
        "mid",
        at,
        (4,),
        [pl.BlockSpec((features, quarter), lambda q, n: (0, (n[1] + q) % 4))] * 6
        + [fixed(w_o.shape)]
        + [pl.BlockSpec((quarter, width), lambda q, n: (q, 0))]
        + [fixed((1, width))] * 2,
        [fixed((quarter, width)), pl.BlockSpec((quarter, width), lambda q, n: (q, 0))],
        [like((quarter, width), F32), like((rows, width), BF)],
        (*pieces, w_o, tokens, gain, bias),
    )


def add_up(refs):
    total = refs[0][...]
    for ref in refs[1:]:
        total = total + ref[...].astype(F32)
    return total


def mid_back_kernel(at_ref, db_ref, *refs):
    dests, backs, refs = refs[:2], refs[2:4], refs[4:]
    w_ref, h_ref, dy_ref, gain_ref, dh_ref, low_ref, sums_ref = refs[:7]
    do_refs = refs[7:]
    db = db_ref[...].astype(F32)
    for dest_ref, back_ref in zip(dests, backs):
        shape = (dest_ref.shape[0], back_ref.shape[0])
        lane = lax.broadcasted_iota(jnp.int32, shape, 1)
        db = db + mm(one_hot(lane, dest_ref[...]), back_ref[...])
    normal, scale = normalize(h_ref[...])
    dh = dy_ref[...].astype(F32) + norm_back(db, gain_ref[...], normal, scale)
    dh_ref[...] = dh
    low = dh.astype(BF)
    low_ref[...] = low
    sums_ref[0:1, :] = jnp.sum(db * normal, axis=0, keepdims=True)
    sums_ref[1:2, :] = jnp.sum(db, axis=0, keepdims=True)
    for r in range(4):
        rows = heads_of(at_ref[1], r, do_refs[r].shape[0])
        do_refs[r][...] = mm_t(w_ref[rows, :], low).astype(BF)


def mid_back(at, db, dests, backs, w_o, h, dy, gain):
    quarter, width = h.shape
    whole = fixed((quarter, width))
    piece = (w_o.shape[0] // 4, quarter)
    return call(
        mid_back_kernel,
        "mid_back",
        at,
        (1,),
        [whole]
        + [fixed((quarter, 1))] * 2
        + [fixed(backs[0].shape)] * 2
        + [fixed(w_o.shape), whole, whole, fixed((1, width))],
        [whole] * 2 + [fixed((2, width))] + [fixed(piece)] * 4,
        [like((quarter, width), F32), like((quarter, width), BF), like((2, width), F32)]
        + [like(piece, BF)] * 4,
        (db, *dests, *backs, w_o, h, dy, gain),
    )


def first_back_kernel(at_ref, *refs):
    shares = refs[:4]
    x_ref, dh_ref, gain_ref, out_ref = refs[4:]
    normal, scale = normalize(x_ref[...].astype(F32))
    out_ref[...] = (dh_ref[...] + norm_back(add_up(shares), gain_ref[...], normal, scale)).astype(BF)


def first_back(at, shares, x, dh, gain):
    quarter, width = dh.shape
    whole = fixed((quarter, width))
    return call(
        first_back_kernel,
        "first_back",
        at,
        (1,),
        [whole] * 6 + [fixed((1, width))],
        whole,
        like((quarter, width), BF),
        (*shares, x, dh, gain),
    )


def in_order(mine, own, right, left, far, right_two, left_two):
    one = jnp.where(mine == 3, far, left)
    two = jnp.where(mine < 2, left_two, right_two)
    three = jnp.where(mine == 0, far, right)
    return own, one, two, three


def one_hot(slots, dest):
    return jnp.where(slots == dest, 1.0, 0.0).astype(BF)


def dispatch_kernel(at_ref, dest_ref, rows_ref, out_ref, spread_s):
    blk, rows = min(256, spread_s.shape[0]), dest_ref.shape[1]

    @pl.when(pl.program_id(0) == 0)
    def _():
        slot = lax.broadcasted_iota(jnp.int32, (blk, rows), 0)
        for start in range(0, spread_s.shape[0], blk):
            spread_s[start : start + blk, :] = one_hot(slot + start, dest_ref[...])

    out_ref[...] = mm(spread_s[...], rows_ref[...]).astype(BF)


def columns(rows, width):
    return pl.BlockSpec((rows, width), lambda i, n: (0, i))


def dispatch(at, dest_row, values, slots):
    rows, width = values.shape
    blk = min(256, width)
    return call(
        dispatch_kernel,
        "dispatch",
        at,
        (width // blk,),
        [fixed((1, rows)), columns(rows, blk)],
        columns(slots, blk),
        like((slots, width), BF),
        (dest_row, values),
        scratch=[pltpu.VMEM((slots, rows), BF)],
    )


def restore_kernel(at_ref, pos_ref, *refs):
    pieces, (out_ref, turn_s) = refs[:-2], refs[-2:]
    rows = turn_s.shape[0]
    blk = min(256, rows)

    @pl.when(pl.program_id(0) == 0)
    def _():
        lane = lax.broadcasted_iota(jnp.int32, (blk, rows), 1)
        for start in range(0, rows, blk):
            turn_s[start : start + blk, :] = one_hot(lane, pos_ref[start : start + blk, :])

    pieces = [ref[...] for ref in pieces]
    if len(pieces) > 1:
        pieces = in_order(at_ref[1], *pieces)
    total, start = 0.0, 0
    for piece in pieces:
        total = total + mm(turn_s[:, start : start + piece.shape[0]], piece)
        start += piece.shape[0]
    out_ref[...] = total.astype(BF)


def restore(at, pos_col, pieces):
    rows, width = pos_col.shape[0], pieces[0].shape[1]
    blk = min(256, width)
    return call(
        restore_kernel,
        "restore",
        at,
        (width // blk,),
        [fixed((rows, 1))] + [columns(piece.shape[0], blk) for piece in pieces],
        columns(rows, blk),
        like((rows, width), BF),
        (pos_col, *pieces),
        scratch=[pltpu.VMEM((rows, rows), BF)],
    )


def write_shares(mine, total, own_ref, one_ref, two_ref, three_ref, end_ref):
    rows = own_ref.shape[0]
    own_ref[...] = total[:rows]
    one, two, three = [total[r * rows : (r + 1) * rows].astype(BF) for r in (1, 2, 3)]
    one_ref[...] = one
    two_ref[...] = two
    three_ref[...] = three
    end_ref[...] = jnp.where(mine == 0, three, one)


def share_shapes(rows, width):
    return [like((rows, width), F32)] + [like((rows, width), BF)] * 4


def combine_kernel(count, whole, at_ref, *refs):
    dests, backs = refs[:count], refs[count : 2 * count]
    base_ref, refs, pick_s = refs[2 * count], refs[2 * count + 1 : -1], refs[-1]
    rows, slots = base_ref.shape[0], backs[0].shape[0]
    blk = rows // 4

    @pl.when(pl.program_id(0) == 0)
    def _():
        lane = lax.broadcasted_iota(jnp.int32, (blk, slots), 1)
        for k in range(count):
            for start in range(0, rows, blk):
                dest = dests[k][start : start + blk, :]
                pick_s[start : start + blk, k * slots : (k + 1) * slots] = one_hot(lane, dest)

    total = base_ref[...].astype(F32)
    for k in range(count):
        total = total + mm(pick_s[:, k * slots : (k + 1) * slots], backs[k][...])
    mine = at_ref[1]
    if whole:
        h_ref, out_ref = refs
        for r in range(4):
            part = total[r * blk : (r + 1) * blk]
            if r == 0:
                part = part + h_ref[...]
            place = pl.ds(pl.multiple_of(((mine + r) % 4) * blk, blk), blk)
            out_ref[place, :] = part.astype(BF)
    else:
        write_shares(mine, total, *refs)


def combine(at, dests, backs, base, h=None):
    count, (slots, width), rows = len(backs), backs[0].shape, base.shape[0]
    blk = min(256, width)
    whole = h is not None
    quarter = columns(rows // 4, blk)
    return call(
        partial(combine_kernel, count, whole),
        "combine",
        at,
        (width // blk,),
        [fixed((rows, 1))] * count
        + [columns(slots, blk)] * count
        + [columns(rows, blk)]
        + [quarter] * whole,
        columns(rows, blk) if whole else [quarter] * 5,
        like(base.shape, BF) if whole else share_shapes(rows // 4, width),
        (*dests, *backs, base) + ((h,) if whole else ()),
        scratch=[pltpu.VMEM((rows, count * slots), BF)],
    )


def mm_t(a, b):
    return lax.dot_general(a, b, (((1,), (1,)), ((), ())), preferred_element_type=F32)


def gelu_both(u):
    c = 0.7978845608028654
    square = u * u
    t = jnp.tanh(u * (c + (c * 0.044715) * square))
    half = 0.5 + 0.5 * t
    slope = half + (0.5 * u) * (1.0 - t * t) * (c + (3.0 * c * 0.044715) * square)
    return u * half, slope


def high_low(value):
    high = value.astype(BF)
    return high, (value - high.astype(F32)).astype(BF)


def two_coefs(logits, lane, experts):
    inside = (lane >= experts) & (lane < experts + 2)
    top = jnp.max(jnp.where(inside, logits, HIDE), axis=1, keepdims=True)
    e = jnp.where(inside, jnp.exp(logits - top), 0.0)
    e = e / jnp.sum(e, axis=1, keepdims=True)
    first = jnp.sum(jnp.where(lane == experts, e, 0.0), axis=1, keepdims=True)
    second = jnp.sum(jnp.where(lane == experts + 1, e, 0.0), axis=1, keepdims=True)
    return first, second


def small_back(d_small, rows, w_small_ref, small_ref, i):
    high, low = high_low(d_small)
    w_small = w_small_ref[...]
    high_t, low_t = high_low(d_small.T)

    @pl.when(i == 0)
    def _():
        small_ref[...] = jnp.zeros(small_ref.shape, F32)

    small_ref[...] += mm(high_t, rows) + mm(low_t, rows)
    return mm_t(high, w_small) + mm_t(low, w_small)


def expert_kernel(experts, half, at_ref, rows_ref, dy_ref, up_ref, down_ref, w_small_ref, *outs):
    if half:
        outs = outs[4:]
    rows_out_ref, hid_ref, dy_out_ref, deu_ref, y_ref, small_ref = outs[:6]
    own_ref, one_ref, two_ref, three_ref, end_ref = outs[6:]
    i, mine = pl.program_id(0), at_ref[1]
    rows = rows_ref[...].reshape(rows_out_ref.shape)
    rows_out_ref[...] = rows
    up = mm(rows, up_ref[...])
    logits = mm(rows, w_small_ref[...])
    lane = lax.broadcasted_iota(jnp.int32, logits.shape, 1)
    routed = lane < experts
    top = jnp.max(jnp.where(routed, logits, HIDE), axis=1, keepdims=True)
    probs = jnp.where(routed, jnp.exp(logits - top), 0.0)
    probs = probs / jnp.sum(probs, axis=1, keepdims=True)
    own = jnp.where(lane == at_ref[2], 1.0, 0.0)
    gate = jnp.sum(probs * own, axis=1, keepdims=True)
    first, second = two_coefs(logits, lane, experts)
    weight = second * gate
    dy = dy_ref[...].reshape(rows.shape).astype(F32)
    d_y = (weight * dy).astype(BF)
    dy_out_ref[...] = d_y
    d_hidden = mm_t(d_y, down_ref[...])
    hidden, slope = gelu_both(up)
    hidden = hidden.astype(BF)
    hid_ref[...] = hidden
    d_up = (d_hidden * slope).astype(BF)
    deu_ref[...] = d_up
    y = mm(hidden, down_ref[...])
    y_ref[...] = (weight * y).astype(BF).reshape(y_ref.shape)
    along = gate * jnp.sum(dy * y, axis=1, keepdims=True)
    mixed = first * second * along
    d_small = (second * along) * (own - probs)
    d_small = jnp.where(routed, d_small, 0.0)
    d_small = d_small + jnp.where(lane == experts + 1, mixed, 0.0)
    d_small = d_small - jnp.where(lane == experts, mixed, 0.0)
    d_rows = mm_t(d_up, up_ref[...]) + small_back(d_small, rows, w_small_ref, small_ref, i)
    low = d_rows.astype(BF)

    @pl.when(i == 0)
    def _():
        own_ref[...] = d_rows

    for r, ref in ((1, one_ref), (2, two_ref), (3, three_ref)):

        @pl.when(i == r)
        def _():
            ref[...] = low

    @pl.when(i == jnp.where(mine == 0, 3, 1))
    def _():
        end_ref[...] = low


def expert_rows(at, rows, dy, w_up, w_down, w_small, experts, half, before):
    devices, _, capacity, width = rows.shape
    hid, lanes = w_up.shape[1], w_small.shape[1]
    blk = devices * capacity
    slots = pl.BlockSpec((devices, 1, capacity, width), lambda i, n: (0, i, 0, 0))
    kept = [pl.BlockSpec((blk, size), lambda i, n: (i + half * 4, 0)) for size in (width, hid, width, hid)]
    return call(
        partial(expert_kernel, experts, half),
        "expert_rows",
        at,
        (4,),
        [
            slots,
            pl.BlockSpec((devices, 1, 1, capacity, width), lambda i, n: (0, half, i, 0, 0)),
            fixed((width, hid)),
            fixed((hid, width)),
            fixed((width, lanes)),
        ]
        + [pl.BlockSpec(memory_space=pl.ANY)] * (4 * half),
        kept + [slots, fixed((lanes, width))] + [fixed((blk, width))] * 5,
        [like((8 * blk, size), BF) for size in (width, hid, width, hid)]
        + [like(rows.shape, BF), like((lanes, width), F32)]
        + share_shapes(blk, width),
        (rows, dy, w_up, w_down, w_small, *before),
        alias={6 + k: k for k in range(4)} if half else None,
        vmem=56,
    )


def dense_kernel(experts, at_ref, rows_ref, dy_ref, in_ref, out_ref, w_small_ref, *outs):
    hid_ref, grad_ref, d_up_ref, mix_ref, db_ref, small_ref = outs
    rows = rows_ref[...]
    up = mm(rows, in_ref[...])
    logits = mm(rows, w_small_ref[...])
    lane = lax.broadcasted_iota(jnp.int32, logits.shape, 1)
    first, second = two_coefs(logits, lane, experts)
    dy = dy_ref[...].astype(F32)
    grad = (first * dy).astype(BF)
    grad_ref[...] = grad
    d_hidden = mm_t(grad, out_ref[...])
    hidden, slope = gelu_both(up)
    hidden = hidden.astype(BF)
    hid_ref[...] = hidden
    d_up = (d_hidden * slope).astype(BF)
    d_up_ref[...] = d_up
    dense = mm(hidden, out_ref[...])
    mix_ref[...] = first * dense
    mixed = first * second * jnp.sum(dy * dense, axis=1, keepdims=True)
    d_small = jnp.where(lane == experts, mixed, 0.0) - jnp.where(lane == experts + 1, mixed, 0.0)
    db = mm_t(d_up, in_ref[...]) + small_back(d_small, rows, w_small_ref, small_ref, pl.program_id(0))
    db_ref[...] = db.astype(BF)


def dense_rows(at, rows, dy, w_in, w_out, w_small, experts):
    (count, width), hid, lanes = rows.shape, w_in.shape[1], w_small.shape[1]
    blk = count // 4
    row_out = pl.BlockSpec((blk, width), lambda i, n: (i, 0))
    hid_out = pl.BlockSpec((blk, hid), lambda i, n: (i, 0))
    return call(
        partial(dense_kernel, experts),
        "dense_rows",
        at,
        (count // blk,),
        [row_out, row_out, fixed((width, hid)), fixed((hid, width)), fixed((width, lanes))],
        [hid_out, row_out, hid_out, row_out]
        + [pl.BlockSpec((blk, width), lambda i, n: ((n[1] + i) % 4, 0)), fixed((lanes, width))],
        [
            like((count, hid), BF),
            like((count, width), BF),
            like((count, hid), BF),
            like((count, width), F32),
            like((count, width), BF),
            like((lanes, width), F32),
        ],
        (rows, dy, w_in, w_out, w_small),
        vmem=56,
    )


def turned(value):
    return value.astype(F32).T.astype(BF)


def dense_grads_kernel(at_ref, b_ref, d_up_ref, grad_ref, hid_ref, keep_ref, give_ref):
    width = d_up_ref.shape[1]
    first = mm(turned(b_ref[...]), d_up_ref[...]).astype(BF)
    second = mm(turned(grad_ref[...]), hid_ref[...]).astype(BF)
    half = pl.num_programs(0) // 2
    for side, ref in ((0, keep_ref), (1, give_ref)):

        @pl.when(pl.program_id(0) // half == side)
        def _():
            ref[0, :, :width] = first
            ref[0, :, width:] = second


def dense_grads(at, b, d_up, grad, hidden, parts):
    (rows, width), hid = b.shape, hidden.shape[1]
    own, half, bits = width // parts, parts // 2, parts.bit_length() - 1

    def part(q, n):
        turned_q = sum([((q // 2**k) % 2) * 2 ** (bits - 1 - k) for k in range(bits)])
        return turned_q ^ n[2]

    column = pl.BlockSpec((rows, own), lambda q, n: (0, part(q, n)))
    shape = (1, own, 2 * hid)
    return call(
        dense_grads_kernel,
        "dense_grads",
        at,
        (parts,),
        [column, fixed((rows, hid)), column, fixed((rows, hid))],
        [
            pl.BlockSpec(shape, lambda q, n: (jnp.minimum(q, half - 1), 0, 0)),
            pl.BlockSpec(shape, lambda q, n: (jnp.maximum(q - half, 0), 0, 0)),
        ],
        [like((half, own, 2 * hid), BF)] * 2,
        (b, d_up, grad, hidden),
    )


def attention_grads_kernel(experts, at_ref, *refs):
    grads, o_refs, refs = refs[:GROUP], refs[GROUP : GROUP + 6], refs[GROUP + 6 :]
    a_ref, dh_ref, w_ref, gain_ref, bias_ref, sums_ref = refs[:6]
    small_refs, (out_ref, all_s) = refs[6:-2], refs[-2:]
    heads, features = GROUP * HD, grads[1].shape[0]
    products, plain = 0.0, 0.0
    for k in range(GROUP):
        head = at_ref[0] ^ k
        rows = pl.ds(pl.multiple_of(head * features, features), features)
        grad = grads[k][...]
        weight = w_ref[head].astype(F32)
        total = mm(grad, a_ref[...])
        all_s[rows, :] = total
        each = jnp.sum(grad.astype(F32), axis=1, keepdims=True)
        products = products + jnp.sum(total * weight, axis=0, keepdims=True)
        plain = plain + jnp.sum(each * weight, axis=0, keepdims=True)
    first = GROUP * features
    for r, piece in enumerate(in_order(at_ref[1], *[ref[...] for ref in o_refs])):
        rows = pl.ds(pl.multiple_of(first + ((at_ref[1] + r) % 4) * heads, heads), heads)
        all_s[rows, :] = mm(piece, dh_ref[...])
    first += 4 * heads
    small = add_up(small_refs)
    row = lax.broadcasted_iota(jnp.int32, small.shape, 0)
    d_gain = (products - bias_ref[...] * plain) / gain_ref[...]
    for k, sums in enumerate((sums_ref[0:1, :], sums_ref[1:2, :], d_gain, plain)):
        small = jnp.where(row == experts + 2 + k, sums, small)
    all_s[first:, :] = small
    out_ref[...] = all_s[...].T.astype(BF)


def attention_grads(at, grads, o, a, dh, w_heads, gain, bias, sums, small, experts):
    rows, width = a.shape
    features, lanes = grads[0].shape[0], small[0].shape[0]
    piece = pl.BlockSpec((o[0].shape[0], dh.shape[0]), lambda i, n: (0, n[1]))
    height = GROUP * features + 4 * o[0].shape[0] + lanes
    blk = min(256, width)
    return call(
        partial(attention_grads_kernel, experts),
        "attention_grads",
        at,
        (width // blk,),
        [fixed((features, rows))] * GROUP
        + [piece] * 6
        + [columns(rows, blk), columns(dh.shape[0], blk)]
        + [pl.BlockSpec((GROUP, features, blk), lambda i, n: (0, 0, i))]
        + [columns(1, blk)] * 2
        + [columns(2, blk)]
        + [columns(lanes, blk)] * len(small),
        pl.BlockSpec((blk, height), lambda i, n: (i, 0)),
        like((width, height), BF),
        (*grads, *o, a, dh, w_heads, gain, bias, sums, *small),
        scratch=[pltpu.VMEM((height, blk), F32)],
    )


def project_kernel(at_ref, pos_ref, *refs):
    grads, w_ref, outs, turned_s = refs[:GROUP], refs[GROUP], refs[GROUP + 1 : -1], refs[-1]
    rows = turned_s.shape[1]

    @pl.when(pl.program_id(0) == 0)
    def _():
        lane = lax.broadcasted_iota(jnp.int32, (rows, rows), 1)
        turn = one_hot(lane, pos_ref[...])
        for s in range(GROUP):
            turned_s[s] = mm(grads[s][...], turn).T.astype(BF)

    total = 0.0
    for s in range(GROUP):
        total = total + mm(turned_s[s], w_ref[at_ref[0] ^ s])
    write_shares(at_ref[1], total, *outs)


def project_back(at, pos_col, grads, w_heads):
    features, rows = grads[0].shape
    width = w_heads.shape[2]
    blk = min(256, width)
    return call(
        project_kernel,
        "project_back",
        at,
        (width // blk,),
        [fixed((rows, 1))]
        + [fixed((features, rows))] * GROUP
        + [pl.BlockSpec((GROUP, features, blk), lambda i, n: (0, 0, i))],
        [columns(rows // 4, blk)] * 5,
        share_shapes(rows // 4, width),
        (pos_col, *grads, w_heads),
        scratch=[pltpu.VMEM((GROUP, rows, features), BF)],
    )


def hop(value, *pairs):
    return lax.ppermute(value, "mp", pairs)


def rotate(value, steps):
    return hop(value, *[(s, (s + steps) % 4) for s in range(4)])


def gather_near(own):
    right = hop(own, (0, 1), (1, 2), (2, 3))
    left = hop(own, (1, 0), (2, 1), (3, 2))
    return own, right, left, hop(own, (0, 3), (3, 0))


def gather_far(near):
    _, right, left, _ = near
    return *near, hop(right, (1, 2), (2, 3)), hop(left, (1, 0), (2, 1))


def gather_pieces(own):
    return gather_far(gather_near(own))


def scatter_far(shares):
    _, _, two, _, end = shares
    return hop(two, (2, 1), (3, 2)), hop(two, (0, 1), (1, 2)), hop(end, (0, 3), (3, 0))


def scatter_near(shares, came):
    own, one, _, three, _ = shares
    from_right, from_left, from_end = came
    three = (three.astype(F32) + from_right.astype(F32)).astype(BF)
    one = (one.astype(F32) + from_left.astype(F32)).astype(BF)
    return own, hop(three, (1, 0), (2, 1), (3, 2)), hop(one, (0, 1), (1, 2), (2, 3)), from_end


def group_swap(value, s):
    count = lax.axis_size("dp")
    return lax.ppermute(value, "dp", [(t, t ^ s) for t in range(count)])


def expert_swap(value, experts):
    wide = value.reshape(experts, value.shape[0] // experts, value.shape[1])
    return lax.all_to_all(wide, "dp", 0, 0, tiled=True).reshape(value.shape)


def add_halves(keep, came):
    return (keep.astype(F32) + came.astype(F32)).astype(BF)


def body(
    tokens,
    cotangent,
    ln_gains,
    ln_biases,
    w_qkv,
    w_o,
    w_in,
    w_out,
    w_router,
    w_coef,
    w_up,
    w_down,
    routes,
    long_group,
):
    rows, width = tokens.shape
    dps = lax.axis_size("dp")
    mine, position = lax.axis_index("mp"), lax.axis_index("dp")
    quarter = rows // 4
    heads_loc = w_qkv.shape[2] // HD
    hid = w_in.shape[1]
    experts = w_router.shape[1]
    capacity = max(2, 2 * rows // experts)
    each = capacity // 8
    barrier = lax.optimization_barrier
    first_len = lax.dynamic_index_in_dim(long_group, position // GROUP, 0, keepdims=False)
    at = jnp.stack([position % GROUP, mine, position, first_len]).astype(jnp.int32)
    gains = [ln_gains[0:1], ln_gains[1:2]]
    biases = [ln_biases[0:1], ln_biases[1:2]]
    w_o_all = lax.all_gather(w_o, "mp", axis=0, tiled=True)

    w_heads = w_qkv.reshape(width, 3, heads_loc, HD).transpose(2, 1, 3, 0)
    w_heads = w_heads.reshape(heads_loc, 3 * HD, width)
    a_r, *qkv = project(at, tokens, gains[0], biases[0], w_heads)
    qkv = [qkv[0]] + [group_swap(qkv[s], s) for s in (1, 2, 3)]

    route = routes[:, 0]
    picked = (route[:, None] == jnp.arange(experts, dtype=jnp.int32)[None, :]).astype(jnp.int32)
    before = jnp.cumsum(picked, axis=0) - picked
    counts = jnp.sum(picked, axis=0)
    ends = jnp.cumsum(counts)
    order = jnp.sum(before * picked, axis=1)
    rank = jnp.sum(picked * (ends - counts)[None, :], axis=1) + order

    def slot_of(expert, order, turn):
        deep = order // 4
        return deep // each, (expert * 4 + turn) * each + deep % each

    turn = (rank + 4 - mine) % 4
    pos, pos_mesh = turn * quarter + rank // 4, (rank % 4) * quarter + rank // 4
    pos_col, pos_row, mesh_col = pos[:, None], pos[None, :], pos_mesh[:, None]
    half, place = slot_of(route, order, turn)
    full = route * capacity + half * (4 * each) + place - route * (4 * each)
    send_dy = dispatch(at, full[None, :], cotangent, experts * capacity)
    line = jnp.arange(rows, dtype=jnp.int32)
    ranks = 4 * (line % quarter) + (line // quarter + mine) % 4
    past = (ranks[:, None] >= ends[None, :]).astype(jnp.int32)
    expert = jnp.sum(past, axis=1)
    order = ranks - jnp.sum(past * counts[None, :], axis=1)
    half, place = slot_of(expert, order, line // quarter)
    dests = [jnp.where(half == k, place, -1).astype(jnp.int32) for k in (0, 1)]
    own_slots = expert * each + (order // 4) % each
    own_dests = [jnp.where(half == k, own_slots, -1)[:quarter, None].astype(jnp.int32) for k in (0, 1)]
    *qkv, send_dy = barrier((*qkv, send_dy))

    *o_t, lse = attend(at, qkv)
    *o_t, w_o_all = barrier((*o_t, w_o_all))
    o_heads = [o_t[0]] + [group_swap(o_t[s], s) for s in (1, 2, 3)]
    lanes = -(-(experts + 2) // 128) * 128
    w_small = jnp.concatenate(
        [w_router, w_coef, jnp.zeros((width, lanes - experts - 2), BF)], axis=1
    )
    x_p = dispatch(at, pos_row, tokens, rows)
    dy_p = dispatch(at, pos_row, cotangent, rows)
    *o_heads, send_dy, w_small = barrier((*o_heads, send_dy, w_small))
    got_dy = expert_swap(send_dy, experts)
    near = gather_near(stack(at, mesh_col, o_heads))
    right, left, x_p, dy_p = barrier((near[1], near[2], x_p, dy_p))
    o_pieces = gather_far((near[0], right, left, near[3]))
    h, b_r = mid(at, o_pieces, w_o_all, x_p, gains[1], biases[1])

    def by_quarter(value, halves):
        value = value.reshape(experts, halves * 4, each, width)
        if each % 16:
            value = value.transpose(1, 0, 2, 3).reshape(1, halves * 4, experts * each, width)
        return value

    def by_device(value):
        if each % 16:
            value = value.reshape(4, experts, each, width).transpose(1, 0, 2, 3)
        return value.reshape(experts * 4 * each, width)

    send_0 = dispatch(at, dests[0][None, :], b_r, experts * 4 * each)
    send_0, got_dy = barrier((send_0, got_dy))
    got_0 = expert_swap(send_0, experts)
    send_1 = dispatch(at, dests[1][None, :], b_r, experts * 4 * each)
    b_r, send_1 = barrier((b_r, send_1))
    hidden, dense_grad, d_up, mix_base, db_dense, small_t = dense_rows(
        at, b_r, dy_p, w_in, w_out, w_small, experts
    )
    send_1, got_0, db_dense = barrier((send_1, got_0, db_dense))
    db_dense = lax.psum_scatter(db_dense, "mp", scatter_dimension=0, tiled=True)
    got_1 = expert_swap(send_1, experts)

    got_dy = by_quarter(got_dy, 2)
    got_dy = got_dy.reshape(got_dy.shape[0], 2, 4, *got_dy.shape[2:])
    *kept, y_0, small_0, s_0, s_1, s_2, s_3, s_4 = expert_rows(
        at, by_quarter(got_0, 1), got_dy, w_up[0], w_down[0], w_small, experts, 0, ()
    )
    shares_0 = (s_0, s_1, s_2, s_3, s_4)
    far_0 = scatter_far(shares_0)
    *kept, y_1, small_1, s_0, s_1, s_2, s_3, s_4 = expert_rows(
        at, by_quarter(got_1, 1), got_dy, w_up[0], w_down[0], w_small, experts, 1, kept
    )
    got, hidden_e, d_y, d_eu = kept
    tied = barrier((s_0, s_1, s_2, s_3, s_4, *far_0))
    shares_1, far_0 = tied[:5], tied[5:]
    far_1 = scatter_far(shares_1)

    def total(addends):
        return sum([part.astype(F32) for part in addends[1:]], addends[0]).astype(BF)

    tok_y = [expert_swap(by_device(y), experts) for y in (y_0, y_1)]
    own_0 = total(scatter_near(shares_0, far_0))
    own_0, t_0, t_1 = barrier((own_0, *tok_y))
    back_0 = expert_swap(own_0, experts)
    own_1 = total(scatter_near(shares_1, far_1))

    mix = combine(at, [dest[:, None] for dest in dests], [t_0, t_1], mix_base, h)
    own_1, mix = barrier((own_1, mix))
    output = lax.psum(mix, "mp")
    back_1 = expert_swap(own_1, experts)
    halving = width == dps * 128
    if halving:
        grads = dense_grads(at, b_r, d_up, dense_grad, hidden, dps)
    else:
        grads = [ein("td,tf->df", b_r, d_up).astype(BF), ein("td,tf->df", dense_grad, hidden).astype(BF)]
    back_0, back_1, *grads = barrier((back_0, back_1, *grads))
    dh, dh_r, sums_2, *do_q = mid_back(
        at, db_dense, own_dests, [back_0, back_1], w_o_all, h, dy_p[:quarter], gains[1]
    )
    do_q = [do_q[0]] + [rotate(do_q[r], -r) for r in (1, 2, 3)]
    do_heads = unsplit(at, pos_row, do_q)
    do_t = [do_heads[0]] + [group_swap(do_heads[s], s) for s in (1, 2, 3)]
    if halving:
        came_1 = group_swap(grads[1], 1)
        rest = dps // 4
        give = add_halves(grads[0][rest:], came_1[rest:])
        *do_t, give = barrier((*do_t, give))
        came_2 = group_swap(give, 2)
    d_qkv = attend_back(at, qkv, do_t, o_t, lse)
    if halving:
        keep = add_halves(grads[0][:rest], came_1[:rest])
        *d_qkv, came_2, keep = barrier((*d_qkv, came_2, keep))
        grads = add_halves(keep, came_2)
        bit = 4
        while bit < dps:
            rest = grads.shape[0] // 2
            grads = add_halves(grads[:rest], group_swap(grads[rest:], bit))
            bit *= 2
        grads = [grads[0][:, :hid], grads[0][:, hid:]]
    else:
        grads = [lax.psum_scatter(grad, "dp", scatter_dimension=0, tiled=True) for grad in grads]

    d_own, got, hidden_e, d_y, d_eu = barrier((d_qkv[0], got, hidden_e, d_y, d_eu))
    d_qkv = [d_own] + [group_swap(d_qkv[s], s) for s in (1, 2, 3)]
    grad_down = ein("rf,rd->fd", hidden_e, d_y)
    *d_qkv, grad_down = barrier((*d_qkv, grad_down))
    grads_a = attention_grads(
        at, d_qkv, o_pieces, a_r, dh_r, w_heads, gains[0], biases[0], sums_2, (small_0, small_1, small_t), experts
    )
    *d_qkv, grads_a = barrier((*d_qkv, grads_a))
    shares = project_back(at, pos_col, d_qkv, w_heads)
    far = scatter_far(shares)
    grads_a, output = barrier((grads_a, output))
    grads_a = lax.psum_scatter(grads_a, "dp", scatter_dimension=0, tiled=True).T
    output = restore(at, mesh_col, [output])
    grad_up = ein("rd,rf->df", got, d_eu)
    *far, grad_up, output = barrier((*far, grad_up, output))
    shares = scatter_near(shares, far)
    grad_q = first_back(at, shares, x_p[:quarter], dh, gains[0])
    grad_tokens = restore(at, pos_col, gather_pieces(grad_q))

    own, heads = width // dps, heads_loc * HD
    grad_qkv = grads_a[: 3 * heads].astype(F32).reshape(heads_loc, 3, HD, own).transpose(3, 1, 0, 2)
    grad_qkv = grad_qkv.reshape(own, 3, heads)
    grad_in = grads[0].astype(F32)
    grad_out = grads[1].astype(F32).T
    rest = grads_a[3 * heads : 7 * heads].reshape(4, heads, own)
    small = jnp.broadcast_to(grads_a[7 * heads :], (4, lanes, own))
    rest = lax.all_to_all(jnp.concatenate([rest, small], axis=1), "mp", 0, 0, tiled=True)
    rest = jnp.sum(rest.astype(F32), axis=0)
    grad_o, small = rest[:heads], rest[heads:]
    small_out = small[: experts + 2].T
    return (
        output,
        grad_tokens,
        jnp.stack([small[experts + 4], small[experts + 2]]),
        jnp.stack([small[experts + 5], small[experts + 3]]),
        grad_qkv,
        grad_o,
        grad_in,
        grad_out,
        small_out[:, :experts],
        small_out[:, experts:],
        grad_up[None],
        grad_down[None],
    )


def solution(mesh):
    in_specs = (
        P("dp", None),
        P("dp", None),
        P(),
        P(),
        P(None, None, "mp"),
        P("mp", None),
        P(None, "mp"),
        P("mp", None),
        P(),
        P(),
        P("dp", None, "mp"),
        P("dp", "mp", None),
        P("dp", None),
        P(),
    )
    out_specs = (
        P("dp", None),
        P("dp", None),
        P(None, "dp"),
        P(None, "dp"),
        P("dp", None, "mp"),
        P("mp", "dp"),
        P("dp", "mp"),
        P("mp", "dp"),
        P("dp", None),
        P("dp", None),
        P("dp", None, "mp"),
        P("dp", "mp", None),
    )
    return jax.shard_map(body, mesh=mesh, in_specs=in_specs, out_specs=out_specs, check_vma=False)
```

```python
from functools import partial

import jax
import jax.numpy as jnp
from jax import lax
from jax.experimental import pallas as pl
from jax.experimental.pallas import tpu as pltpu
from jax.sharding import PartitionSpec as P

HD = 64
GROUP = 4
EPS = 1e-05
LOG2E = 1.4426950408889634
SCALE2 = 0.125 * LOG2E
HIDE = -1e30
BF = jnp.bfloat16
F32 = jnp.float32
LIGHT = pl.CostEstimate(flops=1 << 20, bytes_accessed=1 << 20, transcendentals=0)


def mm(a, b):
    return jnp.dot(a, b, preferred_element_type=F32)


def ein(spec, a, b):
    return jnp.einsum(spec, a, b, preferred_element_type=F32)


def call(kernel, name, prefetch, grid, in_specs, out_specs, out_shape, args, scratch=(), alias=None, vmem=48):
    return pl.pallas_call(
        kernel,
        grid_spec=pltpu.PrefetchScalarGridSpec(
            num_scalar_prefetch=1,
            grid=grid,
            in_specs=in_specs,
            out_specs=out_specs,
            scratch_shapes=list(scratch),
        ),
        out_shape=out_shape,
        input_output_aliases=alias or {},
        compiler_params=pltpu.CompilerParams(vmem_limit_bytes=vmem * 2**20),
        cost_estimate=LIGHT,
        name=name,
    )(prefetch, *args)


def fixed(shape):
    zeros = (0,) * len(shape)
    return pl.BlockSpec(shape, lambda *_: zeros)


def like(shape, dtype):
    return jax.ShapeDtypeStruct(shape, dtype)


def normalize(v):
    mean = jnp.mean(v, axis=-1, keepdims=True)
    centred = v - mean
    scale = lax.rsqrt(jnp.mean(centred * centred, axis=-1, keepdims=True) + EPS)
    return centred * scale, scale


def norm_back(grad, gain, normal, scale):
    g = grad * gain
    along = jnp.mean(g * normal, axis=-1, keepdims=True)
    return scale * (g - jnp.mean(g, axis=-1, keepdims=True) - normal * along)


def qkv_kernel(at_ref, x_ref, gain_ref, bias_ref, w_ref, a_ref, *outs):
    normal, _ = normalize(x_ref[...].astype(F32))
    a = (normal * gain_ref[...] + bias_ref[...]).astype(BF)
    a_ref[...] = a
    for s in range(GROUP):
        outs[s][...] = mm_t(w_ref[at_ref[0] ^ s], a).astype(BF)


def project(at, tokens, gain, bias, w_heads):
    rows, width = tokens.shape
    features = w_heads.shape[1]
    blk = min(256, rows)
    moving = pl.BlockSpec((blk, width), lambda i, n: (i, 0))
    return call(
        qkv_kernel,
        "project",
        at,
        (rows // blk,),
        [moving, fixed((1, width)), fixed((1, width)), fixed(w_heads.shape)],
        [moving] + [pl.BlockSpec((features, blk), lambda i, n: (0, i))] * GROUP,
        [like((rows, width), BF)] + [like((features, rows), BF)] * GROUP,
        (tokens, gain, bias, w_heads),
    )


def fill_keys(k_s, place, keys, first_len, blk):
    rows = place * blk + lax.broadcasted_iota(jnp.int32, (blk, 128), 0)
    lane = lax.broadcasted_iota(jnp.int32, (blk, 128), 1)
    wide = jnp.concatenate([keys.astype(F32).T, jnp.zeros((blk, 128 - HD), F32)], axis=1)
    wide = jnp.where((lane == HD) & (rows < first_len), HIDE, wide)
    k_s[pl.ds(place * blk, blk), :] = wide.astype(BF)


def wide_query(query, place, first_len, blk):
    cols = place * blk + lax.broadcasted_iota(jnp.int32, (128 - HD, blk), 1)
    sub = lax.broadcasted_iota(jnp.int32, (128 - HD, blk), 0)
    extra = jnp.where((sub == 0) & (cols >= first_len), 1.0, 0.0)
    return jnp.concatenate([query, extra.astype(BF)], axis=0)


def causal(blk):
    keys = lax.broadcasted_iota(jnp.int32, (blk, blk), 0)
    queries = lax.broadcasted_iota(jnp.int32, (blk, blk), 1)
    return keys <= queries


def attend_kernel(blk, per, at_ref, *refs):
    qkv_refs, o_refs = refs[:GROUP], refs[GROUP : 2 * GROUP]
    lse_ref, k_s, qkv_s = refs[2 * GROUP :]
    i = pl.program_id(0)
    place, first_len = at_ref[0], at_ref[3]

    @pl.when(i == 0)
    def _():
        for s in range(GROUP):
            qkv_s[place ^ s] = qkv_refs[s][...]

    def part(which, j):
        return qkv_s[j // per, HD * which : HD * (which + 1), pl.ds((j % per) * blk, blk)]

    fill_keys(k_s, i, part(1, i), first_len, blk)
    query = wide_query(part(0, i), i, first_len, blk)

    def scores(j):
        return mm(k_s[pl.ds(pl.multiple_of(j * blk, blk), blk), :], query)

    s = jnp.where(causal(blk), scores(i), HIDE)
    top = jnp.max(s, axis=0, keepdims=True)
    p = jnp.exp2((s - top) * SCALE2)
    total = jnp.sum(p, axis=0, keepdims=True)
    acc = mm(part(2, i), p.astype(BF))

    def steps(blocks, carry):
        top, total, acc = carry
        s = [scores(j) for j in blocks]
        new = top
        for one in s:
            new = jnp.maximum(new, jnp.max(one, axis=0, keepdims=True))
        keep = jnp.exp2((top - new) * SCALE2)
        total, acc = total * keep, acc * keep
        for j, one in zip(blocks, s):
            p = jnp.exp2((one - new) * SCALE2)
            total = total + jnp.sum(p, axis=0, keepdims=True)
            acc = acc + mm(part(2, j), p.astype(BF))
        return new, total, acc

    low = jnp.where(i * blk >= first_len, first_len // blk, 0)
    pairs = (i - low) // 2
    carry = lax.fori_loop(
        0, pairs, lambda t, c: steps([low + 2 * t, low + 2 * t + 1], c), (top, total, acc)
    )
    top, total, acc = lax.fori_loop(low + 2 * pairs, i, lambda j, c: steps([j], c), carry)
    out = (acc / total).astype(BF)
    for s in range(GROUP):

        @pl.when((i // per) ^ place == s)
        def _():
            o_refs[s][:, pl.ds((i % per) * blk, blk)] = out

    lse_ref[0] = top * SCALE2 + jnp.log2(total)


def attend(at, qkv):
    features, rows = qkv[0].shape
    blk = min(512, rows)
    per = rows // blk
    count = GROUP * per
    return call(
        partial(attend_kernel, blk, per),
        "attend",
        at,
        (count,),
        [fixed((features, rows))] * GROUP,
        [fixed((HD, rows))] * GROUP + [pl.BlockSpec((1, 1, blk), lambda i, n: (i, 0, 0))],
        [like((HD, rows), BF)] * GROUP + [like((count, 1, blk), F32)],
        qkv,
        scratch=[pltpu.VMEM((GROUP * rows, 128), BF), pltpu.VMEM((GROUP, features, rows), BF)],
    )


def back_kernel(blk, per, count, at_ref, *refs):
    qkv_refs, do_refs, o_refs = refs[:GROUP], refs[GROUP : 2 * GROUP], refs[2 * GROUP : 3 * GROUP]
    lse_ref, refs = refs[3 * GROUP], refs[3 * GROUP + 1 :]
    out_refs, refs = refs[:GROUP], refs[GROUP:]
    dq_ref, out_ref, k_s, kt_s, v_s, wide_s, dot_s, both_s, delta_s, acc_s = refs
    j = pl.program_id(0)
    place, first_len = at_ref[0], at_ref[3]

    @pl.when(j == 0)
    def _():
        dq_ref[...] = jnp.zeros(dq_ref.shape, F32)
        zero = jnp.zeros((blk, HD), F32)
        for s in range(GROUP):
            for sub in range(per):
                i = (place ^ s) * per + sub
                at = pl.ds(pl.multiple_of(i * blk, blk), blk)
                cut = slice(sub * blk, (sub + 1) * blk)
                query = qkv_refs[s][0:HD, cut]
                keys = qkv_refs[s][HD : 2 * HD, cut]
                grad = do_refs[s][:, cut]
                fill_keys(k_s, i, keys, first_len, blk)
                kt_s[:, at] = keys
                dot_s[:, at] = grad
                wide_s[:, at] = wide_query(query, i, first_len, blk)
                grad = grad.astype(F32)
                values = qkv_refs[s][2 * HD :, cut].astype(F32)
                v_s[at, :] = jnp.concatenate([values.T, zero], axis=1).astype(BF)
                both_s[0, at, :] = jnp.concatenate([grad.T, zero], axis=1).astype(BF)
                both_s[1, at, :] = jnp.concatenate([zero, query.astype(F32).T], axis=1).astype(BF)
                held = o_refs[s][:, cut].astype(F32)
                delta_s[i] = jnp.sum(held * grad, axis=0, keepdims=True)

    here = pl.ds(pl.multiple_of(j * blk, blk), blk)
    keys_t = kt_s[:, here]
    values = v_s[here, 0:HD]

    def pair(i, diagonal):
        at = pl.ds(pl.multiple_of(i * blk, blk), blk)
        s = mm(k_s[here, :], wide_s[:, at])
        p = jnp.exp2(s * SCALE2 - lse_ref[i])
        if diagonal:
            p = jnp.where(causal(blk), p, 0.0)
        dp = mm(values, dot_s[:, at])
        ds = (p * (dp - delta_s[i])).astype(BF)
        return mm(p.astype(BF), both_s[0, at, :]) + mm(ds, both_s[1, at, :]), mm(keys_t, ds)

    acc_s[...], dq = pair(j, True)
    dq_ref[:, here] += dq

    def step_two(t, carry):
        i = j + 1 + 2 * t
        (kv_0, dq_0), (kv_1, dq_1) = pair(i, False), pair(i + 1, False)
        acc_s[...] += kv_0 + kv_1
        at = pl.ds(pl.multiple_of(i * blk, blk), 2 * blk)
        dq_ref[:, at] += jnp.concatenate([dq_0, dq_1], axis=1)
        return carry

    def step(i, carry):
        kv, dq = pair(i, False)
        acc_s[...] += kv
        dq_ref[:, pl.ds(pl.multiple_of(i * blk, blk), blk)] += dq
        return carry

    high = jnp.where((j + 1) * blk <= first_len, (first_len + blk - 1) // blk, count)
    pairs = (high - j - 1) // 2
    lax.fori_loop(0, pairs, step_two, 0)
    lax.fori_loop(j + 1 + 2 * pairs, high, step, 0)
    both = acc_s[...].T
    out_ref[0:HD, :] = (dq_ref[:, here] * 0.125).astype(BF)
    out_ref[HD : 2 * HD, :] = (both[HD:, :] * 0.125).astype(BF)
    out_ref[2 * HD :, :] = both[:HD, :].astype(BF)
    for s in range(GROUP):

        @pl.when((j // per) ^ place == s)
        def _():
            out_refs[s][:, pl.ds(pl.multiple_of((j % per) * blk, blk), blk)] = out_ref[...]


def attend_back(at, qkv, do, o, lse):
    features, rows = qkv[0].shape
    blk = min(512, rows)
    per = rows // blk
    count = GROUP * per
    return call(
        partial(back_kernel, blk, per, count),
        "attend_back",
        at,
        (count,),
        [fixed((features, rows))] * GROUP
        + [fixed((HD, rows))] * (2 * GROUP)
        + [fixed((count, 1, blk))],
        [fixed((features, rows))] * GROUP,
        [like((features, rows), BF)] * GROUP,
        (*qkv, *do, *o, lse),
        scratch=[
            pltpu.VMEM((HD, GROUP * rows), F32),
            pltpu.VMEM((features, blk), BF),
            pltpu.VMEM((GROUP * rows, 128), BF),
            pltpu.VMEM((HD, GROUP * rows), BF),
            pltpu.VMEM((GROUP * rows, 128), BF),
            pltpu.VMEM((128, GROUP * rows), BF),
            pltpu.VMEM((HD, GROUP * rows), BF),
            pltpu.VMEM((2, GROUP * rows, 128), BF),
            pltpu.VMEM((count, 1, blk), F32),
            pltpu.VMEM((blk, 128), F32),
        ],
    )


def stack_kernel(at_ref, pos_ref, *refs):
    ins, out_ref, all_s = refs[:GROUP], refs[GROUP], refs[GROUP + 1]
    for s in range(GROUP):
        head = pl.ds(pl.multiple_of((at_ref[0] ^ s) * HD, HD), HD)
        all_s[head, :] = ins[s][...]
    rows = all_s.shape[1]
    lane = lax.broadcasted_iota(jnp.int32, (rows, rows), 1)
    out_ref[...] = mm(all_s[...], one_hot(lane, pos_ref[...])).astype(BF)


def stack(at, pos_col, heads):
    rows = heads[0].shape[1]
    shape = (GROUP * HD, rows)
    return call(
        stack_kernel,
        "stack",
        at,
        (1,),
        [fixed((rows, 1))] + [fixed((HD, rows))] * GROUP,
        fixed(shape),
        like(shape, BF),
        (pos_col, *heads),
        scratch=[pltpu.VMEM(shape, BF)],
    )


def unsplit_kernel(at_ref, pos_ref, *refs):
    ins, outs = refs[:4], refs[4:]
    quarter, rows = ins[0].shape[1], pos_ref.shape[1]
    sub = lax.broadcasted_iota(jnp.int32, (quarter, rows), 0)
    total = 0.0
    for r in range(4):
        total = total + mm(ins[r][...], one_hot(sub + r * quarter, pos_ref[...]))
    total = total.astype(BF)
    for s in range(GROUP):
        for t in range(GROUP):

            @pl.when((at_ref[0] ^ s) == t)
            def _():
                outs[s][...] = total[t * HD : (t + 1) * HD, :]


def unsplit(at, pos_row, pieces):
    shape = (HD, 4 * pieces[0].shape[1])
    return call(
        unsplit_kernel,
        "unsplit",
        at,
        (1,),
        [fixed(pos_row.shape)] + [fixed(pieces[0].shape)] * 4,
        [fixed(shape)] * GROUP,
        [like(shape, BF)] * GROUP,
        (pos_row, *pieces),
    )


def heads_of(mine, r, features):
    return pl.ds(pl.multiple_of(((mine + 4 - r) % 4) * features, features), features)


def mid_kernel(at_ref, *refs):
    pieces, (w_ref, x_ref, gain_ref, bias_ref, h_ref, b_ref) = refs[:6], refs[6:]
    h = x_ref[...].astype(F32)
    for r, piece in enumerate(in_order(at_ref[1], *[ref[...] for ref in pieces])):
        rows = heads_of(at_ref[1], 4 - r, piece.shape[0])
        h = h + mm(turned(piece), w_ref[rows, :])

    @pl.when(pl.program_id(0) == 0)
    def _():
        h_ref[...] = h

    normal, _ = normalize(h)
    b_ref[...] = (normal * gain_ref[...] + bias_ref[...]).astype(BF)


def mid(at, pieces, w_o, tokens, gain, bias):
    features, rows = pieces[0].shape
    width, quarter = tokens.shape[1], rows // 4
    return call(
        mid_kernel,
        "mid",
        at,
        (4,),
        [pl.BlockSpec((features, quarter), lambda q, n: (0, (n[1] + q) % 4))] * 6
        + [fixed(w_o.shape)]
        + [pl.BlockSpec((quarter, width), lambda q, n: (q, 0))]
        + [fixed((1, width))] * 2,
        [fixed((quarter, width)), pl.BlockSpec((quarter, width), lambda q, n: (q, 0))],
        [like((quarter, width), F32), like((rows, width), BF)],
        (*pieces, w_o, tokens, gain, bias),
    )


def add_up(refs):
    total = refs[0][...]
    for ref in refs[1:]:
        total = total + ref[...].astype(F32)
    return total


def mid_back_kernel(at_ref, *refs):
    addends, dests, backs, refs = refs[:4], refs[4:6], refs[6:8], refs[8:]
    w_ref, h_ref, dy_ref, gain_ref, dh_ref, low_ref, sums_ref = refs[:7]
    do_refs = refs[7:]
    db = add_up(addends)
    for dest_ref, back_ref in zip(dests, backs):
        shape = (dest_ref.shape[0], back_ref.shape[0])
        lane = lax.broadcasted_iota(jnp.int32, shape, 1)
        db = db + mm(one_hot(lane, dest_ref[...]), back_ref[...])
    normal, scale = normalize(h_ref[...])
    dh = dy_ref[...].astype(F32) + norm_back(db, gain_ref[...], normal, scale)
    dh_ref[...] = dh
    low = dh.astype(BF)
    low_ref[...] = low
    sums_ref[0:1, :] = jnp.sum(db * normal, axis=0, keepdims=True)
    sums_ref[1:2, :] = jnp.sum(db, axis=0, keepdims=True)
    for r in range(4):
        rows = heads_of(at_ref[1], r, do_refs[r].shape[0])
        do_refs[r][...] = mm_t(w_ref[rows, :], low).astype(BF)


def mid_back(at, addends, dests, backs, w_o, h, dy, gain):
    quarter, width = h.shape
    whole = fixed((quarter, width))
    piece = (w_o.shape[0] // 4, quarter)
    return call(
        mid_back_kernel,
        "mid_back",
        at,
        (1,),
        [whole] * 4
        + [fixed((quarter, 1))] * 2
        + [fixed(backs[0].shape)] * 2
        + [fixed(w_o.shape), whole, whole, fixed((1, width))],
        [whole] * 2 + [fixed((2, width))] + [fixed(piece)] * 4,
        [like((quarter, width), F32), like((quarter, width), BF), like((2, width), F32)]
        + [like(piece, BF)] * 4,
        (*addends, *dests, *backs, w_o, h, dy, gain),
    )


def first_back_kernel(at_ref, *refs):
    shares = refs[:4]
    x_ref, dh_ref, gain_ref, out_ref = refs[4:]
    normal, scale = normalize(x_ref[...].astype(F32))
    out_ref[...] = (dh_ref[...] + norm_back(add_up(shares), gain_ref[...], normal, scale)).astype(BF)


def first_back(at, shares, x, dh, gain):
    quarter, width = dh.shape
    whole = fixed((quarter, width))
    return call(
        first_back_kernel,
        "first_back",
        at,
        (1,),
        [whole] * 6 + [fixed((1, width))],
        whole,
        like((quarter, width), BF),
        (*shares, x, dh, gain),
    )


def in_order(mine, own, right, left, far, right_two, left_two):
    one = jnp.where(mine == 3, far, left)
    two = jnp.where(mine < 2, left_two, right_two)
    three = jnp.where(mine == 0, far, right)
    return own, one, two, three


def one_hot(slots, dest):
    return jnp.where(slots == dest, 1.0, 0.0).astype(BF)


def dispatch_kernel(at_ref, dest_ref, rows_ref, out_ref, spread_s):
    blk, rows = min(256, spread_s.shape[0]), dest_ref.shape[1]

    @pl.when(pl.program_id(0) == 0)
    def _():
        slot = lax.broadcasted_iota(jnp.int32, (blk, rows), 0)
        for start in range(0, spread_s.shape[0], blk):
            spread_s[start : start + blk, :] = one_hot(slot + start, dest_ref[...])

    out_ref[...] = mm(spread_s[...], rows_ref[...]).astype(BF)


def columns(rows, width):
    return pl.BlockSpec((rows, width), lambda i, n: (0, i))


def dispatch(at, dest_row, values, slots):
    rows, width = values.shape
    blk = min(256, width)
    return call(
        dispatch_kernel,
        "dispatch",
        at,
        (width // blk,),
        [fixed((1, rows)), columns(rows, blk)],
        columns(slots, blk),
        like((slots, width), BF),
        (dest_row, values),
        scratch=[pltpu.VMEM((slots, rows), BF)],
    )


def restore_kernel(at_ref, pos_ref, *refs):
    pieces, (out_ref, turn_s) = refs[:-2], refs[-2:]
    rows = turn_s.shape[0]
    blk = min(256, rows)

    @pl.when(pl.program_id(0) == 0)
    def _():
        lane = lax.broadcasted_iota(jnp.int32, (blk, rows), 1)
        for start in range(0, rows, blk):
            turn_s[start : start + blk, :] = one_hot(lane, pos_ref[start : start + blk, :])

    pieces = [ref[...] for ref in pieces]
    if len(pieces) > 1:
        pieces = in_order(at_ref[1], *pieces)
    total, start = 0.0, 0
    for piece in pieces:
        total = total + mm(turn_s[:, start : start + piece.shape[0]], piece)
        start += piece.shape[0]
    out_ref[...] = total.astype(BF)


def restore(at, pos_col, pieces):
    rows, width = pos_col.shape[0], pieces[0].shape[1]
    blk = min(256, width)
    return call(
        restore_kernel,
        "restore",
        at,
        (width // blk,),
        [fixed((rows, 1))] + [columns(piece.shape[0], blk) for piece in pieces],
        columns(rows, blk),
        like((rows, width), BF),
        (pos_col, *pieces),
        scratch=[pltpu.VMEM((rows, rows), BF)],
    )


def write_shares(mine, total, own_ref, one_ref, two_ref, three_ref, end_ref):
    rows = own_ref.shape[0]
    own_ref[...] = total[:rows]
    one, two, three = [total[r * rows : (r + 1) * rows].astype(BF) for r in (1, 2, 3)]
    one_ref[...] = one
    two_ref[...] = two
    three_ref[...] = three
    end_ref[...] = jnp.where(mine == 0, three, one)


def share_shapes(rows, width):
    return [like((rows, width), F32)] + [like((rows, width), BF)] * 4


def combine_kernel(count, whole, at_ref, *refs):
    dests, backs = refs[:count], refs[count : 2 * count]
    base_ref, refs, pick_s = refs[2 * count], refs[2 * count + 1 : -1], refs[-1]
    rows, slots = base_ref.shape[0], backs[0].shape[0]
    blk = rows // 4

    @pl.when(pl.program_id(0) == 0)
    def _():
        lane = lax.broadcasted_iota(jnp.int32, (blk, slots), 1)
        for k in range(count):
            for start in range(0, rows, blk):
                dest = dests[k][start : start + blk, :]
                pick_s[start : start + blk, k * slots : (k + 1) * slots] = one_hot(lane, dest)

    total = base_ref[...].astype(F32)
    for k in range(count):
        total = total + mm(pick_s[:, k * slots : (k + 1) * slots], backs[k][...])
    mine = at_ref[1]
    if whole:
        h_ref, out_ref = refs
        for r in range(4):
            part = total[r * blk : (r + 1) * blk]
            if r == 0:
                part = part + h_ref[...]
            place = pl.ds(pl.multiple_of(((mine + r) % 4) * blk, blk), blk)
            out_ref[place, :] = part.astype(BF)
    else:
        write_shares(mine, total, *refs)


def combine(at, dests, backs, base, h=None):
    count, (slots, width), rows = len(backs), backs[0].shape, base.shape[0]
    blk = min(256, width)
    whole = h is not None
    quarter = columns(rows // 4, blk)
    return call(
        partial(combine_kernel, count, whole),
        "combine",
        at,
        (width // blk,),
        [fixed((rows, 1))] * count
        + [columns(slots, blk)] * count
        + [columns(rows, blk)]
        + [quarter] * whole,
        columns(rows, blk) if whole else [quarter] * 5,
        like(base.shape, BF) if whole else share_shapes(rows // 4, width),
        (*dests, *backs, base) + ((h,) if whole else ()),
        scratch=[pltpu.VMEM((rows, count * slots), BF)],
    )


def mm_t(a, b):
    return lax.dot_general(a, b, (((1,), (1,)), ((), ())), preferred_element_type=F32)


def gelu_both(u):
    c = 0.7978845608028654
    square = u * u
    t = jnp.tanh(u * (c + (c * 0.044715) * square))
    half = 0.5 + 0.5 * t
    slope = half + (0.5 * u) * (1.0 - t * t) * (c + (3.0 * c * 0.044715) * square)
    return u * half, slope


def high_low(value):
    high = value.astype(BF)
    return high, (value - high.astype(F32)).astype(BF)


def two_coefs(logits, lane, experts):
    inside = (lane >= experts) & (lane < experts + 2)
    top = jnp.max(jnp.where(inside, logits, HIDE), axis=1, keepdims=True)
    e = jnp.where(inside, jnp.exp(logits - top), 0.0)
    e = e / jnp.sum(e, axis=1, keepdims=True)
    first = jnp.sum(jnp.where(lane == experts, e, 0.0), axis=1, keepdims=True)
    second = jnp.sum(jnp.where(lane == experts + 1, e, 0.0), axis=1, keepdims=True)
    return first, second


def small_back(d_small, rows, w_small_ref, small_ref, i):
    high, low = high_low(d_small)
    w_small = w_small_ref[...]
    high_t, low_t = high_low(d_small.T)

    @pl.when(i == 0)
    def _():
        small_ref[...] = jnp.zeros(small_ref.shape, F32)

    small_ref[...] += mm(high_t, rows) + mm(low_t, rows)
    return mm_t(high, w_small) + mm_t(low, w_small)


def write_share(r, mine, value, own_ref, one_ref, two_ref, three_ref, end_ref):
    low = value.astype(BF)

    @pl.when(r == 0)
    def _():
        own_ref[...] = value

    for k, ref in ((1, one_ref), (2, two_ref), (3, three_ref)):

        @pl.when(r == k)
        def _():
            ref[...] = low

    @pl.when(r == jnp.where(mine == 0, 3, 1))
    def _():
        end_ref[...] = low


def expert_kernel(experts, half, at_ref, rows_ref, dy_ref, up_ref, down_ref, w_small_ref, *outs):
    if half:
        outs = outs[4:]
    rows_out_ref, hid_ref, dy_out_ref, deu_ref, y_ref, small_ref = outs[:6]
    i, mine = pl.program_id(0), at_ref[1]
    rows = rows_ref[...].reshape(rows_out_ref.shape)
    rows_out_ref[...] = rows
    up = mm(rows, up_ref[...])
    logits = mm(rows, w_small_ref[...])
    lane = lax.broadcasted_iota(jnp.int32, logits.shape, 1)
    routed = lane < experts
    top = jnp.max(jnp.where(routed, logits, HIDE), axis=1, keepdims=True)
    probs = jnp.where(routed, jnp.exp(logits - top), 0.0)
    probs = probs / jnp.sum(probs, axis=1, keepdims=True)
    own = jnp.where(lane == at_ref[2], 1.0, 0.0)
    gate = jnp.sum(probs * own, axis=1, keepdims=True)
    first, second = two_coefs(logits, lane, experts)
    weight = second * gate
    dy = dy_ref[...].reshape(rows.shape).astype(F32)
    d_y = (weight * dy).astype(BF)
    dy_out_ref[...] = d_y
    d_hidden = mm_t(d_y, down_ref[...])
    hidden, slope = gelu_both(up)
    hidden = hidden.astype(BF)
    hid_ref[...] = hidden
    d_up = (d_hidden * slope).astype(BF)
    deu_ref[...] = d_up
    y = mm(hidden, down_ref[...])
    y_ref[...] = (weight * y).astype(BF).reshape(y_ref.shape)
    along = gate * jnp.sum(dy * y, axis=1, keepdims=True)
    mixed = first * second * along
    d_small = (second * along) * (own - probs)
    d_small = jnp.where(routed, d_small, 0.0)
    d_small = d_small + jnp.where(lane == experts + 1, mixed, 0.0)
    d_small = d_small - jnp.where(lane == experts, mixed, 0.0)
    d_rows = mm_t(d_up, up_ref[...]) + small_back(d_small, rows, w_small_ref, small_ref, i)
    write_share(i, mine, d_rows, *outs[6:])


def expert_rows(at, rows, dy, w_up, w_down, w_small, experts, half, before):
    devices, _, capacity, width = rows.shape
    hid, lanes = w_up.shape[1], w_small.shape[1]
    blk = devices * capacity
    slots = pl.BlockSpec((devices, 1, capacity, width), lambda i, n: (0, i, 0, 0))
    kept = [pl.BlockSpec((blk, size), lambda i, n: (i + half * 4, 0)) for size in (width, hid, width, hid)]
    return call(
        partial(expert_kernel, experts, half),
        "expert_rows",
        at,
        (4,),
        [
            slots,
            pl.BlockSpec((devices, 1, 1, capacity, width), lambda i, n: (0, half, i, 0, 0)),
            fixed((width, hid)),
            fixed((hid, width)),
            fixed((width, lanes)),
        ]
        + [pl.BlockSpec(memory_space=pl.ANY)] * (4 * half),
        kept + [slots, fixed((lanes, width))] + [fixed((blk, width))] * 5,
        [like((8 * blk, size), BF) for size in (width, hid, width, hid)]
        + [like(rows.shape, BF), like((lanes, width), F32)]
        + share_shapes(blk, width),
        (rows, dy, w_up, w_down, w_small, *before),
        alias={6 + k: k for k in range(4)} if half else None,
        vmem=56,
    )


def dense_kernel(experts, at_ref, rows_ref, dy_ref, in_ref, out_ref, w_small_ref, *outs):
    hid_ref, grad_ref, d_up_ref, mix_ref, small_ref = outs[:5]
    rows = rows_ref[...]
    up = mm(rows, in_ref[...])
    logits = mm(rows, w_small_ref[...])
    lane = lax.broadcasted_iota(jnp.int32, logits.shape, 1)
    first, second = two_coefs(logits, lane, experts)
    dy = dy_ref[...].astype(F32)
    grad = (first * dy).astype(BF)
    grad_ref[...] = grad
    d_hidden = mm_t(grad, out_ref[...])
    hidden, slope = gelu_both(up)
    hidden = hidden.astype(BF)
    hid_ref[...] = hidden
    d_up = (d_hidden * slope).astype(BF)
    d_up_ref[...] = d_up
    dense = mm(hidden, out_ref[...])
    mix_ref[...] = first * dense
    mixed = first * second * jnp.sum(dy * dense, axis=1, keepdims=True)
    d_small = jnp.where(lane == experts, mixed, 0.0) - jnp.where(lane == experts + 1, mixed, 0.0)
    db = mm_t(d_up, in_ref[...]) + small_back(d_small, rows, w_small_ref, small_ref, pl.program_id(0))
    write_share(pl.program_id(0), at_ref[1], db, *outs[5:])


def dense_rows(at, rows, dy, w_in, w_out, w_small, experts):
    (count, width), hid, lanes = rows.shape, w_in.shape[1], w_small.shape[1]
    blk = count // 4
    row_out = pl.BlockSpec((blk, width), lambda i, n: (i, 0))
    hid_out = pl.BlockSpec((blk, hid), lambda i, n: (i, 0))
    return call(
        partial(dense_kernel, experts),
        "dense_rows",
        at,
        (count // blk,),
        [row_out, row_out, fixed((width, hid)), fixed((hid, width)), fixed((width, lanes))],
        [hid_out, row_out, hid_out, row_out, fixed((lanes, width))] + [fixed((blk, width))] * 5,
        [
            like((count, hid), BF),
            like((count, width), BF),
            like((count, hid), BF),
            like((count, width), F32),
            like((lanes, width), F32),
        ]
        + share_shapes(blk, width),
        (rows, dy, w_in, w_out, w_small),
        vmem=56,
    )


def turned(value):
    return value.astype(F32).T.astype(BF)


def dense_grads_kernel(at_ref, b_ref, d_up_ref, grad_ref, hid_ref, keep_ref, give_ref):
    width = d_up_ref.shape[1]
    first = mm(turned(b_ref[...]), d_up_ref[...]).astype(BF)
    second = mm(turned(grad_ref[...]), hid_ref[...]).astype(BF)
    half = pl.num_programs(0) // 2
    for side, ref in ((0, keep_ref), (1, give_ref)):

        @pl.when(pl.program_id(0) // half == side)
        def _():
            ref[0, :, :width] = first
            ref[0, :, width:] = second


def dense_grads(at, b, d_up, grad, hidden, parts):
    (rows, width), hid = b.shape, hidden.shape[1]
    own, half, bits = width // parts, parts // 2, parts.bit_length() - 1

    def part(q, n):
        turned_q = sum([((q // 2**k) % 2) * 2 ** (bits - 1 - k) for k in range(bits)])
        return turned_q ^ n[2]

    column = pl.BlockSpec((rows, own), lambda q, n: (0, part(q, n)))
    shape = (1, own, 2 * hid)
    return call(
        dense_grads_kernel,
        "dense_grads",
        at,
        (parts,),
        [column, fixed((rows, hid)), column, fixed((rows, hid))],
        [
            pl.BlockSpec(shape, lambda q, n: (jnp.minimum(q, half - 1), 0, 0)),
            pl.BlockSpec(shape, lambda q, n: (jnp.maximum(q - half, 0), 0, 0)),
        ],
        [like((half, own, 2 * hid), BF)] * 2,
        (b, d_up, grad, hidden),
    )


def attention_grads_kernel(experts, at_ref, *refs):
    grads, o_refs, refs = refs[:GROUP], refs[GROUP : GROUP + 6], refs[GROUP + 6 :]
    a_ref, dh_ref, w_ref, gain_ref, bias_ref, sums_ref = refs[:6]
    small_refs, (out_ref, all_s) = refs[6:-2], refs[-2:]
    heads, features = GROUP * HD, grads[1].shape[0]
    products, plain = 0.0, 0.0
    for k in range(GROUP):
        head = at_ref[0] ^ k
        rows = pl.ds(pl.multiple_of(head * features, features), features)
        grad = grads[k][...]
        weight = w_ref[head].astype(F32)
        total = mm(grad, a_ref[...])
        all_s[rows, :] = total
        each = jnp.sum(grad.astype(F32), axis=1, keepdims=True)
        products = products + jnp.sum(total * weight, axis=0, keepdims=True)
        plain = plain + jnp.sum(each * weight, axis=0, keepdims=True)
    first = GROUP * features
    for r, piece in enumerate(in_order(at_ref[1], *[ref[...] for ref in o_refs])):
        rows = pl.ds(pl.multiple_of(first + ((at_ref[1] + r) % 4) * heads, heads), heads)
        all_s[rows, :] = mm(piece, dh_ref[...])
    first += 4 * heads
    small = add_up(small_refs)
    row = lax.broadcasted_iota(jnp.int32, small.shape, 0)
    d_gain = (products - bias_ref[...] * plain) / gain_ref[...]
    for k, sums in enumerate((sums_ref[0:1, :], sums_ref[1:2, :], d_gain, plain)):
        small = jnp.where(row == experts + 2 + k, sums, small)
    all_s[first:, :] = small
    out_ref[...] = all_s[...].T.astype(BF)


def attention_grads(at, grads, o, a, dh, w_heads, gain, bias, sums, small, experts):
    rows, width = a.shape
    features, lanes = grads[0].shape[0], small[0].shape[0]
    piece = pl.BlockSpec((o[0].shape[0], dh.shape[0]), lambda i, n: (0, n[1]))
    height = GROUP * features + 4 * o[0].shape[0] + lanes
    blk = min(256, width)
    return call(
        partial(attention_grads_kernel, experts),
        "attention_grads",
        at,
        (width // blk,),
        [fixed((features, rows))] * GROUP
        + [piece] * 6
        + [columns(rows, blk), columns(dh.shape[0], blk)]
        + [pl.BlockSpec((GROUP, features, blk), lambda i, n: (0, 0, i))]
        + [columns(1, blk)] * 2
        + [columns(2, blk)]
        + [columns(lanes, blk)] * len(small),
        pl.BlockSpec((blk, height), lambda i, n: (i, 0)),
        like((width, height), BF),
        (*grads, *o, a, dh, w_heads, gain, bias, sums, *small),
        scratch=[pltpu.VMEM((height, blk), F32)],
    )


def project_kernel(at_ref, pos_ref, *refs):
    grads, w_ref, outs, turned_s = refs[:GROUP], refs[GROUP], refs[GROUP + 1 : -1], refs[-1]
    rows = turned_s.shape[1]

    @pl.when(pl.program_id(0) == 0)
    def _():
        lane = lax.broadcasted_iota(jnp.int32, (rows, rows), 1)
        turn = one_hot(lane, pos_ref[...])
        for s in range(GROUP):
            turned_s[s] = mm(grads[s][...], turn).T.astype(BF)

    total = 0.0
    for s in range(GROUP):
        total = total + mm(turned_s[s], w_ref[at_ref[0] ^ s])
    write_shares(at_ref[1], total, *outs)


def project_back(at, pos_col, grads, w_heads):
    features, rows = grads[0].shape
    width = w_heads.shape[2]
    blk = min(256, width)
    return call(
        project_kernel,
        "project_back",
        at,
        (width // blk,),
        [fixed((rows, 1))]
        + [fixed((features, rows))] * GROUP
        + [pl.BlockSpec((GROUP, features, blk), lambda i, n: (0, 0, i))],
        [columns(rows // 4, blk)] * 5,
        share_shapes(rows // 4, width),
        (pos_col, *grads, w_heads),
        scratch=[pltpu.VMEM((GROUP, rows, features), BF)],
    )


def hop(value, *pairs):
    return lax.ppermute(value, "mp", pairs)


def rotate(value, steps):
    return hop(value, *[(s, (s + steps) % 4) for s in range(4)])


def gather_near(own):
    right = hop(own, (0, 1), (1, 2), (2, 3))
    left = hop(own, (1, 0), (2, 1), (3, 2))
    return own, right, left, hop(own, (0, 3), (3, 0))


def gather_far(near):
    _, right, left, _ = near
    return *near, hop(right, (1, 2), (2, 3)), hop(left, (1, 0), (2, 1))


def gather_pieces(own):
    return gather_far(gather_near(own))


def scatter_far(shares):
    _, _, two, _, end = shares
    return hop(two, (2, 1), (3, 2)), hop(two, (0, 1), (1, 2)), hop(end, (0, 3), (3, 0))


def scatter_near(shares, came):
    own, one, _, three, _ = shares
    from_right, from_left, from_end = came
    three = (three.astype(F32) + from_right.astype(F32)).astype(BF)
    one = (one.astype(F32) + from_left.astype(F32)).astype(BF)
    return own, hop(three, (1, 0), (2, 1), (3, 2)), hop(one, (0, 1), (1, 2), (2, 3)), from_end


def group_swap(value, s):
    count = lax.axis_size("dp")
    return lax.ppermute(value, "dp", [(t, t ^ s) for t in range(count)])


def expert_swap(value, experts):
    wide = value.reshape(experts, value.shape[0] // experts, value.shape[1])
    return lax.all_to_all(wide, "dp", 0, 0, tiled=True).reshape(value.shape)


def add_halves(keep, came):
    return (keep.astype(F32) + came.astype(F32)).astype(BF)


def body(
    tokens,
    cotangent,
    ln_gains,
    ln_biases,
    w_qkv,
    w_o,
    w_in,
    w_out,
    w_router,
    w_coef,
    w_up,
    w_down,
    routes,
    long_group,
):
    rows, width = tokens.shape
    dps = lax.axis_size("dp")
    mine, position = lax.axis_index("mp"), lax.axis_index("dp")
    quarter = rows // 4
    heads_loc = w_qkv.shape[2] // HD
    hid = w_in.shape[1]
    experts = w_router.shape[1]
    capacity = max(2, 2 * rows // experts)
    each = capacity // 8
    barrier = lax.optimization_barrier
    first_len = lax.dynamic_index_in_dim(long_group, position // GROUP, 0, keepdims=False)
    at = jnp.stack([position % GROUP, mine, position, first_len]).astype(jnp.int32)
    gains = [ln_gains[0:1], ln_gains[1:2]]
    biases = [ln_biases[0:1], ln_biases[1:2]]
    w_o_all = lax.all_gather(w_o, "mp", axis=0, tiled=True)

    w_heads = w_qkv.reshape(width, 3, heads_loc, HD).transpose(2, 1, 3, 0)
    w_heads = w_heads.reshape(heads_loc, 3 * HD, width)
    a_r, *qkv = project(at, tokens, gains[0], biases[0], w_heads)
    qkv = [qkv[0]] + [group_swap(qkv[s], s) for s in (1, 2, 3)]

    route = routes[:, 0]
    picked = (route[:, None] == jnp.arange(experts, dtype=jnp.int32)[None, :]).astype(jnp.int32)
    before = jnp.cumsum(picked, axis=0) - picked
    counts = jnp.sum(picked, axis=0)
    ends = jnp.cumsum(counts)
    order = jnp.sum(before * picked, axis=1)
    rank = jnp.sum(picked * (ends - counts)[None, :], axis=1) + order

    def slot_of(expert, order, turn):
        deep = order // 4
        return deep // each, (expert * 4 + turn) * each + deep % each

    turn = (rank + 4 - mine) % 4
    pos, pos_mesh = turn * quarter + rank // 4, (rank % 4) * quarter + rank // 4
    pos_col, pos_row, mesh_col = pos[:, None], pos[None, :], pos_mesh[:, None]
    half, place = slot_of(route, order, turn)
    full = route * capacity + half * (4 * each) + place - route * (4 * each)
    send_dy = dispatch(at, full[None, :], cotangent, experts * capacity)
    line = jnp.arange(rows, dtype=jnp.int32)
    ranks = 4 * (line % quarter) + (line // quarter + mine) % 4
    past = (ranks[:, None] >= ends[None, :]).astype(jnp.int32)
    expert = jnp.sum(past, axis=1)
    order = ranks - jnp.sum(past * counts[None, :], axis=1)
    half, place = slot_of(expert, order, line // quarter)
    dests = [jnp.where(half == k, place, -1).astype(jnp.int32) for k in (0, 1)]
    own_slots = expert * each + (order // 4) % each
    own_dests = [jnp.where(half == k, own_slots, -1)[:quarter, None].astype(jnp.int32) for k in (0, 1)]
    *qkv, send_dy = barrier((*qkv, send_dy))

    *o_t, lse = attend(at, qkv)
    *o_t, w_o_all = barrier((*o_t, w_o_all))
    o_heads = [o_t[0]] + [group_swap(o_t[s], s) for s in (1, 2, 3)]
    lanes = -(-(experts + 2) // 128) * 128
    w_small = jnp.concatenate(
        [w_router, w_coef, jnp.zeros((width, lanes - experts - 2), BF)], axis=1
    )
    x_p = dispatch(at, pos_row, tokens, rows)
    dy_p = dispatch(at, pos_row, cotangent, rows)
    *o_heads, send_dy, w_small = barrier((*o_heads, send_dy, w_small))
    got_dy = expert_swap(send_dy, experts)
    near = gather_near(stack(at, mesh_col, o_heads))
    dest_cols = [dest[:, None] for dest in dests]
    tied = barrier((near[1], near[2], x_p, dy_p, *dest_cols, *own_dests))
    right, left, x_p, dy_p, dest_cols, own_dests = *tied[:4], tied[4:6], tied[6:]
    o_pieces = gather_far((near[0], right, left, near[3]))
    h, b_r = mid(at, o_pieces, w_o_all, x_p, gains[1], biases[1])

    def by_quarter(value, halves):
        value = value.reshape(experts, halves * 4, each, width)
        if each % 16:
            value = value.transpose(1, 0, 2, 3).reshape(1, halves * 4, experts * each, width)
        return value

    def by_device(value):
        if each % 16:
            value = value.reshape(4, experts, each, width).transpose(1, 0, 2, 3)
        return value.reshape(experts * 4 * each, width)

    send_0 = dispatch(at, dests[0][None, :], b_r, experts * 4 * each)
    send_0, got_dy = barrier((send_0, got_dy))
    got_0 = expert_swap(send_0, experts)
    send_1 = dispatch(at, dests[1][None, :], b_r, experts * 4 * each)
    b_r, send_1 = barrier((b_r, send_1))
    hidden, dense_grad, d_up, mix_base, small_t, *dense = dense_rows(
        at, b_r, dy_p, w_in, w_out, w_small, experts
    )
    send_1, got_0, *dense = barrier((send_1, got_0, *dense))
    got_1 = expert_swap(send_1, experts)
    far_d = scatter_far(dense)

    got_dy = by_quarter(got_dy, 2)
    got_dy = got_dy.reshape(got_dy.shape[0], 2, 4, *got_dy.shape[2:])
    *kept, y_0, small_0, s_0, s_1, s_2, s_3, s_4 = expert_rows(
        at, by_quarter(got_0, 1), got_dy, w_up[0], w_down[0], w_small, experts, 0, ()
    )
    tied = barrier((y_0, s_0, s_1, s_2, s_3, s_4, *far_d))
    y_0, shares_0, far_d = tied[0], tied[1:6], tied[6:]
    tok_y0 = expert_swap(by_device(y_0), experts)
    far_0 = scatter_far(shares_0)
    dense = scatter_near(dense, far_d)
    *kept, y_1, small_1, s_0, s_1, s_2, s_3, s_4 = expert_rows(
        at, by_quarter(got_1, 1), got_dy, w_up[0], w_down[0], w_small, experts, 1, kept
    )
    got, hidden_e, d_y, d_eu = kept
    tied = barrier((y_1, s_0, s_1, s_2, s_3, s_4, *far_0, *dense))
    y_1, shares_1, far_0, dense = tied[0], tied[1:6], tied[6:9], tied[9:]
    far_1 = scatter_far(shares_1)

    def total(addends):
        return sum([part.astype(F32) for part in addends[1:]], addends[0]).astype(BF)

    own_0 = total(scatter_near(shares_0, far_0))
    tok_y1 = expert_swap(by_device(y_1), experts)
    halving = width == dps * 128
    if halving:
        grads = dense_grads(at, b_r, d_up, dense_grad, hidden, dps)
    else:
        grads = [ein("td,tf->df", b_r, d_up).astype(BF), ein("td,tf->df", dense_grad, hidden).astype(BF)]
    own_0, tok_y0, tok_y1, *grads = barrier((own_0, tok_y0, tok_y1, *grads))
    back_0 = expert_swap(own_0, experts)
    own_1 = total(scatter_near(shares_1, far_1))
    back_1 = expert_swap(own_1, experts)

    mix = combine(at, dest_cols, [tok_y0, tok_y1], mix_base, h)
    back_0, back_1, mix = barrier((back_0, back_1, mix))
    output = lax.psum(mix, "mp")
    dh, dh_r, sums_2, *do_q = mid_back(
        at, dense, own_dests, [back_0, back_1], w_o_all, h, dy_p, gains[1]
    )
    do_q = [do_q[0]] + [rotate(do_q[r], -r) for r in (1, 2, 3)]
    do_heads = unsplit(at, pos_row, do_q)
    do_t = [do_heads[0]] + [group_swap(do_heads[s], s) for s in (1, 2, 3)]
    if halving:
        came_1 = group_swap(grads[1], 1)
        rest = dps // 4
        give = add_halves(grads[0][rest:], came_1[rest:])
        *do_t, give = barrier((*do_t, give))
        came_2 = group_swap(give, 2)
    d_qkv = attend_back(at, qkv, do_t, o_t, lse)
    if halving:
        keep = add_halves(grads[0][:rest], came_1[:rest])
        *d_qkv, came_2, keep = barrier((*d_qkv, came_2, keep))
        grads = add_halves(keep, came_2)
        bit = 4
        while bit < dps:
            rest = grads.shape[0] // 2
            grads = add_halves(grads[:rest], group_swap(grads[rest:], bit))
            bit *= 2
        grads = [grads[0][:, :hid], grads[0][:, hid:]]
    else:
        grads = [lax.psum_scatter(grad, "dp", scatter_dimension=0, tiled=True) for grad in grads]

    d_own, got, hidden_e, d_y, d_eu = barrier((d_qkv[0], got, hidden_e, d_y, d_eu))
    d_qkv = [d_own] + [group_swap(d_qkv[s], s) for s in (1, 2, 3)]
    grad_down = ein("rf,rd->fd", hidden_e, d_y)
    *d_qkv, grad_down = barrier((*d_qkv, grad_down))
    grads_a = attention_grads(
        at, d_qkv, o_pieces, a_r, dh_r, w_heads, gains[0], biases[0], sums_2, (small_0, small_1, small_t), experts
    )
    *d_qkv, grads_a = barrier((*d_qkv, grads_a))
    shares = project_back(at, pos_col, d_qkv, w_heads)
    far = scatter_far(shares)
    grads_a, output = barrier((grads_a, output))
    grads_a = lax.psum_scatter(grads_a, "dp", scatter_dimension=0, tiled=True).T
    output = restore(at, mesh_col, [output])
    grad_up = ein("rd,rf->df", got, d_eu)
    *far, grad_up, output = barrier((*far, grad_up, output))
    shares = scatter_near(shares, far)
    grad_q = first_back(at, shares, x_p, dh, gains[0])
    grad_tokens = restore(at, pos_col, gather_pieces(grad_q))

    own, heads = width // dps, heads_loc * HD
    grad_qkv = grads_a[: 3 * heads].astype(F32).reshape(heads_loc, 3, HD, own).transpose(3, 1, 0, 2)
    grad_qkv = grad_qkv.reshape(own, 3, heads)
    grad_in = grads[0].astype(F32)
    grad_out = grads[1].astype(F32).T
    rest = grads_a[3 * heads : 7 * heads].reshape(4, heads, own)
    small = jnp.broadcast_to(grads_a[7 * heads :], (4, lanes, own))
    rest = lax.all_to_all(jnp.concatenate([rest, small], axis=1), "mp", 0, 0, tiled=True)
    rest = jnp.sum(rest.astype(F32), axis=0)
    grad_o, small = rest[:heads], rest[heads:]
    small_out = small[: experts + 2].T
    return (
        output,
        grad_tokens,
        jnp.stack([small[experts + 4], small[experts + 2]]),
        jnp.stack([small[experts + 5], small[experts + 3]]),
        grad_qkv,
        grad_o,
        grad_in,
        grad_out,
        small_out[:, :experts],
        small_out[:, experts:],
        grad_up[None],
        grad_down[None],
    )


def solution(mesh):
    in_specs = (
        P("dp", None),
        P("dp", None),
        P(),
        P(),
        P(None, None, "mp"),
        P("mp", None),
        P(None, "mp"),
        P("mp", None),
        P(),
        P(),
        P("dp", None, "mp"),
        P("dp", "mp", None),
        P("dp", None),
        P(),
    )
    out_specs = (
        P("dp", None),
        P("dp", None),
        P(None, "dp"),
        P(None, "dp"),
        P("dp", None, "mp"),
        P("mp", "dp"),
        P("dp", "mp"),
        P("mp", "dp"),
        P("dp", None),
        P("dp", None),
        P("dp", None, "mp"),
        P("dp", "mp", None),
    )
    return jax.shard_map(body, mesh=mesh, in_specs=in_specs, out_specs=out_specs, check_vma=False)
```

```python
from functools import partial

import jax
import jax.numpy as jnp
from jax import lax
from jax.experimental import pallas as pl
from jax.experimental.pallas import tpu as pltpu
from jax.sharding import PartitionSpec as P

HD = 64
GROUP = 4
EPS = 1e-05
LOG2E = 1.4426950408889634
SCALE2 = 0.125 * LOG2E
HIDE = -1e30
BF = jnp.bfloat16
F32 = jnp.float32
LIGHT = pl.CostEstimate(flops=1 << 20, bytes_accessed=1 << 20, transcendentals=0)


def mm(a, b):
    return jnp.dot(a, b, preferred_element_type=F32)


def ein(spec, a, b):
    return jnp.einsum(spec, a, b, preferred_element_type=F32)


def call(kernel, name, prefetch, grid, in_specs, out_specs, out_shape, args, scratch=(), alias=None, vmem=48):
    return pl.pallas_call(
        kernel,
        grid_spec=pltpu.PrefetchScalarGridSpec(
            num_scalar_prefetch=1,
            grid=grid,
            in_specs=in_specs,
            out_specs=out_specs,
            scratch_shapes=list(scratch),
        ),
        out_shape=out_shape,
        input_output_aliases=alias or {},
        compiler_params=pltpu.CompilerParams(vmem_limit_bytes=vmem * 2**20),
        cost_estimate=LIGHT,
        name=name,
    )(prefetch, *args)


def fixed(shape):
    zeros = (0,) * len(shape)
    return pl.BlockSpec(shape, lambda *_: zeros)


def like(shape, dtype):
    return jax.ShapeDtypeStruct(shape, dtype)


def normalize(v):
    mean = jnp.mean(v, axis=-1, keepdims=True)
    centred = v - mean
    scale = lax.rsqrt(jnp.mean(centred * centred, axis=-1, keepdims=True) + EPS)
    return centred * scale, scale


def norm_back(grad, gain, normal, scale):
    g = grad * gain
    along = jnp.mean(g * normal, axis=-1, keepdims=True)
    return scale * (g - jnp.mean(g, axis=-1, keepdims=True) - normal * along)


def qkv_kernel(at_ref, x_ref, gain_ref, bias_ref, w_ref, a_ref, *outs):
    normal, _ = normalize(x_ref[...].astype(F32))
    a = (normal * gain_ref[...] + bias_ref[...]).astype(BF)
    a_ref[...] = a
    for s in range(GROUP):
        outs[s][...] = mm_t(w_ref[at_ref[0] ^ s], a).astype(BF)


def project(at, tokens, gain, bias, w_heads):
    rows, width = tokens.shape
    features = w_heads.shape[1]
    blk = min(256, rows)
    moving = pl.BlockSpec((blk, width), lambda i, n: (i, 0))
    return call(
        qkv_kernel,
        "project",
        at,
        (rows // blk,),
        [moving, fixed((1, width)), fixed((1, width)), fixed(w_heads.shape)],
        [moving] + [pl.BlockSpec((features, blk), lambda i, n: (0, i))] * GROUP,
        [like((rows, width), BF)] + [like((features, rows), BF)] * GROUP,
        (tokens, gain, bias, w_heads),
    )


def fill_keys(k_s, place, keys, first_len, blk):
    rows = place * blk + lax.broadcasted_iota(jnp.int32, (blk, 128), 0)
    lane = lax.broadcasted_iota(jnp.int32, (blk, 128), 1)
    wide = jnp.concatenate([keys.astype(F32).T, jnp.zeros((blk, 128 - HD), F32)], axis=1)
    wide = jnp.where((lane == HD) & (rows < first_len), HIDE, wide)
    k_s[pl.ds(place * blk, blk), :] = wide.astype(BF)


def wide_query(query, place, first_len, blk):
    cols = place * blk + lax.broadcasted_iota(jnp.int32, (128 - HD, blk), 1)
    sub = lax.broadcasted_iota(jnp.int32, (128 - HD, blk), 0)
    extra = jnp.where((sub == 0) & (cols >= first_len), 1.0, 0.0)
    return jnp.concatenate([query, extra.astype(BF)], axis=0)


def causal(blk):
    keys = lax.broadcasted_iota(jnp.int32, (blk, blk), 0)
    queries = lax.broadcasted_iota(jnp.int32, (blk, blk), 1)
    return keys <= queries


def attend_kernel(blk, per, at_ref, *refs):
    qkv_refs, o_refs = refs[:GROUP], refs[GROUP : 2 * GROUP]
    lse_ref, k_s, qkv_s = refs[2 * GROUP :]
    i = pl.program_id(0)
    place, first_len = at_ref[0], at_ref[3]

    @pl.when(i == 0)
    def _():
        for s in range(GROUP):
            qkv_s[place ^ s] = qkv_refs[s][...]

    def part(which, j):
        return qkv_s[j // per, HD * which : HD * (which + 1), pl.ds((j % per) * blk, blk)]

    fill_keys(k_s, i, part(1, i), first_len, blk)
    query = wide_query(part(0, i), i, first_len, blk)

    def scores(j):
        return mm(k_s[pl.ds(pl.multiple_of(j * blk, blk), blk), :], query)

    s = jnp.where(causal(blk), scores(i), HIDE)
    top = jnp.max(s, axis=0, keepdims=True)
    p = jnp.exp2((s - top) * SCALE2)
    total = jnp.sum(p, axis=0, keepdims=True)
    acc = mm(part(2, i), p.astype(BF))

    def steps(blocks, carry):
        top, total, acc = carry
        s = [scores(j) for j in blocks]
        new = top
        for one in s:
            new = jnp.maximum(new, jnp.max(one, axis=0, keepdims=True))
        keep = jnp.exp2((top - new) * SCALE2)
        total, acc = total * keep, acc * keep
        for j, one in zip(blocks, s):
            p = jnp.exp2((one - new) * SCALE2)
            total = total + jnp.sum(p, axis=0, keepdims=True)
            acc = acc + mm(part(2, j), p.astype(BF))
        return new, total, acc

    low = jnp.where(i * blk >= first_len, first_len // blk, 0)
    pairs = (i - low) // 2
    carry = lax.fori_loop(
        0, pairs, lambda t, c: steps([low + 2 * t, low + 2 * t + 1], c), (top, total, acc)
    )
    top, total, acc = lax.fori_loop(low + 2 * pairs, i, lambda j, c: steps([j], c), carry)
    out = (acc / total).astype(BF)
    for s in range(GROUP):

        @pl.when((i // per) ^ place == s)
        def _():
            o_refs[s][:, pl.ds((i % per) * blk, blk)] = out

    lse_ref[0] = top * SCALE2 + jnp.log2(total)


def attend(at, qkv):
    features, rows = qkv[0].shape
    blk = min(512, rows)
    per = rows // blk
    count = GROUP * per
    return call(
        partial(attend_kernel, blk, per),
        "attend",
        at,
        (count,),
        [fixed((features, rows))] * GROUP,
        [fixed((HD, rows))] * GROUP + [pl.BlockSpec((1, 1, blk), lambda i, n: (i, 0, 0))],
        [like((HD, rows), BF)] * GROUP + [like((count, 1, blk), F32)],
        qkv,
        scratch=[pltpu.VMEM((GROUP * rows, 128), BF), pltpu.VMEM((GROUP, features, rows), BF)],
    )


def back_kernel(blk, per, count, at_ref, *refs):
    qkv_refs, do_refs, o_refs = refs[:GROUP], refs[GROUP : 2 * GROUP], refs[2 * GROUP : 3 * GROUP]
    lse_ref, refs = refs[3 * GROUP], refs[3 * GROUP + 1 :]
    out_refs, refs = refs[:GROUP], refs[GROUP:]
    dq_ref, out_ref, k_s, kt_s, v_s, wide_s, dot_s, both_s, delta_s, acc_s = refs
    j = pl.program_id(0)
    place, first_len = at_ref[0], at_ref[3]

    @pl.when(j == 0)
    def _():
        dq_ref[...] = jnp.zeros(dq_ref.shape, F32)
        zero = jnp.zeros((blk, HD), F32)
        for s in range(GROUP):
            for sub in range(per):
                i = (place ^ s) * per + sub
                at = pl.ds(pl.multiple_of(i * blk, blk), blk)
                cut = slice(sub * blk, (sub + 1) * blk)
                query = qkv_refs[s][0:HD, cut]
                keys = qkv_refs[s][HD : 2 * HD, cut]
                grad = do_refs[s][:, cut]
                fill_keys(k_s, i, keys, first_len, blk)
                kt_s[:, at] = keys
                dot_s[:, at] = grad
                wide_s[:, at] = wide_query(query, i, first_len, blk)
                grad = grad.astype(F32)
                values = qkv_refs[s][2 * HD :, cut].astype(F32)
                v_s[at, :] = jnp.concatenate([values.T, zero], axis=1).astype(BF)
                both_s[0, at, :] = jnp.concatenate([grad.T, zero], axis=1).astype(BF)
                both_s[1, at, :] = jnp.concatenate([zero, query.astype(F32).T], axis=1).astype(BF)
                held = o_refs[s][:, cut].astype(F32)
                delta_s[i] = jnp.sum(held * grad, axis=0, keepdims=True)

    here = pl.ds(pl.multiple_of(j * blk, blk), blk)
    keys_t = kt_s[:, here]
    values = v_s[here, 0:HD]

    def pair(i, diagonal):
        at = pl.ds(pl.multiple_of(i * blk, blk), blk)
        s = mm(k_s[here, :], wide_s[:, at])
        p = jnp.exp2(s * SCALE2 - lse_ref[i])
        if diagonal:
            p = jnp.where(causal(blk), p, 0.0)
        dp = mm(values, dot_s[:, at])
        ds = (p * (dp - delta_s[i])).astype(BF)
        return mm(p.astype(BF), both_s[0, at, :]) + mm(ds, both_s[1, at, :]), mm(keys_t, ds)

    acc_s[...], dq = pair(j, True)
    dq_ref[:, here] += dq

    def step_two(t, carry):
        i = j + 1 + 2 * t
        (kv_0, dq_0), (kv_1, dq_1) = pair(i, False), pair(i + 1, False)
        acc_s[...] += kv_0 + kv_1
        at = pl.ds(pl.multiple_of(i * blk, blk), 2 * blk)
        dq_ref[:, at] += jnp.concatenate([dq_0, dq_1], axis=1)
        return carry

    def step(i, carry):
        kv, dq = pair(i, False)
        acc_s[...] += kv
        dq_ref[:, pl.ds(pl.multiple_of(i * blk, blk), blk)] += dq
        return carry

    high = jnp.where((j + 1) * blk <= first_len, (first_len + blk - 1) // blk, count)
    pairs = (high - j - 1) // 2
    lax.fori_loop(0, pairs, step_two, 0)
    lax.fori_loop(j + 1 + 2 * pairs, high, step, 0)
    both = acc_s[...].T
    out_ref[0:HD, :] = (dq_ref[:, here] * 0.125).astype(BF)
    out_ref[HD : 2 * HD, :] = (both[HD:, :] * 0.125).astype(BF)
    out_ref[2 * HD :, :] = both[:HD, :].astype(BF)
    for s in range(GROUP):

        @pl.when((j // per) ^ place == s)
        def _():
            out_refs[s][:, pl.ds(pl.multiple_of((j % per) * blk, blk), blk)] = out_ref[...]


def attend_back(at, qkv, do, o, lse):
    features, rows = qkv[0].shape
    blk = min(512, rows)
    per = rows // blk
    count = GROUP * per
    return call(
        partial(back_kernel, blk, per, count),
        "attend_back",
        at,
        (count,),
        [fixed((features, rows))] * GROUP
        + [fixed((HD, rows))] * (2 * GROUP)
        + [fixed((count, 1, blk))],
        [fixed((features, rows))] * GROUP,
        [like((features, rows), BF)] * GROUP,
        (*qkv, *do, *o, lse),
        scratch=[
            pltpu.VMEM((HD, GROUP * rows), F32),
            pltpu.VMEM((features, blk), BF),
            pltpu.VMEM((GROUP * rows, 128), BF),
            pltpu.VMEM((HD, GROUP * rows), BF),
            pltpu.VMEM((GROUP * rows, 128), BF),
            pltpu.VMEM((128, GROUP * rows), BF),
            pltpu.VMEM((HD, GROUP * rows), BF),
            pltpu.VMEM((2, GROUP * rows, 128), BF),
            pltpu.VMEM((count, 1, blk), F32),
            pltpu.VMEM((blk, 128), F32),
        ],
    )


def stack_kernel(at_ref, *refs):
    ins, out_ref = refs[:GROUP], refs[GROUP]
    for s in range(GROUP):
        head = pl.ds(pl.multiple_of((at_ref[0] ^ s) * HD, HD), HD)
        out_ref[head, :] = ins[s][...]


def stack(at, heads):
    rows = heads[0].shape[1]
    return call(
        stack_kernel,
        "stack",
        at,
        (1,),
        [fixed((HD, rows))] * GROUP,
        fixed((GROUP * HD, rows)),
        like((GROUP * HD, rows), BF),
        heads,
    )


def unsplit_kernel(at_ref, *refs):
    ins, outs = refs[:4], refs[4:]
    cols = ins[0].shape[1]
    for r in range(4):
        lanes = pl.ds(pl.multiple_of(((at_ref[1] + r) % 4) * cols, cols), cols)
        for s in range(GROUP):
            head = pl.ds(pl.multiple_of((at_ref[0] ^ s) * HD, HD), HD)
            outs[s][:, lanes] = ins[r][head, :]


def unsplit(at, pieces):
    shape = (HD, 4 * pieces[0].shape[1])
    return call(
        unsplit_kernel,
        "unsplit",
        at,
        (1,),
        [fixed(pieces[0].shape)] * 4,
        [fixed(shape)] * GROUP,
        [like(shape, BF)] * GROUP,
        pieces,
    )


def heads_of(mine, r, features):
    return pl.ds(pl.multiple_of(((mine + 4 - r) % 4) * features, features), features)


def mid_kernel(at_ref, *refs):
    pieces, (w_ref, x_ref, gain_ref, bias_ref, h_ref, b_ref) = refs[:6], refs[6:]
    h = x_ref[...].astype(F32)
    for r, piece in enumerate(in_order(at_ref[1], *[ref[...] for ref in pieces])):
        rows = heads_of(at_ref[1], 4 - r, piece.shape[0])
        h = h + mm(turned(piece), w_ref[rows, :])

    @pl.when(pl.program_id(0) == 0)
    def _():
        h_ref[...] = h

    normal, _ = normalize(h)
    b_ref[...] = (normal * gain_ref[...] + bias_ref[...]).astype(BF)


def mid(at, pieces, w_o, tokens, gain, bias):
    features, rows = pieces[0].shape
    width, quarter = tokens.shape[1], rows // 4
    return call(
        mid_kernel,
        "mid",
        at,
        (4,),
        [pl.BlockSpec((features, quarter), lambda q, n: (0, (n[1] + q) % 4))] * 6
        + [fixed(w_o.shape)]
        + [pl.BlockSpec((quarter, width), lambda q, n: ((n[1] + q) % 4, 0))]
        + [fixed((1, width))] * 2,
        [fixed((quarter, width)), pl.BlockSpec((quarter, width), lambda q, n: (q, 0))],
        [like((quarter, width), F32), like((rows, width), BF)],
        (*pieces, w_o, tokens, gain, bias),
    )


def add_up(refs):
    total = refs[0][...]
    for ref in refs[1:]:
        total = total + ref[...].astype(F32)
    return total


def mid_back_kernel(at_ref, *refs):
    shares, (w_ref, h_ref, dy_ref, gain_ref, dh_ref, low_ref, sums_ref) = refs[:4], refs[4:11]
    do_refs = refs[11:]
    db = add_up(shares)
    normal, scale = normalize(h_ref[...])
    dh = dy_ref[...].astype(F32) + norm_back(db, gain_ref[...], normal, scale)
    dh_ref[...] = dh
    low = dh.astype(BF)
    low_ref[...] = low
    sums_ref[0:1, :] = jnp.sum(db * normal, axis=0, keepdims=True)
    sums_ref[1:2, :] = jnp.sum(db, axis=0, keepdims=True)
    for r in range(4):
        rows = heads_of(at_ref[1], r, do_refs[r].shape[0])
        do_refs[r][...] = mm_t(w_ref[rows, :], low).astype(BF)


def mid_back(at, shares, w_o, h, dy, gain):
    quarter, width = h.shape
    whole = fixed((quarter, width))
    piece = (w_o.shape[0] // 4, quarter)
    return call(
        mid_back_kernel,
        "mid_back",
        at,
        (1,),
        [whole] * 4 + [fixed(w_o.shape), whole, whole, fixed((1, width))],
        [whole] * 2 + [fixed((2, width))] + [fixed(piece)] * 4,
        [like((quarter, width), F32), like((quarter, width), BF), like((2, width), F32)]
        + [like(piece, BF)] * 4,
        (*shares, w_o, h, dy, gain),
    )


def first_back_kernel(at_ref, *refs):
    shares = refs[:4]
    x_ref, dh_ref, gain_ref, out_ref = refs[4:]
    d_a = add_up(shares)
    normal, scale = normalize(x_ref[...].astype(F32))
    out_ref[...] = (dh_ref[...] + norm_back(d_a, gain_ref[...], normal, scale)).astype(BF)


def first_back(at, shares, tokens, dh, gain):
    quarter, width = dh.shape
    return call(
        first_back_kernel,
        "first_back",
        at,
        (1,),
        [fixed((quarter, width))] * 4
        + [pl.BlockSpec((quarter, width), lambda i, n: (n[1], 0))]
        + [fixed((quarter, width)), fixed((1, width))],
        fixed((quarter, width)),
        like((quarter, width), BF),
        (*shares, tokens, dh, gain),
    )


def in_order(mine, own, right, left, far, right_two, left_two):
    one = jnp.where(mine == 3, far, left)
    two = jnp.where(mine < 2, left_two, right_two)
    three = jnp.where(mine == 0, far, right)
    return own, one, two, three


def one_hot(slots, dest):
    return jnp.where(slots == dest, 1.0, 0.0).astype(BF)


def dispatch_kernel(at_ref, dest_ref, rows_ref, out_ref, spread_s):
    blk, rows = min(256, spread_s.shape[0]), dest_ref.shape[1]

    @pl.when(pl.program_id(0) == 0)
    def _():
        slot = lax.broadcasted_iota(jnp.int32, (blk, rows), 0)
        for start in range(0, spread_s.shape[0], blk):
            spread_s[start : start + blk, :] = one_hot(slot + start, dest_ref[...])

    out_ref[...] = mm(spread_s[...], rows_ref[...]).astype(BF)


def columns(rows, width):
    return pl.BlockSpec((rows, width), lambda i, n: (0, i))


def dispatch(at, dest_row, values, slots):
    rows, width = values.shape
    blk = min(256, width)
    return call(
        dispatch_kernel,
        "dispatch",
        at,
        (width // blk,),
        [fixed((1, rows)), columns(rows, blk)],
        columns(slots, blk),
        like((slots, width), BF),
        (dest_row, values),
        scratch=[pltpu.VMEM((slots, rows), BF)],
    )


def join_kernel(at_ref, *refs):
    pieces, out_ref = refs[:6], refs[6]
    r = pl.program_id(0)
    for place, piece in enumerate(in_order(at_ref[1], *[ref[...] for ref in pieces])):

        @pl.when(r == place)
        def _():
            out_ref[...] = piece


def join(at, pieces):
    each, width = pieces[0].shape
    return call(
        join_kernel,
        "join",
        at,
        (4,),
        [fixed((each, width))] * 6,
        pl.BlockSpec((each, width), lambda r, n: ((n[1] + r) % 4, 0)),
        like((4 * each, width), BF),
        pieces,
    )


def write_shares(mine, total, own_ref, one_ref, two_ref, three_ref, end_ref):
    rows = own_ref.shape[0]
    own_ref[...] = total[:rows]
    one, two, three = [total[r * rows : (r + 1) * rows].astype(BF) for r in (1, 2, 3)]
    one_ref[...] = one
    two_ref[...] = two
    three_ref[...] = three
    end_ref[...] = jnp.where(mine == 0, three, one)


def share_shapes(rows, width):
    return [like((rows, width), F32)] + [like((rows, width), BF)] * 4


def combine_kernel(count, whole, at_ref, *refs):
    dests, backs = refs[:count], refs[count : 2 * count]
    base_ref, refs, pick_s = refs[2 * count], refs[2 * count + 1 : -1], refs[-1]
    rows, slots = base_ref.shape[0], backs[0].shape[0]
    blk = rows // 4

    @pl.when(pl.program_id(0) == 0)
    def _():
        lane = lax.broadcasted_iota(jnp.int32, (blk, slots), 1)
        for k in range(count):
            for start in range(0, rows, blk):
                dest = dests[k][start : start + blk, :]
                pick_s[start : start + blk, k * slots : (k + 1) * slots] = one_hot(lane, dest)

    total = base_ref[...].astype(F32)
    for k in range(count):
        total = total + mm(pick_s[:, k * slots : (k + 1) * slots], backs[k][...])
    mine = at_ref[1]
    if whole:
        h_ref, out_ref = refs
        for r in range(4):
            part = total[r * blk : (r + 1) * blk]
            if r == 0:
                part = part + h_ref[...]
            place = pl.ds(pl.multiple_of(((mine + r) % 4) * blk, blk), blk)
            out_ref[place, :] = part.astype(BF)
    else:
        write_shares(mine, total, *refs)


def combine(at, dests, backs, base, h=None):
    count, (slots, width), rows = len(backs), backs[0].shape, base.shape[0]
    blk = min(256, width)
    whole = h is not None
    quarter = columns(rows // 4, blk)
    return call(
        partial(combine_kernel, count, whole),
        "combine",
        at,
        (width // blk,),
        [fixed((rows, 1))] * count
        + [columns(slots, blk)] * count
        + [columns(rows, blk)]
        + [quarter] * whole,
        columns(rows, blk) if whole else [quarter] * 5,
        like(base.shape, BF) if whole else share_shapes(rows // 4, width),
        (*dests, *backs, base) + ((h,) if whole else ()),
        scratch=[pltpu.VMEM((rows, count * slots), BF)],
    )


def mm_t(a, b):
    return lax.dot_general(a, b, (((1,), (1,)), ((), ())), preferred_element_type=F32)


def gelu_both(u):
    c = 0.7978845608028654
    square = u * u
    t = jnp.tanh(u * (c + (c * 0.044715) * square))
    half = 0.5 + 0.5 * t
    slope = half + (0.5 * u) * (1.0 - t * t) * (c + (3.0 * c * 0.044715) * square)
    return u * half, slope


def high_low(value):
    high = value.astype(BF)
    return high, (value - high.astype(F32)).astype(BF)


def two_coefs(logits, lane, experts):
    inside = (lane >= experts) & (lane < experts + 2)
    top = jnp.max(jnp.where(inside, logits, HIDE), axis=1, keepdims=True)
    e = jnp.where(inside, jnp.exp(logits - top), 0.0)
    e = e / jnp.sum(e, axis=1, keepdims=True)
    first = jnp.sum(jnp.where(lane == experts, e, 0.0), axis=1, keepdims=True)
    second = jnp.sum(jnp.where(lane == experts + 1, e, 0.0), axis=1, keepdims=True)
    return first, second


def small_back(d_small, rows, w_small_ref, small_ref, i):
    high, low = high_low(d_small)
    w_small = w_small_ref[...]
    high_t, low_t = high_low(d_small.T)

    @pl.when(i == 0)
    def _():
        small_ref[...] = jnp.zeros(small_ref.shape, F32)

    small_ref[...] += mm(high_t, rows) + mm(low_t, rows)
    return mm_t(high, w_small) + mm_t(low, w_small)


def expert_kernel(experts, half, at_ref, rows_ref, dy_ref, up_ref, down_ref, w_small_ref, *outs):
    if half:
        outs = outs[5:]
    rows_out_ref, hid_ref, dy_out_ref, deu_ref, y_ref, d_rows_ref, small_ref = outs
    rows = rows_ref[...]
    rows_out_ref[...] = rows
    up = mm(rows, up_ref[...])
    logits = mm(rows, w_small_ref[...])
    lane = lax.broadcasted_iota(jnp.int32, logits.shape, 1)
    routed = lane < experts
    top = jnp.max(jnp.where(routed, logits, HIDE), axis=1, keepdims=True)
    probs = jnp.where(routed, jnp.exp(logits - top), 0.0)
    probs = probs / jnp.sum(probs, axis=1, keepdims=True)
    own = jnp.where(lane == at_ref[2], 1.0, 0.0)
    gate = jnp.sum(probs * own, axis=1, keepdims=True)
    first, second = two_coefs(logits, lane, experts)
    weight = second * gate
    dy = dy_ref[...].reshape(rows.shape).astype(F32)
    d_y = (weight * dy).astype(BF)
    dy_out_ref[...] = d_y
    d_hidden = mm_t(d_y, down_ref[...])
    hidden, slope = gelu_both(up)
    hidden = hidden.astype(BF)
    hid_ref[...] = hidden
    d_up = (d_hidden * slope).astype(BF)
    deu_ref[...] = d_up
    y = mm(hidden, down_ref[...])
    y_ref[...] = (weight * y).astype(BF).reshape(y_ref.shape)
    along = gate * jnp.sum(dy * y, axis=1, keepdims=True)
    mixed = first * second * along
    d_small = (second * along) * (own - probs)
    d_small = jnp.where(routed, d_small, 0.0)
    d_small = d_small + jnp.where(lane == experts + 1, mixed, 0.0)
    d_small = d_small - jnp.where(lane == experts, mixed, 0.0)
    d_rows = mm_t(d_up, up_ref[...]) + small_back(d_small, rows, w_small_ref, small_ref, pl.program_id(0))
    d_rows_ref[...] = d_rows.astype(BF)


def expert_rows(at, rows, dy, w_up, w_down, w_small, experts, half, before):
    count, width = rows.shape
    hid, lanes = w_up.shape[1], w_small.shape[1]
    blk = min(512, count)
    capacity = count // dy.shape[0]
    steps = count // blk
    moving = pl.BlockSpec((blk, width), lambda i, n: (i, 0))
    slots = pl.BlockSpec((blk // capacity, capacity, width), lambda i, n: (i, half, 0))
    kept = [pl.BlockSpec((blk, size), lambda i, n: (i + half * steps, 0)) for size in (width, hid, width, hid)]
    return call(
        partial(expert_kernel, experts, half),
        "expert_rows",
        at,
        (steps,),
        [
            moving,
            slots,
            fixed((width, hid)),
            fixed((hid, width)),
            fixed((width, lanes)),
        ]
        + [pl.BlockSpec(memory_space=pl.ANY)] * (5 * half),
        kept + [slots, moving, fixed((lanes, width))],
        [like((2 * count, size), BF) for size in (width, hid, width, hid)]
        + [like(dy.shape, BF), like((count, width), BF)]
        + [like((lanes, width), F32)],
        (rows, dy, w_up, w_down, w_small, *before),
        alias={6 + k: k for k in range(5)} if half else None,
        vmem=56,
    )


def dense_kernel(experts, at_ref, rows_ref, dy_ref, in_ref, out_ref, w_small_ref, *outs):
    hid_ref, grad_ref, d_up_ref, mix_ref, db_ref, small_ref = outs
    rows = rows_ref[...]
    up = mm(rows, in_ref[...])
    logits = mm(rows, w_small_ref[...])
    lane = lax.broadcasted_iota(jnp.int32, logits.shape, 1)
    first, second = two_coefs(logits, lane, experts)
    dy = dy_ref[...].astype(F32)
    grad = (first * dy).astype(BF)
    grad_ref[...] = grad
    d_hidden = mm_t(grad, out_ref[...])
    hidden, slope = gelu_both(up)
    hidden = hidden.astype(BF)
    hid_ref[...] = hidden
    d_up = (d_hidden * slope).astype(BF)
    d_up_ref[...] = d_up
    dense = mm(hidden, out_ref[...])
    mix_ref[...] = first * dense
    mixed = first * second * jnp.sum(dy * dense, axis=1, keepdims=True)
    d_small = jnp.where(lane == experts, mixed, 0.0) - jnp.where(lane == experts + 1, mixed, 0.0)
    db_ref[...] = mm_t(d_up, in_ref[...]) + small_back(d_small, rows, w_small_ref, small_ref, pl.program_id(0))


def dense_rows(at, rows, dy, w_in, w_out, w_small, experts):
    (count, width), hid, lanes = rows.shape, w_in.shape[1], w_small.shape[1]
    blk = min(512, count)
    row_out = pl.BlockSpec((blk, width), lambda i, n: (i, 0))
    hid_out = pl.BlockSpec((blk, hid), lambda i, n: (i, 0))
    return call(
        partial(dense_kernel, experts),
        "dense_rows",
        at,
        (count // blk,),
        [row_out, row_out, fixed((width, hid)), fixed((hid, width)), fixed((width, lanes))],
        [hid_out, row_out, hid_out, row_out, row_out, fixed((lanes, width))],
        [
            like((count, hid), BF),
            like((count, width), BF),
            like((count, hid), BF),
            like((count, width), F32),
            like((count, width), F32),
            like((lanes, width), F32),
        ],
        (rows, dy, w_in, w_out, w_small),
        vmem=56,
    )


def turned(value):
    return value.astype(F32).T.astype(BF)


def dense_grads_kernel(at_ref, b_ref, d_up_ref, grad_ref, hid_ref, keep_ref, give_ref):
    width = d_up_ref.shape[1]
    first = mm(turned(b_ref[...]), d_up_ref[...]).astype(BF)
    second = mm(turned(grad_ref[...]), hid_ref[...]).astype(BF)
    half = pl.num_programs(0) // 2
    for side, ref in ((0, keep_ref), (1, give_ref)):

        @pl.when(pl.program_id(0) // half == side)
        def _():
            ref[0, :, :width] = first
            ref[0, :, width:] = second


def dense_grads(at, b, d_up, grad, hidden, parts):
    (rows, width), hid = b.shape, hidden.shape[1]
    own, half, bits = width // parts, parts // 2, parts.bit_length() - 1

    def part(q, n):
        turned_q = sum([((q // 2**k) % 2) * 2 ** (bits - 1 - k) for k in range(bits)])
        return turned_q ^ n[2]

    column = pl.BlockSpec((rows, own), lambda q, n: (0, part(q, n)))
    shape = (1, own, 2 * hid)
    return call(
        dense_grads_kernel,
        "dense_grads",
        at,
        (parts,),
        [column, fixed((rows, hid)), column, fixed((rows, hid))],
        [
            pl.BlockSpec(shape, lambda q, n: (jnp.minimum(q, half - 1), 0, 0)),
            pl.BlockSpec(shape, lambda q, n: (jnp.maximum(q - half, 0), 0, 0)),
        ],
        [like((half, own, 2 * hid), BF)] * 2,
        (b, d_up, grad, hidden),
    )


def attention_grads_kernel(experts, at_ref, *refs):
    grads, o_refs, refs = refs[:GROUP], refs[GROUP : GROUP + 6], refs[GROUP + 6 :]
    a_ref, dh_ref, w_ref, gain_ref, bias_ref, sums_ref = refs[:6]
    small_refs, (out_ref, all_s) = refs[6:-2], refs[-2:]
    heads, features = GROUP * HD, grads[1].shape[0]
    products, plain = 0.0, 0.0
    for k in range(GROUP):
        head = at_ref[0] ^ k
        rows = pl.ds(pl.multiple_of(head * features, features), features)
        grad = grads[k][...]
        weight = w_ref[head].astype(F32)
        total = mm(grad, a_ref[...])
        all_s[rows, :] = total
        each = jnp.sum(grad.astype(F32), axis=1, keepdims=True)
        products = products + jnp.sum(total * weight, axis=0, keepdims=True)
        plain = plain + jnp.sum(each * weight, axis=0, keepdims=True)
    first = GROUP * features
    for r, piece in enumerate(in_order(at_ref[1], *[ref[...] for ref in o_refs])):
        rows = pl.ds(pl.multiple_of(first + ((at_ref[1] + r) % 4) * heads, heads), heads)
        all_s[rows, :] = mm(piece, dh_ref[...])
    first += 4 * heads
    small = add_up(small_refs)
    row = lax.broadcasted_iota(jnp.int32, small.shape, 0)
    d_gain = (products - bias_ref[...] * plain) / gain_ref[...]
    for k, sums in enumerate((sums_ref[0:1, :], sums_ref[1:2, :], d_gain, plain)):
        small = jnp.where(row == experts + 2 + k, sums, small)
    all_s[first:, :] = small
    out_ref[...] = all_s[...].T.astype(BF)


def attention_grads(at, grads, o, a, dh, w_heads, gain, bias, sums, small, experts):
    rows, width = a.shape
    features, lanes = grads[0].shape[0], small[0].shape[0]
    piece = pl.BlockSpec((o[0].shape[0], dh.shape[0]), lambda i, n: (0, n[1]))
    height = GROUP * features + 4 * o[0].shape[0] + lanes
    blk = min(256, width)
    return call(
        partial(attention_grads_kernel, experts),
        "attention_grads",
        at,
        (width // blk,),
        [fixed((features, rows))] * GROUP
        + [piece] * 6
        + [columns(rows, blk), columns(dh.shape[0], blk)]
        + [pl.BlockSpec((GROUP, features, blk), lambda i, n: (0, 0, i))]
        + [columns(1, blk)] * 2
        + [columns(2, blk)]
        + [columns(lanes, blk)] * len(small),
        pl.BlockSpec((blk, height), lambda i, n: (i, 0)),
        like((width, height), BF),
        (*grads, *o, a, dh, w_heads, gain, bias, sums, *small),
        scratch=[pltpu.VMEM((height, blk), F32)],
    )


def project_kernel(at_ref, *refs):
    grads, w_ref, outs, turned_s = refs[:GROUP], refs[GROUP], refs[GROUP + 1 : -1], refs[-1]
    rows = turned_s.shape[1]
    blk = rows // 4

    @pl.when(pl.program_id(0) == 0)
    def _():
        for s in range(GROUP):
            for r in range(4):
                lanes = pl.ds(pl.multiple_of(((at_ref[1] + r) % 4) * blk, blk), blk)
                turned_s[s, r * blk : (r + 1) * blk, :] = turned(grads[s][:, lanes])

    total = 0.0
    for s in range(GROUP):
        total = total + mm(turned_s[s], w_ref[at_ref[0] ^ s])
    write_shares(at_ref[1], total, *outs)


def project_back(at, grads, w_heads):
    features, rows = grads[0].shape
    width = w_heads.shape[2]
    blk = min(256, width)
    return call(
        project_kernel,
        "project_back",
        at,
        (width // blk,),
        [fixed((features, rows))] * GROUP
        + [pl.BlockSpec((GROUP, features, blk), lambda i, n: (0, 0, i))],
        [columns(rows // 4, blk)] * 5,
        share_shapes(rows // 4, width),
        (*grads, w_heads),
        scratch=[pltpu.VMEM((GROUP, rows, features), BF)],
    )


def hop(value, *pairs):
    return lax.ppermute(value, "mp", pairs)


def rotate(value, steps):
    return hop(value, *[(s, (s + steps) % 4) for s in range(4)])


def gather_near(own):
    right = hop(own, (0, 1), (1, 2), (2, 3))
    left = hop(own, (1, 0), (2, 1), (3, 2))
    return own, right, left, hop(own, (0, 3), (3, 0))


def gather_far(near):
    _, right, left, _ = near
    return *near, hop(right, (1, 2), (2, 3)), hop(left, (1, 0), (2, 1))


def gather_pieces(own):
    return gather_far(gather_near(own))


def scatter_far(shares):
    _, _, two, _, end = shares
    return hop(two, (2, 1), (3, 2)), hop(two, (0, 1), (1, 2)), hop(end, (0, 3), (3, 0))


def scatter_near(shares, came):
    own, one, _, three, _ = shares
    from_right, from_left, from_end = came
    three = (three.astype(F32) + from_right.astype(F32)).astype(BF)
    one = (one.astype(F32) + from_left.astype(F32)).astype(BF)
    return own, hop(three, (1, 0), (2, 1), (3, 2)), hop(one, (0, 1), (1, 2), (2, 3)), from_end


def group_swap(value, s):
    count = lax.axis_size("dp")
    return lax.ppermute(value, "dp", [(t, t ^ s) for t in range(count)])


def expert_swap(value, experts):
    wide = value.reshape(experts, value.shape[0] // experts, value.shape[1])
    return lax.all_to_all(wide, "dp", 0, 0, tiled=True).reshape(value.shape)


def roll_rows(value, start):
    twice = jnp.concatenate([value, value], axis=0)
    return lax.dynamic_slice_in_dim(twice, start, value.shape[0], 0)


def add_halves(keep, came):
    return (keep.astype(F32) + came.astype(F32)).astype(BF)


def body(
    tokens,
    cotangent,
    ln_gains,
    ln_biases,
    w_qkv,
    w_o,
    w_in,
    w_out,
    w_router,
    w_coef,
    w_up,
    w_down,
    routes,
    long_group,
):
    rows, width = tokens.shape
    dps = lax.axis_size("dp")
    mine, position = lax.axis_index("mp"), lax.axis_index("dp")
    quarter = rows // 4
    start = mine * quarter
    heads_loc = w_qkv.shape[2] // HD
    hid = w_in.shape[1]
    experts = w_router.shape[1]
    capacity = max(2, 2 * rows // experts)
    half = capacity // 2
    barrier = lax.optimization_barrier
    first_len = lax.dynamic_index_in_dim(long_group, position // GROUP, 0, keepdims=False)
    at = jnp.stack([position % GROUP, mine, position, first_len]).astype(jnp.int32)
    gains = [ln_gains[0:1], ln_gains[1:2]]
    biases = [ln_biases[0:1], ln_biases[1:2]]
    w_o_all = lax.all_gather(w_o, "mp", axis=0, tiled=True)

    w_heads = w_qkv.reshape(width, 3, heads_loc, HD).transpose(2, 1, 3, 0)
    w_heads = w_heads.reshape(heads_loc, 3 * HD, width)
    a_r, *qkv = project(at, tokens, gains[0], biases[0], w_heads)
    qkv = [qkv[0]] + [group_swap(qkv[s], s) for s in (1, 2, 3)]

    route = roll_rows(routes, start)[:, 0]
    picked = (route[:, None] == jnp.arange(experts, dtype=jnp.int32)[None, :]).astype(jnp.int32)
    slot = jnp.sum((jnp.cumsum(picked, axis=0) - picked) * picked, axis=1)
    dy_b = roll_rows(cotangent, start)
    send_dy = dispatch(at, (route * capacity + slot)[None, :], dy_b, experts * capacity)
    *qkv, send_dy = barrier((*qkv, send_dy))
    in_half = [slot < half, slot >= half]
    dests = [
        jnp.where(in_half[k], route * half + slot - k * half, -1).astype(jnp.int32) for k in (0, 1)
    ]

    *o_t, lse = attend(at, qkv)
    *o_t, w_o_all = barrier((*o_t, w_o_all))
    o_heads = [o_t[0]] + [group_swap(o_t[s], s) for s in (1, 2, 3)]
    lanes = -(-(experts + 2) // 128) * 128
    w_small = jnp.concatenate(
        [w_router, w_coef, jnp.zeros((width, lanes - experts - 2), BF)], axis=1
    )
    *o_heads, send_dy, w_small = barrier((*o_heads, send_dy, w_small))
    got_dy = expert_swap(send_dy, experts).reshape(experts, capacity, width)
    o_pieces = gather_pieces(stack(at, o_heads))
    h, b_r = mid(at, o_pieces, w_o_all, tokens, gains[1], biases[1])

    send_0 = dispatch(at, dests[0][None, :], b_r, experts * half)
    send_0, got_dy = barrier((send_0, got_dy))
    got_0 = expert_swap(send_0, experts)
    send_1 = dispatch(at, dests[1][None, :], b_r, experts * half)
    b_r, send_1 = barrier((b_r, send_1))
    hidden, dense_grad, d_up, mix_base, db_base, small_t = dense_rows(
        at, b_r, dy_b, w_in, w_out, w_small, experts
    )
    send_1, got_0, db_base = barrier((send_1, got_0, db_base))
    got_1 = expert_swap(send_1, experts)

    *kept, d_rows_0, small_0 = expert_rows(
        at, got_0, got_dy, w_up[0], w_down[0], w_small, experts, 0, ()
    )
    back_0 = expert_swap(d_rows_0, experts)
    *kept, d_rows_1, small_1 = expert_rows(
        at, got_1, got_dy, w_up[0], w_down[0], w_small, experts, 1, kept
    )
    got, hidden_e, d_y, d_eu, back_y = kept
    back_1 = expert_swap(d_rows_1, experts)
    d_rows_1, b_r = barrier((d_rows_1, b_r))
    halving = width == dps * 128
    if halving:
        grads = dense_grads(at, b_r, d_up, dense_grad, hidden, dps)
    else:
        grads = [ein("td,tf->df", b_r, d_up).astype(BF), ein("td,tf->df", dense_grad, hidden).astype(BF)]
    back_0, back_1, back_y, *grads = barrier((back_0, back_1, back_y, *grads))

    dest_cols = [dest[:, None] for dest in dests]
    tok_y = expert_swap(back_y.reshape(experts * capacity, width), experts)
    shares = combine(at, dest_cols, [back_0, back_1], db_base)
    far = scatter_far(shares)
    *far, g_0, g_1 = barrier((*far, *grads))
    grads = [g_0, g_1]
    shares = scatter_near(shares, far)
    dh, dh_r, sums_2, *do_q = mid_back(at, shares, w_o_all, h, dy_b[:quarter], gains[1])
    do_q = [do_q[0]] + [rotate(do_q[r], -r) for r in (1, 2, 3)]

    mix = combine(at, [(route * capacity + slot)[:, None]], [tok_y], mix_base, h)
    *do_q, mix = barrier((*do_q, mix))
    output = lax.psum(mix, "mp")
    do_heads = unsplit(at, do_q)
    do_t = [do_heads[0]] + [group_swap(do_heads[s], s) for s in (1, 2, 3)]
    if halving:
        came_1 = group_swap(grads[1], 1)
        half = dps // 4
        give = add_halves(grads[0][half:], came_1[half:])
        *do_t, give = barrier((*do_t, give))
        came_2 = group_swap(give, 2)
    d_qkv = attend_back(at, qkv, do_t, o_t, lse)
    if halving:
        keep = add_halves(grads[0][:half], came_1[:half])
        *d_qkv, came_2, keep = barrier((*d_qkv, came_2, keep))
        grads = add_halves(keep, came_2)
        bit = 4
        while bit < dps:
            half = grads.shape[0] // 2
            grads = add_halves(grads[:half], group_swap(grads[half:], bit))
            bit *= 2
        grads = [grads[0][:, :hid], grads[0][:, hid:]]
    else:
        grads = [lax.psum_scatter(grad, "dp", scatter_dimension=0, tiled=True) for grad in grads]

    d_own, got, hidden_e, d_y, d_eu = barrier((d_qkv[0], got, hidden_e, d_y, d_eu))
    d_qkv = [d_own] + [group_swap(d_qkv[s], s) for s in (1, 2, 3)]
    grad_down = ein("rf,rd->fd", hidden_e, d_y)
    *d_qkv, grad_down = barrier((*d_qkv, grad_down))
    shares = project_back(at, d_qkv, w_heads)
    far = scatter_far(shares)
    grads_a = attention_grads(
        at, d_qkv, o_pieces, a_r, dh_r, w_heads, gains[0], biases[0], sums_2, (small_0, small_1, small_t), experts
    )
    grad_up = ein("rd,rf->df", got, d_eu)
    grads_a, output, grad_up, *far = barrier((grads_a, output, grad_up, *far))
    grads_a = lax.psum_scatter(grads_a, "dp", scatter_dimension=0, tiled=True).T
    shares = scatter_near(shares, far)
    grad_q = first_back(at, shares, tokens, dh, gains[0])
    grad_tokens = join(at, gather_pieces(grad_q))

    own, heads = width // dps, heads_loc * HD
    grad_qkv = grads_a[: 3 * heads].astype(F32).reshape(heads_loc, 3, HD, own).transpose(3, 1, 0, 2)
    grad_qkv = grad_qkv.reshape(own, 3, heads)
    grad_in = grads[0].astype(F32)
    grad_out = grads[1].astype(F32).T
    rest = grads_a[3 * heads : 7 * heads].reshape(4, heads, own)
    small = jnp.broadcast_to(grads_a[7 * heads :], (4, lanes, own))
    rest = lax.all_to_all(jnp.concatenate([rest, small], axis=1), "mp", 0, 0, tiled=True)
    rest = jnp.sum(rest.astype(F32), axis=0)
    grad_o, small = rest[:heads], rest[heads:]
    small_out = small[: experts + 2].T
    return (
        output,
        grad_tokens,
        jnp.stack([small[experts + 4], small[experts + 2]]),
        jnp.stack([small[experts + 5], small[experts + 3]]),
        grad_qkv,
        grad_o,
        grad_in,
        grad_out,
        small_out[:, :experts],
        small_out[:, experts:],
        grad_up[None],
        grad_down[None],
    )


def solution(mesh):
    in_specs = (
        P("dp", None),
        P("dp", None),
        P(),
        P(),
        P(None, None, "mp"),
        P("mp", None),
        P(None, "mp"),
        P("mp", None),
        P(),
        P(),
        P("dp", None, "mp"),
        P("dp", "mp", None),
        P("dp", None),
        P(),
    )
    out_specs = (
        P("dp", None),
        P("dp", None),
        P(None, "dp"),
        P(None, "dp"),
        P("dp", None, "mp"),
        P("mp", "dp"),
        P("dp", "mp"),
        P("mp", "dp"),
        P("dp", None),
        P("dp", None),
        P("dp", None, "mp"),
        P("dp", "mp", None),
    )
    return jax.shard_map(body, mesh=mesh, in_specs=in_specs, out_specs=out_specs, check_vma=False)
```

```python
from functools import partial

import jax
import jax.numpy as jnp
from jax import lax
from jax.experimental import pallas as pl
from jax.experimental.pallas import tpu as pltpu
from jax.sharding import PartitionSpec as P

HD = 64
GROUP = 4
EPS = 1e-05
LOG2E = 1.4426950408889634
SCALE2 = 0.125 * LOG2E
HIDE = -1e30
BF = jnp.bfloat16
F32 = jnp.float32
LIGHT = pl.CostEstimate(flops=1 << 20, bytes_accessed=1 << 20, transcendentals=0)


def mm(a, b):
    return jnp.dot(a, b, preferred_element_type=F32)


def ein(spec, a, b):
    return jnp.einsum(spec, a, b, preferred_element_type=F32)


def call(kernel, name, prefetch, grid, in_specs, out_specs, out_shape, args, scratch=(), alias=None, vmem=28):
    return pl.pallas_call(
        kernel,
        grid_spec=pltpu.PrefetchScalarGridSpec(
            num_scalar_prefetch=1,
            grid=grid,
            in_specs=in_specs,
            out_specs=out_specs,
            scratch_shapes=list(scratch),
        ),
        out_shape=out_shape,
        input_output_aliases=alias or {},
        compiler_params=pltpu.CompilerParams(vmem_limit_bytes=vmem * 2**20),
        cost_estimate=LIGHT,
        name=name,
    )(prefetch, *args)


def fixed(shape):
    zeros = (0,) * len(shape)
    return pl.BlockSpec(shape, lambda *_: zeros)


def like(shape, dtype):
    return jax.ShapeDtypeStruct(shape, dtype)


def normalize(v):
    mean = jnp.mean(v, axis=-1, keepdims=True)
    centred = v - mean
    scale = lax.rsqrt(jnp.mean(centred * centred, axis=-1, keepdims=True) + EPS)
    return centred * scale, scale


def norm_back(grad, gain, normal, scale):
    g = grad * gain
    along = jnp.mean(g * normal, axis=-1, keepdims=True)
    return scale * (g - jnp.mean(g, axis=-1, keepdims=True) - normal * along)


def qkv_kernel(at_ref, x_ref, gain_ref, bias_ref, w_ref, a_ref, *outs):
    normal, _ = normalize(x_ref[...].astype(F32))
    a = (normal * gain_ref[...] + bias_ref[...]).astype(BF)
    a_ref[...] = a
    for s in range(GROUP):
        outs[s][...] = mm_t(w_ref[at_ref[0] ^ s], a).astype(BF)


def project(at, tokens, gain, bias, w_heads):
    rows, width = tokens.shape
    features = w_heads.shape[1]
    blk = min(256, rows)
    moving = pl.BlockSpec((blk, width), lambda i, n: (i, 0))
    return call(
        qkv_kernel,
        "project",
        at,
        (rows // blk,),
        [moving, fixed((1, width)), fixed((1, width)), fixed(w_heads.shape)],
        [moving] + [pl.BlockSpec((features, blk), lambda i, n: (0, i))] * GROUP,
        [like((rows, width), BF)] + [like((features, rows), BF)] * GROUP,
        (tokens, gain, bias, w_heads),
    )


def fill_keys(k_s, place, keys, first_len, blk):
    rows = place * blk + lax.broadcasted_iota(jnp.int32, (blk, 128), 0)
    lane = lax.broadcasted_iota(jnp.int32, (blk, 128), 1)
    wide = jnp.concatenate([keys.astype(F32).T, jnp.zeros((blk, 128 - HD), F32)], axis=1)
    wide = jnp.where((lane == HD) & (rows < first_len), HIDE, wide)
    wide = jnp.where((lane > HD) & (lane < HD + 4), 1.0, wide)
    k_s[pl.ds(place * blk, blk), :] = wide.astype(BF)


def three_parts(value):
    high = value.astype(BF).astype(F32)
    middle = (value - high).astype(BF).astype(F32)
    return high, middle, value - high - middle


def below(rows, blk):
    sub = lax.broadcasted_iota(jnp.int32, (128 - HD, blk), 0)
    out = jnp.zeros((128 - HD, blk), F32)
    for k, row in enumerate(rows):
        out = jnp.where(sub == k, row, out)
    return out.astype(BF)


def wide_query(query, place, first_len, blk, shift=()):
    cols = place * blk + lax.broadcasted_iota(jnp.int32, (1, blk), 1)
    second = jnp.where(cols >= first_len, 1.0, 0.0)
    return jnp.concatenate([query, below([second, *shift], blk)], axis=0)


def causal(blk):
    keys = lax.broadcasted_iota(jnp.int32, (blk, blk), 0)
    queries = lax.broadcasted_iota(jnp.int32, (blk, blk), 1)
    return keys <= queries


def attend_kernel(blk, per, at_ref, *refs):
    qkv_refs, o_refs = refs[:GROUP], refs[GROUP : 2 * GROUP]
    lse_ref, k_s, v_s, qkv_s = refs[2 * GROUP :]
    i = pl.program_id(0)
    place, first_len = at_ref[0], at_ref[3]

    @pl.when(i == 0)
    def _():
        for s in range(GROUP):
            qkv_s[place ^ s] = qkv_refs[s][...]

    def part(which, j):
        return qkv_s[j // per, HD * which : HD * (which + 1), pl.ds((j % per) * blk, blk)]

    fill_keys(k_s, i, part(1, i), first_len, blk)
    query = wide_query(part(0, i), i, first_len, blk)
    ones = jnp.where(lax.broadcasted_iota(jnp.int32, (16, blk), 0) == 0, 1.0, 0.0)
    here = pl.ds(pl.multiple_of(i * blk, blk), blk)
    v_s[:, here] = jnp.concatenate([part(2, i), ones.astype(BF)], axis=0)

    def values(j):
        return v_s[:, pl.ds(pl.multiple_of(j * blk, blk), blk)]

    def scores(j):
        return mm(k_s[pl.ds(pl.multiple_of(j * blk, blk), blk), :], query)

    s = jnp.where(causal(blk), scores(i), HIDE)
    top = jnp.max(s, axis=0, keepdims=True)
    acc = mm(values(i), jnp.exp2((s - top) * SCALE2).astype(BF))

    def steps(blocks, carry):
        top, acc = carry
        s = [scores(j) for j in blocks]
        new = top
        for one in s:
            new = jnp.maximum(new, jnp.max(one, axis=0, keepdims=True))
        acc = acc * jnp.exp2((top - new) * SCALE2)
        for j, one in zip(blocks, s):
            acc = acc + mm(values(j), jnp.exp2((one - new) * SCALE2).astype(BF))
        return new, acc

    low = jnp.where(i * blk >= first_len, first_len // blk, 0)
    pairs = (i - low) // 2
    carry = lax.fori_loop(
        0, pairs, lambda t, c: steps([low + 2 * t, low + 2 * t + 1], c), (top, acc)
    )
    top, acc = lax.fori_loop(low + 2 * pairs, i, lambda j, c: steps([j], c), carry)
    total = acc[HD : HD + 1]
    out = (acc[:HD] / total).astype(BF)
    for s in range(GROUP):

        @pl.when((i // per) ^ place == s)
        def _():
            o_refs[s][:, pl.ds((i % per) * blk, blk)] = out

    lse_ref[0] = top * SCALE2 + jnp.log2(total)


def attend(at, qkv):
    features, rows = qkv[0].shape
    blk = min(512, rows)
    per = rows // blk
    count = GROUP * per
    return call(
        partial(attend_kernel, blk, per),
        "attend",
        at,
        (count,),
        [fixed((features, rows))] * GROUP,
        [fixed((HD, rows))] * GROUP + [pl.BlockSpec((1, 1, blk), lambda i, n: (i, 0, 0))],
        [like((HD, rows), BF)] * GROUP + [like((count, 1, blk), F32)],
        qkv,
        scratch=[
            pltpu.VMEM((GROUP * rows, 128), BF),
            pltpu.VMEM((HD + 16, GROUP * rows), BF),
            pltpu.VMEM((GROUP, features, rows), BF),
        ],
    )


def back_kernel(blk, per, count, at_ref, *refs):
    qkv_refs, do_refs, o_refs = refs[:GROUP], refs[GROUP : 2 * GROUP], refs[2 * GROUP : 3 * GROUP]
    lse_ref, refs = refs[3 * GROUP], refs[3 * GROUP + 1 :]
    out_refs, refs = refs[:GROUP], refs[GROUP:]
    dq_ref, out_ref, k_s, kt_s, v_s, wide_s, dot_s, both_s, acc_s = refs
    j = pl.program_id(0)
    place, first_len = at_ref[0], at_ref[3]

    @pl.when(j == 0)
    def _():
        dq_ref[...] = jnp.zeros(dq_ref.shape, F32)
        zero = jnp.zeros((blk, HD), F32)
        ones = jnp.where(lax.broadcasted_iota(jnp.int32, (blk, HD), 1) < 3, 1.0, 0.0)
        for s in range(GROUP):
            for sub in range(per):
                i = (place ^ s) * per + sub
                at = pl.ds(pl.multiple_of(i * blk, blk), blk)
                cut = slice(sub * blk, (sub + 1) * blk)
                query = qkv_refs[s][0:HD, cut]
                keys = qkv_refs[s][HD : 2 * HD, cut]
                grad = do_refs[s][:, cut]
                fill_keys(k_s, i, keys, first_len, blk)
                kt_s[:, at] = keys
                shift = three_parts(lse_ref[i] * (-1.0 / SCALE2))
                wide_s[:, at] = wide_query(query, i, first_len, blk, shift)
                held = o_refs[s][:, cut].astype(F32)
                delta = jnp.sum(held * grad.astype(F32), axis=0, keepdims=True)
                dot_s[:, at] = jnp.concatenate([grad, below(three_parts(-delta), blk)], axis=0)
                grad = grad.astype(F32)
                values = qkv_refs[s][2 * HD :, cut].astype(F32)
                v_s[at, :] = jnp.concatenate([values.T, ones], axis=1).astype(BF)
                both_s[0, at, :] = jnp.concatenate([grad.T, zero], axis=1).astype(BF)
                both_s[1, at, :] = jnp.concatenate([zero, query.astype(F32).T], axis=1).astype(BF)

    here = pl.ds(pl.multiple_of(j * blk, blk), blk)
    keys_t = kt_s[:, here]
    values = v_s[here, :]

    def pair(i, diagonal):
        at = pl.ds(pl.multiple_of(i * blk, blk), blk)
        s = mm(k_s[here, :], wide_s[:, at])
        p = jnp.exp2(s * SCALE2)
        if diagonal:
            p = jnp.where(causal(blk), p, 0.0)
        dp = mm(values, dot_s[:, at])
        ds = (p * dp).astype(BF)
        return mm(p.astype(BF), both_s[0, at, :]) + mm(ds, both_s[1, at, :]), mm(keys_t, ds)

    acc_s[...], dq = pair(j, True)
    dq_ref[:, here] += dq

    def step_two(t, carry):
        i = j + 1 + 2 * t
        (kv_0, dq_0), (kv_1, dq_1) = pair(i, False), pair(i + 1, False)
        acc_s[...] += kv_0 + kv_1
        at = pl.ds(pl.multiple_of(i * blk, blk), 2 * blk)
        dq_ref[:, at] += jnp.concatenate([dq_0, dq_1], axis=1)
        return carry

    def step(i, carry):
        kv, dq = pair(i, False)
        acc_s[...] += kv
        dq_ref[:, pl.ds(pl.multiple_of(i * blk, blk), blk)] += dq
        return carry

    high = jnp.where((j + 1) * blk <= first_len, (first_len + blk - 1) // blk, count)
    pairs = (high - j - 1) // 2
    lax.fori_loop(0, pairs, step_two, 0)
    lax.fori_loop(j + 1 + 2 * pairs, high, step, 0)
    both = acc_s[...].T
    out_ref[0:HD, :] = (dq_ref[:, here] * 0.125).astype(BF)
    out_ref[HD : 2 * HD, :] = (both[HD:, :] * 0.125).astype(BF)
    out_ref[2 * HD :, :] = both[:HD, :].astype(BF)
    for s in range(GROUP):

        @pl.when((j // per) ^ place == s)
        def _():
            out_refs[s][:, pl.ds(pl.multiple_of((j % per) * blk, blk), blk)] = out_ref[...]


def attend_back(at, qkv, do, o, lse):
    features, rows = qkv[0].shape
    blk = min(512, rows)
    per = rows // blk
    count = GROUP * per
    return call(
        partial(back_kernel, blk, per, count),
        "attend_back",
        at,
        (count,),
        [fixed((features, rows))] * GROUP
        + [fixed((HD, rows))] * (2 * GROUP)
        + [fixed((count, 1, blk))],
        [fixed((features, rows))] * GROUP,
        [like((features, rows), BF)] * GROUP,
        (*qkv, *do, *o, lse),
        scratch=[
            pltpu.VMEM((HD, GROUP * rows), F32),
            pltpu.VMEM((features, blk), BF),
            pltpu.VMEM((GROUP * rows, 128), BF),
            pltpu.VMEM((HD, GROUP * rows), BF),
            pltpu.VMEM((GROUP * rows, 128), BF),
            pltpu.VMEM((128, GROUP * rows), BF),
            pltpu.VMEM((128, GROUP * rows), BF),
            pltpu.VMEM((2, GROUP * rows, 128), BF),
            pltpu.VMEM((blk, 128), F32),
        ],
        vmem=36,
    )


def stack_kernel(at_ref, *refs):
    ins, out_ref = refs[:GROUP], refs[GROUP]
    for s in range(GROUP):
        head = pl.ds(pl.multiple_of((at_ref[0] ^ s) * HD, HD), HD)
        out_ref[head, :] = ins[s][...]


def stack(at, heads):
    rows = heads[0].shape[1]
    return call(
        stack_kernel,
        "stack",
        at,
        (1,),
        [fixed((HD, rows))] * GROUP,
        fixed((GROUP * HD, rows)),
        like((GROUP * HD, rows), BF),
        heads,
    )


def unsplit_kernel(at_ref, *refs):
    ins, outs = refs[:4], refs[4:]
    cols = ins[0].shape[1]
    for r in range(4):
        lanes = pl.ds(pl.multiple_of(((at_ref[1] + r) % 4) * cols, cols), cols)
        for s in range(GROUP):
            head = pl.ds(pl.multiple_of((at_ref[0] ^ s) * HD, HD), HD)
            outs[s][:, lanes] = ins[r][head, :]


def unsplit(at, pieces):
    shape = (HD, 4 * pieces[0].shape[1])
    return call(
        unsplit_kernel,
        "unsplit",
        at,
        (1,),
        [fixed(pieces[0].shape)] * 4,
        [fixed(shape)] * GROUP,
        [like(shape, BF)] * GROUP,
        pieces,
    )


def heads_of(mine, r, features):
    return pl.ds(pl.multiple_of(((mine + 4 - r) % 4) * features, features), features)


def mid_kernel(at_ref, *refs):
    pieces, (w_ref, x_ref, gain_ref, bias_ref, h_ref, b_ref) = refs[:6], refs[6:]
    h = x_ref[...].astype(F32)
    for r, piece in enumerate(in_order(at_ref[1], *[ref[...] for ref in pieces])):
        rows = heads_of(at_ref[1], 4 - r, piece.shape[0])
        h = h + mm(turned(piece), w_ref[rows, :])

    @pl.when(pl.program_id(0) == 0)
    def _():
        h_ref[...] = h

    normal, _ = normalize(h)
    b_ref[...] = (normal * gain_ref[...] + bias_ref[...]).astype(BF)


def mid(at, pieces, w_o, tokens, gain, bias):
    features, rows = pieces[0].shape
    width, quarter = tokens.shape[1], rows // 4
    return call(
        mid_kernel,
        "mid",
        at,
        (4,),
        [pl.BlockSpec((features, quarter), lambda q, n: (0, (n[1] + q) % 4))] * 6
        + [fixed(w_o.shape)]
        + [pl.BlockSpec((quarter, width), lambda q, n: ((n[1] + q) % 4, 0))]
        + [fixed((1, width))] * 2,
        [fixed((quarter, width)), pl.BlockSpec((quarter, width), lambda q, n: (q, 0))],
        [like((quarter, width), F32), like((rows, width), BF)],
        (*pieces, w_o, tokens, gain, bias),
    )


def add_up(refs):
    total = refs[0][...]
    for ref in refs[1:]:
        total = total + ref[...].astype(F32)
    return total


def mid_back_kernel(at_ref, *refs):
    shares, (w_ref, h_ref, dy_ref, gain_ref, dh_ref, low_ref, sums_ref) = refs[:4], refs[4:11]
    do_refs = refs[11:]
    db = add_up(shares)
    normal, scale = normalize(h_ref[...])
    dh = dy_ref[...].astype(F32) + norm_back(db, gain_ref[...], normal, scale)
    dh_ref[...] = dh
    low = dh.astype(BF)
    low_ref[...] = low
    sums_ref[0:1, :] = jnp.sum(db * normal, axis=0, keepdims=True)
    sums_ref[1:2, :] = jnp.sum(db, axis=0, keepdims=True)
    for r in range(4):
        rows = heads_of(at_ref[1], r, do_refs[r].shape[0])
        do_refs[r][...] = mm_t(w_ref[rows, :], low).astype(BF)


def mid_back(at, shares, w_o, h, dy, gain):
    quarter, width = h.shape
    whole = fixed((quarter, width))
    piece = (w_o.shape[0] // 4, quarter)
    return call(
        mid_back_kernel,
        "mid_back",
        at,
        (1,),
        [whole] * 4 + [fixed(w_o.shape), whole, whole, fixed((1, width))],
        [whole] * 2 + [fixed((2, width))] + [fixed(piece)] * 4,
        [like((quarter, width), F32), like((quarter, width), BF), like((2, width), F32)]
        + [like(piece, BF)] * 4,
        (*shares, w_o, h, dy, gain),
    )


def first_back_kernel(at_ref, *refs):
    shares = refs[:4]
    x_ref, dh_ref, gain_ref, out_ref = refs[4:]
    d_a = add_up(shares)
    normal, scale = normalize(x_ref[...].astype(F32))
    out_ref[...] = (dh_ref[...] + norm_back(d_a, gain_ref[...], normal, scale)).astype(BF)


def first_back(at, shares, tokens, dh, gain):
    quarter, width = dh.shape
    return call(
        first_back_kernel,
        "first_back",
        at,
        (1,),
        [fixed((quarter, width))] * 4
        + [pl.BlockSpec((quarter, width), lambda i, n: (n[1], 0))]
        + [fixed((quarter, width)), fixed((1, width))],
        fixed((quarter, width)),
        like((quarter, width), BF),
        (*shares, tokens, dh, gain),
    )


def in_order(mine, own, right, left, far, right_two, left_two):
    one = jnp.where(mine == 3, far, left)
    two = jnp.where(mine < 2, left_two, right_two)
    three = jnp.where(mine == 0, far, right)
    return own, one, two, three


def one_hot(slots, dest):
    return jnp.where(slots == dest, 1.0, 0.0).astype(BF)


def dispatch_kernel(at_ref, dest_ref, rows_ref, out_ref, spread_s):
    blk, rows = min(256, spread_s.shape[0]), dest_ref.shape[1]

    @pl.when(pl.program_id(0) == 0)
    def _():
        slot = lax.broadcasted_iota(jnp.int32, (blk, rows), 0)
        for start in range(0, spread_s.shape[0], blk):
            spread_s[start : start + blk, :] = one_hot(slot + start, dest_ref[...])

    out_ref[...] = mm(spread_s[...], rows_ref[...]).astype(BF)


def columns(rows, width):
    return pl.BlockSpec((rows, width), lambda i, n: (0, i))


def dispatch(at, dest_row, values, slots):
    rows, width = values.shape
    blk = min(256, width)
    return call(
        dispatch_kernel,
        "dispatch",
        at,
        (width // blk,),
        [fixed((1, rows)), columns(rows, blk)],
        columns(slots, blk),
        like((slots, width), BF),
        (dest_row, values),
        scratch=[pltpu.VMEM((slots, rows), BF)],
    )


def join_kernel(at_ref, *refs):
    pieces, out_ref = refs[:6], refs[6]
    r = pl.program_id(0)
    for place, piece in enumerate(in_order(at_ref[1], *[ref[...] for ref in pieces])):

        @pl.when(r == place)
        def _():
            out_ref[...] = piece


def join(at, pieces):
    each, width = pieces[0].shape
    return call(
        join_kernel,
        "join",
        at,
        (4,),
        [fixed((each, width))] * 6,
        pl.BlockSpec((each, width), lambda r, n: ((n[1] + r) % 4, 0)),
        like((4 * each, width), BF),
        pieces,
    )


def write_shares(mine, total, own_ref, one_ref, two_ref, three_ref, end_ref):
    rows = own_ref.shape[0]
    own_ref[...] = total[:rows]
    one, two, three = [total[r * rows : (r + 1) * rows].astype(BF) for r in (1, 2, 3)]
    one_ref[...] = one
    two_ref[...] = two
    three_ref[...] = three
    end_ref[...] = jnp.where(mine == 0, three, one)


def share_shapes(rows, width):
    return [like((rows, width), F32)] + [like((rows, width), BF)] * 4


def combine_kernel(count, whole, at_ref, *refs):
    dests, backs = refs[:count], refs[count : 2 * count]
    base_ref, refs, pick_s = refs[2 * count], refs[2 * count + 1 : -1], refs[-1]
    rows, slots = base_ref.shape[0], backs[0].shape[0]
    blk = rows // 4

    @pl.when(pl.program_id(0) == 0)
    def _():
        lane = lax.broadcasted_iota(jnp.int32, (blk, slots), 1)
        for k in range(count):
            for start in range(0, rows, blk):
                dest = dests[k][start : start + blk, :]
                pick_s[start : start + blk, k * slots : (k + 1) * slots] = one_hot(lane, dest)

    total = base_ref[...].astype(F32)
    for k in range(count):
        total = total + mm(pick_s[:, k * slots : (k + 1) * slots], backs[k][...])
    mine = at_ref[1]
    if whole:
        h_ref, out_ref = refs
        for r in range(4):
            part = total[r * blk : (r + 1) * blk]
            if r == 0:
                part = part + h_ref[...]
            place = pl.ds(pl.multiple_of(((mine + r) % 4) * blk, blk), blk)
            out_ref[place, :] = part.astype(BF)
    else:
        write_shares(mine, total, *refs)


def combine(at, dests, backs, base, h=None):
    count, (slots, width), rows = len(backs), backs[0].shape, base.shape[0]
    blk = min(256, width)
    whole = h is not None
    quarter = columns(rows // 4, blk)
    return call(
        partial(combine_kernel, count, whole),
        "combine",
        at,
        (width // blk,),
        [fixed((rows, 1))] * count
        + [columns(slots, blk)] * count
        + [columns(rows, blk)]
        + [quarter] * whole,
        columns(rows, blk) if whole else [quarter] * 5,
        like(base.shape, BF) if whole else share_shapes(rows // 4, width),
        (*dests, *backs, base) + ((h,) if whole else ()),
        scratch=[pltpu.VMEM((rows, count * slots), BF)],
    )


def mm_t(a, b):
    return lax.dot_general(a, b, (((1,), (1,)), ((), ())), preferred_element_type=F32)


def gelu_both(u):
    c = 0.7978845608028654
    square = u * u
    t = jnp.tanh(u * (c + (c * 0.044715) * square))
    half = 0.5 + 0.5 * t
    slope = half + (0.5 * u) * (1.0 - t * t) * (c + (3.0 * c * 0.044715) * square)
    return u * half, slope


def high_low(value):
    high = value.astype(BF)
    return high, (value - high.astype(F32)).astype(BF)


def two_coefs(logits, lane, experts):
    inside = (lane >= experts) & (lane < experts + 2)
    top = jnp.max(jnp.where(inside, logits, HIDE), axis=1, keepdims=True)
    e = jnp.where(inside, jnp.exp(logits - top), 0.0)
    e = e / jnp.sum(e, axis=1, keepdims=True)
    first = jnp.sum(jnp.where(lane == experts, e, 0.0), axis=1, keepdims=True)
    second = jnp.sum(jnp.where(lane == experts + 1, e, 0.0), axis=1, keepdims=True)
    return first, second


def small_back(d_small, rows, w_small_ref, small_ref, i):
    high, low = high_low(d_small)
    w_small = w_small_ref[...]
    high_t, low_t = high_low(d_small.T)

    @pl.when(i == 0)
    def _():
        small_ref[...] = jnp.zeros(small_ref.shape, F32)

    small_ref[...] += mm(high_t, rows) + mm(low_t, rows)
    return mm_t(high, w_small) + mm_t(low, w_small)


def expert_kernel(experts, half, at_ref, rows_ref, dy_ref, up_ref, down_ref, w_small_ref, *outs):
    if half:
        outs = outs[5:]
    rows_out_ref, hid_ref, dy_out_ref, deu_ref, y_ref, d_rows_ref, small_ref = outs
    rows = rows_ref[...]
    rows_out_ref[...] = rows
    up = mm(rows, up_ref[...])
    logits = mm(rows, w_small_ref[...])
    lane = lax.broadcasted_iota(jnp.int32, logits.shape, 1)
    routed = lane < experts
    top = jnp.max(jnp.where(routed, logits, HIDE), axis=1, keepdims=True)
    probs = jnp.where(routed, jnp.exp(logits - top), 0.0)
    probs = probs / jnp.sum(probs, axis=1, keepdims=True)
    own = jnp.where(lane == at_ref[2], 1.0, 0.0)
    gate = jnp.sum(probs * own, axis=1, keepdims=True)
    first, second = two_coefs(logits, lane, experts)
    weight = second * gate
    dy = dy_ref[...].reshape(rows.shape).astype(F32)
    d_y = (weight * dy).astype(BF)
    dy_out_ref[...] = d_y
    d_hidden = mm_t(d_y, down_ref[...])
    hidden, slope = gelu_both(up)
    hidden = hidden.astype(BF)
    hid_ref[...] = hidden
    d_up = (d_hidden * slope).astype(BF)
    deu_ref[...] = d_up
    y = mm(hidden, down_ref[...])
    y_ref[...] = (weight * y).astype(BF).reshape(y_ref.shape)
    along = gate * jnp.sum(dy * y, axis=1, keepdims=True)
    mixed = first * second * along
    d_small = (second * along) * (own - probs)
    d_small = jnp.where(routed, d_small, 0.0)
    d_small = d_small + jnp.where(lane == experts + 1, mixed, 0.0)
    d_small = d_small - jnp.where(lane == experts, mixed, 0.0)
    d_rows = mm_t(d_up, up_ref[...]) + small_back(d_small, rows, w_small_ref, small_ref, pl.program_id(0))
    d_rows_ref[...] = d_rows.astype(BF)


def expert_rows(at, rows, dy, w_up, w_down, w_small, experts, half, before):
    count, width = rows.shape
    hid, lanes = w_up.shape[1], w_small.shape[1]
    blk = min(256, count)
    capacity = count // dy.shape[0]
    steps = count // blk
    moving = pl.BlockSpec((blk, width), lambda i, n: (i, 0))
    slots = pl.BlockSpec((blk // capacity, capacity, width), lambda i, n: (i, half, 0))
    kept = [pl.BlockSpec((blk, size), lambda i, n: (i + half * steps, 0)) for size in (width, hid, width, hid)]
    return call(
        partial(expert_kernel, experts, half),
        "expert_rows",
        at,
        (steps,),
        [
            moving,
            slots,
            fixed((width, hid)),
            fixed((hid, width)),
            fixed((width, lanes)),
        ]
        + [pl.BlockSpec(memory_space=pl.ANY)] * (5 * half),
        kept + [slots, moving, fixed((lanes, width))],
        [like((2 * count, size), BF) for size in (width, hid, width, hid)]
        + [like(dy.shape, BF), like((count, width), BF)]
        + [like((lanes, width), F32)],
        (rows, dy, w_up, w_down, w_small, *before),
        alias={6 + k: k for k in range(5)} if half else None,
        vmem=34,
    )


def dense_kernel(experts, at_ref, rows_ref, dy_ref, in_ref, out_ref, w_small_ref, *outs):
    hid_ref, grad_ref, d_up_ref, mix_ref, db_ref, small_ref = outs
    rows = rows_ref[...]
    up = mm(rows, in_ref[...])
    logits = mm(rows, w_small_ref[...])
    lane = lax.broadcasted_iota(jnp.int32, logits.shape, 1)
    first, second = two_coefs(logits, lane, experts)
    dy = dy_ref[...].astype(F32)
    grad = (first * dy).astype(BF)
    grad_ref[...] = grad
    d_hidden = mm_t(grad, out_ref[...])
    hidden, slope = gelu_both(up)
    hidden = hidden.astype(BF)
    hid_ref[...] = hidden
    d_up = (d_hidden * slope).astype(BF)
    d_up_ref[...] = d_up
    dense = mm(hidden, out_ref[...])
    mix_ref[...] = first * dense
    mixed = first * second * jnp.sum(dy * dense, axis=1, keepdims=True)
    d_small = jnp.where(lane == experts, mixed, 0.0) - jnp.where(lane == experts + 1, mixed, 0.0)
    db_ref[...] = mm_t(d_up, in_ref[...]) + small_back(d_small, rows, w_small_ref, small_ref, pl.program_id(0))


def dense_rows(at, rows, dy, w_in, w_out, w_small, experts):
    (count, width), hid, lanes = rows.shape, w_in.shape[1], w_small.shape[1]
    blk = min(256, count)
    row_out = pl.BlockSpec((blk, width), lambda i, n: (i, 0))
    hid_out = pl.BlockSpec((blk, hid), lambda i, n: (i, 0))
    return call(
        partial(dense_kernel, experts),
        "dense_rows",
        at,
        (count // blk,),
        [row_out, row_out, fixed((width, hid)), fixed((hid, width)), fixed((width, lanes))],
        [hid_out, row_out, hid_out, row_out, row_out, fixed((lanes, width))],
        [
            like((count, hid), BF),
            like((count, width), BF),
            like((count, hid), BF),
            like((count, width), F32),
            like((count, width), F32),
            like((lanes, width), F32),
        ],
        (rows, dy, w_in, w_out, w_small),
        vmem=34,
    )


def turned(value):
    return value.astype(F32).T.astype(BF)


def dense_grads_kernel(at_ref, b_ref, d_up_ref, grad_ref, hid_ref, keep_ref, give_ref):
    width = d_up_ref.shape[1]
    first = mm(turned(b_ref[...]), d_up_ref[...]).astype(BF)
    second = mm(turned(grad_ref[...]), hid_ref[...]).astype(BF)
    half = pl.num_programs(0) // 2
    for side, ref in ((0, keep_ref), (1, give_ref)):

        @pl.when(pl.program_id(0) // half == side)
        def _():
            ref[0, :, :width] = first
            ref[0, :, width:] = second


def dense_grads(at, b, d_up, grad, hidden, parts):
    (rows, width), hid = b.shape, hidden.shape[1]
    own, half, bits = width // parts, parts // 2, parts.bit_length() - 1

    def part(q, n):
        turned_q = sum([((q // 2**k) % 2) * 2 ** (bits - 1 - k) for k in range(bits)])
        return turned_q ^ n[2]

    column = pl.BlockSpec((rows, own), lambda q, n: (0, part(q, n)))
    shape = (1, own, 2 * hid)
    return call(
        dense_grads_kernel,
        "dense_grads",
        at,
        (parts,),
        [column, fixed((rows, hid)), column, fixed((rows, hid))],
        [
            pl.BlockSpec(shape, lambda q, n: (jnp.minimum(q, half - 1), 0, 0)),
            pl.BlockSpec(shape, lambda q, n: (jnp.maximum(q - half, 0), 0, 0)),
        ],
        [like((half, own, 2 * hid), BF)] * 2,
        (b, d_up, grad, hidden),
    )


def attention_grads_kernel(experts, at_ref, *refs):
    grads, o_refs, refs = refs[:GROUP], refs[GROUP : GROUP + 6], refs[GROUP + 6 :]
    a_ref, dh_ref, w_ref, gain_ref, bias_ref, sums_ref = refs[:6]
    small_refs, (out_ref, all_s) = refs[6:-2], refs[-2:]
    heads, features = GROUP * HD, grads[1].shape[0]
    products, plain = 0.0, 0.0
    for k in range(GROUP):
        head = at_ref[0] ^ k
        rows = pl.ds(pl.multiple_of(head * features, features), features)
        grad = grads[k][...]
        weight = w_ref[head].astype(F32)
        total = mm(grad, a_ref[...])
        all_s[rows, :] = total
        each = jnp.sum(grad.astype(F32), axis=1, keepdims=True)
        products = products + jnp.sum(total * weight, axis=0, keepdims=True)
        plain = plain + jnp.sum(each * weight, axis=0, keepdims=True)
    first = GROUP * features
    for r, piece in enumerate(in_order(at_ref[1], *[ref[...] for ref in o_refs])):
        rows = pl.ds(pl.multiple_of(first + ((at_ref[1] + r) % 4) * heads, heads), heads)
        all_s[rows, :] = mm(piece, dh_ref[...])
    first += 4 * heads
    small = add_up(small_refs)
    row = lax.broadcasted_iota(jnp.int32, small.shape, 0)
    d_gain = (products - bias_ref[...] * plain) / gain_ref[...]
    for k, sums in enumerate((sums_ref[0:1, :], sums_ref[1:2, :], d_gain, plain)):
        small = jnp.where(row == experts + 2 + k, sums, small)
    all_s[first:, :] = small
    out_ref[...] = all_s[...].T.astype(BF)


def attention_grads(at, grads, o, a, dh, w_heads, gain, bias, sums, small, experts):
    rows, width = a.shape
    features, lanes = grads[0].shape[0], small[0].shape[0]
    piece = pl.BlockSpec((o[0].shape[0], dh.shape[0]), lambda i, n: (0, n[1]))
    height = GROUP * features + 4 * o[0].shape[0] + lanes
    blk = min(256, width)
    return call(
        partial(attention_grads_kernel, experts),
        "attention_grads",
        at,
        (width // blk,),
        [fixed((features, rows))] * GROUP
        + [piece] * 6
        + [columns(rows, blk), columns(dh.shape[0], blk)]
        + [pl.BlockSpec((GROUP, features, blk), lambda i, n: (0, 0, i))]
        + [columns(1, blk)] * 2
        + [columns(2, blk)]
        + [columns(lanes, blk)] * len(small),
        pl.BlockSpec((blk, height), lambda i, n: (i, 0)),
        like((width, height), BF),
        (*grads, *o, a, dh, w_heads, gain, bias, sums, *small),
        scratch=[pltpu.VMEM((height, blk), F32)],
    )


def project_kernel(at_ref, *refs):
    grads, w_ref, outs, turned_s = refs[:GROUP], refs[GROUP], refs[GROUP + 1 : -1], refs[-1]
    rows = turned_s.shape[1]
    blk = rows // 4

    @pl.when(pl.program_id(0) == 0)
    def _():
        for s in range(GROUP):
            for r in range(4):
                lanes = pl.ds(pl.multiple_of(((at_ref[1] + r) % 4) * blk, blk), blk)
                turned_s[s, r * blk : (r + 1) * blk, :] = turned(grads[s][:, lanes])

    total = 0.0
    for s in range(GROUP):
        total = total + mm(turned_s[s], w_ref[at_ref[0] ^ s])
    write_shares(at_ref[1], total, *outs)


def project_back(at, grads, w_heads):
    features, rows = grads[0].shape
    width = w_heads.shape[2]
    blk = min(256, width)
    return call(
        project_kernel,
        "project_back",
        at,
        (width // blk,),
        [fixed((features, rows))] * GROUP
        + [pl.BlockSpec((GROUP, features, blk), lambda i, n: (0, 0, i))],
        [columns(rows // 4, blk)] * 5,
        share_shapes(rows // 4, width),
        (*grads, w_heads),
        scratch=[pltpu.VMEM((GROUP, rows, features), BF)],
    )


def hop(value, *pairs):
    return lax.ppermute(value, "mp", pairs)


def rotate(value, steps):
    return hop(value, *[(s, (s + steps) % 4) for s in range(4)])


def gather_near(own):
    right = hop(own, (0, 1), (1, 2), (2, 3))
    left = hop(own, (1, 0), (2, 1), (3, 2))
    return own, right, left, hop(own, (0, 3), (3, 0))


def gather_far(near):
    _, right, left, _ = near
    return *near, hop(right, (1, 2), (2, 3)), hop(left, (1, 0), (2, 1))


def gather_pieces(own):
    return gather_far(gather_near(own))


def scatter_far(shares):
    _, _, two, _, end = shares
    return hop(two, (2, 1), (3, 2)), hop(two, (0, 1), (1, 2)), hop(end, (0, 3), (3, 0))


def scatter_near(shares, came):
    own, one, _, three, _ = shares
    from_right, from_left, from_end = came
    three = (three.astype(F32) + from_right.astype(F32)).astype(BF)
    one = (one.astype(F32) + from_left.astype(F32)).astype(BF)
    return own, hop(three, (1, 0), (2, 1), (3, 2)), hop(one, (0, 1), (1, 2), (2, 3)), from_end


def group_swap(value, s):
    count = lax.axis_size("dp")
    return lax.ppermute(value, "dp", [(t, t ^ s) for t in range(count)])


def expert_swap(value, experts):
    wide = value.reshape(experts, value.shape[0] // experts, value.shape[1])
    return lax.all_to_all(wide, "dp", 0, 0, tiled=True).reshape(value.shape)


def roll_rows(value, start):
    twice = jnp.concatenate([value, value], axis=0)
    return lax.dynamic_slice_in_dim(twice, start, value.shape[0], 0)


def add_halves(keep, came):
    return (keep.astype(F32) + came.astype(F32)).astype(BF)


def body(
    tokens,
    cotangent,
    ln_gains,
    ln_biases,
    w_qkv,
    w_o,
    w_in,
    w_out,
    w_router,
    w_coef,
    w_up,
    w_down,
    routes,
    long_group,
):
    rows, width = tokens.shape
    dps = lax.axis_size("dp")
    mine, position = lax.axis_index("mp"), lax.axis_index("dp")
    quarter = rows // 4
    start = mine * quarter
    heads_loc = w_qkv.shape[2] // HD
    hid = w_in.shape[1]
    experts = w_router.shape[1]
    capacity = max(2, 2 * rows // experts)
    half = capacity // 2
    barrier = lax.optimization_barrier
    first_len = lax.dynamic_index_in_dim(long_group, position // GROUP, 0, keepdims=False)
    at = jnp.stack([position % GROUP, mine, position, first_len]).astype(jnp.int32)
    gains = [ln_gains[0:1], ln_gains[1:2]]
    biases = [ln_biases[0:1], ln_biases[1:2]]
    w_o_all = lax.all_gather(w_o, "mp", axis=0, tiled=True)

    w_heads = w_qkv.reshape(width, 3, heads_loc, HD).transpose(2, 1, 3, 0)
    w_heads = w_heads.reshape(heads_loc, 3 * HD, width)
    a_r, *qkv = project(at, tokens, gains[0], biases[0], w_heads)
    qkv = [qkv[0]] + [group_swap(qkv[s], s) for s in (1, 2, 3)]

    route = roll_rows(routes, start)[:, 0]
    picked = (route[:, None] == jnp.arange(experts, dtype=jnp.int32)[None, :]).astype(jnp.int32)
    slot = jnp.sum((jnp.cumsum(picked, axis=0) - picked) * picked, axis=1)
    dy_b = roll_rows(cotangent, start)
    send_dy = dispatch(at, (route * capacity + slot)[None, :], dy_b, experts * capacity)
    *qkv, send_dy = barrier((*qkv, send_dy))
    in_half = [slot < half, slot >= half]
    dests = [
        jnp.where(in_half[k], route * half + slot - k * half, -1).astype(jnp.int32) for k in (0, 1)
    ]

    *o_t, lse = attend(at, qkv)
    *o_t, w_o_all = barrier((*o_t, w_o_all))
    o_heads = [o_t[0]] + [group_swap(o_t[s], s) for s in (1, 2, 3)]
    lanes = -(-(experts + 2) // 128) * 128
    w_small = jnp.concatenate(
        [w_router, w_coef, jnp.zeros((width, lanes - experts - 2), BF)], axis=1
    )
    *o_heads, send_dy, w_small = barrier((*o_heads, send_dy, w_small))
    got_dy = expert_swap(send_dy, experts).reshape(experts, capacity, width)
    o_pieces = gather_pieces(stack(at, o_heads))
    h, b_r = mid(at, o_pieces, w_o_all, tokens, gains[1], biases[1])

    send_0 = dispatch(at, dests[0][None, :], b_r, experts * half)
    send_0, got_dy = barrier((send_0, got_dy))
    got_0 = expert_swap(send_0, experts)
    send_1 = dispatch(at, dests[1][None, :], b_r, experts * half)
    b_r, send_1 = barrier((b_r, send_1))
    hidden, dense_grad, d_up, mix_base, db_base, small_t = dense_rows(
        at, b_r, dy_b, w_in, w_out, w_small, experts
    )
    send_1, got_0, db_base = barrier((send_1, got_0, db_base))
    got_1 = expert_swap(send_1, experts)

    *kept, d_rows_0, small_0 = expert_rows(
        at, got_0, got_dy, w_up[0], w_down[0], w_small, experts, 0, ()
    )
    back_0 = expert_swap(d_rows_0, experts)
    *kept, d_rows_1, small_1 = expert_rows(
        at, got_1, got_dy, w_up[0], w_down[0], w_small, experts, 1, kept
    )
    got, hidden_e, d_y, d_eu, back_y = kept
    back_1 = expert_swap(d_rows_1, experts)
    d_rows_1, b_r = barrier((d_rows_1, b_r))
    halving = width == dps * 128
    if halving:
        grads = dense_grads(at, b_r, d_up, dense_grad, hidden, dps)
    else:
        grads = [ein("td,tf->df", b_r, d_up).astype(BF), ein("td,tf->df", dense_grad, hidden).astype(BF)]
    back_0, back_1, back_y, *grads = barrier((back_0, back_1, back_y, *grads))

    dest_cols = [dest[:, None] for dest in dests]
    tok_y = expert_swap(back_y.reshape(experts * capacity, width), experts)
    shares = combine(at, dest_cols, [back_0, back_1], db_base)
    far = scatter_far(shares)
    *far, g_0, g_1 = barrier((*far, *grads))
    grads = [g_0, g_1]
    shares = scatter_near(shares, far)

    mix = combine(at, [(route * capacity + slot)[:, None]], [tok_y], mix_base, h)
    *shares, mix = barrier((*shares, mix))
    output = lax.psum(mix, "mp")
    dh, dh_r, sums_2, *do_q = mid_back(at, shares, w_o_all, h, dy_b[:quarter], gains[1])
    do_q = [do_q[0]] + [rotate(do_q[r], -r) for r in (1, 2, 3)]
    do_heads = unsplit(at, do_q)
    do_t = [do_heads[0]] + [group_swap(do_heads[s], s) for s in (1, 2, 3)]
    if halving:
        came_1 = group_swap(grads[1], 1)
    d_qkv = attend_back(at, qkv, do_t, o_t, lse)
    if not halving:
        grads = [lax.psum_scatter(grad, "dp", scatter_dimension=0, tiled=True) for grad in grads]

    d_own, got, hidden_e, d_y, d_eu = barrier((d_qkv[0], got, hidden_e, d_y, d_eu))
    d_qkv = [d_own] + [group_swap(d_qkv[s], s) for s in (1, 2, 3)]
    grad_down = ein("rf,rd->fd", hidden_e, d_y)
    if halving:
        *d_qkv, grad_down, came_1 = barrier((*d_qkv, grad_down, came_1))
        half = dps // 4
        came_2 = group_swap(add_halves(grads[0][half:], came_1[half:]), 2)
        grads = add_halves(add_halves(grads[0][:half], came_1[:half]), came_2)
        bit = 4
        while bit < dps:
            half = grads.shape[0] // 2
            grads = add_halves(grads[:half], group_swap(grads[half:], bit))
            bit *= 2
        grads = [grads[0][:, :hid], grads[0][:, hid:]]
    else:
        *d_qkv, grad_down = barrier((*d_qkv, grad_down))
    shares = project_back(at, d_qkv, w_heads)
    far = scatter_far(shares)
    grads_a = attention_grads(
        at, d_qkv, o_pieces, a_r, dh_r, w_heads, gains[0], biases[0], sums_2, (small_0, small_1, small_t), experts
    )
    grad_up = ein("rd,rf->df", got, d_eu)
    grads_a, output, grad_up, *far = barrier((grads_a, output, grad_up, *far))
    grads_a = lax.psum_scatter(grads_a, "dp", scatter_dimension=0, tiled=True).T
    shares = scatter_near(shares, far)
    grad_q = first_back(at, shares, tokens, dh, gains[0])
    grad_tokens = join(at, gather_pieces(grad_q))

    own, heads = width // dps, heads_loc * HD
    grad_qkv = grads_a[: 3 * heads].astype(F32).reshape(heads_loc, 3, HD, own).transpose(3, 1, 0, 2)
    grad_qkv = grad_qkv.reshape(own, 3, heads)
    grad_in = grads[0].astype(F32)
    grad_out = grads[1].astype(F32).T
    rest = grads_a[3 * heads : 7 * heads].reshape(4, heads, own)
    small = jnp.broadcast_to(grads_a[7 * heads :], (4, lanes, own))
    rest = lax.all_to_all(jnp.concatenate([rest, small], axis=1), "mp", 0, 0, tiled=True)
    rest = jnp.sum(rest.astype(F32), axis=0)
    grad_o, small = rest[:heads], rest[heads:]
    small_out = small[: experts + 2].T
    return (
        output,
        grad_tokens,
        jnp.stack([small[experts + 4], small[experts + 2]]),
        jnp.stack([small[experts + 5], small[experts + 3]]),
        grad_qkv,
        grad_o,
        grad_in,
        grad_out,
        small_out[:, :experts],
        small_out[:, experts:],
        grad_up[None],
        grad_down[None],
    )


def solution(mesh):
    in_specs = (
        P("dp", None),
        P("dp", None),
        P(),
        P(),
        P(None, None, "mp"),
        P("mp", None),
        P(None, "mp"),
        P("mp", None),
        P(),
        P(),
        P("dp", None, "mp"),
        P("dp", "mp", None),
        P("dp", None),
        P(),
    )
    out_specs = (
        P("dp", None),
        P("dp", None),
        P(None, "dp"),
        P(None, "dp"),
        P("dp", None, "mp"),
        P("mp", "dp"),
        P("dp", "mp"),
        P("mp", "dp"),
        P("dp", None),
        P("dp", None),
        P("dp", None, "mp"),
        P("dp", "mp", None),
    )
    return jax.shard_map(body, mesh=mesh, in_specs=in_specs, out_specs=out_specs, check_vma=False)
```

```python
from functools import partial

import jax
import jax.numpy as jnp
from jax import lax
from jax.experimental import pallas as pl
from jax.experimental.pallas import tpu as pltpu
from jax.sharding import PartitionSpec as P

HD = 64
GROUP = 4
EPS = 1e-05
LOG2E = 1.4426950408889634
SCALE2 = 0.125 * LOG2E
HIDE = -1e30
BF = jnp.bfloat16
F32 = jnp.float32
LIGHT = pl.CostEstimate(flops=1 << 20, bytes_accessed=1 << 20, transcendentals=0)


def mm(a, b):
    return jnp.dot(a, b, preferred_element_type=F32)


def ein(spec, a, b):
    return jnp.einsum(spec, a, b, preferred_element_type=F32)


def call(kernel, name, prefetch, grid, in_specs, out_specs, out_shape, args, scratch=(), alias=None, vmem=48):
    return pl.pallas_call(
        kernel,
        grid_spec=pltpu.PrefetchScalarGridSpec(
            num_scalar_prefetch=1,
            grid=grid,
            in_specs=in_specs,
            out_specs=out_specs,
            scratch_shapes=list(scratch),
        ),
        out_shape=out_shape,
        input_output_aliases=alias or {},
        compiler_params=pltpu.CompilerParams(vmem_limit_bytes=vmem * 2**20),
        cost_estimate=LIGHT,
        name=name,
    )(prefetch, *args)


def fixed(shape):
    zeros = (0,) * len(shape)
    return pl.BlockSpec(shape, lambda *_: zeros)


def like(shape, dtype):
    return jax.ShapeDtypeStruct(shape, dtype)


def normalize(v):
    mean = jnp.mean(v, axis=-1, keepdims=True)
    centred = v - mean
    scale = lax.rsqrt(jnp.mean(centred * centred, axis=-1, keepdims=True) + EPS)
    return centred * scale, scale


def norm_back(grad, gain, normal, scale):
    g = grad * gain
    along = jnp.mean(g * normal, axis=-1, keepdims=True)
    return scale * (g - jnp.mean(g, axis=-1, keepdims=True) - normal * along)


def qkv_kernel(at_ref, x_ref, gain_ref, bias_ref, w_ref, a_ref, *outs):
    normal, _ = normalize(x_ref[...].astype(F32))
    a = (normal * gain_ref[...] + bias_ref[...]).astype(BF)
    a_ref[...] = a
    for s in range(GROUP):
        outs[s][...] = mm_t(w_ref[at_ref[0] ^ s], a).astype(BF)


def project(at, tokens, gain, bias, w_heads):
    rows, width = tokens.shape
    features = w_heads.shape[1]
    blk = min(256, rows)
    moving = pl.BlockSpec((blk, width), lambda i, n: (i, 0))
    return call(
        qkv_kernel,
        "project",
        at,
        (rows // blk,),
        [moving, fixed((1, width)), fixed((1, width)), fixed(w_heads.shape)],
        [moving] + [pl.BlockSpec((features, blk), lambda i, n: (0, i))] * GROUP,
        [like((rows, width), BF)] + [like((features, rows), BF)] * GROUP,
        (tokens, gain, bias, w_heads),
    )


def fill_keys(k_s, place, keys, first_len, blk):
    rows = place * blk + lax.broadcasted_iota(jnp.int32, (blk, 128), 0)
    lane = lax.broadcasted_iota(jnp.int32, (blk, 128), 1)
    wide = jnp.concatenate([keys.astype(F32).T, jnp.zeros((blk, 128 - HD), F32)], axis=1)
    wide = jnp.where((lane == HD) & (rows < first_len), HIDE, wide)
    k_s[pl.ds(place * blk, blk), :] = wide.astype(BF)


def wide_query(query, place, first_len, blk):
    cols = place * blk + lax.broadcasted_iota(jnp.int32, (128 - HD, blk), 1)
    sub = lax.broadcasted_iota(jnp.int32, (128 - HD, blk), 0)
    extra = jnp.where((sub == 0) & (cols >= first_len), 1.0, 0.0)
    return jnp.concatenate([query, extra.astype(BF)], axis=0)


def causal(blk):
    keys = lax.broadcasted_iota(jnp.int32, (blk, blk), 0)
    queries = lax.broadcasted_iota(jnp.int32, (blk, blk), 1)
    return keys <= queries


def attend_kernel(blk, per, at_ref, *refs):
    qkv_refs, o_refs = refs[:GROUP], refs[GROUP : 2 * GROUP]
    lse_ref, k_s, qkv_s = refs[2 * GROUP :]
    i = pl.program_id(0)
    place, first_len = at_ref[0], at_ref[3]

    @pl.when(i == 0)
    def _():
        for s in range(GROUP):
            qkv_s[place ^ s] = qkv_refs[s][...]

    def part(which, j):
        return qkv_s[j // per, HD * which : HD * (which + 1), pl.ds((j % per) * blk, blk)]

    fill_keys(k_s, i, part(1, i), first_len, blk)
    query = wide_query(part(0, i), i, first_len, blk)

    def scores(j):
        return mm(k_s[pl.ds(pl.multiple_of(j * blk, blk), blk), :], query)

    s = jnp.where(causal(blk), scores(i), HIDE)
    top = jnp.max(s, axis=0, keepdims=True)
    p = jnp.exp2((s - top) * SCALE2)
    total = jnp.sum(p, axis=0, keepdims=True)
    acc = mm(part(2, i), p.astype(BF))

    def steps(blocks, carry):
        top, total, acc = carry
        s = [scores(j) for j in blocks]
        new = top
        for one in s:
            new = jnp.maximum(new, jnp.max(one, axis=0, keepdims=True))
        keep = jnp.exp2((top - new) * SCALE2)
        total, acc = total * keep, acc * keep
        for j, one in zip(blocks, s):
            p = jnp.exp2((one - new) * SCALE2)
            total = total + jnp.sum(p, axis=0, keepdims=True)
            acc = acc + mm(part(2, j), p.astype(BF))
        return new, total, acc

    low = jnp.where(i * blk >= first_len, first_len // blk, 0)
    pairs = (i - low) // 2
    carry = lax.fori_loop(
        0, pairs, lambda t, c: steps([low + 2 * t, low + 2 * t + 1], c), (top, total, acc)
    )
    top, total, acc = lax.fori_loop(low + 2 * pairs, i, lambda j, c: steps([j], c), carry)
    out = (acc / total).astype(BF)
    for s in range(GROUP):

        @pl.when((i // per) ^ place == s)
        def _():
            o_refs[s][:, pl.ds((i % per) * blk, blk)] = out

    lse_ref[0] = top * SCALE2 + jnp.log2(total)


def attend(at, qkv):
    features, rows = qkv[0].shape
    blk = min(512, rows)
    per = rows // blk
    count = GROUP * per
    return call(
        partial(attend_kernel, blk, per),
        "attend",
        at,
        (count,),
        [fixed((features, rows))] * GROUP,
        [fixed((HD, rows))] * GROUP + [pl.BlockSpec((1, 1, blk), lambda i, n: (i, 0, 0))],
        [like((HD, rows), BF)] * GROUP + [like((count, 1, blk), F32)],
        qkv,
        scratch=[pltpu.VMEM((GROUP * rows, 128), BF), pltpu.VMEM((GROUP, features, rows), BF)],
    )


def back_kernel(blk, per, count, at_ref, *refs):
    qkv_refs, do_refs, o_refs = refs[:GROUP], refs[GROUP : 2 * GROUP], refs[2 * GROUP : 3 * GROUP]
    lse_ref, refs = refs[3 * GROUP], refs[3 * GROUP + 1 :]
    out_refs, refs = refs[:GROUP], refs[GROUP:]
    dq_ref, out_ref, k_s, kt_s, v_s, wide_s, dot_s, both_s, delta_s, acc_s = refs
    j = pl.program_id(0)
    place, first_len = at_ref[0], at_ref[3]

    @pl.when(j == 0)
    def _():
        dq_ref[...] = jnp.zeros(dq_ref.shape, F32)
        zero = jnp.zeros((blk, HD), F32)
        for s in range(GROUP):
            for sub in range(per):
                i = (place ^ s) * per + sub
                at = pl.ds(pl.multiple_of(i * blk, blk), blk)
                cut = slice(sub * blk, (sub + 1) * blk)
                query = qkv_refs[s][0:HD, cut]
                keys = qkv_refs[s][HD : 2 * HD, cut]
                grad = do_refs[s][:, cut]
                fill_keys(k_s, i, keys, first_len, blk)
                kt_s[:, at] = keys
                dot_s[:, at] = grad
                wide_s[:, at] = wide_query(query, i, first_len, blk)
                grad = grad.astype(F32)
                values = qkv_refs[s][2 * HD :, cut].astype(F32)
                v_s[at, :] = jnp.concatenate([values.T, zero], axis=1).astype(BF)
                both_s[0, at, :] = jnp.concatenate([grad.T, zero], axis=1).astype(BF)
                both_s[1, at, :] = jnp.concatenate([zero, query.astype(F32).T], axis=1).astype(BF)
                held = o_refs[s][:, cut].astype(F32)
                delta_s[i] = jnp.sum(held * grad, axis=0, keepdims=True)

    here = pl.ds(pl.multiple_of(j * blk, blk), blk)
    keys_t = kt_s[:, here]
    values = v_s[here, 0:HD]

    def pair(i, diagonal):
        at = pl.ds(pl.multiple_of(i * blk, blk), blk)
        s = mm(k_s[here, :], wide_s[:, at])
        p = jnp.exp2(s * SCALE2 - lse_ref[i])
        if diagonal:
            p = jnp.where(causal(blk), p, 0.0)
        dp = mm(values, dot_s[:, at])
        ds = (p * (dp - delta_s[i])).astype(BF)
        return mm(p.astype(BF), both_s[0, at, :]) + mm(ds, both_s[1, at, :]), mm(keys_t, ds)

    acc_s[...], dq = pair(j, True)
    dq_ref[:, here] += dq

    def step_two(t, carry):
        i = j + 1 + 2 * t
        (kv_0, dq_0), (kv_1, dq_1) = pair(i, False), pair(i + 1, False)
        acc_s[...] += kv_0 + kv_1
        at = pl.ds(pl.multiple_of(i * blk, blk), 2 * blk)
        dq_ref[:, at] += jnp.concatenate([dq_0, dq_1], axis=1)
        return carry

    def step(i, carry):
        kv, dq = pair(i, False)
        acc_s[...] += kv
        dq_ref[:, pl.ds(pl.multiple_of(i * blk, blk), blk)] += dq
        return carry

    high = jnp.where((j + 1) * blk <= first_len, (first_len + blk - 1) // blk, count)
    pairs = (high - j - 1) // 2
    lax.fori_loop(0, pairs, step_two, 0)
    lax.fori_loop(j + 1 + 2 * pairs, high, step, 0)
    both = acc_s[...].T
    out_ref[0:HD, :] = (dq_ref[:, here] * 0.125).astype(BF)
    out_ref[HD : 2 * HD, :] = (both[HD:, :] * 0.125).astype(BF)
    out_ref[2 * HD :, :] = both[:HD, :].astype(BF)
    for s in range(GROUP):

        @pl.when((j // per) ^ place == s)
        def _():
            out_refs[s][:, pl.ds(pl.multiple_of((j % per) * blk, blk), blk)] = out_ref[...]


def attend_back(at, qkv, do, o, lse):
    features, rows = qkv[0].shape
    blk = min(512, rows)
    per = rows // blk
    count = GROUP * per
    return call(
        partial(back_kernel, blk, per, count),
        "attend_back",
        at,
        (count,),
        [fixed((features, rows))] * GROUP
        + [fixed((HD, rows))] * (2 * GROUP)
        + [fixed((count, 1, blk))],
        [fixed((features, rows))] * GROUP,
        [like((features, rows), BF)] * GROUP,
        (*qkv, *do, *o, lse),
        scratch=[
            pltpu.VMEM((HD, GROUP * rows), F32),
            pltpu.VMEM((features, blk), BF),
            pltpu.VMEM((GROUP * rows, 128), BF),
            pltpu.VMEM((HD, GROUP * rows), BF),
            pltpu.VMEM((GROUP * rows, 128), BF),
            pltpu.VMEM((128, GROUP * rows), BF),
            pltpu.VMEM((HD, GROUP * rows), BF),
            pltpu.VMEM((2, GROUP * rows, 128), BF),
            pltpu.VMEM((count, 1, blk), F32),
            pltpu.VMEM((blk, 128), F32),
        ],
    )


def stack_kernel(at_ref, *refs):
    ins, out_ref = refs[:GROUP], refs[GROUP]
    for s in range(GROUP):
        head = pl.ds(pl.multiple_of((at_ref[0] ^ s) * HD, HD), HD)
        out_ref[head, :] = ins[s][...]


def stack(at, heads):
    rows = heads[0].shape[1]
    return call(
        stack_kernel,
        "stack",
        at,
        (1,),
        [fixed((HD, rows))] * GROUP,
        fixed((GROUP * HD, rows)),
        like((GROUP * HD, rows), BF),
        heads,
    )


def unsplit_kernel(at_ref, *refs):
    ins, outs = refs[:4], refs[4:]
    cols = ins[0].shape[1]
    for r in range(4):
        lanes = pl.ds(pl.multiple_of(((at_ref[1] + r) % 4) * cols, cols), cols)
        for s in range(GROUP):
            head = pl.ds(pl.multiple_of((at_ref[0] ^ s) * HD, HD), HD)
            outs[s][:, lanes] = ins[r][head, :]


def unsplit(at, pieces):
    shape = (HD, 4 * pieces[0].shape[1])
    return call(
        unsplit_kernel,
        "unsplit",
        at,
        (1,),
        [fixed(pieces[0].shape)] * 4,
        [fixed(shape)] * GROUP,
        [like(shape, BF)] * GROUP,
        pieces,
    )


def heads_of(mine, r, features):
    return pl.ds(pl.multiple_of(((mine + 4 - r) % 4) * features, features), features)


def mid_kernel(at_ref, *refs):
    pieces, (w_ref, x_ref, gain_ref, bias_ref, h_ref, b_ref) = refs[:6], refs[6:]
    h = x_ref[...].astype(F32)
    for r, piece in enumerate(in_order(at_ref[1], *[ref[...] for ref in pieces])):
        rows = heads_of(at_ref[1], 4 - r, piece.shape[0])
        h = h + mm(turned(piece), w_ref[rows, :])

    @pl.when(pl.program_id(0) == 0)
    def _():
        h_ref[...] = h

    normal, _ = normalize(h)
    b_ref[...] = (normal * gain_ref[...] + bias_ref[...]).astype(BF)


def mid(at, pieces, w_o, tokens, gain, bias):
    features, rows = pieces[0].shape
    width, quarter = tokens.shape[1], rows // 4
    return call(
        mid_kernel,
        "mid",
        at,
        (4,),
        [pl.BlockSpec((features, quarter), lambda q, n: (0, (n[1] + q) % 4))] * 6
        + [fixed(w_o.shape)]
        + [pl.BlockSpec((quarter, width), lambda q, n: ((n[1] + q) % 4, 0))]
        + [fixed((1, width))] * 2,
        [fixed((quarter, width)), pl.BlockSpec((quarter, width), lambda q, n: (q, 0))],
        [like((quarter, width), F32), like((rows, width), BF)],
        (*pieces, w_o, tokens, gain, bias),
    )


def add_up(refs):
    total = refs[0][...]
    for ref in refs[1:]:
        total = total + ref[...].astype(F32)
    return total


def mid_back_kernel(at_ref, *refs):
    shares, (w_ref, h_ref, dy_ref, gain_ref, dh_ref, low_ref, sums_ref) = refs[:4], refs[4:11]
    do_refs = refs[11:]
    db = add_up(shares)
    normal, scale = normalize(h_ref[...])
    dh = dy_ref[...].astype(F32) + norm_back(db, gain_ref[...], normal, scale)
    dh_ref[...] = dh
    low = dh.astype(BF)
    low_ref[...] = low
    sums_ref[0:1, :] = jnp.sum(db * normal, axis=0, keepdims=True)
    sums_ref[1:2, :] = jnp.sum(db, axis=0, keepdims=True)
    for r in range(4):
        rows = heads_of(at_ref[1], r, do_refs[r].shape[0])
        do_refs[r][...] = mm_t(w_ref[rows, :], low).astype(BF)


def mid_back(at, shares, w_o, h, dy, gain):
    quarter, width = h.shape
    whole = fixed((quarter, width))
    piece = (w_o.shape[0] // 4, quarter)
    return call(
        mid_back_kernel,
        "mid_back",
        at,
        (1,),
        [whole] * 4 + [fixed(w_o.shape), whole, whole, fixed((1, width))],
        [whole] * 2 + [fixed((2, width))] + [fixed(piece)] * 4,
        [like((quarter, width), F32), like((quarter, width), BF), like((2, width), F32)]
        + [like(piece, BF)] * 4,
        (*shares, w_o, h, dy, gain),
    )


def first_back_kernel(at_ref, *refs):
    shares = refs[:4]
    x_ref, dh_ref, gain_ref, out_ref = refs[4:]
    d_a = add_up(shares)
    normal, scale = normalize(x_ref[...].astype(F32))
    out_ref[...] = (dh_ref[...] + norm_back(d_a, gain_ref[...], normal, scale)).astype(BF)


def first_back(at, shares, tokens, dh, gain):
    quarter, width = dh.shape
    return call(
        first_back_kernel,
        "first_back",
        at,
        (1,),
        [fixed((quarter, width))] * 4
        + [pl.BlockSpec((quarter, width), lambda i, n: (n[1], 0))]
        + [fixed((quarter, width)), fixed((1, width))],
        fixed((quarter, width)),
        like((quarter, width), BF),
        (*shares, tokens, dh, gain),
    )


def in_order(mine, own, right, left, far, right_two, left_two):
    one = jnp.where(mine == 3, far, left)
    two = jnp.where(mine < 2, left_two, right_two)
    three = jnp.where(mine == 0, far, right)
    return own, one, two, three


def one_hot(slots, dest):
    return jnp.where(slots == dest, 1.0, 0.0).astype(BF)


def dispatch_kernel(at_ref, dest_ref, rows_ref, out_ref, spread_s):
    blk, rows = min(256, spread_s.shape[0]), dest_ref.shape[1]

    @pl.when(pl.program_id(0) == 0)
    def _():
        slot = lax.broadcasted_iota(jnp.int32, (blk, rows), 0)
        for start in range(0, spread_s.shape[0], blk):
            spread_s[start : start + blk, :] = one_hot(slot + start, dest_ref[...])

    out_ref[...] = mm(spread_s[...], rows_ref[...]).astype(BF)


def columns(rows, width):
    return pl.BlockSpec((rows, width), lambda i, n: (0, i))


def dispatch(at, dest_row, values, slots):
    rows, width = values.shape
    blk = min(256, width)
    return call(
        dispatch_kernel,
        "dispatch",
        at,
        (width // blk,),
        [fixed((1, rows)), columns(rows, blk)],
        columns(slots, blk),
        like((slots, width), BF),
        (dest_row, values),
        scratch=[pltpu.VMEM((slots, rows), BF)],
    )


def join_kernel(at_ref, *refs):
    pieces, out_ref = refs[:6], refs[6]
    r = pl.program_id(0)
    for place, piece in enumerate(in_order(at_ref[1], *[ref[...] for ref in pieces])):

        @pl.when(r == place)
        def _():
            out_ref[...] = piece


def join(at, pieces):
    each, width = pieces[0].shape
    return call(
        join_kernel,
        "join",
        at,
        (4,),
        [fixed((each, width))] * 6,
        pl.BlockSpec((each, width), lambda r, n: ((n[1] + r) % 4, 0)),
        like((4 * each, width), BF),
        pieces,
    )


def write_shares(mine, total, own_ref, one_ref, two_ref, three_ref, end_ref):
    rows = own_ref.shape[0]
    own_ref[...] = total[:rows]
    one, two, three = [total[r * rows : (r + 1) * rows].astype(BF) for r in (1, 2, 3)]
    one_ref[...] = one
    two_ref[...] = two
    three_ref[...] = three
    end_ref[...] = jnp.where(mine == 0, three, one)


def share_shapes(rows, width):
    return [like((rows, width), F32)] + [like((rows, width), BF)] * 4


def combine_kernel(count, whole, at_ref, *refs):
    dests, backs = refs[:count], refs[count : 2 * count]
    base_ref, refs, pick_s = refs[2 * count], refs[2 * count + 1 : -1], refs[-1]
    rows, slots = base_ref.shape[0], backs[0].shape[0]
    blk = rows // 4

    @pl.when(pl.program_id(0) == 0)
    def _():
        lane = lax.broadcasted_iota(jnp.int32, (blk, slots), 1)
        for k in range(count):
            for start in range(0, rows, blk):
                dest = dests[k][start : start + blk, :]
                pick_s[start : start + blk, k * slots : (k + 1) * slots] = one_hot(lane, dest)

    total = base_ref[...].astype(F32)
    for k in range(count):
        total = total + mm(pick_s[:, k * slots : (k + 1) * slots], backs[k][...])
    mine = at_ref[1]
    if whole:
        h_ref, out_ref = refs
        for r in range(4):
            part = total[r * blk : (r + 1) * blk]
            if r == 0:
                part = part + h_ref[...]
            place = pl.ds(pl.multiple_of(((mine + r) % 4) * blk, blk), blk)
            out_ref[place, :] = part.astype(BF)
    else:
        write_shares(mine, total, *refs)


def combine(at, dests, backs, base, h=None):
    count, (slots, width), rows = len(backs), backs[0].shape, base.shape[0]
    blk = min(256, width)
    whole = h is not None
    quarter = columns(rows // 4, blk)
    return call(
        partial(combine_kernel, count, whole),
        "combine",
        at,
        (width // blk,),
        [fixed((rows, 1))] * count
        + [columns(slots, blk)] * count
        + [columns(rows, blk)]
        + [quarter] * whole,
        columns(rows, blk) if whole else [quarter] * 5,
        like(base.shape, BF) if whole else share_shapes(rows // 4, width),
        (*dests, *backs, base) + ((h,) if whole else ()),
        scratch=[pltpu.VMEM((rows, count * slots), BF)],
    )


def mm_t(a, b):
    return lax.dot_general(a, b, (((1,), (1,)), ((), ())), preferred_element_type=F32)


def gelu_both(u):
    c = 0.7978845608028654
    square = u * u
    t = jnp.tanh(u * (c + (c * 0.044715) * square))
    half = 0.5 + 0.5 * t
    slope = half + (0.5 * u) * (1.0 - t * t) * (c + (3.0 * c * 0.044715) * square)
    return u * half, slope


def high_low(value):
    high = value.astype(BF)
    return high, (value - high.astype(F32)).astype(BF)


def two_coefs(logits, lane, experts):
    inside = (lane >= experts) & (lane < experts + 2)
    top = jnp.max(jnp.where(inside, logits, HIDE), axis=1, keepdims=True)
    e = jnp.where(inside, jnp.exp(logits - top), 0.0)
    e = e / jnp.sum(e, axis=1, keepdims=True)
    first = jnp.sum(jnp.where(lane == experts, e, 0.0), axis=1, keepdims=True)
    second = jnp.sum(jnp.where(lane == experts + 1, e, 0.0), axis=1, keepdims=True)
    return first, second


def small_back(d_small, rows, w_small_ref, small_ref, i):
    high, low = high_low(d_small)
    w_small = w_small_ref[...]
    high_t, low_t = high_low(d_small.T)

    @pl.when(i == 0)
    def _():
        small_ref[...] = jnp.zeros(small_ref.shape, F32)

    small_ref[...] += mm(high_t, rows) + mm(low_t, rows)
    return mm_t(high, w_small) + mm_t(low, w_small)


def expert_kernel(experts, half, at_ref, rows_ref, dy_ref, up_ref, down_ref, w_small_ref, *outs):
    if half:
        outs = outs[5:]
    rows_out_ref, hid_ref, dy_out_ref, deu_ref, y_ref, d_rows_ref, small_ref = outs
    rows = rows_ref[...]
    rows_out_ref[...] = rows
    up = mm(rows, up_ref[...])
    logits = mm(rows, w_small_ref[...])
    lane = lax.broadcasted_iota(jnp.int32, logits.shape, 1)
    routed = lane < experts
    top = jnp.max(jnp.where(routed, logits, HIDE), axis=1, keepdims=True)
    probs = jnp.where(routed, jnp.exp(logits - top), 0.0)
    probs = probs / jnp.sum(probs, axis=1, keepdims=True)
    own = jnp.where(lane == at_ref[2], 1.0, 0.0)
    gate = jnp.sum(probs * own, axis=1, keepdims=True)
    first, second = two_coefs(logits, lane, experts)
    weight = second * gate
    dy = dy_ref[...].reshape(rows.shape).astype(F32)
    d_y = (weight * dy).astype(BF)
    dy_out_ref[...] = d_y
    d_hidden = mm_t(d_y, down_ref[...])
    hidden, slope = gelu_both(up)
    hidden = hidden.astype(BF)
    hid_ref[...] = hidden
    d_up = (d_hidden * slope).astype(BF)
    deu_ref[...] = d_up
    y = mm(hidden, down_ref[...])
    y_ref[...] = (weight * y).astype(BF).reshape(y_ref.shape)
    along = gate * jnp.sum(dy * y, axis=1, keepdims=True)
    mixed = first * second * along
    d_small = (second * along) * (own - probs)
    d_small = jnp.where(routed, d_small, 0.0)
    d_small = d_small + jnp.where(lane == experts + 1, mixed, 0.0)
    d_small = d_small - jnp.where(lane == experts, mixed, 0.0)
    d_rows = mm_t(d_up, up_ref[...]) + small_back(d_small, rows, w_small_ref, small_ref, pl.program_id(0))
    d_rows_ref[...] = d_rows.astype(BF)


def expert_rows(at, rows, dy, w_up, w_down, w_small, experts, half, before):
    count, width = rows.shape
    hid, lanes = w_up.shape[1], w_small.shape[1]
    blk = min(512, count)
    capacity = count // dy.shape[0]
    steps = count // blk
    moving = pl.BlockSpec((blk, width), lambda i, n: (i, 0))
    slots = pl.BlockSpec((blk // capacity, capacity, width), lambda i, n: (i, half, 0))
    kept = [pl.BlockSpec((blk, size), lambda i, n: (i + half * steps, 0)) for size in (width, hid, width, hid)]
    return call(
        partial(expert_kernel, experts, half),
        "expert_rows",
        at,
        (steps,),
        [
            moving,
            slots,
            fixed((width, hid)),
            fixed((hid, width)),
            fixed((width, lanes)),
        ]
        + [pl.BlockSpec(memory_space=pl.ANY)] * (5 * half),
        kept + [slots, moving, fixed((lanes, width))],
        [like((2 * count, size), BF) for size in (width, hid, width, hid)]
        + [like(dy.shape, BF), like((count, width), BF)]
        + [like((lanes, width), F32)],
        (rows, dy, w_up, w_down, w_small, *before),
        alias={6 + k: k for k in range(5)} if half else None,
        vmem=56,
    )


def dense_kernel(experts, at_ref, rows_ref, dy_ref, in_ref, out_ref, w_small_ref, *outs):
    hid_ref, grad_ref, d_up_ref, mix_ref, db_ref, small_ref = outs
    rows = rows_ref[...]
    up = mm(rows, in_ref[...])
    logits = mm(rows, w_small_ref[...])
    lane = lax.broadcasted_iota(jnp.int32, logits.shape, 1)
    first, second = two_coefs(logits, lane, experts)
    dy = dy_ref[...].astype(F32)
    grad = (first * dy).astype(BF)
    grad_ref[...] = grad
    d_hidden = mm_t(grad, out_ref[...])
    hidden, slope = gelu_both(up)
    hidden = hidden.astype(BF)
    hid_ref[...] = hidden
    d_up = (d_hidden * slope).astype(BF)
    d_up_ref[...] = d_up
    dense = mm(hidden, out_ref[...])
    mix_ref[...] = first * dense
    mixed = first * second * jnp.sum(dy * dense, axis=1, keepdims=True)
    d_small = jnp.where(lane == experts, mixed, 0.0) - jnp.where(lane == experts + 1, mixed, 0.0)
    db_ref[...] = mm_t(d_up, in_ref[...]) + small_back(d_small, rows, w_small_ref, small_ref, pl.program_id(0))


def dense_rows(at, rows, dy, w_in, w_out, w_small, experts):
    (count, width), hid, lanes = rows.shape, w_in.shape[1], w_small.shape[1]
    blk = min(512, count)
    row_out = pl.BlockSpec((blk, width), lambda i, n: (i, 0))
    hid_out = pl.BlockSpec((blk, hid), lambda i, n: (i, 0))
    return call(
        partial(dense_kernel, experts),
        "dense_rows",
        at,
        (count // blk,),
        [row_out, row_out, fixed((width, hid)), fixed((hid, width)), fixed((width, lanes))],
        [hid_out, row_out, hid_out, row_out, row_out, fixed((lanes, width))],
        [
            like((count, hid), BF),
            like((count, width), BF),
            like((count, hid), BF),
            like((count, width), F32),
            like((count, width), F32),
            like((lanes, width), F32),
        ],
        (rows, dy, w_in, w_out, w_small),
        vmem=56,
    )


def turned(value):
    return value.astype(F32).T.astype(BF)


def dense_grads_kernel(at_ref, b_ref, d_up_ref, grad_ref, hid_ref, keep_ref, give_ref):
    width = d_up_ref.shape[1]
    first = mm(turned(b_ref[...]), d_up_ref[...]).astype(BF)
    second = mm(turned(grad_ref[...]), hid_ref[...]).astype(BF)
    half = pl.num_programs(0) // 2
    for side, ref in ((0, keep_ref), (1, give_ref)):

        @pl.when(pl.program_id(0) // half == side)
        def _():
            ref[0, :, :width] = first
            ref[0, :, width:] = second


def dense_grads(at, b, d_up, grad, hidden, parts):
    (rows, width), hid = b.shape, hidden.shape[1]
    own, half, bits = width // parts, parts // 2, parts.bit_length() - 1

    def part(q, n):
        turned_q = sum([((q // 2**k) % 2) * 2 ** (bits - 1 - k) for k in range(bits)])
        return turned_q ^ n[2]

    column = pl.BlockSpec((rows, own), lambda q, n: (0, part(q, n)))
    shape = (1, own, 2 * hid)
    return call(
        dense_grads_kernel,
        "dense_grads",
        at,
        (parts,),
        [column, fixed((rows, hid)), column, fixed((rows, hid))],
        [
            pl.BlockSpec(shape, lambda q, n: (jnp.minimum(q, half - 1), 0, 0)),
            pl.BlockSpec(shape, lambda q, n: (jnp.maximum(q - half, 0), 0, 0)),
        ],
        [like((half, own, 2 * hid), BF)] * 2,
        (b, d_up, grad, hidden),
    )


def attention_grads_kernel(experts, at_ref, *refs):
    grads, o_refs, refs = refs[:GROUP], refs[GROUP : GROUP + 6], refs[GROUP + 6 :]
    a_ref, dh_ref, w_ref, gain_ref, bias_ref, sums_ref = refs[:6]
    small_refs, (out_ref, all_s) = refs[6:-2], refs[-2:]
    heads, features = GROUP * HD, grads[1].shape[0]
    products, plain = 0.0, 0.0
    for k in range(GROUP):
        head = at_ref[0] ^ k
        rows = pl.ds(pl.multiple_of(head * features, features), features)
        grad = grads[k][...]
        weight = w_ref[head].astype(F32)
        total = mm(grad, a_ref[...])
        all_s[rows, :] = total
        each = jnp.sum(grad.astype(F32), axis=1, keepdims=True)
        products = products + jnp.sum(total * weight, axis=0, keepdims=True)
        plain = plain + jnp.sum(each * weight, axis=0, keepdims=True)
    first = GROUP * features
    for r, piece in enumerate(in_order(at_ref[1], *[ref[...] for ref in o_refs])):
        rows = pl.ds(pl.multiple_of(first + ((at_ref[1] + r) % 4) * heads, heads), heads)
        all_s[rows, :] = mm(piece, dh_ref[...])
    first += 4 * heads
    small = add_up(small_refs)
    row = lax.broadcasted_iota(jnp.int32, small.shape, 0)
    d_gain = (products - bias_ref[...] * plain) / gain_ref[...]
    for k, sums in enumerate((sums_ref[0:1, :], sums_ref[1:2, :], d_gain, plain)):
        small = jnp.where(row == experts + 2 + k, sums, small)
    all_s[first:, :] = small
    out_ref[...] = all_s[...].T.astype(BF)


def attention_grads(at, grads, o, a, dh, w_heads, gain, bias, sums, small, experts):
    rows, width = a.shape
    features, lanes = grads[0].shape[0], small[0].shape[0]
    piece = pl.BlockSpec((o[0].shape[0], dh.shape[0]), lambda i, n: (0, n[1]))
    height = GROUP * features + 4 * o[0].shape[0] + lanes
    blk = min(256, width)
    return call(
        partial(attention_grads_kernel, experts),
        "attention_grads",
        at,
        (width // blk,),
        [fixed((features, rows))] * GROUP
        + [piece] * 6
        + [columns(rows, blk), columns(dh.shape[0], blk)]
        + [pl.BlockSpec((GROUP, features, blk), lambda i, n: (0, 0, i))]
        + [columns(1, blk)] * 2
        + [columns(2, blk)]
        + [columns(lanes, blk)] * len(small),
        pl.BlockSpec((blk, height), lambda i, n: (i, 0)),
        like((width, height), BF),
        (*grads, *o, a, dh, w_heads, gain, bias, sums, *small),
        scratch=[pltpu.VMEM((height, blk), F32)],
    )


def project_kernel(at_ref, *refs):
    grads, w_ref, outs, turned_s = refs[:GROUP], refs[GROUP], refs[GROUP + 1 : -1], refs[-1]
    rows = turned_s.shape[1]
    blk = rows // 4

    @pl.when(pl.program_id(0) == 0)
    def _():
        for s in range(GROUP):
            for r in range(4):
                lanes = pl.ds(pl.multiple_of(((at_ref[1] + r) % 4) * blk, blk), blk)
                turned_s[s, r * blk : (r + 1) * blk, :] = turned(grads[s][:, lanes])

    total = 0.0
    for s in range(GROUP):
        total = total + mm(turned_s[s], w_ref[at_ref[0] ^ s])
    write_shares(at_ref[1], total, *outs)


def project_back(at, grads, w_heads):
    features, rows = grads[0].shape
    width = w_heads.shape[2]
    blk = min(256, width)
    return call(
        project_kernel,
        "project_back",
        at,
        (width // blk,),
        [fixed((features, rows))] * GROUP
        + [pl.BlockSpec((GROUP, features, blk), lambda i, n: (0, 0, i))],
        [columns(rows // 4, blk)] * 5,
        share_shapes(rows // 4, width),
        (*grads, w_heads),
        scratch=[pltpu.VMEM((GROUP, rows, features), BF)],
    )


def hop(value, *pairs):
    return lax.ppermute(value, "mp", pairs)


def rotate(value, steps):
    return hop(value, *[(s, (s + steps) % 4) for s in range(4)])


def gather_near(own):
    right = hop(own, (0, 1), (1, 2), (2, 3))
    left = hop(own, (1, 0), (2, 1), (3, 2))
    return own, right, left, hop(own, (0, 3), (3, 0))


def gather_far(near):
    _, right, left, _ = near
    return *near, hop(right, (1, 2), (2, 3)), hop(left, (1, 0), (2, 1))


def gather_pieces(own):
    return gather_far(gather_near(own))


def scatter_far(shares):
    _, _, two, _, end = shares
    return hop(two, (2, 1), (3, 2)), hop(two, (0, 1), (1, 2)), hop(end, (0, 3), (3, 0))


def scatter_near(shares, came):
    own, one, _, three, _ = shares
    from_right, from_left, from_end = came
    three = (three.astype(F32) + from_right.astype(F32)).astype(BF)
    one = (one.astype(F32) + from_left.astype(F32)).astype(BF)
    return own, hop(three, (1, 0), (2, 1), (3, 2)), hop(one, (0, 1), (1, 2), (2, 3)), from_end


def group_swap(value, s):
    count = lax.axis_size("dp")
    return lax.ppermute(value, "dp", [(t, t ^ s) for t in range(count)])


def expert_swap(value, experts):
    wide = value.reshape(experts, value.shape[0] // experts, value.shape[1])
    return lax.all_to_all(wide, "dp", 0, 0, tiled=True).reshape(value.shape)


def roll_rows(value, start):
    twice = jnp.concatenate([value, value], axis=0)
    return lax.dynamic_slice_in_dim(twice, start, value.shape[0], 0)


def add_halves(keep, came):
    return (keep.astype(F32) + came.astype(F32)).astype(BF)


def body(
    tokens,
    cotangent,
    ln_gains,
    ln_biases,
    w_qkv,
    w_o,
    w_in,
    w_out,
    w_router,
    w_coef,
    w_up,
    w_down,
    routes,
    long_group,
):
    rows, width = tokens.shape
    dps = lax.axis_size("dp")
    mine, position = lax.axis_index("mp"), lax.axis_index("dp")
    quarter = rows // 4
    start = mine * quarter
    heads_loc = w_qkv.shape[2] // HD
    hid = w_in.shape[1]
    experts = w_router.shape[1]
    capacity = max(2, 2 * rows // experts)
    half = capacity // 2
    barrier = lax.optimization_barrier
    first_len = lax.dynamic_index_in_dim(long_group, position // GROUP, 0, keepdims=False)
    at = jnp.stack([position % GROUP, mine, position, first_len]).astype(jnp.int32)
    gains = [ln_gains[0:1], ln_gains[1:2]]
    biases = [ln_biases[0:1], ln_biases[1:2]]
    w_o_all = lax.all_gather(w_o, "mp", axis=0, tiled=True)

    w_heads = w_qkv.reshape(width, 3, heads_loc, HD).transpose(2, 1, 3, 0)
    w_heads = w_heads.reshape(heads_loc, 3 * HD, width)
    a_r, *qkv = project(at, tokens, gains[0], biases[0], w_heads)
    qkv = [qkv[0]] + [group_swap(qkv[s], s) for s in (1, 2, 3)]

    route = roll_rows(routes, start)[:, 0]
    picked = (route[:, None] == jnp.arange(experts, dtype=jnp.int32)[None, :]).astype(jnp.int32)
    slot = jnp.sum((jnp.cumsum(picked, axis=0) - picked) * picked, axis=1)
    dy_b = roll_rows(cotangent, start)
    send_dy = dispatch(at, (route * capacity + slot)[None, :], dy_b, experts * capacity)
    *qkv, send_dy = barrier((*qkv, send_dy))
    in_half = [slot < half, slot >= half]
    dests = [
        jnp.where(in_half[k], route * half + slot - k * half, -1).astype(jnp.int32) for k in (0, 1)
    ]

    *o_t, lse = attend(at, qkv)
    *o_t, w_o_all = barrier((*o_t, w_o_all))
    o_heads = [o_t[0]] + [group_swap(o_t[s], s) for s in (1, 2, 3)]
    lanes = -(-(experts + 2) // 128) * 128
    w_small = jnp.concatenate(
        [w_router, w_coef, jnp.zeros((width, lanes - experts - 2), BF)], axis=1
    )
    *o_heads, send_dy, w_small = barrier((*o_heads, send_dy, w_small))
    got_dy = expert_swap(send_dy, experts).reshape(experts, capacity, width)
    o_pieces = gather_pieces(stack(at, o_heads))
    h, b_r = mid(at, o_pieces, w_o_all, tokens, gains[1], biases[1])

    send_0 = dispatch(at, dests[0][None, :], b_r, experts * half)
    send_0, got_dy = barrier((send_0, got_dy))
    got_0 = expert_swap(send_0, experts)
    send_1 = dispatch(at, dests[1][None, :], b_r, experts * half)
    b_r, send_1 = barrier((b_r, send_1))
    hidden, dense_grad, d_up, mix_base, db_base, small_t = dense_rows(
        at, b_r, dy_b, w_in, w_out, w_small, experts
    )
    send_1, got_0, db_base = barrier((send_1, got_0, db_base))
    got_1 = expert_swap(send_1, experts)

    *kept, d_rows_0, small_0 = expert_rows(
        at, got_0, got_dy, w_up[0], w_down[0], w_small, experts, 0, ()
    )
    back_0 = expert_swap(d_rows_0, experts)
    *kept, d_rows_1, small_1 = expert_rows(
        at, got_1, got_dy, w_up[0], w_down[0], w_small, experts, 1, kept
    )
    got, hidden_e, d_y, d_eu, back_y = kept
    back_1 = expert_swap(d_rows_1, experts)
    d_rows_1, b_r = barrier((d_rows_1, b_r))
    halving = width == dps * 128
    if halving:
        grads = dense_grads(at, b_r, d_up, dense_grad, hidden, dps)
    else:
        grads = [ein("td,tf->df", b_r, d_up).astype(BF), ein("td,tf->df", dense_grad, hidden).astype(BF)]
    back_0, back_1, back_y, *grads = barrier((back_0, back_1, back_y, *grads))

    dest_cols = [dest[:, None] for dest in dests]
    tok_y = expert_swap(back_y.reshape(experts * capacity, width), experts)
    shares = combine(at, dest_cols, [back_0, back_1], db_base)
    far = scatter_far(shares)
    *far, g_0, g_1 = barrier((*far, *grads))
    grads = [g_0, g_1]
    shares = scatter_near(shares, far)

    mix = combine(at, [(route * capacity + slot)[:, None]], [tok_y], mix_base, h)
    *shares, mix = barrier((*shares, mix))
    out_q = lax.psum_scatter(mix, "mp", scatter_dimension=0, tiled=True)
    dh, dh_r, sums_2, *do_q = mid_back(at, shares, w_o_all, h, dy_b[:quarter], gains[1])
    do_q = [do_q[0]] + [rotate(do_q[r], -r) for r in (1, 2, 3)]
    do_heads = unsplit(at, do_q)
    do_t = [do_heads[0]] + [group_swap(do_heads[s], s) for s in (1, 2, 3)]
    if halving:
        came_1 = group_swap(grads[1], 1)
    d_qkv = attend_back(at, qkv, do_t, o_t, lse)
    d_own, got, hidden_e, d_y, d_eu, out_q = barrier((d_qkv[0], got, hidden_e, d_y, d_eu, out_q))
    out_near = gather_near(out_q)
    d_qkv = [d_own] + [group_swap(d_qkv[s], s) for s in (1, 2, 3)]
    grad_down = ein("rf,rd->fd", hidden_e, d_y)
    tied = barrier((*d_qkv, grad_down, *out_near[1:3]))
    d_qkv, grad_down, out_near = tied[:4], tied[4], (out_near[0], *tied[5:], out_near[3])
    if halving:
        came_1, grad_down = barrier((came_1, grad_down))
        half = dps // 4
        came_2 = group_swap(add_halves(grads[0][half:], came_1[half:]), 2)
        grads = add_halves(add_halves(grads[0][:half], came_1[:half]), came_2)
        bit = 4
        while bit < dps:
            half = grads.shape[0] // 2
            grads = add_halves(grads[:half], group_swap(grads[half:], bit))
            bit *= 2
        grads = [grads[0][:, :hid], grads[0][:, hid:]]
    else:
        grads = [lax.psum_scatter(grad, "dp", scatter_dimension=0, tiled=True) for grad in grads]
    shares = project_back(at, d_qkv, w_heads)
    far = scatter_far(shares)
    output = join(at, gather_far(out_near))
    grads_a = attention_grads(
        at, d_qkv, o_pieces, a_r, dh_r, w_heads, gains[0], biases[0], sums_2, (small_0, small_1, small_t), experts
    )
    grad_up = ein("rd,rf->df", got, d_eu)
    grads_a, output, grad_up, *far = barrier((grads_a, output, grad_up, *far))
    grads_a = lax.psum_scatter(grads_a, "dp", scatter_dimension=0, tiled=True).T
    shares = scatter_near(shares, far)
    grad_q = first_back(at, shares, tokens, dh, gains[0])
    grad_tokens = join(at, gather_pieces(grad_q))

    own, heads = width // dps, heads_loc * HD
    grad_qkv = grads_a[: 3 * heads].astype(F32).reshape(heads_loc, 3, HD, own).transpose(3, 1, 0, 2)
    grad_qkv = grad_qkv.reshape(own, 3, heads)
    grad_in = grads[0].astype(F32)
    grad_out = grads[1].astype(F32).T
    rest = grads_a[3 * heads : 7 * heads].reshape(4, heads, own)
    small = jnp.broadcast_to(grads_a[7 * heads :], (4, lanes, own))
    rest = lax.all_to_all(jnp.concatenate([rest, small], axis=1), "mp", 0, 0, tiled=True)
    rest = jnp.sum(rest.astype(F32), axis=0)
    grad_o, small = rest[:heads], rest[heads:]
    small_out = small[: experts + 2].T
    return (
        output,
        grad_tokens,
        jnp.stack([small[experts + 4], small[experts + 2]]),
        jnp.stack([small[experts + 5], small[experts + 3]]),
        grad_qkv,
        grad_o,
        grad_in,
        grad_out,
        small_out[:, :experts],
        small_out[:, experts:],
        grad_up[None],
        grad_down[None],
    )


def solution(mesh):
    in_specs = (
        P("dp", None),
        P("dp", None),
        P(),
        P(),
        P(None, None, "mp"),
        P("mp", None),
        P(None, "mp"),
        P("mp", None),
        P(),
        P(),
        P("dp", None, "mp"),
        P("dp", "mp", None),
        P("dp", None),
        P(),
    )
    out_specs = (
        P("dp", None),
        P("dp", None),
        P(None, "dp"),
        P(None, "dp"),
        P("dp", None, "mp"),
        P("mp", "dp"),
        P("dp", "mp"),
        P("mp", "dp"),
        P("dp", None),
        P("dp", None),
        P("dp", None, "mp"),
        P("dp", "mp", None),
    )
    return jax.shard_map(body, mesh=mesh, in_specs=in_specs, out_specs=out_specs, check_vma=False)
```

```python
from functools import partial

import jax
import jax.numpy as jnp
from jax import lax
from jax.experimental import pallas as pl
from jax.experimental.pallas import tpu as pltpu
from jax.sharding import PartitionSpec as P

HD = 64
GROUP = 4
EPS = 1e-05
LOG2E = 1.4426950408889634
SCALE2 = 0.125 * LOG2E
HIDE = -1e30
BF = jnp.bfloat16
F32 = jnp.float32
LIGHT = pl.CostEstimate(flops=1 << 20, bytes_accessed=1 << 20, transcendentals=0)


def mm(a, b):
    return jnp.dot(a, b, preferred_element_type=F32)


def ein(spec, a, b):
    return jnp.einsum(spec, a, b, preferred_element_type=F32)


def call(kernel, name, prefetch, grid, in_specs, out_specs, out_shape, args, scratch=(), alias=None, vmem=48):
    return pl.pallas_call(
        kernel,
        grid_spec=pltpu.PrefetchScalarGridSpec(
            num_scalar_prefetch=1,
            grid=grid,
            in_specs=in_specs,
            out_specs=out_specs,
            scratch_shapes=list(scratch),
        ),
        out_shape=out_shape,
        input_output_aliases=alias or {},
        compiler_params=pltpu.CompilerParams(vmem_limit_bytes=vmem * 2**20),
        cost_estimate=LIGHT,
        name=name,
    )(prefetch, *args)


def fixed(shape):
    zeros = (0,) * len(shape)
    return pl.BlockSpec(shape, lambda *_: zeros)


def like(shape, dtype):
    return jax.ShapeDtypeStruct(shape, dtype)


def normalize(v):
    mean = jnp.mean(v, axis=-1, keepdims=True)
    centred = v - mean
    scale = lax.rsqrt(jnp.mean(centred * centred, axis=-1, keepdims=True) + EPS)
    return centred * scale, scale


def norm_back(grad, gain, normal, scale):
    g = grad * gain
    along = jnp.mean(g * normal, axis=-1, keepdims=True)
    return scale * (g - jnp.mean(g, axis=-1, keepdims=True) - normal * along)


def qkv_kernel(at_ref, x_ref, gain_ref, bias_ref, w_ref, a_ref, *outs):
    normal, _ = normalize(x_ref[...].astype(F32))
    a = (normal * gain_ref[...] + bias_ref[...]).astype(BF)
    a_ref[...] = a
    for s in range(GROUP):
        outs[s][...] = mm_t(w_ref[at_ref[0] ^ s], a).astype(BF)


def project(at, tokens, gain, bias, w_heads):
    rows, width = tokens.shape
    features = w_heads.shape[1]
    blk = min(256, rows)
    moving = pl.BlockSpec((blk, width), lambda i, n: (i, 0))
    return call(
        qkv_kernel,
        "project",
        at,
        (rows // blk,),
        [moving, fixed((1, width)), fixed((1, width)), fixed(w_heads.shape)],
        [moving] + [pl.BlockSpec((features, blk), lambda i, n: (0, i))] * GROUP,
        [like((rows, width), BF)] + [like((features, rows), BF)] * GROUP,
        (tokens, gain, bias, w_heads),
    )


def fill_keys(k_s, place, keys, first_len, blk):
    rows = place * blk + lax.broadcasted_iota(jnp.int32, (blk, 128), 0)
    lane = lax.broadcasted_iota(jnp.int32, (blk, 128), 1)
    wide = jnp.concatenate([keys.astype(F32).T, jnp.zeros((blk, 128 - HD), F32)], axis=1)
    wide = jnp.where((lane == HD) & (rows < first_len), HIDE, wide)
    k_s[pl.ds(place * blk, blk), :] = wide.astype(BF)


def wide_query(query, place, first_len, blk):
    cols = place * blk + lax.broadcasted_iota(jnp.int32, (128 - HD, blk), 1)
    sub = lax.broadcasted_iota(jnp.int32, (128 - HD, blk), 0)
    extra = jnp.where((sub == 0) & (cols >= first_len), 1.0, 0.0)
    return jnp.concatenate([query, extra.astype(BF)], axis=0)


def causal(blk):
    keys = lax.broadcasted_iota(jnp.int32, (blk, blk), 0)
    queries = lax.broadcasted_iota(jnp.int32, (blk, blk), 1)
    return keys <= queries


def attend_kernel(blk, per, at_ref, *refs):
    qkv_refs, o_refs = refs[:GROUP], refs[GROUP : 2 * GROUP]
    lse_ref, k_s, qkv_s = refs[2 * GROUP :]
    i = pl.program_id(0)
    place, first_len = at_ref[0], at_ref[3]

    @pl.when(i == 0)
    def _():
        for s in range(GROUP):
            qkv_s[place ^ s] = qkv_refs[s][...]

    def part(which, j):
        return qkv_s[j // per, HD * which : HD * (which + 1), pl.ds((j % per) * blk, blk)]

    fill_keys(k_s, i, part(1, i), first_len, blk)
    query = wide_query(part(0, i), i, first_len, blk)

    def scores(j):
        return mm(k_s[pl.ds(pl.multiple_of(j * blk, blk), blk), :], query)

    s = jnp.where(causal(blk), scores(i), HIDE)
    top = jnp.max(s, axis=0, keepdims=True)
    p = jnp.exp2((s - top) * SCALE2)
    total = jnp.sum(p, axis=0, keepdims=True)
    acc = mm(part(2, i), p.astype(BF))

    def steps(blocks, carry):
        top, total, acc = carry
        s = [scores(j) for j in blocks]
        new = top
        for one in s:
            new = jnp.maximum(new, jnp.max(one, axis=0, keepdims=True))
        keep = jnp.exp2((top - new) * SCALE2)
        total, acc = total * keep, acc * keep
        for j, one in zip(blocks, s):
            p = jnp.exp2((one - new) * SCALE2)
            total = total + jnp.sum(p, axis=0, keepdims=True)
            acc = acc + mm(part(2, j), p.astype(BF))
        return new, total, acc

    low = jnp.where(i * blk >= first_len, first_len // blk, 0)
    pairs = (i - low) // 2
    carry = lax.fori_loop(
        0, pairs, lambda t, c: steps([low + 2 * t, low + 2 * t + 1], c), (top, total, acc)
    )
    top, total, acc = lax.fori_loop(low + 2 * pairs, i, lambda j, c: steps([j], c), carry)
    out = (acc / total).astype(BF)
    for s in range(GROUP):

        @pl.when((i // per) ^ place == s)
        def _():
            o_refs[s][:, pl.ds((i % per) * blk, blk)] = out

    lse_ref[0] = top * SCALE2 + jnp.log2(total)


def attend(at, qkv):
    features, rows = qkv[0].shape
    blk = min(512, rows)
    per = rows // blk
    count = GROUP * per
    return call(
        partial(attend_kernel, blk, per),
        "attend",
        at,
        (count,),
        [fixed((features, rows))] * GROUP,
        [fixed((HD, rows))] * GROUP + [pl.BlockSpec((1, 1, blk), lambda i, n: (i, 0, 0))],
        [like((HD, rows), BF)] * GROUP + [like((count, 1, blk), F32)],
        qkv,
        scratch=[pltpu.VMEM((GROUP * rows, 128), BF), pltpu.VMEM((GROUP, features, rows), BF)],
    )


def back_kernel(blk, per, count, at_ref, *refs):
    qkv_refs, do_refs, o_refs = refs[:GROUP], refs[GROUP : 2 * GROUP], refs[2 * GROUP : 3 * GROUP]
    lse_ref, refs = refs[3 * GROUP], refs[3 * GROUP + 1 :]
    out_refs, refs = refs[:GROUP], refs[GROUP:]
    dq_ref, out_ref, k_s, kt_s, v_s, wide_s, dot_s, both_s, delta_s, acc_s = refs
    j = pl.program_id(0)
    place, first_len = at_ref[0], at_ref[3]

    @pl.when(j == 0)
    def _():
        dq_ref[...] = jnp.zeros(dq_ref.shape, F32)
        zero = jnp.zeros((blk, HD), F32)
        for s in range(GROUP):
            for sub in range(per):
                i = (place ^ s) * per + sub
                at = pl.ds(pl.multiple_of(i * blk, blk), blk)
                cut = slice(sub * blk, (sub + 1) * blk)
                query = qkv_refs[s][0:HD, cut]
                keys = qkv_refs[s][HD : 2 * HD, cut]
                grad = do_refs[s][:, cut]
                fill_keys(k_s, i, keys, first_len, blk)
                kt_s[:, at] = keys
                dot_s[:, at] = grad
                wide_s[:, at] = wide_query(query, i, first_len, blk)
                grad = grad.astype(F32)
                values = qkv_refs[s][2 * HD :, cut].astype(F32)
                v_s[at, :] = jnp.concatenate([values.T, zero], axis=1).astype(BF)
                both_s[0, at, :] = jnp.concatenate([grad.T, zero], axis=1).astype(BF)
                both_s[1, at, :] = jnp.concatenate([zero, query.astype(F32).T], axis=1).astype(BF)
                held = o_refs[s][:, cut].astype(F32)
                delta_s[i] = jnp.sum(held * grad, axis=0, keepdims=True)

    here = pl.ds(pl.multiple_of(j * blk, blk), blk)
    keys_t = kt_s[:, here]
    values = v_s[here, 0:HD]

    def pair(i, diagonal):
        at = pl.ds(pl.multiple_of(i * blk, blk), blk)
        s = mm(k_s[here, :], wide_s[:, at])
        p = jnp.exp2(s * SCALE2 - lse_ref[i])
        if diagonal:
            p = jnp.where(causal(blk), p, 0.0)
        dp = mm(values, dot_s[:, at])
        ds = (p * (dp - delta_s[i])).astype(BF)
        return mm(p.astype(BF), both_s[0, at, :]) + mm(ds, both_s[1, at, :]), mm(keys_t, ds)

    acc_s[...], dq = pair(j, True)
    dq_ref[:, here] += dq

    def step_two(t, carry):
        i = j + 1 + 2 * t
        (kv_0, dq_0), (kv_1, dq_1) = pair(i, False), pair(i + 1, False)
        acc_s[...] += kv_0 + kv_1
        at = pl.ds(pl.multiple_of(i * blk, blk), 2 * blk)
        dq_ref[:, at] += jnp.concatenate([dq_0, dq_1], axis=1)
        return carry

    def step(i, carry):
        kv, dq = pair(i, False)
        acc_s[...] += kv
        dq_ref[:, pl.ds(pl.multiple_of(i * blk, blk), blk)] += dq
        return carry

    high = jnp.where((j + 1) * blk <= first_len, (first_len + blk - 1) // blk, count)
    pairs = (high - j - 1) // 2
    lax.fori_loop(0, pairs, step_two, 0)
    lax.fori_loop(j + 1 + 2 * pairs, high, step, 0)
    both = acc_s[...].T
    out_ref[0:HD, :] = (dq_ref[:, here] * 0.125).astype(BF)
    out_ref[HD : 2 * HD, :] = (both[HD:, :] * 0.125).astype(BF)
    out_ref[2 * HD :, :] = both[:HD, :].astype(BF)
    for s in range(GROUP):

        @pl.when((j // per) ^ place == s)
        def _():
            out_refs[s][:, pl.ds(pl.multiple_of((j % per) * blk, blk), blk)] = out_ref[...]


def attend_back(at, qkv, do, o, lse):
    features, rows = qkv[0].shape
    blk = min(512, rows)
    per = rows // blk
    count = GROUP * per
    return call(
        partial(back_kernel, blk, per, count),
        "attend_back",
        at,
        (count,),
        [fixed((features, rows))] * GROUP
        + [fixed((HD, rows))] * (2 * GROUP)
        + [fixed((count, 1, blk))],
        [fixed((features, rows))] * GROUP,
        [like((features, rows), BF)] * GROUP,
        (*qkv, *do, *o, lse),
        scratch=[
            pltpu.VMEM((HD, GROUP * rows), F32),
            pltpu.VMEM((features, blk), BF),
            pltpu.VMEM((GROUP * rows, 128), BF),
            pltpu.VMEM((HD, GROUP * rows), BF),
            pltpu.VMEM((GROUP * rows, 128), BF),
            pltpu.VMEM((128, GROUP * rows), BF),
            pltpu.VMEM((HD, GROUP * rows), BF),
            pltpu.VMEM((2, GROUP * rows, 128), BF),
            pltpu.VMEM((count, 1, blk), F32),
            pltpu.VMEM((blk, 128), F32),
        ],
        vmem=36,
    )


def stack_kernel(at_ref, *refs):
    ins, out_ref = refs[:GROUP], refs[GROUP]
    for s in range(GROUP):
        head = pl.ds(pl.multiple_of((at_ref[0] ^ s) * HD, HD), HD)
        out_ref[head, :] = ins[s][...]


def stack(at, heads):
    rows = heads[0].shape[1]
    return call(
        stack_kernel,
        "stack",
        at,
        (1,),
        [fixed((HD, rows))] * GROUP,
        fixed((GROUP * HD, rows)),
        like((GROUP * HD, rows), BF),
        heads,
    )


def unsplit_kernel(at_ref, *refs):
    ins, outs = refs[:4], refs[4:]
    cols = ins[0].shape[1]
    for r in range(4):
        lanes = pl.ds(pl.multiple_of(((at_ref[1] + r) % 4) * cols, cols), cols)
        for s in range(GROUP):
            head = pl.ds(pl.multiple_of((at_ref[0] ^ s) * HD, HD), HD)
            outs[s][:, lanes] = ins[r][head, :]


def unsplit(at, pieces):
    shape = (HD, 4 * pieces[0].shape[1])
    return call(
        unsplit_kernel,
        "unsplit",
        at,
        (1,),
        [fixed(pieces[0].shape)] * 4,
        [fixed(shape)] * GROUP,
        [like(shape, BF)] * GROUP,
        pieces,
    )


def heads_of(mine, r, features):
    return pl.ds(pl.multiple_of(((mine + 4 - r) % 4) * features, features), features)


def mid_kernel(at_ref, *refs):
    pieces, (w_ref, x_ref, gain_ref, bias_ref, h_ref, b_ref) = refs[:6], refs[6:]
    h = x_ref[...].astype(F32)
    for r, piece in enumerate(in_order(at_ref[1], *[ref[...] for ref in pieces])):
        rows = heads_of(at_ref[1], 4 - r, piece.shape[0])
        h = h + mm(turned(piece), w_ref[rows, :])

    @pl.when(pl.program_id(0) == 0)
    def _():
        h_ref[...] = h

    normal, _ = normalize(h)
    b_ref[...] = (normal * gain_ref[...] + bias_ref[...]).astype(BF)


def mid(at, pieces, w_o, tokens, gain, bias):
    features, rows = pieces[0].shape
    width, quarter = tokens.shape[1], rows // 4
    return call(
        mid_kernel,
        "mid",
        at,
        (4,),
        [pl.BlockSpec((features, quarter), lambda q, n: (0, (n[1] + q) % 4))] * 6
        + [fixed(w_o.shape)]
        + [pl.BlockSpec((quarter, width), lambda q, n: ((n[1] + q) % 4, 0))]
        + [fixed((1, width))] * 2,
        [fixed((quarter, width)), pl.BlockSpec((quarter, width), lambda q, n: (q, 0))],
        [like((quarter, width), F32), like((rows, width), BF)],
        (*pieces, w_o, tokens, gain, bias),
    )


def add_up(refs):
    total = refs[0][...]
    for ref in refs[1:]:
        total = total + ref[...].astype(F32)
    return total


def mid_back_kernel(at_ref, *refs):
    shares, (w_ref, h_ref, dy_ref, gain_ref, dh_ref, low_ref, sums_ref) = refs[:4], refs[4:11]
    do_refs = refs[11:]
    db = add_up(shares)
    normal, scale = normalize(h_ref[...])
    dh = dy_ref[...].astype(F32) + norm_back(db, gain_ref[...], normal, scale)
    dh_ref[...] = dh
    low = dh.astype(BF)
    low_ref[...] = low
    sums_ref[0:1, :] = jnp.sum(db * normal, axis=0, keepdims=True)
    sums_ref[1:2, :] = jnp.sum(db, axis=0, keepdims=True)
    for r in range(4):
        rows = heads_of(at_ref[1], r, do_refs[r].shape[0])
        do_refs[r][...] = mm_t(w_ref[rows, :], low).astype(BF)


def mid_back(at, shares, w_o, h, dy, gain):
    quarter, width = h.shape
    whole = fixed((quarter, width))
    piece = (w_o.shape[0] // 4, quarter)
    return call(
        mid_back_kernel,
        "mid_back",
        at,
        (1,),
        [whole] * 4 + [fixed(w_o.shape), whole, whole, fixed((1, width))],
        [whole] * 2 + [fixed((2, width))] + [fixed(piece)] * 4,
        [like((quarter, width), F32), like((quarter, width), BF), like((2, width), F32)]
        + [like(piece, BF)] * 4,
        (*shares, w_o, h, dy, gain),
    )


def first_back_kernel(at_ref, *refs):
    shares = refs[:4]
    x_ref, dh_ref, gain_ref, out_ref = refs[4:]
    d_a = add_up(shares)
    normal, scale = normalize(x_ref[...].astype(F32))
    out_ref[...] = (dh_ref[...] + norm_back(d_a, gain_ref[...], normal, scale)).astype(BF)


def first_back(at, shares, tokens, dh, gain):
    quarter, width = dh.shape
    return call(
        first_back_kernel,
        "first_back",
        at,
        (1,),
        [fixed((quarter, width))] * 4
        + [pl.BlockSpec((quarter, width), lambda i, n: (n[1], 0))]
        + [fixed((quarter, width)), fixed((1, width))],
        fixed((quarter, width)),
        like((quarter, width), BF),
        (*shares, tokens, dh, gain),
    )


def in_order(mine, own, right, left, far, right_two, left_two):
    one = jnp.where(mine == 3, far, left)
    two = jnp.where(mine < 2, left_two, right_two)
    three = jnp.where(mine == 0, far, right)
    return own, one, two, three


def one_hot(slots, dest):
    return jnp.where(slots == dest, 1.0, 0.0).astype(BF)


def dispatch_kernel(at_ref, dest_ref, rows_ref, out_ref, spread_s):
    blk, rows = min(256, spread_s.shape[0]), dest_ref.shape[1]

    @pl.when(pl.program_id(0) == 0)
    def _():
        slot = lax.broadcasted_iota(jnp.int32, (blk, rows), 0)
        for start in range(0, spread_s.shape[0], blk):
            spread_s[start : start + blk, :] = one_hot(slot + start, dest_ref[...])

    out_ref[...] = mm(spread_s[...], rows_ref[...]).astype(BF)


def columns(rows, width):
    return pl.BlockSpec((rows, width), lambda i, n: (0, i))


def dispatch(at, dest_row, values, slots):
    rows, width = values.shape
    blk = min(256, width)
    return call(
        dispatch_kernel,
        "dispatch",
        at,
        (width // blk,),
        [fixed((1, rows)), columns(rows, blk)],
        columns(slots, blk),
        like((slots, width), BF),
        (dest_row, values),
        scratch=[pltpu.VMEM((slots, rows), BF)],
    )


def join_kernel(at_ref, *refs):
    pieces, out_ref = refs[:6], refs[6]
    r = pl.program_id(0)
    for place, piece in enumerate(in_order(at_ref[1], *[ref[...] for ref in pieces])):

        @pl.when(r == place)
        def _():
            out_ref[...] = piece


def join(at, pieces):
    each, width = pieces[0].shape
    return call(
        join_kernel,
        "join",
        at,
        (4,),
        [fixed((each, width))] * 6,
        pl.BlockSpec((each, width), lambda r, n: ((n[1] + r) % 4, 0)),
        like((4 * each, width), BF),
        pieces,
    )


def write_shares(mine, total, own_ref, one_ref, two_ref, three_ref, end_ref):
    rows = own_ref.shape[0]
    own_ref[...] = total[:rows]
    one, two, three = [total[r * rows : (r + 1) * rows].astype(BF) for r in (1, 2, 3)]
    one_ref[...] = one
    two_ref[...] = two
    three_ref[...] = three
    end_ref[...] = jnp.where(mine == 0, three, one)


def share_shapes(rows, width):
    return [like((rows, width), F32)] + [like((rows, width), BF)] * 4


def combine_kernel(count, whole, at_ref, *refs):
    dests, backs = refs[:count], refs[count : 2 * count]
    base_ref, refs, pick_s = refs[2 * count], refs[2 * count + 1 : -1], refs[-1]
    rows, slots = base_ref.shape[0], backs[0].shape[0]
    blk = rows // 4

    @pl.when(pl.program_id(0) == 0)
    def _():
        lane = lax.broadcasted_iota(jnp.int32, (blk, slots), 1)
        for k in range(count):
            for start in range(0, rows, blk):
                dest = dests[k][start : start + blk, :]
                pick_s[start : start + blk, k * slots : (k + 1) * slots] = one_hot(lane, dest)

    total = base_ref[...].astype(F32)
    for k in range(count):
        total = total + mm(pick_s[:, k * slots : (k + 1) * slots], backs[k][...])
    mine = at_ref[1]
    if whole:
        h_ref, out_ref = refs
        for r in range(4):
            part = total[r * blk : (r + 1) * blk]
            if r == 0:
                part = part + h_ref[...]
            place = pl.ds(pl.multiple_of(((mine + r) % 4) * blk, blk), blk)
            out_ref[place, :] = part.astype(BF)
    else:
        write_shares(mine, total, *refs)


def combine(at, dests, backs, base, h=None):
    count, (slots, width), rows = len(backs), backs[0].shape, base.shape[0]
    blk = min(256, width)
    whole = h is not None
    quarter = columns(rows // 4, blk)
    return call(
        partial(combine_kernel, count, whole),
        "combine",
        at,
        (width // blk,),
        [fixed((rows, 1))] * count
        + [columns(slots, blk)] * count
        + [columns(rows, blk)]
        + [quarter] * whole,
        columns(rows, blk) if whole else [quarter] * 5,
        like(base.shape, BF) if whole else share_shapes(rows // 4, width),
        (*dests, *backs, base) + ((h,) if whole else ()),
        scratch=[pltpu.VMEM((rows, count * slots), BF)],
    )


def mm_t(a, b):
    return lax.dot_general(a, b, (((1,), (1,)), ((), ())), preferred_element_type=F32)


def gelu_both(u):
    c = 0.7978845608028654
    square = u * u
    t = jnp.tanh(u * (c + (c * 0.044715) * square))
    half = 0.5 + 0.5 * t
    slope = half + (0.5 * u) * (1.0 - t * t) * (c + (3.0 * c * 0.044715) * square)
    return u * half, slope


def high_low(value):
    high = value.astype(BF)
    return high, (value - high.astype(F32)).astype(BF)


def two_coefs(logits, lane, experts):
    inside = (lane >= experts) & (lane < experts + 2)
    top = jnp.max(jnp.where(inside, logits, HIDE), axis=1, keepdims=True)
    e = jnp.where(inside, jnp.exp(logits - top), 0.0)
    e = e / jnp.sum(e, axis=1, keepdims=True)
    first = jnp.sum(jnp.where(lane == experts, e, 0.0), axis=1, keepdims=True)
    second = jnp.sum(jnp.where(lane == experts + 1, e, 0.0), axis=1, keepdims=True)
    return first, second


def small_back(d_small, rows, w_small_ref, small_ref, i):
    high, low = high_low(d_small)
    w_small = w_small_ref[...]
    high_t, low_t = high_low(d_small.T)

    @pl.when(i == 0)
    def _():
        small_ref[...] = jnp.zeros(small_ref.shape, F32)

    small_ref[...] += mm(high_t, rows) + mm(low_t, rows)
    return mm_t(high, w_small) + mm_t(low, w_small)


def expert_kernel(experts, half, at_ref, rows_ref, dy_ref, up_ref, down_ref, w_small_ref, *outs):
    if half:
        outs = outs[5:]
    rows_out_ref, hid_ref, dy_out_ref, deu_ref, y_ref, d_rows_ref, small_ref = outs
    rows = rows_ref[...]
    rows_out_ref[...] = rows
    up = mm(rows, up_ref[...])
    logits = mm(rows, w_small_ref[...])
    lane = lax.broadcasted_iota(jnp.int32, logits.shape, 1)
    routed = lane < experts
    top = jnp.max(jnp.where(routed, logits, HIDE), axis=1, keepdims=True)
    probs = jnp.where(routed, jnp.exp(logits - top), 0.0)
    probs = probs / jnp.sum(probs, axis=1, keepdims=True)
    own = jnp.where(lane == at_ref[2], 1.0, 0.0)
    gate = jnp.sum(probs * own, axis=1, keepdims=True)
    first, second = two_coefs(logits, lane, experts)
    weight = second * gate
    dy = dy_ref[...].reshape(rows.shape).astype(F32)
    d_y = (weight * dy).astype(BF)
    dy_out_ref[...] = d_y
    d_hidden = mm_t(d_y, down_ref[...])
    hidden, slope = gelu_both(up)
    hidden = hidden.astype(BF)
    hid_ref[...] = hidden
    d_up = (d_hidden * slope).astype(BF)
    deu_ref[...] = d_up
    y = mm(hidden, down_ref[...])
    y_ref[...] = (weight * y).astype(BF).reshape(y_ref.shape)
    along = gate * jnp.sum(dy * y, axis=1, keepdims=True)
    mixed = first * second * along
    d_small = (second * along) * (own - probs)
    d_small = jnp.where(routed, d_small, 0.0)
    d_small = d_small + jnp.where(lane == experts + 1, mixed, 0.0)
    d_small = d_small - jnp.where(lane == experts, mixed, 0.0)
    d_rows = mm_t(d_up, up_ref[...]) + small_back(d_small, rows, w_small_ref, small_ref, pl.program_id(0))
    d_rows_ref[...] = d_rows.astype(BF)


def expert_rows(at, rows, dy, w_up, w_down, w_small, experts, half, before):
    count, width = rows.shape
    hid, lanes = w_up.shape[1], w_small.shape[1]
    blk = min(512, count)
    capacity = count // dy.shape[0]
    steps = count // blk
    moving = pl.BlockSpec((blk, width), lambda i, n: (i, 0))
    slots = pl.BlockSpec((blk // capacity, capacity, width), lambda i, n: (i, half, 0))
    kept = [pl.BlockSpec((blk, size), lambda i, n: (i + half * steps, 0)) for size in (width, hid, width, hid)]
    return call(
        partial(expert_kernel, experts, half),
        "expert_rows",
        at,
        (steps,),
        [
            moving,
            slots,
            fixed((width, hid)),
            fixed((hid, width)),
            fixed((width, lanes)),
        ]
        + [pl.BlockSpec(memory_space=pl.ANY)] * (5 * half),
        kept + [slots, moving, fixed((lanes, width))],
        [like((2 * count, size), BF) for size in (width, hid, width, hid)]
        + [like(dy.shape, BF), like((count, width), BF)]
        + [like((lanes, width), F32)],
        (rows, dy, w_up, w_down, w_small, *before),
        alias={6 + k: k for k in range(5)} if half else None,
        vmem=56,
    )


def dense_kernel(experts, at_ref, rows_ref, dy_ref, in_ref, out_ref, w_small_ref, *outs):
    hid_ref, grad_ref, d_up_ref, mix_ref, db_ref, small_ref = outs
    rows = rows_ref[...]
    up = mm(rows, in_ref[...])
    logits = mm(rows, w_small_ref[...])
    lane = lax.broadcasted_iota(jnp.int32, logits.shape, 1)
    first, second = two_coefs(logits, lane, experts)
    dy = dy_ref[...].astype(F32)
    grad = (first * dy).astype(BF)
    grad_ref[...] = grad
    d_hidden = mm_t(grad, out_ref[...])
    hidden, slope = gelu_both(up)
    hidden = hidden.astype(BF)
    hid_ref[...] = hidden
    d_up = (d_hidden * slope).astype(BF)
    d_up_ref[...] = d_up
    dense = mm(hidden, out_ref[...])
    mix_ref[...] = first * dense
    mixed = first * second * jnp.sum(dy * dense, axis=1, keepdims=True)
    d_small = jnp.where(lane == experts, mixed, 0.0) - jnp.where(lane == experts + 1, mixed, 0.0)
    db_ref[...] = mm_t(d_up, in_ref[...]) + small_back(d_small, rows, w_small_ref, small_ref, pl.program_id(0))


def dense_rows(at, rows, dy, w_in, w_out, w_small, experts):
    (count, width), hid, lanes = rows.shape, w_in.shape[1], w_small.shape[1]
    blk = min(512, count)
    row_out = pl.BlockSpec((blk, width), lambda i, n: (i, 0))
    hid_out = pl.BlockSpec((blk, hid), lambda i, n: (i, 0))
    return call(
        partial(dense_kernel, experts),
        "dense_rows",
        at,
        (count // blk,),
        [row_out, row_out, fixed((width, hid)), fixed((hid, width)), fixed((width, lanes))],
        [hid_out, row_out, hid_out, row_out, row_out, fixed((lanes, width))],
        [
            like((count, hid), BF),
            like((count, width), BF),
            like((count, hid), BF),
            like((count, width), F32),
            like((count, width), F32),
            like((lanes, width), F32),
        ],
        (rows, dy, w_in, w_out, w_small),
        vmem=56,
    )


def turned(value):
    return value.astype(F32).T.astype(BF)


def dense_grads_kernel(at_ref, b_ref, d_up_ref, grad_ref, hid_ref, keep_ref, give_ref):
    width = d_up_ref.shape[1]
    first = mm(turned(b_ref[...]), d_up_ref[...]).astype(BF)
    second = mm(turned(grad_ref[...]), hid_ref[...]).astype(BF)
    half = pl.num_programs(0) // 2
    for side, ref in ((0, keep_ref), (1, give_ref)):

        @pl.when(pl.program_id(0) // half == side)
        def _():
            ref[0, :, :width] = first
            ref[0, :, width:] = second


def dense_grads(at, b, d_up, grad, hidden, parts):
    (rows, width), hid = b.shape, hidden.shape[1]
    own, half, bits = width // parts, parts // 2, parts.bit_length() - 1

    def part(q, n):
        turned_q = sum([((q // 2**k) % 2) * 2 ** (bits - 1 - k) for k in range(bits)])
        return turned_q ^ n[2]

    column = pl.BlockSpec((rows, own), lambda q, n: (0, part(q, n)))
    shape = (1, own, 2 * hid)
    return call(
        dense_grads_kernel,
        "dense_grads",
        at,
        (parts,),
        [column, fixed((rows, hid)), column, fixed((rows, hid))],
        [
            pl.BlockSpec(shape, lambda q, n: (jnp.minimum(q, half - 1), 0, 0)),
            pl.BlockSpec(shape, lambda q, n: (jnp.maximum(q - half, 0), 0, 0)),
        ],
        [like((half, own, 2 * hid), BF)] * 2,
        (b, d_up, grad, hidden),
    )


def attention_grads_kernel(experts, at_ref, *refs):
    grads, o_refs, refs = refs[:GROUP], refs[GROUP : GROUP + 6], refs[GROUP + 6 :]
    a_ref, dh_ref, w_ref, gain_ref, bias_ref, sums_ref = refs[:6]
    small_refs, (out_ref, all_s) = refs[6:-2], refs[-2:]
    heads, features = GROUP * HD, grads[1].shape[0]
    products, plain = 0.0, 0.0
    for k in range(GROUP):
        head = at_ref[0] ^ k
        rows = pl.ds(pl.multiple_of(head * features, features), features)
        grad = grads[k][...]
        weight = w_ref[head].astype(F32)
        total = mm(grad, a_ref[...])
        all_s[rows, :] = total
        each = jnp.sum(grad.astype(F32), axis=1, keepdims=True)
        products = products + jnp.sum(total * weight, axis=0, keepdims=True)
        plain = plain + jnp.sum(each * weight, axis=0, keepdims=True)
    first = GROUP * features
    for r, piece in enumerate(in_order(at_ref[1], *[ref[...] for ref in o_refs])):
        rows = pl.ds(pl.multiple_of(first + ((at_ref[1] + r) % 4) * heads, heads), heads)
        all_s[rows, :] = mm(piece, dh_ref[...])
    first += 4 * heads
    small = add_up(small_refs)
    row = lax.broadcasted_iota(jnp.int32, small.shape, 0)
    d_gain = (products - bias_ref[...] * plain) / gain_ref[...]
    for k, sums in enumerate((sums_ref[0:1, :], sums_ref[1:2, :], d_gain, plain)):
        small = jnp.where(row == experts + 2 + k, sums, small)
    all_s[first:, :] = small
    out_ref[...] = all_s[...].T.astype(BF)


def attention_grads(at, grads, o, a, dh, w_heads, gain, bias, sums, small, experts):
    rows, width = a.shape
    features, lanes = grads[0].shape[0], small[0].shape[0]
    piece = pl.BlockSpec((o[0].shape[0], dh.shape[0]), lambda i, n: (0, n[1]))
    height = GROUP * features + 4 * o[0].shape[0] + lanes
    blk = min(256, width)
    return call(
        partial(attention_grads_kernel, experts),
        "attention_grads",
        at,
        (width // blk,),
        [fixed((features, rows))] * GROUP
        + [piece] * 6
        + [columns(rows, blk), columns(dh.shape[0], blk)]
        + [pl.BlockSpec((GROUP, features, blk), lambda i, n: (0, 0, i))]
        + [columns(1, blk)] * 2
        + [columns(2, blk)]
        + [columns(lanes, blk)] * len(small),
        pl.BlockSpec((blk, height), lambda i, n: (i, 0)),
        like((width, height), BF),
        (*grads, *o, a, dh, w_heads, gain, bias, sums, *small),
        scratch=[pltpu.VMEM((height, blk), F32)],
    )


def project_kernel(at_ref, *refs):
    grads, w_ref, outs, turned_s = refs[:GROUP], refs[GROUP], refs[GROUP + 1 : -1], refs[-1]
    rows = turned_s.shape[1]
    blk = rows // 4

    @pl.when(pl.program_id(0) == 0)
    def _():
        for s in range(GROUP):
            for r in range(4):
                lanes = pl.ds(pl.multiple_of(((at_ref[1] + r) % 4) * blk, blk), blk)
                turned_s[s, r * blk : (r + 1) * blk, :] = turned(grads[s][:, lanes])

    total = 0.0
    for s in range(GROUP):
        total = total + mm(turned_s[s], w_ref[at_ref[0] ^ s])
    write_shares(at_ref[1], total, *outs)


def project_back(at, grads, w_heads):
    features, rows = grads[0].shape
    width = w_heads.shape[2]
    blk = min(256, width)
    return call(
        project_kernel,
        "project_back",
        at,
        (width // blk,),
        [fixed((features, rows))] * GROUP
        + [pl.BlockSpec((GROUP, features, blk), lambda i, n: (0, 0, i))],
        [columns(rows // 4, blk)] * 5,
        share_shapes(rows // 4, width),
        (*grads, w_heads),
        scratch=[pltpu.VMEM((GROUP, rows, features), BF)],
    )


def hop(value, *pairs):
    return lax.ppermute(value, "mp", pairs)


def rotate(value, steps):
    return hop(value, *[(s, (s + steps) % 4) for s in range(4)])


def gather_near(own):
    right = hop(own, (0, 1), (1, 2), (2, 3))
    left = hop(own, (1, 0), (2, 1), (3, 2))
    return own, right, left, hop(own, (0, 3), (3, 0))


def gather_far(near):
    _, right, left, _ = near
    return *near, hop(right, (1, 2), (2, 3)), hop(left, (1, 0), (2, 1))


def gather_pieces(own):
    return gather_far(gather_near(own))


def scatter_far(shares):
    _, _, two, _, end = shares
    return hop(two, (2, 1), (3, 2)), hop(two, (0, 1), (1, 2)), hop(end, (0, 3), (3, 0))


def scatter_near(shares, came):
    own, one, _, three, _ = shares
    from_right, from_left, from_end = came
    three = (three.astype(F32) + from_right.astype(F32)).astype(BF)
    one = (one.astype(F32) + from_left.astype(F32)).astype(BF)
    return own, hop(three, (1, 0), (2, 1), (3, 2)), hop(one, (0, 1), (1, 2), (2, 3)), from_end


def group_swap(value, s):
    count = lax.axis_size("dp")
    return lax.ppermute(value, "dp", [(t, t ^ s) for t in range(count)])


def expert_swap(value, experts):
    wide = value.reshape(experts, value.shape[0] // experts, value.shape[1])
    return lax.all_to_all(wide, "dp", 0, 0, tiled=True).reshape(value.shape)


def roll_rows(value, start):
    twice = jnp.concatenate([value, value], axis=0)
    return lax.dynamic_slice_in_dim(twice, start, value.shape[0], 0)


def add_halves(keep, came):
    return (keep.astype(F32) + came.astype(F32)).astype(BF)


def body(
    tokens,
    cotangent,
    ln_gains,
    ln_biases,
    w_qkv,
    w_o,
    w_in,
    w_out,
    w_router,
    w_coef,
    w_up,
    w_down,
    routes,
    long_group,
):
    rows, width = tokens.shape
    dps = lax.axis_size("dp")
    mine, position = lax.axis_index("mp"), lax.axis_index("dp")
    quarter = rows // 4
    start = mine * quarter
    heads_loc = w_qkv.shape[2] // HD
    hid = w_in.shape[1]
    experts = w_router.shape[1]
    capacity = max(2, 2 * rows // experts)
    half = capacity // 2
    barrier = lax.optimization_barrier
    first_len = lax.dynamic_index_in_dim(long_group, position // GROUP, 0, keepdims=False)
    at = jnp.stack([position % GROUP, mine, position, first_len]).astype(jnp.int32)
    gains = [ln_gains[0:1], ln_gains[1:2]]
    biases = [ln_biases[0:1], ln_biases[1:2]]
    w_o_all = lax.all_gather(w_o, "mp", axis=0, tiled=True)

    w_heads = w_qkv.reshape(width, 3, heads_loc, HD).transpose(2, 1, 3, 0)
    w_heads = w_heads.reshape(heads_loc, 3 * HD, width)
    a_r, *qkv = project(at, tokens, gains[0], biases[0], w_heads)
    qkv = [qkv[0]] + [group_swap(qkv[s], s) for s in (1, 2, 3)]

    route = roll_rows(routes, start)[:, 0]
    picked = (route[:, None] == jnp.arange(experts, dtype=jnp.int32)[None, :]).astype(jnp.int32)
    slot = jnp.sum((jnp.cumsum(picked, axis=0) - picked) * picked, axis=1)
    dy_b = roll_rows(cotangent, start)
    full = route * capacity + slot
    send_dy = dispatch(at, full[None, :], dy_b, experts * capacity)
    *qkv, send_dy = barrier((*qkv, send_dy))
    in_half = [slot < half, slot >= half]
    dests = [
        jnp.where(in_half[k], route * half + slot - k * half, -1).astype(jnp.int32) for k in (0, 1)
    ]

    *o_t, lse = attend(at, qkv)
    *o_t, w_o_all = barrier((*o_t, w_o_all))
    o_heads = [o_t[0]] + [group_swap(o_t[s], s) for s in (1, 2, 3)]
    lanes = -(-(experts + 2) // 128) * 128
    w_small = jnp.concatenate(
        [w_router, w_coef, jnp.zeros((width, lanes - experts - 2), BF)], axis=1
    )
    *o_heads, send_dy, w_small = barrier((*o_heads, send_dy, w_small))
    got_dy = expert_swap(send_dy, experts).reshape(experts, capacity, width)
    o_pieces = gather_pieces(stack(at, o_heads))
    h, b_r = mid(at, o_pieces, w_o_all, tokens, gains[1], biases[1])

    send_0 = dispatch(at, dests[0][None, :], b_r, experts * half)
    send_0, got_dy = barrier((send_0, got_dy))
    got_0 = expert_swap(send_0, experts)
    send_1 = dispatch(at, dests[1][None, :], b_r, experts * half)
    b_r, send_1 = barrier((b_r, send_1))
    hidden, dense_grad, d_up, mix_base, db_base, small_t = dense_rows(
        at, b_r, dy_b, w_in, w_out, w_small, experts
    )
    send_1, got_0, db_base = barrier((send_1, got_0, db_base))
    got_1 = expert_swap(send_1, experts)

    *kept, d_rows_0, small_0 = expert_rows(
        at, got_0, got_dy, w_up[0], w_down[0], w_small, experts, 0, ()
    )
    back_0 = expert_swap(d_rows_0, experts)
    *kept, d_rows_1, small_1 = expert_rows(
        at, got_1, got_dy, w_up[0], w_down[0], w_small, experts, 1, kept
    )
    got, hidden_e, d_y, d_eu, back_y = kept
    back_1 = expert_swap(d_rows_1, experts)
    d_rows_1, b_r = barrier((d_rows_1, b_r))
    halving = width == dps * 128
    if halving:
        grads = dense_grads(at, b_r, d_up, dense_grad, hidden, dps)
    else:
        grads = [ein("td,tf->df", b_r, d_up).astype(BF), ein("td,tf->df", dense_grad, hidden).astype(BF)]
    back_0, back_1, back_y, *grads = barrier((back_0, back_1, back_y, *grads))

    dest_cols = [dest[:, None] for dest in dests]
    tok_y = expert_swap(back_y.reshape(experts * capacity, width), experts)
    shares = combine(at, dest_cols, [back_0, back_1], db_base)
    far = scatter_far(shares)
    *far, g_0, g_1 = barrier((*far, *grads))
    grads = [g_0, g_1]
    shares = scatter_near(shares, far)

    mix = combine(at, [full[:, None]], [tok_y], mix_base, h)
    *shares, mix = barrier((*shares, mix))
    output = lax.psum(mix, "mp")
    dh, dh_r, sums_2, *do_q = mid_back(at, shares, w_o_all, h, dy_b, gains[1])
    do_q = [do_q[0]] + [rotate(do_q[r], -r) for r in (1, 2, 3)]
    do_heads = unsplit(at, do_q)
    do_t = [do_heads[0]] + [group_swap(do_heads[s], s) for s in (1, 2, 3)]
    if halving:
        came_1 = group_swap(grads[1], 1)
        half = dps // 4
        give = add_halves(grads[0][half:], came_1[half:])
        *do_t, give = barrier((*do_t, give))
        came_2 = group_swap(give, 2)
    d_qkv = attend_back(at, qkv, do_t, o_t, lse)
    if halving:
        keep = add_halves(grads[0][:half], came_1[:half])
        *d_qkv, came_2, keep = barrier((*d_qkv, came_2, keep))
        grads = add_halves(keep, came_2)
        bit = 4
        while bit < dps:
            half = grads.shape[0] // 2
            grads = add_halves(grads[:half], group_swap(grads[half:], bit))
            bit *= 2
        grads = [grads[0][:, :hid], grads[0][:, hid:]]
    else:
        grads = [lax.psum_scatter(grad, "dp", scatter_dimension=0, tiled=True) for grad in grads]

    d_own, got, hidden_e, d_y, d_eu = barrier((d_qkv[0], got, hidden_e, d_y, d_eu))
    d_qkv = [d_own] + [group_swap(d_qkv[s], s) for s in (1, 2, 3)]
    grad_down = ein("rf,rd->fd", hidden_e, d_y)
    *d_qkv, grad_down = barrier((*d_qkv, grad_down))
    shares = project_back(at, d_qkv, w_heads)
    far = scatter_far(shares)
    grads_a = attention_grads(
        at, d_qkv, o_pieces, a_r, dh_r, w_heads, gains[0], biases[0], sums_2, (small_0, small_1, small_t), experts
    )
    grad_up = ein("rd,rf->df", got, d_eu)
    grads_a, output, grad_up, *far = barrier((grads_a, output, grad_up, *far))
    grads_a = lax.psum_scatter(grads_a, "dp", scatter_dimension=0, tiled=True).T
    shares = scatter_near(shares, far)
    grad_q = first_back(at, shares, tokens, dh, gains[0])
    grad_tokens = join(at, gather_pieces(grad_q))

    own, heads = width // dps, heads_loc * HD
    grad_qkv = grads_a[: 3 * heads].astype(F32).reshape(heads_loc, 3, HD, own).transpose(3, 1, 0, 2)
    grad_qkv = grad_qkv.reshape(own, 3, heads)
    grad_in = grads[0].astype(F32)
    grad_out = grads[1].astype(F32).T
    rest = grads_a[3 * heads : 7 * heads].reshape(4, heads, own)
    small = jnp.broadcast_to(grads_a[7 * heads :], (4, lanes, own))
    rest = lax.all_to_all(jnp.concatenate([rest, small], axis=1), "mp", 0, 0, tiled=True)
    rest = jnp.sum(rest.astype(F32), axis=0)
    grad_o, small = rest[:heads], rest[heads:]
    small_out = small[: experts + 2].T
    return (
        output,
        grad_tokens,
        jnp.stack([small[experts + 4], small[experts + 2]]),
        jnp.stack([small[experts + 5], small[experts + 3]]),
        grad_qkv,
        grad_o,
        grad_in,
        grad_out,
        small_out[:, :experts],
        small_out[:, experts:],
        grad_up[None],
        grad_down[None],
    )


def solution(mesh):
    in_specs = (
        P("dp", None),
        P("dp", None),
        P(),
        P(),
        P(None, None, "mp"),
        P("mp", None),
        P(None, "mp"),
        P("mp", None),
        P(),
        P(),
        P("dp", None, "mp"),
        P("dp", "mp", None),
        P("dp", None),
        P(),
    )
    out_specs = (
        P("dp", None),
        P("dp", None),
        P(None, "dp"),
        P(None, "dp"),
        P("dp", None, "mp"),
        P("mp", "dp"),
        P("dp", "mp"),
        P("mp", "dp"),
        P("dp", None),
        P("dp", None),
        P("dp", None, "mp"),
        P("dp", "mp", None),
    )
    return jax.shard_map(body, mesh=mesh, in_specs=in_specs, out_specs=out_specs, check_vma=False)
```

```python
from functools import partial

import jax
import jax.numpy as jnp
from jax import lax
from jax.experimental import pallas as pl
from jax.experimental.pallas import tpu as pltpu
from jax.sharding import PartitionSpec as P

HD = 64
GROUP = 4
EPS = 1e-05
LOG2E = 1.4426950408889634
SCALE2 = 0.125 * LOG2E
HIDE = -1e30
BF = jnp.bfloat16
F32 = jnp.float32
LIGHT = pl.CostEstimate(flops=1 << 20, bytes_accessed=1 << 20, transcendentals=0)


def mm(a, b):
    return jnp.dot(a, b, preferred_element_type=F32)


def ein(spec, a, b):
    return jnp.einsum(spec, a, b, preferred_element_type=F32)


def call(kernel, name, prefetch, grid, in_specs, out_specs, out_shape, args, scratch=(), alias=None, vmem=48):
    return pl.pallas_call(
        kernel,
        grid_spec=pltpu.PrefetchScalarGridSpec(
            num_scalar_prefetch=1,
            grid=grid,
            in_specs=in_specs,
            out_specs=out_specs,
            scratch_shapes=list(scratch),
        ),
        out_shape=out_shape,
        input_output_aliases=alias or {},
        compiler_params=pltpu.CompilerParams(vmem_limit_bytes=vmem * 2**20),
        cost_estimate=LIGHT,
        name=name,
    )(prefetch, *args)


def fixed(shape):
    zeros = (0,) * len(shape)
    return pl.BlockSpec(shape, lambda *_: zeros)


def like(shape, dtype):
    return jax.ShapeDtypeStruct(shape, dtype)


def normalize(v):
    mean = jnp.mean(v, axis=-1, keepdims=True)
    centred = v - mean
    scale = lax.rsqrt(jnp.mean(centred * centred, axis=-1, keepdims=True) + EPS)
    return centred * scale, scale


def norm_back(grad, gain, normal, scale):
    g = grad * gain
    along = jnp.mean(g * normal, axis=-1, keepdims=True)
    return scale * (g - jnp.mean(g, axis=-1, keepdims=True) - normal * along)


def qkv_kernel(at_ref, x_ref, gain_ref, bias_ref, w_ref, a_ref, *outs):
    normal, _ = normalize(x_ref[...].astype(F32))
    a = (normal * gain_ref[...] + bias_ref[...]).astype(BF)
    a_ref[...] = a
    for s in range(GROUP):
        outs[s][...] = mm_t(w_ref[at_ref[0] ^ s], a).astype(BF)


def project(at, tokens, gain, bias, w_heads):
    rows, width = tokens.shape
    features = w_heads.shape[1]
    blk = min(256, rows)
    moving = pl.BlockSpec((blk, width), lambda i, n: (i, 0))
    return call(
        qkv_kernel,
        "project",
        at,
        (rows // blk,),
        [moving, fixed((1, width)), fixed((1, width)), fixed(w_heads.shape)],
        [moving] + [pl.BlockSpec((features, blk), lambda i, n: (0, i))] * GROUP,
        [like((rows, width), BF)] + [like((features, rows), BF)] * GROUP,
        (tokens, gain, bias, w_heads),
    )


def fill_keys(k_s, place, keys, first_len, blk):
    rows = place * blk + lax.broadcasted_iota(jnp.int32, (blk, 128), 0)
    lane = lax.broadcasted_iota(jnp.int32, (blk, 128), 1)
    wide = jnp.concatenate([keys.astype(F32).T, jnp.zeros((blk, 128 - HD), F32)], axis=1)
    wide = jnp.where((lane == HD) & (rows < first_len), HIDE, wide)
    k_s[pl.ds(place * blk, blk), :] = wide.astype(BF)


def wide_query(query, place, first_len, blk):
    cols = place * blk + lax.broadcasted_iota(jnp.int32, (128 - HD, blk), 1)
    sub = lax.broadcasted_iota(jnp.int32, (128 - HD, blk), 0)
    extra = jnp.where((sub == 0) & (cols >= first_len), 1.0, 0.0)
    return jnp.concatenate([query, extra.astype(BF)], axis=0)


def causal(blk):
    keys = lax.broadcasted_iota(jnp.int32, (blk, blk), 0)
    queries = lax.broadcasted_iota(jnp.int32, (blk, blk), 1)
    return keys <= queries


def attend_kernel(blk, per, at_ref, *refs):
    qkv_refs, o_refs = refs[:GROUP], refs[GROUP : 2 * GROUP]
    lse_ref, k_s, qkv_s = refs[2 * GROUP :]
    i = pl.program_id(0)
    place, first_len = at_ref[0], at_ref[3]

    @pl.when(i == 0)
    def _():
        for s in range(GROUP):
            qkv_s[place ^ s] = qkv_refs[s][...]

    def part(which, j):
        return qkv_s[j // per, HD * which : HD * (which + 1), pl.ds((j % per) * blk, blk)]

    fill_keys(k_s, i, part(1, i), first_len, blk)
    query = wide_query(part(0, i), i, first_len, blk)

    def scores(j):
        return mm(k_s[pl.ds(pl.multiple_of(j * blk, blk), blk), :], query)

    s = jnp.where(causal(blk), scores(i), HIDE)
    top = jnp.max(s, axis=0, keepdims=True)
    p = jnp.exp2((s - top) * SCALE2)
    total = jnp.sum(p, axis=0, keepdims=True)
    acc = mm(part(2, i), p.astype(BF))

    def steps(blocks, carry):
        top, total, acc = carry
        s = [scores(j) for j in blocks]
        new = top
        for one in s:
            new = jnp.maximum(new, jnp.max(one, axis=0, keepdims=True))
        keep = jnp.exp2((top - new) * SCALE2)
        total, acc = total * keep, acc * keep
        for j, one in zip(blocks, s):
            p = jnp.exp2((one - new) * SCALE2)
            total = total + jnp.sum(p, axis=0, keepdims=True)
            acc = acc + mm(part(2, j), p.astype(BF))
        return new, total, acc

    low = jnp.where(i * blk >= first_len, first_len // blk, 0)
    pairs = (i - low) // 2
    carry = lax.fori_loop(
        0, pairs, lambda t, c: steps([low + 2 * t, low + 2 * t + 1], c), (top, total, acc)
    )
    top, total, acc = lax.fori_loop(low + 2 * pairs, i, lambda j, c: steps([j], c), carry)
    out = (acc / total).astype(BF)
    for s in range(GROUP):

        @pl.when((i // per) ^ place == s)
        def _():
            o_refs[s][:, pl.ds((i % per) * blk, blk)] = out

    lse_ref[0] = top * SCALE2 + jnp.log2(total)


def attend(at, qkv):
    features, rows = qkv[0].shape
    blk = min(512, rows)
    per = rows // blk
    count = GROUP * per
    return call(
        partial(attend_kernel, blk, per),
        "attend",
        at,
        (count,),
        [fixed((features, rows))] * GROUP,
        [fixed((HD, rows))] * GROUP + [pl.BlockSpec((1, 1, blk), lambda i, n: (i, 0, 0))],
        [like((HD, rows), BF)] * GROUP + [like((count, 1, blk), F32)],
        qkv,
        scratch=[pltpu.VMEM((GROUP * rows, 128), BF), pltpu.VMEM((GROUP, features, rows), BF)],
    )


def back_kernel(blk, per, count, at_ref, *refs):
    qkv_refs, do_refs, o_refs = refs[:GROUP], refs[GROUP : 2 * GROUP], refs[2 * GROUP : 3 * GROUP]
    lse_ref, refs = refs[3 * GROUP], refs[3 * GROUP + 1 :]
    out_refs, refs = refs[:GROUP], refs[GROUP:]
    dq_ref, out_ref, k_s, kt_s, v_s, wide_s, dot_s, both_s, delta_s, acc_s = refs
    j = pl.program_id(0)
    place, first_len = at_ref[0], at_ref[3]

    @pl.when(j == 0)
    def _():
        dq_ref[...] = jnp.zeros(dq_ref.shape, F32)
        zero = jnp.zeros((blk, HD), F32)
        for s in range(GROUP):
            for sub in range(per):
                i = (place ^ s) * per + sub
                at = pl.ds(pl.multiple_of(i * blk, blk), blk)
                cut = slice(sub * blk, (sub + 1) * blk)
                query = qkv_refs[s][0:HD, cut]
                keys = qkv_refs[s][HD : 2 * HD, cut]
                grad = do_refs[s][:, cut]
                fill_keys(k_s, i, keys, first_len, blk)
                kt_s[:, at] = keys
                dot_s[:, at] = grad
                wide_s[:, at] = wide_query(query, i, first_len, blk)
                grad = grad.astype(F32)
                values = qkv_refs[s][2 * HD :, cut].astype(F32)
                v_s[at, :] = jnp.concatenate([values.T, zero], axis=1).astype(BF)
                both_s[0, at, :] = jnp.concatenate([grad.T, zero], axis=1).astype(BF)
                both_s[1, at, :] = jnp.concatenate([zero, query.astype(F32).T], axis=1).astype(BF)
                held = o_refs[s][:, cut].astype(F32)
                delta_s[i] = jnp.sum(held * grad, axis=0, keepdims=True)

    here = pl.ds(pl.multiple_of(j * blk, blk), blk)
    keys_t = kt_s[:, here]
    values = v_s[here, 0:HD]

    def pair(i, diagonal):
        at = pl.ds(pl.multiple_of(i * blk, blk), blk)
        s = mm(k_s[here, :], wide_s[:, at])
        p = jnp.exp2(s * SCALE2 - lse_ref[i])
        if diagonal:
            p = jnp.where(causal(blk), p, 0.0)
        dp = mm(values, dot_s[:, at])
        ds = (p * (dp - delta_s[i])).astype(BF)
        return mm(p.astype(BF), both_s[0, at, :]) + mm(ds, both_s[1, at, :]), mm(keys_t, ds)

    acc_s[...], dq = pair(j, True)
    dq_ref[:, here] += dq

    def step_two(t, carry):
        i = j + 1 + 2 * t
        (kv_0, dq_0), (kv_1, dq_1) = pair(i, False), pair(i + 1, False)
        acc_s[...] += kv_0 + kv_1
        at = pl.ds(pl.multiple_of(i * blk, blk), 2 * blk)
        dq_ref[:, at] += jnp.concatenate([dq_0, dq_1], axis=1)
        return carry

    def step(i, carry):
        kv, dq = pair(i, False)
        acc_s[...] += kv
        dq_ref[:, pl.ds(pl.multiple_of(i * blk, blk), blk)] += dq
        return carry

    high = jnp.where((j + 1) * blk <= first_len, (first_len + blk - 1) // blk, count)
    pairs = (high - j - 1) // 2
    lax.fori_loop(0, pairs, step_two, 0)
    lax.fori_loop(j + 1 + 2 * pairs, high, step, 0)
    both = acc_s[...].T
    out_ref[0:HD, :] = (dq_ref[:, here] * 0.125).astype(BF)
    out_ref[HD : 2 * HD, :] = (both[HD:, :] * 0.125).astype(BF)
    out_ref[2 * HD :, :] = both[:HD, :].astype(BF)
    for s in range(GROUP):

        @pl.when((j // per) ^ place == s)
        def _():
            out_refs[s][:, pl.ds(pl.multiple_of((j % per) * blk, blk), blk)] = out_ref[...]


def attend_back(at, qkv, do, o, lse):
    features, rows = qkv[0].shape
    blk = min(512, rows)
    per = rows // blk
    count = GROUP * per
    return call(
        partial(back_kernel, blk, per, count),
        "attend_back",
        at,
        (count,),
        [fixed((features, rows))] * GROUP
        + [fixed((HD, rows))] * (2 * GROUP)
        + [fixed((count, 1, blk))],
        [fixed((features, rows))] * GROUP,
        [like((features, rows), BF)] * GROUP,
        (*qkv, *do, *o, lse),
        scratch=[
            pltpu.VMEM((HD, GROUP * rows), F32),
            pltpu.VMEM((features, blk), BF),
            pltpu.VMEM((GROUP * rows, 128), BF),
            pltpu.VMEM((HD, GROUP * rows), BF),
            pltpu.VMEM((GROUP * rows, 128), BF),
            pltpu.VMEM((128, GROUP * rows), BF),
            pltpu.VMEM((HD, GROUP * rows), BF),
            pltpu.VMEM((2, GROUP * rows, 128), BF),
            pltpu.VMEM((count, 1, blk), F32),
            pltpu.VMEM((blk, 128), F32),
        ],
        vmem=36,
    )


def stack_kernel(at_ref, *refs):
    ins, out_ref = refs[:GROUP], refs[GROUP]
    for s in range(GROUP):
        head = pl.ds(pl.multiple_of((at_ref[0] ^ s) * HD, HD), HD)
        out_ref[head, :] = ins[s][...]


def stack(at, heads):
    rows = heads[0].shape[1]
    return call(
        stack_kernel,
        "stack",
        at,
        (1,),
        [fixed((HD, rows))] * GROUP,
        fixed((GROUP * HD, rows)),
        like((GROUP * HD, rows), BF),
        heads,
    )


def unsplit_kernel(at_ref, *refs):
    ins, outs = refs[:4], refs[4:]
    cols = ins[0].shape[1]
    for r in range(4):
        lanes = pl.ds(pl.multiple_of(((at_ref[1] + r) % 4) * cols, cols), cols)
        for s in range(GROUP):
            head = pl.ds(pl.multiple_of((at_ref[0] ^ s) * HD, HD), HD)
            outs[s][:, lanes] = ins[r][head, :]


def unsplit(at, pieces):
    shape = (HD, 4 * pieces[0].shape[1])
    return call(
        unsplit_kernel,
        "unsplit",
        at,
        (1,),
        [fixed(pieces[0].shape)] * 4,
        [fixed(shape)] * GROUP,
        [like(shape, BF)] * GROUP,
        pieces,
    )


def heads_of(mine, r, features):
    return pl.ds(pl.multiple_of(((mine + 4 - r) % 4) * features, features), features)


def mid_kernel(at_ref, *refs):
    pieces, (w_ref, x_ref, gain_ref, bias_ref, h_ref, b_ref) = refs[:6], refs[6:]
    h = x_ref[...].astype(F32)
    for r, piece in enumerate(in_order(at_ref[1], *[ref[...] for ref in pieces])):
        rows = heads_of(at_ref[1], 4 - r, piece.shape[0])
        h = h + mm(turned(piece), w_ref[rows, :])

    @pl.when(pl.program_id(0) == 0)
    def _():
        h_ref[...] = h

    normal, _ = normalize(h)
    b_ref[...] = (normal * gain_ref[...] + bias_ref[...]).astype(BF)


def mid(at, pieces, w_o, tokens, gain, bias):
    features, rows = pieces[0].shape
    width, quarter = tokens.shape[1], rows // 4
    return call(
        mid_kernel,
        "mid",
        at,
        (4,),
        [pl.BlockSpec((features, quarter), lambda q, n: (0, (n[1] + q) % 4))] * 6
        + [fixed(w_o.shape)]
        + [pl.BlockSpec((quarter, width), lambda q, n: ((n[1] + q) % 4, 0))]
        + [fixed((1, width))] * 2,
        [fixed((quarter, width)), pl.BlockSpec((quarter, width), lambda q, n: (q, 0))],
        [like((quarter, width), F32), like((rows, width), BF)],
        (*pieces, w_o, tokens, gain, bias),
    )


def add_up(refs):
    total = refs[0][...]
    for ref in refs[1:]:
        total = total + ref[...].astype(F32)
    return total


def mid_back_kernel(at_ref, *refs):
    shares, (w_ref, h_ref, dy_ref, gain_ref, dh_ref, low_ref, sums_ref) = refs[:4], refs[4:11]
    do_refs = refs[11:]
    db = add_up(shares)
    normal, scale = normalize(h_ref[...])
    dh = dy_ref[...].astype(F32) + norm_back(db, gain_ref[...], normal, scale)
    dh_ref[...] = dh
    low = dh.astype(BF)
    low_ref[...] = low
    sums_ref[0:1, :] = jnp.sum(db * normal, axis=0, keepdims=True)
    sums_ref[1:2, :] = jnp.sum(db, axis=0, keepdims=True)
    for r in range(4):
        rows = heads_of(at_ref[1], r, do_refs[r].shape[0])
        do_refs[r][...] = mm_t(w_ref[rows, :], low).astype(BF)


def mid_back(at, shares, w_o, h, dy, gain):
    quarter, width = h.shape
    whole = fixed((quarter, width))
    piece = (w_o.shape[0] // 4, quarter)
    return call(
        mid_back_kernel,
        "mid_back",
        at,
        (1,),
        [whole] * 4 + [fixed(w_o.shape), whole, whole, fixed((1, width))],
        [whole] * 2 + [fixed((2, width))] + [fixed(piece)] * 4,
        [like((quarter, width), F32), like((quarter, width), BF), like((2, width), F32)]
        + [like(piece, BF)] * 4,
        (*shares, w_o, h, dy, gain),
    )


def first_back_kernel(at_ref, *refs):
    shares = refs[:4]
    x_ref, dh_ref, gain_ref, out_ref = refs[4:]
    d_a = add_up(shares)
    normal, scale = normalize(x_ref[...].astype(F32))
    out_ref[...] = (dh_ref[...] + norm_back(d_a, gain_ref[...], normal, scale)).astype(BF)


def first_back(at, shares, tokens, dh, gain):
    quarter, width = dh.shape
    return call(
        first_back_kernel,
        "first_back",
        at,
        (1,),
        [fixed((quarter, width))] * 4
        + [pl.BlockSpec((quarter, width), lambda i, n: (n[1], 0))]
        + [fixed((quarter, width)), fixed((1, width))],
        fixed((quarter, width)),
        like((quarter, width), BF),
        (*shares, tokens, dh, gain),
    )


def in_order(mine, own, right, left, far, right_two, left_two):
    one = jnp.where(mine == 3, far, left)
    two = jnp.where(mine < 2, left_two, right_two)
    three = jnp.where(mine == 0, far, right)
    return own, one, two, three


def one_hot(slots, dest):
    return jnp.where(slots == dest, 1.0, 0.0).astype(BF)


def dispatch_kernel(at_ref, dest_ref, rows_ref, out_ref, spread_s):
    blk, rows = min(256, spread_s.shape[0]), dest_ref.shape[1]

    @pl.when(pl.program_id(0) == 0)
    def _():
        slot = lax.broadcasted_iota(jnp.int32, (blk, rows), 0)
        for start in range(0, spread_s.shape[0], blk):
            spread_s[start : start + blk, :] = one_hot(slot + start, dest_ref[...])

    out_ref[...] = mm(spread_s[...], rows_ref[...]).astype(BF)


def columns(rows, width):
    return pl.BlockSpec((rows, width), lambda i, n: (0, i))


def dispatch(at, dest_row, values, slots):
    rows, width = values.shape
    blk = min(256, width)
    return call(
        dispatch_kernel,
        "dispatch",
        at,
        (width // blk,),
        [fixed((1, rows)), columns(rows, blk)],
        columns(slots, blk),
        like((slots, width), BF),
        (dest_row, values),
        scratch=[pltpu.VMEM((slots, rows), BF)],
    )


def join_kernel(at_ref, *refs):
    pieces, out_ref = refs[:6], refs[-1]
    r = pl.program_id(0)
    for place, piece in enumerate(in_order(at_ref[1], *[ref[...] for ref in pieces])):

        @pl.when(r == place)
        def _():
            out_ref[...] = piece


def join(at, pieces, after=()):
    each, width = pieces[0].shape
    return call(
        join_kernel,
        "join",
        at,
        (4,),
        [fixed((each, width))] * 6 + [pl.BlockSpec(memory_space=pl.ANY)] * len(after),
        pl.BlockSpec((each, width), lambda r, n: ((n[1] + r) % 4, 0)),
        like((4 * each, width), BF),
        (*pieces, *after),
    )


def write_shares(mine, total, own_ref, one_ref, two_ref, three_ref, end_ref):
    rows = own_ref.shape[0]
    own_ref[...] = total[:rows]
    one, two, three = [total[r * rows : (r + 1) * rows].astype(BF) for r in (1, 2, 3)]
    one_ref[...] = one
    two_ref[...] = two
    three_ref[...] = three
    end_ref[...] = jnp.where(mine == 0, three, one)


def share_shapes(rows, width):
    return [like((rows, width), F32)] + [like((rows, width), BF)] * 4


def combine_kernel(count, whole, at_ref, *refs):
    dests, backs = refs[:count], refs[count : 2 * count]
    base_ref, refs, pick_s = refs[2 * count], refs[2 * count + 1 : -1], refs[-1]
    rows, slots = base_ref.shape[0], backs[0].shape[0]
    blk = rows // 4

    @pl.when(pl.program_id(0) == 0)
    def _():
        lane = lax.broadcasted_iota(jnp.int32, (blk, slots), 1)
        for k in range(count):
            for start in range(0, rows, blk):
                dest = dests[k][start : start + blk, :]
                pick_s[start : start + blk, k * slots : (k + 1) * slots] = one_hot(lane, dest)

    total = base_ref[...].astype(F32)
    for k in range(count):
        total = total + mm(pick_s[:, k * slots : (k + 1) * slots], backs[k][...])
    mine = at_ref[1]
    if whole:
        h_ref, out_ref = refs
        for r in range(4):
            part = total[r * blk : (r + 1) * blk]
            if r == 0:
                part = part + h_ref[...]
            place = pl.ds(pl.multiple_of(((mine + r) % 4) * blk, blk), blk)
            out_ref[place, :] = part.astype(BF)
    else:
        write_shares(mine, total, *refs)


def combine(at, dests, backs, base, h=None):
    count, (slots, width), rows = len(backs), backs[0].shape, base.shape[0]
    blk = min(256, width)
    whole = h is not None
    quarter = columns(rows // 4, blk)
    return call(
        partial(combine_kernel, count, whole),
        "combine",
        at,
        (width // blk,),
        [fixed((rows, 1))] * count
        + [columns(slots, blk)] * count
        + [columns(rows, blk)]
        + [quarter] * whole,
        columns(rows, blk) if whole else [quarter] * 5,
        like(base.shape, BF) if whole else share_shapes(rows // 4, width),
        (*dests, *backs, base) + ((h,) if whole else ()),
        scratch=[pltpu.VMEM((rows, count * slots), BF)],
    )


def mm_t(a, b):
    return lax.dot_general(a, b, (((1,), (1,)), ((), ())), preferred_element_type=F32)


def gelu_both(u):
    c = 0.7978845608028654
    square = u * u
    t = jnp.tanh(u * (c + (c * 0.044715) * square))
    half = 0.5 + 0.5 * t
    slope = half + (0.5 * u) * (1.0 - t * t) * (c + (3.0 * c * 0.044715) * square)
    return u * half, slope


def high_low(value):
    high = value.astype(BF)
    return high, (value - high.astype(F32)).astype(BF)


def two_coefs(logits, lane, experts):
    inside = (lane >= experts) & (lane < experts + 2)
    top = jnp.max(jnp.where(inside, logits, HIDE), axis=1, keepdims=True)
    e = jnp.where(inside, jnp.exp(logits - top), 0.0)
    e = e / jnp.sum(e, axis=1, keepdims=True)
    first = jnp.sum(jnp.where(lane == experts, e, 0.0), axis=1, keepdims=True)
    second = jnp.sum(jnp.where(lane == experts + 1, e, 0.0), axis=1, keepdims=True)
    return first, second


def small_back(d_small, rows, w_small_ref, small_ref, i):
    high, low = high_low(d_small)
    w_small = w_small_ref[...]
    high_t, low_t = high_low(d_small.T)

    @pl.when(i == 0)
    def _():
        small_ref[...] = jnp.zeros(small_ref.shape, F32)

    small_ref[...] += mm(high_t, rows) + mm(low_t, rows)
    return mm_t(high, w_small) + mm_t(low, w_small)


def expert_kernel(experts, half, at_ref, rows_ref, dy_ref, up_ref, down_ref, w_small_ref, *outs):
    if half:
        outs = outs[5:]
    rows_out_ref, hid_ref, dy_out_ref, deu_ref, y_ref, d_rows_ref, small_ref = outs
    rows = rows_ref[...]
    rows_out_ref[...] = rows
    up = mm(rows, up_ref[...])
    logits = mm(rows, w_small_ref[...])
    lane = lax.broadcasted_iota(jnp.int32, logits.shape, 1)
    routed = lane < experts
    top = jnp.max(jnp.where(routed, logits, HIDE), axis=1, keepdims=True)
    probs = jnp.where(routed, jnp.exp(logits - top), 0.0)
    probs = probs / jnp.sum(probs, axis=1, keepdims=True)
    own = jnp.where(lane == at_ref[2], 1.0, 0.0)
    gate = jnp.sum(probs * own, axis=1, keepdims=True)
    first, second = two_coefs(logits, lane, experts)
    weight = second * gate
    dy = dy_ref[...].reshape(rows.shape).astype(F32)
    d_y = (weight * dy).astype(BF)
    dy_out_ref[...] = d_y
    d_hidden = mm_t(d_y, down_ref[...])
    hidden, slope = gelu_both(up)
    hidden = hidden.astype(BF)
    hid_ref[...] = hidden
    d_up = (d_hidden * slope).astype(BF)
    deu_ref[...] = d_up
    y = mm(hidden, down_ref[...])
    y_ref[...] = (weight * y).astype(BF).reshape(y_ref.shape)
    along = gate * jnp.sum(dy * y, axis=1, keepdims=True)
    mixed = first * second * along
    d_small = (second * along) * (own - probs)
    d_small = jnp.where(routed, d_small, 0.0)
    d_small = d_small + jnp.where(lane == experts + 1, mixed, 0.0)
    d_small = d_small - jnp.where(lane == experts, mixed, 0.0)
    d_rows = mm_t(d_up, up_ref[...]) + small_back(d_small, rows, w_small_ref, small_ref, pl.program_id(0))
    d_rows_ref[...] = d_rows.astype(BF)


def expert_rows(at, rows, dy, w_up, w_down, w_small, experts, half, before):
    count, width = rows.shape
    hid, lanes = w_up.shape[1], w_small.shape[1]
    blk = min(512, count)
    capacity = count // dy.shape[0]
    steps = count // blk
    moving = pl.BlockSpec((blk, width), lambda i, n: (i, 0))
    slots = pl.BlockSpec((blk // capacity, capacity, width), lambda i, n: (i, half, 0))
    kept = [pl.BlockSpec((blk, size), lambda i, n: (i + half * steps, 0)) for size in (width, hid, width, hid)]
    return call(
        partial(expert_kernel, experts, half),
        "expert_rows",
        at,
        (steps,),
        [
            moving,
            slots,
            fixed((width, hid)),
            fixed((hid, width)),
            fixed((width, lanes)),
        ]
        + [pl.BlockSpec(memory_space=pl.ANY)] * (5 * half),
        kept + [slots, moving, fixed((lanes, width))],
        [like((2 * count, size), BF) for size in (width, hid, width, hid)]
        + [like(dy.shape, BF), like((count, width), BF)]
        + [like((lanes, width), F32)],
        (rows, dy, w_up, w_down, w_small, *before),
        alias={6 + k: k for k in range(5)} if half else None,
        vmem=56,
    )


def dense_kernel(experts, at_ref, rows_ref, dy_ref, in_ref, out_ref, w_small_ref, *outs):
    hid_ref, grad_ref, d_up_ref, mix_ref, db_ref, small_ref = outs
    rows = rows_ref[...]
    up = mm(rows, in_ref[...])
    logits = mm(rows, w_small_ref[...])
    lane = lax.broadcasted_iota(jnp.int32, logits.shape, 1)
    first, second = two_coefs(logits, lane, experts)
    dy = dy_ref[...].astype(F32)
    grad = (first * dy).astype(BF)
    grad_ref[...] = grad
    d_hidden = mm_t(grad, out_ref[...])
    hidden, slope = gelu_both(up)
    hidden = hidden.astype(BF)
    hid_ref[...] = hidden
    d_up = (d_hidden * slope).astype(BF)
    d_up_ref[...] = d_up
    dense = mm(hidden, out_ref[...])
    mix_ref[...] = first * dense
    mixed = first * second * jnp.sum(dy * dense, axis=1, keepdims=True)
    d_small = jnp.where(lane == experts, mixed, 0.0) - jnp.where(lane == experts + 1, mixed, 0.0)
    db_ref[...] = mm_t(d_up, in_ref[...]) + small_back(d_small, rows, w_small_ref, small_ref, pl.program_id(0))


def dense_rows(at, rows, dy, w_in, w_out, w_small, experts):
    (count, width), hid, lanes = rows.shape, w_in.shape[1], w_small.shape[1]
    blk = min(512, count)
    row_out = pl.BlockSpec((blk, width), lambda i, n: (i, 0))
    hid_out = pl.BlockSpec((blk, hid), lambda i, n: (i, 0))
    return call(
        partial(dense_kernel, experts),
        "dense_rows",
        at,
        (count // blk,),
        [row_out, row_out, fixed((width, hid)), fixed((hid, width)), fixed((width, lanes))],
        [hid_out, row_out, hid_out, row_out, row_out, fixed((lanes, width))],
        [
            like((count, hid), BF),
            like((count, width), BF),
            like((count, hid), BF),
            like((count, width), F32),
            like((count, width), F32),
            like((lanes, width), F32),
        ],
        (rows, dy, w_in, w_out, w_small),
        vmem=56,
    )


def turned(value):
    return value.astype(F32).T.astype(BF)


def dense_grads_kernel(at_ref, b_ref, d_up_ref, grad_ref, hid_ref, keep_ref, give_ref):
    width = d_up_ref.shape[1]
    first = mm(turned(b_ref[...]), d_up_ref[...]).astype(BF)
    second = mm(turned(grad_ref[...]), hid_ref[...]).astype(BF)
    half = pl.num_programs(0) // 2
    for side, ref in ((0, keep_ref), (1, give_ref)):

        @pl.when(pl.program_id(0) // half == side)
        def _():
            ref[0, :, :width] = first
            ref[0, :, width:] = second


def dense_grads(at, b, d_up, grad, hidden, parts):
    (rows, width), hid = b.shape, hidden.shape[1]
    own, half, bits = width // parts, parts // 2, parts.bit_length() - 1

    def part(q, n):
        turned_q = sum([((q // 2**k) % 2) * 2 ** (bits - 1 - k) for k in range(bits)])
        return turned_q ^ n[2]

    column = pl.BlockSpec((rows, own), lambda q, n: (0, part(q, n)))
    shape = (1, own, 2 * hid)
    return call(
        dense_grads_kernel,
        "dense_grads",
        at,
        (parts,),
        [column, fixed((rows, hid)), column, fixed((rows, hid))],
        [
            pl.BlockSpec(shape, lambda q, n: (jnp.minimum(q, half - 1), 0, 0)),
            pl.BlockSpec(shape, lambda q, n: (jnp.maximum(q - half, 0), 0, 0)),
        ],
        [like((half, own, 2 * hid), BF)] * 2,
        (b, d_up, grad, hidden),
    )


def attention_grads_kernel(experts, at_ref, *refs):
    grads, o_refs, refs = refs[:GROUP], refs[GROUP : GROUP + 6], refs[GROUP + 6 :]
    a_ref, dh_ref, w_ref, gain_ref, bias_ref, sums_ref = refs[:6]
    small_refs, outs, all_s = refs[6:9], refs[9:-1], refs[-1]
    heads, features = GROUP * HD, grads[1].shape[0]
    products, plain = 0.0, 0.0
    for k in range(GROUP):
        head = at_ref[0] ^ k
        rows = pl.ds(pl.multiple_of(head * features, features), features)
        grad = grads[k][...]
        weight = w_ref[head].astype(F32)
        total = mm(grad, a_ref[...])
        all_s[rows, :] = total
        each = jnp.sum(grad.astype(F32), axis=1, keepdims=True)
        products = products + jnp.sum(total * weight, axis=0, keepdims=True)
        plain = plain + jnp.sum(each * weight, axis=0, keepdims=True)
    first = GROUP * features
    for r, piece in enumerate(in_order(at_ref[1], *[ref[...] for ref in o_refs])):
        rows = pl.ds(pl.multiple_of(first + ((at_ref[1] + r) % 4) * heads, heads), heads)
        all_s[rows, :] = mm(piece, dh_ref[...])
    first += 4 * heads
    small = add_up(small_refs)
    row = lax.broadcasted_iota(jnp.int32, small.shape, 0)
    d_gain = (products - bias_ref[...] * plain) / gain_ref[...]
    for k, sums in enumerate((sums_ref[0:1, :], sums_ref[1:2, :], d_gain, plain)):
        small = jnp.where(row == experts + 2 + k, sums, small)
    all_s[first:, :] = small
    both = all_s[...].T.astype(BF)
    if len(outs) == 1:
        outs[0][...] = both
    else:
        own, even = outs[0].shape[1], at_ref[2] % 2 == 0
        outs[0][0] = jnp.where(even, both[:own], both[own:])
        outs[1][0] = jnp.where(even, both[own:], both[:own])


def attention_grads(at, grads, o, a, dh, w_heads, gain, bias, sums, small, experts):
    rows, width = a.shape
    features, lanes = grads[0].shape[0], small[0].shape[0]
    piece = pl.BlockSpec((o[0].shape[0], dh.shape[0]), lambda i, n: (0, n[1]))
    height = GROUP * features + 4 * o[0].shape[0] + lanes
    parts = lax.axis_size("dp")
    own, half, bits = width // parts, parts // 2, parts.bit_length() - 2
    blk = min(256, width)

    def slot(i, n):
        rest = i ^ (n[2] // 2)
        return sum([((rest // 2**k) % 2) * 2 ** (bits - 1 - k) for k in range(bits)]), 0, 0

    out_specs = [pl.BlockSpec((1, own, height), slot)] * 2
    out_shape = [like((half, own, height), BF)] * 2
    if blk != 2 * own:
        out_specs = [pl.BlockSpec((blk, height), lambda i, n: (i, 0))]
        out_shape = [like((width, height), BF)]
    return call(
        partial(attention_grads_kernel, experts),
        "attention_grads",
        at,
        (width // blk,),
        [fixed((features, rows))] * GROUP
        + [piece] * 6
        + [columns(rows, blk), columns(dh.shape[0], blk)]
        + [pl.BlockSpec((GROUP, features, blk), lambda i, n: (0, 0, i))]
        + [columns(1, blk)] * 2
        + [columns(2, blk)]
        + [columns(lanes, blk)] * len(small),
        out_specs,
        out_shape,
        (*grads, *o, a, dh, w_heads, gain, bias, sums, *small),
        scratch=[pltpu.VMEM((height, blk), F32)],
    )


def project_kernel(at_ref, *refs):
    grads, w_ref, outs, turned_s = refs[:GROUP], refs[GROUP], refs[GROUP + 1 : -1], refs[-1]
    rows = turned_s.shape[1]
    blk = rows // 4

    @pl.when(pl.program_id(0) == 0)
    def _():
        for s in range(GROUP):
            for r in range(4):
                lanes = pl.ds(pl.multiple_of(((at_ref[1] + r) % 4) * blk, blk), blk)
                turned_s[s, r * blk : (r + 1) * blk, :] = turned(grads[s][:, lanes])

    total = 0.0
    for s in range(GROUP):
        total = total + mm(turned_s[s], w_ref[at_ref[0] ^ s])
    write_shares(at_ref[1], total, *outs)


def project_back(at, grads, w_heads):
    features, rows = grads[0].shape
    width = w_heads.shape[2]
    blk = min(256, width)
    return call(
        project_kernel,
        "project_back",
        at,
        (width // blk,),
        [fixed((features, rows))] * GROUP
        + [pl.BlockSpec((GROUP, features, blk), lambda i, n: (0, 0, i))],
        [columns(rows // 4, blk)] * 5,
        share_shapes(rows // 4, width),
        (*grads, w_heads),
        scratch=[pltpu.VMEM((GROUP, rows, features), BF)],
    )


def hop(value, *pairs):
    return lax.ppermute(value, "mp", pairs)


def rotate(value, steps):
    return hop(value, *[(s, (s + steps) % 4) for s in range(4)])


def gather_near(own):
    right = hop(own, (0, 1), (1, 2), (2, 3))
    left = hop(own, (1, 0), (2, 1), (3, 2))
    return own, right, left, hop(own, (0, 3), (3, 0))


def gather_far(near):
    _, right, left, _ = near
    return *near, hop(right, (1, 2), (2, 3)), hop(left, (1, 0), (2, 1))


def gather_pieces(own):
    return gather_far(gather_near(own))


def scatter_far(shares):
    _, _, two, _, end = shares
    return hop(two, (2, 1), (3, 2)), hop(two, (0, 1), (1, 2)), hop(end, (0, 3), (3, 0))


def scatter_near(shares, came):
    own, one, _, three, _ = shares
    from_right, from_left, from_end = came
    three = (three.astype(F32) + from_right.astype(F32)).astype(BF)
    one = (one.astype(F32) + from_left.astype(F32)).astype(BF)
    return own, hop(three, (1, 0), (2, 1), (3, 2)), hop(one, (0, 1), (1, 2), (2, 3)), from_end


def group_swap(value, s):
    count = lax.axis_size("dp")
    return lax.ppermute(value, "dp", [(t, t ^ s) for t in range(count)])


def expert_swap(value, experts):
    wide = value.reshape(experts, value.shape[0] // experts, value.shape[1])
    return lax.all_to_all(wide, "dp", 0, 0, tiled=True).reshape(value.shape)


def roll_rows(value, start):
    twice = jnp.concatenate([value, value], axis=0)
    return lax.dynamic_slice_in_dim(twice, start, value.shape[0], 0)


def dp_halving(keep, give):
    grads, bit = (keep, group_swap(give, 1)), 2
    while grads[0].shape[0] > 1:
        half = grads[0].shape[0] // 2
        give = add_halves(grads[0][half:], grads[1][half:])
        keep = add_halves(grads[0][:half], grads[1][:half])
        grads, bit = (keep, group_swap(give, bit)), 2 * bit
    return add_halves(*grads)[0]


def add_halves(keep, came):
    return (keep.astype(F32) + came.astype(F32)).astype(BF)


def body(
    tokens,
    cotangent,
    ln_gains,
    ln_biases,
    w_qkv,
    w_o,
    w_in,
    w_out,
    w_router,
    w_coef,
    w_up,
    w_down,
    routes,
    long_group,
):
    rows, width = tokens.shape
    dps = lax.axis_size("dp")
    mine, position = lax.axis_index("mp"), lax.axis_index("dp")
    quarter = rows // 4
    start = mine * quarter
    heads_loc = w_qkv.shape[2] // HD
    hid = w_in.shape[1]
    experts = w_router.shape[1]
    capacity = max(2, 2 * rows // experts)
    half = capacity // 2
    barrier = lax.optimization_barrier
    first_len = lax.dynamic_index_in_dim(long_group, position // GROUP, 0, keepdims=False)
    at = jnp.stack([position % GROUP, mine, position, first_len]).astype(jnp.int32)
    gains = [ln_gains[0:1], ln_gains[1:2]]
    biases = [ln_biases[0:1], ln_biases[1:2]]
    w_o_all = lax.all_gather(w_o, "mp", axis=0, tiled=True)

    w_heads = w_qkv.reshape(width, 3, heads_loc, HD).transpose(2, 1, 3, 0)
    w_heads = w_heads.reshape(heads_loc, 3 * HD, width)
    a_r, *qkv = project(at, tokens, gains[0], biases[0], w_heads)
    qkv = [qkv[0]] + [group_swap(qkv[s], s) for s in (1, 2, 3)]

    route = roll_rows(routes, start)[:, 0]
    picked = (route[:, None] == jnp.arange(experts, dtype=jnp.int32)[None, :]).astype(jnp.int32)
    slot = jnp.sum((jnp.cumsum(picked, axis=0) - picked) * picked, axis=1)
    dy_b = roll_rows(cotangent, start)
    full = route * capacity + slot
    send_dy = dispatch(at, full[None, :], dy_b, experts * capacity)
    *qkv, send_dy = barrier((*qkv, send_dy))
    in_half = [slot < half, slot >= half]
    dests = [
        jnp.where(in_half[k], route * half + slot - k * half, -1).astype(jnp.int32) for k in (0, 1)
    ]

    *o_t, lse = attend(at, qkv)
    *o_t, w_o_all = barrier((*o_t, w_o_all))
    o_heads = [o_t[0]] + [group_swap(o_t[s], s) for s in (1, 2, 3)]
    lanes = -(-(experts + 2) // 128) * 128
    w_small = jnp.concatenate(
        [w_router, w_coef, jnp.zeros((width, lanes - experts - 2), BF)], axis=1
    )
    *o_heads, send_dy, w_small = barrier((*o_heads, send_dy, w_small))
    got_dy = expert_swap(send_dy, experts).reshape(experts, capacity, width)
    o_pieces = gather_pieces(stack(at, o_heads))
    h, b_r = mid(at, o_pieces, w_o_all, tokens, gains[1], biases[1])

    send_0 = dispatch(at, dests[0][None, :], b_r, experts * half)
    send_0, got_dy = barrier((send_0, got_dy))
    got_0 = expert_swap(send_0, experts)
    send_1 = dispatch(at, dests[1][None, :], b_r, experts * half)
    b_r, send_1 = barrier((b_r, send_1))
    hidden, dense_grad, d_up, mix_base, db_base, small_t = dense_rows(
        at, b_r, dy_b, w_in, w_out, w_small, experts
    )
    send_1, got_0, db_base = barrier((send_1, got_0, db_base))
    got_1 = expert_swap(send_1, experts)

    *kept, d_rows_0, small_0 = expert_rows(
        at, got_0, got_dy, w_up[0], w_down[0], w_small, experts, 0, ()
    )
    back_0 = expert_swap(d_rows_0, experts)
    *kept, d_rows_1, small_1 = expert_rows(
        at, got_1, got_dy, w_up[0], w_down[0], w_small, experts, 1, kept
    )
    got, hidden_e, d_y, d_eu, back_y = kept
    back_1 = expert_swap(d_rows_1, experts)
    d_rows_1, b_r = barrier((d_rows_1, b_r))
    halving = width == dps * 128
    if halving:
        grads = dense_grads(at, b_r, d_up, dense_grad, hidden, dps)
    else:
        grads = [ein("td,tf->df", b_r, d_up).astype(BF), ein("td,tf->df", dense_grad, hidden).astype(BF)]
    back_0, back_1, back_y, *grads = barrier((back_0, back_1, back_y, *grads))

    dest_cols = [dest[:, None] for dest in dests]
    tok_y = expert_swap(back_y.reshape(experts * capacity, width), experts)
    shares = combine(at, dest_cols, [back_0, back_1], db_base)
    far = scatter_far(shares)
    *far, g_0, g_1 = barrier((*far, *grads))
    grads = [g_0, g_1]
    shares = scatter_near(shares, far)

    mix = combine(at, [full[:, None]], [tok_y], mix_base, h)
    *shares, mix = barrier((*shares, mix))
    output = lax.psum(mix, "mp")
    dh, dh_r, sums_2, *do_q = mid_back(at, shares, w_o_all, h, dy_b, gains[1])
    do_q = [do_q[0]] + [rotate(do_q[r], -r) for r in (1, 2, 3)]
    do_heads = unsplit(at, do_q)
    do_t = [do_heads[0]] + [group_swap(do_heads[s], s) for s in (1, 2, 3)]
    if halving:
        came_1 = group_swap(grads[1], 1)
        half = dps // 4
        give = add_halves(grads[0][half:], came_1[half:])
        *do_t, give = barrier((*do_t, give))
        came_2 = group_swap(give, 2)
    d_qkv = attend_back(at, qkv, do_t, o_t, lse)
    if halving:
        keep = add_halves(grads[0][:half], came_1[:half])
        *d_qkv, came_2, keep = barrier((*d_qkv, came_2, keep))
        grads = add_halves(keep, came_2)
        bit = 4
        while bit < dps:
            half = grads.shape[0] // 2
            grads = add_halves(grads[:half], group_swap(grads[half:], bit))
            bit *= 2
        grads = [grads[0][:, :hid], grads[0][:, hid:]]
    else:
        grads = [lax.psum_scatter(grad, "dp", scatter_dimension=0, tiled=True) for grad in grads]

    d_own, got, hidden_e, d_y, d_eu = barrier((d_qkv[0], got, hidden_e, d_y, d_eu))
    d_qkv = [d_own] + [group_swap(d_qkv[s], s) for s in (1, 2, 3)]
    grad_down = ein("rf,rd->fd", hidden_e, d_y)
    *d_qkv, grad_down = barrier((*d_qkv, grad_down))
    shares = project_back(at, d_qkv, w_heads)
    far = scatter_far(shares)
    grads_a = attention_grads(
        at, d_qkv, o_pieces, a_r, dh_r, w_heads, gains[0], biases[0], sums_2, (small_0, small_1, small_t), experts
    )
    grad_up = ein("rd,rf->df", got, d_eu)
    output, grad_up, *tied = barrier((output, grad_up, *far, *grads_a))
    far, grads_a = tied[:3], tied[3:]
    if halving:
        grads_a = dp_halving(*grads_a).T
    else:
        grads_a = lax.psum_scatter(grads_a[0], "dp", scatter_dimension=0, tiled=True).T
    shares = scatter_near(shares, far)
    grad_q = first_back(at, shares, tokens, dh, gains[0])
    pieces = gather_pieces(grad_q)

    own, heads = width // dps, heads_loc * HD
    grad_qkv = grads_a[: 3 * heads].astype(F32).reshape(heads_loc, 3, HD, own).transpose(3, 1, 0, 2)
    grad_qkv = grad_qkv.reshape(own, 3, heads)
    grad_in = grads[0].astype(F32)
    grad_out = grads[1].astype(F32).T
    rest = grads_a[3 * heads : 7 * heads].reshape(4, heads, own)
    small = jnp.broadcast_to(grads_a[7 * heads :], (4, lanes, own))
    rest = lax.all_to_all(jnp.concatenate([rest, small], axis=1), "mp", 0, 0, tiled=True)
    rest = jnp.sum(rest.astype(F32), axis=0)
    grad_tokens = join(at, pieces, (rest, grad_in, grad_out, grad_qkv))
    grad_o, small = rest[:heads], rest[heads:]
    small_out = small[: experts + 2].T
    return (
        output,
        grad_tokens,
        jnp.stack([small[experts + 4], small[experts + 2]]),
        jnp.stack([small[experts + 5], small[experts + 3]]),
        grad_qkv,
        grad_o,
        grad_in,
        grad_out,
        small_out[:, :experts],
        small_out[:, experts:],
        grad_up[None],
        grad_down[None],
    )


def solution(mesh):
    in_specs = (
        P("dp", None),
        P("dp", None),
        P(),
        P(),
        P(None, None, "mp"),
        P("mp", None),
        P(None, "mp"),
        P("mp", None),
        P(),
        P(),
        P("dp", None, "mp"),
        P("dp", "mp", None),
        P("dp", None),
        P(),
    )
    out_specs = (
        P("dp", None),
        P("dp", None),
        P(None, "dp"),
        P(None, "dp"),
        P("dp", None, "mp"),
        P("mp", "dp"),
        P("dp", "mp"),
        P("mp", "dp"),
        P("dp", None),
        P("dp", None),
        P("dp", None, "mp"),
        P("dp", "mp", None),
    )
    return jax.shard_map(body, mesh=mesh, in_specs=in_specs, out_specs=out_specs, check_vma=False)
```

```python
from functools import partial

import jax
import jax.numpy as jnp
from jax import lax
from jax.experimental import pallas as pl
from jax.experimental.pallas import tpu as pltpu
from jax.sharding import PartitionSpec as P

HD = 64
GROUP = 4
EPS = 1e-05
LOG2E = 1.4426950408889634
SCALE2 = 0.125 * LOG2E
HIDE = -1e30
BF = jnp.bfloat16
F32 = jnp.float32
LIGHT = pl.CostEstimate(flops=1 << 20, bytes_accessed=1 << 20, transcendentals=0)


def mm(a, b):
    return jnp.dot(a, b, preferred_element_type=F32)


def ein(spec, a, b):
    return jnp.einsum(spec, a, b, preferred_element_type=F32)


def call(kernel, name, prefetch, grid, in_specs, out_specs, out_shape, args, scratch=(), alias=None, vmem=48):
    return pl.pallas_call(
        kernel,
        grid_spec=pltpu.PrefetchScalarGridSpec(
            num_scalar_prefetch=1,
            grid=grid,
            in_specs=in_specs,
            out_specs=out_specs,
            scratch_shapes=list(scratch),
        ),
        out_shape=out_shape,
        input_output_aliases=alias or {},
        compiler_params=pltpu.CompilerParams(vmem_limit_bytes=vmem * 2**20),
        cost_estimate=LIGHT,
        name=name,
    )(prefetch, *args)


def fixed(shape):
    zeros = (0,) * len(shape)
    return pl.BlockSpec(shape, lambda *_: zeros)


def like(shape, dtype):
    return jax.ShapeDtypeStruct(shape, dtype)


def normalize(v):
    mean = jnp.mean(v, axis=-1, keepdims=True)
    centred = v - mean
    scale = lax.rsqrt(jnp.mean(centred * centred, axis=-1, keepdims=True) + EPS)
    return centred * scale, scale


def norm_back(grad, gain, normal, scale):
    g = grad * gain
    along = jnp.mean(g * normal, axis=-1, keepdims=True)
    return scale * (g - jnp.mean(g, axis=-1, keepdims=True) - normal * along)


def qkv_kernel(at_ref, x_ref, gain_ref, bias_ref, w_ref, a_ref, *outs):
    normal, _ = normalize(x_ref[...].astype(F32))
    a = (normal * gain_ref[...] + bias_ref[...]).astype(BF)
    a_ref[...] = a
    for s in range(GROUP):
        outs[s][...] = mm_t(w_ref[at_ref[0] ^ s], a).astype(BF)


def project(at, tokens, gain, bias, w_heads):
    rows, width = tokens.shape
    features = w_heads.shape[1]
    blk = min(256, rows)
    moving = pl.BlockSpec((blk, width), lambda i, n: (i, 0))
    return call(
        qkv_kernel,
        "project",
        at,
        (rows // blk,),
        [moving, fixed((1, width)), fixed((1, width)), fixed(w_heads.shape)],
        [moving] + [pl.BlockSpec((features, blk), lambda i, n: (0, i))] * GROUP,
        [like((rows, width), BF)] + [like((features, rows), BF)] * GROUP,
        (tokens, gain, bias, w_heads),
    )


def fill_keys(k_s, place, keys, first_len, blk):
    rows = place * blk + lax.broadcasted_iota(jnp.int32, (blk, 128), 0)
    lane = lax.broadcasted_iota(jnp.int32, (blk, 128), 1)
    wide = jnp.concatenate([keys.astype(F32).T, jnp.zeros((blk, 128 - HD), F32)], axis=1)
    wide = jnp.where((lane == HD) & (rows < first_len), HIDE, wide)
    k_s[pl.ds(place * blk, blk), :] = wide.astype(BF)


def wide_query(query, place, first_len, blk):
    cols = place * blk + lax.broadcasted_iota(jnp.int32, (128 - HD, blk), 1)
    sub = lax.broadcasted_iota(jnp.int32, (128 - HD, blk), 0)
    extra = jnp.where((sub == 0) & (cols >= first_len), 1.0, 0.0)
    return jnp.concatenate([query, extra.astype(BF)], axis=0)


def causal(blk):
    keys = lax.broadcasted_iota(jnp.int32, (blk, blk), 0)
    queries = lax.broadcasted_iota(jnp.int32, (blk, blk), 1)
    return keys <= queries


def attend_kernel(blk, per, at_ref, *refs):
    qkv_refs, o_refs = refs[:GROUP], refs[GROUP : 2 * GROUP]
    lse_ref, k_s, qkv_s = refs[2 * GROUP :]
    i = pl.program_id(0)
    place, first_len = at_ref[0], at_ref[3]

    @pl.when(i == 0)
    def _():
        for s in range(GROUP):
            qkv_s[place ^ s] = qkv_refs[s][...]

    def part(which, j):
        return qkv_s[j // per, HD * which : HD * (which + 1), pl.ds((j % per) * blk, blk)]

    fill_keys(k_s, i, part(1, i), first_len, blk)
    query = wide_query(part(0, i), i, first_len, blk)

    def scores(j):
        return mm(k_s[pl.ds(pl.multiple_of(j * blk, blk), blk), :], query)

    s = jnp.where(causal(blk), scores(i), HIDE)
    top = jnp.max(s, axis=0, keepdims=True)
    p = jnp.exp2((s - top) * SCALE2)
    total = jnp.sum(p, axis=0, keepdims=True)
    acc = mm(part(2, i), p.astype(BF))

    def steps(blocks, carry):
        top, total, acc = carry
        s = [scores(j) for j in blocks]
        new = top
        for one in s:
            new = jnp.maximum(new, jnp.max(one, axis=0, keepdims=True))
        keep = jnp.exp2((top - new) * SCALE2)
        total, acc = total * keep, acc * keep
        for j, one in zip(blocks, s):
            p = jnp.exp2((one - new) * SCALE2)
            total = total + jnp.sum(p, axis=0, keepdims=True)
            acc = acc + mm(part(2, j), p.astype(BF))
        return new, total, acc

    low = jnp.where(i * blk >= first_len, first_len // blk, 0)
    pairs = (i - low) // 2
    carry = lax.fori_loop(
        0, pairs, lambda t, c: steps([low + 2 * t, low + 2 * t + 1], c), (top, total, acc)
    )
    top, total, acc = lax.fori_loop(low + 2 * pairs, i, lambda j, c: steps([j], c), carry)
    out = (acc / total).astype(BF)
    for s in range(GROUP):

        @pl.when((i // per) ^ place == s)
        def _():
            o_refs[s][:, pl.ds((i % per) * blk, blk)] = out

    lse_ref[0] = top * SCALE2 + jnp.log2(total)


def attend(at, qkv):
    features, rows = qkv[0].shape
    blk = min(512, rows)
    per = rows // blk
    count = GROUP * per
    return call(
        partial(attend_kernel, blk, per),
        "attend",
        at,
        (count,),
        [fixed((features, rows))] * GROUP,
        [fixed((HD, rows))] * GROUP + [pl.BlockSpec((1, 1, blk), lambda i, n: (i, 0, 0))],
        [like((HD, rows), BF)] * GROUP + [like((count, 1, blk), F32)],
        qkv,
        scratch=[pltpu.VMEM((GROUP * rows, 128), BF), pltpu.VMEM((GROUP, features, rows), BF)],
    )


def back_kernel(blk, per, count, at_ref, *refs):
    qkv_refs, do_refs, o_refs = refs[:GROUP], refs[GROUP : 2 * GROUP], refs[2 * GROUP : 3 * GROUP]
    lse_ref, refs = refs[3 * GROUP], refs[3 * GROUP + 1 :]
    out_refs, refs = refs[:GROUP], refs[GROUP:]
    dq_ref, out_ref, k_s, kt_s, v_s, wide_s, dot_s, both_s, delta_s, acc_s = refs
    j = pl.program_id(0)
    place, first_len = at_ref[0], at_ref[3]

    @pl.when(j == 0)
    def _():
        dq_ref[...] = jnp.zeros(dq_ref.shape, F32)
        zero = jnp.zeros((blk, HD), F32)
        for s in range(GROUP):
            for sub in range(per):
                i = (place ^ s) * per + sub
                at = pl.ds(pl.multiple_of(i * blk, blk), blk)
                cut = slice(sub * blk, (sub + 1) * blk)
                query = qkv_refs[s][0:HD, cut]
                keys = qkv_refs[s][HD : 2 * HD, cut]
                grad = do_refs[s][:, cut]
                fill_keys(k_s, i, keys, first_len, blk)
                kt_s[:, at] = keys
                dot_s[:, at] = grad
                wide_s[:, at] = wide_query(query, i, first_len, blk)
                grad = grad.astype(F32)
                values = qkv_refs[s][2 * HD :, cut].astype(F32)
                v_s[at, :] = jnp.concatenate([values.T, zero], axis=1).astype(BF)
                both_s[0, at, :] = jnp.concatenate([grad.T, zero], axis=1).astype(BF)
                both_s[1, at, :] = jnp.concatenate([zero, query.astype(F32).T], axis=1).astype(BF)
                held = o_refs[s][:, cut].astype(F32)
                delta_s[i] = jnp.sum(held * grad, axis=0, keepdims=True)

    here = pl.ds(pl.multiple_of(j * blk, blk), blk)
    keys_t = kt_s[:, here]
    values = v_s[here, 0:HD]

    def pair(i, diagonal):
        at = pl.ds(pl.multiple_of(i * blk, blk), blk)
        s = mm(k_s[here, :], wide_s[:, at])
        p = jnp.exp2(s * SCALE2 - lse_ref[i])
        if diagonal:
            p = jnp.where(causal(blk), p, 0.0)
        dp = mm(values, dot_s[:, at])
        ds = (p * (dp - delta_s[i])).astype(BF)
        return mm(p.astype(BF), both_s[0, at, :]) + mm(ds, both_s[1, at, :]), mm(keys_t, ds)

    acc_s[...], dq = pair(j, True)
    dq_ref[:, here] += dq

    def step_two(t, carry):
        i = j + 1 + 2 * t
        (kv_0, dq_0), (kv_1, dq_1) = pair(i, False), pair(i + 1, False)
        acc_s[...] += kv_0 + kv_1
        at = pl.ds(pl.multiple_of(i * blk, blk), 2 * blk)
        dq_ref[:, at] += jnp.concatenate([dq_0, dq_1], axis=1)
        return carry

    def step(i, carry):
        kv, dq = pair(i, False)
        acc_s[...] += kv
        dq_ref[:, pl.ds(pl.multiple_of(i * blk, blk), blk)] += dq
        return carry

    high = jnp.where((j + 1) * blk <= first_len, (first_len + blk - 1) // blk, count)
    pairs = (high - j - 1) // 2
    lax.fori_loop(0, pairs, step_two, 0)
    lax.fori_loop(j + 1 + 2 * pairs, high, step, 0)
    both = acc_s[...].T
    out_ref[0:HD, :] = (dq_ref[:, here] * 0.125).astype(BF)
    out_ref[HD : 2 * HD, :] = (both[HD:, :] * 0.125).astype(BF)
    out_ref[2 * HD :, :] = both[:HD, :].astype(BF)
    for s in range(GROUP):

        @pl.when((j // per) ^ place == s)
        def _():
            out_refs[s][:, pl.ds(pl.multiple_of((j % per) * blk, blk), blk)] = out_ref[...]


def attend_back(at, qkv, do, o, lse):
    features, rows = qkv[0].shape
    blk = min(512, rows)
    per = rows // blk
    count = GROUP * per
    return call(
        partial(back_kernel, blk, per, count),
        "attend_back",
        at,
        (count,),
        [fixed((features, rows))] * GROUP
        + [fixed((HD, rows))] * (2 * GROUP)
        + [fixed((count, 1, blk))],
        [fixed((features, rows))] * GROUP,
        [like((features, rows), BF)] * GROUP,
        (*qkv, *do, *o, lse),
        scratch=[
            pltpu.VMEM((HD, GROUP * rows), F32),
            pltpu.VMEM((features, blk), BF),
            pltpu.VMEM((GROUP * rows, 128), BF),
            pltpu.VMEM((HD, GROUP * rows), BF),
            pltpu.VMEM((GROUP * rows, 128), BF),
            pltpu.VMEM((128, GROUP * rows), BF),
            pltpu.VMEM((HD, GROUP * rows), BF),
            pltpu.VMEM((2, GROUP * rows, 128), BF),
            pltpu.VMEM((count, 1, blk), F32),
            pltpu.VMEM((blk, 128), F32),
        ],
        vmem=36,
    )


def stack_kernel(at_ref, *refs):
    ins, out_ref = refs[:GROUP], refs[GROUP]
    for s in range(GROUP):
        head = pl.ds(pl.multiple_of((at_ref[0] ^ s) * HD, HD), HD)
        out_ref[head, :] = ins[s][...]


def stack(at, heads):
    rows = heads[0].shape[1]
    return call(
        stack_kernel,
        "stack",
        at,
        (1,),
        [fixed((HD, rows))] * GROUP,
        fixed((GROUP * HD, rows)),
        like((GROUP * HD, rows), BF),
        heads,
    )


def unsplit_kernel(at_ref, *refs):
    ins, outs = refs[:4], refs[4:]
    cols = ins[0].shape[1]
    for r in range(4):
        lanes = pl.ds(pl.multiple_of(((at_ref[1] + r) % 4) * cols, cols), cols)
        for s in range(GROUP):
            head = pl.ds(pl.multiple_of((at_ref[0] ^ s) * HD, HD), HD)
            outs[s][:, lanes] = ins[r][head, :]


def unsplit(at, pieces):
    shape = (HD, 4 * pieces[0].shape[1])
    return call(
        unsplit_kernel,
        "unsplit",
        at,
        (1,),
        [fixed(pieces[0].shape)] * 4,
        [fixed(shape)] * GROUP,
        [like(shape, BF)] * GROUP,
        pieces,
    )


def heads_of(mine, r, features):
    return pl.ds(pl.multiple_of(((mine + 4 - r) % 4) * features, features), features)


def mid_kernel(at_ref, *refs):
    pieces, (w_ref, x_ref, gain_ref, bias_ref, h_ref, b_ref) = refs[:6], refs[6:]
    h = x_ref[...].astype(F32)
    for r, piece in enumerate(in_order(at_ref[1], *[ref[...] for ref in pieces])):
        rows = heads_of(at_ref[1], 4 - r, piece.shape[0])
        h = h + mm(turned(piece), w_ref[rows, :])

    @pl.when(pl.program_id(0) == 0)
    def _():
        h_ref[...] = h

    normal, _ = normalize(h)
    b_ref[...] = (normal * gain_ref[...] + bias_ref[...]).astype(BF)


def mid(at, pieces, w_o, tokens, gain, bias):
    features, rows = pieces[0].shape
    width, quarter = tokens.shape[1], rows // 4
    return call(
        mid_kernel,
        "mid",
        at,
        (4,),
        [pl.BlockSpec((features, quarter), lambda q, n: (0, (n[1] + q) % 4))] * 6
        + [fixed(w_o.shape)]
        + [pl.BlockSpec((quarter, width), lambda q, n: ((n[1] + q) % 4, 0))]
        + [fixed((1, width))] * 2,
        [fixed((quarter, width)), pl.BlockSpec((quarter, width), lambda q, n: (q, 0))],
        [like((quarter, width), F32), like((rows, width), BF)],
        (*pieces, w_o, tokens, gain, bias),
    )


def add_up(refs):
    total = refs[0][...]
    for ref in refs[1:]:
        total = total + ref[...].astype(F32)
    return total


def mid_back_kernel(at_ref, *refs):
    shares, (w_ref, h_ref, dy_ref, gain_ref, dh_ref, low_ref, sums_ref) = refs[:4], refs[4:11]
    do_refs = refs[11:]
    db = add_up(shares)
    normal, scale = normalize(h_ref[...])
    dh = dy_ref[...].astype(F32) + norm_back(db, gain_ref[...], normal, scale)
    dh_ref[...] = dh
    low = dh.astype(BF)
    low_ref[...] = low
    sums_ref[0:1, :] = jnp.sum(db * normal, axis=0, keepdims=True)
    sums_ref[1:2, :] = jnp.sum(db, axis=0, keepdims=True)
    for r in range(4):
        rows = heads_of(at_ref[1], r, do_refs[r].shape[0])
        do_refs[r][...] = mm_t(w_ref[rows, :], low).astype(BF)


def mid_back(at, shares, w_o, h, dy, gain):
    quarter, width = h.shape
    whole = fixed((quarter, width))
    piece = (w_o.shape[0] // 4, quarter)
    return call(
        mid_back_kernel,
        "mid_back",
        at,
        (1,),
        [whole] * 4 + [fixed(w_o.shape), whole, whole, fixed((1, width))],
        [whole] * 2 + [fixed((2, width))] + [fixed(piece)] * 4,
        [like((quarter, width), F32), like((quarter, width), BF), like((2, width), F32)]
        + [like(piece, BF)] * 4,
        (*shares, w_o, h, dy, gain),
    )


def first_back_kernel(at_ref, *refs):
    shares = refs[:4]
    x_ref, dh_ref, gain_ref, out_ref = refs[4:]
    d_a = add_up(shares)
    normal, scale = normalize(x_ref[...].astype(F32))
    out_ref[...] = (dh_ref[...] + norm_back(d_a, gain_ref[...], normal, scale)).astype(BF)


def first_back(at, shares, tokens, dh, gain):
    quarter, width = dh.shape
    return call(
        first_back_kernel,
        "first_back",
        at,
        (1,),
        [fixed((quarter, width))] * 4
        + [pl.BlockSpec((quarter, width), lambda i, n: (n[1], 0))]
        + [fixed((quarter, width)), fixed((1, width))],
        fixed((quarter, width)),
        like((quarter, width), BF),
        (*shares, tokens, dh, gain),
    )


def in_order(mine, own, right, left, far, right_two, left_two):
    one = jnp.where(mine == 3, far, left)
    two = jnp.where(mine < 2, left_two, right_two)
    three = jnp.where(mine == 0, far, right)
    return own, one, two, three


def one_hot(slots, dest):
    return jnp.where(slots == dest, 1.0, 0.0).astype(BF)


def dispatch_kernel(at_ref, dest_ref, rows_ref, out_ref, spread_s):
    blk, rows = min(256, spread_s.shape[0]), dest_ref.shape[1]

    @pl.when(pl.program_id(0) == 0)
    def _():
        slot = lax.broadcasted_iota(jnp.int32, (blk, rows), 0)
        for start in range(0, spread_s.shape[0], blk):
            spread_s[start : start + blk, :] = one_hot(slot + start, dest_ref[...])

    out_ref[...] = mm(spread_s[...], rows_ref[...]).astype(BF)


def columns(rows, width):
    return pl.BlockSpec((rows, width), lambda i, n: (0, i))


def dispatch(at, dest_row, values, slots):
    rows, width = values.shape
    blk = min(256, width)
    return call(
        dispatch_kernel,
        "dispatch",
        at,
        (width // blk,),
        [fixed((1, rows)), columns(rows, blk)],
        columns(slots, blk),
        like((slots, width), BF),
        (dest_row, values),
        scratch=[pltpu.VMEM((slots, rows), BF)],
    )


def join_kernel(at_ref, *refs):
    pieces, out_ref = refs[:6], refs[6]
    r = pl.program_id(0)
    for place, piece in enumerate(in_order(at_ref[1], *[ref[...] for ref in pieces])):

        @pl.when(r == place)
        def _():
            out_ref[...] = piece


def join(at, pieces):
    each, width = pieces[0].shape
    return call(
        join_kernel,
        "join",
        at,
        (4,),
        [fixed((each, width))] * 6,
        pl.BlockSpec((each, width), lambda r, n: ((n[1] + r) % 4, 0)),
        like((4 * each, width), BF),
        pieces,
    )


def write_shares(mine, total, own_ref, one_ref, two_ref, three_ref, end_ref):
    rows = own_ref.shape[0]
    own_ref[...] = total[:rows]
    one, two, three = [total[r * rows : (r + 1) * rows].astype(BF) for r in (1, 2, 3)]
    one_ref[...] = one
    two_ref[...] = two
    three_ref[...] = three
    end_ref[...] = jnp.where(mine == 0, three, one)


def share_shapes(rows, width):
    return [like((rows, width), F32)] + [like((rows, width), BF)] * 4


def combine_kernel(count, whole, at_ref, *refs):
    dests, backs = refs[:count], refs[count : 2 * count]
    base_ref, refs, pick_s = refs[2 * count], refs[2 * count + 1 : -1], refs[-1]
    rows, slots = base_ref.shape[0], backs[0].shape[0]
    blk = rows // 4

    @pl.when(pl.program_id(0) == 0)
    def _():
        lane = lax.broadcasted_iota(jnp.int32, (blk, slots), 1)
        for k in range(count):
            for start in range(0, rows, blk):
                dest = dests[k][start : start + blk, :]
                pick_s[start : start + blk, k * slots : (k + 1) * slots] = one_hot(lane, dest)

    total = base_ref[...].astype(F32)
    for k in range(count):
        total = total + mm(pick_s[:, k * slots : (k + 1) * slots], backs[k][...])
    mine = at_ref[1]
    if whole:
        h_ref, out_ref = refs
        for r in range(4):
            part = total[r * blk : (r + 1) * blk]
            if r == 0:
                part = part + h_ref[...]
            place = pl.ds(pl.multiple_of(((mine + r) % 4) * blk, blk), blk)
            out_ref[place, :] = part.astype(BF)
    else:
        write_shares(mine, total, *refs)


def combine(at, dests, backs, base, h=None):
    count, (slots, width), rows = len(backs), backs[0].shape, base.shape[0]
    blk = min(256, width)
    whole = h is not None
    quarter = columns(rows // 4, blk)
    return call(
        partial(combine_kernel, count, whole),
        "combine",
        at,
        (width // blk,),
        [fixed((rows, 1))] * count
        + [columns(slots, blk)] * count
        + [columns(rows, blk)]
        + [quarter] * whole,
        columns(rows, blk) if whole else [quarter] * 5,
        like(base.shape, BF) if whole else share_shapes(rows // 4, width),
        (*dests, *backs, base) + ((h,) if whole else ()),
        scratch=[pltpu.VMEM((rows, count * slots), BF)],
    )


def mm_t(a, b):
    return lax.dot_general(a, b, (((1,), (1,)), ((), ())), preferred_element_type=F32)


def gelu_both(u):
    c = 0.7978845608028654
    square = u * u
    t = jnp.tanh(u * (c + (c * 0.044715) * square))
    half = 0.5 + 0.5 * t
    slope = half + (0.5 * u) * (1.0 - t * t) * (c + (3.0 * c * 0.044715) * square)
    return u * half, slope


def high_low(value):
    high = value.astype(BF)
    return high, (value - high.astype(F32)).astype(BF)


def two_coefs(logits, lane, experts):
    inside = (lane >= experts) & (lane < experts + 2)
    top = jnp.max(jnp.where(inside, logits, HIDE), axis=1, keepdims=True)
    e = jnp.where(inside, jnp.exp(logits - top), 0.0)
    e = e / jnp.sum(e, axis=1, keepdims=True)
    first = jnp.sum(jnp.where(lane == experts, e, 0.0), axis=1, keepdims=True)
    second = jnp.sum(jnp.where(lane == experts + 1, e, 0.0), axis=1, keepdims=True)
    return first, second


def small_back(d_small, rows, w_small_ref, small_ref, i):
    high, low = high_low(d_small)
    w_small = w_small_ref[...]
    high_t, low_t = high_low(d_small.T)

    @pl.when(i == 0)
    def _():
        small_ref[...] = jnp.zeros(small_ref.shape, F32)

    small_ref[...] += mm(high_t, rows) + mm(low_t, rows)
    return mm_t(high, w_small) + mm_t(low, w_small)


def expert_kernel(experts, half, at_ref, rows_ref, dy_ref, up_ref, down_ref, w_small_ref, *outs):
    if half:
        outs = outs[5:]
    rows_out_ref, hid_ref, dy_out_ref, deu_ref, y_ref, d_rows_ref, small_ref = outs
    rows = rows_ref[...]
    rows_out_ref[...] = rows
    up = mm(rows, up_ref[...])
    logits = mm(rows, w_small_ref[...])
    lane = lax.broadcasted_iota(jnp.int32, logits.shape, 1)
    routed = lane < experts
    top = jnp.max(jnp.where(routed, logits, HIDE), axis=1, keepdims=True)
    probs = jnp.where(routed, jnp.exp(logits - top), 0.0)
    probs = probs / jnp.sum(probs, axis=1, keepdims=True)
    own = jnp.where(lane == at_ref[2], 1.0, 0.0)
    gate = jnp.sum(probs * own, axis=1, keepdims=True)
    first, second = two_coefs(logits, lane, experts)
    weight = second * gate
    dy = dy_ref[...].reshape(rows.shape).astype(F32)
    d_y = (weight * dy).astype(BF)
    dy_out_ref[...] = d_y
    d_hidden = mm_t(d_y, down_ref[...])
    hidden, slope = gelu_both(up)
    hidden = hidden.astype(BF)
    hid_ref[...] = hidden
    d_up = (d_hidden * slope).astype(BF)
    deu_ref[...] = d_up
    y = mm(hidden, down_ref[...])
    y_ref[...] = (weight * y).astype(BF).reshape(y_ref.shape)
    along = gate * jnp.sum(dy * y, axis=1, keepdims=True)
    mixed = first * second * along
    d_small = (second * along) * (own - probs)
    d_small = jnp.where(routed, d_small, 0.0)
    d_small = d_small + jnp.where(lane == experts + 1, mixed, 0.0)
    d_small = d_small - jnp.where(lane == experts, mixed, 0.0)
    d_rows = mm_t(d_up, up_ref[...]) + small_back(d_small, rows, w_small_ref, small_ref, pl.program_id(0))
    d_rows_ref[...] = d_rows.astype(BF)


def expert_rows(at, rows, dy, w_up, w_down, w_small, experts, half, before):
    count, width = rows.shape
    hid, lanes = w_up.shape[1], w_small.shape[1]
    blk = min(512, count)
    capacity = count // dy.shape[0]
    steps = count // blk
    moving = pl.BlockSpec((blk, width), lambda i, n: (i, 0))
    slots = pl.BlockSpec((blk // capacity, capacity, width), lambda i, n: (i, half, 0))
    kept = [pl.BlockSpec((blk, size), lambda i, n: (i + half * steps, 0)) for size in (width, hid, width, hid)]
    return call(
        partial(expert_kernel, experts, half),
        "expert_rows",
        at,
        (steps,),
        [
            moving,
            slots,
            fixed((width, hid)),
            fixed((hid, width)),
            fixed((width, lanes)),
        ]
        + [pl.BlockSpec(memory_space=pl.ANY)] * (5 * half),
        kept + [slots, moving, fixed((lanes, width))],
        [like((2 * count, size), BF) for size in (width, hid, width, hid)]
        + [like(dy.shape, BF), like((count, width), BF)]
        + [like((lanes, width), F32)],
        (rows, dy, w_up, w_down, w_small, *before),
        alias={6 + k: k for k in range(5)} if half else None,
        vmem=56,
    )


def dense_kernel(experts, at_ref, rows_ref, dy_ref, in_ref, out_ref, w_small_ref, *outs):
    hid_ref, grad_ref, d_up_ref, mix_ref, db_ref, small_ref = outs
    rows = rows_ref[...]
    up = mm(rows, in_ref[...])
    logits = mm(rows, w_small_ref[...])
    lane = lax.broadcasted_iota(jnp.int32, logits.shape, 1)
    first, second = two_coefs(logits, lane, experts)
    dy = dy_ref[...].astype(F32)
    grad = (first * dy).astype(BF)
    grad_ref[...] = grad
    d_hidden = mm_t(grad, out_ref[...])
    hidden, slope = gelu_both(up)
    hidden = hidden.astype(BF)
    hid_ref[...] = hidden
    d_up = (d_hidden * slope).astype(BF)
    d_up_ref[...] = d_up
    dense = mm(hidden, out_ref[...])
    mix_ref[...] = first * dense
    mixed = first * second * jnp.sum(dy * dense, axis=1, keepdims=True)
    d_small = jnp.where(lane == experts, mixed, 0.0) - jnp.where(lane == experts + 1, mixed, 0.0)
    db_ref[...] = mm_t(d_up, in_ref[...]) + small_back(d_small, rows, w_small_ref, small_ref, pl.program_id(0))


def dense_rows(at, rows, dy, w_in, w_out, w_small, experts):
    (count, width), hid, lanes = rows.shape, w_in.shape[1], w_small.shape[1]
    blk = min(512, count)
    row_out = pl.BlockSpec((blk, width), lambda i, n: (i, 0))
    hid_out = pl.BlockSpec((blk, hid), lambda i, n: (i, 0))
    return call(
        partial(dense_kernel, experts),
        "dense_rows",
        at,
        (count // blk,),
        [row_out, row_out, fixed((width, hid)), fixed((hid, width)), fixed((width, lanes))],
        [hid_out, row_out, hid_out, row_out, row_out, fixed((lanes, width))],
        [
            like((count, hid), BF),
            like((count, width), BF),
            like((count, hid), BF),
            like((count, width), F32),
            like((count, width), F32),
            like((lanes, width), F32),
        ],
        (rows, dy, w_in, w_out, w_small),
        vmem=56,
    )


def turned(value):
    return value.astype(F32).T.astype(BF)


def dense_grads_kernel(at_ref, b_ref, d_up_ref, grad_ref, hid_ref, keep_ref, give_ref):
    width = d_up_ref.shape[1]
    first = mm(turned(b_ref[...]), d_up_ref[...]).astype(BF)
    second = mm(turned(grad_ref[...]), hid_ref[...]).astype(BF)
    half = pl.num_programs(0) // 2
    for side, ref in ((0, keep_ref), (1, give_ref)):

        @pl.when(pl.program_id(0) // half == side)
        def _():
            ref[0, :, :width] = first
            ref[0, :, width:] = second


def dense_grads(at, b, d_up, grad, hidden, parts):
    (rows, width), hid = b.shape, hidden.shape[1]
    own, half, bits = width // parts, parts // 2, parts.bit_length() - 1

    def part(q, n):
        turned_q = sum([((q // 2**k) % 2) * 2 ** (bits - 1 - k) for k in range(bits)])
        return turned_q ^ n[2]

    column = pl.BlockSpec((rows, own), lambda q, n: (0, part(q, n)))
    shape = (1, own, 2 * hid)
    return call(
        dense_grads_kernel,
        "dense_grads",
        at,
        (parts,),
        [column, fixed((rows, hid)), column, fixed((rows, hid))],
        [
            pl.BlockSpec(shape, lambda q, n: (jnp.minimum(q, half - 1), 0, 0)),
            pl.BlockSpec(shape, lambda q, n: (jnp.maximum(q - half, 0), 0, 0)),
        ],
        [like((half, own, 2 * hid), BF)] * 2,
        (b, d_up, grad, hidden),
    )


def attention_grads_kernel(experts, at_ref, *refs):
    grads, o_refs, refs = refs[:GROUP], refs[GROUP : GROUP + 6], refs[GROUP + 6 :]
    a_ref, dh_ref, w_ref, gain_ref, bias_ref, sums_ref = refs[:6]
    small_refs, (out_ref, all_s) = refs[6:-2], refs[-2:]
    heads, features = GROUP * HD, grads[1].shape[0]
    products, plain = 0.0, 0.0
    for k in range(GROUP):
        head = at_ref[0] ^ k
        rows = pl.ds(pl.multiple_of(head * features, features), features)
        grad = grads[k][...]
        weight = w_ref[head].astype(F32)
        total = mm(grad, a_ref[...])
        all_s[rows, :] = total
        each = jnp.sum(grad.astype(F32), axis=1, keepdims=True)
        products = products + jnp.sum(total * weight, axis=0, keepdims=True)
        plain = plain + jnp.sum(each * weight, axis=0, keepdims=True)
    first = GROUP * features
    for r, piece in enumerate(in_order(at_ref[1], *[ref[...] for ref in o_refs])):
        rows = pl.ds(pl.multiple_of(first + ((at_ref[1] + r) % 4) * heads, heads), heads)
        all_s[rows, :] = mm(piece, dh_ref[...])
    first += 4 * heads
    small = add_up(small_refs)
    row = lax.broadcasted_iota(jnp.int32, small.shape, 0)
    d_gain = (products - bias_ref[...] * plain) / gain_ref[...]
    for k, sums in enumerate((sums_ref[0:1, :], sums_ref[1:2, :], d_gain, plain)):
        small = jnp.where(row == experts + 2 + k, sums, small)
    all_s[first:, :] = small
    out_ref[...] = all_s[...].T.astype(BF)


def attention_grads(at, grads, o, a, dh, w_heads, gain, bias, sums, small, experts):
    rows, width = a.shape
    features, lanes = grads[0].shape[0], small[0].shape[0]
    piece = pl.BlockSpec((o[0].shape[0], dh.shape[0]), lambda i, n: (0, n[1]))
    height = GROUP * features + 4 * o[0].shape[0] + lanes
    blk = min(256, width)
    return call(
        partial(attention_grads_kernel, experts),
        "attention_grads",
        at,
        (width // blk,),
        [fixed((features, rows))] * GROUP
        + [piece] * 6
        + [columns(rows, blk), columns(dh.shape[0], blk)]
        + [pl.BlockSpec((GROUP, features, blk), lambda i, n: (0, 0, i))]
        + [columns(1, blk)] * 2
        + [columns(2, blk)]
        + [columns(lanes, blk)] * len(small),
        pl.BlockSpec((blk, height), lambda i, n: (i, 0)),
        like((width, height), BF),
        (*grads, *o, a, dh, w_heads, gain, bias, sums, *small),
        scratch=[pltpu.VMEM((height, blk), F32)],
    )


def project_kernel(at_ref, *refs):
    grads, w_ref, outs, turned_s = refs[:GROUP], refs[GROUP], refs[GROUP + 1 : -1], refs[-1]
    rows = turned_s.shape[1]
    blk = rows // 4

    @pl.when(pl.program_id(0) == 0)
    def _():
        for s in range(GROUP):
            for r in range(4):
                lanes = pl.ds(pl.multiple_of(((at_ref[1] + r) % 4) * blk, blk), blk)
                turned_s[s, r * blk : (r + 1) * blk, :] = turned(grads[s][:, lanes])

    total = 0.0
    for s in range(GROUP):
        total = total + mm(turned_s[s], w_ref[at_ref[0] ^ s])
    write_shares(at_ref[1], total, *outs)


def project_back(at, grads, w_heads):
    features, rows = grads[0].shape
    width = w_heads.shape[2]
    blk = min(256, width)
    return call(
        project_kernel,
        "project_back",
        at,
        (width // blk,),
        [fixed((features, rows))] * GROUP
        + [pl.BlockSpec((GROUP, features, blk), lambda i, n: (0, 0, i))],
        [columns(rows // 4, blk)] * 5,
        share_shapes(rows // 4, width),
        (*grads, w_heads),
        scratch=[pltpu.VMEM((GROUP, rows, features), BF)],
    )


def hop(value, *pairs):
    return lax.ppermute(value, "mp", pairs)


def rotate(value, steps):
    return hop(value, *[(s, (s + steps) % 4) for s in range(4)])


def gather_near(own):
    right = hop(own, (0, 1), (1, 2), (2, 3))
    left = hop(own, (1, 0), (2, 1), (3, 2))
    return own, right, left, hop(own, (0, 3), (3, 0))


def gather_far(near):
    _, right, left, _ = near
    return *near, hop(right, (1, 2), (2, 3)), hop(left, (1, 0), (2, 1))


def gather_pieces(own):
    return gather_far(gather_near(own))


def scatter_far(shares):
    _, _, two, _, end = shares
    return hop(two, (2, 1), (3, 2)), hop(two, (0, 1), (1, 2)), hop(end, (0, 3), (3, 0))


def scatter_near(shares, came):
    own, one, _, three, _ = shares
    from_right, from_left, from_end = came
    three = (three.astype(F32) + from_right.astype(F32)).astype(BF)
    one = (one.astype(F32) + from_left.astype(F32)).astype(BF)
    return own, hop(three, (1, 0), (2, 1), (3, 2)), hop(one, (0, 1), (1, 2), (2, 3)), from_end


def group_swap(value, s):
    count = lax.axis_size("dp")
    return lax.ppermute(value, "dp", [(t, t ^ s) for t in range(count)])


def expert_swap(value, experts):
    wide = value.reshape(experts, value.shape[0] // experts, value.shape[1])
    return lax.all_to_all(wide, "dp", 0, 0, tiled=True).reshape(value.shape)


def roll_rows(value, start):
    twice = jnp.concatenate([value, value], axis=0)
    return lax.dynamic_slice_in_dim(twice, start, value.shape[0], 0)


def add_halves(keep, came):
    return (keep.astype(F32) + came.astype(F32)).astype(BF)


def body(
    tokens,
    cotangent,
    ln_gains,
    ln_biases,
    w_qkv,
    w_o,
    w_in,
    w_out,
    w_router,
    w_coef,
    w_up,
    w_down,
    routes,
    long_group,
):
    rows, width = tokens.shape
    dps = lax.axis_size("dp")
    mine, position = lax.axis_index("mp"), lax.axis_index("dp")
    quarter = rows // 4
    start = mine * quarter
    heads_loc = w_qkv.shape[2] // HD
    hid = w_in.shape[1]
    experts = w_router.shape[1]
    capacity = max(2, 2 * rows // experts)
    half = capacity // 2
    barrier = lax.optimization_barrier
    first_len = lax.dynamic_index_in_dim(long_group, position // GROUP, 0, keepdims=False)
    at = jnp.stack([position % GROUP, mine, position, first_len]).astype(jnp.int32)
    gains = [ln_gains[0:1], ln_gains[1:2]]
    biases = [ln_biases[0:1], ln_biases[1:2]]
    w_o_all = lax.all_gather(w_o, "mp", axis=0, tiled=True)

    w_heads = w_qkv.reshape(width, 3, heads_loc, HD).transpose(2, 1, 3, 0)
    w_heads = w_heads.reshape(heads_loc, 3 * HD, width)
    a_r, *qkv = project(at, tokens, gains[0], biases[0], w_heads)
    qkv = [qkv[0]] + [group_swap(qkv[s], s) for s in (1, 2, 3)]

    route = roll_rows(routes, start)[:, 0]
    picked = (route[:, None] == jnp.arange(experts, dtype=jnp.int32)[None, :]).astype(jnp.int32)
    slot = jnp.sum((jnp.cumsum(picked, axis=0) - picked) * picked, axis=1)
    dy_b = roll_rows(cotangent, start)
    full = route * capacity + slot
    send_dy = dispatch(at, full[None, :], dy_b, experts * capacity)
    *qkv, send_dy = barrier((*qkv, send_dy))
    in_half = [slot < half, slot >= half]
    dests = [
        jnp.where(in_half[k], route * half + slot - k * half, -1).astype(jnp.int32) for k in (0, 1)
    ]

    *o_t, lse = attend(at, qkv)
    *o_t, w_o_all = barrier((*o_t, w_o_all))
    o_heads = [o_t[0]] + [group_swap(o_t[s], s) for s in (1, 2, 3)]
    lanes = -(-(experts + 2) // 128) * 128
    w_small = jnp.concatenate(
        [w_router, w_coef, jnp.zeros((width, lanes - experts - 2), BF)], axis=1
    )
    *o_heads, send_dy, w_small = barrier((*o_heads, send_dy, w_small))
    got_dy = expert_swap(send_dy, experts).reshape(experts, capacity, width)
    o_pieces = gather_pieces(stack(at, o_heads))
    h, b_r = mid(at, o_pieces, w_o_all, tokens, gains[1], biases[1])

    send_0 = dispatch(at, dests[0][None, :], b_r, experts * half)
    send_0, got_dy = barrier((send_0, got_dy))
    got_0 = expert_swap(send_0, experts)
    send_1 = dispatch(at, dests[1][None, :], b_r, experts * half)
    b_r, send_1 = barrier((b_r, send_1))
    hidden, dense_grad, d_up, mix_base, db_base, small_t = dense_rows(
        at, b_r, dy_b, w_in, w_out, w_small, experts
    )
    send_1, got_0, db_base = barrier((send_1, got_0, db_base))
    got_1 = expert_swap(send_1, experts)

    *kept, d_rows_0, small_0 = expert_rows(
        at, got_0, got_dy, w_up[0], w_down[0], w_small, experts, 0, ()
    )
    back_0 = expert_swap(d_rows_0, experts)
    *kept, d_rows_1, small_1 = expert_rows(
        at, got_1, got_dy, w_up[0], w_down[0], w_small, experts, 1, kept
    )
    got, hidden_e, d_y, d_eu, back_y = kept
    back_1 = expert_swap(d_rows_1, experts)
    d_rows_1, b_r = barrier((d_rows_1, b_r))
    halving = width == dps * 128
    if halving:
        grads = dense_grads(at, b_r, d_up, dense_grad, hidden, dps)
    else:
        grads = [ein("td,tf->df", b_r, d_up).astype(BF), ein("td,tf->df", dense_grad, hidden).astype(BF)]
    back_0, back_1, back_y, *grads = barrier((back_0, back_1, back_y, *grads))

    dest_cols = [dest[:, None] for dest in dests]
    tok_y = expert_swap(back_y.reshape(experts * capacity, width), experts)
    shares = combine(at, dest_cols, [back_0, back_1], db_base)
    far = scatter_far(shares)
    grad_down = ein("rf,rd->fd", hidden_e, d_y)
    grad_up = ein("rd,rf->df", got, d_eu)
    *far, g_0, g_1, grad_down, grad_up = barrier((*far, *grads, grad_down, grad_up))
    grads = [g_0, g_1]
    shares = scatter_near(shares, far)

    mix = combine(at, [full[:, None]], [tok_y], mix_base, h)
    *shares, mix = barrier((*shares, mix))
    output = lax.psum(mix, "mp")
    dh, dh_r, sums_2, *do_q = mid_back(at, shares, w_o_all, h, dy_b, gains[1])
    do_q = [do_q[0]] + [rotate(do_q[r], -r) for r in (1, 2, 3)]
    do_heads = unsplit(at, do_q)
    do_t = [do_heads[0]] + [group_swap(do_heads[s], s) for s in (1, 2, 3)]
    if halving:
        came_1 = group_swap(grads[1], 1)
        half = dps // 4
        give = add_halves(grads[0][half:], came_1[half:])
        *do_t, give = barrier((*do_t, give))
        came_2 = group_swap(give, 2)
    d_qkv = attend_back(at, qkv, do_t, o_t, lse)
    if halving:
        keep = add_halves(grads[0][:half], came_1[:half])
        *d_qkv, came_2, keep = barrier((*d_qkv, came_2, keep))
        grads = add_halves(keep, came_2)
        bit = 4
        while bit < dps:
            half = grads.shape[0] // 2
            grads = add_halves(grads[:half], group_swap(grads[half:], bit))
            bit *= 2
        grads = [grads[0][:, :hid], grads[0][:, hid:]]
    else:
        grads = [lax.psum_scatter(grad, "dp", scatter_dimension=0, tiled=True) for grad in grads]

    d_qkv = [d_qkv[0]] + [group_swap(d_qkv[s], s) for s in (1, 2, 3)]
    *d_qkv, output = barrier((*d_qkv, output))
    shares = project_back(at, d_qkv, w_heads)
    far = scatter_far(shares)
    grads_a = attention_grads(
        at, d_qkv, o_pieces, a_r, dh_r, w_heads, gains[0], biases[0], sums_2, (small_0, small_1, small_t), experts
    )
    grads_a, *far = barrier((grads_a, *far))
    grads_a = lax.psum_scatter(grads_a, "dp", scatter_dimension=0, tiled=True).T
    shares = scatter_near(shares, far)
    grad_q = first_back(at, shares, tokens, dh, gains[0])
    grad_tokens = join(at, gather_pieces(grad_q))

    own, heads = width // dps, heads_loc * HD
    grad_qkv = grads_a[: 3 * heads].astype(F32).reshape(heads_loc, 3, HD, own).transpose(3, 1, 0, 2)
    grad_qkv = grad_qkv.reshape(own, 3, heads)
    grad_in = grads[0].astype(F32)
    grad_out = grads[1].astype(F32).T
    rest = grads_a[3 * heads : 7 * heads].reshape(4, heads, own)
    small = jnp.broadcast_to(grads_a[7 * heads :], (4, lanes, own))
    rest = lax.all_to_all(jnp.concatenate([rest, small], axis=1), "mp", 0, 0, tiled=True)
    rest = jnp.sum(rest.astype(F32), axis=0)
    grad_o, small = rest[:heads], rest[heads:]
    small_out = small[: experts + 2].T
    return (
        output,
        grad_tokens,
        jnp.stack([small[experts + 4], small[experts + 2]]),
        jnp.stack([small[experts + 5], small[experts + 3]]),
        grad_qkv,
        grad_o,
        grad_in,
        grad_out,
        small_out[:, :experts],
        small_out[:, experts:],
        grad_up[None],
        grad_down[None],
    )


def solution(mesh):
    in_specs = (
        P("dp", None),
        P("dp", None),
        P(),
        P(),
        P(None, None, "mp"),
        P("mp", None),
        P(None, "mp"),
        P("mp", None),
        P(),
        P(),
        P("dp", None, "mp"),
        P("dp", "mp", None),
        P("dp", None),
        P(),
    )
    out_specs = (
        P("dp", None),
        P("dp", None),
        P(None, "dp"),
        P(None, "dp"),
        P("dp", None, "mp"),
        P("mp", "dp"),
        P("dp", "mp"),
        P("mp", "dp"),
        P("dp", None),
        P("dp", None),
        P("dp", None, "mp"),
        P("dp", "mp", None),
    )
    return jax.shard_map(body, mesh=mesh, in_specs=in_specs, out_specs=out_specs, check_vma=False)
```

```python
from functools import partial

import jax
import jax.numpy as jnp
from jax import lax
from jax.experimental import pallas as pl
from jax.experimental.pallas import tpu as pltpu
from jax.sharding import PartitionSpec as P

HD = 64
GROUP = 4
EPS = 1e-05
LOG2E = 1.4426950408889634
SCALE2 = 0.125 * LOG2E
HIDE = -1e30
BF = jnp.bfloat16
F32 = jnp.float32
LIGHT = pl.CostEstimate(flops=1 << 20, bytes_accessed=1 << 20, transcendentals=0)


def mm(a, b):
    return jnp.dot(a, b, preferred_element_type=F32)


def ein(spec, a, b):
    return jnp.einsum(spec, a, b, preferred_element_type=F32)


def call(kernel, name, prefetch, grid, in_specs, out_specs, out_shape, args, scratch=(), alias=None, vmem=48):
    return pl.pallas_call(
        kernel,
        grid_spec=pltpu.PrefetchScalarGridSpec(
            num_scalar_prefetch=1,
            grid=grid,
            in_specs=in_specs,
            out_specs=out_specs,
            scratch_shapes=list(scratch),
        ),
        out_shape=out_shape,
        input_output_aliases=alias or {},
        compiler_params=pltpu.CompilerParams(vmem_limit_bytes=vmem * 2**20),
        cost_estimate=LIGHT,
        name=name,
    )(prefetch, *args)


def fixed(shape):
    zeros = (0,) * len(shape)
    return pl.BlockSpec(shape, lambda *_: zeros)


def like(shape, dtype):
    return jax.ShapeDtypeStruct(shape, dtype)


def normalize(v):
    mean = jnp.mean(v, axis=-1, keepdims=True)
    centred = v - mean
    scale = lax.rsqrt(jnp.mean(centred * centred, axis=-1, keepdims=True) + EPS)
    return centred * scale, scale


def norm_back(grad, gain, normal, scale):
    g = grad * gain
    along = jnp.mean(g * normal, axis=-1, keepdims=True)
    return scale * (g - jnp.mean(g, axis=-1, keepdims=True) - normal * along)


def qkv_kernel(at_ref, x_ref, gain_ref, bias_ref, w_ref, a_ref, *outs):
    normal, _ = normalize(x_ref[...].astype(F32))
    a = (normal * gain_ref[...] + bias_ref[...]).astype(BF)
    a_ref[...] = a
    for s in range(GROUP):
        outs[s][...] = mm_t(w_ref[at_ref[0] ^ s], a).astype(BF)


def project(at, tokens, gain, bias, w_heads):
    rows, width = tokens.shape
    features = w_heads.shape[1]
    blk = min(256, rows)
    moving = pl.BlockSpec((blk, width), lambda i, n: (i, 0))
    return call(
        qkv_kernel,
        "project",
        at,
        (rows // blk,),
        [moving, fixed((1, width)), fixed((1, width)), fixed(w_heads.shape)],
        [moving] + [pl.BlockSpec((features, blk), lambda i, n: (0, i))] * GROUP,
        [like((rows, width), BF)] + [like((features, rows), BF)] * GROUP,
        (tokens, gain, bias, w_heads),
    )


def fill_keys(k_s, place, keys, first_len, blk):
    rows = place * blk + lax.broadcasted_iota(jnp.int32, (blk, 128), 0)
    lane = lax.broadcasted_iota(jnp.int32, (blk, 128), 1)
    wide = jnp.concatenate([keys.astype(F32).T, jnp.zeros((blk, 128 - HD), F32)], axis=1)
    wide = jnp.where((lane == HD) & (rows < first_len), HIDE, wide)
    k_s[pl.ds(place * blk, blk), :] = wide.astype(BF)


def wide_query(query, place, first_len, blk):
    cols = place * blk + lax.broadcasted_iota(jnp.int32, (128 - HD, blk), 1)
    sub = lax.broadcasted_iota(jnp.int32, (128 - HD, blk), 0)
    extra = jnp.where((sub == 0) & (cols >= first_len), 1.0, 0.0)
    return jnp.concatenate([query, extra.astype(BF)], axis=0)


def causal(blk):
    keys = lax.broadcasted_iota(jnp.int32, (blk, blk), 0)
    queries = lax.broadcasted_iota(jnp.int32, (blk, blk), 1)
    return keys <= queries


def attend_kernel(blk, per, at_ref, *refs):
    qkv_refs, o_refs = refs[:GROUP], refs[GROUP : 2 * GROUP]
    lse_ref, k_s, v_s, qkv_s = refs[2 * GROUP :]
    i = pl.program_id(0)
    place, first_len = at_ref[0], at_ref[3]

    @pl.when(i == 0)
    def _():
        for s in range(GROUP):
            qkv_s[place ^ s] = qkv_refs[s][...]

    def part(which, j):
        return qkv_s[j // per, HD * which : HD * (which + 1), pl.ds((j % per) * blk, blk)]

    fill_keys(k_s, i, part(1, i), first_len, blk)
    query = wide_query(part(0, i), i, first_len, blk)
    ones = jnp.where(lax.broadcasted_iota(jnp.int32, (16, blk), 0) == 0, 1.0, 0.0)
    here = pl.ds(pl.multiple_of(i * blk, blk), blk)
    v_s[:, here] = jnp.concatenate([part(2, i), ones.astype(BF)], axis=0)

    def values(j):
        return v_s[:, pl.ds(pl.multiple_of(j * blk, blk), blk)]

    def scores(j):
        return mm(k_s[pl.ds(pl.multiple_of(j * blk, blk), blk), :], query)

    s = jnp.where(causal(blk), scores(i), HIDE)
    top = jnp.max(s, axis=0, keepdims=True)
    acc = mm(values(i), jnp.exp2(((s - top) * SCALE2).astype(BF)))

    def steps(blocks, carry):
        top, acc = carry
        s = [scores(j) for j in blocks]
        new = top
        for one in s:
            new = jnp.maximum(new, jnp.max(one, axis=0, keepdims=True))
        acc = acc * jnp.exp2((top - new) * SCALE2)
        for j, one in zip(blocks, s):
            acc = acc + mm(values(j), jnp.exp2(((one - new) * SCALE2).astype(BF)))
        return new, acc

    low = jnp.where(i * blk >= first_len, first_len // blk, 0)
    pairs = (i - low) // 2
    carry = lax.fori_loop(
        0, pairs, lambda t, c: steps([low + 2 * t, low + 2 * t + 1], c), (top, acc)
    )
    top, acc = lax.fori_loop(low + 2 * pairs, i, lambda j, c: steps([j], c), carry)
    total = acc[HD : HD + 1]
    out = (acc[:HD] / total).astype(BF)
    for s in range(GROUP):

        @pl.when((i // per) ^ place == s)
        def _():
            o_refs[s][:, pl.ds((i % per) * blk, blk)] = out

    lse_ref[0] = top * SCALE2 + jnp.log2(total)


def attend(at, qkv):
    features, rows = qkv[0].shape
    blk = min(512, rows)
    per = rows // blk
    count = GROUP * per
    return call(
        partial(attend_kernel, blk, per),
        "attend",
        at,
        (count,),
        [fixed((features, rows))] * GROUP,
        [fixed((HD, rows))] * GROUP + [pl.BlockSpec((1, 1, blk), lambda i, n: (i, 0, 0))],
        [like((HD, rows), BF)] * GROUP + [like((count, 1, blk), F32)],
        qkv,
        scratch=[
            pltpu.VMEM((GROUP * rows, 128), BF),
            pltpu.VMEM((HD + 16, GROUP * rows), BF),
            pltpu.VMEM((GROUP, features, rows), BF),
        ],
    )


def back_kernel(blk, per, count, at_ref, *refs):
    qkv_refs, do_refs, o_refs = refs[:GROUP], refs[GROUP : 2 * GROUP], refs[2 * GROUP : 3 * GROUP]
    lse_ref, refs = refs[3 * GROUP], refs[3 * GROUP + 1 :]
    out_refs, refs = refs[:GROUP], refs[GROUP:]
    dq_ref, out_ref, k_s, kt_s, v_s, wide_s, dot_s, both_s, delta_s, acc_s = refs
    j = pl.program_id(0)
    place, first_len = at_ref[0], at_ref[3]

    @pl.when(j == 0)
    def _():
        dq_ref[...] = jnp.zeros(dq_ref.shape, F32)
        zero = jnp.zeros((blk, HD), F32)
        for s in range(GROUP):
            for sub in range(per):
                i = (place ^ s) * per + sub
                at = pl.ds(pl.multiple_of(i * blk, blk), blk)
                cut = slice(sub * blk, (sub + 1) * blk)
                query = qkv_refs[s][0:HD, cut]
                keys = qkv_refs[s][HD : 2 * HD, cut]
                grad = do_refs[s][:, cut]
                fill_keys(k_s, i, keys, first_len, blk)
                kt_s[:, at] = keys
                dot_s[:, at] = grad
                wide_s[:, at] = wide_query(query, i, first_len, blk)
                grad = grad.astype(F32)
                values = qkv_refs[s][2 * HD :, cut].astype(F32)
                v_s[at, :] = jnp.concatenate([values.T, zero], axis=1).astype(BF)
                both_s[0, at, :] = jnp.concatenate([grad.T, zero], axis=1).astype(BF)
                both_s[1, at, :] = jnp.concatenate([zero, query.astype(F32).T], axis=1).astype(BF)
                held = o_refs[s][:, cut].astype(F32)
                delta_s[i] = jnp.sum(held * grad, axis=0, keepdims=True)

    here = pl.ds(pl.multiple_of(j * blk, blk), blk)
    keys_t = kt_s[:, here]
    values = v_s[here, 0:HD]

    def pair(i, diagonal):
        at = pl.ds(pl.multiple_of(i * blk, blk), blk)
        s = mm(k_s[here, :], wide_s[:, at])
        p = jnp.exp2(s * SCALE2 - lse_ref[i])
        if diagonal:
            p = jnp.where(causal(blk), p, 0.0)
        dp = mm(values, dot_s[:, at])
        ds = (p * (dp - delta_s[i])).astype(BF)
        return mm(p.astype(BF), both_s[0, at, :]) + mm(ds, both_s[1, at, :]), mm(keys_t, ds)

    acc_s[...], dq = pair(j, True)
    dq_ref[:, here] += dq

    def step_two(t, carry):
        i = j + 1 + 2 * t
        (kv_0, dq_0), (kv_1, dq_1) = pair(i, False), pair(i + 1, False)
        acc_s[...] += kv_0 + kv_1
        at = pl.ds(pl.multiple_of(i * blk, blk), 2 * blk)
        dq_ref[:, at] += jnp.concatenate([dq_0, dq_1], axis=1)
        return carry

    def step(i, carry):
        kv, dq = pair(i, False)
        acc_s[...] += kv
        dq_ref[:, pl.ds(pl.multiple_of(i * blk, blk), blk)] += dq
        return carry

    high = jnp.where((j + 1) * blk <= first_len, (first_len + blk - 1) // blk, count)
    pairs = (high - j - 1) // 2
    lax.fori_loop(0, pairs, step_two, 0)
    lax.fori_loop(j + 1 + 2 * pairs, high, step, 0)
    both = acc_s[...].T
    out_ref[0:HD, :] = (dq_ref[:, here] * 0.125).astype(BF)
    out_ref[HD : 2 * HD, :] = (both[HD:, :] * 0.125).astype(BF)
    out_ref[2 * HD :, :] = both[:HD, :].astype(BF)
    for s in range(GROUP):

        @pl.when((j // per) ^ place == s)
        def _():
            out_refs[s][:, pl.ds(pl.multiple_of((j % per) * blk, blk), blk)] = out_ref[...]


def attend_back(at, qkv, do, o, lse):
    features, rows = qkv[0].shape
    blk = min(512, rows)
    per = rows // blk
    count = GROUP * per
    return call(
        partial(back_kernel, blk, per, count),
        "attend_back",
        at,
        (count,),
        [fixed((features, rows))] * GROUP
        + [fixed((HD, rows))] * (2 * GROUP)
        + [fixed((count, 1, blk))],
        [fixed((features, rows))] * GROUP,
        [like((features, rows), BF)] * GROUP,
        (*qkv, *do, *o, lse),
        scratch=[
            pltpu.VMEM((HD, GROUP * rows), F32),
            pltpu.VMEM((features, blk), BF),
            pltpu.VMEM((GROUP * rows, 128), BF),
            pltpu.VMEM((HD, GROUP * rows), BF),
            pltpu.VMEM((GROUP * rows, 128), BF),
            pltpu.VMEM((128, GROUP * rows), BF),
            pltpu.VMEM((HD, GROUP * rows), BF),
            pltpu.VMEM((2, GROUP * rows, 128), BF),
            pltpu.VMEM((count, 1, blk), F32),
            pltpu.VMEM((blk, 128), F32),
        ],
        vmem=36,
    )


def stack_kernel(at_ref, *refs):
    ins, out_ref = refs[:GROUP], refs[GROUP]
    for s in range(GROUP):
        head = pl.ds(pl.multiple_of((at_ref[0] ^ s) * HD, HD), HD)
        out_ref[head, :] = ins[s][...]


def stack(at, heads):
    rows = heads[0].shape[1]
    return call(
        stack_kernel,
        "stack",
        at,
        (1,),
        [fixed((HD, rows))] * GROUP,
        fixed((GROUP * HD, rows)),
        like((GROUP * HD, rows), BF),
        heads,
    )


def unsplit_kernel(at_ref, *refs):
    ins, outs = refs[:4], refs[4:]
    cols = ins[0].shape[1]
    for r in range(4):
        lanes = pl.ds(pl.multiple_of(((at_ref[1] + r) % 4) * cols, cols), cols)
        for s in range(GROUP):
            head = pl.ds(pl.multiple_of((at_ref[0] ^ s) * HD, HD), HD)
            outs[s][:, lanes] = ins[r][head, :]


def unsplit(at, pieces):
    shape = (HD, 4 * pieces[0].shape[1])
    return call(
        unsplit_kernel,
        "unsplit",
        at,
        (1,),
        [fixed(pieces[0].shape)] * 4,
        [fixed(shape)] * GROUP,
        [like(shape, BF)] * GROUP,
        pieces,
    )


def heads_of(mine, r, features):
    return pl.ds(pl.multiple_of(((mine + 4 - r) % 4) * features, features), features)


def mid_kernel(at_ref, *refs):
    pieces, (w_ref, x_ref, gain_ref, bias_ref, h_ref, b_ref) = refs[:6], refs[6:]
    h = x_ref[...].astype(F32)
    for r, piece in enumerate(in_order(at_ref[1], *[ref[...] for ref in pieces])):
        rows = heads_of(at_ref[1], 4 - r, piece.shape[0])
        h = h + mm(turned(piece), w_ref[rows, :])

    @pl.when(pl.program_id(0) == 0)
    def _():
        h_ref[...] = h

    normal, _ = normalize(h)
    b_ref[...] = (normal * gain_ref[...] + bias_ref[...]).astype(BF)


def mid(at, pieces, w_o, tokens, gain, bias):
    features, rows = pieces[0].shape
    width, quarter = tokens.shape[1], rows // 4
    return call(
        mid_kernel,
        "mid",
        at,
        (4,),
        [pl.BlockSpec((features, quarter), lambda q, n: (0, (n[1] + q) % 4))] * 6
        + [fixed(w_o.shape)]
        + [pl.BlockSpec((quarter, width), lambda q, n: ((n[1] + q) % 4, 0))]
        + [fixed((1, width))] * 2,
        [fixed((quarter, width)), pl.BlockSpec((quarter, width), lambda q, n: (q, 0))],
        [like((quarter, width), F32), like((rows, width), BF)],
        (*pieces, w_o, tokens, gain, bias),
    )


def add_up(refs):
    total = refs[0][...]
    for ref in refs[1:]:
        total = total + ref[...].astype(F32)
    return total


def mid_back_kernel(at_ref, *refs):
    shares, (w_ref, h_ref, dy_ref, gain_ref, dh_ref, low_ref, sums_ref) = refs[:4], refs[4:11]
    do_refs = refs[11:]
    db = add_up(shares)
    normal, scale = normalize(h_ref[...])
    dh = dy_ref[...].astype(F32) + norm_back(db, gain_ref[...], normal, scale)
    dh_ref[...] = dh
    low = dh.astype(BF)
    low_ref[...] = low
    sums_ref[0:1, :] = jnp.sum(db * normal, axis=0, keepdims=True)
    sums_ref[1:2, :] = jnp.sum(db, axis=0, keepdims=True)
    for r in range(4):
        rows = heads_of(at_ref[1], r, do_refs[r].shape[0])
        do_refs[r][...] = mm_t(w_ref[rows, :], low).astype(BF)


def mid_back(at, shares, w_o, h, dy, gain):
    quarter, width = h.shape
    whole = fixed((quarter, width))
    piece = (w_o.shape[0] // 4, quarter)
    return call(
        mid_back_kernel,
        "mid_back",
        at,
        (1,),
        [whole] * 4 + [fixed(w_o.shape), whole, whole, fixed((1, width))],
        [whole] * 2 + [fixed((2, width))] + [fixed(piece)] * 4,
        [like((quarter, width), F32), like((quarter, width), BF), like((2, width), F32)]
        + [like(piece, BF)] * 4,
        (*shares, w_o, h, dy, gain),
    )


def first_back_kernel(at_ref, *refs):
    shares = refs[:4]
    x_ref, dh_ref, gain_ref, _, out_ref = refs[4:]
    d_a = add_up(shares)
    normal, scale = normalize(x_ref[...].astype(F32))
    out_ref[...] = (dh_ref[...] + norm_back(d_a, gain_ref[...], normal, scale)).astype(BF)


def first_back(at, shares, tokens, dh, gain, after):
    quarter, width = dh.shape
    return call(
        first_back_kernel,
        "first_back",
        at,
        (1,),
        [fixed((quarter, width))] * 4
        + [pl.BlockSpec((quarter, width), lambda i, n: (n[1], 0))]
        + [fixed((quarter, width)), fixed((1, width)), pl.BlockSpec(memory_space=pl.ANY)],
        fixed((quarter, width)),
        like((quarter, width), BF),
        (*shares, tokens, dh, gain, after),
    )


def in_order(mine, own, right, left, far, right_two, left_two):
    one = jnp.where(mine == 3, far, left)
    two = jnp.where(mine < 2, left_two, right_two)
    three = jnp.where(mine == 0, far, right)
    return own, one, two, three


def one_hot(slots, dest):
    return jnp.where(slots == dest, 1.0, 0.0).astype(BF)


def dispatch_kernel(at_ref, dest_ref, rows_ref, out_ref, spread_s):
    blk, rows = min(256, spread_s.shape[0]), dest_ref.shape[1]

    @pl.when(pl.program_id(0) == 0)
    def _():
        slot = lax.broadcasted_iota(jnp.int32, (blk, rows), 0)
        for start in range(0, spread_s.shape[0], blk):
            spread_s[start : start + blk, :] = one_hot(slot + start, dest_ref[...])

    out_ref[...] = mm(spread_s[...], rows_ref[...]).astype(BF)


def columns(rows, width):
    return pl.BlockSpec((rows, width), lambda i, n: (0, i))


def dispatch(at, dest_row, values, slots):
    rows, width = values.shape
    blk = min(256, width)
    return call(
        dispatch_kernel,
        "dispatch",
        at,
        (width // blk,),
        [fixed((1, rows)), columns(rows, blk)],
        columns(slots, blk),
        like((slots, width), BF),
        (dest_row, values),
        scratch=[pltpu.VMEM((slots, rows), BF)],
    )


def join_kernel(at_ref, *refs):
    pieces, out_ref = refs[:6], refs[6]
    r = pl.program_id(0)
    for place, piece in enumerate(in_order(at_ref[1], *[ref[...] for ref in pieces])):

        @pl.when(r == place)
        def _():
            out_ref[...] = piece


def join(at, pieces):
    each, width = pieces[0].shape
    return call(
        join_kernel,
        "join",
        at,
        (4,),
        [fixed((each, width))] * 6,
        pl.BlockSpec((each, width), lambda r, n: ((n[1] + r) % 4, 0)),
        like((4 * each, width), BF),
        pieces,
    )


def write_shares(mine, total, own_ref, one_ref, two_ref, three_ref, end_ref):
    rows = own_ref.shape[0]
    own_ref[...] = total[:rows]
    one, two, three = [total[r * rows : (r + 1) * rows].astype(BF) for r in (1, 2, 3)]
    one_ref[...] = one
    two_ref[...] = two
    three_ref[...] = three
    end_ref[...] = jnp.where(mine == 0, three, one)


def share_shapes(rows, width):
    return [like((rows, width), F32)] + [like((rows, width), BF)] * 4


def combine_kernel(count, whole, at_ref, *refs):
    dests, backs = refs[:count], refs[count : 2 * count]
    base_ref, refs, pick_s = refs[2 * count], refs[2 * count + 1 : -1], refs[-1]
    rows, slots = base_ref.shape[0], backs[0].shape[0]
    blk = rows // 4

    @pl.when(pl.program_id(0) == 0)
    def _():
        lane = lax.broadcasted_iota(jnp.int32, (blk, slots), 1)
        for k in range(count):
            for start in range(0, rows, blk):
                dest = dests[k][start : start + blk, :]
                pick_s[start : start + blk, k * slots : (k + 1) * slots] = one_hot(lane, dest)

    total = base_ref[...].astype(F32)
    for k in range(count):
        total = total + mm(pick_s[:, k * slots : (k + 1) * slots], backs[k][...])
    mine = at_ref[1]
    if whole:
        h_ref, out_ref = refs
        for r in range(4):
            part = total[r * blk : (r + 1) * blk]
            if r == 0:
                part = part + h_ref[...]
            place = pl.ds(pl.multiple_of(((mine + r) % 4) * blk, blk), blk)
            out_ref[place, :] = part.astype(BF)
    else:
        write_shares(mine, total, *refs)


def combine(at, dests, backs, base, h=None):
    count, (slots, width), rows = len(backs), backs[0].shape, base.shape[0]
    blk = min(256, width)
    whole = h is not None
    quarter = columns(rows // 4, blk)
    return call(
        partial(combine_kernel, count, whole),
        "combine",
        at,
        (width // blk,),
        [fixed((rows, 1))] * count
        + [columns(slots, blk)] * count
        + [columns(rows, blk)]
        + [quarter] * whole,
        columns(rows, blk) if whole else [quarter] * 5,
        like(base.shape, BF) if whole else share_shapes(rows // 4, width),
        (*dests, *backs, base) + ((h,) if whole else ()),
        scratch=[pltpu.VMEM((rows, count * slots), BF)],
    )


def mm_t(a, b):
    return lax.dot_general(a, b, (((1,), (1,)), ((), ())), preferred_element_type=F32)


def gelu_both(u):
    c = 0.7978845608028654
    square = u * u
    t = jnp.tanh(u * (c + (c * 0.044715) * square))
    half = 0.5 + 0.5 * t
    slope = half + (0.5 * u) * (1.0 - t * t) * (c + (3.0 * c * 0.044715) * square)
    return u * half, slope


def high_low(value):
    high = value.astype(BF)
    return high, (value - high.astype(F32)).astype(BF)


def two_coefs(logits, lane, experts):
    inside = (lane >= experts) & (lane < experts + 2)
    top = jnp.max(jnp.where(inside, logits, HIDE), axis=1, keepdims=True)
    e = jnp.where(inside, jnp.exp(logits - top), 0.0)
    e = e / jnp.sum(e, axis=1, keepdims=True)
    first = jnp.sum(jnp.where(lane == experts, e, 0.0), axis=1, keepdims=True)
    second = jnp.sum(jnp.where(lane == experts + 1, e, 0.0), axis=1, keepdims=True)
    return first, second


def small_back(d_small, rows, w_small_ref, small_ref, i):
    high, low = high_low(d_small)
    w_small = w_small_ref[...]
    high_t, low_t = high_low(d_small.T)

    @pl.when(i == 0)
    def _():
        small_ref[...] = jnp.zeros(small_ref.shape, F32)

    small_ref[...] += mm(high_t, rows) + mm(low_t, rows)
    return mm_t(high, w_small) + mm_t(low, w_small)


def expert_kernel(experts, half, at_ref, rows_ref, dy_ref, up_ref, down_ref, w_small_ref, *outs):
    if half:
        outs = outs[5:]
    rows_out_ref, hid_ref, dy_out_ref, deu_ref, y_ref, d_rows_ref, small_ref = outs
    rows = rows_ref[...]
    rows_out_ref[...] = rows
    up = mm(rows, up_ref[...])
    logits = mm(rows, w_small_ref[...])
    lane = lax.broadcasted_iota(jnp.int32, logits.shape, 1)
    routed = lane < experts
    top = jnp.max(jnp.where(routed, logits, HIDE), axis=1, keepdims=True)
    probs = jnp.where(routed, jnp.exp(logits - top), 0.0)
    probs = probs / jnp.sum(probs, axis=1, keepdims=True)
    own = jnp.where(lane == at_ref[2], 1.0, 0.0)
    gate = jnp.sum(probs * own, axis=1, keepdims=True)
    first, second = two_coefs(logits, lane, experts)
    weight = second * gate
    dy = dy_ref[...].reshape(rows.shape).astype(F32)
    d_y = (weight * dy).astype(BF)
    dy_out_ref[...] = d_y
    d_hidden = mm_t(d_y, down_ref[...])
    hidden, slope = gelu_both(up)
    hidden = hidden.astype(BF)
    hid_ref[...] = hidden
    d_up = (d_hidden * slope).astype(BF)
    deu_ref[...] = d_up
    y = mm(hidden, down_ref[...])
    y_ref[...] = (weight * y).astype(BF).reshape(y_ref.shape)
    along = gate * jnp.sum(dy * y, axis=1, keepdims=True)
    mixed = first * second * along
    d_small = (second * along) * (own - probs)
    d_small = jnp.where(routed, d_small, 0.0)
    d_small = d_small + jnp.where(lane == experts + 1, mixed, 0.0)
    d_small = d_small - jnp.where(lane == experts, mixed, 0.0)
    d_rows = mm_t(d_up, up_ref[...]) + small_back(d_small, rows, w_small_ref, small_ref, pl.program_id(0))
    d_rows_ref[...] = d_rows.astype(BF)


def expert_rows(at, rows, dy, w_up, w_down, w_small, experts, half, before):
    count, width = rows.shape
    hid, lanes = w_up.shape[1], w_small.shape[1]
    blk = min(512, count)
    capacity = count // dy.shape[0]
    steps = count // blk
    moving = pl.BlockSpec((blk, width), lambda i, n: (i, 0))
    slots = pl.BlockSpec((blk // capacity, capacity, width), lambda i, n: (i, half, 0))
    kept = [pl.BlockSpec((blk, size), lambda i, n: (i + half * steps, 0)) for size in (width, hid, width, hid)]
    return call(
        partial(expert_kernel, experts, half),
        "expert_rows",
        at,
        (steps,),
        [
            moving,
            slots,
            fixed((width, hid)),
            fixed((hid, width)),
            fixed((width, lanes)),
        ]
        + [pl.BlockSpec(memory_space=pl.ANY)] * (5 * half),
        kept + [slots, moving, fixed((lanes, width))],
        [like((2 * count, size), BF) for size in (width, hid, width, hid)]
        + [like(dy.shape, BF), like((count, width), BF)]
        + [like((lanes, width), F32)],
        (rows, dy, w_up, w_down, w_small, *before),
        alias={6 + k: k for k in range(5)} if half else None,
        vmem=56,
    )


def dense_kernel(experts, at_ref, rows_ref, dy_ref, in_ref, out_ref, w_small_ref, *outs):
    hid_ref, grad_ref, d_up_ref, mix_ref, db_ref, small_ref = outs
    rows = rows_ref[...]
    up = mm(rows, in_ref[...])
    logits = mm(rows, w_small_ref[...])
    lane = lax.broadcasted_iota(jnp.int32, logits.shape, 1)
    first, second = two_coefs(logits, lane, experts)
    dy = dy_ref[...].astype(F32)
    grad = (first * dy).astype(BF)
    grad_ref[...] = grad
    d_hidden = mm_t(grad, out_ref[...])
    hidden, slope = gelu_both(up)
    hidden = hidden.astype(BF)
    hid_ref[...] = hidden
    d_up = (d_hidden * slope).astype(BF)
    d_up_ref[...] = d_up
    dense = mm(hidden, out_ref[...])
    mix_ref[...] = first * dense
    mixed = first * second * jnp.sum(dy * dense, axis=1, keepdims=True)
    d_small = jnp.where(lane == experts, mixed, 0.0) - jnp.where(lane == experts + 1, mixed, 0.0)
    db_ref[...] = mm_t(d_up, in_ref[...]) + small_back(d_small, rows, w_small_ref, small_ref, pl.program_id(0))


def dense_rows(at, rows, dy, w_in, w_out, w_small, experts):
    (count, width), hid, lanes = rows.shape, w_in.shape[1], w_small.shape[1]
    blk = min(512, count)
    row_out = pl.BlockSpec((blk, width), lambda i, n: (i, 0))
    hid_out = pl.BlockSpec((blk, hid), lambda i, n: (i, 0))
    return call(
        partial(dense_kernel, experts),
        "dense_rows",
        at,
        (count // blk,),
        [row_out, row_out, fixed((width, hid)), fixed((hid, width)), fixed((width, lanes))],
        [hid_out, row_out, hid_out, row_out, row_out, fixed((lanes, width))],
        [
            like((count, hid), BF),
            like((count, width), BF),
            like((count, hid), BF),
            like((count, width), F32),
            like((count, width), F32),
            like((lanes, width), F32),
        ],
        (rows, dy, w_in, w_out, w_small),
        vmem=56,
    )


def turned(value):
    return value.astype(F32).T.astype(BF)


def dense_grads_kernel(at_ref, b_ref, d_up_ref, grad_ref, hid_ref, keep_ref, give_ref):
    width = d_up_ref.shape[1]
    first = mm(turned(b_ref[...]), d_up_ref[...]).astype(BF)
    second = mm(turned(grad_ref[...]), hid_ref[...]).astype(BF)
    half = pl.num_programs(0) // 2
    for side, ref in ((0, keep_ref), (1, give_ref)):

        @pl.when(pl.program_id(0) // half == side)
        def _():
            ref[0, :, :width] = first
            ref[0, :, width:] = second


def dense_grads(at, b, d_up, grad, hidden, parts):
    (rows, width), hid = b.shape, hidden.shape[1]
    own, half, bits = width // parts, parts // 2, parts.bit_length() - 1

    def part(q, n):
        turned_q = sum([((q // 2**k) % 2) * 2 ** (bits - 1 - k) for k in range(bits)])
        return turned_q ^ n[2]

    column = pl.BlockSpec((rows, own), lambda q, n: (0, part(q, n)))
    shape = (1, own, 2 * hid)
    return call(
        dense_grads_kernel,
        "dense_grads",
        at,
        (parts,),
        [column, fixed((rows, hid)), column, fixed((rows, hid))],
        [
            pl.BlockSpec(shape, lambda q, n: (jnp.minimum(q, half - 1), 0, 0)),
            pl.BlockSpec(shape, lambda q, n: (jnp.maximum(q - half, 0), 0, 0)),
        ],
        [like((half, own, 2 * hid), BF)] * 2,
        (b, d_up, grad, hidden),
    )


def attention_grads_kernel(experts, at_ref, *refs):
    grads, o_refs, refs = refs[:GROUP], refs[GROUP : GROUP + 6], refs[GROUP + 6 :]
    a_ref, dh_ref, w_ref, gain_ref, bias_ref, sums_ref = refs[:6]
    small_refs, (out_ref, all_s) = refs[6:-2], refs[-2:]
    heads, features = GROUP * HD, grads[1].shape[0]
    products, plain = 0.0, 0.0
    for k in range(GROUP):
        head = at_ref[0] ^ k
        rows = pl.ds(pl.multiple_of(head * features, features), features)
        grad = grads[k][...]
        weight = w_ref[head].astype(F32)
        total = mm(grad, a_ref[...])
        all_s[rows, :] = total
        each = jnp.sum(grad.astype(F32), axis=1, keepdims=True)
        products = products + jnp.sum(total * weight, axis=0, keepdims=True)
        plain = plain + jnp.sum(each * weight, axis=0, keepdims=True)
    first = GROUP * features
    for r, piece in enumerate(in_order(at_ref[1], *[ref[...] for ref in o_refs])):
        rows = pl.ds(pl.multiple_of(first + ((at_ref[1] + r) % 4) * heads, heads), heads)
        all_s[rows, :] = mm(piece, dh_ref[...])
    first += 4 * heads
    small = add_up(small_refs)
    row = lax.broadcasted_iota(jnp.int32, small.shape, 0)
    d_gain = (products - bias_ref[...] * plain) / gain_ref[...]
    for k, sums in enumerate((sums_ref[0:1, :], sums_ref[1:2, :], d_gain, plain)):
        small = jnp.where(row == experts + 2 + k, sums, small)
    all_s[first:, :] = small
    out_ref[...] = all_s[...].T.astype(BF)


def attention_grads(at, grads, o, a, dh, w_heads, gain, bias, sums, small, experts):
    rows, width = a.shape
    features, lanes = grads[0].shape[0], small[0].shape[0]
    piece = pl.BlockSpec((o[0].shape[0], dh.shape[0]), lambda i, n: (0, n[1]))
    height = GROUP * features + 4 * o[0].shape[0] + lanes
    blk = min(256, width)
    return call(
        partial(attention_grads_kernel, experts),
        "attention_grads",
        at,
        (width // blk,),
        [fixed((features, rows))] * GROUP
        + [piece] * 6
        + [columns(rows, blk), columns(dh.shape[0], blk)]
        + [pl.BlockSpec((GROUP, features, blk), lambda i, n: (0, 0, i))]
        + [columns(1, blk)] * 2
        + [columns(2, blk)]
        + [columns(lanes, blk)] * len(small),
        pl.BlockSpec((blk, height), lambda i, n: (i, 0)),
        like((width, height), BF),
        (*grads, *o, a, dh, w_heads, gain, bias, sums, *small),
        scratch=[pltpu.VMEM((height, blk), F32)],
    )


def project_kernel(at_ref, *refs):
    grads, w_ref, outs, turned_s = refs[:GROUP], refs[GROUP], refs[GROUP + 1 : -1], refs[-1]
    rows = turned_s.shape[1]
    blk = rows // 4

    @pl.when(pl.program_id(0) == 0)
    def _():
        for s in range(GROUP):
            for r in range(4):
                lanes = pl.ds(pl.multiple_of(((at_ref[1] + r) % 4) * blk, blk), blk)
                turned_s[s, r * blk : (r + 1) * blk, :] = turned(grads[s][:, lanes])

    total = 0.0
    for s in range(GROUP):
        total = total + mm(turned_s[s], w_ref[at_ref[0] ^ s])
    write_shares(at_ref[1], total, *outs)


def project_back(at, grads, w_heads):
    features, rows = grads[0].shape
    width = w_heads.shape[2]
    blk = min(256, width)
    return call(
        project_kernel,
        "project_back",
        at,
        (width // blk,),
        [fixed((features, rows))] * GROUP
        + [pl.BlockSpec((GROUP, features, blk), lambda i, n: (0, 0, i))],
        [columns(rows // 4, blk)] * 5,
        share_shapes(rows // 4, width),
        (*grads, w_heads),
        scratch=[pltpu.VMEM((GROUP, rows, features), BF)],
    )


def hop(value, *pairs):
    return lax.ppermute(value, "mp", pairs)


def rotate(value, steps):
    return hop(value, *[(s, (s + steps) % 4) for s in range(4)])


def gather_near(own):
    right = hop(own, (0, 1), (1, 2), (2, 3))
    left = hop(own, (1, 0), (2, 1), (3, 2))
    return own, right, left, hop(own, (0, 3), (3, 0))


def gather_far(near):
    _, right, left, _ = near
    return *near, hop(right, (1, 2), (2, 3)), hop(left, (1, 0), (2, 1))


def gather_pieces(own):
    return gather_far(gather_near(own))


def scatter_far(shares):
    _, _, two, _, end = shares
    return hop(two, (2, 1), (3, 2)), hop(two, (0, 1), (1, 2)), hop(end, (0, 3), (3, 0))


def scatter_near(shares, came):
    own, one, _, three, _ = shares
    from_right, from_left, from_end = came
    three = (three.astype(F32) + from_right.astype(F32)).astype(BF)
    one = (one.astype(F32) + from_left.astype(F32)).astype(BF)
    return own, hop(three, (1, 0), (2, 1), (3, 2)), hop(one, (0, 1), (1, 2), (2, 3)), from_end


def group_swap(value, s):
    count = lax.axis_size("dp")
    return lax.ppermute(value, "dp", [(t, t ^ s) for t in range(count)])


def expert_swap(value, experts):
    wide = value.reshape(experts, value.shape[0] // experts, value.shape[1])
    return lax.all_to_all(wide, "dp", 0, 0, tiled=True).reshape(value.shape)


def roll_rows(value, start):
    twice = jnp.concatenate([value, value], axis=0)
    return lax.dynamic_slice_in_dim(twice, start, value.shape[0], 0)


def add_halves(keep, came):
    return (keep.astype(F32) + came.astype(F32)).astype(BF)


def body(
    tokens,
    cotangent,
    ln_gains,
    ln_biases,
    w_qkv,
    w_o,
    w_in,
    w_out,
    w_router,
    w_coef,
    w_up,
    w_down,
    routes,
    long_group,
):
    rows, width = tokens.shape
    dps = lax.axis_size("dp")
    mine, position = lax.axis_index("mp"), lax.axis_index("dp")
    quarter = rows // 4
    start = mine * quarter
    heads_loc = w_qkv.shape[2] // HD
    hid = w_in.shape[1]
    experts = w_router.shape[1]
    capacity = max(2, 2 * rows // experts)
    half = capacity // 2
    barrier = lax.optimization_barrier
    first_len = lax.dynamic_index_in_dim(long_group, position // GROUP, 0, keepdims=False)
    at = jnp.stack([position % GROUP, mine, position, first_len]).astype(jnp.int32)
    gains = [ln_gains[0:1], ln_gains[1:2]]
    biases = [ln_biases[0:1], ln_biases[1:2]]
    w_o_all = lax.all_gather(w_o, "mp", axis=0, tiled=True)

    w_heads = w_qkv.reshape(width, 3, heads_loc, HD).transpose(2, 1, 3, 0)
    w_heads = w_heads.reshape(heads_loc, 3 * HD, width)
    a_r, *qkv = project(at, tokens, gains[0], biases[0], w_heads)
    qkv = [qkv[0]] + [group_swap(qkv[s], s) for s in (1, 2, 3)]

    route = roll_rows(routes, start)[:, 0]
    picked = (route[:, None] == jnp.arange(experts, dtype=jnp.int32)[None, :]).astype(jnp.int32)
    slot = jnp.sum((jnp.cumsum(picked, axis=0) - picked) * picked, axis=1)
    dy_b = roll_rows(cotangent, start)
    full = route * capacity + slot
    send_dy = dispatch(at, full[None, :], dy_b, experts * capacity)
    *qkv, send_dy = barrier((*qkv, send_dy))
    in_half = [slot < half, slot >= half]
    dests = [
        jnp.where(in_half[k], route * half + slot - k * half, -1).astype(jnp.int32) for k in (0, 1)
    ]

    *o_t, lse = attend(at, qkv)
    *o_t, w_o_all = barrier((*o_t, w_o_all))
    o_heads = [o_t[0]] + [group_swap(o_t[s], s) for s in (1, 2, 3)]
    lanes = -(-(experts + 2) // 128) * 128
    w_small = jnp.concatenate(
        [w_router, w_coef, jnp.zeros((width, lanes - experts - 2), BF)], axis=1
    )
    *o_heads, send_dy, w_small = barrier((*o_heads, send_dy, w_small))
    got_dy = expert_swap(send_dy, experts).reshape(experts, capacity, width)
    o_pieces = gather_pieces(stack(at, o_heads))
    h, b_r = mid(at, o_pieces, w_o_all, tokens, gains[1], biases[1])

    send_0 = dispatch(at, dests[0][None, :], b_r, experts * half)
    send_0, got_dy = barrier((send_0, got_dy))
    got_0 = expert_swap(send_0, experts)
    send_1 = dispatch(at, dests[1][None, :], b_r, experts * half)
    b_r, send_1 = barrier((b_r, send_1))
    hidden, dense_grad, d_up, mix_base, db_base, small_t = dense_rows(
        at, b_r, dy_b, w_in, w_out, w_small, experts
    )
    send_1, got_0, db_base = barrier((send_1, got_0, db_base))
    got_1 = expert_swap(send_1, experts)

    *kept, d_rows_0, small_0 = expert_rows(
        at, got_0, got_dy, w_up[0], w_down[0], w_small, experts, 0, ()
    )
    back_0 = expert_swap(d_rows_0, experts)
    *kept, d_rows_1, small_1 = expert_rows(
        at, got_1, got_dy, w_up[0], w_down[0], w_small, experts, 1, kept
    )
    got, hidden_e, d_y, d_eu, back_y = kept
    back_1 = expert_swap(d_rows_1, experts)
    d_rows_1, b_r = barrier((d_rows_1, b_r))
    halving = width == dps * 128
    if halving:
        grads = dense_grads(at, b_r, d_up, dense_grad, hidden, dps)
    else:
        grads = [ein("td,tf->df", b_r, d_up).astype(BF), ein("td,tf->df", dense_grad, hidden).astype(BF)]
    back_0, back_1, back_y, *grads = barrier((back_0, back_1, back_y, *grads))

    dest_cols = [dest[:, None] for dest in dests]
    tok_y = expert_swap(back_y.reshape(experts * capacity, width), experts)
    shares = combine(at, dest_cols, [back_0, back_1], db_base)
    far = scatter_far(shares)
    *far, g_0, g_1 = barrier((*far, *grads))
    grads = [g_0, g_1]
    shares = scatter_near(shares, far)

    mix = combine(at, [full[:, None]], [tok_y], mix_base, h)
    *shares, mix = barrier((*shares, mix))
    output = lax.psum(mix, "mp")
    dh, dh_r, sums_2, *do_q = mid_back(at, shares, w_o_all, h, dy_b, gains[1])
    do_q = [do_q[0]] + [rotate(do_q[r], -r) for r in (1, 2, 3)]
    do_heads = unsplit(at, do_q)
    do_t = [do_heads[0]] + [group_swap(do_heads[s], s) for s in (1, 2, 3)]
    if halving:
        came_1 = group_swap(grads[1], 1)
        half = dps // 4
        give = add_halves(grads[0][half:], came_1[half:])
        *do_t, give = barrier((*do_t, give))
        came_2 = group_swap(give, 2)
    d_qkv = attend_back(at, qkv, do_t, o_t, lse)
    if halving:
        keep = add_halves(grads[0][:half], came_1[:half])
        *d_qkv, came_2, keep = barrier((*d_qkv, came_2, keep))
        grads = add_halves(keep, came_2)
        bit = 4
        while bit < dps:
            half = grads.shape[0] // 2
            grads = add_halves(grads[:half], group_swap(grads[half:], bit))
            bit *= 2
        grads = [grads[0][:, :hid], grads[0][:, hid:]]
    else:
        grads = [lax.psum_scatter(grad, "dp", scatter_dimension=0, tiled=True) for grad in grads]

    d_own, got, hidden_e, d_y, d_eu = barrier((d_qkv[0], got, hidden_e, d_y, d_eu))
    d_qkv = [d_own] + [group_swap(d_qkv[s], s) for s in (1, 2, 3)]
    grad_down = ein("rf,rd->fd", hidden_e, d_y)
    *d_qkv, grad_down = barrier((*d_qkv, grad_down))
    shares = project_back(at, d_qkv, w_heads)
    far = scatter_far(shares)
    grads_a = attention_grads(
        at, d_qkv, o_pieces, a_r, dh_r, w_heads, gains[0], biases[0], sums_2, (small_0, small_1, small_t), experts
    )
    grad_up = ein("rd,rf->df", got, d_eu)
    grads_a, corner, grad_up, *far = barrier((grads_a, output[:16, :128], grad_up, *far))
    grads_a = lax.psum_scatter(grads_a, "dp", scatter_dimension=0, tiled=True).T
    shares = scatter_near(shares, far)
    grad_q = first_back(at, shares, tokens, dh, gains[0], corner)
    grad_tokens = join(at, gather_pieces(grad_q))

    own, heads = width // dps, heads_loc * HD
    grad_qkv = grads_a[: 3 * heads].astype(F32).reshape(heads_loc, 3, HD, own).transpose(3, 1, 0, 2)
    grad_qkv = grad_qkv.reshape(own, 3, heads)
    grad_in = grads[0].astype(F32)
    grad_out = grads[1].astype(F32).T
    rest = grads_a[3 * heads : 7 * heads].reshape(4, heads, own)
    small = jnp.broadcast_to(grads_a[7 * heads :], (4, lanes, own))
    rest = lax.all_to_all(jnp.concatenate([rest, small], axis=1), "mp", 0, 0, tiled=True)
    rest = jnp.sum(rest.astype(F32), axis=0)
    grad_o, small = rest[:heads], rest[heads:]
    small_out = small[: experts + 2].T
    return (
        output,
        grad_tokens,
        jnp.stack([small[experts + 4], small[experts + 2]]),
        jnp.stack([small[experts + 5], small[experts + 3]]),
        grad_qkv,
        grad_o,
        grad_in,
        grad_out,
        small_out[:, :experts],
        small_out[:, experts:],
        grad_up[None],
        grad_down[None],
    )


def solution(mesh):
    in_specs = (
        P("dp", None),
        P("dp", None),
        P(),
        P(),
        P(None, None, "mp"),
        P("mp", None),
        P(None, "mp"),
        P("mp", None),
        P(),
        P(),
        P("dp", None, "mp"),
        P("dp", "mp", None),
        P("dp", None),
        P(),
    )
    out_specs = (
        P("dp", None),
        P("dp", None),
        P(None, "dp"),
        P(None, "dp"),
        P("dp", None, "mp"),
        P("mp", "dp"),
        P("dp", "mp"),
        P("mp", "dp"),
        P("dp", None),
        P("dp", None),
        P("dp", None, "mp"),
        P("dp", "mp", None),
    )
    return jax.shard_map(body, mesh=mesh, in_specs=in_specs, out_specs=out_specs, check_vma=False)
```

```python
from functools import partial

import jax
import jax.numpy as jnp
from jax import lax
from jax.experimental import pallas as pl
from jax.experimental.pallas import tpu as pltpu
from jax.sharding import PartitionSpec as P

HD = 64
GROUP = 4
EPS = 1e-05
LOG2E = 1.4426950408889634
SCALE2 = 0.125 * LOG2E
HIDE = -1e30
BF = jnp.bfloat16
F32 = jnp.float32
LIGHT = pl.CostEstimate(flops=1 << 20, bytes_accessed=1 << 20, transcendentals=0)


def mm(a, b):
    return jnp.dot(a, b, preferred_element_type=F32)


def ein(spec, a, b):
    return jnp.einsum(spec, a, b, preferred_element_type=F32)


def call(kernel, name, prefetch, grid, in_specs, out_specs, out_shape, args, scratch=(), alias=None, vmem=48):
    return pl.pallas_call(
        kernel,
        grid_spec=pltpu.PrefetchScalarGridSpec(
            num_scalar_prefetch=1,
            grid=grid,
            in_specs=in_specs,
            out_specs=out_specs,
            scratch_shapes=list(scratch),
        ),
        out_shape=out_shape,
        input_output_aliases=alias or {},
        compiler_params=pltpu.CompilerParams(vmem_limit_bytes=vmem * 2**20),
        cost_estimate=LIGHT,
        name=name,
    )(prefetch, *args)


def fixed(shape):
    zeros = (0,) * len(shape)
    return pl.BlockSpec(shape, lambda *_: zeros)


def like(shape, dtype):
    return jax.ShapeDtypeStruct(shape, dtype)


def normalize(v):
    mean = jnp.mean(v, axis=-1, keepdims=True)
    centred = v - mean
    scale = lax.rsqrt(jnp.mean(centred * centred, axis=-1, keepdims=True) + EPS)
    return centred * scale, scale


def norm_back(grad, gain, normal, scale):
    g = grad * gain
    along = jnp.mean(g * normal, axis=-1, keepdims=True)
    return scale * (g - jnp.mean(g, axis=-1, keepdims=True) - normal * along)


def qkv_kernel(at_ref, x_ref, gain_ref, bias_ref, w_ref, a_ref, *outs):
    normal, _ = normalize(x_ref[...].astype(F32))
    a = (normal * gain_ref[...] + bias_ref[...]).astype(BF)
    a_ref[...] = a
    for s in range(GROUP):
        outs[s][...] = mm_t(w_ref[at_ref[0] ^ s], a).astype(BF)


def project(at, tokens, gain, bias, w_heads):
    rows, width = tokens.shape
    features = w_heads.shape[1]
    blk = min(256, rows)
    moving = pl.BlockSpec((blk, width), lambda i, n: (i, 0))
    return call(
        qkv_kernel,
        "project",
        at,
        (rows // blk,),
        [moving, fixed((1, width)), fixed((1, width)), fixed(w_heads.shape)],
        [moving] + [pl.BlockSpec((features, blk), lambda i, n: (0, i))] * GROUP,
        [like((rows, width), BF)] + [like((features, rows), BF)] * GROUP,
        (tokens, gain, bias, w_heads),
    )


def fill_keys(k_s, place, keys, first_len, blk):
    rows = place * blk + lax.broadcasted_iota(jnp.int32, (blk, 128), 0)
    lane = lax.broadcasted_iota(jnp.int32, (blk, 128), 1)
    wide = jnp.concatenate([keys.astype(F32).T, jnp.zeros((blk, 128 - HD), F32)], axis=1)
    wide = jnp.where((lane == HD) & (rows < first_len), HIDE, wide)
    k_s[pl.ds(place * blk, blk), :] = wide.astype(BF)


def wide_query(query, place, first_len, blk):
    cols = place * blk + lax.broadcasted_iota(jnp.int32, (128 - HD, blk), 1)
    sub = lax.broadcasted_iota(jnp.int32, (128 - HD, blk), 0)
    extra = jnp.where((sub == 0) & (cols >= first_len), 1.0, 0.0)
    return jnp.concatenate([query, extra.astype(BF)], axis=0)


def causal(blk):
    keys = lax.broadcasted_iota(jnp.int32, (blk, blk), 0)
    queries = lax.broadcasted_iota(jnp.int32, (blk, blk), 1)
    return keys <= queries


def attend_kernel(blk, per, at_ref, *refs):
    qkv_refs, o_refs = refs[:GROUP], refs[GROUP : 2 * GROUP]
    lse_ref, k_s, qkv_s = refs[2 * GROUP :]
    i = pl.program_id(0)
    place, first_len = at_ref[0], at_ref[3]

    @pl.when(i == 0)
    def _():
        for s in range(GROUP):
            qkv_s[place ^ s] = qkv_refs[s][...]

    def part(which, j):
        return qkv_s[j // per, HD * which : HD * (which + 1), pl.ds((j % per) * blk, blk)]

    fill_keys(k_s, i, part(1, i), first_len, blk)
    query = wide_query(part(0, i), i, first_len, blk)

    def scores(j):
        return mm(k_s[pl.ds(pl.multiple_of(j * blk, blk), blk), :], query)

    s = jnp.where(causal(blk), scores(i), HIDE)
    top = jnp.max(s, axis=0, keepdims=True)
    p = jnp.exp2((s - top) * SCALE2)
    total = jnp.sum(p, axis=0, keepdims=True)
    acc = mm(part(2, i), p.astype(BF))

    def steps(blocks, carry):
        top, total, acc = carry
        s = [scores(j) for j in blocks]
        new = top
        for one in s:
            new = jnp.maximum(new, jnp.max(one, axis=0, keepdims=True))
        keep = jnp.exp2((top - new) * SCALE2)
        total, acc = total * keep, acc * keep
        for j, one in zip(blocks, s):
            p = jnp.exp2((one - new) * SCALE2)
            total = total + jnp.sum(p, axis=0, keepdims=True)
            acc = acc + mm(part(2, j), p.astype(BF))
        return new, total, acc

    low = jnp.where(i * blk >= first_len, first_len // blk, 0)
    pairs = (i - low) // 2
    carry = lax.fori_loop(
        0, pairs, lambda t, c: steps([low + 2 * t, low + 2 * t + 1], c), (top, total, acc)
    )
    top, total, acc = lax.fori_loop(low + 2 * pairs, i, lambda j, c: steps([j], c), carry)
    out = (acc / total).astype(BF)
    for s in range(GROUP):

        @pl.when((i // per) ^ place == s)
        def _():
            o_refs[s][:, pl.ds((i % per) * blk, blk)] = out

    lse_ref[0] = top * SCALE2 + jnp.log2(total)


def attend(at, qkv):
    features, rows = qkv[0].shape
    blk = min(512, rows)
    per = rows // blk
    count = GROUP * per
    return call(
        partial(attend_kernel, blk, per),
        "attend",
        at,
        (count,),
        [fixed((features, rows))] * GROUP,
        [fixed((HD, rows))] * GROUP + [pl.BlockSpec((1, 1, blk), lambda i, n: (i, 0, 0))],
        [like((HD, rows), BF)] * GROUP + [like((count, 1, blk), F32)],
        qkv,
        scratch=[pltpu.VMEM((GROUP * rows, 128), BF), pltpu.VMEM((GROUP, features, rows), BF)],
    )


def back_kernel(blk, per, count, at_ref, *refs):
    qkv_refs, do_refs, o_refs = refs[:GROUP], refs[GROUP : 2 * GROUP], refs[2 * GROUP : 3 * GROUP]
    lse_ref, refs = refs[3 * GROUP], refs[3 * GROUP + 1 :]
    out_refs, refs = refs[:GROUP], refs[GROUP:]
    dq_ref, out_ref, k_s, kt_s, v_s, wide_s, dot_s, both_s, delta_s, acc_s = refs
    j = pl.program_id(0)
    place, first_len = at_ref[0], at_ref[3]

    @pl.when(j == 0)
    def _():
        dq_ref[...] = jnp.zeros(dq_ref.shape, F32)
        zero = jnp.zeros((blk, HD), F32)
        for s in range(GROUP):
            for sub in range(per):
                i = (place ^ s) * per + sub
                at = pl.ds(pl.multiple_of(i * blk, blk), blk)
                cut = slice(sub * blk, (sub + 1) * blk)
                query = qkv_refs[s][0:HD, cut]
                keys = qkv_refs[s][HD : 2 * HD, cut]
                grad = do_refs[s][:, cut]
                fill_keys(k_s, i, keys, first_len, blk)
                kt_s[:, at] = keys
                dot_s[:, at] = grad
                wide_s[:, at] = wide_query(query, i, first_len, blk)
                grad = grad.astype(F32)
                values = qkv_refs[s][2 * HD :, cut].astype(F32)
                v_s[at, :] = jnp.concatenate([values.T, zero], axis=1).astype(BF)
                both_s[0, at, :] = jnp.concatenate([grad.T, zero], axis=1).astype(BF)
                both_s[1, at, :] = jnp.concatenate([zero, query.astype(F32).T], axis=1).astype(BF)
                held = o_refs[s][:, cut].astype(F32)
                delta_s[i] = jnp.sum(held * grad, axis=0, keepdims=True)

    here = pl.ds(pl.multiple_of(j * blk, blk), blk)
    keys_t = kt_s[:, here]
    values = v_s[here, 0:HD]

    def pair(i, diagonal):
        at = pl.ds(pl.multiple_of(i * blk, blk), blk)
        s = mm(k_s[here, :], wide_s[:, at])
        p = jnp.exp2(s * SCALE2 - lse_ref[i])
        if diagonal:
            p = jnp.where(causal(blk), p, 0.0)
        dp = mm(values, dot_s[:, at])
        ds = (p * (dp - delta_s[i])).astype(BF)
        return mm(p.astype(BF), both_s[0, at, :]) + mm(ds, both_s[1, at, :]), mm(keys_t, ds)

    acc_s[...], dq = pair(j, True)
    dq_ref[:, here] += dq

    def step_two(t, carry):
        i = j + 1 + 2 * t
        (kv_0, dq_0), (kv_1, dq_1) = pair(i, False), pair(i + 1, False)
        acc_s[...] += kv_0 + kv_1
        at = pl.ds(pl.multiple_of(i * blk, blk), 2 * blk)
        dq_ref[:, at] += jnp.concatenate([dq_0, dq_1], axis=1)
        return carry

    def step(i, carry):
        kv, dq = pair(i, False)
        acc_s[...] += kv
        dq_ref[:, pl.ds(pl.multiple_of(i * blk, blk), blk)] += dq
        return carry

    high = jnp.where((j + 1) * blk <= first_len, (first_len + blk - 1) // blk, count)
    pairs = (high - j - 1) // 2
    lax.fori_loop(0, pairs, step_two, 0)
    lax.fori_loop(j + 1 + 2 * pairs, high, step, 0)
    both = acc_s[...].T
    out_ref[0:HD, :] = (dq_ref[:, here] * 0.125).astype(BF)
    out_ref[HD : 2 * HD, :] = (both[HD:, :] * 0.125).astype(BF)
    out_ref[2 * HD :, :] = both[:HD, :].astype(BF)
    for s in range(GROUP):

        @pl.when((j // per) ^ place == s)
        def _():
            out_refs[s][:, pl.ds(pl.multiple_of((j % per) * blk, blk), blk)] = out_ref[...]


def attend_back(at, qkv, do, o, lse):
    features, rows = qkv[0].shape
    blk = min(512, rows)
    per = rows // blk
    count = GROUP * per
    return call(
        partial(back_kernel, blk, per, count),
        "attend_back",
        at,
        (count,),
        [fixed((features, rows))] * GROUP
        + [fixed((HD, rows))] * (2 * GROUP)
        + [fixed((count, 1, blk))],
        [fixed((features, rows))] * GROUP,
        [like((features, rows), BF)] * GROUP,
        (*qkv, *do, *o, lse),
        scratch=[
            pltpu.VMEM((HD, GROUP * rows), F32),
            pltpu.VMEM((features, blk), BF),
            pltpu.VMEM((GROUP * rows, 128), BF),
            pltpu.VMEM((HD, GROUP * rows), BF),
            pltpu.VMEM((GROUP * rows, 128), BF),
            pltpu.VMEM((128, GROUP * rows), BF),
            pltpu.VMEM((HD, GROUP * rows), BF),
            pltpu.VMEM((2, GROUP * rows, 128), BF),
            pltpu.VMEM((count, 1, blk), F32),
            pltpu.VMEM((blk, 128), F32),
        ],
        vmem=36,
    )


def stack_kernel(at_ref, *refs):
    ins, out_ref = refs[:GROUP], refs[GROUP]
    for s in range(GROUP):
        head = pl.ds(pl.multiple_of((at_ref[0] ^ s) * HD, HD), HD)
        out_ref[head, :] = ins[s][...]


def stack(at, heads):
    rows = heads[0].shape[1]
    return call(
        stack_kernel,
        "stack",
        at,
        (1,),
        [fixed((HD, rows))] * GROUP,
        fixed((GROUP * HD, rows)),
        like((GROUP * HD, rows), BF),
        heads,
    )


def unsplit_kernel(at_ref, *refs):
    ins, outs = refs[:4], refs[4:]
    cols = ins[0].shape[1]
    for r in range(4):
        lanes = pl.ds(pl.multiple_of(((at_ref[1] + r) % 4) * cols, cols), cols)
        for s in range(GROUP):
            head = pl.ds(pl.multiple_of((at_ref[0] ^ s) * HD, HD), HD)
            outs[s][:, lanes] = ins[r][head, :]


def unsplit(at, pieces):
    shape = (HD, 4 * pieces[0].shape[1])
    return call(
        unsplit_kernel,
        "unsplit",
        at,
        (1,),
        [fixed(pieces[0].shape)] * 4,
        [fixed(shape)] * GROUP,
        [like(shape, BF)] * GROUP,
        pieces,
    )


def heads_of(mine, r, features):
    return pl.ds(pl.multiple_of(((mine + 4 - r) % 4) * features, features), features)


def mid_kernel(at_ref, *refs):
    pieces, (w_ref, x_ref, gain_ref, bias_ref, h_ref, b_ref) = refs[:6], refs[6:]
    h = x_ref[...].astype(F32)
    for r, piece in enumerate(in_order(at_ref[1], *[ref[...] for ref in pieces])):
        rows = heads_of(at_ref[1], 4 - r, piece.shape[0])
        h = h + mm(turned(piece), w_ref[rows, :])

    @pl.when(pl.program_id(0) == 0)
    def _():
        h_ref[...] = h

    normal, _ = normalize(h)
    b_ref[...] = (normal * gain_ref[...] + bias_ref[...]).astype(BF)


def mid(at, pieces, w_o, tokens, gain, bias):
    features, rows = pieces[0].shape
    width, quarter = tokens.shape[1], rows // 4
    return call(
        mid_kernel,
        "mid",
        at,
        (4,),
        [pl.BlockSpec((features, quarter), lambda q, n: (0, (n[1] + q) % 4))] * 6
        + [fixed(w_o.shape)]
        + [pl.BlockSpec((quarter, width), lambda q, n: ((n[1] + q) % 4, 0))]
        + [fixed((1, width))] * 2,
        [fixed((quarter, width)), pl.BlockSpec((quarter, width), lambda q, n: (q, 0))],
        [like((quarter, width), F32), like((rows, width), BF)],
        (*pieces, w_o, tokens, gain, bias),
    )


def add_up(refs):
    total = refs[0][...]
    for ref in refs[1:]:
        total = total + ref[...].astype(F32)
    return total


def mid_back_kernel(at_ref, *refs):
    shares, (w_ref, h_ref, dy_ref, gain_ref, dh_ref, low_ref, sums_ref) = refs[:4], refs[4:11]
    do_refs = refs[11:]
    db = add_up(shares)
    normal, scale = normalize(h_ref[...])
    dh = dy_ref[...].astype(F32) + norm_back(db, gain_ref[...], normal, scale)
    dh_ref[...] = dh
    low = dh.astype(BF)
    low_ref[...] = low
    sums_ref[0:1, :] = jnp.sum(db * normal, axis=0, keepdims=True)
    sums_ref[1:2, :] = jnp.sum(db, axis=0, keepdims=True)
    for r in range(4):
        rows = heads_of(at_ref[1], r, do_refs[r].shape[0])
        do_refs[r][...] = mm_t(w_ref[rows, :], low).astype(BF)


def mid_back(at, shares, w_o, h, dy, gain):
    quarter, width = h.shape
    whole = fixed((quarter, width))
    piece = (w_o.shape[0] // 4, quarter)
    return call(
        mid_back_kernel,
        "mid_back",
        at,
        (1,),
        [whole] * 4 + [fixed(w_o.shape), whole, whole, fixed((1, width))],
        [whole] * 2 + [fixed((2, width))] + [fixed(piece)] * 4,
        [like((quarter, width), F32), like((quarter, width), BF), like((2, width), F32)]
        + [like(piece, BF)] * 4,
        (*shares, w_o, h, dy, gain),
    )


def first_back_kernel(at_ref, *refs):
    shares = refs[:4]
    x_ref, dh_ref, gain_ref, out_ref = refs[4:]
    d_a = add_up(shares)
    normal, scale = normalize(x_ref[...].astype(F32))
    out_ref[...] = (dh_ref[...] + norm_back(d_a, gain_ref[...], normal, scale)).astype(BF)


def first_back(at, shares, tokens, dh, gain):
    quarter, width = dh.shape
    return call(
        first_back_kernel,
        "first_back",
        at,
        (1,),
        [fixed((quarter, width))] * 4
        + [pl.BlockSpec((quarter, width), lambda i, n: (n[1], 0))]
        + [fixed((quarter, width)), fixed((1, width))],
        fixed((quarter, width)),
        like((quarter, width), BF),
        (*shares, tokens, dh, gain),
    )


def in_order(mine, own, right, left, far, right_two, left_two):
    one = jnp.where(mine == 3, far, left)
    two = jnp.where(mine < 2, left_two, right_two)
    three = jnp.where(mine == 0, far, right)
    return own, one, two, three


def one_hot(slots, dest):
    return jnp.where(slots == dest, 1.0, 0.0).astype(BF)


def dispatch_kernel(at_ref, dest_ref, rows_ref, out_ref, spread_s):
    blk, rows = min(256, spread_s.shape[0]), dest_ref.shape[1]

    @pl.when(pl.program_id(0) == 0)
    def _():
        slot = lax.broadcasted_iota(jnp.int32, (blk, rows), 0)
        for start in range(0, spread_s.shape[0], blk):
            spread_s[start : start + blk, :] = one_hot(slot + start, dest_ref[...])

    out_ref[...] = mm(spread_s[...], rows_ref[...]).astype(BF)


def columns(rows, width):
    return pl.BlockSpec((rows, width), lambda i, n: (0, i))


def dispatch(at, dest_row, values, slots):
    rows, width = values.shape
    blk = min(256, width)
    return call(
        dispatch_kernel,
        "dispatch",
        at,
        (width // blk,),
        [fixed((1, rows)), columns(rows, blk)],
        columns(slots, blk),
        like((slots, width), BF),
        (dest_row, values),
        scratch=[pltpu.VMEM((slots, rows), BF)],
    )


def join_kernel(at_ref, *refs):
    pieces, out_ref = refs[:6], refs[6]
    r = pl.program_id(0)
    for place, piece in enumerate(in_order(at_ref[1], *[ref[...] for ref in pieces])):

        @pl.when(r == place)
        def _():
            out_ref[...] = piece


def join(at, pieces):
    each, width = pieces[0].shape
    return call(
        join_kernel,
        "join",
        at,
        (4,),
        [fixed((each, width))] * 6,
        pl.BlockSpec((each, width), lambda r, n: ((n[1] + r) % 4, 0)),
        like((4 * each, width), BF),
        pieces,
    )


def write_shares(mine, total, own_ref, one_ref, two_ref, three_ref, end_ref):
    rows = own_ref.shape[0]
    own_ref[...] = total[:rows]
    one, two, three = [total[r * rows : (r + 1) * rows].astype(BF) for r in (1, 2, 3)]
    one_ref[...] = one
    two_ref[...] = two
    three_ref[...] = three
    end_ref[...] = jnp.where(mine == 0, three, one)


def share_shapes(rows, width):
    return [like((rows, width), F32)] + [like((rows, width), BF)] * 4


def combine_kernel(count, whole, at_ref, *refs):
    dests, backs = refs[:count], refs[count : 2 * count]
    base_ref, refs, pick_s = refs[2 * count], refs[2 * count + 1 : -1], refs[-1]
    rows, slots = base_ref.shape[0], backs[0].shape[0]
    blk = rows // 4

    @pl.when(pl.program_id(0) == 0)
    def _():
        lane = lax.broadcasted_iota(jnp.int32, (blk, slots), 1)
        for k in range(count):
            for start in range(0, rows, blk):
                dest = dests[k][start : start + blk, :]
                pick_s[start : start + blk, k * slots : (k + 1) * slots] = one_hot(lane, dest)

    total = base_ref[...].astype(F32)
    for k in range(count):
        total = total + mm(pick_s[:, k * slots : (k + 1) * slots], backs[k][...])
    mine = at_ref[1]
    if whole:
        h_ref, out_ref = refs
        for r in range(4):
            part = total[r * blk : (r + 1) * blk]
            if r == 0:
                part = part + h_ref[...]
            place = pl.ds(pl.multiple_of(((mine + r) % 4) * blk, blk), blk)
            out_ref[place, :] = part.astype(BF)
    else:
        write_shares(mine, total, *refs)


def combine(at, dests, backs, base, h=None):
    count, (slots, width), rows = len(backs), backs[0].shape, base.shape[0]
    blk = min(256, width)
    whole = h is not None
    quarter = columns(rows // 4, blk)
    return call(
        partial(combine_kernel, count, whole),
        "combine",
        at,
        (width // blk,),
        [fixed((rows, 1))] * count
        + [columns(slots, blk)] * count
        + [columns(rows, blk)]
        + [quarter] * whole,
        columns(rows, blk) if whole else [quarter] * 5,
        like(base.shape, BF) if whole else share_shapes(rows // 4, width),
        (*dests, *backs, base) + ((h,) if whole else ()),
        scratch=[pltpu.VMEM((rows, count * slots), BF)],
    )


def mm_t(a, b):
    return lax.dot_general(a, b, (((1,), (1,)), ((), ())), preferred_element_type=F32)


def gelu_both(u):
    c = 0.7978845608028654
    square = u * u
    t = jnp.tanh(u * (c + (c * 0.044715) * square))
    half = 0.5 + 0.5 * t
    slope = half + (0.5 * u) * (1.0 - t * t) * (c + (3.0 * c * 0.044715) * square)
    return u * half, slope


def high_low(value):
    high = value.astype(BF)
    return high, (value - high.astype(F32)).astype(BF)


def two_coefs(logits, lane, experts):
    inside = (lane >= experts) & (lane < experts + 2)
    top = jnp.max(jnp.where(inside, logits, HIDE), axis=1, keepdims=True)
    e = jnp.where(inside, jnp.exp(logits - top), 0.0)
    e = e / jnp.sum(e, axis=1, keepdims=True)
    first = jnp.sum(jnp.where(lane == experts, e, 0.0), axis=1, keepdims=True)
    second = jnp.sum(jnp.where(lane == experts + 1, e, 0.0), axis=1, keepdims=True)
    return first, second


def small_back(d_small, rows, w_small_ref, small_ref, i):
    high, low = high_low(d_small)
    w_small = w_small_ref[...]
    high_t, low_t = high_low(d_small.T)

    @pl.when(i == 0)
    def _():
        small_ref[...] = jnp.zeros(small_ref.shape, F32)

    small_ref[...] += mm(high_t, rows) + mm(low_t, rows)
    return mm_t(high, w_small) + mm_t(low, w_small)


def expert_kernel(experts, half, at_ref, rows_ref, dy_ref, up_ref, down_ref, w_small_ref, *outs):
    if half:
        outs = outs[5:]
    rows_out_ref, hid_ref, dy_out_ref, deu_ref, y_ref, d_rows_ref, small_ref = outs
    rows = rows_ref[...]
    rows_out_ref[...] = rows
    up = mm(rows, up_ref[...])
    logits = mm(rows, w_small_ref[...])
    lane = lax.broadcasted_iota(jnp.int32, logits.shape, 1)
    routed = lane < experts
    top = jnp.max(jnp.where(routed, logits, HIDE), axis=1, keepdims=True)
    probs = jnp.where(routed, jnp.exp(logits - top), 0.0)
    probs = probs / jnp.sum(probs, axis=1, keepdims=True)
    own = jnp.where(lane == at_ref[2], 1.0, 0.0)
    gate = jnp.sum(probs * own, axis=1, keepdims=True)
    first, second = two_coefs(logits, lane, experts)
    weight = second * gate
    dy = dy_ref[...].reshape(rows.shape).astype(F32)
    d_y = (weight * dy).astype(BF)
    dy_out_ref[...] = d_y
    d_hidden = mm_t(d_y, down_ref[...])
    hidden, slope = gelu_both(up)
    hidden = hidden.astype(BF)
    hid_ref[...] = hidden
    d_up = (d_hidden * slope).astype(BF)
    deu_ref[...] = d_up
    y = mm(hidden, down_ref[...])
    y_ref[...] = (weight * y).astype(BF).reshape(y_ref.shape)
    along = gate * jnp.sum(dy * y, axis=1, keepdims=True)
    mixed = first * second * along
    d_small = (second * along) * (own - probs)
    d_small = jnp.where(routed, d_small, 0.0)
    d_small = d_small + jnp.where(lane == experts + 1, mixed, 0.0)
    d_small = d_small - jnp.where(lane == experts, mixed, 0.0)
    d_rows = mm_t(d_up, up_ref[...]) + small_back(d_small, rows, w_small_ref, small_ref, pl.program_id(0))
    d_rows_ref[...] = d_rows.astype(BF)


def expert_rows(at, rows, dy, w_up, w_down, w_small, experts, half, before):
    count, width = rows.shape
    hid, lanes = w_up.shape[1], w_small.shape[1]
    blk = min(512, count)
    capacity = count // dy.shape[0]
    steps = count // blk
    moving = pl.BlockSpec((blk, width), lambda i, n: (i, 0))
    slots = pl.BlockSpec((blk // capacity, capacity, width), lambda i, n: (i, half, 0))
    kept = [pl.BlockSpec((blk, size), lambda i, n: (i + half * steps, 0)) for size in (width, hid, width, hid)]
    return call(
        partial(expert_kernel, experts, half),
        "expert_rows",
        at,
        (steps,),
        [
            moving,
            slots,
            fixed((width, hid)),
            fixed((hid, width)),
            fixed((width, lanes)),
        ]
        + [pl.BlockSpec(memory_space=pl.ANY)] * (5 * half),
        kept + [slots, moving, fixed((lanes, width))],
        [like((2 * count, size), BF) for size in (width, hid, width, hid)]
        + [like(dy.shape, BF), like((count, width), BF)]
        + [like((lanes, width), F32)],
        (rows, dy, w_up, w_down, w_small, *before),
        alias={6 + k: k for k in range(5)} if half else None,
        vmem=56,
    )


def dense_kernel(experts, at_ref, rows_ref, dy_ref, in_ref, out_ref, w_small_ref, *outs):
    hid_ref, grad_ref, d_up_ref, mix_ref, db_ref, small_ref = outs
    rows = rows_ref[...]
    up = mm(rows, in_ref[...])
    logits = mm(rows, w_small_ref[...])
    lane = lax.broadcasted_iota(jnp.int32, logits.shape, 1)
    first, second = two_coefs(logits, lane, experts)
    dy = dy_ref[...].astype(F32)
    grad = (first * dy).astype(BF)
    grad_ref[...] = grad
    d_hidden = mm_t(grad, out_ref[...])
    hidden, slope = gelu_both(up)
    hidden = hidden.astype(BF)
    hid_ref[...] = hidden
    d_up = (d_hidden * slope).astype(BF)
    d_up_ref[...] = d_up
    dense = mm(hidden, out_ref[...])
    mix_ref[...] = first * dense
    mixed = first * second * jnp.sum(dy * dense, axis=1, keepdims=True)
    d_small = jnp.where(lane == experts, mixed, 0.0) - jnp.where(lane == experts + 1, mixed, 0.0)
    db_ref[...] = mm_t(d_up, in_ref[...]) + small_back(d_small, rows, w_small_ref, small_ref, pl.program_id(0))


def dense_rows(at, rows, dy, w_in, w_out, w_small, experts):
    (count, width), hid, lanes = rows.shape, w_in.shape[1], w_small.shape[1]
    blk = min(512, count)
    row_out = pl.BlockSpec((blk, width), lambda i, n: (i, 0))
    hid_out = pl.BlockSpec((blk, hid), lambda i, n: (i, 0))
    return call(
        partial(dense_kernel, experts),
        "dense_rows",
        at,
        (count // blk,),
        [row_out, row_out, fixed((width, hid)), fixed((hid, width)), fixed((width, lanes))],
        [hid_out, row_out, hid_out, row_out, row_out, fixed((lanes, width))],
        [
            like((count, hid), BF),
            like((count, width), BF),
            like((count, hid), BF),
            like((count, width), F32),
            like((count, width), F32),
            like((lanes, width), F32),
        ],
        (rows, dy, w_in, w_out, w_small),
        vmem=56,
    )


def turned(value):
    return value.astype(F32).T.astype(BF)


def dense_grads_kernel(at_ref, b_ref, d_up_ref, grad_ref, hid_ref, keep_ref, give_ref):
    width = d_up_ref.shape[1]
    first = mm(turned(b_ref[...]), d_up_ref[...]).astype(BF)
    second = mm(turned(grad_ref[...]), hid_ref[...]).astype(BF)
    half = pl.num_programs(0) // 2
    for side, ref in ((0, keep_ref), (1, give_ref)):

        @pl.when(pl.program_id(0) // half == side)
        def _():
            ref[0, :, :width] = first
            ref[0, :, width:] = second


def dense_grads(at, b, d_up, grad, hidden, parts):
    (rows, width), hid = b.shape, hidden.shape[1]
    own, half, bits = width // parts, parts // 2, parts.bit_length() - 1

    def part(q, n):
        turned_q = sum([((q // 2**k) % 2) * 2 ** (bits - 1 - k) for k in range(bits)])
        return turned_q ^ n[2]

    column = pl.BlockSpec((rows, own), lambda q, n: (0, part(q, n)))
    shape = (1, own, 2 * hid)
    return call(
        dense_grads_kernel,
        "dense_grads",
        at,
        (parts,),
        [column, fixed((rows, hid)), column, fixed((rows, hid))],
        [
            pl.BlockSpec(shape, lambda q, n: (jnp.minimum(q, half - 1), 0, 0)),
            pl.BlockSpec(shape, lambda q, n: (jnp.maximum(q - half, 0), 0, 0)),
        ],
        [like((half, own, 2 * hid), BF)] * 2,
        (b, d_up, grad, hidden),
    )


def attention_grads_kernel(at_ref, *refs):
    grads, (a_ref, w_ref, gain_ref, bias_ref, out_ref, all_s) = refs[:GROUP], refs[GROUP:]
    features = grads[0].shape[0]
    products, plain = 0.0, 0.0
    for k in range(GROUP):
        head = at_ref[0] ^ k
        rows = pl.ds(pl.multiple_of(head * features, features), features)
        grad = grads[k][...]
        weight = w_ref[head].astype(F32)
        total = mm(grad, a_ref[...])
        all_s[rows, :] = total
        each = jnp.sum(grad.astype(F32), axis=1, keepdims=True)
        products = products + jnp.sum(total * weight, axis=0, keepdims=True)
        plain = plain + jnp.sum(each * weight, axis=0, keepdims=True)
    first = GROUP * features
    row = lax.broadcasted_iota(jnp.int32, (all_s.shape[0] - first, all_s.shape[1]), 0)
    d_gain = (products - bias_ref[...] * plain) / gain_ref[...]
    all_s[first:, :] = jnp.where(row == 0, d_gain, jnp.where(row == 1, plain, 0.0))
    out_ref[...] = all_s[...].T.astype(BF)


def attention_grads(at, grads, a, w_heads, gain, bias):
    rows, width = a.shape
    features = grads[0].shape[0]
    height = GROUP * features + 128
    blk = min(256, width)
    return call(
        attention_grads_kernel,
        "attention_grads",
        at,
        (width // blk,),
        [fixed((features, rows))] * GROUP
        + [columns(rows, blk)]
        + [pl.BlockSpec((GROUP, features, blk), lambda i, n: (0, 0, i))]
        + [columns(1, blk)] * 2,
        pl.BlockSpec((blk, height), lambda i, n: (i, 0)),
        like((width, height), BF),
        (*grads, a, w_heads, gain, bias),
        scratch=[pltpu.VMEM((height, blk), F32)],
    )


def output_grads_kernel(experts, at_ref, *refs):
    o_refs, (dh_ref, sums_ref), smalls, outs, all_s = refs[:6], refs[6:8], refs[8:11], refs[11:-1], refs[-1]
    heads = GROUP * HD
    for r, piece in enumerate(in_order(at_ref[1], *[ref[...] for ref in o_refs])):
        rows = pl.ds(pl.multiple_of(((at_ref[1] + r) % 4) * heads, heads), heads)
        all_s[rows, :] = mm(piece, dh_ref[...])
    small = add_up(smalls)
    row = lax.broadcasted_iota(jnp.int32, small.shape, 0)
    for k in range(2):
        small = jnp.where(row == experts + 2 + k, sums_ref[k : k + 1, :], small)
    all_s[4 * heads :, :] = small
    both = all_s[...].T.astype(BF)
    if len(outs) == 1:
        outs[0][...] = both
    else:
        own, even = outs[0].shape[1], at_ref[2] % 2 == 0
        outs[0][0] = jnp.where(even, both[:own], both[own:])
        outs[1][0] = jnp.where(even, both[own:], both[:own])


def output_grads(at, o, dh, sums, small, experts, parts):
    quarter, width = dh.shape
    lanes = small[0].shape[0]
    height = 4 * o[0].shape[0] + lanes
    own, half, bits = width // parts, parts // 2, parts.bit_length() - 2
    blk = min(256, width)

    def slot(i, n):
        rest = i ^ (n[2] // 2)
        return sum([((rest // 2**k) % 2) * 2 ** (bits - 1 - k) for k in range(bits)]), 0, 0

    out_specs = [pl.BlockSpec((1, own, height), slot)] * 2
    out_shape = [like((half, own, height), BF)] * 2
    if blk != 2 * own:
        out_specs = [pl.BlockSpec((blk, height), lambda i, n: (i, 0))]
        out_shape = [like((width, height), BF)]
    return call(
        partial(output_grads_kernel, experts),
        "output_grads",
        at,
        (width // blk,),
        [pl.BlockSpec((o[0].shape[0], quarter), lambda i, n: (0, n[1]))] * 6
        + [columns(quarter, blk), columns(2, blk)]
        + [columns(lanes, blk)] * 3,
        out_specs,
        out_shape,
        (*o, dh, sums, *small),
        scratch=[pltpu.VMEM((height, blk), F32)],
    )


def project_kernel(at_ref, *refs):
    grads, w_ref, outs, turned_s = refs[:GROUP], refs[GROUP], refs[GROUP + 1 : -1], refs[-1]
    rows = turned_s.shape[1]
    blk = rows // 4

    @pl.when(pl.program_id(0) == 0)
    def _():
        for s in range(GROUP):
            for r in range(4):
                lanes = pl.ds(pl.multiple_of(((at_ref[1] + r) % 4) * blk, blk), blk)
                turned_s[s, r * blk : (r + 1) * blk, :] = turned(grads[s][:, lanes])

    total = 0.0
    for s in range(GROUP):
        total = total + mm(turned_s[s], w_ref[at_ref[0] ^ s])
    write_shares(at_ref[1], total, *outs)


def project_back(at, grads, w_heads):
    features, rows = grads[0].shape
    width = w_heads.shape[2]
    blk = min(256, width)
    return call(
        project_kernel,
        "project_back",
        at,
        (width // blk,),
        [fixed((features, rows))] * GROUP
        + [pl.BlockSpec((GROUP, features, blk), lambda i, n: (0, 0, i))],
        [columns(rows // 4, blk)] * 5,
        share_shapes(rows // 4, width),
        (*grads, w_heads),
        scratch=[pltpu.VMEM((GROUP, rows, features), BF)],
    )


def hop(value, *pairs):
    return lax.ppermute(value, "mp", pairs)


def rotate(value, steps):
    return hop(value, *[(s, (s + steps) % 4) for s in range(4)])


def gather_near(own):
    right = hop(own, (0, 1), (1, 2), (2, 3))
    left = hop(own, (1, 0), (2, 1), (3, 2))
    return own, right, left, hop(own, (0, 3), (3, 0))


def gather_far(near):
    _, right, left, _ = near
    return *near, hop(right, (1, 2), (2, 3)), hop(left, (1, 0), (2, 1))


def gather_pieces(own):
    return gather_far(gather_near(own))


def scatter_far(shares):
    _, _, two, _, end = shares
    return hop(two, (2, 1), (3, 2)), hop(two, (0, 1), (1, 2)), hop(end, (0, 3), (3, 0))


def scatter_near(shares, came):
    own, one, _, three, _ = shares
    from_right, from_left, from_end = came
    three = (three.astype(F32) + from_right.astype(F32)).astype(BF)
    one = (one.astype(F32) + from_left.astype(F32)).astype(BF)
    return own, hop(three, (1, 0), (2, 1), (3, 2)), hop(one, (0, 1), (1, 2), (2, 3)), from_end


def group_swap(value, s):
    count = lax.axis_size("dp")
    return lax.ppermute(value, "dp", [(t, t ^ s) for t in range(count)])


def expert_swap(value, experts):
    wide = value.reshape(experts, value.shape[0] // experts, value.shape[1])
    return lax.all_to_all(wide, "dp", 0, 0, tiled=True).reshape(value.shape)


def roll_rows(value, start):
    twice = jnp.concatenate([value, value], axis=0)
    return lax.dynamic_slice_in_dim(twice, start, value.shape[0], 0)


def add_halves(keep, came):
    return (keep.astype(F32) + came.astype(F32)).astype(BF)


def body(
    tokens,
    cotangent,
    ln_gains,
    ln_biases,
    w_qkv,
    w_o,
    w_in,
    w_out,
    w_router,
    w_coef,
    w_up,
    w_down,
    routes,
    long_group,
):
    rows, width = tokens.shape
    dps = lax.axis_size("dp")
    mine, position = lax.axis_index("mp"), lax.axis_index("dp")
    quarter = rows // 4
    start = mine * quarter
    heads_loc = w_qkv.shape[2] // HD
    hid = w_in.shape[1]
    experts = w_router.shape[1]
    capacity = max(2, 2 * rows // experts)
    half = capacity // 2
    barrier = lax.optimization_barrier
    first_len = lax.dynamic_index_in_dim(long_group, position // GROUP, 0, keepdims=False)
    at = jnp.stack([position % GROUP, mine, position, first_len]).astype(jnp.int32)
    gains = [ln_gains[0:1], ln_gains[1:2]]
    biases = [ln_biases[0:1], ln_biases[1:2]]
    w_o_all = lax.all_gather(w_o, "mp", axis=0, tiled=True)

    w_heads = w_qkv.reshape(width, 3, heads_loc, HD).transpose(2, 1, 3, 0)
    w_heads = w_heads.reshape(heads_loc, 3 * HD, width)
    a_r, *qkv = project(at, tokens, gains[0], biases[0], w_heads)
    qkv = [qkv[0]] + [group_swap(qkv[s], s) for s in (1, 2, 3)]

    route = roll_rows(routes, start)[:, 0]
    picked = (route[:, None] == jnp.arange(experts, dtype=jnp.int32)[None, :]).astype(jnp.int32)
    slot = jnp.sum((jnp.cumsum(picked, axis=0) - picked) * picked, axis=1)
    dy_b = roll_rows(cotangent, start)
    full = route * capacity + slot
    send_dy = dispatch(at, full[None, :], dy_b, experts * capacity)
    *qkv, send_dy = barrier((*qkv, send_dy))
    in_half = [slot < half, slot >= half]
    dests = [
        jnp.where(in_half[k], route * half + slot - k * half, -1).astype(jnp.int32) for k in (0, 1)
    ]

    *o_t, lse = attend(at, qkv)
    *o_t, w_o_all = barrier((*o_t, w_o_all))
    o_heads = [o_t[0]] + [group_swap(o_t[s], s) for s in (1, 2, 3)]
    lanes = -(-(experts + 2) // 128) * 128
    w_small = jnp.concatenate(
        [w_router, w_coef, jnp.zeros((width, lanes - experts - 2), BF)], axis=1
    )
    *o_heads, send_dy, w_small = barrier((*o_heads, send_dy, w_small))
    got_dy = expert_swap(send_dy, experts).reshape(experts, capacity, width)
    o_pieces = gather_pieces(stack(at, o_heads))
    h, b_r = mid(at, o_pieces, w_o_all, tokens, gains[1], biases[1])

    send_0 = dispatch(at, dests[0][None, :], b_r, experts * half)
    send_0, got_dy = barrier((send_0, got_dy))
    got_0 = expert_swap(send_0, experts)
    send_1 = dispatch(at, dests[1][None, :], b_r, experts * half)
    b_r, send_1 = barrier((b_r, send_1))
    hidden, dense_grad, d_up, mix_base, db_base, small_t = dense_rows(
        at, b_r, dy_b, w_in, w_out, w_small, experts
    )
    send_1, got_0, db_base = barrier((send_1, got_0, db_base))
    got_1 = expert_swap(send_1, experts)

    *kept, d_rows_0, small_0 = expert_rows(
        at, got_0, got_dy, w_up[0], w_down[0], w_small, experts, 0, ()
    )
    back_0 = expert_swap(d_rows_0, experts)
    *kept, d_rows_1, small_1 = expert_rows(
        at, got_1, got_dy, w_up[0], w_down[0], w_small, experts, 1, kept
    )
    got, hidden_e, d_y, d_eu, back_y = kept
    back_1 = expert_swap(d_rows_1, experts)
    d_rows_1, b_r = barrier((d_rows_1, b_r))
    halving = width == dps * 128
    if halving:
        grads = dense_grads(at, b_r, d_up, dense_grad, hidden, dps)
    else:
        grads = [ein("td,tf->df", b_r, d_up).astype(BF), ein("td,tf->df", dense_grad, hidden).astype(BF)]
    back_0, back_1, back_y, *grads = barrier((back_0, back_1, back_y, *grads))

    dest_cols = [dest[:, None] for dest in dests]
    tok_y = expert_swap(back_y.reshape(experts * capacity, width), experts)
    shares = combine(at, dest_cols, [back_0, back_1], db_base)
    far = scatter_far(shares)
    *far, g_0, g_1 = barrier((*far, *grads))
    grads = [g_0, g_1]
    shares = scatter_near(shares, far)

    mix = combine(at, [full[:, None]], [tok_y], mix_base, h)
    *shares, mix = barrier((*shares, mix))
    output = lax.psum(mix, "mp")
    dh, dh_r, sums_2, *do_q = mid_back(at, shares, w_o_all, h, dy_b, gains[1])
    do_q = [do_q[0]] + [rotate(do_q[r], -r) for r in (1, 2, 3)]
    do_heads = unsplit(at, do_q)
    do_t = [do_heads[0]] + [group_swap(do_heads[s], s) for s in (1, 2, 3)]
    grads_o = output_grads(at, o_pieces, dh_r, sums_2, (small_0, small_1, small_t), experts, dps)
    if halving:
        pairs = [grads, grads_o]
        came_1 = [group_swap(pair[1], 1) for pair in pairs]
        half = dps // 4
        give = [add_halves(pair[0][half:], came[half:]) for pair, came in zip(pairs, came_1)]
        tied = barrier((*do_t, *give))
        do_t, give = tied[:4], tied[4:]
        came_2 = [group_swap(value, 2) for value in give]
    d_qkv = attend_back(at, qkv, do_t, o_t, lse)
    if halving:
        keep = [add_halves(pair[0][:half], came[:half]) for pair, came in zip(pairs, came_1)]
        tied = barrier((*d_qkv, *came_2, *keep))
        d_qkv, came_2, keep = tied[:4], tied[4:6], tied[6:]
        done = []
        for value, came in zip(keep, came_2):
            value, bit = add_halves(value, came), 4
            while bit < dps:
                half = value.shape[0] // 2
                value = add_halves(value[:half], group_swap(value[half:], bit))
                bit *= 2
            done.append(value[0])
        grads, grads_o = [done[0][:, :hid], done[0][:, hid:]], done[1]
    else:
        *grads, grads_o = [
            lax.psum_scatter(value, "dp", scatter_dimension=0, tiled=True) for value in (*grads, *grads_o)
        ]

    d_own, got, hidden_e, d_y, d_eu = barrier((d_qkv[0], got, hidden_e, d_y, d_eu))
    d_qkv = [d_own] + [group_swap(d_qkv[s], s) for s in (1, 2, 3)]
    grad_down = ein("rf,rd->fd", hidden_e, d_y)
    *d_qkv, grad_down = barrier((*d_qkv, grad_down))
    shares = project_back(at, d_qkv, w_heads)
    far = scatter_far(shares)
    grads_a = attention_grads(at, d_qkv, a_r, w_heads, gains[0], biases[0])
    grad_up = ein("rd,rf->df", got, d_eu)
    grads_a, output, grad_up, *far = barrier((grads_a, output, grad_up, *far))
    grads_a = lax.psum_scatter(grads_a, "dp", scatter_dimension=0, tiled=True).T
    shares = scatter_near(shares, far)
    grad_q = first_back(at, shares, tokens, dh, gains[0])
    grad_tokens = join(at, gather_pieces(grad_q))

    own, heads = width // dps, heads_loc * HD
    grad_qkv = grads_a[: 3 * heads].astype(F32).reshape(heads_loc, 3, HD, own).transpose(3, 1, 0, 2)
    grad_qkv = grad_qkv.reshape(own, 3, heads)
    grad_in = grads[0].astype(F32)
    grad_out = grads[1].astype(F32).T
    def over_mp(value):
        return jnp.sum(lax.all_to_all(value, "mp", 0, 0, tiled=True).astype(F32), axis=0)

    grads_o = grads_o.T
    small = jnp.broadcast_to(grads_o[4 * heads :], (4, lanes, own))
    rest = over_mp(jnp.concatenate([grads_o[: 4 * heads].reshape(4, heads, own), small], axis=1))
    grad_o, small = rest[:heads], rest[heads:]
    first = over_mp(jnp.broadcast_to(grads_a[3 * heads : 3 * heads + 16], (4, 16, own)))
    small_out = small[: experts + 2].T
    return (
        output,
        grad_tokens,
        jnp.stack([first[0], small[experts + 2]]),
        jnp.stack([first[1], small[experts + 3]]),
        grad_qkv,
        grad_o,
        grad_in,
        grad_out,
        small_out[:, :experts],
        small_out[:, experts:],
        grad_up[None],
        grad_down[None],
    )


def solution(mesh):
    in_specs = (
        P("dp", None),
        P("dp", None),
        P(),
        P(),
        P(None, None, "mp"),
        P("mp", None),
        P(None, "mp"),
        P("mp", None),
        P(),
        P(),
        P("dp", None, "mp"),
        P("dp", "mp", None),
        P("dp", None),
        P(),
    )
    out_specs = (
        P("dp", None),
        P("dp", None),
        P(None, "dp"),
        P(None, "dp"),
        P("dp", None, "mp"),
        P("mp", "dp"),
        P("dp", "mp"),
        P("mp", "dp"),
        P("dp", None),
        P("dp", None),
        P("dp", None, "mp"),
        P("dp", "mp", None),
    )
    return jax.shard_map(body, mesh=mesh, in_specs=in_specs, out_specs=out_specs, check_vma=False)
```

```python
from functools import partial

import jax
import jax.numpy as jnp
from jax import lax
from jax.experimental import pallas as pl
from jax.experimental.pallas import tpu as pltpu
from jax.sharding import PartitionSpec as P

HD = 64
GROUP = 4
EPS = 1e-05
LOG2E = 1.4426950408889634
SCALE2 = 0.125 * LOG2E
HIDE = -1e30
BF = jnp.bfloat16
F32 = jnp.float32
LIGHT = pl.CostEstimate(flops=1 << 20, bytes_accessed=1 << 20, transcendentals=0)


def mm(a, b):
    return jnp.dot(a, b, preferred_element_type=F32)


def ein(spec, a, b):
    return jnp.einsum(spec, a, b, preferred_element_type=F32)


def call(kernel, name, prefetch, grid, in_specs, out_specs, out_shape, args, scratch=(), alias=None, vmem=48):
    return pl.pallas_call(
        kernel,
        grid_spec=pltpu.PrefetchScalarGridSpec(
            num_scalar_prefetch=1,
            grid=grid,
            in_specs=in_specs,
            out_specs=out_specs,
            scratch_shapes=list(scratch),
        ),
        out_shape=out_shape,
        input_output_aliases=alias or {},
        compiler_params=pltpu.CompilerParams(vmem_limit_bytes=vmem * 2**20),
        cost_estimate=LIGHT,
        name=name,
    )(prefetch, *args)


def fixed(shape):
    zeros = (0,) * len(shape)
    return pl.BlockSpec(shape, lambda *_: zeros)


def like(shape, dtype):
    return jax.ShapeDtypeStruct(shape, dtype)


def normalize(v):
    mean = jnp.mean(v, axis=-1, keepdims=True)
    centred = v - mean
    scale = lax.rsqrt(jnp.mean(centred * centred, axis=-1, keepdims=True) + EPS)
    return centred * scale, scale


def norm_back(grad, gain, normal, scale):
    g = grad * gain
    along = jnp.mean(g * normal, axis=-1, keepdims=True)
    return scale * (g - jnp.mean(g, axis=-1, keepdims=True) - normal * along)


def qkv_kernel(at_ref, x_ref, gain_ref, bias_ref, w_ref, a_ref, *outs):
    normal, _ = normalize(x_ref[...].astype(F32))
    a = (normal * gain_ref[...] + bias_ref[...]).astype(BF)
    a_ref[...] = a
    for s in range(GROUP):
        outs[s][...] = mm_t(w_ref[at_ref[0] ^ s], a).astype(BF)


def project(at, tokens, gain, bias, w_heads):
    rows, width = tokens.shape
    features = w_heads.shape[1]
    blk = min(256, rows)
    moving = pl.BlockSpec((blk, width), lambda i, n: (i, 0))
    return call(
        qkv_kernel,
        "project",
        at,
        (rows // blk,),
        [moving, fixed((1, width)), fixed((1, width)), fixed(w_heads.shape)],
        [moving] + [pl.BlockSpec((features, blk), lambda i, n: (0, i))] * GROUP,
        [like((rows, width), BF)] + [like((features, rows), BF)] * GROUP,
        (tokens, gain, bias, w_heads),
    )


def fill_keys(k_s, place, keys, first_len, blk):
    rows = place * blk + lax.broadcasted_iota(jnp.int32, (blk, 128), 0)
    lane = lax.broadcasted_iota(jnp.int32, (blk, 128), 1)
    wide = jnp.concatenate([keys.astype(F32).T, jnp.zeros((blk, 128 - HD), F32)], axis=1)
    wide = jnp.where((lane == HD) & (rows < first_len), HIDE, wide)
    k_s[pl.ds(place * blk, blk), :] = wide.astype(BF)


def wide_query(query, place, first_len, blk):
    cols = place * blk + lax.broadcasted_iota(jnp.int32, (128 - HD, blk), 1)
    sub = lax.broadcasted_iota(jnp.int32, (128 - HD, blk), 0)
    extra = jnp.where((sub == 0) & (cols >= first_len), 1.0, 0.0)
    return jnp.concatenate([query, extra.astype(BF)], axis=0)


def causal(blk):
    keys = lax.broadcasted_iota(jnp.int32, (blk, blk), 0)
    queries = lax.broadcasted_iota(jnp.int32, (blk, blk), 1)
    return keys <= queries


def attend_kernel(blk, per, at_ref, *refs):
    qkv_refs, o_refs = refs[:GROUP], refs[GROUP : 2 * GROUP]
    lse_ref, k_s, qkv_s = refs[2 * GROUP :]
    i = pl.program_id(0)
    place, first_len = at_ref[0], at_ref[3]

    @pl.when(i == 0)
    def _():
        for s in range(GROUP):
            qkv_s[place ^ s] = qkv_refs[s][...]

    def part(which, j):
        return qkv_s[j // per, HD * which : HD * (which + 1), pl.ds((j % per) * blk, blk)]

    fill_keys(k_s, i, part(1, i), first_len, blk)
    query = wide_query(part(0, i), i, first_len, blk)

    def scores(j):
        return mm(k_s[pl.ds(pl.multiple_of(j * blk, blk), blk), :], query)

    s = jnp.where(causal(blk), scores(i), HIDE)
    top = jnp.max(s, axis=0, keepdims=True)
    p = jnp.exp2((s - top) * SCALE2)
    total = jnp.sum(p, axis=0, keepdims=True)
    acc = mm(part(2, i), p.astype(BF))

    def steps(blocks, carry):
        top, total, acc = carry
        s = [scores(j) for j in blocks]
        new = top
        for one in s:
            new = jnp.maximum(new, jnp.max(one, axis=0, keepdims=True))
        keep = jnp.exp2((top - new) * SCALE2)
        total, acc = total * keep, acc * keep
        for j, one in zip(blocks, s):
            p = jnp.exp2((one - new) * SCALE2)
            total = total + jnp.sum(p, axis=0, keepdims=True)
            acc = acc + mm(part(2, j), p.astype(BF))
        return new, total, acc

    low = jnp.where(i * blk >= first_len, first_len // blk, 0)
    pairs = (i - low) // 2
    carry = lax.fori_loop(
        0, pairs, lambda t, c: steps([low + 2 * t, low + 2 * t + 1], c), (top, total, acc)
    )
    top, total, acc = lax.fori_loop(low + 2 * pairs, i, lambda j, c: steps([j], c), carry)
    out = (acc / total).astype(BF)
    for s in range(GROUP):

        @pl.when((i // per) ^ place == s)
        def _():
            o_refs[s][:, pl.ds((i % per) * blk, blk)] = out

    lse_ref[0] = top * SCALE2 + jnp.log2(total)


def attend(at, qkv):
    features, rows = qkv[0].shape
    blk = min(512, rows)
    per = rows // blk
    count = GROUP * per
    return call(
        partial(attend_kernel, blk, per),
        "attend",
        at,
        (count,),
        [fixed((features, rows))] * GROUP,
        [fixed((HD, rows))] * GROUP + [pl.BlockSpec((1, 1, blk), lambda i, n: (i, 0, 0))],
        [like((HD, rows), BF)] * GROUP + [like((count, 1, blk), F32)],
        qkv,
        scratch=[pltpu.VMEM((GROUP * rows, 128), BF), pltpu.VMEM((GROUP, features, rows), BF)],
    )


def back_kernel(blk, per, count, at_ref, *refs):
    qkv_refs, do_refs, o_refs = refs[:GROUP], refs[GROUP : 2 * GROUP], refs[2 * GROUP : 3 * GROUP]
    lse_ref, refs = refs[3 * GROUP], refs[3 * GROUP + 1 :]
    out_refs, refs = refs[:GROUP], refs[GROUP:]
    dq_ref, out_ref, k_s, kt_s, v_s, wide_s, dot_s, both_s, delta_s, acc_s = refs
    j = pl.program_id(0)
    place, first_len = at_ref[0], at_ref[3]

    @pl.when(j == 0)
    def _():
        dq_ref[...] = jnp.zeros(dq_ref.shape, F32)
        zero = jnp.zeros((blk, HD), F32)
        for s in range(GROUP):
            for sub in range(per):
                i = (place ^ s) * per + sub
                at = pl.ds(pl.multiple_of(i * blk, blk), blk)
                cut = slice(sub * blk, (sub + 1) * blk)
                query = qkv_refs[s][0:HD, cut]
                keys = qkv_refs[s][HD : 2 * HD, cut]
                grad = do_refs[s][:, cut]
                fill_keys(k_s, i, keys, first_len, blk)
                kt_s[:, at] = keys
                dot_s[:, at] = grad
                wide_s[:, at] = wide_query(query, i, first_len, blk)
                grad = grad.astype(F32)
                values = qkv_refs[s][2 * HD :, cut].astype(F32)
                v_s[at, :] = jnp.concatenate([values.T, zero], axis=1).astype(BF)
                both_s[0, at, :] = jnp.concatenate([grad.T, zero], axis=1).astype(BF)
                both_s[1, at, :] = jnp.concatenate([zero, query.astype(F32).T], axis=1).astype(BF)
                held = o_refs[s][:, cut].astype(F32)
                delta_s[i] = jnp.sum(held * grad, axis=0, keepdims=True)

    here = pl.ds(pl.multiple_of(j * blk, blk), blk)
    keys_t = kt_s[:, here]
    values = v_s[here, 0:HD]

    def pair(i, diagonal):
        at = pl.ds(pl.multiple_of(i * blk, blk), blk)
        s = mm(k_s[here, :], wide_s[:, at])
        p = jnp.exp2(s * SCALE2 - lse_ref[i])
        if diagonal:
            p = jnp.where(causal(blk), p, 0.0)
        dp = mm(values, dot_s[:, at])
        ds = (p * (dp - delta_s[i])).astype(BF)
        return mm(p.astype(BF), both_s[0, at, :]) + mm(ds, both_s[1, at, :]), mm(keys_t, ds)

    acc_s[...], dq = pair(j, True)
    dq_ref[:, here] += dq

    def step_two(t, carry):
        i = j + 1 + 2 * t
        (kv_0, dq_0), (kv_1, dq_1) = pair(i, False), pair(i + 1, False)
        acc_s[...] += kv_0 + kv_1
        at = pl.ds(pl.multiple_of(i * blk, blk), 2 * blk)
        dq_ref[:, at] += jnp.concatenate([dq_0, dq_1], axis=1)
        return carry

    def step(i, carry):
        kv, dq = pair(i, False)
        acc_s[...] += kv
        dq_ref[:, pl.ds(pl.multiple_of(i * blk, blk), blk)] += dq
        return carry

    high = jnp.where((j + 1) * blk <= first_len, (first_len + blk - 1) // blk, count)
    pairs = (high - j - 1) // 2
    lax.fori_loop(0, pairs, step_two, 0)
    lax.fori_loop(j + 1 + 2 * pairs, high, step, 0)
    both = acc_s[...].T
    out_ref[0:HD, :] = (dq_ref[:, here] * 0.125).astype(BF)
    out_ref[HD : 2 * HD, :] = (both[HD:, :] * 0.125).astype(BF)
    out_ref[2 * HD :, :] = both[:HD, :].astype(BF)
    for s in range(GROUP):

        @pl.when((j // per) ^ place == s)
        def _():
            out_refs[s][:, pl.ds(pl.multiple_of((j % per) * blk, blk), blk)] = out_ref[...]


def attend_back(at, qkv, do, o, lse):
    features, rows = qkv[0].shape
    blk = min(512, rows)
    per = rows // blk
    count = GROUP * per
    return call(
        partial(back_kernel, blk, per, count),
        "attend_back",
        at,
        (count,),
        [fixed((features, rows))] * GROUP
        + [fixed((HD, rows))] * (2 * GROUP)
        + [fixed((count, 1, blk))],
        [fixed((features, rows))] * GROUP,
        [like((features, rows), BF)] * GROUP,
        (*qkv, *do, *o, lse),
        scratch=[
            pltpu.VMEM((HD, GROUP * rows), F32),
            pltpu.VMEM((features, blk), BF),
            pltpu.VMEM((GROUP * rows, 128), BF),
            pltpu.VMEM((HD, GROUP * rows), BF),
            pltpu.VMEM((GROUP * rows, 128), BF),
            pltpu.VMEM((128, GROUP * rows), BF),
            pltpu.VMEM((HD, GROUP * rows), BF),
            pltpu.VMEM((2, GROUP * rows, 128), BF),
            pltpu.VMEM((count, 1, blk), F32),
            pltpu.VMEM((blk, 128), F32),
        ],
        vmem=36,
    )


def stack_kernel(at_ref, *refs):
    ins, out_ref = refs[:GROUP], refs[GROUP]
    for s in range(GROUP):
        head = pl.ds(pl.multiple_of((at_ref[0] ^ s) * HD, HD), HD)
        out_ref[head, :] = ins[s][...]


def stack(at, heads):
    rows = heads[0].shape[1]
    return call(
        stack_kernel,
        "stack",
        at,
        (1,),
        [fixed((HD, rows))] * GROUP,
        fixed((GROUP * HD, rows)),
        like((GROUP * HD, rows), BF),
        heads,
    )


def unsplit_kernel(at_ref, *refs):
    ins, outs = refs[:4], refs[4:]
    cols = ins[0].shape[1]
    for r in range(4):
        lanes = pl.ds(pl.multiple_of(((at_ref[1] + r) % 4) * cols, cols), cols)
        for s in range(GROUP):
            head = pl.ds(pl.multiple_of((at_ref[0] ^ s) * HD, HD), HD)
            outs[s][:, lanes] = ins[r][head, :]


def unsplit(at, pieces):
    shape = (HD, 4 * pieces[0].shape[1])
    return call(
        unsplit_kernel,
        "unsplit",
        at,
        (1,),
        [fixed(pieces[0].shape)] * 4,
        [fixed(shape)] * GROUP,
        [like(shape, BF)] * GROUP,
        pieces,
    )


def heads_of(mine, r, features):
    return pl.ds(pl.multiple_of(((mine + 4 - r) % 4) * features, features), features)


def mid_kernel(at_ref, *refs):
    pieces, (w_ref, x_ref, gain_ref, bias_ref, h_ref, b_ref) = refs[:6], refs[6:]
    h = x_ref[...].astype(F32)
    for r, piece in enumerate(in_order(at_ref[1], *[ref[...] for ref in pieces])):
        rows = heads_of(at_ref[1], 4 - r, piece.shape[0])
        h = h + mm(turned(piece), w_ref[rows, :])

    @pl.when(pl.program_id(0) == 0)
    def _():
        h_ref[...] = h

    normal, _ = normalize(h)
    b_ref[...] = (normal * gain_ref[...] + bias_ref[...]).astype(BF)


def mid(at, pieces, w_o, tokens, gain, bias):
    features, rows = pieces[0].shape
    width, quarter = tokens.shape[1], rows // 4
    return call(
        mid_kernel,
        "mid",
        at,
        (4,),
        [pl.BlockSpec((features, quarter), lambda q, n: (0, (n[1] + q) % 4))] * 6
        + [fixed(w_o.shape)]
        + [pl.BlockSpec((quarter, width), lambda q, n: ((n[1] + q) % 4, 0))]
        + [fixed((1, width))] * 2,
        [fixed((quarter, width)), pl.BlockSpec((quarter, width), lambda q, n: (q, 0))],
        [like((quarter, width), F32), like((rows, width), BF)],
        (*pieces, w_o, tokens, gain, bias),
    )


def add_up(refs):
    total = refs[0][...]
    for ref in refs[1:]:
        total = total + ref[...].astype(F32)
    return total


def mid_back_kernel(at_ref, *refs):
    shares, (w_ref, h_ref, dy_ref, gain_ref, dh_ref, low_ref, sums_ref) = refs[:4], refs[4:11]
    do_refs = refs[11:]
    db = add_up(shares)
    normal, scale = normalize(h_ref[...])
    dh = dy_ref[...].astype(F32) + norm_back(db, gain_ref[...], normal, scale)
    dh_ref[...] = dh
    low = dh.astype(BF)
    low_ref[...] = low
    sums_ref[0:1, :] = jnp.sum(db * normal, axis=0, keepdims=True)
    sums_ref[1:2, :] = jnp.sum(db, axis=0, keepdims=True)
    for r in range(4):
        rows = heads_of(at_ref[1], r, do_refs[r].shape[0])
        do_refs[r][...] = mm_t(w_ref[rows, :], low).astype(BF)


def mid_back(at, shares, w_o, h, dy, gain):
    quarter, width = h.shape
    whole = fixed((quarter, width))
    piece = (w_o.shape[0] // 4, quarter)
    return call(
        mid_back_kernel,
        "mid_back",
        at,
        (1,),
        [whole] * 4 + [fixed(w_o.shape), whole, whole, fixed((1, width))],
        [whole] * 2 + [fixed((2, width))] + [fixed(piece)] * 4,
        [like((quarter, width), F32), like((quarter, width), BF), like((2, width), F32)]
        + [like(piece, BF)] * 4,
        (*shares, w_o, h, dy, gain),
    )


def first_back_kernel(at_ref, *refs):
    shares = refs[:4]
    x_ref, dh_ref, gain_ref, out_ref = refs[4:]
    d_a = add_up(shares)
    normal, scale = normalize(x_ref[...].astype(F32))
    out_ref[...] = (dh_ref[...] + norm_back(d_a, gain_ref[...], normal, scale)).astype(BF)


def first_back(at, shares, tokens, dh, gain):
    quarter, width = dh.shape
    return call(
        first_back_kernel,
        "first_back",
        at,
        (1,),
        [fixed((quarter, width))] * 4
        + [pl.BlockSpec((quarter, width), lambda i, n: (n[1], 0))]
        + [fixed((quarter, width)), fixed((1, width))],
        fixed((quarter, width)),
        like((quarter, width), BF),
        (*shares, tokens, dh, gain),
    )


def in_order(mine, own, right, left, far, right_two, left_two):
    one = jnp.where(mine == 3, far, left)
    two = jnp.where(mine < 2, left_two, right_two)
    three = jnp.where(mine == 0, far, right)
    return own, one, two, three


def one_hot(slots, dest):
    return jnp.where(slots == dest, 1.0, 0.0).astype(BF)


def dispatch_kernel(at_ref, dest_ref, rows_ref, out_ref, spread_s):
    blk, rows = min(256, spread_s.shape[0]), dest_ref.shape[1]

    @pl.when(pl.program_id(0) == 0)
    def _():
        slot = lax.broadcasted_iota(jnp.int32, (blk, rows), 0)
        for start in range(0, spread_s.shape[0], blk):
            spread_s[start : start + blk, :] = one_hot(slot + start, dest_ref[...])

    out_ref[...] = mm(spread_s[...], rows_ref[...]).astype(BF)


def columns(rows, width):
    return pl.BlockSpec((rows, width), lambda i, n: (0, i))


def dispatch(at, dest_row, values, slots):
    rows, width = values.shape
    blk = min(256, width)
    return call(
        dispatch_kernel,
        "dispatch",
        at,
        (width // blk,),
        [fixed((1, rows)), columns(rows, blk)],
        columns(slots, blk),
        like((slots, width), BF),
        (dest_row, values),
        scratch=[pltpu.VMEM((slots, rows), BF)],
    )


def join_kernel(at_ref, *refs):
    pieces, out_ref = refs[:6], refs[6]
    r = pl.program_id(0)
    for place, piece in enumerate(in_order(at_ref[1], *[ref[...] for ref in pieces])):

        @pl.when(r == place)
        def _():
            out_ref[...] = piece


def join(at, pieces):
    each, width = pieces[0].shape
    return call(
        join_kernel,
        "join",
        at,
        (4,),
        [fixed((each, width))] * 6,
        pl.BlockSpec((each, width), lambda r, n: ((n[1] + r) % 4, 0)),
        like((4 * each, width), BF),
        pieces,
    )


def write_shares(mine, total, own_ref, one_ref, two_ref, three_ref, end_ref):
    rows = own_ref.shape[0]
    own_ref[...] = total[:rows]
    one, two, three = [total[r * rows : (r + 1) * rows].astype(BF) for r in (1, 2, 3)]
    one_ref[...] = one
    two_ref[...] = two
    three_ref[...] = three
    end_ref[...] = jnp.where(mine == 0, three, one)


def share_shapes(rows, width):
    return [like((rows, width), F32)] + [like((rows, width), BF)] * 4


def combine_kernel(count, whole, at_ref, *refs):
    dests, backs = refs[:count], refs[count : 2 * count]
    base_ref, refs, pick_s = refs[2 * count], refs[2 * count + 1 : -1], refs[-1]
    rows, slots = base_ref.shape[0], backs[0].shape[0]
    blk = rows // 4

    @pl.when(pl.program_id(0) == 0)
    def _():
        lane = lax.broadcasted_iota(jnp.int32, (blk, slots), 1)
        for k in range(count):
            for start in range(0, rows, blk):
                dest = dests[k][start : start + blk, :]
                pick_s[start : start + blk, k * slots : (k + 1) * slots] = one_hot(lane, dest)

    total = base_ref[...].astype(F32)
    for k in range(count):
        total = total + mm(pick_s[:, k * slots : (k + 1) * slots], backs[k][...])
    mine = at_ref[1]
    if whole:
        h_ref, out_ref = refs
        for r in range(4):
            part = total[r * blk : (r + 1) * blk]
            if r == 0:
                part = part + h_ref[...]
            place = pl.ds(pl.multiple_of(((mine + r) % 4) * blk, blk), blk)
            out_ref[place, :] = part.astype(BF)
    else:
        write_shares(mine, total, *refs)


def combine(at, dests, backs, base, h=None):
    count, (slots, width), rows = len(backs), backs[0].shape, base.shape[0]
    blk = min(256, width)
    whole = h is not None
    quarter = columns(rows // 4, blk)
    return call(
        partial(combine_kernel, count, whole),
        "combine",
        at,
        (width // blk,),
        [fixed((rows, 1))] * count
        + [columns(slots, blk)] * count
        + [columns(rows, blk)]
        + [quarter] * whole,
        columns(rows, blk) if whole else [quarter] * 5,
        like(base.shape, BF) if whole else share_shapes(rows // 4, width),
        (*dests, *backs, base) + ((h,) if whole else ()),
        scratch=[pltpu.VMEM((rows, count * slots), BF)],
    )


def mm_t(a, b):
    return lax.dot_general(a, b, (((1,), (1,)), ((), ())), preferred_element_type=F32)


def gelu_both(u):
    c = 0.7978845608028654
    square = u * u
    t = jnp.tanh(u * (c + (c * 0.044715) * square))
    half = 0.5 + 0.5 * t
    slope = half + (0.5 * u) * (1.0 - t * t) * (c + (3.0 * c * 0.044715) * square)
    return u * half, slope


def high_low(value):
    high = value.astype(BF)
    return high, (value - high.astype(F32)).astype(BF)


def two_coefs(logits, lane, experts):
    inside = (lane >= experts) & (lane < experts + 2)
    top = jnp.max(jnp.where(inside, logits, HIDE), axis=1, keepdims=True)
    e = jnp.where(inside, jnp.exp(logits - top), 0.0)
    e = e / jnp.sum(e, axis=1, keepdims=True)
    first = jnp.sum(jnp.where(lane == experts, e, 0.0), axis=1, keepdims=True)
    second = jnp.sum(jnp.where(lane == experts + 1, e, 0.0), axis=1, keepdims=True)
    return first, second


def small_back(d_small, rows, w_small_ref, small_ref, i):
    high, low = high_low(d_small)
    w_small = w_small_ref[...]
    high_t, low_t = high_low(d_small.T)

    @pl.when(i == 0)
    def _():
        small_ref[...] = jnp.zeros(small_ref.shape, F32)

    small_ref[...] += mm(high_t, rows) + mm(low_t, rows)
    return mm_t(high, w_small) + mm_t(low, w_small)


def expert_kernel(experts, half, at_ref, rows_ref, dy_ref, up_ref, down_ref, w_small_ref, *outs):
    if half:
        outs = outs[5:]
    rows_out_ref, hid_ref, dy_out_ref, deu_ref, y_ref, d_rows_ref, small_ref = outs
    rows = rows_ref[...]
    rows_out_ref[...] = rows
    up = mm(rows, up_ref[...])
    logits = mm(rows, w_small_ref[...])
    lane = lax.broadcasted_iota(jnp.int32, logits.shape, 1)
    routed = lane < experts
    top = jnp.max(jnp.where(routed, logits, HIDE), axis=1, keepdims=True)
    probs = jnp.where(routed, jnp.exp(logits - top), 0.0)
    probs = probs / jnp.sum(probs, axis=1, keepdims=True)
    own = jnp.where(lane == at_ref[2], 1.0, 0.0)
    gate = jnp.sum(probs * own, axis=1, keepdims=True)
    first, second = two_coefs(logits, lane, experts)
    weight = second * gate
    dy = dy_ref[...].reshape(rows.shape).astype(F32)
    d_y = (weight * dy).astype(BF)
    dy_out_ref[...] = d_y
    d_hidden = mm_t(d_y, down_ref[...])
    hidden, slope = gelu_both(up)
    hidden = hidden.astype(BF)
    hid_ref[...] = hidden
    d_up = (d_hidden * slope).astype(BF)
    deu_ref[...] = d_up
    y = mm(hidden, down_ref[...])
    y_ref[...] = (weight * y).astype(BF).reshape(y_ref.shape)
    along = gate * jnp.sum(dy * y, axis=1, keepdims=True)
    mixed = first * second * along
    d_small = (second * along) * (own - probs)
    d_small = jnp.where(routed, d_small, 0.0)
    d_small = d_small + jnp.where(lane == experts + 1, mixed, 0.0)
    d_small = d_small - jnp.where(lane == experts, mixed, 0.0)
    d_rows = mm_t(d_up, up_ref[...]) + small_back(d_small, rows, w_small_ref, small_ref, pl.program_id(0))
    d_rows_ref[...] = d_rows.astype(BF)


def expert_rows(at, rows, dy, w_up, w_down, w_small, experts, half, before):
    count, width = rows.shape
    hid, lanes = w_up.shape[1], w_small.shape[1]
    blk = min(512, count)
    capacity = count // dy.shape[0]
    steps = count // blk
    moving = pl.BlockSpec((blk, width), lambda i, n: (i, 0))
    slots = pl.BlockSpec((blk // capacity, capacity, width), lambda i, n: (i, half, 0))
    kept = [pl.BlockSpec((blk, size), lambda i, n: (i + half * steps, 0)) for size in (width, hid, width, hid)]
    return call(
        partial(expert_kernel, experts, half),
        "expert_rows",
        at,
        (steps,),
        [
            moving,
            slots,
            fixed((width, hid)),
            fixed((hid, width)),
            fixed((width, lanes)),
        ]
        + [pl.BlockSpec(memory_space=pl.ANY)] * (5 * half),
        kept + [slots, moving, fixed((lanes, width))],
        [like((2 * count, size), BF) for size in (width, hid, width, hid)]
        + [like(dy.shape, BF), like((count, width), BF)]
        + [like((lanes, width), F32)],
        (rows, dy, w_up, w_down, w_small, *before),
        alias={6 + k: k for k in range(5)} if half else None,
        vmem=56,
    )


def dense_kernel(experts, at_ref, rows_ref, dy_ref, in_ref, out_ref, w_small_ref, *outs):
    hid_ref, grad_ref, d_up_ref, mix_ref, db_ref, small_ref = outs
    rows = rows_ref[...]
    up = mm(rows, in_ref[...])
    logits = mm(rows, w_small_ref[...])
    lane = lax.broadcasted_iota(jnp.int32, logits.shape, 1)
    first, second = two_coefs(logits, lane, experts)
    dy = dy_ref[...].astype(F32)
    grad = (first * dy).astype(BF)
    grad_ref[...] = grad
    d_hidden = mm_t(grad, out_ref[...])
    hidden, slope = gelu_both(up)
    hidden = hidden.astype(BF)
    hid_ref[...] = hidden
    d_up = (d_hidden * slope).astype(BF)
    d_up_ref[...] = d_up
    dense = mm(hidden, out_ref[...])
    mix_ref[...] = first * dense
    mixed = first * second * jnp.sum(dy * dense, axis=1, keepdims=True)
    d_small = jnp.where(lane == experts, mixed, 0.0) - jnp.where(lane == experts + 1, mixed, 0.0)
    db_ref[...] = mm_t(d_up, in_ref[...]) + small_back(d_small, rows, w_small_ref, small_ref, pl.program_id(0))


def dense_rows(at, rows, dy, w_in, w_out, w_small, experts):
    (count, width), hid, lanes = rows.shape, w_in.shape[1], w_small.shape[1]
    blk = min(512, count)
    row_out = pl.BlockSpec((blk, width), lambda i, n: (i, 0))
    hid_out = pl.BlockSpec((blk, hid), lambda i, n: (i, 0))
    return call(
        partial(dense_kernel, experts),
        "dense_rows",
        at,
        (count // blk,),
        [row_out, row_out, fixed((width, hid)), fixed((hid, width)), fixed((width, lanes))],
        [hid_out, row_out, hid_out, row_out, row_out, fixed((lanes, width))],
        [
            like((count, hid), BF),
            like((count, width), BF),
            like((count, hid), BF),
            like((count, width), F32),
            like((count, width), F32),
            like((lanes, width), F32),
        ],
        (rows, dy, w_in, w_out, w_small),
        vmem=56,
    )


def turned(value):
    return value.astype(F32).T.astype(BF)


def dense_grads_kernel(at_ref, b_ref, d_up_ref, grad_ref, hid_ref, keep_ref, give_ref):
    width = d_up_ref.shape[1]
    first = mm(turned(b_ref[...]), d_up_ref[...]).astype(BF)
    second = mm(turned(grad_ref[...]), hid_ref[...]).astype(BF)
    half = pl.num_programs(0) // 2
    for side, ref in ((0, keep_ref), (1, give_ref)):

        @pl.when(pl.program_id(0) // half == side)
        def _():
            ref[0, :, :width] = first
            ref[0, :, width:] = second


def dense_grads(at, b, d_up, grad, hidden, parts):
    (rows, width), hid = b.shape, hidden.shape[1]
    own, half, bits = width // parts, parts // 2, parts.bit_length() - 1

    def part(q, n):
        turned_q = sum([((q // 2**k) % 2) * 2 ** (bits - 1 - k) for k in range(bits)])
        return turned_q ^ n[2]

    column = pl.BlockSpec((rows, own), lambda q, n: (0, part(q, n)))
    shape = (1, own, 2 * hid)
    return call(
        dense_grads_kernel,
        "dense_grads",
        at,
        (parts,),
        [column, fixed((rows, hid)), column, fixed((rows, hid))],
        [
            pl.BlockSpec(shape, lambda q, n: (jnp.minimum(q, half - 1), 0, 0)),
            pl.BlockSpec(shape, lambda q, n: (jnp.maximum(q - half, 0), 0, 0)),
        ],
        [like((half, own, 2 * hid), BF)] * 2,
        (b, d_up, grad, hidden),
    )


def attention_grads_kernel(experts, at_ref, *refs):
    grads, o_refs, refs = refs[:GROUP], refs[GROUP : GROUP + 6], refs[GROUP + 6 :]
    a_ref, dh_ref, w_ref, gain_ref, bias_ref, sums_ref = refs[:6]
    small_refs, (out_ref, all_s) = refs[6:-2], refs[-2:]
    heads, features = GROUP * HD, grads[1].shape[0]
    products, plain = 0.0, 0.0
    for k in range(GROUP):
        head = at_ref[0] ^ k
        rows = pl.ds(pl.multiple_of(head * features, features), features)
        grad = grads[k][...]
        weight = w_ref[head].astype(F32)
        total = mm(grad, a_ref[...])
        all_s[rows, :] = total
        each = jnp.sum(grad.astype(F32), axis=1, keepdims=True)
        products = products + jnp.sum(total * weight, axis=0, keepdims=True)
        plain = plain + jnp.sum(each * weight, axis=0, keepdims=True)
    first = GROUP * features
    for r, piece in enumerate(in_order(at_ref[1], *[ref[...] for ref in o_refs])):
        rows = pl.ds(pl.multiple_of(first + ((at_ref[1] + r) % 4) * heads, heads), heads)
        all_s[rows, :] = mm(piece, dh_ref[...])
    first += 4 * heads
    small = add_up(small_refs)
    row = lax.broadcasted_iota(jnp.int32, small.shape, 0)
    d_gain = (products - bias_ref[...] * plain) / gain_ref[...]
    for k, sums in enumerate((sums_ref[0:1, :], sums_ref[1:2, :], d_gain, plain)):
        small = jnp.where(row == experts + 2 + k, sums, small)
    all_s[first:, :] = small
    out_ref[...] = all_s[...].T.astype(BF)


def attention_grads(at, grads, o, a, dh, w_heads, gain, bias, sums, small, experts):
    rows, width = a.shape
    features, lanes = grads[0].shape[0], small[0].shape[0]
    piece = pl.BlockSpec((o[0].shape[0], dh.shape[0]), lambda i, n: (0, n[1]))
    height = GROUP * features + 4 * o[0].shape[0] + lanes
    blk = min(256, width)
    return call(
        partial(attention_grads_kernel, experts),
        "attention_grads",
        at,
        (width // blk,),
        [fixed((features, rows))] * GROUP
        + [piece] * 6
        + [columns(rows, blk), columns(dh.shape[0], blk)]
        + [pl.BlockSpec((GROUP, features, blk), lambda i, n: (0, 0, i))]
        + [columns(1, blk)] * 2
        + [columns(2, blk)]
        + [columns(lanes, blk)] * len(small),
        pl.BlockSpec((blk, height), lambda i, n: (i, 0)),
        like((width, height), BF),
        (*grads, *o, a, dh, w_heads, gain, bias, sums, *small),
        scratch=[pltpu.VMEM((height, blk), F32)],
    )


def project_kernel(at_ref, *refs):
    grads, w_ref, outs, turned_s = refs[:GROUP], refs[GROUP], refs[GROUP + 1 : -1], refs[-1]
    rows = turned_s.shape[1]
    blk = rows // 4

    @pl.when(pl.program_id(0) == 0)
    def _():
        for s in range(GROUP):
            for r in range(4):
                lanes = pl.ds(pl.multiple_of(((at_ref[1] + r) % 4) * blk, blk), blk)
                turned_s[s, r * blk : (r + 1) * blk, :] = turned(grads[s][:, lanes])

    total = 0.0
    for s in range(GROUP):
        total = total + mm(turned_s[s], w_ref[at_ref[0] ^ s])
    write_shares(at_ref[1], total, *outs)


def project_back(at, grads, w_heads):
    features, rows = grads[0].shape
    width = w_heads.shape[2]
    blk = min(256, width)
    return call(
        project_kernel,
        "project_back",
        at,
        (width // blk,),
        [fixed((features, rows))] * GROUP
        + [pl.BlockSpec((GROUP, features, blk), lambda i, n: (0, 0, i))],
        [columns(rows // 4, blk)] * 5,
        share_shapes(rows // 4, width),
        (*grads, w_heads),
        scratch=[pltpu.VMEM((GROUP, rows, features), BF)],
    )


def hop(value, *pairs):
    return lax.ppermute(value, "mp", pairs)


def rotate(value, steps):
    return hop(value, *[(s, (s + steps) % 4) for s in range(4)])


def gather_near(own):
    right = hop(own, (0, 1), (1, 2), (2, 3))
    left = hop(own, (1, 0), (2, 1), (3, 2))
    return own, right, left, hop(own, (0, 3), (3, 0))


def gather_far(near):
    _, right, left, _ = near
    return *near, hop(right, (1, 2), (2, 3)), hop(left, (1, 0), (2, 1))


def gather_pieces(own):
    return gather_far(gather_near(own))


def scatter_far(shares):
    _, _, two, _, end = shares
    return hop(two, (2, 1), (3, 2)), hop(two, (0, 1), (1, 2)), hop(end, (0, 3), (3, 0))


def scatter_near(shares, came):
    own, one, _, three, _ = shares
    from_right, from_left, from_end = came
    three = (three.astype(F32) + from_right.astype(F32)).astype(BF)
    one = (one.astype(F32) + from_left.astype(F32)).astype(BF)
    return own, hop(three, (1, 0), (2, 1), (3, 2)), hop(one, (0, 1), (1, 2), (2, 3)), from_end


def group_swap(value, s):
    count = lax.axis_size("dp")
    return lax.ppermute(value, "dp", [(t, t ^ s) for t in range(count)])


def expert_swap(value, experts):
    wide = value.reshape(experts, value.shape[0] // experts, value.shape[1])
    return lax.all_to_all(wide, "dp", 0, 0, tiled=True).reshape(value.shape)


def roll_rows(value, start):
    twice = jnp.concatenate([value, value], axis=0)
    return lax.dynamic_slice_in_dim(twice, start, value.shape[0], 0)


def add_halves(keep, came):
    return (keep.astype(F32) + came.astype(F32)).astype(BF)


def body(
    tokens,
    cotangent,
    ln_gains,
    ln_biases,
    w_qkv,
    w_o,
    w_in,
    w_out,
    w_router,
    w_coef,
    w_up,
    w_down,
    routes,
    long_group,
):
    rows, width = tokens.shape
    dps = lax.axis_size("dp")
    mine, position = lax.axis_index("mp"), lax.axis_index("dp")
    quarter = rows // 4
    start = mine * quarter
    heads_loc = w_qkv.shape[2] // HD
    hid = w_in.shape[1]
    experts = w_router.shape[1]
    capacity = max(2, 2 * rows // experts)
    half = capacity // 2
    barrier = lax.optimization_barrier
    first_len = lax.dynamic_index_in_dim(long_group, position // GROUP, 0, keepdims=False)
    at = jnp.stack([position % GROUP, mine, position, first_len]).astype(jnp.int32)
    gains = [ln_gains[0:1], ln_gains[1:2]]
    biases = [ln_biases[0:1], ln_biases[1:2]]
    w_o_all = lax.all_gather(w_o, "mp", axis=0, tiled=True)

    w_heads = w_qkv.reshape(width, 3, heads_loc, HD).transpose(2, 1, 3, 0)
    w_heads = w_heads.reshape(heads_loc, 3 * HD, width)
    a_r, *qkv = project(at, tokens, gains[0], biases[0], w_heads)
    qkv = [qkv[0]] + [group_swap(qkv[s], s) for s in (1, 2, 3)]

    route = roll_rows(routes, start)[:, 0]
    picked = (route[:, None] == jnp.arange(experts, dtype=jnp.int32)[None, :]).astype(jnp.int32)
    slot = jnp.sum((jnp.cumsum(picked, axis=0) - picked) * picked, axis=1)
    dy_b = roll_rows(cotangent, start)
    send_dy = dispatch(at, (route * capacity + slot)[None, :], dy_b, experts * capacity)
    *qkv, send_dy = barrier((*qkv, send_dy))
    in_half = [slot < half, slot >= half]
    dests = [
        jnp.where(in_half[k], route * half + slot - k * half, -1).astype(jnp.int32) for k in (0, 1)
    ]

    *o_t, lse = attend(at, qkv)
    *o_t, w_o_all = barrier((*o_t, w_o_all))
    o_heads = [o_t[0]] + [group_swap(o_t[s], s) for s in (1, 2, 3)]
    lanes = -(-(experts + 2) // 128) * 128
    w_small = jnp.concatenate(
        [w_router, w_coef, jnp.zeros((width, lanes - experts - 2), BF)], axis=1
    )
    *o_heads, send_dy, w_small = barrier((*o_heads, send_dy, w_small))
    got_dy = expert_swap(send_dy, experts).reshape(experts, capacity, width)
    o_pieces = gather_pieces(stack(at, o_heads))
    h, b_r = mid(at, o_pieces, w_o_all, tokens, gains[1], biases[1])

    send_0 = dispatch(at, dests[0][None, :], b_r, experts * half)
    send_0, got_dy = barrier((send_0, got_dy))
    got_0 = expert_swap(send_0, experts)
    send_1 = dispatch(at, dests[1][None, :], b_r, experts * half)
    b_r, send_1 = barrier((b_r, send_1))
    hidden, dense_grad, d_up, mix_base, db_base, small_t = dense_rows(
        at, b_r, dy_b, w_in, w_out, w_small, experts
    )
    send_1, got_0, db_base = barrier((send_1, got_0, db_base))
    got_1 = expert_swap(send_1, experts)

    *kept, d_rows_0, small_0 = expert_rows(
        at, got_0, got_dy, w_up[0], w_down[0], w_small, experts, 0, ()
    )
    back_0 = expert_swap(d_rows_0, experts)
    *kept, d_rows_1, small_1 = expert_rows(
        at, got_1, got_dy, w_up[0], w_down[0], w_small, experts, 1, kept
    )
    got, hidden_e, d_y, d_eu, back_y = kept
    back_1 = expert_swap(d_rows_1, experts)
    d_rows_1, b_r = barrier((d_rows_1, b_r))
    halving = width == dps * 128
    if halving:
        grads = dense_grads(at, b_r, d_up, dense_grad, hidden, dps)
    else:
        grads = [ein("td,tf->df", b_r, d_up).astype(BF), ein("td,tf->df", dense_grad, hidden).astype(BF)]
    back_0, back_1, back_y, *grads = barrier((back_0, back_1, back_y, *grads))

    dest_cols = [dest[:, None] for dest in dests]
    tok_y = expert_swap(back_y.reshape(experts * capacity, width), experts)
    shares = combine(at, dest_cols, [back_0, back_1], db_base)
    far = scatter_far(shares)
    *far, g_0, g_1 = barrier((*far, *grads))
    grads = [g_0, g_1]
    shares = scatter_near(shares, far)
    dh, dh_r, sums_2, *do_q = mid_back(at, shares, w_o_all, h, dy_b, gains[1])
    do_q = [do_q[0]] + [rotate(do_q[r], -r) for r in (1, 2, 3)]

    mix = combine(at, [(route * capacity + slot)[:, None]], [tok_y], mix_base, h)
    *do_q, mix = barrier((*do_q, mix))
    output = lax.psum(mix, "mp")
    do_heads = unsplit(at, do_q)
    do_t = [do_heads[0]] + [group_swap(do_heads[s], s) for s in (1, 2, 3)]
    if halving:
        came_1 = group_swap(grads[1], 1)
        half = dps // 4
        give = add_halves(grads[0][half:], came_1[half:])
        *do_t, give = barrier((*do_t, give))
        came_2 = group_swap(give, 2)
    d_qkv = attend_back(at, qkv, do_t, o_t, lse)
    if halving:
        keep = add_halves(grads[0][:half], came_1[:half])
        *d_qkv, came_2, keep = barrier((*d_qkv, came_2, keep))
        grads = add_halves(keep, came_2)
        bit = 4
        while bit < dps:
            half = grads.shape[0] // 2
            grads = add_halves(grads[:half], group_swap(grads[half:], bit))
            bit *= 2
        grads = [grads[0][:, :hid], grads[0][:, hid:]]
    else:
        grads = [lax.psum_scatter(grad, "dp", scatter_dimension=0, tiled=True) for grad in grads]

    d_own, got, hidden_e, d_y, d_eu = barrier((d_qkv[0], got, hidden_e, d_y, d_eu))
    d_qkv = [d_own] + [group_swap(d_qkv[s], s) for s in (1, 2, 3)]
    grad_down = ein("rf,rd->fd", hidden_e, d_y)
    *d_qkv, grad_down = barrier((*d_qkv, grad_down))
    shares = project_back(at, d_qkv, w_heads)
    far = scatter_far(shares)
    grads_a = attention_grads(
        at, d_qkv, o_pieces, a_r, dh_r, w_heads, gains[0], biases[0], sums_2, (small_0, small_1, small_t), experts
    )
    grad_up = ein("rd,rf->df", got, d_eu)
    grads_a, output, grad_up, *far = barrier((grads_a, output, grad_up, *far))
    grads_a = lax.psum_scatter(grads_a, "dp", scatter_dimension=0, tiled=True).T
    shares = scatter_near(shares, far)
    grad_q = first_back(at, shares, tokens, dh, gains[0])
    grad_tokens = join(at, gather_pieces(grad_q))

    own, heads = width // dps, heads_loc * HD
    grad_qkv = grads_a[: 3 * heads].astype(F32).reshape(heads_loc, 3, HD, own).transpose(3, 1, 0, 2)
    grad_qkv = grad_qkv.reshape(own, 3, heads)
    grad_in = grads[0].astype(F32)
    grad_out = grads[1].astype(F32).T
    rest = grads_a[3 * heads : 7 * heads].reshape(4, heads, own)
    small = jnp.broadcast_to(grads_a[7 * heads :], (4, lanes, own))
    rest = lax.all_to_all(jnp.concatenate([rest, small], axis=1), "mp", 0, 0, tiled=True)
    rest = jnp.sum(rest.astype(F32), axis=0)
    grad_o, small = rest[:heads], rest[heads:]
    small_out = small[: experts + 2].T
    return (
        output,
        grad_tokens,
        jnp.stack([small[experts + 4], small[experts + 2]]),
        jnp.stack([small[experts + 5], small[experts + 3]]),
        grad_qkv,
        grad_o,
        grad_in,
        grad_out,
        small_out[:, :experts],
        small_out[:, experts:],
        grad_up[None],
        grad_down[None],
    )


def solution(mesh):
    in_specs = (
        P("dp", None),
        P("dp", None),
        P(),
        P(),
        P(None, None, "mp"),
        P("mp", None),
        P(None, "mp"),
        P("mp", None),
        P(),
        P(),
        P("dp", None, "mp"),
        P("dp", "mp", None),
        P("dp", None),
        P(),
    )
    out_specs = (
        P("dp", None),
        P("dp", None),
        P(None, "dp"),
        P(None, "dp"),
        P("dp", None, "mp"),
        P("mp", "dp"),
        P("dp", "mp"),
        P("mp", "dp"),
        P("dp", None),
        P("dp", None),
        P("dp", None, "mp"),
        P("dp", "mp", None),
    )
    return jax.shard_map(body, mesh=mesh, in_specs=in_specs, out_specs=out_specs, check_vma=False)
```
